32 devices in a mesh: dp: 16 (over z, y, core), tensor: 2 (over x).
Axes of the slice: x: 2, y: 2, z: 4, core: 2. Of those that a mesh axis runs over, the one named last changes fastest.
Arguments:
- tokens: bfloat16 [16384, 1536], P(('dp', 'tensor')), may hold values from -6 to 6
- cotangent: bfloat16 [16384, 1536], P(('dp', 'tensor')), may hold values from -6 to 6
- lengths: int32 [16, 4], P('dp'), may hold values from 0 to 1024, as said below
- norm_gain: bfloat16 [1536], P(('dp', 'tensor')), may hold values from 0.099609375 to 1.8984375
- w_zx: bfloat16 [2, 1536, 3072], P(None, 'dp', 'tensor'), may hold values from -0.15625 to 0.15625
- w_bc: bfloat16 [2, 1536, 128], P(None, ('dp', 'tensor')), may hold values from -0.15625 to 0.15625
- w_dt: bfloat16 [1536, 48], P('dp', 'tensor'), may hold values from -0.15625 to 0.15625
- conv_x: bfloat16 [48, 256], P('tensor', 'dp'), may hold values from -0.5 to 0.5
- conv_x_bias: bfloat16 [48, 64], P('tensor', 'dp'), may hold values from -0.5 to 0.5
- conv_bc: bfloat16 [2, 512], P(None, ('dp', 'tensor')), may hold values from -0.5 to 0.5
- conv_bc_bias: bfloat16 [2, 128], P(None, ('dp', 'tensor')), may hold values from -0.5 to 0.5
- dt_bias: float32 [48], P('tensor'), may hold values from -7 to -3
- a_log: float32 [48], P('tensor'), may hold values from -1 to 1.5
- d_skip: float32 [48], P('tensor'), may hold values from 0.5 to 2
- gate_gain: bfloat16 [48, 64], P('tensor', 'dp'), may hold values from 0.099609375 to 1.8984375
- w_out: bfloat16 [3072, 1536], P('tensor', 'dp'), may hold values from -0.109375 to 0.109375
Outputs:
- layer_out: bfloat16 [16384, 1536], P(('dp', 'tensor'))
- grad_tokens: float32 [16384, 1536], P(('dp', 'tensor'))
- grad_norm_gain: float32 [1536], P(('dp', 'tensor'))
- grad_w_zx: float32 [2, 1536, 3072], P(None, 'dp', 'tensor')
- grad_w_bc: float32 [2, 1536, 128], P(None, ('dp', 'tensor'))
- grad_w_dt: float32 [1536, 48], P('dp', 'tensor')
- grad_conv_x: float32 [48, 256], P('tensor', 'dp')
- grad_conv_x_bias: float32 [48, 64], P('tensor', 'dp')
- grad_conv_bc: float32 [2, 512], P(None, ('dp', 'tensor'))
- grad_conv_bc_bias: float32 [2, 128], P(None, ('dp', 'tensor'))
- grad_dt_bias: float32 [48], P('tensor')
- grad_a_log: float32 [48], P('tensor')
- grad_d_skip: float32 [48], P('tensor')
- grad_gate_gain: float32 [48, 64], P('tensor', 'dp')
- grad_w_out: float32 [3072, 1536], P('tensor', 'dp')
The draws below stay inside these ranges and needn't reach their ends.
Inputs may be any that keep to these rules, and one draw needn't show every extreme that they name: Row g lists the lengths of up to 4 sequences packed in order from the first row of group g (zero entries are empty slots); a row sums to at most 1024, rows past the sum are padding; the first entry of every row exceeds 1024 - 512; some row is 1024 followed by zeros.
All inputs are finite; a program needn't handle non-finite values.
Results may differ from the reference program's by a relative error of at most 0.011.
Values may be sent and summed in bfloat16 or wider, within the bound.
No kernel may reach another device: no remote copies, remote signals or barrier semaphores. Data moves between devices by JAX's collectives and lax.ppermute only.
A program may use at most 256 MiB of HBM per device.

```python
import jax
import jax.numpy as jnp
from jax import lax

D = 1536
H = 48
HEADDIM = 64
N = 128
K = 4
BLOCK = 256
DI = 3072
TOK_DEV = 512
SEQS = 4
GROUP = 1024
TOKENS = 16384
N_DP = 16


def draw_lengths(key, part):
    key = jax.random.fold_in(key, 7)
    key_total, key_first, key_cuts, key_full = jax.random.split(key, 4)
    lowest_total = GROUP - TOK_DEV + 1
    totals = jax.random.randint(key_total, (N_DP,), lowest_total, GROUP + 1).astype(jnp.int32)
    firsts = lowest_total + jax.random.randint(key_first, (N_DP,), 0, GROUP + 1) % (totals - lowest_total + 1)
    remainders = totals - firsts
    cut_points = jnp.sort(jax.random.randint(key_cuts, (N_DP, SEQS - 2), 0, GROUP + 1) % (remainders[:, None] + 1), axis=1)
    bounds = jnp.concatenate([jnp.zeros((N_DP, 1), jnp.int32), cut_points.astype(jnp.int32), remainders[:, None].astype(jnp.int32)], axis=1)
    others = bounds[:, 1:] - bounds[:, :-1]
    drawn_rows = jnp.concatenate([firsts[:, None].astype(jnp.int32), others], axis=1)
    full_group = jax.random.randint(key_full, (), 0, N_DP)
    single = jnp.concatenate([jnp.full((1,), GROUP, jnp.int32), jnp.zeros((SEQS - 1,), jnp.int32)])
    group_index = jnp.arange(N_DP)
    return jnp.where((group_index == full_group)[:, None], single[None, :], drawn_rows).astype(jnp.int32)


def levels(own_key, dims, cuts, least, high):
    loudness, own = 1.0, jax.random.fold_in(own_key, 6)
    for dim, parts in cuts:
        heights = jnp.exp(jax.random.uniform(jax.random.fold_in(own, dim), (parts,), jnp.float32, least / len(cuts), high / len(cuts)))
        loudness = loudness * jnp.repeat(heights, dims[dim] // parts).reshape([-1 if axis == dim else 1 for axis in range(len(dims))])
    return loudness


def bell_draw(rng, shape, width, bound, cuts=(), held_as=jnp.bfloat16):
    level = levels(rng, shape, cuts, -0.22, 0.18) if cuts else 1.0
    drawn = jax.random.normal(rng, shape, jnp.float32) * width * level
    return jnp.minimum(jnp.maximum(drawn, -bound), bound).astype(held_as)


def setup_inputs(seed: int = 0) -> dict:
    splits = jax.random.split(jax.random.key(seed), 17)
    return {
        "tokens": bell_draw(splits[0], (TOKENS, D), 1.0, 6.0, ((0, 32),)),
        "cotangent": bell_draw(splits[1], (TOKENS, D), 1.0, 6.0, ((0, 32),)),
        "lengths": draw_lengths(jax.random.fold_in(splits[16], 71), 0),
        "norm_gain": jnp.clip(1.0 + 0.18 * jax.random.normal(splits[3], (D,), jnp.float32), 0.099609375, 1.8984375).astype(jnp.bfloat16),
        "w_zx": bell_draw(splits[4], (2, D, DI), D ** -0.5, 0.15625, ((1, 16), (2, 2))),
        "w_bc": bell_draw(splits[5], (2, D, N), D ** -0.5, 0.15625, ((1, 32),)),
        "w_dt": bell_draw(splits[6], (D, H), D ** -0.5, 0.15625, ((0, 16), (1, 2))),
        "conv_x": jnp.clip(jax.random.uniform(splits[7], (H, HEADDIM * K), jnp.float32, -0.5, 0.5) * levels(splits[7], (H, HEADDIM * K), ((0, 2), (1, 16)), -0.4, 0.0), -0.5, 0.5).astype(jnp.bfloat16),
        "conv_x_bias": jnp.clip(jax.random.uniform(splits[8], (H, HEADDIM), jnp.float32, -0.5, 0.5) * levels(splits[8], (H, HEADDIM), ((0, 2), (1, 16)), -0.4, 0.0), -0.5, 0.5).astype(jnp.bfloat16),
        "conv_bc": jnp.clip(jax.random.uniform(splits[9], (2, N * K), jnp.float32, -0.5, 0.5) * levels(splits[9], (2, N * K), ((1, 32),), -0.4, 0.0), -0.5, 0.5).astype(jnp.bfloat16),
        "conv_bc_bias": jnp.clip(jax.random.uniform(splits[10], (2, N), jnp.float32, -0.5, 0.5) * levels(splits[10], (2, N), ((1, 32),), -0.4, 0.0), -0.5, 0.5).astype(jnp.bfloat16),
        "dt_bias": jnp.clip(-7.0 + 4.0 * jax.random.uniform(splits[11], (H,), jnp.float32) ** levels(splits[11], (H,), ((0, 2),), -0.2, 0.2), -7.0, -3.0),
        "a_log": jnp.clip(-1.0 + 2.5 * jax.random.uniform(splits[12], (H,), jnp.float32) ** levels(splits[12], (H,), ((0, 2),), -0.2, 0.2), -1.0, 1.5),
        "d_skip": jnp.clip(0.5 + 1.5 * jax.random.uniform(splits[13], (H,), jnp.float32) ** levels(splits[13], (H,), ((0, 2),), -0.2, 0.2), 0.5, 2.0),
        "gate_gain": jnp.clip(1.0 + 0.18 * jax.random.normal(splits[14], (H, HEADDIM), jnp.float32), 0.099609375, 1.8984375).astype(jnp.bfloat16),
        "w_out": bell_draw(splits[15], (DI, D), DI ** -0.5, 0.109375, ((0, 2), (1, 16))),
    }


EPSILON = 1e-05
HIGHEST = lax.Precision.HIGHEST

@jax.custom_vjp
def low(v):
    return lax.optimization_barrier(v.astype(jnp.bfloat16)).astype(jnp.float32)

@jax.custom_vjp
def low_back(v):
    return v

def low_keep(v):
    return (low(v), None)

def low_pass(kept, grad):
    return (grad,)

def back_keep(v):
    return (v, None)

def back_low(kept, grad):
    return (low(grad),)
low.defvjp(low_keep, low_pass)
low_back.defvjp(back_keep, back_low)

def segment_rows(seq_lengths, row_count):
    ends = jnp.cumsum(seq_lengths).astype(jnp.int32)
    places = jnp.arange(row_count).astype(jnp.int32)
    segment_ids = lax.optimization_barrier(jnp.sum((places[:, None] >= ends[None, :]).astype(jnp.int32), axis=1)).astype(jnp.int32)
    live_rows = (segment_ids < seq_lengths.shape[0]).astype(jnp.float32)
    return (segment_ids, live_rows)

def causal_conv(signal, taps, offset, segment_ids):
    row_count = signal.shape[0]
    last_tap = taps.shape[1] - 1
    total = signal * taps[:, last_tap] + offset
    for lag_rows in range(1, last_tap + 1):
        earlier = jnp.concatenate([jnp.zeros((lag_rows, signal.shape[1]), signal.dtype), signal[:row_count - lag_rows]], axis=0)
        earlier_ids = jnp.concatenate([jnp.full((lag_rows,), -1, jnp.int32), segment_ids[:row_count - lag_rows]])
        same_doc = (earlier_ids == segment_ids).astype(signal.dtype)
        total = total + earlier * taps[:, last_tap - lag_rows] * same_doc[:, None]
    return jax.nn.silu(total)

def block_scan(heads_x, b_rows, c_rows, step_size, rate, segment_ids):
    row_count, head_count, head_width = heads_x.shape
    blocks = row_count // BLOCK
    inputs = (heads_x.reshape(blocks, BLOCK, head_count, head_width), b_rows.reshape(blocks, BLOCK, -1), c_rows.reshape(blocks, BLOCK, -1), step_size.reshape(blocks, BLOCK, head_count), rate.reshape(blocks, BLOCK, head_count), segment_ids.reshape(blocks, BLOCK))
    places = jnp.arange(BLOCK).astype(jnp.int32)
    causal = places[:, None] >= places[None, :]

    def advance(carry, block_data):
        state, last_id = carry
        x_block, b_block, c_block, dt_block, rate_block, id_block = block_data
        decayed = jnp.cumsum(rate_block, axis=0)
        visible = ((id_block[:, None] == id_block[None, :]) & causal)[:, :, None]
        spacing = decayed[:, None, :] - decayed[None, :, :]
        factor = jnp.where(visible, jnp.exp(jnp.where(visible, spacing, 0.0)), 0.0)
        scores = jnp.dot(c_block, b_block.T, precision=HIGHEST)
        mixing = scores[:, :, None] * factor * dt_block[None, :, :]
        inside = jnp.einsum('rsh,shp->rhp', mixing, x_block, precision=HIGHEST)
        carried = (id_block == last_id).astype(x_block.dtype)[:, None] * jnp.exp(decayed)
        outside = jnp.einsum('rn,hnp->rhp', c_block, state, precision=HIGHEST) * carried[:, :, None]
        final_id = id_block[BLOCK - 1]
        closing = decayed[BLOCK - 1]
        weight_end = (id_block == final_id).astype(x_block.dtype)[:, None] * jnp.exp(closing[None, :] - decayed) * dt_block
        fresh = jnp.einsum('sn,shp->hnp', b_block, x_block * weight_end[:, :, None], precision=HIGHEST)
        passing = (final_id == last_id).astype(x_block.dtype) * jnp.exp(closing)
        return ((state * passing[:, None, None] + fresh, final_id), inside + outside)
    start = (jnp.zeros((head_count, b_rows.shape[1], head_width), jnp.float32), jnp.array(-1, jnp.int32))
    finished, outputs = lax.scan(jax.checkpoint(advance), start, inputs)
    return outputs.reshape(row_count, head_count, head_width)

def group_layer(tokens, seq_lengths, norm_gain, w_zx, w_bc, w_dt, conv_x, conv_x_bias, conv_bc, conv_bc_bias, dt_bias, a_log, d_skip, gate_gain, w_out):
    segment_ids, live_rows = segment_rows(seq_lengths, GROUP)
    normed = low(tokens * lax.rsqrt(lax.optimization_barrier(jnp.mean(tokens * tokens, axis=1, keepdims=True)) + EPSILON) * norm_gain)
    z_rows = low_back(jnp.dot(normed, w_zx[0], precision=HIGHEST))
    x_rows = low_back(jnp.dot(normed, w_zx[1], precision=HIGHEST))
    b_raw = low_back(jnp.dot(normed, w_bc[0], precision=HIGHEST))
    c_raw = low_back(jnp.dot(normed, w_bc[1], precision=HIGHEST))
    dt_raw = low_back(jnp.dot(normed, w_dt, precision=HIGHEST))
    x_conv = low(causal_conv(x_rows, conv_x.reshape(DI, K), conv_x_bias.reshape(DI), segment_ids))
    taps_bc = conv_bc.reshape(2, N, K)
    b_rows = low(causal_conv(b_raw, taps_bc[0], conv_bc_bias[0], segment_ids))
    c_rows = low(causal_conv(c_raw, taps_bc[1], conv_bc_bias[1], segment_ids))
    step_size = jax.nn.softplus(dt_raw + dt_bias)
    rate = -jnp.exp(a_log) * step_size
    heads_x = x_conv.reshape(GROUP, H, HEADDIM)
    scanned = block_scan(heads_x, b_rows, c_rows, step_size, rate, segment_ids) + d_skip[None, :, None] * heads_x
    gated = scanned.reshape(GROUP, DI) * jax.nn.silu(z_rows)
    scaled = low(gated * lax.rsqrt(lax.optimization_barrier(jnp.mean(gated * gated, axis=1, keepdims=True)) + EPSILON) * gate_gain.reshape(DI))
    return tokens + live_rows[:, None] * jnp.dot(scaled, w_out, precision=HIGHEST)

def reference(tokens, cotangent, lengths, norm_gain, w_zx, w_bc, w_dt, conv_x, conv_x_bias, conv_bc, conv_bc_bias, dt_bias, a_log, d_skip, gate_gain, w_out):
    params = (norm_gain, w_zx, w_bc, w_dt, conv_x, conv_x_bias, conv_bc, conv_bc_bias, dt_bias, a_log, d_skip, gate_gain, w_out)
    params = tuple((member.astype(jnp.float32) for member in params))

    def whole_layer(flat_tokens, *weights):
        grouped = flat_tokens.reshape(N_DP, GROUP, D)

        def one_group(group_pair):
            return group_layer(group_pair[0], group_pair[1], *weights)
        return lax.map(jax.checkpoint(one_group), (grouped, lengths)).reshape(TOKENS, D)
    result, pullback = jax.vjp(whole_layer, tokens.astype(jnp.float32), *params)
    grads = pullback(cotangent.astype(jnp.float32))
    return (result.astype(jnp.bfloat16), grads[0], grads[1], grads[2], grads[3], grads[4], grads[5], grads[6], grads[7], grads[8], grads[9], grads[10], grads[11], grads[12], grads[13])
```

```python
from functools import partial

import jax
import jax.numpy as jnp
from jax import lax
from jax.experimental import pallas as pl
from jax.experimental.pallas import tpu as pltpu
from jax.sharding import PartitionSpec as P

EPSILON = 1e-05
HIGHEST = lax.Precision.HIGHEST
K = 4
WIDTH = 64
STATE = 128
Q = 128
LANES = 128
LOG2E = 1.4426950408889634
VMEM_LIMIT = 60 * 1024 * 1024
F32 = jnp.float32
BF16 = jnp.bfloat16

NN = (((1,), (0,)), ((), ()))
NT = (((1,), (1,)), ((), ()))
TN = (((0,), (0,)), ((), ()))


def mm(a, b, dims=NN):
    return lax.dot_general(a, b, dims, preferred_element_type=F32)


def mm_exact(a, b, dims=NN):
    return lax.dot_general(a, b, dims, preferred_element_type=F32, precision=HIGHEST)


def iota(shape, dim):
    return lax.broadcasted_iota(jnp.int32, shape, dim)


def segment_of(rows, ends_ref, count):
    total = (rows >= ends_ref[0]).astype(jnp.int32)
    for j in range(1, count):
        total = total + (rows >= ends_ref[j]).astype(jnp.int32)
    return total


def scalar_segment(row, ends_ref, count):
    total = jnp.where(row >= ends_ref[0], 1, 0)
    for j in range(1, count):
        total = total + jnp.where(row >= ends_ref[j], 1, 0)
    return total


def sigmoid(v):
    return 0.5 * jnp.tanh(0.5 * v) + 0.5


def softplus(v):
    return jnp.maximum(v, 0.0) + jnp.log1p(jnp.exp(-jnp.abs(v)))


def chunk_masks(chunk, ends_ref, count):
    base = chunk * Q
    rows = iota((Q, Q), 0) + base
    cols = iota((Q, Q), 1) + base
    row_ids = segment_of(rows, ends_ref, count)
    col_ids = segment_of(cols, ends_ref, count)
    same = row_ids == col_ids
    before_id = jnp.where(chunk == 0, -1, scalar_segment(base - 1, ends_ref, count))
    final_id = scalar_segment(base + Q - 1, ends_ref, count)
    carry = (row_ids == before_id).astype(F32)
    last = (row_ids == final_id).astype(F32)
    passing = jnp.where(before_id == final_id, 1.0, 0.0).astype(F32)
    return rows, cols, row_ids, same, carry, last, passing


def decays(dt_raw, par_ref):
    shifted = dt_raw + par_ref[0:1, :]
    step = softplus(shifted)
    decay_rate = jnp.exp(par_ref[1:2, :])
    return shifted, step, decay_rate


def pair_columns(values, pair, first):
    left = jnp.broadcast_to(values[:, 2 * pair : 2 * pair + 1], (Q, LANES))
    right = jnp.broadcast_to(values[:, 2 * pair + 1 : 2 * pair + 2], (Q, LANES))
    return left, right, jnp.where(first, left, right)


def scan_forward(
    heads, ends_ref, xr_ref, small_ref, taps_ref, par_ref, skip_ref,
    xc_ref, pre_ref, bc_ref, y_ref, st_ref, buf, state,
):
    count = ends_ref.shape[0]
    inner = heads * WIDTH
    chunk = pl.program_id(0)

    @pl.when(chunk == 0)
    def _():
        buf[0:8, :] = jnp.zeros((8, buf.shape[1]), F32)
        state[...] = jnp.zeros(state.shape, F32)

    rows, cols, row_ids, same, carry, last, passing = chunk_masks(chunk, ends_ref, count)
    causal = rows >= cols
    visible = same & causal
    lag_mask = [None]
    for lag in range(1, K):
        earlier = rows - lag
        keep = (segment_of(earlier, ends_ref, count) == row_ids) & (earlier >= 0)
        lag_mask.append(keep.astype(F32))

    small = small_ref[...]
    for lo in range(0, inner, LANES):
        buf[8 : 8 + Q, lo : lo + LANES] = xr_ref[:, lo : lo + LANES].astype(F32)
    buf[8 : 8 + Q, inner : inner + 2 * STATE] = small[:, : 2 * STATE]

    def convolve(lo):
        span = slice(lo, lo + LANES)
        pre = taps_ref[K : K + 1, span] + taps_ref[K - 1 : K, span] * buf[8 : 8 + Q, span]
        for lag in range(1, K):
            pre = pre + taps_ref[K - 1 - lag : K - lag, span] * (
                buf[8 - lag : 8 - lag + Q, span] * lag_mask[lag]
            )
        pre_ref[:, span] = pre.astype(BF16)
        return pre * sigmoid(pre)

    b_f = convolve(inner).astype(BF16).astype(F32)
    c_b = convolve(inner + STATE).astype(BF16)
    b_b = b_f.astype(BF16)
    bc_ref[:, :STATE] = b_b
    bc_ref[:, STATE:] = c_b
    b_t = b_f.T.astype(BF16)

    _, step, decay_rate = decays(small[:, 2 * STATE :], par_ref)
    csum = mm_exact(causal.astype(F32), step * (-LOG2E * decay_rate))
    csum_t = csum.T
    scores = jnp.where(visible, mm(c_b, b_b, NT), 0.0)
    first = iota((Q, LANES), 1) < WIDTH
    first_row = iota((1, LANES), 1) < WIDTH

    for pair in range(heads // 2):
        span = slice(pair * LANES, (pair + 1) * LANES)
        xc = convolve(pair * LANES).astype(BF16)
        xc_ref[:, span] = xc
        xc = xc.astype(F32)
        left, right, both = pair_columns(csum, pair, first)
        _, _, step_pair = pair_columns(step, pair, first)
        mix = jnp.concatenate(
            [
                (scores * jnp.exp2(jnp.minimum(left - csum_t[2 * pair : 2 * pair + 1, :], 0.0))).astype(BF16),
                (scores * jnp.exp2(jnp.minimum(right - csum_t[2 * pair + 1 : 2 * pair + 2, :], 0.0))).astype(BF16),
            ],
            axis=1,
        )
        fed = xc * step_pair
        fed_b = fed.astype(BF16)
        zero = jnp.zeros((Q, LANES), BF16)
        stacked = jnp.concatenate([jnp.where(first, fed_b, zero), jnp.where(first, zero, fed_b)], axis=0)
        held = state[:, span]
        held_b = held.astype(BF16)
        st_ref[0, :, span] = held_b
        y = mm(mix, stacked) + mm(c_b, held_b) * (jnp.exp2(both) * carry)
        y_ref[:, span] = (y + skip_ref[:, span] * xc).astype(BF16)
        closing = both[Q - 1 : Q, :]
        weighted = (fed_b.astype(F32) * (jnp.exp2(closing - both) * last)).astype(BF16)
        state[:, span] = held * (jnp.exp2(closing) * passing) + mm(b_t, weighted)

    buf[0:8, :] = buf[Q : Q + 8, :]


def scan_backward(
    heads, chunks, ends_ref, dy_ref, xc_ref, pre_ref, xr_ref, small_ref, bc_ref, st_ref, taps_ref, par_ref,
    skip_ref, sel_ref, dx_ref, acc_ref, hacc_ref,
    dstate, dpre, ab_hi, ab_lo, v_b, u_b, dyd, fedw, dst_b, through,
):
    count = ends_ref.shape[0]
    inner = heads * WIDTH
    total_rows = chunks * Q
    chunk = chunks - 1 - pl.program_id(0)

    @pl.when(pl.program_id(0) == 0)
    def _():
        dpre[Q : Q + 8, :] = jnp.zeros((8, dpre.shape[1]), F32)
        dstate[...] = jnp.zeros(dstate.shape, F32)
        acc_ref[...] = jnp.zeros(acc_ref.shape, F32)
        hacc_ref[...] = jnp.zeros(hacc_ref.shape, F32)

    rows, cols, row_ids, same, carry, last, passing = chunk_masks(chunk, ends_ref, count)
    causal = rows >= cols
    visible = same & causal
    lag_mask = [None]
    for lag in range(1, K):
        later = rows + lag
        keep = (segment_of(later, ends_ref, count) == row_ids) & (later < total_rows)
        lag_mask.append(keep.astype(F32))

    small = small_ref[...]
    shifted, step, decay_rate = decays(small[:, 2 * STATE :], par_ref)
    csum = mm_exact(causal.astype(F32), step * (-LOG2E * decay_rate))
    csum_t = csum.T
    b_b = bc_ref[:, :STATE]
    c_b = bc_ref[:, STATE:]
    c_t = c_b.astype(F32).T.astype(BF16)
    scores = jnp.where(visible, mm(c_b, b_b, NT), 0.0)
    first = iota((Q, LANES), 1) < WIDTH

    def fold(values):
        return values.reshape(Q // 8, 8, values.shape[1]).sum(axis=0)

    def conv_back(lo, d_conv, raw):
        span = slice(lo, lo + LANES)
        pre = pre_ref[:, span].astype(F32)
        gate = sigmoid(pre)
        d_pre = d_conv * (gate * (1.0 + pre * (1.0 - gate)))
        dpre[0:Q, span] = d_pre
        d_raw = taps_ref[K - 1 : K, span] * d_pre
        acc_ref[8 * (K - 1) : 8 * K, span] += fold(d_pre * raw)
        acc_ref[8 * K : 8 * K + 8, span] += fold(d_pre)
        for lag in range(1, K):
            moved = dpre[lag : lag + Q, span] * lag_mask[lag]
            d_raw = d_raw + taps_ref[K - 1 - lag : K - lag, span] * moved
            acc_ref[8 * (K - 1 - lag) : 8 * (K - lag), span] += fold(moved * raw)
        dx_ref[:, span] = d_raw.astype(BF16)

    d_scores = jnp.zeros((Q, Q), F32)
    for pair in range(heads // 2):
        span = slice(pair * LANES, (pair + 1) * LANES)
        xc = xc_ref[:, span].astype(F32)
        dy_b = dy_ref[:, span]
        dy = dy_b.astype(F32)
        left, right, both = pair_columns(csum, pair, first)
        _, _, step_pair = pair_columns(step, pair, first)
        fall_left = jnp.exp2(jnp.minimum(left - csum_t[2 * pair : 2 * pair + 1, :], 0.0))
        fall_right = jnp.exp2(jnp.minimum(right - csum_t[2 * pair + 1 : 2 * pair + 2, :], 0.0))
        mix = jnp.concatenate([(scores * fall_left).astype(BF16), (scores * fall_right).astype(BF16)], axis=1)
        fed_b = (xc * step_pair).astype(BF16)
        fed = fed_b.astype(F32)
        zero = jnp.zeros((Q, LANES), BF16)
        stacked = jnp.concatenate([jnp.where(first, fed_b, zero), jnp.where(first, zero, fed_b)], axis=0)
        held_b = st_ref[0, :, span]
        grown = jnp.exp2(both) * carry
        y = mm(mix, stacked) + mm(c_b, held_b) * grown
        d_mix = mm(dy_b, stacked, NT)
        d_scores = d_scores + d_mix[:, :Q] * fall_left + d_mix[:, Q:] * fall_right
        d_fed2 = mm(mix, dy_b, TN)
        d_fed_in = jnp.where(first, d_fed2[:Q], d_fed2[Q:])
        closing = both[Q - 1 : Q, :]
        shrink = jnp.exp2(closing - both) * last
        d_held = dstate[:, span]
        d_held_b = d_held.astype(BF16)
        dst_b[:, span] = d_held_b
        d_fed_out = mm(b_b, d_held_b) * shrink
        d_fed = d_fed_in + d_fed_out
        straddle = dy * y - fed * d_fed_in
        hi = straddle.astype(BF16)
        ab_hi[:, span] = hi
        ab_lo[:, span] = (straddle - hi.astype(F32)).astype(BF16)
        v_b[:, span] = (fed * d_fed_out).astype(BF16)
        u_b[:, span] = (xc * d_fed).astype(BF16)
        fedw[:, span] = (fed * shrink).astype(BF16)
        dy_grown = (dy * grown).astype(BF16)
        dyd[:, span] = dy_grown
        kept = jnp.exp2(closing) * passing
        through[:, span] = (d_held * held_b.astype(F32)).reshape(STATE // 8, 8, LANES).sum(axis=0) * kept
        dstate[:, span] = d_held * kept + mm(c_t, dy_grown)
        acc_ref[8 * K + 8 : 8 * K + 16, span] += fold(dy * xc)
        d_conv = d_fed * step_pair + skip_ref[:, span] * dy
        conv_back(pair * LANES, d_conv, xr_ref[:, span].astype(F32))

    d_scores_b = jnp.where(visible, d_scores, 0.0).astype(BF16)
    d_c = mm(dyd[...], st_ref[0], NT) + mm(d_scores_b, b_b)
    d_b = mm(fedw[...], dst_b[...], NT) + mm(d_scores_b, c_b, TN)
    conv_back(inner, d_b, small[:, :STATE])
    conv_back(inner + STATE, d_c, small[:, STATE : 2 * STATE])

    sel = sel_ref[...]
    red_ab = mm(ab_hi[...], sel) + mm(ab_lo[...], sel)
    red_v = mm(v_b[...], sel)
    red_u = mm(u_b[...], sel)
    thr = through[...]
    thr_hi = thr.astype(BF16)
    red_t = mm(thr_hi, sel) + mm((thr - thr_hi.astype(F32)).astype(BF16), sel)
    red_t = jnp.sum(red_t, axis=0, keepdims=True)
    d_rate = (
        mm_exact((same & (cols >= rows)).astype(F32), red_ab)
        + mm_exact((same & (cols < rows)).astype(F32), red_v)
        + red_t
    )
    d_step = red_u - d_rate * decay_rate
    d_dt = d_step * sigmoid(shifted)
    dx_ref[:, inner + 2 * STATE :] = d_dt.astype(BF16)
    hacc_ref[0:8, :] += fold(d_dt)
    hacc_ref[8:16, :] += fold(d_rate * (-decay_rate * step))
    dpre[Q : Q + 8, :] = dpre[0:8, :]


def gate_forward(normed_ref, w_ref, y_ref, gain_ref, z_ref, gg_ref, sq_ref):
    width = w_ref.shape[1]
    tile = 256
    rows = normed_ref[...]
    square = jnp.zeros((rows.shape[0], LANES), F32)
    for lo in range(0, width, tile):
        span = slice(lo, lo + tile)
        z = mm(rows, w_ref[:, span])
        z_b = z.astype(BF16)
        z_ref[:, span] = z_b
        z = z_b.astype(F32)
        gated = y_ref[:, span].astype(F32) * (z * sigmoid(z))
        gg_ref[:, span] = (gated * gain_ref[:, span]).astype(BF16)
        twice = gated * gated
        for part in range(0, tile, LANES):
            square = square + twice[:, part : part + LANES]
    sq_ref[...] = square


def out_pair(gg_ref, cot_ref, live_ref, w_ref, u_ref, ds_ref, prod_ref):
    width = w_ref.shape[0]
    tile = 256
    gg = gg_ref[...]
    cot = cot_ref[...]
    live = live_ref[...]
    product = jnp.zeros((gg.shape[0], LANES), F32)
    for lo in range(0, width, tile):
        span = slice(lo, lo + tile)
        u = mm(gg, w_ref[span, :], NT)
        u_ref[:, span] = u.astype(BF16)
        term = u * cot[:, span].astype(F32)
        for part in range(0, tile, LANES):
            product = product + term[:, part : part + LANES]
        wide = jnp.concatenate([live] * (tile // LANES), axis=1)
        ds_ref[:, span] = (mm(cot, w_ref[:, span]) * wide).astype(BF16)
    prod_ref[...] = product * live


def gate_backward(ds_ref, y_ref, z_ref, rg_ref, coef_ref, gain_ref, dy_ref, dz_ref, acc_ref):
    @pl.when(pl.program_id(0) == 0)
    def _():
        acc_ref[...] = jnp.zeros(acc_ref.shape, F32)

    rg = rg_ref[...]
    coef = coef_ref[...]
    count = rg.shape[0]
    for lo in range(0, ds_ref.shape[1], LANES):
        span = slice(lo, lo + LANES)
        z = z_ref[:, span].astype(F32)
        y = y_ref[:, span].astype(F32)
        gate = sigmoid(z)
        silu = z * gate
        gated = y * silu
        d_normal = ds_ref[:, span].astype(F32) * rg
        acc_ref[:, span] += (d_normal * gated).reshape(count // 8, 8, LANES).sum(axis=0)
        d_gated = d_normal * gain_ref[:, span] - gated * coef
        dy_ref[:, span] = (d_gated * silu).astype(BF16)
        dz_ref[:, span] = (d_gated * y * (gate + silu * (1.0 - gate))).astype(BF16)


def normed_back(dz_ref, dx_ref, wz_ref, wx_ref, normed_ref, out_ref, acc_ref):
    @pl.when(pl.program_id(0) == 0)
    def _():
        acc_ref[...] = jnp.zeros(acc_ref.shape, F32)

    dz = dz_ref[...]
    dx = dx_ref[...]
    tile = 256
    count = dz.shape[0]
    for lo in range(0, wz_ref.shape[0], tile):
        span = slice(lo, lo + tile)
        d_normed = mm(dz, wz_ref[span, :], NT) + mm(dx, wx_ref[span, :], NT)
        out_ref[:, span] = d_normed.astype(BF16)
        term = d_normed * normed_ref[:, span].astype(F32)
        acc_ref[:, span] += term.reshape(count // 8, 8, tile).sum(axis=0)


def params():
    return pltpu.CompilerParams(dimension_semantics=("arbitrary",), vmem_limit_bytes=VMEM_LIMIT)


def rows_spec(block, width, column=0):
    return pl.BlockSpec((block, width), lambda i: (i, column))


def whole_spec(shape, column=0):
    return pl.BlockSpec(shape, lambda i: (0, column))


def local(
    tokens,
    cotangent,
    lengths,
    norm_gain,
    w_zx,
    w_bc,
    w_dt,
    conv_x,
    conv_x_bias,
    conv_bc,
    conv_bc_bias,
    dt_bias,
    a_log,
    d_skip,
    gate_gain,
    w_out,
):
    n_t = lax.axis_size("tensor")
    n_dp = lax.axis_size("dp")
    me_t = lax.axis_index("tensor")
    me_dp = lax.axis_index("dp")
    own_rows, depth = tokens.shape
    group = own_rows * n_t
    chunks = group // Q
    heads = dt_bias.shape[0]
    inner = heads * WIDTH
    inner_total = inner * n_t
    shard = w_zx.shape[1]
    pairs = [(i, n_t - 1 - i) for i in range(n_t)]

    def swap(v):
        return lax.ppermute(v, "tensor", pairs)

    def in_order(mine, other, axis=0):
        low = jnp.where(me_t == 0, mine, other)
        high = jnp.where(me_t == 0, other, mine)
        return jnp.concatenate([low, high], axis=axis)

    def sum_dp(v):
        step = 1
        while step < n_dp:
            v = v + lax.ppermute(v, "dp", [(i, i ^ step) for i in range(n_dp)])
            step *= 2
        return v

    ends = jnp.cumsum(lengths[0]).astype(jnp.int32)
    places = lax.iota(jnp.int32, group)
    ids = jnp.sum((places[:, None] >= ends[None, :]).astype(jnp.int32), axis=1)
    live = (ids < lengths.shape[1]).astype(F32)
    live_own = lax.dynamic_slice_in_dim(live, me_t * own_rows, own_rows, 0)

    other_tokens = swap(tokens)
    other_bc = swap(w_bc)
    bc_pair = in_order(w_bc, other_bc, axis=1)
    pad = jnp.zeros((shard, LANES - heads), BF16)
    packed = jnp.concatenate([w_zx[1], bc_pair[0], bc_pair[1], w_dt, pad], axis=1)
    wx_all = lax.all_gather(packed, "dp", axis=0, tiled=True)
    pieces = [conv_x, conv_x_bias, gate_gain, conv_bc, conv_bc_bias, norm_gain]
    flat = jnp.concatenate([piece.reshape(-1) for piece in pieces])
    used = flat.shape[0]
    full = -(-used // 1024) * 1024
    flat = jnp.concatenate([flat, jnp.zeros((full - used,), BF16)])
    little = lax.all_gather(flat[None], ("dp", "tensor"), axis=0, tiled=True).reshape(n_dp, n_t, full)
    zo_all = lax.all_gather(jnp.concatenate([w_zx[0], w_out.T], axis=1), "dp", axis=0, tiled=True)
    other_cot = swap(cotangent)

    mine = lax.dynamic_index_in_dim(little, me_t, axis=1, keepdims=False)
    cuts, at = [], 0
    for piece in pieces:
        cuts.append((at, at + piece.size))
        at += piece.size
    span_p = conv_x_bias.shape[1]
    span_n = conv_bc_bias.shape[1]
    taps_x = mine[:, slice(*cuts[0])].reshape(n_dp, heads, span_p, K).transpose(3, 1, 0, 2).reshape(K, inner)
    bias_x = mine[:, slice(*cuts[1])].reshape(n_dp, heads, span_p).transpose(1, 0, 2).reshape(1, inner)
    gain_out = mine[:, slice(*cuts[2])].reshape(n_dp, heads, span_p).transpose(1, 0, 2).reshape(1, inner).astype(F32)
    taps_bc = (
        little[:, :, slice(*cuts[3])].reshape(n_dp, n_t, 2, span_n, K).transpose(4, 2, 0, 1, 3).reshape(K, 2 * STATE)
    )
    bias_bc = little[:, :, slice(*cuts[4])].reshape(n_dp, n_t, 2, span_n).transpose(2, 0, 1, 3).reshape(1, 2 * STATE)
    gain_in = little[:, :, slice(*cuts[5])].reshape(1, depth).astype(F32)
    taps = jnp.concatenate(
        [
            jnp.concatenate([taps_x, taps_bc], axis=1),
            jnp.concatenate([bias_x, bias_bc], axis=1),
            jnp.zeros((8 - K - 1, inner + 2 * STATE), BF16),
        ],
        axis=0,
    ).astype(F32)
    par = jnp.concatenate([dt_bias[None], a_log[None], jnp.zeros((6, heads), F32)], axis=0)
    par = jnp.concatenate([par, jnp.zeros((8, LANES - heads), F32)], axis=1)
    skip = jnp.repeat(d_skip, WIDTH)[None]
    sel = (lax.iota(jnp.int32, inner)[:, None] // WIDTH == lax.iota(jnp.int32, LANES)[None, :]).astype(BF16)

    tok_all = in_order(tokens, other_tokens)
    tok_f = tok_all.astype(F32)
    inv_in = lax.rsqrt(jnp.mean(tok_f * tok_f, axis=1, keepdims=True) + EPSILON)
    normed = (tok_f * inv_in * gain_in).astype(BF16)
    cot_all = in_order(cotangent, other_cot)

    x_raw = lax.dot_general(normed, wx_all[:, :inner], NN, preferred_element_type=F32).astype(BF16)
    small = lax.dot_general(normed, wx_all[:, inner:], NN, preferred_element_type=F32)
    n_small = 2 * STATE + LANES
    n_conv = inner + 2 * STATE
    smem = pl.BlockSpec(memory_space=pltpu.SMEM)
    xc, pre, bc, y_all, states = pl.pallas_call(
        partial(scan_forward, heads),
        grid=(chunks,),
        in_specs=[
            smem,
            rows_spec(Q, inner),
            rows_spec(Q, n_small),
            whole_spec((8, n_conv)),
            whole_spec((8, LANES)),
            whole_spec((1, inner)),
        ],
        out_specs=[
            rows_spec(Q, inner),
            rows_spec(Q, n_conv),
            rows_spec(Q, 2 * STATE),
            rows_spec(Q, inner),
            pl.BlockSpec((1, STATE, inner), lambda i: (i, 0, 0)),
        ],
        out_shape=[
            jax.ShapeDtypeStruct((group, inner), BF16),
            jax.ShapeDtypeStruct((group, n_conv), BF16),
            jax.ShapeDtypeStruct((group, 2 * STATE), BF16),
            jax.ShapeDtypeStruct((group, inner), BF16),
            jax.ShapeDtypeStruct((chunks, STATE, inner), BF16),
        ],
        scratch_shapes=[pltpu.VMEM((Q + 8, n_conv), F32), pltpu.VMEM((STATE, inner), F32)],
        compiler_params=params(),
        name="scan_forward",
    )(ends, x_raw, small, taps, par, skip)

    block = 256
    steps = group // block
    z_all, gg, sq = pl.pallas_call(
        gate_forward,
        grid=(steps,),
        in_specs=[
            rows_spec(block, depth),
            whole_spec((depth, inner), 0),
            rows_spec(block, inner),
            whole_spec((1, inner)),
        ],
        out_specs=[rows_spec(block, inner), rows_spec(block, inner), rows_spec(block, LANES)],
        out_shape=[
            jax.ShapeDtypeStruct((group, inner), BF16),
            jax.ShapeDtypeStruct((group, inner), BF16),
            jax.ShapeDtypeStruct((group, LANES), F32),
        ],
        compiler_params=params(),
        name="gate_forward",
    )(normed, zo_all, y_all, gain_out)
    sq_part = jnp.sum(sq, axis=1)
    sq_all = sq_part + swap(sq_part)

    live_wide = jnp.broadcast_to(live[:, None], (group, LANES))
    u_part, d_scaled, prod = pl.pallas_call(
        out_pair,
        grid=(steps,),
        in_specs=[
            rows_spec(block, inner),
            rows_spec(block, depth),
            rows_spec(block, LANES),
            whole_spec((depth, inner), 1),
        ],
        out_specs=[rows_spec(block, depth), rows_spec(block, inner), rows_spec(block, LANES)],
        out_shape=[
            jax.ShapeDtypeStruct((group, depth), BF16),
            jax.ShapeDtypeStruct((group, inner), BF16),
            jax.ShapeDtypeStruct((group, LANES), F32),
        ],
        compiler_params=params(),
        name="out_pair",
    )(gg, cot_all, live_wide, zo_all)
    prod_part = jnp.sum(prod, axis=1)
    prod_all = prod_part + swap(prod_part)
    inv_gate = lax.rsqrt(sq_all / inner_total + EPSILON)

    u_own = lax.dynamic_slice_in_dim(u_part, me_t * own_rows, own_rows, 0)
    u_send = lax.dynamic_slice_in_dim(u_part, (n_t - 1 - me_t) * own_rows, own_rows, 0)
    u_recv = swap(u_send)
    inv_own = lax.dynamic_slice_in_dim(inv_gate, me_t * own_rows, own_rows, 0)
    branch = (u_own.astype(F32) + u_recv.astype(F32)) * (inv_own * live_own)[:, None]
    layer_out = (tokens.astype(F32) + branch).astype(BF16)

    d_branch = (cot_all.astype(F32) * (live * inv_gate)[:, None]).astype(BF16)
    g_out = lax.dot_general(d_branch, gg, TN, preferred_element_type=F32).astype(BF16)
    grad_out = lax.psum_scatter(g_out, "dp", scatter_dimension=0, tiled=True)

    coef = inv_gate * inv_gate * inv_gate * (prod_all / inner_total)
    rg_wide = jnp.broadcast_to(inv_gate[:, None], (group, LANES))
    coef_wide = jnp.broadcast_to(coef[:, None], (group, LANES))
    dy, dz, gain_acc = pl.pallas_call(
        gate_backward,
        grid=(steps,),
        in_specs=[
            rows_spec(block, inner),
            rows_spec(block, inner),
            rows_spec(block, inner),
            rows_spec(block, LANES),
            rows_spec(block, LANES),
            whole_spec((1, inner)),
        ],
        out_specs=[rows_spec(block, inner), rows_spec(block, inner), whole_spec((8, inner))],
        out_shape=[
            jax.ShapeDtypeStruct((group, inner), BF16),
            jax.ShapeDtypeStruct((group, inner), BF16),
            jax.ShapeDtypeStruct((8, inner), F32),
        ],
        compiler_params=params(),
        name="gate_backward",
    )(d_scaled, y_all, z_all, rg_wide, coef_wide, gain_out)
    g_z = lax.dot_general(normed, dz, TN, preferred_element_type=F32).astype(BF16)
    grad_z = lax.psum_scatter(g_z, "dp", scatter_dimension=0, tiled=True)

    back = lambda width: pl.BlockSpec((Q, width), lambda i: (chunks - 1 - i, 0))
    dx, acc, hacc = pl.pallas_call(
        partial(scan_backward, heads, chunks),
        grid=(chunks,),
        in_specs=[
            smem,
            back(inner),
            back(inner),
            back(n_conv),
            back(inner),
            back(n_small),
            back(2 * STATE),
            pl.BlockSpec((1, STATE, inner), lambda i: (chunks - 1 - i, 0, 0)),
            whole_spec((8, n_conv)),
            whole_spec((8, LANES)),
            whole_spec((1, inner)),
            whole_spec((inner, LANES)),
        ],
        out_specs=[back(inner + n_small), whole_spec((8 * (K + 2), n_conv)), whole_spec((16, LANES))],
        out_shape=[
            jax.ShapeDtypeStruct((group, inner + n_small), BF16),
            jax.ShapeDtypeStruct((8 * (K + 2), n_conv), F32),
            jax.ShapeDtypeStruct((16, LANES), F32),
        ],
        scratch_shapes=[
            pltpu.VMEM((STATE, inner), F32),
            pltpu.VMEM((Q + 8, n_conv), F32),
            pltpu.VMEM((Q, inner), BF16),
            pltpu.VMEM((Q, inner), BF16),
            pltpu.VMEM((Q, inner), BF16),
            pltpu.VMEM((Q, inner), BF16),
            pltpu.VMEM((Q, inner), BF16),
            pltpu.VMEM((Q, inner), BF16),
            pltpu.VMEM((STATE, inner), BF16),
            pltpu.VMEM((8, inner), F32),
        ],
        compiler_params=params(),
        name="scan_backward",
    )(ends, dy, xc, pre, x_raw, small, bc, states, taps, par, skip, sel)

    g_x = lax.dot_general(normed, dx, TN, preferred_element_type=F32).astype(BF16)
    grad_x = lax.psum_scatter(g_x, "dp", scatter_dimension=0, tiled=True)

    d_normed, in_acc = pl.pallas_call(
        normed_back,
        grid=(steps,),
        in_specs=[
            rows_spec(block, inner),
            rows_spec(block, inner + n_small),
            whole_spec((depth, inner), 0),
            whole_spec((depth, inner + n_small)),
            rows_spec(block, depth),
        ],
        out_specs=[rows_spec(block, depth), whole_spec((8, depth))],
        out_shape=[jax.ShapeDtypeStruct((group, depth), BF16), jax.ShapeDtypeStruct((8, depth), F32)],
        compiler_params=params(),
        name="normed_back",
    )(dz, dx, zo_all, wx_all, normed)
    dn_own = lax.dynamic_slice_in_dim(d_normed, me_t * own_rows, own_rows, 0)
    dn_send = lax.dynamic_slice_in_dim(d_normed, (n_t - 1 - me_t) * own_rows, own_rows, 0)
    dn = dn_own.astype(F32) + swap(dn_send).astype(F32)
    tok_own = tokens.astype(F32)
    inv_tok = lax.dynamic_slice_in_dim(inv_in, me_t * own_rows, own_rows, 0)
    spread = dn * gain_in
    grad_tokens = (
        cotangent.astype(F32)
        + inv_tok * spread
        - tok_own * inv_tok * inv_tok * inv_tok * jnp.mean(spread * tok_own, axis=1, keepdims=True)
    )

    acc = acc.reshape(K + 2, 8, n_conv).sum(axis=1)
    hsum = hacc.reshape(2, 8, LANES).sum(axis=1)
    d_gate = gain_acc.sum(axis=0)
    d_in = in_acc.sum(axis=0) / gain_in[0]
    d_sk = acc[K + 1, :inner].reshape(heads, WIDTH).sum(axis=1)
    shared = [acc[: K + 1, inner:].reshape(-1), d_in]
    headed = [acc[: K + 1, :inner].reshape(-1), d_gate, hsum[:, :heads].reshape(-1), d_sk]
    shared_size = sum(piece.size for piece in shared)
    vector = jnp.concatenate(shared + headed)
    size = vector.shape[0]
    vector = jnp.concatenate([vector, jnp.zeros((-size % 1024,), F32)]).reshape(-1, LANES)
    vector = sum_dp(vector)
    cut_rows = -(-shared_size // (8 * LANES)) * 8
    joint = (vector[:cut_rows] + swap(vector[:cut_rows])).reshape(-1)
    vector = vector.reshape(-1)

    n_bc = (K + 1) * 2 * STATE
    bc_sum = joint[:n_bc].reshape(K + 1, 2, STATE)
    me_all = me_dp * n_t + me_t
    bc_sum = lax.dynamic_slice_in_dim(bc_sum, me_all * span_n, span_n, 2)
    grad_bc_taps = bc_sum[:K].transpose(1, 2, 0).reshape(conv_bc.shape)
    grad_bc_bias = bc_sum[K]
    grad_in = lax.dynamic_slice_in_dim(joint[n_bc : n_bc + depth], me_all * norm_gain.shape[0], norm_gain.shape[0], 0)
    at = shared_size
    x_sum = vector[at : at + (K + 1) * inner].reshape(K + 1, heads, WIDTH)
    at += (K + 1) * inner
    x_sum = lax.dynamic_slice_in_dim(x_sum, me_dp * span_p, span_p, 2)
    grad_x_taps = x_sum[:K].transpose(1, 2, 0).reshape(conv_x.shape)
    grad_x_bias = x_sum[K]
    grad_gate = lax.dynamic_slice_in_dim(vector[at : at + inner].reshape(heads, WIDTH), me_dp * span_p, span_p, 1)
    at += inner
    grad_dt_bias = vector[at : at + heads]
    grad_a_log = vector[at + heads : at + 2 * heads]
    grad_skip = vector[at + 2 * heads : at + 3 * heads]

    grad_zx = jnp.stack([grad_z.astype(F32), grad_x[:, :inner].astype(F32)])
    grad_dt = grad_x[:, inner + 2 * STATE : inner + 2 * STATE + heads].astype(F32)
    bc_part = grad_x[:, inner : inner + 2 * STATE]
    half = w_bc.shape[1]
    bc_own = lax.dynamic_slice_in_dim(bc_part, me_t * half, half, 0)
    bc_send = lax.dynamic_slice_in_dim(bc_part, (n_t - 1 - me_t) * half, half, 0)
    bc_total = bc_own.astype(F32) + swap(bc_send).astype(F32)
    grad_bc = bc_total.reshape(half, 2, STATE).transpose(1, 0, 2)
    return (
        layer_out,
        grad_tokens,
        grad_in,
        grad_zx,
        grad_bc,
        grad_dt,
        grad_x_taps,
        grad_x_bias,
        grad_bc_taps,
        grad_bc_bias,
        grad_dt_bias,
        grad_a_log,
        grad_skip,
        grad_gate,
        grad_out.astype(F32).T,
    )


def solution(mesh):
    both = ("dp", "tensor")
    in_specs = (
        P(both, None),
        P(both, None),
        P("dp", None),
        P(both),
        P(None, "dp", "tensor"),
        P(None, both, None),
        P("dp", "tensor"),
        P("tensor", "dp"),
        P("tensor", "dp"),
        P(None, both),
        P(None, both),
        P("tensor"),
        P("tensor"),
        P("tensor"),
        P("tensor", "dp"),
        P("tensor", "dp"),
    )
    out_specs = (
        P(both, None),
        P(both, None),
        P(both),
        P(None, "dp", "tensor"),
        P(None, both, None),
        P("dp", "tensor"),
        P("tensor", "dp"),
        P("tensor", "dp"),
        P(None, both),
        P(None, both),
        P("tensor"),
        P("tensor"),
        P("tensor"),
        P("tensor", "dp"),
        P("tensor", "dp"),
    )
    return jax.shard_map(local, mesh=mesh, in_specs=in_specs, out_specs=out_specs, check_vma=False)
```

```python
from functools import partial

import jax
import jax.numpy as jnp
from jax import lax
from jax.experimental import pallas as pl
from jax.experimental.pallas import tpu as pltpu
from jax.sharding import PartitionSpec as P

EPSILON = 1e-05
HIGHEST = lax.Precision.HIGHEST
K = 4
WIDTH = 64
STATE = 128
Q = 128
LANES = 128
LOG2E = 1.4426950408889634
VMEM_LIMIT = 60 * 1024 * 1024
F32 = jnp.float32
BF16 = jnp.bfloat16

NN = (((1,), (0,)), ((), ()))
NT = (((1,), (1,)), ((), ()))
TN = (((0,), (0,)), ((), ()))


def mm(a, b, dims=NN):
    return lax.dot_general(a, b, dims, preferred_element_type=F32)


def mm_exact(a, b, dims=NN):
    return lax.dot_general(a, b, dims, preferred_element_type=F32, precision=HIGHEST)


def iota(shape, dim):
    return lax.broadcasted_iota(jnp.int32, shape, dim)


def segment_of(rows, ends_ref, count):
    total = (rows >= ends_ref[0]).astype(jnp.int32)
    for j in range(1, count):
        total = total + (rows >= ends_ref[j]).astype(jnp.int32)
    return total


def scalar_segment(row, ends_ref, count):
    total = jnp.where(row >= ends_ref[0], 1, 0)
    for j in range(1, count):
        total = total + jnp.where(row >= ends_ref[j], 1, 0)
    return total


def sigmoid(v):
    return 0.5 * jnp.tanh(0.5 * v) + 0.5


def softplus(v):
    return jnp.maximum(v, 0.0) + jnp.log1p(jnp.exp(-jnp.abs(v)))


def chunk_masks(chunk, ends_ref, count):
    base = chunk * Q
    rows = iota((Q, Q), 0) + base
    cols = iota((Q, Q), 1) + base
    row_ids = segment_of(rows, ends_ref, count)
    col_ids = segment_of(cols, ends_ref, count)
    same = row_ids == col_ids
    before_id = jnp.where(chunk == 0, -1, scalar_segment(base - 1, ends_ref, count))
    final_id = scalar_segment(base + Q - 1, ends_ref, count)
    carry = (row_ids == before_id).astype(F32)
    last = (row_ids == final_id).astype(F32)
    passing = jnp.where(before_id == final_id, 1.0, 0.0).astype(F32)
    return rows, cols, row_ids, same, carry, last, passing


def decays(dt_raw, par_ref):
    shifted = dt_raw + par_ref[0:1, :]
    step = softplus(shifted)
    decay_rate = jnp.exp(par_ref[1:2, :])
    return shifted, step, decay_rate


def pair_columns(values, pair, first):
    left = jnp.broadcast_to(values[:, 2 * pair : 2 * pair + 1], (Q, LANES))
    right = jnp.broadcast_to(values[:, 2 * pair + 1 : 2 * pair + 2], (Q, LANES))
    return left, right, jnp.where(first, left, right)


def scan_forward(
    heads, ends_ref, xr_ref, small_ref, taps_ref, par_ref, skip_ref,
    xc_ref, pre_ref, bc_ref, y_ref, st_ref, buf, state,
):
    count = ends_ref.shape[0]
    inner = heads * WIDTH
    chunk = pl.program_id(0)

    @pl.when(chunk == 0)
    def _():
        buf[0:8, :] = jnp.zeros((8, buf.shape[1]), F32)
        state[...] = jnp.zeros(state.shape, F32)

    rows, cols, row_ids, same, carry, last, passing = chunk_masks(chunk, ends_ref, count)
    causal = rows >= cols
    visible = same & causal
    lag_mask = [None]
    for lag in range(1, K):
        earlier = rows - lag
        keep = (segment_of(earlier, ends_ref, count) == row_ids) & (earlier >= 0)
        lag_mask.append(keep.astype(F32))

    small = small_ref[...]
    for lo in range(0, inner, LANES):
        buf[8 : 8 + Q, lo : lo + LANES] = xr_ref[:, lo : lo + LANES].astype(F32)
    buf[8 : 8 + Q, inner : inner + 2 * STATE] = small[:, : 2 * STATE]

    def convolve(lo):
        span = slice(lo, lo + LANES)
        pre = taps_ref[K : K + 1, span] + taps_ref[K - 1 : K, span] * buf[8 : 8 + Q, span]
        for lag in range(1, K):
            pre = pre + taps_ref[K - 1 - lag : K - lag, span] * (
                buf[8 - lag : 8 - lag + Q, span] * lag_mask[lag]
            )
        pre_ref[:, span] = pre.astype(BF16)
        return pre * sigmoid(pre)

    b_f = convolve(inner).astype(BF16).astype(F32)
    c_b = convolve(inner + STATE).astype(BF16)
    b_b = b_f.astype(BF16)
    bc_ref[:, :STATE] = b_b
    bc_ref[:, STATE:] = c_b
    b_t = b_f.T.astype(BF16)

    _, step, decay_rate = decays(small[:, 2 * STATE :], par_ref)
    csum = mm_exact(causal.astype(F32), step * (-LOG2E * decay_rate))
    csum_t = csum.T
    scores = jnp.where(visible, mm(c_b, b_b, NT), 0.0)
    first = iota((Q, LANES), 1) < WIDTH
    first_row = iota((1, LANES), 1) < WIDTH

    for pair in range(heads // 2):
        span = slice(pair * LANES, (pair + 1) * LANES)
        xc = convolve(pair * LANES).astype(BF16)
        xc_ref[:, span] = xc
        xc = xc.astype(F32)
        left, right, both = pair_columns(csum, pair, first)
        _, _, step_pair = pair_columns(step, pair, first)
        mix = jnp.concatenate(
            [
                (scores * jnp.exp2(jnp.minimum(left - csum_t[2 * pair : 2 * pair + 1, :], 0.0))).astype(BF16),
                (scores * jnp.exp2(jnp.minimum(right - csum_t[2 * pair + 1 : 2 * pair + 2, :], 0.0))).astype(BF16),
            ],
            axis=1,
        )
        fed = xc * step_pair
        fed_b = fed.astype(BF16)
        zero = jnp.zeros((Q, LANES), BF16)
        stacked = jnp.concatenate([jnp.where(first, fed_b, zero), jnp.where(first, zero, fed_b)], axis=0)
        held = state[:, span]
        held_b = held.astype(BF16)
        st_ref[0, :, span] = held_b
        y = mm(mix, stacked) + mm(c_b, held_b) * (jnp.exp2(both) * carry)
        y_ref[:, span] = (y + skip_ref[:, span] * xc).astype(BF16)
        closing = both[Q - 1 : Q, :]
        weighted = (fed_b.astype(F32) * (jnp.exp2(closing - both) * last)).astype(BF16)
        state[:, span] = held * (jnp.exp2(closing) * passing) + mm(b_t, weighted)

    buf[0:8, :] = buf[Q : Q + 8, :]


def scan_backward(
    heads, chunks, ends_ref, dy_ref, xc_ref, pre_ref, xr_ref, small_ref, bc_ref, st_ref, taps_ref, par_ref,
    skip_ref, sel_ref, dx_ref, acc_ref, hacc_ref,
    dstate, dpre, ab_hi, ab_lo, v_b, u_b, dyd, fedw, dst_b, through,
):
    count = ends_ref.shape[0]
    inner = heads * WIDTH
    total_rows = chunks * Q
    chunk = chunks - 1 - pl.program_id(0)

    @pl.when(pl.program_id(0) == 0)
    def _():
        dpre[Q : Q + 8, :] = jnp.zeros((8, dpre.shape[1]), F32)
        dstate[...] = jnp.zeros(dstate.shape, F32)
        acc_ref[...] = jnp.zeros(acc_ref.shape, F32)
        hacc_ref[...] = jnp.zeros(hacc_ref.shape, F32)

    rows, cols, row_ids, same, carry, last, passing = chunk_masks(chunk, ends_ref, count)
    causal = rows >= cols
    visible = same & causal
    lag_mask = [None]
    for lag in range(1, K):
        later = rows + lag
        keep = (segment_of(later, ends_ref, count) == row_ids) & (later < total_rows)
        lag_mask.append(keep.astype(F32))

    small = small_ref[...]
    shifted, step, decay_rate = decays(small[:, 2 * STATE :], par_ref)
    csum = mm_exact(causal.astype(F32), step * (-LOG2E * decay_rate))
    csum_t = csum.T
    b_b = bc_ref[:, :STATE]
    c_b = bc_ref[:, STATE:]
    c_t = c_b.astype(F32).T.astype(BF16)
    scores = jnp.where(visible, mm(c_b, b_b, NT), 0.0)
    first = iota((Q, LANES), 1) < WIDTH

    def fold(values):
        return values.reshape(Q // 8, 8, values.shape[1]).sum(axis=0)

    def conv_back(lo, d_conv, raw):
        span = slice(lo, lo + LANES)
        pre = pre_ref[:, span].astype(F32)
        gate = sigmoid(pre)
        d_pre = d_conv * (gate * (1.0 + pre * (1.0 - gate)))
        dpre[0:Q, span] = d_pre
        d_raw = taps_ref[K - 1 : K, span] * d_pre
        acc_ref[8 * (K - 1) : 8 * K, span] += fold(d_pre * raw)
        acc_ref[8 * K : 8 * K + 8, span] += fold(d_pre)
        for lag in range(1, K):
            moved = dpre[lag : lag + Q, span] * lag_mask[lag]
            d_raw = d_raw + taps_ref[K - 1 - lag : K - lag, span] * moved
            acc_ref[8 * (K - 1 - lag) : 8 * (K - lag), span] += fold(moved * raw)
        dx_ref[:, span] = d_raw.astype(BF16)

    d_scores = jnp.zeros((Q, Q), F32)
    for pair in range(heads // 2):
        span = slice(pair * LANES, (pair + 1) * LANES)
        xc = xc_ref[:, span].astype(F32)
        dy_b = dy_ref[:, span]
        dy = dy_b.astype(F32)
        left, right, both = pair_columns(csum, pair, first)
        _, _, step_pair = pair_columns(step, pair, first)
        fall_left = jnp.exp2(jnp.minimum(left - csum_t[2 * pair : 2 * pair + 1, :], 0.0))
        fall_right = jnp.exp2(jnp.minimum(right - csum_t[2 * pair + 1 : 2 * pair + 2, :], 0.0))
        mix = jnp.concatenate([(scores * fall_left).astype(BF16), (scores * fall_right).astype(BF16)], axis=1)
        fed_b = (xc * step_pair).astype(BF16)
        fed = fed_b.astype(F32)
        zero = jnp.zeros((Q, LANES), BF16)
        stacked = jnp.concatenate([jnp.where(first, fed_b, zero), jnp.where(first, zero, fed_b)], axis=0)
        held_b = st_ref[0, :, span]
        grown = jnp.exp2(both) * carry
        y = mm(mix, stacked) + mm(c_b, held_b) * grown
        d_mix = mm(dy_b, stacked, NT)
        d_scores = d_scores + d_mix[:, :Q] * fall_left + d_mix[:, Q:] * fall_right
        d_fed2 = mm(mix, dy_b, TN)
        d_fed_in = jnp.where(first, d_fed2[:Q], d_fed2[Q:])
        closing = both[Q - 1 : Q, :]
        shrink = jnp.exp2(closing - both) * last
        d_held = dstate[:, span]
        d_held_b = d_held.astype(BF16)
        dst_b[:, span] = d_held_b
        d_fed_out = mm(b_b, d_held_b) * shrink
        d_fed = d_fed_in + d_fed_out
        straddle = dy * y - fed * d_fed_in
        hi = straddle.astype(BF16)
        ab_hi[:, span] = hi
        ab_lo[:, span] = (straddle - hi.astype(F32)).astype(BF16)
        v_b[:, span] = (fed * d_fed_out).astype(BF16)
        u_b[:, span] = (xc * d_fed).astype(BF16)
        fedw[:, span] = (fed * shrink).astype(BF16)
        dy_grown = (dy * grown).astype(BF16)
        dyd[:, span] = dy_grown
        kept = jnp.exp2(closing) * passing
        through[:, span] = (d_held * held_b.astype(F32)).reshape(STATE // 8, 8, LANES).sum(axis=0) * kept
        dstate[:, span] = d_held * kept + mm(c_t, dy_grown)
        acc_ref[8 * K + 8 : 8 * K + 16, span] += fold(dy * xc)
        d_conv = d_fed * step_pair + skip_ref[:, span] * dy
        conv_back(pair * LANES, d_conv, xr_ref[:, span].astype(F32))

    d_scores_b = jnp.where(visible, d_scores, 0.0).astype(BF16)
    d_c = mm(dyd[...], st_ref[0], NT) + mm(d_scores_b, b_b)
    d_b = mm(fedw[...], dst_b[...], NT) + mm(d_scores_b, c_b, TN)
    conv_back(inner, d_b, small[:, :STATE])
    conv_back(inner + STATE, d_c, small[:, STATE : 2 * STATE])

    sel = sel_ref[...]
    red_ab = mm(ab_hi[...], sel) + mm(ab_lo[...], sel)
    red_v = mm(v_b[...], sel)
    red_u = mm(u_b[...], sel)
    thr = through[...]
    thr_hi = thr.astype(BF16)
    red_t = mm(thr_hi, sel) + mm((thr - thr_hi.astype(F32)).astype(BF16), sel)
    red_t = jnp.sum(red_t, axis=0, keepdims=True)
    d_rate = (
        mm_exact((same & (cols >= rows)).astype(F32), red_ab)
        + mm_exact((same & (cols < rows)).astype(F32), red_v)
        + red_t
    )
    d_step = red_u - d_rate * decay_rate
    d_dt = d_step * sigmoid(shifted)
    dx_ref[:, inner + 2 * STATE :] = d_dt.astype(BF16)
    hacc_ref[0:8, :] += fold(d_dt)
    hacc_ref[8:16, :] += fold(d_rate * (-decay_rate * step))
    dpre[Q : Q + 8, :] = dpre[0:8, :]


def load_blocks(offsets_ref, blocks, whole, sems):
    @pl.when(pl.program_id(0) == 0)
    def _():
        copies = []
        for k, block in enumerate(blocks):
            size = block.shape[0]
            start = pl.multiple_of(offsets_ref[k], 32) if len(blocks) > 1 else 0
            copies.append(pltpu.make_async_copy(block, whole.at[pl.ds(start, size), :], sems.at[k]))
        for copy in copies:
            copy.start()
        for copy in copies:
            copy.wait()


def project(count, offsets_ref, normed_ref, *refs):
    blocks, (x_ref, small_ref, w_ref, sems) = refs[:count], refs[count:]
    load_blocks(offsets_ref, blocks, w_ref, sems)
    inner = x_ref.shape[1]
    tile = 256
    rows = normed_ref[...]
    for lo in range(0, inner, tile):
        x_ref[:, lo : lo + tile] = mm(rows, w_ref[:, lo : lo + tile]).astype(BF16)
    small_ref[...] = mm(rows, w_ref[:, inner:])


def gate_forward(count, offsets_ref, normed_ref, y_ref, gain_ref, *refs):
    blocks, (z_ref, gg_ref, sq_ref, w_ref, sems) = refs[:count], refs[count:]
    load_blocks(offsets_ref, blocks, w_ref, sems)
    width = w_ref.shape[1]
    tile = 256
    rows = normed_ref[...]
    square = jnp.zeros((rows.shape[0], LANES), F32)
    for lo in range(0, width, tile):
        span = slice(lo, lo + tile)
        z = mm(rows, w_ref[:, span])
        z_b = z.astype(BF16)
        z_ref[:, span] = z_b
        z = z_b.astype(F32)
        gated = y_ref[:, span].astype(F32) * (z * sigmoid(z))
        gg_ref[:, span] = (gated * gain_ref[:, span]).astype(BF16)
        twice = gated * gated
        for part in range(0, tile, LANES):
            square = square + twice[:, part : part + LANES]
    sq_ref[...] = square


def out_pair(count, offsets_ref, gg_ref, cot_ref, live_ref, *refs):
    blocks, (u_ref, ds_ref, prod_ref, w_ref, sems) = refs[:count], refs[count:]
    load_blocks(offsets_ref, blocks, w_ref, sems)
    width = w_ref.shape[0]
    tile = 256
    gg = gg_ref[...]
    cot = cot_ref[...]
    live = live_ref[...]
    product = jnp.zeros((gg.shape[0], LANES), F32)
    for lo in range(0, width, tile):
        span = slice(lo, lo + tile)
        u = mm(gg, w_ref[span, :], NT)
        u_ref[:, span] = u.astype(BF16)
        term = u * cot[:, span].astype(F32)
        for part in range(0, tile, LANES):
            product = product + term[:, part : part + LANES]
        wide = jnp.concatenate([live] * (tile // LANES), axis=1)
        ds_ref[:, span] = (mm(cot, w_ref[:, span]) * wide).astype(BF16)
    prod_ref[...] = product * live


def gate_backward(ds_ref, y_ref, z_ref, rg_ref, coef_ref, gain_ref, dy_ref, dz_ref, acc_ref):
    @pl.when(pl.program_id(0) == 0)
    def _():
        acc_ref[...] = jnp.zeros(acc_ref.shape, F32)

    rg = rg_ref[...]
    coef = coef_ref[...]
    count = rg.shape[0]
    for lo in range(0, ds_ref.shape[1], LANES):
        span = slice(lo, lo + LANES)
        z = z_ref[:, span].astype(F32)
        y = y_ref[:, span].astype(F32)
        gate = sigmoid(z)
        silu = z * gate
        gated = y * silu
        d_normal = ds_ref[:, span].astype(F32) * rg
        acc_ref[:, span] += (d_normal * gated).reshape(count // 8, 8, LANES).sum(axis=0)
        d_gated = d_normal * gain_ref[:, span] - gated * coef
        dy_ref[:, span] = (d_gated * silu).astype(BF16)
        dz_ref[:, span] = (d_gated * y * (gate + silu * (1.0 - gate))).astype(BF16)


def normed_back(count, offsets_ref, dz_ref, dx_ref, normed_ref, *refs):
    z_blocks, x_blocks = refs[:count], refs[count : 2 * count]
    out_ref, acc_ref, wz_ref, wx_ref, z_sems, x_sems = refs[2 * count :]
    load_blocks(offsets_ref, z_blocks, wz_ref, z_sems)
    load_blocks(offsets_ref, x_blocks, wx_ref, x_sems)

    @pl.when(pl.program_id(0) == 0)
    def _():
        acc_ref[...] = jnp.zeros(acc_ref.shape, F32)

    dz = dz_ref[...]
    dx = dx_ref[...]
    tile = 256
    count = dz.shape[0]
    for lo in range(0, wz_ref.shape[0], tile):
        span = slice(lo, lo + tile)
        d_normed = mm(dz, wz_ref[span, :], NT) + mm(dx, wx_ref[span, :], NT)
        out_ref[:, span] = d_normed.astype(BF16)
        term = d_normed * normed_ref[:, span].astype(F32)
        acc_ref[:, span] += term.reshape(count // 8, 8, tile).sum(axis=0)


def params():
    return pltpu.CompilerParams(dimension_semantics=("arbitrary",), vmem_limit_bytes=VMEM_LIMIT)


def rows_spec(block, width, column=0):
    return pl.BlockSpec((block, width), lambda i: (i, column))


def whole_spec(shape, column=0):
    return pl.BlockSpec(shape, lambda i: (0, column))


def local(
    tokens,
    cotangent,
    lengths,
    norm_gain,
    w_zx,
    w_bc,
    w_dt,
    conv_x,
    conv_x_bias,
    conv_bc,
    conv_bc_bias,
    dt_bias,
    a_log,
    d_skip,
    gate_gain,
    w_out,
):
    n_t = lax.axis_size("tensor")
    n_dp = lax.axis_size("dp")
    me_t = lax.axis_index("tensor")
    me_dp = lax.axis_index("dp")
    own_rows, depth = tokens.shape
    group = own_rows * n_t
    chunks = group // Q
    heads = dt_bias.shape[0]
    inner = heads * WIDTH
    inner_total = inner * n_t
    shard = w_zx.shape[1]
    pairs = [(i, n_t - 1 - i) for i in range(n_t)]

    def swap(v):
        return lax.ppermute(v, "tensor", pairs)

    def in_order(mine, other, axis=0):
        low = jnp.where(me_t == 0, mine, other)
        high = jnp.where(me_t == 0, other, mine)
        return jnp.concatenate([low, high], axis=axis)

    def sum_dp(v):
        step = 1
        while step < n_dp:
            v = v + lax.ppermute(v, "dp", [(i, i ^ step) for i in range(n_dp)])
            step *= 2
        return v

    def after(value, *others):
        return lax.optimization_barrier((value, *others))[0]

    ring = 4
    plane = n_dp // (2 * ring)

    def gather_blocks(v):
        if plane != 2 or v.shape[0] % 32:
            return [lax.all_gather(v, "dp", axis=0, tiled=True)], v
        around = [(i, (i + 2 * plane) % n_dp) for i in range(n_dp)]
        across = [(i, i ^ 2) for i in range(n_dp)]
        beside = [(i, i ^ 1) for i in range(n_dp)]
        line = [v]
        for _ in range(ring - 1):
            line.append(lax.ppermute(line[-1], "dp", around))
        face = line + [lax.ppermute(block, "dp", across) for block in line]
        return face + [lax.ppermute(block, "dp", beside) for block in face], line[2]

    def block_offsets(count, size):
        if count == 1:
            return jnp.zeros((1,), jnp.int32)
        places = []
        for core in range(2):
            for side in range(2):
                for turn in range(ring):
                    level = (me_dp // (2 * plane) - turn + ring) % ring
                    places.append(level * (2 * plane) + ((me_dp % (2 * plane)) ^ (2 * side + core)))
        return jnp.stack(places).astype(jnp.int32) * size

    def gather_little(v):
        step = 1
        while step < n_dp:
            other = lax.ppermute(v, "dp", [(i, i ^ step) for i in range(n_dp)])
            upper = (me_dp // step) % 2 == 1
            v = jnp.concatenate([jnp.where(upper, other, v), jnp.where(upper, v, other)], axis=0)
            step *= 2
        other = swap(v)
        return jnp.stack([jnp.where(me_t == 0, v, other), jnp.where(me_t == 0, other, v)], axis=1)

    ends = jnp.cumsum(lengths[0]).astype(jnp.int32)
    places = lax.iota(jnp.int32, group)
    ids = jnp.sum((places[:, None] >= ends[None, :]).astype(jnp.int32), axis=1)
    live = (ids < lengths.shape[1]).astype(F32)
    live_own = lax.dynamic_slice_in_dim(live, me_t * own_rows, own_rows, 0)

    other_bc = swap(w_bc)
    other_tokens = swap(tokens)
    bc_pair = in_order(w_bc, other_bc, axis=1)
    pad = jnp.zeros((shard, LANES - heads), BF16)
    packed = jnp.concatenate([w_zx[1], bc_pair[0], bc_pair[1], w_dt, pad], axis=1)
    wx_blocks, wx_late = gather_blocks(packed)
    pieces = [conv_x, conv_x_bias, gate_gain, conv_bc, conv_bc_bias, norm_gain]
    flat = jnp.concatenate([piece.reshape(-1) for piece in pieces])
    used = flat.shape[0]
    full = -(-used // 1024) * 1024
    flat = jnp.concatenate([flat, jnp.zeros((full - used,), BF16)])
    little = gather_little(flat.reshape(1, full // LANES, LANES)).reshape(n_dp, n_t, full)
    wz_blocks, wz_late = gather_blocks(after(w_zx[0], wx_late))
    wo_blocks, _ = gather_blocks(after(w_out.T, wz_late))
    other_cot = swap(after(cotangent, other_tokens))
    count = len(wx_blocks)
    offsets = block_offsets(count, shard)
    hbm = pl.BlockSpec(memory_space=pl.ANY)
    sems = pltpu.SemaphoreType.DMA((count,))

    mine = lax.dynamic_index_in_dim(little, me_t, axis=1, keepdims=False)
    cuts, at = [], 0
    for piece in pieces:
        cuts.append((at, at + piece.size))
        at += piece.size
    span_p = conv_x_bias.shape[1]
    span_n = conv_bc_bias.shape[1]
    taps_x = mine[:, slice(*cuts[0])].reshape(n_dp, heads, span_p, K).transpose(3, 1, 0, 2).reshape(K, inner)
    bias_x = mine[:, slice(*cuts[1])].reshape(n_dp, heads, span_p).transpose(1, 0, 2).reshape(1, inner)
    gain_out = mine[:, slice(*cuts[2])].reshape(n_dp, heads, span_p).transpose(1, 0, 2).reshape(1, inner).astype(F32)
    taps_bc = (
        little[:, :, slice(*cuts[3])].reshape(n_dp, n_t, 2, span_n, K).transpose(4, 2, 0, 1, 3).reshape(K, 2 * STATE)
    )
    bias_bc = little[:, :, slice(*cuts[4])].reshape(n_dp, n_t, 2, span_n).transpose(2, 0, 1, 3).reshape(1, 2 * STATE)
    gain_in = little[:, :, slice(*cuts[5])].reshape(1, depth).astype(F32)
    taps = jnp.concatenate(
        [
            jnp.concatenate([taps_x, taps_bc], axis=1),
            jnp.concatenate([bias_x, bias_bc], axis=1),
            jnp.zeros((8 - K - 1, inner + 2 * STATE), BF16),
        ],
        axis=0,
    ).astype(F32)
    par = jnp.concatenate([dt_bias[None], a_log[None], jnp.zeros((6, heads), F32)], axis=0)
    par = jnp.concatenate([par, jnp.zeros((8, LANES - heads), F32)], axis=1)
    skip = jnp.repeat(d_skip, WIDTH)[None]
    sel = (lax.iota(jnp.int32, inner)[:, None] // WIDTH == lax.iota(jnp.int32, LANES)[None, :]).astype(BF16)

    tok_all = in_order(tokens, other_tokens)
    tok_f = tok_all.astype(F32)
    inv_in = lax.rsqrt(jnp.mean(tok_f * tok_f, axis=1, keepdims=True) + EPSILON)
    normed = (tok_f * inv_in * gain_in).astype(BF16)
    cot_all = in_order(cotangent, other_cot)

    n_small = 2 * STATE + LANES
    n_conv = inner + 2 * STATE
    smem = pl.BlockSpec(memory_space=pltpu.SMEM)
    block = 512
    steps = group // block
    x_raw, small = pl.pallas_call(
        partial(project, count),
        grid=(steps,),
        in_specs=[smem, rows_spec(block, depth)] + [hbm] * count,
        out_specs=[rows_spec(block, inner), rows_spec(block, n_small)],
        out_shape=[
            jax.ShapeDtypeStruct((group, inner), BF16),
            jax.ShapeDtypeStruct((group, n_small), F32),
        ],
        scratch_shapes=[pltpu.VMEM((depth, inner + n_small), BF16), sems],
        compiler_params=params(),
        name="project",
    )(offsets, normed, *wx_blocks)
    xc, pre, bc, y_all, states = pl.pallas_call(
        partial(scan_forward, heads),
        grid=(chunks,),
        in_specs=[
            smem,
            rows_spec(Q, inner),
            rows_spec(Q, n_small),
            whole_spec((8, n_conv)),
            whole_spec((8, LANES)),
            whole_spec((1, inner)),
        ],
        out_specs=[
            rows_spec(Q, inner),
            rows_spec(Q, n_conv),
            rows_spec(Q, 2 * STATE),
            rows_spec(Q, inner),
            pl.BlockSpec((1, STATE, inner), lambda i: (i, 0, 0)),
        ],
        out_shape=[
            jax.ShapeDtypeStruct((group, inner), BF16),
            jax.ShapeDtypeStruct((group, n_conv), BF16),
            jax.ShapeDtypeStruct((group, 2 * STATE), BF16),
            jax.ShapeDtypeStruct((group, inner), BF16),
            jax.ShapeDtypeStruct((chunks, STATE, inner), BF16),
        ],
        scratch_shapes=[pltpu.VMEM((Q + 8, n_conv), F32), pltpu.VMEM((STATE, inner), F32)],
        compiler_params=params(),
        name="scan_forward",
    )(ends, x_raw, small, taps, par, skip)

    z_all, gg, sq = pl.pallas_call(
        partial(gate_forward, count),
        grid=(steps,),
        in_specs=[
            smem,
            rows_spec(block, depth),
            rows_spec(block, inner),
            whole_spec((1, inner)),
        ]
        + [hbm] * count,
        out_specs=[rows_spec(block, inner), rows_spec(block, inner), rows_spec(block, LANES)],
        out_shape=[
            jax.ShapeDtypeStruct((group, inner), BF16),
            jax.ShapeDtypeStruct((group, inner), BF16),
            jax.ShapeDtypeStruct((group, LANES), F32),
        ],
        scratch_shapes=[pltpu.VMEM((depth, inner), BF16), sems],
        compiler_params=params(),
        name="gate_forward",
    )(offsets, normed, y_all, gain_out, *wz_blocks)
    sq_part = jnp.sum(sq, axis=1)
    sq_all = sq_part + swap(sq_part)

    live_wide = jnp.broadcast_to(live[:, None], (group, LANES))
    u_part, d_scaled, prod = pl.pallas_call(
        partial(out_pair, count),
        grid=(steps,),
        in_specs=[
            smem,
            rows_spec(block, inner),
            rows_spec(block, depth),
            rows_spec(block, LANES),
        ]
        + [hbm] * count,
        out_specs=[rows_spec(block, depth), rows_spec(block, inner), rows_spec(block, LANES)],
        out_shape=[
            jax.ShapeDtypeStruct((group, depth), BF16),
            jax.ShapeDtypeStruct((group, inner), BF16),
            jax.ShapeDtypeStruct((group, LANES), F32),
        ],
        scratch_shapes=[pltpu.VMEM((depth, inner), BF16), sems],
        compiler_params=params(),
        name="out_pair",
    )(offsets, gg, cot_all, live_wide, *wo_blocks)
    prod_part = jnp.sum(prod, axis=1)
    prod_all = prod_part + swap(prod_part)
    inv_gate = lax.rsqrt(sq_all / inner_total + EPSILON)

    u_own = lax.dynamic_slice_in_dim(u_part, me_t * own_rows, own_rows, 0)
    u_send = lax.dynamic_slice_in_dim(u_part, (n_t - 1 - me_t) * own_rows, own_rows, 0)
    u_recv = swap(u_send)
    inv_own = lax.dynamic_slice_in_dim(inv_gate, me_t * own_rows, own_rows, 0)
    branch = (u_own.astype(F32) + u_recv.astype(F32)) * (inv_own * live_own)[:, None]
    layer_out = (tokens.astype(F32) + branch).astype(BF16)

    d_branch = (cot_all.astype(F32) * (live * inv_gate)[:, None]).astype(BF16)
    g_out = lax.dot_general(d_branch, gg, TN, preferred_element_type=F32).astype(BF16)
    grad_out = lax.psum_scatter(g_out, "dp", scatter_dimension=0, tiled=True)

    coef = inv_gate * inv_gate * inv_gate * (prod_all / inner_total)
    rg_wide = jnp.broadcast_to(inv_gate[:, None], (group, LANES))
    coef_wide = jnp.broadcast_to(coef[:, None], (group, LANES))
    dy, dz, gain_acc = pl.pallas_call(
        gate_backward,
        grid=(steps,),
        in_specs=[
            rows_spec(block, inner),
            rows_spec(block, inner),
            rows_spec(block, inner),
            rows_spec(block, LANES),
            rows_spec(block, LANES),
            whole_spec((1, inner)),
        ],
        out_specs=[rows_spec(block, inner), rows_spec(block, inner), whole_spec((8, inner))],
        out_shape=[
            jax.ShapeDtypeStruct((group, inner), BF16),
            jax.ShapeDtypeStruct((group, inner), BF16),
            jax.ShapeDtypeStruct((8, inner), F32),
        ],
        compiler_params=params(),
        name="gate_backward",
    )(d_scaled, y_all, z_all, rg_wide, coef_wide, gain_out)
    g_z = lax.dot_general(normed, dz, TN, preferred_element_type=F32).astype(BF16)
    grad_z = lax.psum_scatter(g_z, "dp", scatter_dimension=0, tiled=True)

    dy = after(dy, g_z)
    back = lambda width: pl.BlockSpec((Q, width), lambda i: (chunks - 1 - i, 0))
    dx, acc, hacc = pl.pallas_call(
        partial(scan_backward, heads, chunks),
        grid=(chunks,),
        in_specs=[
            smem,
            back(inner),
            back(inner),
            back(n_conv),
            back(inner),
            back(n_small),
            back(2 * STATE),
            pl.BlockSpec((1, STATE, inner), lambda i: (chunks - 1 - i, 0, 0)),
            whole_spec((8, n_conv)),
            whole_spec((8, LANES)),
            whole_spec((1, inner)),
            whole_spec((inner, LANES)),
        ],
        out_specs=[back(inner + n_small), whole_spec((8 * (K + 2), n_conv)), whole_spec((16, LANES))],
        out_shape=[
            jax.ShapeDtypeStruct((group, inner + n_small), BF16),
            jax.ShapeDtypeStruct((8 * (K + 2), n_conv), F32),
            jax.ShapeDtypeStruct((16, LANES), F32),
        ],
        scratch_shapes=[
            pltpu.VMEM((STATE, inner), F32),
            pltpu.VMEM((Q + 8, n_conv), F32),
            pltpu.VMEM((Q, inner), BF16),
            pltpu.VMEM((Q, inner), BF16),
            pltpu.VMEM((Q, inner), BF16),
            pltpu.VMEM((Q, inner), BF16),
            pltpu.VMEM((Q, inner), BF16),
            pltpu.VMEM((Q, inner), BF16),
            pltpu.VMEM((STATE, inner), BF16),
            pltpu.VMEM((8, inner), F32),
        ],
        compiler_params=params(),
        name="scan_backward",
    )(ends, dy, xc, pre, x_raw, small, bc, states, taps, par, skip, sel)

    dx = after(dx, u_recv)
    g_x = lax.dot_general(normed, dx, TN, preferred_element_type=F32).astype(BF16)
    grad_x = lax.psum_scatter(g_x, "dp", scatter_dimension=0, tiled=True)

    d_normed, in_acc = pl.pallas_call(
        partial(normed_back, count),
        grid=(steps,),
        in_specs=[
            smem,
            rows_spec(block, inner),
            rows_spec(block, inner + n_small),
            rows_spec(block, depth),
        ]
        + [hbm] * (2 * count),
        out_specs=[rows_spec(block, depth), whole_spec((8, depth))],
        out_shape=[jax.ShapeDtypeStruct((group, depth), BF16), jax.ShapeDtypeStruct((8, depth), F32)],
        scratch_shapes=[
            pltpu.VMEM((depth, inner), BF16),
            pltpu.VMEM((depth, inner + n_small), BF16),
            sems,
            sems,
        ],
        compiler_params=params(),
        name="normed_back",
    )(offsets, dz, dx, normed, *wz_blocks, *wx_blocks)
    dn_own = lax.dynamic_slice_in_dim(d_normed, me_t * own_rows, own_rows, 0)
    dn_send = lax.dynamic_slice_in_dim(d_normed, (n_t - 1 - me_t) * own_rows, own_rows, 0)
    dn = dn_own.astype(F32) + swap(dn_send).astype(F32)
    tok_own = tokens.astype(F32)
    inv_tok = lax.dynamic_slice_in_dim(inv_in, me_t * own_rows, own_rows, 0)
    spread = dn * gain_in
    grad_tokens = (
        cotangent.astype(F32)
        + inv_tok * spread
        - tok_own * inv_tok * inv_tok * inv_tok * jnp.mean(spread * tok_own, axis=1, keepdims=True)
    )

    acc = acc.reshape(K + 2, 8, n_conv).sum(axis=1)
    hsum = hacc.reshape(2, 8, LANES).sum(axis=1)
    d_gate = gain_acc.sum(axis=0)
    d_in = in_acc.sum(axis=0) / gain_in[0]
    d_sk = acc[K + 1, :inner].reshape(heads, WIDTH).sum(axis=1)
    shared = [acc[: K + 1, inner:].reshape(-1), d_in]
    headed = [acc[: K + 1, :inner].reshape(-1), d_gate, hsum[:, :heads].reshape(-1), d_sk]
    shared_size = sum(piece.size for piece in shared)
    vector = jnp.concatenate(shared + headed)
    size = vector.shape[0]
    vector = jnp.concatenate([vector, jnp.zeros((-size % 1024,), F32)]).reshape(-1, LANES)
    vector = sum_dp(vector)
    cut_rows = -(-shared_size // (8 * LANES)) * 8
    joint = (vector[:cut_rows] + swap(vector[:cut_rows])).reshape(-1)
    vector = vector.reshape(-1)

    n_bc = (K + 1) * 2 * STATE
    bc_sum = joint[:n_bc].reshape(K + 1, 2, STATE)
    me_all = me_dp * n_t + me_t
    bc_sum = lax.dynamic_slice_in_dim(bc_sum, me_all * span_n, span_n, 2)
    grad_bc_taps = bc_sum[:K].transpose(1, 2, 0).reshape(conv_bc.shape)
    grad_bc_bias = bc_sum[K]
    grad_in = lax.dynamic_slice_in_dim(joint[n_bc : n_bc + depth], me_all * norm_gain.shape[0], norm_gain.shape[0], 0)
    at = shared_size
    x_sum = vector[at : at + (K + 1) * inner].reshape(K + 1, heads, WIDTH)
    at += (K + 1) * inner
    x_sum = lax.dynamic_slice_in_dim(x_sum, me_dp * span_p, span_p, 2)
    grad_x_taps = x_sum[:K].transpose(1, 2, 0).reshape(conv_x.shape)
    grad_x_bias = x_sum[K]
    grad_gate = lax.dynamic_slice_in_dim(vector[at : at + inner].reshape(heads, WIDTH), me_dp * span_p, span_p, 1)
    at += inner
    grad_dt_bias = vector[at : at + heads]
    grad_a_log = vector[at + heads : at + 2 * heads]
    grad_skip = vector[at + 2 * heads : at + 3 * heads]

    grad_zx = jnp.stack([grad_z.astype(F32), grad_x[:, :inner].astype(F32)])
    grad_dt = grad_x[:, inner + 2 * STATE : inner + 2 * STATE + heads].astype(F32)
    bc_part = grad_x[:, inner : inner + 2 * STATE]
    half = w_bc.shape[1]
    bc_own = lax.dynamic_slice_in_dim(bc_part, me_t * half, half, 0)
    bc_send = lax.dynamic_slice_in_dim(bc_part, (n_t - 1 - me_t) * half, half, 0)
    bc_total = bc_own.astype(F32) + swap(bc_send).astype(F32)
    grad_bc = bc_total.reshape(half, 2, STATE).transpose(1, 0, 2)
    return (
        layer_out,
        grad_tokens,
        grad_in,
        grad_zx,
        grad_bc,
        grad_dt,
        grad_x_taps,
        grad_x_bias,
        grad_bc_taps,
        grad_bc_bias,
        grad_dt_bias,
        grad_a_log,
        grad_skip,
        grad_gate,
        grad_out.astype(F32).T,
    )


def solution(mesh):
    both = ("dp", "tensor")
    in_specs = (
        P(both, None),
        P(both, None),
        P("dp", None),
        P(both),
        P(None, "dp", "tensor"),
        P(None, both, None),
        P("dp", "tensor"),
        P("tensor", "dp"),
        P("tensor", "dp"),
        P(None, both),
        P(None, both),
        P("tensor"),
        P("tensor"),
        P("tensor"),
        P("tensor", "dp"),
        P("tensor", "dp"),
    )
    out_specs = (
        P(both, None),
        P(both, None),
        P(both),
        P(None, "dp", "tensor"),
        P(None, both, None),
        P("dp", "tensor"),
        P("tensor", "dp"),
        P("tensor", "dp"),
        P(None, both),
        P(None, both),
        P("tensor"),
        P("tensor"),
        P("tensor"),
        P("tensor", "dp"),
        P("tensor", "dp"),
    )
    return jax.shard_map(local, mesh=mesh, in_specs=in_specs, out_specs=out_specs, check_vma=False)
```

```python
from functools import partial

import jax
import jax.numpy as jnp
from jax import lax
from jax.experimental import pallas as pl
from jax.experimental.pallas import tpu as pltpu
from jax.sharding import PartitionSpec as P

EPSILON = 1e-05
HIGHEST = lax.Precision.HIGHEST
K = 4
WIDTH = 64
STATE = 128
Q = 128
LANES = 128
LOG2E = 1.4426950408889634
VMEM_LIMIT = 60 * 1024 * 1024
F32 = jnp.float32
BF16 = jnp.bfloat16

NN = (((1,), (0,)), ((), ()))
NT = (((1,), (1,)), ((), ()))
TN = (((0,), (0,)), ((), ()))


def mm(a, b, dims=NN):
    return lax.dot_general(a, b, dims, preferred_element_type=F32)


def mm_exact(a, b, dims=NN):
    return lax.dot_general(a, b, dims, preferred_element_type=F32, precision=HIGHEST)


def iota(shape, dim):
    return lax.broadcasted_iota(jnp.int32, shape, dim)


def segment_of(rows, ends_ref, count):
    total = (rows >= ends_ref[0]).astype(jnp.int32)
    for j in range(1, count):
        total = total + (rows >= ends_ref[j]).astype(jnp.int32)
    return total


def scalar_segment(row, ends_ref, count):
    total = jnp.where(row >= ends_ref[0], 1, 0)
    for j in range(1, count):
        total = total + jnp.where(row >= ends_ref[j], 1, 0)
    return total


def sigmoid(v):
    return 0.5 * jnp.tanh(0.5 * v) + 0.5


def softplus(v):
    return jnp.maximum(v, 0.0) + jnp.log1p(jnp.exp(-jnp.abs(v)))


def chunk_masks(chunk, ends_ref, count):
    base = chunk * Q
    rows = iota((Q, Q), 0) + base
    cols = iota((Q, Q), 1) + base
    row_ids = segment_of(rows, ends_ref, count)
    col_ids = segment_of(cols, ends_ref, count)
    same = row_ids == col_ids
    before_id = jnp.where(chunk == 0, -1, scalar_segment(base - 1, ends_ref, count))
    final_id = scalar_segment(base + Q - 1, ends_ref, count)
    carry = (row_ids == before_id).astype(F32)
    last = (row_ids == final_id).astype(F32)
    passing = jnp.where(before_id == final_id, 1.0, 0.0).astype(F32)
    return rows, cols, row_ids, same, carry, last, passing


def decays(dt_raw, par_ref):
    shifted = dt_raw + par_ref[0:1, :]
    step = softplus(shifted)
    decay_rate = jnp.exp(par_ref[1:2, :])
    return shifted, step, decay_rate


def pair_columns(values, pair, first):
    left = jnp.broadcast_to(values[:, 2 * pair : 2 * pair + 1], (Q, LANES))
    right = jnp.broadcast_to(values[:, 2 * pair + 1 : 2 * pair + 2], (Q, LANES))
    return left, right, jnp.where(first, left, right)


def scan_forward(
    heads, ends_ref, xr_ref, small_ref, taps_ref, par_ref, skip_ref,
    xc_ref, pre_ref, bc_ref, y_ref, st_ref, buf, state,
):
    count = ends_ref.shape[0]
    inner = heads * WIDTH
    chunk = pl.program_id(0)

    @pl.when(chunk == 0)
    def _():
        buf[0:8, :] = jnp.zeros((8, buf.shape[1]), F32)
        state[...] = jnp.zeros(state.shape, F32)

    rows, cols, row_ids, same, carry, last, passing = chunk_masks(chunk, ends_ref, count)
    causal = rows >= cols
    visible = same & causal
    lag_mask = [None]
    for lag in range(1, K):
        earlier = rows - lag
        keep = (segment_of(earlier, ends_ref, count) == row_ids) & (earlier >= 0)
        lag_mask.append(keep.astype(F32))

    small = small_ref[...]
    for lo in range(0, inner, LANES):
        buf[8 : 8 + Q, lo : lo + LANES] = xr_ref[:, lo : lo + LANES].astype(F32)
    buf[8 : 8 + Q, inner : inner + 2 * STATE] = small[:, : 2 * STATE]

    def convolve(lo):
        span = slice(lo, lo + LANES)
        pre = taps_ref[K : K + 1, span] + taps_ref[K - 1 : K, span] * buf[8 : 8 + Q, span]
        for lag in range(1, K):
            pre = pre + taps_ref[K - 1 - lag : K - lag, span] * (
                buf[8 - lag : 8 - lag + Q, span] * lag_mask[lag]
            )
        pre_ref[:, span] = pre.astype(BF16)
        return pre * sigmoid(pre)

    b_f = convolve(inner).astype(BF16).astype(F32)
    c_b = convolve(inner + STATE).astype(BF16)
    b_b = b_f.astype(BF16)
    bc_ref[:, :STATE] = b_b
    bc_ref[:, STATE:] = c_b
    b_t = b_f.T.astype(BF16)

    _, step, decay_rate = decays(small[:, 2 * STATE :], par_ref)
    csum = mm_exact(causal.astype(F32), step * (-LOG2E * decay_rate))
    csum_t = csum.T
    scores = jnp.where(visible, mm(c_b, b_b, NT), 0.0)
    first = iota((Q, LANES), 1) < WIDTH
    first_row = iota((1, LANES), 1) < WIDTH

    for pair in range(heads // 2):
        span = slice(pair * LANES, (pair + 1) * LANES)
        xc = convolve(pair * LANES).astype(BF16)
        xc_ref[:, span] = xc
        xc = xc.astype(F32)
        left, right, both = pair_columns(csum, pair, first)
        _, _, step_pair = pair_columns(step, pair, first)
        mix = jnp.concatenate(
            [
                (scores * jnp.exp2(jnp.minimum(left - csum_t[2 * pair : 2 * pair + 1, :], 0.0))).astype(BF16),
                (scores * jnp.exp2(jnp.minimum(right - csum_t[2 * pair + 1 : 2 * pair + 2, :], 0.0))).astype(BF16),
            ],
            axis=1,
        )
        fed = xc * step_pair
        fed_b = fed.astype(BF16)
        zero = jnp.zeros((Q, LANES), BF16)
        stacked = jnp.concatenate([jnp.where(first, fed_b, zero), jnp.where(first, zero, fed_b)], axis=0)
        held = state[:, span]
        held_b = held.astype(BF16)
        st_ref[0, :, span] = held_b
        y = mm(mix, stacked) + mm(c_b, held_b) * (jnp.exp2(both) * carry)
        y_ref[:, span] = (y + skip_ref[:, span] * xc).astype(BF16)
        closing = both[Q - 1 : Q, :]
        weighted = (fed_b.astype(F32) * (jnp.exp2(closing - both) * last)).astype(BF16)
        state[:, span] = held * (jnp.exp2(closing) * passing) + mm(b_t, weighted)

    buf[0:8, :] = buf[Q : Q + 8, :]


def scan_backward(
    heads, chunks, top, ends_ref, dy_ref, xc_ref, pre_ref, xr_ref, small_ref, bc_ref, st_ref, taps_ref, par_ref,
    skip_ref, sel_ref, *refs,
):
    if top + 1 < chunks:
        state_in, halo_in, _ = refs[:3]
        refs = refs[3:]
    dx_ref, acc_ref, hacc_ref, state_out, halo_out = refs[:5]
    dstate, dpre, ab_hi, ab_lo, v_b, u_b, dyd, fedw, dst_b, through = refs[5:]
    count = ends_ref.shape[0]
    inner = heads * WIDTH
    total_rows = chunks * Q
    chunk = top - pl.program_id(0)

    @pl.when(pl.program_id(0) == 0)
    def _():
        if top + 1 < chunks:
            dpre[Q : Q + 8, :] = halo_in[...]
            dstate[...] = state_in[...]
        else:
            dpre[Q : Q + 8, :] = jnp.zeros((8, dpre.shape[1]), F32)
            dstate[...] = jnp.zeros(dstate.shape, F32)
        acc_ref[...] = jnp.zeros(acc_ref.shape, F32)
        hacc_ref[...] = jnp.zeros(hacc_ref.shape, F32)

    rows, cols, row_ids, same, carry, last, passing = chunk_masks(chunk, ends_ref, count)
    causal = rows >= cols
    visible = same & causal
    lag_mask = [None]
    for lag in range(1, K):
        later = rows + lag
        keep = (segment_of(later, ends_ref, count) == row_ids) & (later < total_rows)
        lag_mask.append(keep.astype(F32))

    small = small_ref[...]
    shifted, step, decay_rate = decays(small[:, 2 * STATE :], par_ref)
    csum = mm_exact(causal.astype(F32), step * (-LOG2E * decay_rate))
    csum_t = csum.T
    b_b = bc_ref[:, :STATE]
    c_b = bc_ref[:, STATE:]
    c_t = c_b.astype(F32).T.astype(BF16)
    scores = jnp.where(visible, mm(c_b, b_b, NT), 0.0)
    first = iota((Q, LANES), 1) < WIDTH

    def fold(values):
        return values.reshape(Q // 8, 8, values.shape[1]).sum(axis=0)

    def conv_back(lo, d_conv, raw):
        span = slice(lo, lo + LANES)
        pre = pre_ref[:, span].astype(F32)
        gate = sigmoid(pre)
        d_pre = d_conv * (gate * (1.0 + pre * (1.0 - gate)))
        dpre[0:Q, span] = d_pre
        d_raw = taps_ref[K - 1 : K, span] * d_pre
        acc_ref[8 * (K - 1) : 8 * K, span] += fold(d_pre * raw)
        acc_ref[8 * K : 8 * K + 8, span] += fold(d_pre)
        for lag in range(1, K):
            moved = dpre[lag : lag + Q, span] * lag_mask[lag]
            d_raw = d_raw + taps_ref[K - 1 - lag : K - lag, span] * moved
            acc_ref[8 * (K - 1 - lag) : 8 * (K - lag), span] += fold(moved * raw)
        dx_ref[:, span] = d_raw.astype(BF16)

    d_scores = jnp.zeros((Q, Q), F32)
    for pair in range(heads // 2):
        span = slice(pair * LANES, (pair + 1) * LANES)
        xc = xc_ref[:, span].astype(F32)
        dy_b = dy_ref[:, span]
        dy = dy_b.astype(F32)
        left, right, both = pair_columns(csum, pair, first)
        _, _, step_pair = pair_columns(step, pair, first)
        fall_left = jnp.exp2(jnp.minimum(left - csum_t[2 * pair : 2 * pair + 1, :], 0.0))
        fall_right = jnp.exp2(jnp.minimum(right - csum_t[2 * pair + 1 : 2 * pair + 2, :], 0.0))
        mix = jnp.concatenate([(scores * fall_left).astype(BF16), (scores * fall_right).astype(BF16)], axis=1)
        fed_b = (xc * step_pair).astype(BF16)
        fed = fed_b.astype(F32)
        zero = jnp.zeros((Q, LANES), BF16)
        stacked = jnp.concatenate([jnp.where(first, fed_b, zero), jnp.where(first, zero, fed_b)], axis=0)
        held_b = st_ref[0, :, span]
        grown = jnp.exp2(both) * carry
        y = mm(mix, stacked) + mm(c_b, held_b) * grown
        d_mix = mm(dy_b, stacked, NT)
        d_scores = d_scores + d_mix[:, :Q] * fall_left + d_mix[:, Q:] * fall_right
        d_fed2 = mm(mix, dy_b, TN)
        d_fed_in = jnp.where(first, d_fed2[:Q], d_fed2[Q:])
        closing = both[Q - 1 : Q, :]
        shrink = jnp.exp2(closing - both) * last
        d_held = dstate[:, span]
        d_held_b = d_held.astype(BF16)
        dst_b[:, span] = d_held_b
        d_fed_out = mm(b_b, d_held_b) * shrink
        d_fed = d_fed_in + d_fed_out
        straddle = dy * y - fed * d_fed_in
        hi = straddle.astype(BF16)
        ab_hi[:, span] = hi
        ab_lo[:, span] = (straddle - hi.astype(F32)).astype(BF16)
        v_b[:, span] = (fed * d_fed_out).astype(BF16)
        u_b[:, span] = (xc * d_fed).astype(BF16)
        fedw[:, span] = (fed * shrink).astype(BF16)
        dy_grown = (dy * grown).astype(BF16)
        dyd[:, span] = dy_grown
        kept = jnp.exp2(closing) * passing
        through[:, span] = (d_held * held_b.astype(F32)).reshape(STATE // 8, 8, LANES).sum(axis=0) * kept
        dstate[:, span] = d_held * kept + mm(c_t, dy_grown)
        acc_ref[8 * K + 8 : 8 * K + 16, span] += fold(dy * xc)
        d_conv = d_fed * step_pair + skip_ref[:, span] * dy
        conv_back(pair * LANES, d_conv, xr_ref[:, span].astype(F32))

    d_scores_b = jnp.where(visible, d_scores, 0.0).astype(BF16)
    d_c = mm(dyd[...], st_ref[0], NT) + mm(d_scores_b, b_b)
    d_b = mm(fedw[...], dst_b[...], NT) + mm(d_scores_b, c_b, TN)
    conv_back(inner, d_b, small[:, :STATE])
    conv_back(inner + STATE, d_c, small[:, STATE : 2 * STATE])

    sel = sel_ref[...]
    red_ab = mm(ab_hi[...], sel) + mm(ab_lo[...], sel)
    red_v = mm(v_b[...], sel)
    red_u = mm(u_b[...], sel)
    thr = through[...]
    thr_hi = thr.astype(BF16)
    red_t = mm(thr_hi, sel) + mm((thr - thr_hi.astype(F32)).astype(BF16), sel)
    red_t = jnp.sum(red_t, axis=0, keepdims=True)
    d_rate = (
        mm_exact((same & (cols >= rows)).astype(F32), red_ab)
        + mm_exact((same & (cols < rows)).astype(F32), red_v)
        + red_t
    )
    d_step = red_u - d_rate * decay_rate
    d_dt = d_step * sigmoid(shifted)
    dx_ref[:, inner + 2 * STATE :] = d_dt.astype(BF16)
    hacc_ref[0:8, :] += fold(d_dt)
    hacc_ref[8:16, :] += fold(d_rate * (-decay_rate * step))
    dpre[Q : Q + 8, :] = dpre[0:8, :]
    halo_out[...] = dpre[0:8, :]
    state_out[...] = dstate[...]


def load_blocks(offsets_ref, blocks, whole, sems):
    @pl.when(pl.program_id(0) == 0)
    def _():
        copies = []
        for k, block in enumerate(blocks):
            size = block.shape[0]
            start = pl.multiple_of(offsets_ref[k], 32) if len(blocks) > 1 else 0
            copies.append(pltpu.make_async_copy(block, whole.at[pl.ds(start, size), :], sems.at[k]))
        for copy in copies:
            copy.start()
        for copy in copies:
            copy.wait()


def project(count, heads, offsets_ref, normed_ref, place_ref, *refs):
    blocks, (x_ref, small_ref, taps_ref, w_ref, sems) = refs[:count], refs[count:]
    load_blocks(offsets_ref, blocks, w_ref, sems)
    inner = x_ref.shape[1]

    @pl.when(pl.program_id(0) == 0)
    def _():
        spare = w_ref[:, inner + 2 * STATE :]
        lanes = iota((w_ref.shape[0], LANES), 1)
        for lo in range(0, inner + 2 * STATE, LANES):
            if lo < inner:
                wanted, row = place_ref[:, :LANES] == lanes + lo, heads
            else:
                wanted, row = place_ref[:, LANES:] == lanes + (lo - inner), heads + 8
            moved = mm(spare, jnp.where(wanted, 1.0, 0.0).astype(BF16), TN)
            taps_ref[:, lo : lo + LANES] = moved[row : row + 8, :]

    tile = 256
    rows = normed_ref[...]
    for lo in range(0, inner, tile):
        x_ref[:, lo : lo + tile] = mm(rows, w_ref[:, lo : lo + tile]).astype(BF16)
    small_ref[...] = mm(rows, w_ref[:, inner:])


def gate_forward(normed_ref, y_ref, gain_ref, w_ref, z_ref, gg_ref, sq_ref):
    width = w_ref.shape[1]
    tile = 256
    rows = normed_ref[...]
    square = jnp.zeros((rows.shape[0], LANES), F32)
    for lo in range(0, width, tile):
        span = slice(lo, lo + tile)
        z = mm(rows, w_ref[:, span])
        z_b = z.astype(BF16)
        z_ref[:, span] = z_b
        z = z_b.astype(F32)
        gated = y_ref[:, span].astype(F32) * (z * sigmoid(z))
        gg_ref[:, span] = (gated * gain_ref[K + 1 : K + 2, span]).astype(BF16)
        twice = gated * gated
        for part in range(0, tile, LANES):
            square = square + twice[:, part : part + LANES]
    sq_ref[...] = square


def out_pair(gg_ref, cot_ref, live_ref, w_ref, u_ref, ds_ref, prod_ref):
    width = w_ref.shape[0]
    tile = 256
    gg = gg_ref[...]
    cot = cot_ref[...]
    live = live_ref[...]
    product = jnp.zeros((gg.shape[0], LANES), F32)
    for lo in range(0, width, tile):
        span = slice(lo, lo + tile)
        u = mm(gg, w_ref[span, :], NT)
        u_ref[:, span] = u.astype(BF16)
        term = u * cot[:, span].astype(F32)
        for part in range(0, tile, LANES):
            product = product + term[:, part : part + LANES]
        wide = jnp.concatenate([live] * (tile // LANES), axis=1)
        ds_ref[:, span] = (mm(cot, w_ref[:, span]) * wide).astype(BF16)
    prod_ref[...] = product * live


def gate_backward(ds_ref, y_ref, z_ref, rg_ref, coef_ref, gain_ref, dy_ref, dz_ref, acc_ref):
    @pl.when(pl.program_id(0) == 0)
    def _():
        acc_ref[...] = jnp.zeros(acc_ref.shape, F32)

    rg = rg_ref[...]
    coef = coef_ref[...]
    count = rg.shape[0]
    for lo in range(0, ds_ref.shape[1], LANES):
        span = slice(lo, lo + LANES)
        z = z_ref[:, span].astype(F32)
        y = y_ref[:, span].astype(F32)
        gate = sigmoid(z)
        silu = z * gate
        gated = y * silu
        d_normal = ds_ref[:, span].astype(F32) * rg
        acc_ref[:, span] += (d_normal * gated).reshape(count // 8, 8, LANES).sum(axis=0)
        d_gated = d_normal * gain_ref[K + 1 : K + 2, span] - gated * coef
        dy_ref[:, span] = (d_gated * silu).astype(BF16)
        dz_ref[:, span] = (d_gated * y * (gate + silu * (1.0 - gate))).astype(BF16)


def normed_back(count, offsets_ref, dz_ref, dx_ref, normed_ref, wz_ref, *refs):
    blocks, (out_ref, acc_ref, wx_ref, sems) = refs[:count], refs[count:]
    load_blocks(offsets_ref, blocks, wx_ref, sems)

    @pl.when(pl.program_id(0) == 0)
    def _():
        acc_ref[...] = jnp.zeros(acc_ref.shape, F32)

    dz = dz_ref[...]
    dx = dx_ref[...]
    tile = 256
    count = dz.shape[0]
    for lo in range(0, wz_ref.shape[0], tile):
        span = slice(lo, lo + tile)
        d_normed = mm(dz, wz_ref[span, :], NT) + mm(dx, wx_ref[span, :], NT)
        out_ref[:, span] = d_normed.astype(BF16)
        term = d_normed * normed_ref[:, span].astype(F32)
        acc_ref[:, span] += term.reshape(count // 8, 8, tile).sum(axis=0)


def params():
    return pltpu.CompilerParams(dimension_semantics=("arbitrary",), vmem_limit_bytes=VMEM_LIMIT)


def rows_spec(block, width, column=0):
    return pl.BlockSpec((block, width), lambda i: (i, column))


def whole_spec(shape, column=0):
    return pl.BlockSpec(shape, lambda i: (0, column))


def local(
    tokens,
    cotangent,
    lengths,
    norm_gain,
    w_zx,
    w_bc,
    w_dt,
    conv_x,
    conv_x_bias,
    conv_bc,
    conv_bc_bias,
    dt_bias,
    a_log,
    d_skip,
    gate_gain,
    w_out,
):
    n_t = lax.axis_size("tensor")
    n_dp = lax.axis_size("dp")
    me_t = lax.axis_index("tensor")
    me_dp = lax.axis_index("dp")
    own_rows, depth = tokens.shape
    group = own_rows * n_t
    chunks = group // Q
    heads = dt_bias.shape[0]
    inner = heads * WIDTH
    inner_total = inner * n_t
    shard = w_zx.shape[1]
    pairs = [(i, n_t - 1 - i) for i in range(n_t)]

    def swap(v):
        return lax.ppermute(v, "tensor", pairs)

    def in_order(mine, other, axis=0):
        low = jnp.where(me_t == 0, mine, other)
        high = jnp.where(me_t == 0, other, mine)
        return jnp.concatenate([low, high], axis=axis)

    def sum_dp(v):
        step = 1
        while step < n_dp:
            v = v + lax.ppermute(v, "dp", [(i, i ^ step) for i in range(n_dp)])
            step *= 2
        return v

    def after(value, *others):
        return lax.optimization_barrier((value, *others))[0]

    ring = 4
    plane = n_dp // (2 * ring)

    around = [(i, (i + 2 * plane) % n_dp) for i in range(n_dp)]
    across = [(i, i ^ 2) for i in range(n_dp)]
    beside = [(i, i ^ 1) for i in range(n_dp)]

    def send(v, way):
        return lax.ppermute(v, "dp", way)

    def gather_blocks(v):
        if plane != 2 or v.shape[0] % 32:
            return [lax.all_gather(v, "dp", axis=0, tiled=True)]
        line, other, line_c, other_c = [v], [], [], []
        for turn in range(ring + 1):
            made = []
            if turn < ring - 1:
                made.append((line, send(line[turn], around)))
            if turn < ring:
                made.append((other, send(line[turn], across)))
                made.append((line_c, send(line[turn], beside)))
            if turn:
                made.append((other_c, send(other[turn - 1], beside)))
            fresh = lax.optimization_barrier(tuple(value for _, value in made))
            for (place, _), value in zip(made, fresh):
                place.append(value)
        return line + other + line_c + other_c

    def block_offsets(count, size):
        if count == 1:
            return jnp.zeros((1,), jnp.int32)
        places = []
        for core in range(2):
            for side in range(2):
                for turn in range(ring):
                    level = (me_dp // (2 * plane) - turn + ring) % ring
                    places.append(level * (2 * plane) + ((me_dp % (2 * plane)) ^ (2 * side + core)))
        return jnp.stack(places).astype(jnp.int32) * size

    def scatter_start(v):
        split = v.reshape(ring, 2, 2, shard, v.shape[1])
        side = me_dp % 2
        keep = lax.dynamic_index_in_dim(split, side, 2, keepdims=False)
        return keep, send(lax.dynamic_index_in_dim(split, 1 - side, 2, keepdims=False), beside)

    def scatter_across(keep, got):
        total = keep.astype(F32) + got.astype(F32)
        side = (me_dp // 2) % 2
        keep = lax.dynamic_index_in_dim(total, side, 1, keepdims=False)
        away = lax.dynamic_index_in_dim(total, 1 - side, 1, keepdims=False).astype(BF16)
        return keep, send(away, across)

    def scatter_sum(keep, got):
        return keep + got.astype(F32)

    def scatter_turn(total, got, turn):
        level = me_dp // (2 * plane)
        part = lax.dynamic_index_in_dim(total, (level - turn + ring) % ring, 0, keepdims=False)
        if got is not None:
            part = part + got.astype(F32)
        return part if turn == ring else send(part.astype(BF16), around)

    ends = jnp.cumsum(lengths[0]).astype(jnp.int32)
    places = lax.iota(jnp.int32, group)
    ids = jnp.sum((places[:, None] >= ends[None, :]).astype(jnp.int32), axis=1)
    live = (ids < lengths.shape[1]).astype(F32)
    live_own = lax.dynamic_slice_in_dim(live, me_t * own_rows, own_rows, 0)

    span_p = conv_x_bias.shape[1]
    span_n = conv_bc_bias.shape[1]
    bits = jnp.concatenate([norm_gain, conv_bc.reshape(-1), conv_bc_bias.reshape(-1)])
    other_bits = swap(bits)
    other_bc = swap(w_bc)
    other_tokens = swap(tokens)
    at = norm_gain.shape[0]
    gain_pair = in_order(norm_gain, other_bits[:at]).astype(F32)[:, None]
    cuts = [bits[at:], other_bits[at:]]
    taps_bc = in_order(*[cut[: conv_bc.size].reshape(2, span_n, K) for cut in cuts], axis=1)
    bias_bc = in_order(*[cut[conv_bc.size :].reshape(2, span_n, 1) for cut in cuts], axis=1)
    spare_bc = jnp.concatenate([taps_bc, bias_bc], axis=2).reshape(4 * span_n, K + 1)
    spare_x = jnp.concatenate(
        [conv_x.reshape(shard, K), conv_x_bias.reshape(shard, 1), gate_gain.reshape(shard, 1)], axis=1
    )
    spare = jnp.concatenate(
        [
            w_dt.astype(F32) * gain_pair,
            jnp.pad(spare_x.astype(F32), ((0, 0), (0, 8 - K - 2))),
            jnp.pad(spare_bc.astype(F32), ((0, shard - 4 * span_n), (0, LANES - heads - 8 - K - 1))),
        ],
        axis=1,
    )
    bc_pair = in_order(w_bc, other_bc, axis=1).astype(F32) * gain_pair
    packed = jnp.concatenate([w_zx[1].astype(F32) * gain_pair, bc_pair[0], bc_pair[1], spare], axis=1).astype(BF16)
    z_own = (w_zx[0].astype(F32) * gain_pair).astype(BF16)
    zo_all = lax.all_gather(jnp.concatenate([z_own, w_out.T], axis=1), "dp", axis=0, tiled=True)
    wx_blocks = gather_blocks(packed)
    other_cot = swap(after(cotangent, other_tokens))
    count = len(wx_blocks)
    offsets = block_offsets(count, shard)
    hbm = pl.BlockSpec(memory_space=pl.ANY)
    sems = pltpu.SemaphoreType.DMA((count,))
    where = lax.iota(jnp.int32, depth)
    home, inside = where // shard, where % shard
    place_x = (inside // span_p) * WIDTH + home * span_p + inside % span_p
    half_n = 2 * span_n
    place_bc = (inside // half_n) * STATE + home * half_n + inside % half_n
    place = jnp.concatenate(
        [jnp.broadcast_to(place_x[:, None], (depth, LANES)), jnp.broadcast_to(place_bc[:, None], (depth, LANES))], axis=1
    )

    par = jnp.concatenate([dt_bias[None], a_log[None], jnp.zeros((6, heads), F32)], axis=0)
    par = jnp.concatenate([par, jnp.zeros((8, LANES - heads), F32)], axis=1)
    skip = jnp.repeat(d_skip, WIDTH)[None]
    sel = (lax.iota(jnp.int32, inner)[:, None] // WIDTH == lax.iota(jnp.int32, LANES)[None, :]).astype(BF16)

    tok_all = in_order(tokens, other_tokens)
    tok_f = tok_all.astype(F32)
    inv_in = lax.rsqrt(jnp.mean(tok_f * tok_f, axis=1, keepdims=True) + EPSILON)
    normed = (tok_f * inv_in).astype(BF16)
    cot_all = in_order(cotangent, other_cot)

    n_small = 2 * STATE + LANES
    n_conv = inner + 2 * STATE
    smem = pl.BlockSpec(memory_space=pltpu.SMEM)
    block = 512
    steps = group // block
    x_raw, small, taps = pl.pallas_call(
        partial(project, count, heads),
        grid=(steps,),
        in_specs=[smem, rows_spec(block, depth), whole_spec((depth, 2 * LANES))] + [hbm] * count,
        out_specs=[rows_spec(block, inner), rows_spec(block, n_small), whole_spec((8, n_conv))],
        out_shape=[
            jax.ShapeDtypeStruct((group, inner), BF16),
            jax.ShapeDtypeStruct((group, n_small), F32),
            jax.ShapeDtypeStruct((8, n_conv), F32),
        ],
        scratch_shapes=[pltpu.VMEM((depth, inner + n_small), BF16), sems],
        compiler_params=params(),
        name="project",
    )(offsets, normed, place, *wx_blocks)
    xc, pre, bc, y_all, states = pl.pallas_call(
        partial(scan_forward, heads),
        grid=(chunks,),
        in_specs=[
            smem,
            rows_spec(Q, inner),
            rows_spec(Q, n_small),
            whole_spec((8, n_conv)),
            whole_spec((8, LANES)),
            whole_spec((1, inner)),
        ],
        out_specs=[
            rows_spec(Q, inner),
            rows_spec(Q, n_conv),
            rows_spec(Q, 2 * STATE),
            rows_spec(Q, inner),
            pl.BlockSpec((1, STATE, inner), lambda i: (i, 0, 0)),
        ],
        out_shape=[
            jax.ShapeDtypeStruct((group, inner), BF16),
            jax.ShapeDtypeStruct((group, n_conv), BF16),
            jax.ShapeDtypeStruct((group, 2 * STATE), BF16),
            jax.ShapeDtypeStruct((group, inner), BF16),
            jax.ShapeDtypeStruct((chunks, STATE, inner), BF16),
        ],
        scratch_shapes=[pltpu.VMEM((Q + 8, n_conv), F32), pltpu.VMEM((STATE, inner), F32)],
        compiler_params=params(),
        name="scan_forward",
    )(ends, x_raw, small, taps, par, skip)

    z_all, gg, sq = pl.pallas_call(
        gate_forward,
        grid=(steps,),
        in_specs=[
            rows_spec(block, depth),
            rows_spec(block, inner),
            whole_spec((8, inner)),
            whole_spec((depth, inner), 0),
        ],
        out_specs=[rows_spec(block, inner), rows_spec(block, inner), rows_spec(block, LANES)],
        out_shape=[
            jax.ShapeDtypeStruct((group, inner), BF16),
            jax.ShapeDtypeStruct((group, inner), BF16),
            jax.ShapeDtypeStruct((group, LANES), F32),
        ],
        compiler_params=params(),
        name="gate_forward",
    )(normed, y_all, taps, zo_all)
    sq_part = jnp.sum(sq, axis=1)
    sq_all = sq_part + swap(sq_part)

    live_wide = jnp.broadcast_to(live[:, None], (group, LANES))
    u_part, d_scaled, prod = pl.pallas_call(
        out_pair,
        grid=(steps,),
        in_specs=[
            rows_spec(block, inner),
            rows_spec(block, depth),
            rows_spec(block, LANES),
            whole_spec((depth, inner), 1),
        ],
        out_specs=[rows_spec(block, depth), rows_spec(block, inner), rows_spec(block, LANES)],
        out_shape=[
            jax.ShapeDtypeStruct((group, depth), BF16),
            jax.ShapeDtypeStruct((group, inner), BF16),
            jax.ShapeDtypeStruct((group, LANES), F32),
        ],
        compiler_params=params(),
        name="out_pair",
    )(gg, cot_all, live_wide, zo_all)
    prod_part = jnp.sum(prod, axis=1)
    prod_all = prod_part + swap(prod_part)
    inv_gate = lax.rsqrt(sq_all / inner_total + EPSILON)

    u_own = lax.dynamic_slice_in_dim(u_part, me_t * own_rows, own_rows, 0)
    u_send = lax.dynamic_slice_in_dim(u_part, (n_t - 1 - me_t) * own_rows, own_rows, 0)
    u_recv = swap(u_send)
    inv_own = lax.dynamic_slice_in_dim(inv_gate, me_t * own_rows, own_rows, 0)
    branch = (u_own.astype(F32) + u_recv.astype(F32)) * (inv_own * live_own)[:, None]
    layer_out = (tokens.astype(F32) + branch).astype(BF16)

    d_branch = (cot_all.astype(F32) * (live * inv_gate)[:, None]).astype(BF16)
    g_out = lax.dot_general(d_branch, gg, TN, preferred_element_type=F32).astype(BF16)
    grad_out = lax.psum_scatter(g_out, "dp", scatter_dimension=0, tiled=True)

    coef = inv_gate * inv_gate * inv_gate * (prod_all / inner_total)
    rg_wide = jnp.broadcast_to(inv_gate[:, None], (group, LANES))
    coef_wide = jnp.broadcast_to(coef[:, None], (group, LANES))
    dy, dz, gain_acc = pl.pallas_call(
        gate_backward,
        grid=(steps,),
        in_specs=[
            rows_spec(block, inner),
            rows_spec(block, inner),
            rows_spec(block, inner),
            rows_spec(block, LANES),
            rows_spec(block, LANES),
            whole_spec((8, inner)),
        ],
        out_specs=[rows_spec(block, inner), rows_spec(block, inner), whole_spec((8, inner))],
        out_shape=[
            jax.ShapeDtypeStruct((group, inner), BF16),
            jax.ShapeDtypeStruct((group, inner), BF16),
            jax.ShapeDtypeStruct((8, inner), F32),
        ],
        compiler_params=params(),
        name="gate_backward",
    )(d_scaled, y_all, z_all, rg_wide, coef_wide, taps)
    g_z = lax.dot_general(normed, dz, TN, preferred_element_type=F32).astype(BF16)
    by_hand = count > 1
    if by_hand:
        z_keep, z_got = scatter_start(g_z)
    else:
        grad_z = lax.psum_scatter(g_z, "dp", scatter_dimension=0, tiled=True)

    dy = after(dy, g_z)

    def backward(top, number, carry):
        back = lambda width: pl.BlockSpec((Q, width), lambda i: (top - i, 0))
        operands = [ends, dy, xc, pre, x_raw, small, bc, states, taps, par, skip, sel, *carry]
        return pl.pallas_call(
            partial(scan_backward, heads, chunks, top),
            grid=(number,),
            in_specs=[
                smem,
                back(inner),
                back(inner),
                back(n_conv),
                back(inner),
                back(n_small),
                back(2 * STATE),
                pl.BlockSpec((1, STATE, inner), lambda i: (top - i, 0, 0)),
                whole_spec((8, n_conv)),
                whole_spec((8, LANES)),
                whole_spec((1, inner)),
                whole_spec((inner, LANES)),
            ]
            + ([whole_spec((STATE, inner)), whole_spec((8, n_conv)), hbm] if carry else []),
            out_specs=[
                back(inner + n_small),
                whole_spec((8 * (K + 2), n_conv)),
                whole_spec((16, LANES)),
                whole_spec((STATE, inner)),
                whole_spec((8, n_conv)),
            ],
            out_shape=[
                jax.ShapeDtypeStruct((group, inner + n_small), BF16),
                jax.ShapeDtypeStruct((8 * (K + 2), n_conv), F32),
                jax.ShapeDtypeStruct((16, LANES), F32),
                jax.ShapeDtypeStruct((STATE, inner), F32),
                jax.ShapeDtypeStruct((8, n_conv), F32),
            ],
            scratch_shapes=[
                pltpu.VMEM((STATE, inner), F32),
                pltpu.VMEM((Q + 8, n_conv), F32),
                pltpu.VMEM((Q, inner), BF16),
                pltpu.VMEM((Q, inner), BF16),
                pltpu.VMEM((Q, inner), BF16),
                pltpu.VMEM((Q, inner), BF16),
                pltpu.VMEM((Q, inner), BF16),
                pltpu.VMEM((Q, inner), BF16),
                pltpu.VMEM((STATE, inner), BF16),
                pltpu.VMEM((8, inner), F32),
            ],
            input_output_aliases={len(operands) - 1: 0} if carry else {},
            compiler_params=params(),
            name="scan_backward",
        )(*operands)

    half_chunks = chunks // 2
    dx, acc_a, hacc_a, d_state, halo = backward(chunks - 1, chunks - half_chunks, ())
    if by_hand:
        z_got, dx = lax.optimization_barrier((z_got, dx))
        z_keep, z_got = scatter_across(z_keep, z_got)
        dx, d_state = lax.optimization_barrier((dx, d_state, z_keep))[:2]
    dx, acc, hacc, _, _ = backward(half_chunks - 1, half_chunks, (d_state, halo, dx))
    acc = acc + acc_a
    hacc = hacc + hacc_a
    if by_hand:
        z_got, dx = lax.optimization_barrier((z_got, dx))
        z_total = scatter_sum(z_keep, z_got)
        z_got = scatter_turn(z_total, None, 1)

    dx = after(dx, u_recv)
    g_x = lax.dot_general(normed, dx, TN, preferred_element_type=F32).astype(BF16)
    grad_x = lax.psum_scatter(g_x, "dp", scatter_dimension=0, tiled=True)
    if by_hand:
        z_got, dx = lax.optimization_barrier((z_got, dx, g_x))[:2]
        z_got = scatter_turn(z_total, z_got, 2)

    d_normed, in_acc = pl.pallas_call(
        partial(normed_back, count),
        grid=(steps,),
        in_specs=[
            smem,
            rows_spec(block, inner),
            rows_spec(block, inner + n_small),
            rows_spec(block, depth),
            whole_spec((depth, inner), 0),
        ]
        + [hbm] * count,
        out_specs=[rows_spec(block, depth), whole_spec((8, depth))],
        out_shape=[jax.ShapeDtypeStruct((group, depth), BF16), jax.ShapeDtypeStruct((8, depth), F32)],
        scratch_shapes=[
            pltpu.VMEM((depth, inner + n_small), BF16),
            sems,
        ],
        compiler_params=params(),
        name="normed_back",
    )(offsets, dz, dx, normed, zo_all, *wx_blocks)
    if by_hand:
        z_got, d_normed = lax.optimization_barrier((z_got, d_normed))
        z_got = scatter_turn(z_total, z_got, 3)
        grad_z = scatter_turn(z_total, z_got, ring)
    dn_own = lax.dynamic_slice_in_dim(d_normed, me_t * own_rows, own_rows, 0)
    dn_send = lax.dynamic_slice_in_dim(d_normed, (n_t - 1 - me_t) * own_rows, own_rows, 0)
    dn = dn_own.astype(F32) + swap(dn_send).astype(F32)
    tok_own = tokens.astype(F32)
    inv_tok = lax.dynamic_slice_in_dim(inv_in, me_t * own_rows, own_rows, 0)
    spread = dn
    grad_tokens = (
        cotangent.astype(F32)
        + inv_tok * spread
        - tok_own * inv_tok * inv_tok * inv_tok * jnp.mean(spread * tok_own, axis=1, keepdims=True)
    )

    acc = acc.reshape(K + 2, 8, n_conv).sum(axis=1)
    hsum = hacc.reshape(2, 8, LANES).sum(axis=1)
    d_gate = gain_acc.sum(axis=0)
    d_in = in_acc.sum(axis=0)
    d_sk = acc[K + 1, :inner].reshape(heads, WIDTH).sum(axis=1)
    shared = [acc[: K + 1, inner:].reshape(-1), d_in]
    headed = [acc[: K + 1, :inner].reshape(-1), d_gate, hsum[:, :heads].reshape(-1), d_sk]
    shared_size = sum(piece.size for piece in shared)
    vector = jnp.concatenate(shared + headed)
    size = vector.shape[0]
    vector = jnp.concatenate([vector, jnp.zeros((-size % 1024,), F32)]).reshape(-1, LANES)
    vector = sum_dp(vector)
    cut_rows = -(-shared_size // (8 * LANES)) * 8
    joint = (vector[:cut_rows] + swap(vector[:cut_rows])).reshape(-1)
    vector = vector.reshape(-1)

    n_bc = (K + 1) * 2 * STATE
    bc_sum = joint[:n_bc].reshape(K + 1, 2, STATE)
    me_all = me_dp * n_t + me_t
    bc_sum = lax.dynamic_slice_in_dim(bc_sum, me_all * span_n, span_n, 2)
    grad_bc_taps = bc_sum[:K].transpose(1, 2, 0).reshape(conv_bc.shape)
    grad_bc_bias = bc_sum[K]
    grad_in = lax.dynamic_slice_in_dim(joint[n_bc : n_bc + depth], me_all * norm_gain.shape[0], norm_gain.shape[0], 0)
    grad_in = grad_in / norm_gain.astype(F32)
    at = shared_size
    x_sum = vector[at : at + (K + 1) * inner].reshape(K + 1, heads, WIDTH)
    at += (K + 1) * inner
    x_sum = lax.dynamic_slice_in_dim(x_sum, me_dp * span_p, span_p, 2)
    grad_x_taps = x_sum[:K].transpose(1, 2, 0).reshape(conv_x.shape)
    grad_x_bias = x_sum[K]
    grad_gate = lax.dynamic_slice_in_dim(vector[at : at + inner].reshape(heads, WIDTH), me_dp * span_p, span_p, 1)
    at += inner
    grad_dt_bias = vector[at : at + heads]
    grad_a_log = vector[at + heads : at + 2 * heads]
    grad_skip = vector[at + 2 * heads : at + 3 * heads]

    grad_zx = jnp.stack([grad_z.astype(F32) * gain_pair, grad_x[:, :inner].astype(F32) * gain_pair])
    grad_dt = grad_x[:, inner + 2 * STATE : inner + 2 * STATE + heads].astype(F32) * gain_pair
    bc_part = grad_x[:, inner : inner + 2 * STATE]
    half = w_bc.shape[1]
    bc_own = lax.dynamic_slice_in_dim(bc_part, me_t * half, half, 0)
    bc_send = lax.dynamic_slice_in_dim(bc_part, (n_t - 1 - me_t) * half, half, 0)
    bc_total = bc_own.astype(F32) + swap(bc_send).astype(F32)
    bc_total = bc_total * norm_gain.astype(F32)[:, None]
    grad_bc = bc_total.reshape(half, 2, STATE).transpose(1, 0, 2)
    return (
        layer_out,
        grad_tokens,
        grad_in,
        grad_zx,
        grad_bc,
        grad_dt,
        grad_x_taps,
        grad_x_bias,
        grad_bc_taps,
        grad_bc_bias,
        grad_dt_bias,
        grad_a_log,
        grad_skip,
        grad_gate,
        grad_out.astype(F32).T,
    )


def solution(mesh):
    both = ("dp", "tensor")
    in_specs = (
        P(both, None),
        P(both, None),
        P("dp", None),
        P(both),
        P(None, "dp", "tensor"),
        P(None, both, None),
        P("dp", "tensor"),
        P("tensor", "dp"),
        P("tensor", "dp"),
        P(None, both),
        P(None, both),
        P("tensor"),
        P("tensor"),
        P("tensor"),
        P("tensor", "dp"),
        P("tensor", "dp"),
    )
    out_specs = (
        P(both, None),
        P(both, None),
        P(both),
        P(None, "dp", "tensor"),
        P(None, both, None),
        P("dp", "tensor"),
        P("tensor", "dp"),
        P("tensor", "dp"),
        P(None, both),
        P(None, both),
        P("tensor"),
        P("tensor"),
        P("tensor"),
        P("tensor", "dp"),
        P("tensor", "dp"),
    )
    return jax.shard_map(local, mesh=mesh, in_specs=in_specs, out_specs=out_specs, check_vma=False)
```

```python
from functools import partial

import jax
import jax.numpy as jnp
from jax import lax
from jax.experimental import pallas as pl
from jax.experimental.pallas import tpu as pltpu
from jax.sharding import PartitionSpec as P

EPSILON = 1e-05
HIGHEST = lax.Precision.HIGHEST
K = 4
WIDTH = 64
STATE = 128
Q = 128
LANES = 128
LOG2E = 1.4426950408889634
VMEM_LIMIT = 60 * 1024 * 1024
F32 = jnp.float32
BF16 = jnp.bfloat16

NN = (((1,), (0,)), ((), ()))
NT = (((1,), (1,)), ((), ()))
TN = (((0,), (0,)), ((), ()))


def mm(a, b, dims=NN):
    return lax.dot_general(a, b, dims, preferred_element_type=F32)


def mm_exact(a, b, dims=NN):
    return lax.dot_general(a, b, dims, preferred_element_type=F32, precision=HIGHEST)


def iota(shape, dim):
    return lax.broadcasted_iota(jnp.int32, shape, dim)


def segment_of(rows, ends_ref, count):
    total = (rows >= ends_ref[0]).astype(jnp.int32)
    for j in range(1, count):
        total = total + (rows >= ends_ref[j]).astype(jnp.int32)
    return total


def scalar_segment(row, ends_ref, count):
    total = jnp.where(row >= ends_ref[0], 1, 0)
    for j in range(1, count):
        total = total + jnp.where(row >= ends_ref[j], 1, 0)
    return total


def sigmoid(v):
    return 0.5 * jnp.tanh(0.5 * v) + 0.5


def softplus(v):
    return jnp.maximum(v, 0.0) + jnp.log1p(jnp.exp(-jnp.abs(v)))


def chunk_masks(chunk, ends_ref, count):
    base = chunk * Q
    rows = iota((Q, Q), 0) + base
    cols = iota((Q, Q), 1) + base
    row_ids = segment_of(rows, ends_ref, count)
    col_ids = segment_of(cols, ends_ref, count)
    same = row_ids == col_ids
    before_id = jnp.where(chunk == 0, -1, scalar_segment(base - 1, ends_ref, count))
    final_id = scalar_segment(base + Q - 1, ends_ref, count)
    carry = (row_ids == before_id).astype(F32)
    last = (row_ids == final_id).astype(F32)
    passing = jnp.where(before_id == final_id, 1.0, 0.0).astype(F32)
    return rows, cols, row_ids, same, carry, last, passing


def decays(dt_raw, par_ref):
    shifted = dt_raw + par_ref[0:1, :]
    step = softplus(shifted)
    decay_rate = jnp.exp(par_ref[1:2, :])
    return shifted, step, decay_rate


def pair_columns(values, pair, first):
    left = jnp.broadcast_to(values[:, 2 * pair : 2 * pair + 1], (Q, LANES))
    right = jnp.broadcast_to(values[:, 2 * pair + 1 : 2 * pair + 2], (Q, LANES))
    return left, right, jnp.where(first, left, right)


def scan_forward(
    heads, ends_ref, xr_ref, small_ref, taps_ref, par_ref, skip_ref,
    xc_ref, pre_ref, bc_ref, y_ref, st_ref, buf, state,
):
    count = ends_ref.shape[0]
    inner = heads * WIDTH
    chunk = pl.program_id(0)

    @pl.when(chunk == 0)
    def _():
        buf[0:8, :] = jnp.zeros((8, buf.shape[1]), F32)
        state[...] = jnp.zeros(state.shape, F32)

    rows, cols, row_ids, same, carry, last, passing = chunk_masks(chunk, ends_ref, count)
    causal = rows >= cols
    visible = same & causal
    lag_mask = [None]
    for lag in range(1, K):
        earlier = rows - lag
        keep = (segment_of(earlier, ends_ref, count) == row_ids) & (earlier >= 0)
        lag_mask.append(keep.astype(F32))

    small = small_ref[...]
    for lo in range(0, inner, LANES):
        buf[8 : 8 + Q, lo : lo + LANES] = xr_ref[:, lo : lo + LANES].astype(F32)
    buf[8 : 8 + Q, inner : inner + 2 * STATE] = small[:, : 2 * STATE]

    def convolve(lo):
        span = slice(lo, lo + LANES)
        pre = taps_ref[K : K + 1, span] + taps_ref[K - 1 : K, span] * buf[8 : 8 + Q, span]
        for lag in range(1, K):
            pre = pre + taps_ref[K - 1 - lag : K - lag, span] * (
                buf[8 - lag : 8 - lag + Q, span] * lag_mask[lag]
            )
        pre_ref[:, span] = pre.astype(BF16)
        return pre * sigmoid(pre)

    b_f = convolve(inner).astype(BF16).astype(F32)
    c_b = convolve(inner + STATE).astype(BF16)
    b_b = b_f.astype(BF16)
    bc_ref[:, :STATE] = b_b
    bc_ref[:, STATE:] = c_b
    b_t = b_f.T.astype(BF16)

    _, step, decay_rate = decays(small[:, 2 * STATE :], par_ref)
    csum = mm_exact(causal.astype(F32), step * (-LOG2E * decay_rate))
    csum_t = csum.T
    scores = jnp.where(visible, mm(c_b, b_b, NT), 0.0)
    first = iota((Q, LANES), 1) < WIDTH
    first_row = iota((1, LANES), 1) < WIDTH

    for pair in range(heads // 2):
        span = slice(pair * LANES, (pair + 1) * LANES)
        xc = convolve(pair * LANES).astype(BF16)
        xc_ref[:, span] = xc
        xc = xc.astype(F32)
        left, right, both = pair_columns(csum, pair, first)
        _, _, step_pair = pair_columns(step, pair, first)
        mix = jnp.concatenate(
            [
                (scores * jnp.exp2(jnp.minimum(left - csum_t[2 * pair : 2 * pair + 1, :], 0.0))).astype(BF16),
                (scores * jnp.exp2(jnp.minimum(right - csum_t[2 * pair + 1 : 2 * pair + 2, :], 0.0))).astype(BF16),
            ],
            axis=1,
        )
        fed = xc * step_pair
        fed_b = fed.astype(BF16)
        zero = jnp.zeros((Q, LANES), BF16)
        stacked = jnp.concatenate([jnp.where(first, fed_b, zero), jnp.where(first, zero, fed_b)], axis=0)
        held = state[:, span]
        held_b = held.astype(BF16)
        st_ref[0, :, span] = held_b
        y = mm(mix, stacked) + mm(c_b, held_b) * (jnp.exp2(both) * carry)
        y_ref[:, span] = (y + skip_ref[:, span] * xc).astype(BF16)
        closing = both[Q - 1 : Q, :]
        weighted = (fed_b.astype(F32) * (jnp.exp2(closing - both) * last)).astype(BF16)
        state[:, span] = held * (jnp.exp2(closing) * passing) + mm(b_t, weighted)

    buf[0:8, :] = buf[Q : Q + 8, :]


def scan_backward(
    heads, chunks, top, ends_ref, dy_ref, xc_ref, pre_ref, xr_ref, small_ref, bc_ref, st_ref, taps_ref, par_ref,
    skip_ref, sel_ref, *refs,
):
    if top + 1 < chunks:
        state_in, halo_in, _ = refs[:3]
        refs = refs[3:]
    dx_ref, acc_ref, hacc_ref, state_out, halo_out = refs[:5]
    dstate, dpre, ab_hi, ab_lo, v_b, u_b, dyd, fedw, dst_b, through = refs[5:]
    count = ends_ref.shape[0]
    inner = heads * WIDTH
    total_rows = chunks * Q
    chunk = top - pl.program_id(0)

    @pl.when(pl.program_id(0) == 0)
    def _():
        if top + 1 < chunks:
            dpre[Q : Q + 8, :] = halo_in[...]
            dstate[...] = state_in[...]
        else:
            dpre[Q : Q + 8, :] = jnp.zeros((8, dpre.shape[1]), F32)
            dstate[...] = jnp.zeros(dstate.shape, F32)
        acc_ref[...] = jnp.zeros(acc_ref.shape, F32)
        hacc_ref[...] = jnp.zeros(hacc_ref.shape, F32)

    rows, cols, row_ids, same, carry, last, passing = chunk_masks(chunk, ends_ref, count)
    causal = rows >= cols
    visible = same & causal
    lag_mask = [None]
    for lag in range(1, K):
        later = rows + lag
        keep = (segment_of(later, ends_ref, count) == row_ids) & (later < total_rows)
        lag_mask.append(keep.astype(F32))

    small = small_ref[...]
    shifted, step, decay_rate = decays(small[:, 2 * STATE :], par_ref)
    csum = mm_exact(causal.astype(F32), step * (-LOG2E * decay_rate))
    csum_t = csum.T
    b_b = bc_ref[:, :STATE]
    c_b = bc_ref[:, STATE:]
    c_t = c_b.astype(F32).T.astype(BF16)
    scores = jnp.where(visible, mm(c_b, b_b, NT), 0.0)
    first = iota((Q, LANES), 1) < WIDTH

    def fold(values):
        return values.reshape(Q // 8, 8, values.shape[1]).sum(axis=0)

    def conv_back(lo, d_conv, raw):
        span = slice(lo, lo + LANES)
        pre = pre_ref[:, span].astype(F32)
        gate = sigmoid(pre)
        d_pre = d_conv * (gate * (1.0 + pre * (1.0 - gate)))
        dpre[0:Q, span] = d_pre
        d_raw = taps_ref[K - 1 : K, span] * d_pre
        acc_ref[8 * (K - 1) : 8 * K, span] += fold(d_pre * raw)
        acc_ref[8 * K : 8 * K + 8, span] += fold(d_pre)
        for lag in range(1, K):
            moved = dpre[lag : lag + Q, span] * lag_mask[lag]
            d_raw = d_raw + taps_ref[K - 1 - lag : K - lag, span] * moved
            acc_ref[8 * (K - 1 - lag) : 8 * (K - lag), span] += fold(moved * raw)
        dx_ref[:, span] = d_raw.astype(BF16)

    d_scores = jnp.zeros((Q, Q), F32)
    for pair in range(heads // 2):
        span = slice(pair * LANES, (pair + 1) * LANES)
        xc = xc_ref[:, span].astype(F32)
        dy_b = dy_ref[:, span]
        dy = dy_b.astype(F32)
        left, right, both = pair_columns(csum, pair, first)
        _, _, step_pair = pair_columns(step, pair, first)
        fall_left = jnp.exp2(jnp.minimum(left - csum_t[2 * pair : 2 * pair + 1, :], 0.0))
        fall_right = jnp.exp2(jnp.minimum(right - csum_t[2 * pair + 1 : 2 * pair + 2, :], 0.0))
        mix = jnp.concatenate([(scores * fall_left).astype(BF16), (scores * fall_right).astype(BF16)], axis=1)
        fed_b = (xc * step_pair).astype(BF16)
        fed = fed_b.astype(F32)
        zero = jnp.zeros((Q, LANES), BF16)
        stacked = jnp.concatenate([jnp.where(first, fed_b, zero), jnp.where(first, zero, fed_b)], axis=0)
        held_b = st_ref[0, :, span]
        grown = jnp.exp2(both) * carry
        y = mm(mix, stacked) + mm(c_b, held_b) * grown
        d_mix = mm(dy_b, stacked, NT)
        d_scores = d_scores + d_mix[:, :Q] * fall_left + d_mix[:, Q:] * fall_right
        d_fed2 = mm(mix, dy_b, TN)
        d_fed_in = jnp.where(first, d_fed2[:Q], d_fed2[Q:])
        closing = both[Q - 1 : Q, :]
        shrink = jnp.exp2(closing - both) * last
        d_held = dstate[:, span]
        d_held_b = d_held.astype(BF16)
        dst_b[:, span] = d_held_b
        d_fed_out = mm(b_b, d_held_b) * shrink
        d_fed = d_fed_in + d_fed_out
        straddle = dy * y - fed * d_fed_in
        hi = straddle.astype(BF16)
        ab_hi[:, span] = hi
        ab_lo[:, span] = (straddle - hi.astype(F32)).astype(BF16)
        v_b[:, span] = (fed * d_fed_out).astype(BF16)
        u_b[:, span] = (xc * d_fed).astype(BF16)
        fedw[:, span] = (fed * shrink).astype(BF16)
        dy_grown = (dy * grown).astype(BF16)
        dyd[:, span] = dy_grown
        kept = jnp.exp2(closing) * passing
        through[:, span] = (d_held * held_b.astype(F32)).reshape(STATE // 8, 8, LANES).sum(axis=0) * kept
        dstate[:, span] = d_held * kept + mm(c_t, dy_grown)
        acc_ref[8 * K + 8 : 8 * K + 16, span] += fold(dy * xc)
        d_conv = d_fed * step_pair + skip_ref[:, span] * dy
        conv_back(pair * LANES, d_conv, xr_ref[:, span].astype(F32))

    d_scores_b = jnp.where(visible, d_scores, 0.0).astype(BF16)
    d_c = mm(dyd[...], st_ref[0], NT) + mm(d_scores_b, b_b)
    d_b = mm(fedw[...], dst_b[...], NT) + mm(d_scores_b, c_b, TN)
    conv_back(inner, d_b, small[:, :STATE])
    conv_back(inner + STATE, d_c, small[:, STATE : 2 * STATE])

    sel = sel_ref[...]
    red_ab = mm(ab_hi[...], sel) + mm(ab_lo[...], sel)
    red_v = mm(v_b[...], sel)
    red_u = mm(u_b[...], sel)
    thr = through[...]
    thr_hi = thr.astype(BF16)
    red_t = mm(thr_hi, sel) + mm((thr - thr_hi.astype(F32)).astype(BF16), sel)
    red_t = jnp.sum(red_t, axis=0, keepdims=True)
    d_rate = (
        mm_exact((same & (cols >= rows)).astype(F32), red_ab)
        + mm_exact((same & (cols < rows)).astype(F32), red_v)
        + red_t
    )
    d_step = red_u - d_rate * decay_rate
    d_dt = d_step * sigmoid(shifted)
    dx_ref[:, inner + 2 * STATE :] = d_dt.astype(BF16)
    hacc_ref[0:8, :] += fold(d_dt)
    hacc_ref[8:16, :] += fold(d_rate * (-decay_rate * step))
    dpre[Q : Q + 8, :] = dpre[0:8, :]
    halo_out[...] = dpre[0:8, :]
    state_out[...] = dstate[...]


def load_blocks(offsets_ref, parts, whole, sems):
    @pl.when(pl.program_id(0) == 0)
    def _():
        copies = []
        count = sems.shape[0]
        size = whole.shape[0] // count
        for part in parts:
            for j in range(part.shape[0] // size):
                k = len(copies)
                start = pl.multiple_of(offsets_ref[k], 32) if count > 1 else 0
                source = part.at[pl.ds(j * size, size), :]
                copies.append(pltpu.make_async_copy(source, whole.at[pl.ds(start, size), :], sems.at[k]))
        for copy in copies:
            copy.start()
        for copy in copies:
            copy.wait()


def turn_rows(offsets_ref, me_ref, own_ref, other_ref, out_ref, turned):
    depth = own_ref.shape[1]
    rows = own_ref.shape[0]
    for index, source in enumerate((own_ref, other_ref)):
        at = pl.multiple_of(jnp.where(index == 0, me_ref[0], 1 - me_ref[0]) * rows, LANES)
        for lo in range(0, rows, Q):
            tile = source[lo : lo + Q, :].astype(F32)
            scale = lax.rsqrt(jnp.mean(tile * tile, axis=1, keepdims=True) + EPSILON)
            tile = tile * scale
            for left in range(0, depth, LANES):
                turned[left : left + LANES, pl.ds(at + lo, Q)] = tile[:, left : left + LANES].T.astype(BF16)
    count = offsets_ref.shape[0]
    size = depth // count
    for k in range(count):
        start = pl.multiple_of(offsets_ref[k], 32)
        out_ref[k * size : (k + 1) * size, :] = turned[pl.ds(start, size), :]


def unpack_small(count, heads, offsets_ref, place_ref, *refs):
    parts, (small_ref, taps_ref, gain_ref, sems) = refs[:count], refs[count:]
    load_blocks(offsets_ref, parts, small_ref, sems)
    spare = small_ref[:, 2 * STATE :]
    depth = small_ref.shape[0]
    lanes = iota((depth, LANES), 1)
    width = taps_ref.shape[1]
    for lo in range(0, width, LANES):
        if lo < width - 2 * STATE:
            wanted, row = place_ref[:, :LANES] == lanes + lo, heads
        else:
            wanted, row = place_ref[:, LANES:] == lanes + (lo - (width - 2 * STATE)), heads + 8
        moved = mm(spare, jnp.where(wanted, 1.0, 0.0).astype(BF16), TN)
        taps_ref[:, lo : lo + LANES] = moved[row : row + 8, :]
    pick = jnp.where(iota((8, LANES), 1) == heads + K + 2, 1.0, 0.0).astype(BF16)
    gain_ref[...] = mm(pick, spare, NT)


def project(count, offsets_ref, me_ref, own_ref, other_ref, gain_ref, small_w_ref, *refs):
    blocks, (x_ref, small_ref, normed_ref, w_ref, sems) = refs[:count], refs[count:]
    load_blocks(offsets_ref, blocks, w_ref, sems)
    inner = x_ref.shape[1]
    tile = 256
    rows = jnp.where(pl.program_id(0) == me_ref[0], own_ref[...], other_ref[...]).astype(F32)
    scale = lax.rsqrt(jnp.mean(rows * rows, axis=1, keepdims=True) + EPSILON)
    rows = (rows * scale * gain_ref[0:1, :]).astype(BF16)
    normed_ref[...] = rows
    for lo in range(0, inner, tile):
        x_ref[:, lo : lo + tile] = mm(rows, w_ref[:, lo : lo + tile]).astype(BF16)
    small_ref[...] = mm(rows, small_w_ref[...])


def row_sums(lanes):
    return mm_exact(jnp.ones((8, LANES), F32), lanes, NT)


def spread_rows(values):
    pick = jnp.where(iota((8, LANES), 0) == 0, 1.0, 0.0).astype(F32)
    return mm_exact(values, pick, TN)


def gate_forward(normed_ref, y_ref, gain_ref, w_ref, z_ref, gg_ref, sq_ref):
    width = w_ref.shape[1]
    tile = 256
    rows = normed_ref[...]
    square = jnp.zeros((rows.shape[0], LANES), F32)
    for lo in range(0, width, tile):
        span = slice(lo, lo + tile)
        z = mm(rows, w_ref[:, span])
        z_b = z.astype(BF16)
        z_ref[:, span] = z_b
        z = z_b.astype(F32)
        gated = y_ref[:, span].astype(F32) * (z * sigmoid(z))
        gg_ref[:, span] = (gated * gain_ref[K + 1 : K + 2, span]).astype(BF16)
        twice = gated * gated
        for part in range(0, tile, LANES):
            square = square + twice[:, part : part + LANES]
    sq_ref[...] = row_sums(square)


def out_pair(ends_ref, me_ref, gg_ref, own_ref, other_ref, w_ref, u_ref, ds_ref, prod_ref):
    width = w_ref.shape[0]
    tile = 256
    step = pl.program_id(0)
    gg = gg_ref[...]
    rows = gg.shape[0]
    cot = jnp.where(step == me_ref[0], own_ref[...], other_ref[...])
    live = (iota((rows, LANES), 0) + step * rows < ends_ref[ends_ref.shape[0] - 1]).astype(F32)
    product = jnp.zeros((gg.shape[0], LANES), F32)
    for lo in range(0, width, tile):
        span = slice(lo, lo + tile)
        u = mm(gg, w_ref[span, :], NT)
        u_ref[:, span] = u.astype(BF16)
        term = u * cot[:, span].astype(F32)
        for part in range(0, tile, LANES):
            product = product + term[:, part : part + LANES]
        wide = jnp.concatenate([live] * (tile // LANES), axis=1)
        ds_ref[:, span] = (mm(cot, w_ref[:, span]) * wide).astype(BF16)
    prod_ref[...] = row_sums(product * live)


def gate_backward(ds_ref, y_ref, z_ref, rg_ref, coef_ref, gain_ref, dy_ref, dz_ref, acc_ref):
    @pl.when(pl.program_id(0) == 0)
    def _():
        acc_ref[...] = jnp.zeros(acc_ref.shape, F32)

    rg = spread_rows(rg_ref[...])
    coef = spread_rows(coef_ref[...])
    count = rg.shape[0]
    for lo in range(0, ds_ref.shape[1], LANES):
        span = slice(lo, lo + LANES)
        z = z_ref[:, span].astype(F32)
        y = y_ref[:, span].astype(F32)
        gate = sigmoid(z)
        silu = z * gate
        gated = y * silu
        d_normal = ds_ref[:, span].astype(F32) * rg
        acc_ref[:, span] += (d_normal * gated).reshape(count // 8, 8, LANES).sum(axis=0)
        d_gated = d_normal * gain_ref[K + 1 : K + 2, span] - gated * coef
        dy_ref[:, span] = (d_gated * silu).astype(BF16)
        dz_ref[:, span] = (d_gated * y * (gate + silu * (1.0 - gate))).astype(BF16)


def normed_back(count, offsets_ref, dz_ref, dx_ref, wz_ref, small_w_ref, *refs):
    blocks, (out_ref, wx_ref, sems) = refs[:count], refs[count:]
    load_blocks(offsets_ref, blocks, wx_ref, sems)
    inner = wx_ref.shape[1]
    dz = dz_ref[...]
    dx = dx_ref[:, :inner]
    ds = dx_ref[:, inner:]
    tile = 256
    for lo in range(0, wz_ref.shape[0], tile):
        span = slice(lo, lo + tile)
        total = mm(dz, wz_ref[span, :], NT) + mm(dx, wx_ref[span, :], NT) + mm(ds, small_w_ref[span, :], NT)
        out_ref[:, span] = total.astype(BF16)


def params():
    return pltpu.CompilerParams(dimension_semantics=("arbitrary",), vmem_limit_bytes=VMEM_LIMIT)


SMALL_COST = pl.CostEstimate(flops=1000, bytes_accessed=1000, transcendentals=0)


def rows_spec(block, width, column=0):
    return pl.BlockSpec((block, width), lambda i: (i, column))


def whole_spec(shape, column=0):
    return pl.BlockSpec(shape, lambda i: (0, column))


def local(
    tokens,
    cotangent,
    lengths,
    norm_gain,
    w_zx,
    w_bc,
    w_dt,
    conv_x,
    conv_x_bias,
    conv_bc,
    conv_bc_bias,
    dt_bias,
    a_log,
    d_skip,
    gate_gain,
    w_out,
):
    n_t = lax.axis_size("tensor")
    n_dp = lax.axis_size("dp")
    me_t = lax.axis_index("tensor")
    me_dp = lax.axis_index("dp")
    own_rows, depth = tokens.shape
    group = own_rows * n_t
    chunks = group // Q
    heads = dt_bias.shape[0]
    inner = heads * WIDTH
    inner_total = inner * n_t
    shard = w_zx.shape[1]
    pairs = [(i, n_t - 1 - i) for i in range(n_t)]

    def swap(v):
        return lax.ppermute(v, "tensor", pairs)

    def in_order(mine, other, axis=0):
        low = jnp.where(me_t == 0, mine, other)
        high = jnp.where(me_t == 0, other, mine)
        return jnp.concatenate([low, high], axis=axis)

    def sum_dp(v):
        step = 1
        while step < n_dp:
            v = v + lax.ppermute(v, "dp", [(i, i ^ step) for i in range(n_dp)])
            step *= 2
        return v

    def after(value, *others):
        return lax.optimization_barrier((value, *others))[0]

    ring = 4
    plane = n_dp // (2 * ring)

    around = [(i, (i + 2 * plane) % n_dp) for i in range(n_dp)]
    across = [(i, i ^ 2) for i in range(n_dp)]
    beside = [(i, i ^ 1) for i in range(n_dp)]

    def send(v, way):
        return lax.ppermute(v, "dp", way)

    by_hand = plane == 2 and shard % 32 == 0

    def whole(v):
        return [lax.all_gather(v, "dp", axis=0, tiled=True)]

    def block_offsets(count, size):
        if count == 1:
            return jnp.zeros((1,), jnp.int32)
        places = []
        for core in range(2):
            for side in range(2):
                for turn in range(ring):
                    level = (me_dp // (2 * plane) - turn + ring) % ring
                    places.append(level * (2 * plane) + ((me_dp % (2 * plane)) ^ (2 * side + core)))
        return jnp.stack(places).astype(jnp.int32) * size

    def relative_order():
        level, side, core = me_dp // 4, (me_dp // 2) % 2, me_dp % 2
        order = []
        for dc in (1, 0):
            for dy in (1, 0):
                for dz in range(1, ring + 1):
                    order.append(((level - dz + ring) % ring) * 4 + (side ^ dy) * 2 + (core ^ dc))
        return order

    def fold_beside(keep, got):
        half = keep.shape[0] // 2
        away = (keep[:half].astype(F32) + got[:half].astype(F32)).astype(BF16)
        return away, keep[half:].astype(F32) + got[half:].astype(F32)

    def fold_turn(total, got, turn):
        part = total[(turn - 1) * shard : turn * shard] + got.astype(F32)
        return part if turn == ring else part.astype(BF16)

    ends = jnp.cumsum(lengths[0]).astype(jnp.int32)
    live = (lax.iota(jnp.int32, group) < ends[-1]).astype(F32)
    live_own = lax.dynamic_slice_in_dim(live, me_t * own_rows, own_rows, 0)
    me = me_t.astype(jnp.int32).reshape(1)

    span_p = conv_x_bias.shape[1]
    span_n = conv_bc_bias.shape[1]
    w_x = w_zx[1]
    other_gain, other_bc, other_taps, other_bias = [swap(v) for v in (norm_gain, w_bc, conv_bc, conv_bc_bias)]
    gain_pair = in_order(norm_gain, other_gain)[:, None]
    taps_bc = in_order(conv_bc.reshape(2, span_n, K), other_taps.reshape(2, span_n, K), axis=1)
    bias_bc = in_order(conv_bc_bias, other_bias, axis=1)[:, :, None]
    spare_bc = jnp.concatenate([taps_bc, bias_bc], axis=2).reshape(4 * span_n, K + 1)
    spare_x = [conv_x.reshape(shard, K), conv_x_bias.reshape(shard, 1), gate_gain.reshape(shard, 1), gain_pair]
    bc_pair = in_order(w_bc, other_bc, axis=1)
    w_small = jnp.concatenate(
        [bc_pair[0], bc_pair[1], w_dt, *spare_x, jnp.zeros((shard, 8 - K - 3), BF16)]
        + [jnp.pad(spare_bc, ((0, shard - 4 * span_n), (0, LANES - heads - 8 - K - 1)))],
        axis=1,
    )
    gain_pair = gain_pair.astype(F32)
    where = lax.iota(jnp.int32, depth)
    home, inside = where // shard, where % shard
    place_x = (inside // span_p) * WIDTH + home * span_p + inside % span_p
    half_n = 2 * span_n
    place_bc = (inside // half_n) * STATE + home * half_n + inside % half_n
    place = jnp.concatenate([jnp.broadcast_to(v[:, None], (depth, LANES)) for v in (place_x, place_bc)], axis=1)
    par = jnp.concatenate([dt_bias[None], a_log[None], jnp.zeros((6, heads), F32)], axis=0)
    par = jnp.concatenate([par, jnp.zeros((8, LANES - heads), F32)], axis=1)
    skip = jnp.repeat(d_skip, WIDTH)[None]
    members = lax.iota(jnp.int32, inner)[:, None] // WIDTH
    sel = (members == lax.iota(jnp.int32, LANES)[None, :]).astype(BF16)
    smem = pl.BlockSpec(memory_space=pltpu.SMEM)
    vmem = pl.BlockSpec(memory_space=pltpu.VMEM)
    hbm = pl.BlockSpec(memory_space=pl.ANY)
    n_small = 2 * STATE + LANES
    n_conv = inner + 2 * STATE

    other_tokens = swap(tokens)
    w_rest = jnp.concatenate([w_zx[0], w_out.T], axis=1)

    def turn():
        return pl.pallas_call(
            turn_rows,
            in_specs=[smem, smem, vmem, vmem],
            out_specs=vmem,
            out_shape=jax.ShapeDtypeStruct((depth, group), BF16),
            scratch_shapes=[pltpu.VMEM((depth, group), BF16)],
            compiler_params=pltpu.CompilerParams(vmem_limit_bytes=VMEM_LIMIT),
            cost_estimate=SMALL_COST,
            name="turn_rows",
        )((jnp.stack(relative_order()) * shard).astype(jnp.int32), me, tokens, other_tokens)

    if by_hand:
        line, other, line_c, other_c = [w_x], [], [], []
        small_parts = []
        for step in range(ring + 1):
            made = []
            if step < ring - 1:
                made.append((line, send(line[step], around)))
            if step < ring:
                made.append((other, send(line[step], across)))
                made.append((line_c, send(line[step], beside)))
            if step:
                made.append((other_c, send(other[step - 1], beside)))
            if step == 0:
                made.append(([], w_small))
            if step == 1:
                w_rest = after(w_rest, line[1])
                zo_all = lax.all_gather(w_rest, "dp", axis=0, tiled=True)
                w_small = after(w_small, line[1])
                shifts = [[(i, (i + 2 * plane * k) % n_dp) for i in range(n_dp)] for k in range(1, ring)]
                small_line = [send(w_small, shift) for shift in shifts]
                made += [(small_line, None)]
                made = made[:-1] + [(small_parts, value) for value in small_line]
            if step == 2:
                small_parts = [jnp.concatenate([w_small] + small_parts, axis=0)]
                made.append((small_parts, send(small_parts[0], across)))
                held_turn = []
                made.append((held_turn, after(turn(), line[2])))
                other_cot = swap(after(cotangent, other_tokens))
            if step == 3:
                made.append((small_parts, send(jnp.concatenate(small_parts, axis=0), beside)))
            fresh = lax.optimization_barrier(tuple(value for _, value in made))
            for (place_in, _), value in zip(made, fresh):
                place_in.append(value)
        wx_blocks = line + other + line_c + other_c
        turned = held_turn[0]
    else:
        wx_blocks, small_parts = whole(w_x), whole(w_small)
        zo_all = whole(w_rest)[0]
        other_cot = swap(cotangent)
    count = len(wx_blocks)
    offsets = block_offsets(count, shard)
    sems = pltpu.SemaphoreType.DMA((count,))
    w_small_all, taps, gain_in = pl.pallas_call(
        partial(unpack_small, len(small_parts), heads),
        grid=(1,),
        in_specs=[smem, whole_spec((depth, 2 * LANES))] + [hbm] * len(small_parts),
        out_specs=[whole_spec((depth, n_small)), whole_spec((8, n_conv)), whole_spec((8, depth))],
        out_shape=[
            jax.ShapeDtypeStruct((depth, n_small), BF16),
            jax.ShapeDtypeStruct((8, n_conv), F32),
            jax.ShapeDtypeStruct((8, depth), F32),
        ],
        scratch_shapes=[sems],
        compiler_params=params(),
        cost_estimate=SMALL_COST,
        name="unpack_small",
    )(offsets, place, *small_parts)
    tok_own = tokens.astype(F32)
    inv_tok = lax.rsqrt(jnp.mean(tok_own * tok_own, axis=1, keepdims=True) + EPSILON)

    block = own_rows
    steps = group // block
    x_raw, small, normed = pl.pallas_call(
        partial(project, count),
        grid=(steps,),
        in_specs=[
            smem,
            smem,
            whole_spec((block, depth)),
            whole_spec((block, depth)),
            whole_spec((8, depth)),
            whole_spec((depth, n_small)),
        ]
        + [hbm] * count,
        out_specs=[rows_spec(block, inner), rows_spec(block, n_small), rows_spec(block, depth)],
        out_shape=[
            jax.ShapeDtypeStruct((group, inner), BF16),
            jax.ShapeDtypeStruct((group, n_small), F32),
            jax.ShapeDtypeStruct((group, depth), BF16),
        ],
        scratch_shapes=[pltpu.VMEM((depth, inner), BF16), sems],
        compiler_params=params(),
        cost_estimate=SMALL_COST,
        name="project",
    )(offsets, me, tokens, other_tokens, gain_in, w_small_all, *wx_blocks)
    xc, pre, bc, y_all, states = pl.pallas_call(
        partial(scan_forward, heads),
        grid=(chunks,),
        in_specs=[
            smem,
            rows_spec(Q, inner),
            rows_spec(Q, n_small),
            whole_spec((8, n_conv)),
            whole_spec((8, LANES)),
            whole_spec((1, inner)),
        ],
        out_specs=[
            rows_spec(Q, inner),
            rows_spec(Q, n_conv),
            rows_spec(Q, 2 * STATE),
            rows_spec(Q, inner),
            pl.BlockSpec((1, STATE, inner), lambda i: (i, 0, 0)),
        ],
        out_shape=[
            jax.ShapeDtypeStruct((group, inner), BF16),
            jax.ShapeDtypeStruct((group, n_conv), BF16),
            jax.ShapeDtypeStruct((group, 2 * STATE), BF16),
            jax.ShapeDtypeStruct((group, inner), BF16),
            jax.ShapeDtypeStruct((chunks, STATE, inner), BF16),
        ],
        scratch_shapes=[pltpu.VMEM((Q + 8, n_conv), F32), pltpu.VMEM((STATE, inner), F32)],
        compiler_params=params(),
        cost_estimate=SMALL_COST,
        name="scan_forward",
    )(ends, x_raw, small, taps, par, skip)

    row8 = pl.BlockSpec((8, block), lambda i: (0, i))
    z_all, gg, sq = pl.pallas_call(
        gate_forward,
        grid=(steps,),
        in_specs=[
            rows_spec(block, depth),
            rows_spec(block, inner),
            whole_spec((8, inner)),
            whole_spec((depth, inner), 0),
        ],
        out_specs=[rows_spec(block, inner), rows_spec(block, inner), row8],
        out_shape=[
            jax.ShapeDtypeStruct((group, inner), BF16),
            jax.ShapeDtypeStruct((group, inner), BF16),
            jax.ShapeDtypeStruct((8, group), F32),
        ],
        compiler_params=params(),
        cost_estimate=SMALL_COST,
        name="gate_forward",
    )(normed, y_all, taps, zo_all)
    sq_all = sq + swap(sq)

    u_part, d_scaled, prod = pl.pallas_call(
        out_pair,
        grid=(steps,),
        in_specs=[
            smem,
            smem,
            rows_spec(block, inner),
            whole_spec((block, depth)),
            whole_spec((block, depth)),
            whole_spec((depth, inner), 1),
        ],
        out_specs=[rows_spec(block, depth), rows_spec(block, inner), row8],
        out_shape=[
            jax.ShapeDtypeStruct((group, depth), BF16),
            jax.ShapeDtypeStruct((group, inner), BF16),
            jax.ShapeDtypeStruct((8, group), F32),
        ],
        compiler_params=params(),
        cost_estimate=SMALL_COST,
        name="out_pair",
    )(ends, me, gg, cotangent, other_cot, zo_all)
    prod_all = prod + swap(prod)
    inv_gate8 = lax.rsqrt(sq_all / inner_total + EPSILON)
    inv_gate = inv_gate8[0]
    cot_all = in_order(cotangent, other_cot)

    u_own = lax.dynamic_slice_in_dim(u_part, me_t * own_rows, own_rows, 0)
    u_send = lax.dynamic_slice_in_dim(u_part, (n_t - 1 - me_t) * own_rows, own_rows, 0)
    u_recv = swap(u_send)
    inv_own = lax.dynamic_slice_in_dim(inv_gate, me_t * own_rows, own_rows, 0)
    branch = (u_own.astype(F32) + u_recv.astype(F32)) * (inv_own * live_own)[:, None]
    layer_out = (tokens.astype(F32) + branch).astype(BF16)

    d_branch = (cot_all.astype(F32) * (live * inv_gate)[:, None]).astype(BF16)
    g_out = lax.dot_general(d_branch, gg, TN, preferred_element_type=F32).astype(BF16)
    grad_out = lax.psum_scatter(g_out, "dp", scatter_dimension=0, tiled=True)

    coef8 = inv_gate8 * inv_gate8 * inv_gate8 * (prod_all / inner_total)
    dy, dz, gain_acc = pl.pallas_call(
        gate_backward,
        grid=(steps,),
        in_specs=[
            rows_spec(block, inner),
            rows_spec(block, inner),
            rows_spec(block, inner),
            row8,
            row8,
            whole_spec((8, inner)),
        ],
        out_specs=[rows_spec(block, inner), rows_spec(block, inner), whole_spec((8, inner))],
        out_shape=[
            jax.ShapeDtypeStruct((group, inner), BF16),
            jax.ShapeDtypeStruct((group, inner), BF16),
            jax.ShapeDtypeStruct((8, inner), F32),
        ],
        compiler_params=params(),
        cost_estimate=SMALL_COST,
        name="gate_backward",
    )(d_scaled, y_all, z_all, inv_gate8, coef8, taps)
    dot = partial(lax.dot_general, preferred_element_type=F32)
    if by_hand:
        front = depth // 2
        g_send = dot(turned[:front], dz, NN).astype(BF16)
        z_keep = dot(turned[front:], after(dz, g_send), NN).astype(BF16)
        z_got = send(g_send, beside)
        dy = after(dy, z_keep, g_send)
    else:
        grad_z = lax.psum_scatter(dot(normed, dz, TN).astype(BF16), "dp", scatter_dimension=0, tiled=True)

    def backward(top, number, carry):
        back = lambda width: pl.BlockSpec((Q, width), lambda i: (top - i, 0))
        operands = [ends, dy, xc, pre, x_raw, small, bc, states, taps, par, skip, sel, *carry]
        return pl.pallas_call(
            partial(scan_backward, heads, chunks, top),
            grid=(number,),
            in_specs=[
                smem,
                back(inner),
                back(inner),
                back(n_conv),
                back(inner),
                back(n_small),
                back(2 * STATE),
                pl.BlockSpec((1, STATE, inner), lambda i: (top - i, 0, 0)),
                whole_spec((8, n_conv)),
                whole_spec((8, LANES)),
                whole_spec((1, inner)),
                whole_spec((inner, LANES)),
            ]
            + ([whole_spec((STATE, inner)), whole_spec((8, n_conv)), hbm] if carry else []),
            out_specs=[
                back(inner + n_small),
                whole_spec((8 * (K + 2), n_conv)),
                whole_spec((16, LANES)),
                whole_spec((STATE, inner)),
                whole_spec((8, n_conv)),
            ],
            out_shape=[
                jax.ShapeDtypeStruct((group, inner + n_small), BF16),
                jax.ShapeDtypeStruct((8 * (K + 2), n_conv), F32),
                jax.ShapeDtypeStruct((16, LANES), F32),
                jax.ShapeDtypeStruct((STATE, inner), F32),
                jax.ShapeDtypeStruct((8, n_conv), F32),
            ],
            scratch_shapes=[
                pltpu.VMEM((STATE, inner), F32),
                pltpu.VMEM((Q + 8, n_conv), F32),
                pltpu.VMEM((Q, inner), BF16),
                pltpu.VMEM((Q, inner), BF16),
                pltpu.VMEM((Q, inner), BF16),
                pltpu.VMEM((Q, inner), BF16),
                pltpu.VMEM((Q, inner), BF16),
                pltpu.VMEM((Q, inner), BF16),
                pltpu.VMEM((STATE, inner), BF16),
                pltpu.VMEM((8, inner), F32),
            ],
            input_output_aliases={len(operands) - 1: 0} if carry else {},
            compiler_params=params(),
        cost_estimate=SMALL_COST,
            name="scan_backward",
        )(*operands)

    half_chunks = chunks // 2
    dx, acc_a, hacc_a, d_state, halo = backward(chunks - 1, chunks - half_chunks, ())
    if by_hand:
        z_got, dx = lax.optimization_barrier((z_got, dx))
        z_away, z_keep = fold_beside(z_keep, z_got)
        z_got = send(z_away, across)
        d_state = after(d_state, z_away, z_keep)
    dx, acc, hacc, _, _ = backward(half_chunks - 1, half_chunks, (d_state, halo, dx))
    acc = acc + acc_a
    hacc = hacc + hacc_a
    dx = after(dx, u_recv)

    acc = acc.reshape(K + 2, 8, n_conv).sum(axis=1)
    hsum = hacc.reshape(2, 8, LANES).sum(axis=1)
    d_gate = gain_acc.sum(axis=0)
    d_sk = acc[K + 1, :inner].reshape(heads, WIDTH).sum(axis=1)
    shared = acc[: K + 1, inner:]
    headed = [acc[: K + 1, :inner].reshape(-1), d_gate, hsum[:, :heads].reshape(-1), d_sk]
    shared_got = swap(shared)
    n_x = 1024

    if by_hand:
        z_got, dx = lax.optimization_barrier((z_got, dx))
        z_total = z_keep + z_got.astype(F32)
        z_away = z_total[:shard].astype(BF16)
        z_got = send(z_away, around)
        dx = after(dx, z_away, z_total)
        d_late = dx[:, n_x:]
        g_send = dot(turned[:front], d_late, NN).astype(BF16)
        x_got = send(g_send, beside)
        g_x = dot(normed, after(dx, g_send)[:, :n_x], TN).astype(BF16)
        grad_x = lax.psum_scatter(g_x, "dp", scatter_dimension=0, tiled=True)
        x_keep = dot(turned[front:], after(dx, g_x)[:, n_x:], NN).astype(BF16)
        x_got, x_keep, z_got = lax.optimization_barrier((x_got, x_keep, z_got))
        x_away, x_keep = fold_beside(x_keep, x_got)
        x_got = send(x_away, across)
        z_away = fold_turn(z_total, z_got, 2)
        z_got = send(z_away, around)
        dz = after(dz, x_away, x_keep, z_away)
    else:
        grad_x = lax.psum_scatter(dot(normed, dx, TN).astype(BF16), "dp", scatter_dimension=0, tiled=True)

    vector = jnp.concatenate([(shared + shared_got).reshape(-1)] + headed)
    vector = jnp.concatenate([vector, jnp.zeros((-vector.shape[0] % 1024,), F32)]).reshape(-1, LANES)

    d_normed = pl.pallas_call(
        partial(normed_back, count),
        grid=(steps,),
        in_specs=[
            smem,
            rows_spec(block, inner),
            rows_spec(block, inner + n_small),
            whole_spec((depth, inner), 0),
            whole_spec((depth, n_small)),
        ]
        + [hbm] * count,
        out_specs=rows_spec(block, depth),
        out_shape=jax.ShapeDtypeStruct((group, depth), BF16),
        scratch_shapes=[
            pltpu.VMEM((depth, inner), BF16),
            sems,
        ],
        compiler_params=params(),
        cost_estimate=SMALL_COST,
        name="normed_back",
    )(offsets, dz, dx, zo_all, w_small_all, *wx_blocks)
    dn_send = lax.dynamic_slice_in_dim(d_normed, (n_t - 1 - me_t) * own_rows, own_rows, 0)
    dn_own = lax.dynamic_slice_in_dim(d_normed, me_t * own_rows, own_rows, 0)
    if by_hand:
        x_got, z_got, vector, dn_send = lax.optimization_barrier((x_got, z_got, vector, dn_send))
        x_total = x_keep + x_got.astype(F32)
        x_got = x_total[:shard].astype(BF16)
        z_got = fold_turn(z_total, z_got, 3)
        dn_got = []
        for turn in range(2, ring + 1):
            moved = [send(x_got, around), send(vector, [(i, i ^ (1 << (turn - 2))) for i in range(n_dp)])]
            if turn == 2:
                moved.append(swap(dn_send[: own_rows // 2]))
                moved.append(send(z_got, around))
            if turn == 3:
                moved.append(swap(dn_send[own_rows // 2 :]))
            moved = lax.optimization_barrier(tuple(moved))
            x_got = fold_turn(x_total, moved[0], turn)
            vector = vector + moved[1]
            dn_got += moved[2:3]
            if turn == 2:
                grad_z = fold_turn(z_total, moved[3], ring) * gain_pair
        dn_got = jnp.concatenate(dn_got, axis=0)
        vector = vector + send(vector, [(i, i ^ 8) for i in range(n_dp)])
        grad_x = jnp.concatenate([grad_x.astype(F32), x_got * gain_pair], axis=1)
    else:
        vector = sum_dp(vector)
        dn_got = swap(dn_send)
    dn = (dn_own.astype(F32) + dn_got.astype(F32)) * gain_in[0:1, :]
    grad_tokens = (
        cotangent.astype(F32)
        + inv_tok * dn
        - tok_own * inv_tok * inv_tok * inv_tok * jnp.mean(dn * tok_own, axis=1, keepdims=True)
    )

    vector = vector.reshape(-1)
    n_bc = (K + 1) * 2 * STATE
    bc_sum = vector[:n_bc].reshape(K + 1, 2, STATE)
    me_all = me_dp * n_t + me_t
    bc_sum = lax.dynamic_slice_in_dim(bc_sum, me_all * span_n, span_n, 2)
    grad_bc_taps = bc_sum[:K].transpose(1, 2, 0).reshape(conv_bc.shape)
    grad_bc_bias = bc_sum[K]
    at = n_bc
    x_sum = vector[at : at + (K + 1) * inner].reshape(K + 1, heads, WIDTH)
    at += (K + 1) * inner
    x_sum = lax.dynamic_slice_in_dim(x_sum, me_dp * span_p, span_p, 2)
    grad_x_taps = x_sum[:K].transpose(1, 2, 0).reshape(conv_x.shape)
    grad_x_bias = x_sum[K]
    grad_gate = lax.dynamic_slice_in_dim(vector[at : at + inner].reshape(heads, WIDTH), me_dp * span_p, span_p, 1)
    at += inner
    grad_dt_bias = vector[at : at + heads]
    grad_a_log = vector[at + heads : at + 2 * heads]
    grad_skip = vector[at + 2 * heads : at + 3 * heads]

    grad_z = grad_z.astype(F32)
    grad_x = grad_x.astype(F32)
    in_part = jnp.sum(w_zx[0].astype(F32) * grad_z, axis=1) + jnp.sum(w_x.astype(F32) * grad_x[:, :inner], axis=1)
    in_part = (in_part + jnp.sum(w_small.astype(F32) * grad_x[:, inner:], axis=1))[:, None]
    grad_zx = jnp.stack([grad_z, grad_x[:, :inner]])
    grad_dt = grad_x[:, inner + 2 * STATE : inner + 2 * STATE + heads]
    bc_part = jnp.concatenate([grad_x[:, inner : inner + 2 * STATE], jnp.broadcast_to(in_part, (shard, LANES))], axis=1)
    half = w_bc.shape[1]
    bc_own = lax.dynamic_slice_in_dim(bc_part, me_t * half, half, 0)
    bc_send = lax.dynamic_slice_in_dim(bc_part, (n_t - 1 - me_t) * half, half, 0)
    bc_total = bc_own + swap(bc_send)
    own_gain = norm_gain.astype(F32)
    grad_bc = bc_total[:, : 2 * STATE].reshape(half, 2, STATE).transpose(1, 0, 2)
    grad_in = bc_total[:, 2 * STATE] / own_gain
    return (
        layer_out,
        grad_tokens,
        grad_in,
        grad_zx,
        grad_bc,
        grad_dt,
        grad_x_taps,
        grad_x_bias,
        grad_bc_taps,
        grad_bc_bias,
        grad_dt_bias,
        grad_a_log,
        grad_skip,
        grad_gate,
        grad_out.astype(F32).T,
    )


def solution(mesh):
    both = ("dp", "tensor")
    in_specs = (
        P(both, None),
        P(both, None),
        P("dp", None),
        P(both),
        P(None, "dp", "tensor"),
        P(None, both, None),
        P("dp", "tensor"),
        P("tensor", "dp"),
        P("tensor", "dp"),
        P(None, both),
        P(None, both),
        P("tensor"),
        P("tensor"),
        P("tensor"),
        P("tensor", "dp"),
        P("tensor", "dp"),
    )
    out_specs = (
        P(both, None),
        P(both, None),
        P(both),
        P(None, "dp", "tensor"),
        P(None, both, None),
        P("dp", "tensor"),
        P("tensor", "dp"),
        P("tensor", "dp"),
        P(None, both),
        P(None, both),
        P("tensor"),
        P("tensor"),
        P("tensor"),
        P("tensor", "dp"),
        P("tensor", "dp"),
    )
    return jax.shard_map(local, mesh=mesh, in_specs=in_specs, out_specs=out_specs, check_vma=False)
```

```python
from functools import partial

import jax
import jax.numpy as jnp
from jax import lax
from jax.experimental import pallas as pl
from jax.experimental.pallas import tpu as pltpu
from jax.sharding import PartitionSpec as P

EPSILON = 1e-05
HIGHEST = lax.Precision.HIGHEST
K = 4
WIDTH = 64
STATE = 128
Q = 128
LANES = 128
LOG2E = 1.4426950408889634
VMEM_LIMIT = 60 * 1024 * 1024
F32 = jnp.float32
BF16 = jnp.bfloat16

NN = (((1,), (0,)), ((), ()))
NT = (((1,), (1,)), ((), ()))
TN = (((0,), (0,)), ((), ()))


def mm(a, b, dims=NN):
    return lax.dot_general(a, b, dims, preferred_element_type=F32)


def mm_exact(a, b, dims=NN):
    return lax.dot_general(a, b, dims, preferred_element_type=F32, precision=HIGHEST)


def iota(shape, dim):
    return lax.broadcasted_iota(jnp.int32, shape, dim)


def segment_of(rows, ends_ref, count):
    total = (rows >= ends_ref[0]).astype(jnp.int32)
    for j in range(1, count):
        total = total + (rows >= ends_ref[j]).astype(jnp.int32)
    return total


def scalar_segment(row, ends_ref, count):
    total = jnp.where(row >= ends_ref[0], 1, 0)
    for j in range(1, count):
        total = total + jnp.where(row >= ends_ref[j], 1, 0)
    return total


def sigmoid(v):
    return 0.5 * jnp.tanh(0.5 * v) + 0.5


def softplus(v):
    return jnp.maximum(v, 0.0) + jnp.log1p(jnp.exp(-jnp.abs(v)))


def chunk_masks(chunk, ends_ref, count):
    base = chunk * Q
    rows = iota((Q, Q), 0) + base
    cols = iota((Q, Q), 1) + base
    row_ids = segment_of(rows, ends_ref, count)
    col_ids = segment_of(cols, ends_ref, count)
    same = row_ids == col_ids
    before_id = jnp.where(chunk == 0, -1, scalar_segment(base - 1, ends_ref, count))
    final_id = scalar_segment(base + Q - 1, ends_ref, count)
    carry = (row_ids == before_id).astype(F32)
    last = (row_ids == final_id).astype(F32)
    passing = jnp.where(before_id == final_id, 1.0, 0.0).astype(F32)
    return rows, cols, row_ids, same, carry, last, passing


def decays(dt_raw, par_ref):
    shifted = dt_raw + par_ref[0:1, :]
    step = softplus(shifted)
    decay_rate = jnp.exp(par_ref[1:2, :])
    return shifted, step, decay_rate


def pair_columns(values, pair, first):
    left = jnp.broadcast_to(values[:, 2 * pair : 2 * pair + 1], (Q, LANES))
    right = jnp.broadcast_to(values[:, 2 * pair + 1 : 2 * pair + 2], (Q, LANES))
    return left, right, jnp.where(first, left, right)


def scan_forward(
    heads, ends_ref, xr_ref, small_ref, taps_ref, par_ref, skip_ref,
    xc_ref, pre_ref, bc_ref, y_ref, st_ref, buf, state,
):
    count = ends_ref.shape[0]
    inner = heads * WIDTH
    chunk = pl.program_id(0)

    @pl.when(chunk == 0)
    def _():
        buf[0:8, :] = jnp.zeros((8, buf.shape[1]), F32)
        state[...] = jnp.zeros(state.shape, F32)

    rows, cols, row_ids, same, carry, last, passing = chunk_masks(chunk, ends_ref, count)
    causal = rows >= cols
    visible = same & causal
    lag_mask = [None]
    for lag in range(1, K):
        earlier = rows - lag
        keep = (segment_of(earlier, ends_ref, count) == row_ids) & (earlier >= 0)
        lag_mask.append(keep.astype(F32))

    small = small_ref[...]
    for lo in range(0, inner, LANES):
        buf[8 : 8 + Q, lo : lo + LANES] = xr_ref[:, lo : lo + LANES].astype(F32)
    buf[8 : 8 + Q, inner : inner + 2 * STATE] = small[:, : 2 * STATE]

    def convolve(lo):
        span = slice(lo, lo + LANES)
        pre = taps_ref[K : K + 1, span] + taps_ref[K - 1 : K, span] * buf[8 : 8 + Q, span]
        for lag in range(1, K):
            pre = pre + taps_ref[K - 1 - lag : K - lag, span] * (
                buf[8 - lag : 8 - lag + Q, span] * lag_mask[lag]
            )
        pre_ref[:, span] = pre.astype(BF16)
        return pre * sigmoid(pre)

    b_f = convolve(inner).astype(BF16).astype(F32)
    c_b = convolve(inner + STATE).astype(BF16)
    b_b = b_f.astype(BF16)
    bc_ref[:, :STATE] = b_b
    bc_ref[:, STATE:] = c_b
    b_t = b_f.T.astype(BF16)

    _, step, decay_rate = decays(small[:, 2 * STATE :], par_ref)
    csum = mm_exact(causal.astype(F32), step * (-LOG2E * decay_rate))
    csum_t = csum.T
    scores = jnp.where(visible, mm(c_b, b_b, NT), 0.0)
    first = iota((Q, LANES), 1) < WIDTH
    first_row = iota((1, LANES), 1) < WIDTH

    for pair in range(heads // 2):
        span = slice(pair * LANES, (pair + 1) * LANES)
        xc = convolve(pair * LANES).astype(BF16)
        xc_ref[:, span] = xc
        xc = xc.astype(F32)
        left, right, both = pair_columns(csum, pair, first)
        _, _, step_pair = pair_columns(step, pair, first)
        mix = jnp.concatenate(
            [
                (scores * jnp.exp2(jnp.minimum(left - csum_t[2 * pair : 2 * pair + 1, :], 0.0))).astype(BF16),
                (scores * jnp.exp2(jnp.minimum(right - csum_t[2 * pair + 1 : 2 * pair + 2, :], 0.0))).astype(BF16),
            ],
            axis=1,
        )
        fed = xc * step_pair
        fed_b = fed.astype(BF16)
        zero = jnp.zeros((Q, LANES), BF16)
        stacked = jnp.concatenate([jnp.where(first, fed_b, zero), jnp.where(first, zero, fed_b)], axis=0)
        held = state[:, span]
        held_b = held.astype(BF16)
        st_ref[0, :, span] = held_b
        y = mm(mix, stacked) + mm(c_b, held_b) * (jnp.exp2(both) * carry)
        y_ref[:, span] = (y + skip_ref[:, span] * xc).astype(BF16)
        closing = both[Q - 1 : Q, :]
        weighted = (fed_b.astype(F32) * (jnp.exp2(closing - both) * last)).astype(BF16)
        state[:, span] = held * (jnp.exp2(closing) * passing) + mm(b_t, weighted)

    buf[0:8, :] = buf[Q : Q + 8, :]


def scan_backward(
    heads, chunks, top, ends_ref, dy_ref, xc_ref, pre_ref, xr_ref, small_ref, bc_ref, st_ref, taps_ref, par_ref,
    skip_ref, sel_ref, *refs,
):
    if top + 1 < chunks:
        state_in, halo_in, _ = refs[:3]
        refs = refs[3:]
    dx_ref, acc_ref, hacc_ref, state_out, halo_out = refs[:5]
    dstate, dpre, ab_hi, ab_lo, v_b, u_b, dyd, fedw, dst_b, through = refs[5:]
    count = ends_ref.shape[0]
    inner = heads * WIDTH
    total_rows = chunks * Q
    chunk = top - pl.program_id(0)

    @pl.when(pl.program_id(0) == 0)
    def _():
        if top + 1 < chunks:
            dpre[Q : Q + 8, :] = halo_in[...]
            dstate[...] = state_in[...]
        else:
            dpre[Q : Q + 8, :] = jnp.zeros((8, dpre.shape[1]), F32)
            dstate[...] = jnp.zeros(dstate.shape, F32)
        acc_ref[...] = jnp.zeros(acc_ref.shape, F32)
        hacc_ref[...] = jnp.zeros(hacc_ref.shape, F32)

    rows, cols, row_ids, same, carry, last, passing = chunk_masks(chunk, ends_ref, count)
    causal = rows >= cols
    visible = same & causal
    lag_mask = [None]
    for lag in range(1, K):
        later = rows + lag
        keep = (segment_of(later, ends_ref, count) == row_ids) & (later < total_rows)
        lag_mask.append(keep.astype(F32))

    small = small_ref[...]
    shifted, step, decay_rate = decays(small[:, 2 * STATE :], par_ref)
    csum = mm_exact(causal.astype(F32), step * (-LOG2E * decay_rate))
    csum_t = csum.T
    b_b = bc_ref[:, :STATE]
    c_b = bc_ref[:, STATE:]
    c_t = c_b.astype(F32).T.astype(BF16)
    scores = jnp.where(visible, mm(c_b, b_b, NT), 0.0)
    first = iota((Q, LANES), 1) < WIDTH

    def fold(values):
        return values.reshape(Q // 8, 8, values.shape[1]).sum(axis=0)

    def conv_back(lo, d_conv, raw):
        span = slice(lo, lo + LANES)
        pre = pre_ref[:, span].astype(F32)
        gate = sigmoid(pre)
        d_pre = d_conv * (gate * (1.0 + pre * (1.0 - gate)))
        dpre[0:Q, span] = d_pre
        d_raw = taps_ref[K - 1 : K, span] * d_pre
        acc_ref[8 * (K - 1) : 8 * K, span] += fold(d_pre * raw)
        acc_ref[8 * K : 8 * K + 8, span] += fold(d_pre)
        for lag in range(1, K):
            moved = dpre[lag : lag + Q, span] * lag_mask[lag]
            d_raw = d_raw + taps_ref[K - 1 - lag : K - lag, span] * moved
            acc_ref[8 * (K - 1 - lag) : 8 * (K - lag), span] += fold(moved * raw)
        dx_ref[:, span] = d_raw.astype(BF16)

    d_scores = jnp.zeros((Q, Q), F32)
    for pair in range(heads // 2):
        span = slice(pair * LANES, (pair + 1) * LANES)
        xc = xc_ref[:, span].astype(F32)
        dy_b = dy_ref[:, span]
        dy = dy_b.astype(F32)
        left, right, both = pair_columns(csum, pair, first)
        _, _, step_pair = pair_columns(step, pair, first)
        fall_left = jnp.exp2(jnp.minimum(left - csum_t[2 * pair : 2 * pair + 1, :], 0.0))
        fall_right = jnp.exp2(jnp.minimum(right - csum_t[2 * pair + 1 : 2 * pair + 2, :], 0.0))
        mix = jnp.concatenate([(scores * fall_left).astype(BF16), (scores * fall_right).astype(BF16)], axis=1)
        fed_b = (xc * step_pair).astype(BF16)
        fed = fed_b.astype(F32)
        zero = jnp.zeros((Q, LANES), BF16)
        stacked = jnp.concatenate([jnp.where(first, fed_b, zero), jnp.where(first, zero, fed_b)], axis=0)
        held_b = st_ref[0, :, span]
        grown = jnp.exp2(both) * carry
        y = mm(mix, stacked) + mm(c_b, held_b) * grown
        d_mix = mm(dy_b, stacked, NT)
        d_scores = d_scores + d_mix[:, :Q] * fall_left + d_mix[:, Q:] * fall_right
        d_fed2 = mm(mix, dy_b, TN)
        d_fed_in = jnp.where(first, d_fed2[:Q], d_fed2[Q:])
        closing = both[Q - 1 : Q, :]
        shrink = jnp.exp2(closing - both) * last
        d_held = dstate[:, span]
        d_held_b = d_held.astype(BF16)
        dst_b[:, span] = d_held_b
        d_fed_out = mm(b_b, d_held_b) * shrink
        d_fed = d_fed_in + d_fed_out
        straddle = dy * y - fed * d_fed_in
        hi = straddle.astype(BF16)
        ab_hi[:, span] = hi
        ab_lo[:, span] = (straddle - hi.astype(F32)).astype(BF16)
        v_b[:, span] = (fed * d_fed_out).astype(BF16)
        u_b[:, span] = (xc * d_fed).astype(BF16)
        fedw[:, span] = (fed * shrink).astype(BF16)
        dy_grown = (dy * grown).astype(BF16)
        dyd[:, span] = dy_grown
        kept = jnp.exp2(closing) * passing
        through[:, span] = (d_held * held_b.astype(F32)).reshape(STATE // 8, 8, LANES).sum(axis=0) * kept
        dstate[:, span] = d_held * kept + mm(c_t, dy_grown)
        acc_ref[8 * K + 8 : 8 * K + 16, span] += fold(dy * xc)
        d_conv = d_fed * step_pair + skip_ref[:, span] * dy
        conv_back(pair * LANES, d_conv, xr_ref[:, span].astype(F32))

    d_scores_b = jnp.where(visible, d_scores, 0.0).astype(BF16)
    d_c = mm(dyd[...], st_ref[0], NT) + mm(d_scores_b, b_b)
    d_b = mm(fedw[...], dst_b[...], NT) + mm(d_scores_b, c_b, TN)
    conv_back(inner, d_b, small[:, :STATE])
    conv_back(inner + STATE, d_c, small[:, STATE : 2 * STATE])

    sel = sel_ref[...]
    red_ab = mm(ab_hi[...], sel) + mm(ab_lo[...], sel)
    red_v = mm(v_b[...], sel)
    red_u = mm(u_b[...], sel)
    thr = through[...]
    thr_hi = thr.astype(BF16)
    red_t = mm(thr_hi, sel) + mm((thr - thr_hi.astype(F32)).astype(BF16), sel)
    red_t = jnp.sum(red_t, axis=0, keepdims=True)
    d_rate = (
        mm_exact((same & (cols >= rows)).astype(F32), red_ab)
        + mm_exact((same & (cols < rows)).astype(F32), red_v)
        + red_t
    )
    d_step = red_u - d_rate * decay_rate
    d_dt = d_step * sigmoid(shifted)
    dx_ref[:, inner + 2 * STATE :] = d_dt.astype(BF16)
    hacc_ref[0:8, :] += fold(d_dt)
    hacc_ref[8:16, :] += fold(d_rate * (-decay_rate * step))
    dpre[Q : Q + 8, :] = dpre[0:8, :]
    halo_out[...] = dpre[0:8, :]
    state_out[...] = dstate[...]


def load_blocks(offsets_ref, parts, whole, sems):
    @pl.when(pl.program_id(0) == 0)
    def _():
        copies = []
        count = sems.shape[0]
        size = whole.shape[0] // count
        for part in parts:
            for j in range(part.shape[0] // size):
                k = len(copies)
                start = pl.multiple_of(offsets_ref[k], 32) if count > 1 else 0
                source = part.at[pl.ds(j * size, size), :]
                copies.append(pltpu.make_async_copy(source, whole.at[pl.ds(start, size), :], sems.at[k]))
        for copy in copies:
            copy.start()
        for copy in copies:
            copy.wait()


def turn_rows(offsets_ref, me_ref, own_ref, other_ref, out_ref, turned):
    depth = own_ref.shape[1]
    rows = own_ref.shape[0]
    for index, source in enumerate((own_ref, other_ref)):
        at = pl.multiple_of(jnp.where(index == 0, me_ref[0], 1 - me_ref[0]) * rows, LANES)
        for lo in range(0, rows, Q):
            tile = source[lo : lo + Q, :].astype(F32)
            scale = lax.rsqrt(jnp.mean(tile * tile, axis=1, keepdims=True) + EPSILON)
            tile = tile * scale
            for left in range(0, depth, LANES):
                turned[left : left + LANES, pl.ds(at + lo, Q)] = tile[:, left : left + LANES].T.astype(BF16)
    count = offsets_ref.shape[0]
    size = depth // count
    for k in range(count):
        start = pl.multiple_of(offsets_ref[k], 32)
        out_ref[k * size : (k + 1) * size, :] = turned[pl.ds(start, size), :]


def project(count, heads, offsets_ref, me_ref, own_ref, other_ref, place_ref, *refs):
    blocks, (x_ref, small_ref, normed_ref, taps_ref, gain_ref, w_ref, sems) = refs[:count], refs[count:]
    load_blocks(offsets_ref, blocks, w_ref, sems)
    depth, inner = w_ref.shape[0], x_ref.shape[1]
    tile = 256

    @pl.when(pl.program_id(0) == 0)
    def _():
        spare = w_ref[:, inner + 2 * STATE :]
        pick = jnp.where(iota((8, LANES), 1) == heads + K + 2, 1.0, 0.0).astype(BF16)
        gain_ref[...] = mm(pick, spare, NT)
        lanes = iota((depth, LANES), 1)
        for lo in range(0, inner + 2 * STATE, LANES):
            if lo < inner:
                wanted, row = place_ref[:, :LANES] == lanes + lo, heads
            else:
                wanted, row = place_ref[:, LANES:] == lanes + (lo - inner), heads + 8
            moved = mm(spare, jnp.where(wanted, 1.0, 0.0).astype(BF16), TN)
            taps_ref[:, lo : lo + LANES] = moved[row : row + 8, :]

    rows = jnp.where(pl.program_id(0) == me_ref[0], own_ref[...], other_ref[...]).astype(F32)
    scale = lax.rsqrt(jnp.mean(rows * rows, axis=1, keepdims=True) + EPSILON)
    rows = (rows * scale * gain_ref[0:1, :]).astype(BF16)
    normed_ref[...] = rows
    for lo in range(0, inner, tile):
        x_ref[:, lo : lo + tile] = mm(rows, w_ref[:, lo : lo + tile]).astype(BF16)
    small_ref[...] = mm(rows, w_ref[:, inner:])


def row_sums(lanes):
    return mm_exact(jnp.ones((8, LANES), F32), lanes, NT)


def spread_rows(values):
    pick = jnp.where(iota((8, LANES), 0) == 0, 1.0, 0.0).astype(F32)
    return mm_exact(values, pick, TN)


def gate_forward(normed_ref, y_ref, gain_ref, w_ref, z_ref, gg_ref, sq_ref):
    width = w_ref.shape[1]
    tile = 256
    rows = normed_ref[...]
    square = jnp.zeros((rows.shape[0], LANES), F32)
    for lo in range(0, width, tile):
        span = slice(lo, lo + tile)
        z = mm(rows, w_ref[:, span])
        z_b = z.astype(BF16)
        z_ref[:, span] = z_b
        z = z_b.astype(F32)
        gated = y_ref[:, span].astype(F32) * (z * sigmoid(z))
        gg_ref[:, span] = (gated * gain_ref[K + 1 : K + 2, span]).astype(BF16)
        twice = gated * gated
        for part in range(0, tile, LANES):
            square = square + twice[:, part : part + LANES]
    sq_ref[...] = row_sums(square)


def out_pair(ends_ref, me_ref, gg_ref, own_ref, other_ref, w_ref, u_ref, ds_ref, prod_ref):
    width = w_ref.shape[0]
    tile = 256
    step = pl.program_id(0)
    gg = gg_ref[...]
    rows = gg.shape[0]
    cot = jnp.where(step == me_ref[0], own_ref[...], other_ref[...])
    live = (iota((rows, LANES), 0) + step * rows < ends_ref[ends_ref.shape[0] - 1]).astype(F32)
    product = jnp.zeros((gg.shape[0], LANES), F32)
    for lo in range(0, width, tile):
        span = slice(lo, lo + tile)
        u = mm(gg, w_ref[span, :], NT)
        u_ref[:, span] = u.astype(BF16)
        term = u * cot[:, span].astype(F32)
        for part in range(0, tile, LANES):
            product = product + term[:, part : part + LANES]
        wide = jnp.concatenate([live] * (tile // LANES), axis=1)
        ds_ref[:, span] = (mm(cot, w_ref[:, span]) * wide).astype(BF16)
    prod_ref[...] = row_sums(product * live)


def gate_backward(ds_ref, y_ref, z_ref, rg_ref, coef_ref, gain_ref, dy_ref, dz_ref, acc_ref):
    @pl.when(pl.program_id(0) == 0)
    def _():
        acc_ref[...] = jnp.zeros(acc_ref.shape, F32)

    rg = spread_rows(rg_ref[...])
    coef = spread_rows(coef_ref[...])
    count = rg.shape[0]
    for lo in range(0, ds_ref.shape[1], LANES):
        span = slice(lo, lo + LANES)
        z = z_ref[:, span].astype(F32)
        y = y_ref[:, span].astype(F32)
        gate = sigmoid(z)
        silu = z * gate
        gated = y * silu
        d_normal = ds_ref[:, span].astype(F32) * rg
        acc_ref[:, span] += (d_normal * gated).reshape(count // 8, 8, LANES).sum(axis=0)
        d_gated = d_normal * gain_ref[K + 1 : K + 2, span] - gated * coef
        dy_ref[:, span] = (d_gated * silu).astype(BF16)
        dz_ref[:, span] = (d_gated * y * (gate + silu * (1.0 - gate))).astype(BF16)


def normed_back(count, rows_ref, offsets_ref, dz_ref, dx_ref, wz_ref, *refs):
    blocks, (out_ref, wx_ref, sems) = refs[:count], refs[count:]
    load_blocks(offsets_ref, blocks, wx_ref, sems)
    dz = dz_ref[...]
    dx = dx_ref[...]
    tile = 256
    for lo in range(0, wz_ref.shape[0], tile):
        span = slice(lo, lo + tile)
        out_ref[:, span] = (mm(dz, wz_ref[span, :], NT) + mm(dx, wx_ref[span, :], NT)).astype(BF16)


def params():
    return pltpu.CompilerParams(dimension_semantics=("arbitrary",), vmem_limit_bytes=VMEM_LIMIT)


SMALL_COST = pl.CostEstimate(flops=1000, bytes_accessed=1000, transcendentals=0)


def rows_spec(block, width, column=0):
    return pl.BlockSpec((block, width), lambda i: (i, column))


def whole_spec(shape, column=0):
    return pl.BlockSpec(shape, lambda i: (0, column))


def local(
    tokens,
    cotangent,
    lengths,
    norm_gain,
    w_zx,
    w_bc,
    w_dt,
    conv_x,
    conv_x_bias,
    conv_bc,
    conv_bc_bias,
    dt_bias,
    a_log,
    d_skip,
    gate_gain,
    w_out,
):
    n_t = lax.axis_size("tensor")
    n_dp = lax.axis_size("dp")
    me_t = lax.axis_index("tensor")
    me_dp = lax.axis_index("dp")
    own_rows, depth = tokens.shape
    group = own_rows * n_t
    chunks = group // Q
    heads = dt_bias.shape[0]
    inner = heads * WIDTH
    inner_total = inner * n_t
    shard = w_zx.shape[1]
    pairs = [(i, n_t - 1 - i) for i in range(n_t)]

    def swap(v):
        return lax.ppermute(v, "tensor", pairs)

    def in_order(mine, other, axis=0):
        low = jnp.where(me_t == 0, mine, other)
        high = jnp.where(me_t == 0, other, mine)
        return jnp.concatenate([low, high], axis=axis)

    def sum_dp(v):
        step = 1
        while step < n_dp:
            v = v + lax.ppermute(v, "dp", [(i, i ^ step) for i in range(n_dp)])
            step *= 2
        return v

    def after(value, *others):
        return lax.optimization_barrier((value, *others))[0]

    ring = 4
    plane = n_dp // (2 * ring)

    around = [(i, (i + 2 * plane) % n_dp) for i in range(n_dp)]
    across = [(i, i ^ 2) for i in range(n_dp)]
    beside = [(i, i ^ 1) for i in range(n_dp)]

    def send(v, way):
        return lax.ppermute(v, "dp", way)

    by_hand = plane == 2 and shard % 32 == 0

    def whole(v):
        return [lax.all_gather(v, "dp", axis=0, tiled=True)]

    def block_offsets(count, size):
        if count == 1:
            return jnp.zeros((1,), jnp.int32)
        places = []
        for core in range(2):
            for side in range(2):
                for turn in range(ring):
                    level = (me_dp // (2 * plane) - turn + ring) % ring
                    places.append(level * (2 * plane) + ((me_dp % (2 * plane)) ^ (2 * side + core)))
        return jnp.stack(places).astype(jnp.int32) * size

    def relative_order():
        level, side, core = me_dp // 4, (me_dp // 2) % 2, me_dp % 2
        order = []
        for dc in (1, 0):
            for dy in (1, 0):
                for dz in range(1, ring + 1):
                    order.append(((level - dz + ring) % ring) * 4 + (side ^ dy) * 2 + (core ^ dc))
        return order

    def fold_beside(keep, got):
        half = keep.shape[0] // 2
        away = (keep[:half].astype(F32) + got[:half].astype(F32)).astype(BF16)
        return away, keep[half:].astype(F32) + got[half:].astype(F32)

    def fold_turn(total, got, turn):
        part = total[(turn - 1) * shard : turn * shard] + got.astype(F32)
        return part if turn == ring else part.astype(BF16)

    ends = jnp.cumsum(lengths[0]).astype(jnp.int32)
    live = (lax.iota(jnp.int32, group) < ends[-1]).astype(F32)
    live_own = lax.dynamic_slice_in_dim(live, me_t * own_rows, own_rows, 0)
    me = me_t.astype(jnp.int32).reshape(1)

    span_p = conv_x_bias.shape[1]
    span_n = conv_bc_bias.shape[1]
    half_bc = w_bc.shape[1]
    bits = jnp.concatenate([norm_gain, conv_bc.reshape(-1), conv_bc_bias.reshape(-1)])
    bits = jnp.pad(bits, (0, LANES - bits.shape[0]))
    tiny = jnp.concatenate([w_bc.reshape(2 * half_bc, STATE), bits[None]], axis=0)
    other_tiny = swap(tiny)
    other_bc = other_tiny[: 2 * half_bc].reshape(w_bc.shape)
    both_bits = [bits, other_tiny[2 * half_bc]]
    at = norm_gain.shape[0]
    gain_pair = in_order(*[v[:at] for v in both_bits])[:, None]
    taps_bc = in_order(*[v[at : at + conv_bc.size].reshape(2, span_n, K) for v in both_bits], axis=1)
    at += conv_bc.size
    bias_bc = in_order(*[v[at : at + 2 * span_n].reshape(2, span_n, 1) for v in both_bits], axis=1)
    spare_bc = jnp.concatenate([taps_bc, bias_bc], axis=2).reshape(4 * span_n, K + 1)
    spare_x = [conv_x.reshape(shard, K), conv_x_bias.reshape(shard, 1), gate_gain.reshape(shard, 1), gain_pair]
    bc_pair = in_order(w_bc, other_bc, axis=1)
    packed = jnp.concatenate(
        [w_zx[1], bc_pair[0], bc_pair[1], w_dt, *spare_x, jnp.zeros((shard, 8 - K - 3), BF16)]
        + [jnp.pad(spare_bc, ((0, shard - 4 * span_n), (0, LANES - heads - 8 - K - 1)))],
        axis=1,
    )
    gain_pair = gain_pair.astype(F32)
    where = lax.iota(jnp.int32, depth)
    home, inside = where // shard, where % shard
    place_x = (inside // span_p) * WIDTH + home * span_p + inside % span_p
    half_n = 2 * span_n
    place_bc = (inside // half_n) * STATE + home * half_n + inside % half_n
    place = jnp.concatenate([jnp.broadcast_to(v[:, None], (depth, LANES)) for v in (place_x, place_bc)], axis=1)
    par = jnp.concatenate([dt_bias[None], a_log[None], jnp.zeros((6, heads), F32)], axis=0)
    par = jnp.concatenate([par, jnp.zeros((8, LANES - heads), F32)], axis=1)
    skip = jnp.repeat(d_skip, WIDTH)[None]
    members = lax.iota(jnp.int32, inner)[:, None] // WIDTH
    sel = (members == lax.iota(jnp.int32, LANES)[None, :]).astype(BF16)
    smem = pl.BlockSpec(memory_space=pltpu.SMEM)
    vmem = pl.BlockSpec(memory_space=pltpu.VMEM)
    hbm = pl.BlockSpec(memory_space=pl.ANY)
    n_small = 2 * STATE + LANES
    n_conv = inner + 2 * STATE
    w_rest = jnp.concatenate([w_zx[0], w_out.T], axis=1)

    def turn(other_tokens):
        return pl.pallas_call(
            turn_rows,
            in_specs=[smem, smem, vmem, vmem],
            out_specs=vmem,
            out_shape=jax.ShapeDtypeStruct((depth, group), BF16),
            scratch_shapes=[pltpu.VMEM((depth, group), BF16)],
            compiler_params=pltpu.CompilerParams(vmem_limit_bytes=VMEM_LIMIT),
            cost_estimate=SMALL_COST,
            name="turn_rows",
        )((jnp.stack(relative_order()) * shard).astype(jnp.int32), me, tokens, other_tokens)

    if by_hand:
        line, other, line_c, other_c = [packed], [], [], []
        pieces = [tokens[:176], tokens[176:352], tokens[352:]]
        arrived, held_turn, constants = [], [], []
        for step in range(ring + 1):
            made = []
            if step < ring - 1:
                made.append((line, send(line[step], around)))
                made.append((arrived, swap(after(pieces[step], line[step]))))
            if step < ring:
                made.append((other, send(line[step], across)))
                made.append((line_c, send(line[step], beside)))
            if step:
                made.append((other_c, send(other[step - 1], beside)))
            if step == 1:
                zo_all = lax.all_gather(after(w_rest, line[1]), "dp", axis=0, tiled=True)
                made += [(constants, v) for v in (place, par, skip, sel)]
            if step == 3:
                other_tokens = jnp.concatenate(arrived, axis=0)
                made.append((held_turn, turn(after(other_tokens, line[3]))))
                other_cot = swap(after(cotangent, other_tokens))
            fresh = lax.optimization_barrier(tuple(value for _, value in made))
            for (place_in, _), value in zip(made, fresh):
                place_in.append(value)
        wx_blocks = line + other + line_c + other_c
        turned = held_turn[0]
        place, par, skip, sel = constants
    else:
        wx_blocks = whole(packed)
        zo_all = whole(w_rest)[0]
        other_tokens, other_cot = swap(tokens), swap(cotangent)
    count = len(wx_blocks)
    offsets = block_offsets(count, shard)
    sems = pltpu.SemaphoreType.DMA((count,))
    tok_own = tokens.astype(F32)
    inv_tok = lax.rsqrt(jnp.mean(tok_own * tok_own, axis=1, keepdims=True) + EPSILON)

    block = own_rows
    steps = group // block
    x_raw, small, normed, taps, gain_in = pl.pallas_call(
        partial(project, count, heads),
        grid=(steps,),
        in_specs=[
            smem,
            smem,
            whole_spec((block, depth)),
            whole_spec((block, depth)),
            whole_spec((depth, 2 * LANES)),
        ]
        + [hbm] * count,
        out_specs=[
            rows_spec(block, inner),
            rows_spec(block, n_small),
            rows_spec(block, depth),
            whole_spec((8, n_conv)),
            whole_spec((8, depth)),
        ],
        out_shape=[
            jax.ShapeDtypeStruct((group, inner), BF16),
            jax.ShapeDtypeStruct((group, n_small), F32),
            jax.ShapeDtypeStruct((group, depth), BF16),
            jax.ShapeDtypeStruct((8, n_conv), F32),
            jax.ShapeDtypeStruct((8, depth), F32),
        ],
        scratch_shapes=[pltpu.VMEM((depth, inner + n_small), BF16), sems],
        compiler_params=params(),
        cost_estimate=SMALL_COST,
        name="project",
    )(offsets, me, tokens, other_tokens, place, *wx_blocks)
    xc, pre, bc, y_all, states = pl.pallas_call(
        partial(scan_forward, heads),
        grid=(chunks,),
        in_specs=[
            smem,
            rows_spec(Q, inner),
            rows_spec(Q, n_small),
            whole_spec((8, n_conv)),
            whole_spec((8, LANES)),
            whole_spec((1, inner)),
        ],
        out_specs=[
            rows_spec(Q, inner),
            rows_spec(Q, n_conv),
            rows_spec(Q, 2 * STATE),
            rows_spec(Q, inner),
            pl.BlockSpec((1, STATE, inner), lambda i: (i, 0, 0)),
        ],
        out_shape=[
            jax.ShapeDtypeStruct((group, inner), BF16),
            jax.ShapeDtypeStruct((group, n_conv), BF16),
            jax.ShapeDtypeStruct((group, 2 * STATE), BF16),
            jax.ShapeDtypeStruct((group, inner), BF16),
            jax.ShapeDtypeStruct((chunks, STATE, inner), BF16),
        ],
        scratch_shapes=[pltpu.VMEM((Q + 8, n_conv), F32), pltpu.VMEM((STATE, inner), F32)],
        compiler_params=params(),
        cost_estimate=SMALL_COST,
        name="scan_forward",
    )(ends, x_raw, small, taps, par, skip)

    row8 = pl.BlockSpec((8, block), lambda i: (0, i))
    z_all, gg, sq = pl.pallas_call(
        gate_forward,
        grid=(steps,),
        in_specs=[
            rows_spec(block, depth),
            rows_spec(block, inner),
            whole_spec((8, inner)),
            whole_spec((depth, inner), 0),
        ],
        out_specs=[rows_spec(block, inner), rows_spec(block, inner), row8],
        out_shape=[
            jax.ShapeDtypeStruct((group, inner), BF16),
            jax.ShapeDtypeStruct((group, inner), BF16),
            jax.ShapeDtypeStruct((8, group), F32),
        ],
        compiler_params=params(),
        cost_estimate=SMALL_COST,
        name="gate_forward",
    )(normed, y_all, taps, zo_all)
    sq_all = sq + swap(sq)

    u_part, d_scaled, prod = pl.pallas_call(
        out_pair,
        grid=(steps,),
        in_specs=[
            smem,
            smem,
            rows_spec(block, inner),
            whole_spec((block, depth)),
            whole_spec((block, depth)),
            whole_spec((depth, inner), 1),
        ],
        out_specs=[rows_spec(block, depth), rows_spec(block, inner), row8],
        out_shape=[
            jax.ShapeDtypeStruct((group, depth), BF16),
            jax.ShapeDtypeStruct((group, inner), BF16),
            jax.ShapeDtypeStruct((8, group), F32),
        ],
        compiler_params=params(),
        cost_estimate=SMALL_COST,
        name="out_pair",
    )(ends, me, gg, cotangent, other_cot, zo_all)
    prod_all = prod + swap(prod)
    inv_gate8 = lax.rsqrt(sq_all / inner_total + EPSILON)
    inv_gate = inv_gate8[0]
    cot_all = in_order(cotangent, other_cot)

    u_own = lax.dynamic_slice_in_dim(u_part, me_t * own_rows, own_rows, 0)
    u_send = lax.dynamic_slice_in_dim(u_part, (n_t - 1 - me_t) * own_rows, own_rows, 0)
    u_recv = swap(u_send)
    inv_own = lax.dynamic_slice_in_dim(inv_gate, me_t * own_rows, own_rows, 0)
    branch = (u_own.astype(F32) + u_recv.astype(F32)) * (inv_own * live_own)[:, None]
    layer_out = (tokens.astype(F32) + branch).astype(BF16)

    d_branch = (cot_all.astype(F32) * (live * inv_gate)[:, None]).astype(BF16)
    g_out = lax.dot_general(d_branch, gg, TN, preferred_element_type=F32).astype(BF16)
    grad_out = lax.psum_scatter(g_out, "dp", scatter_dimension=0, tiled=True)
    d_scaled = after(d_scaled, g_out)

    coef8 = inv_gate8 * inv_gate8 * inv_gate8 * (prod_all / inner_total)
    dy, dz, gain_acc = pl.pallas_call(
        gate_backward,
        grid=(steps,),
        in_specs=[
            rows_spec(block, inner),
            rows_spec(block, inner),
            rows_spec(block, inner),
            row8,
            row8,
            whole_spec((8, inner)),
        ],
        out_specs=[rows_spec(block, inner), rows_spec(block, inner), whole_spec((8, inner))],
        out_shape=[
            jax.ShapeDtypeStruct((group, inner), BF16),
            jax.ShapeDtypeStruct((group, inner), BF16),
            jax.ShapeDtypeStruct((8, inner), F32),
        ],
        compiler_params=params(),
        cost_estimate=SMALL_COST,
        name="gate_backward",
    )(d_scaled, y_all, z_all, inv_gate8, coef8, taps)
    dot = partial(lax.dot_general, preferred_element_type=F32)
    if by_hand:
        front = depth // 2
        g_send = dot(turned[:front], dz, NN).astype(BF16)
        z_keep = dot(turned[front:], after(dz, g_send), NN).astype(BF16)
        z_got = send(g_send, beside)
        dy = after(dy, z_keep, g_send)
    else:
        grad_z = lax.psum_scatter(dot(normed, dz, TN).astype(BF16), "dp", scatter_dimension=0, tiled=True)

    def backward(top, number, carry):
        back = lambda width: pl.BlockSpec((Q, width), lambda i: (top - i, 0))
        operands = [ends, dy, xc, pre, x_raw, small, bc, states, taps, par, skip, sel, *carry]
        return pl.pallas_call(
            partial(scan_backward, heads, chunks, top),
            grid=(number,),
            in_specs=[
                smem,
                back(inner),
                back(inner),
                back(n_conv),
                back(inner),
                back(n_small),
                back(2 * STATE),
                pl.BlockSpec((1, STATE, inner), lambda i: (top - i, 0, 0)),
                whole_spec((8, n_conv)),
                whole_spec((8, LANES)),
                whole_spec((1, inner)),
                whole_spec((inner, LANES)),
            ]
            + ([whole_spec((STATE, inner)), whole_spec((8, n_conv)), hbm] if carry else []),
            out_specs=[
                back(inner + n_small),
                whole_spec((8 * (K + 2), n_conv)),
                whole_spec((16, LANES)),
                whole_spec((STATE, inner)),
                whole_spec((8, n_conv)),
            ],
            out_shape=[
                jax.ShapeDtypeStruct((group, inner + n_small), BF16),
                jax.ShapeDtypeStruct((8 * (K + 2), n_conv), F32),
                jax.ShapeDtypeStruct((16, LANES), F32),
                jax.ShapeDtypeStruct((STATE, inner), F32),
                jax.ShapeDtypeStruct((8, n_conv), F32),
            ],
            scratch_shapes=[
                pltpu.VMEM((STATE, inner), F32),
                pltpu.VMEM((Q + 8, n_conv), F32),
                pltpu.VMEM((Q, inner), BF16),
                pltpu.VMEM((Q, inner), BF16),
                pltpu.VMEM((Q, inner), BF16),
                pltpu.VMEM((Q, inner), BF16),
                pltpu.VMEM((Q, inner), BF16),
                pltpu.VMEM((Q, inner), BF16),
                pltpu.VMEM((STATE, inner), BF16),
                pltpu.VMEM((8, inner), F32),
            ],
            input_output_aliases={len(operands) - 1: 0} if carry else {},
            compiler_params=params(),
        cost_estimate=SMALL_COST,
            name="scan_backward",
        )(*operands)

    half_chunks = chunks // 2
    dx, acc_a, hacc_a, d_state, halo = backward(chunks - 1, chunks - half_chunks, ())
    if by_hand:
        z_got, dx = lax.optimization_barrier((z_got, dx))
        z_away, z_keep = fold_beside(z_keep, z_got)
        z_got = send(z_away, across)
        d_state = after(d_state, z_away, z_keep)
    dx, acc, hacc, _, _ = backward(half_chunks - 1, half_chunks, (d_state, halo, dx))
    acc = acc + acc_a
    hacc = hacc + hacc_a
    dx = after(dx, u_recv)

    acc = acc.reshape(K + 2, 8, n_conv).sum(axis=1)
    hsum = hacc.reshape(2, 8, LANES).sum(axis=1)
    d_gate = gain_acc.sum(axis=0)
    d_sk = acc[K + 1, :inner].reshape(heads, WIDTH).sum(axis=1)
    shared = acc[: K + 1, inner:]
    headed = [acc[: K + 1, :inner].reshape(-1), d_gate, hsum[:, :heads].reshape(-1), d_sk]
    shared_got = swap(shared)
    n_x = 1024

    if by_hand:
        d_late = dx[:, n_x:]
        g_send = dot(turned[:front], d_late, NN).astype(BF16)
        x_got = send(g_send, beside)
        g_x = dot(normed, after(dx, g_send)[:, :n_x], TN).astype(BF16)
        grad_x = lax.psum_scatter(g_x, "dp", scatter_dimension=0, tiled=True)
        x_keep = dot(turned[front:], after(dx, g_x)[:, n_x:], NN).astype(BF16)
        x_got, x_keep, z_got = lax.optimization_barrier((x_got, x_keep, z_got))
        x_away, x_keep = fold_beside(x_keep, x_got)
        x_got = send(x_away, across)
        z_total = z_keep + z_got.astype(F32)
        z_away = z_total[:shard].astype(BF16)
        z_got = send(z_away, around)
        dz = after(dz, x_away, x_keep, z_away)
    else:
        grad_x = lax.psum_scatter(dot(normed, dx, TN).astype(BF16), "dp", scatter_dimension=0, tiled=True)

    vector = jnp.concatenate([(shared + shared_got).reshape(-1)] + headed)
    vector = jnp.concatenate([vector, jnp.zeros((-vector.shape[0] % 1024,), F32)]).reshape(-1, LANES)

    def back_rows(which, dz):
        pick = lambda width: pl.BlockSpec((own_rows, width), lambda i, rows: (rows[0], 0))
        fixed = lambda shape: pl.BlockSpec(shape, lambda i, rows: (0, 0))
        return pl.pallas_call(
            partial(normed_back, count),
            grid_spec=pltpu.PrefetchScalarGridSpec(
                num_scalar_prefetch=1,
                grid=(1,),
                in_specs=[smem, pick(inner), pick(inner + n_small), fixed((depth, inner))] + [hbm] * count,
                out_specs=fixed((own_rows, depth)),
                scratch_shapes=[pltpu.VMEM((depth, inner + n_small), BF16), sems],
            ),
            out_shape=jax.ShapeDtypeStruct((own_rows, depth), BF16),
            compiler_params=params(),
            cost_estimate=SMALL_COST,
            name="normed_back",
        )(which, offsets, dz, dx, zo_all, *wx_blocks)

    dn_send = back_rows(n_t - 1 - me, dz)
    if by_hand:
        quarter = own_rows // 4
        dn_parts = [dn_send[k * quarter : (k + 1) * quarter] for k in range(4)]
        dn_got = [swap(dn_parts[0])]
        dn_own = back_rows(me, after(dz, dn_send))
        x_got, z_got, dn_own, dn_got[0] = lax.optimization_barrier((x_got, z_got, dn_own, dn_got[0]))
        x_total = x_keep + x_got.astype(F32)
        x_got = x_total[:shard].astype(BF16)
        z_got = fold_turn(z_total, z_got, 2)
        for turn in range(2, ring + 1):
            moved = [send(x_got, around), send(vector, [(i, i ^ (1 << (turn - 2))) for i in range(n_dp)])]
            moved.append(swap(after(dn_parts[turn - 1], x_got)))
            if turn < ring:
                moved.append(send(z_got, around))
            moved = lax.optimization_barrier(tuple(moved))
            x_got = fold_turn(x_total, moved[0], turn)
            vector = vector + moved[1]
            dn_got.append(moved[2])
            if turn < ring:
                z_got = fold_turn(z_total, moved[3], turn + 1)
        grad_z = z_got * gain_pair
        dn_got = jnp.concatenate(dn_got, axis=0)
        vector = vector + send(vector, [(i, i ^ 8) for i in range(n_dp)])
        grad_x = jnp.concatenate([grad_x.astype(F32), x_got * gain_pair], axis=1)
    else:
        vector = sum_dp(vector)
        dn_own = back_rows(me, dz)
        dn_got = swap(dn_send)
    dn = (dn_own.astype(F32) + dn_got.astype(F32)) * gain_in[0:1, :]
    grad_tokens = (
        cotangent.astype(F32)
        + inv_tok * dn
        - tok_own * inv_tok * inv_tok * inv_tok * jnp.mean(dn * tok_own, axis=1, keepdims=True)
    )

    vector = vector.reshape(-1)
    n_bc = (K + 1) * 2 * STATE
    bc_sum = vector[:n_bc].reshape(K + 1, 2, STATE)
    me_all = me_dp * n_t + me_t
    bc_sum = lax.dynamic_slice_in_dim(bc_sum, me_all * span_n, span_n, 2)
    grad_bc_taps = bc_sum[:K].transpose(1, 2, 0).reshape(conv_bc.shape)
    grad_bc_bias = bc_sum[K]
    at = n_bc
    x_sum = vector[at : at + (K + 1) * inner].reshape(K + 1, heads, WIDTH)
    at += (K + 1) * inner
    x_sum = lax.dynamic_slice_in_dim(x_sum, me_dp * span_p, span_p, 2)
    grad_x_taps = x_sum[:K].transpose(1, 2, 0).reshape(conv_x.shape)
    grad_x_bias = x_sum[K]
    grad_gate = lax.dynamic_slice_in_dim(vector[at : at + inner].reshape(heads, WIDTH), me_dp * span_p, span_p, 1)
    at += inner
    grad_dt_bias = vector[at : at + heads]
    grad_a_log = vector[at + heads : at + 2 * heads]
    grad_skip = vector[at + 2 * heads : at + 3 * heads]

    grad_z = grad_z.astype(F32)
    grad_x = grad_x.astype(F32)
    in_part = jnp.sum(w_zx[0].astype(F32) * grad_z, axis=1) + jnp.sum(packed.astype(F32) * grad_x, axis=1)
    in_part = in_part[:, None]
    grad_zx = jnp.stack([grad_z, grad_x[:, :inner]])
    grad_dt = grad_x[:, inner + 2 * STATE : inner + 2 * STATE + heads]
    bc_part = jnp.concatenate([grad_x[:, inner : inner + 2 * STATE], jnp.broadcast_to(in_part, (shard, LANES))], axis=1)
    half = half_bc
    bc_own = lax.dynamic_slice_in_dim(bc_part, me_t * half, half, 0)
    bc_send = lax.dynamic_slice_in_dim(bc_part, (n_t - 1 - me_t) * half, half, 0)
    bc_total = bc_own + swap(bc_send)
    own_gain = norm_gain.astype(F32)
    grad_bc = bc_total[:, : 2 * STATE].reshape(half, 2, STATE).transpose(1, 0, 2)
    grad_in = bc_total[:, 2 * STATE] / own_gain
    return (
        layer_out,
        grad_tokens,
        grad_in,
        grad_zx,
        grad_bc,
        grad_dt,
        grad_x_taps,
        grad_x_bias,
        grad_bc_taps,
        grad_bc_bias,
        grad_dt_bias,
        grad_a_log,
        grad_skip,
        grad_gate,
        grad_out.astype(F32).T,
    )


def solution(mesh):
    both = ("dp", "tensor")
    in_specs = (
        P(both, None),
        P(both, None),
        P("dp", None),
        P(both),
        P(None, "dp", "tensor"),
        P(None, both, None),
        P("dp", "tensor"),
        P("tensor", "dp"),
        P("tensor", "dp"),
        P(None, both),
        P(None, both),
        P("tensor"),
        P("tensor"),
        P("tensor"),
        P("tensor", "dp"),
        P("tensor", "dp"),
    )
    out_specs = (
        P(both, None),
        P(both, None),
        P(both),
        P(None, "dp", "tensor"),
        P(None, both, None),
        P("dp", "tensor"),
        P("tensor", "dp"),
        P("tensor", "dp"),
        P(None, both),
        P(None, both),
        P("tensor"),
        P("tensor"),
        P("tensor"),
        P("tensor", "dp"),
        P("tensor", "dp"),
    )
    return jax.shard_map(local, mesh=mesh, in_specs=in_specs, out_specs=out_specs, check_vma=False)
```

```python
from functools import partial

import jax
import jax.numpy as jnp
from jax import lax
from jax.experimental import pallas as pl
from jax.experimental.pallas import tpu as pltpu
from jax.sharding import PartitionSpec as P

EPSILON = 1e-05
HIGHEST = lax.Precision.HIGHEST
K = 4
WIDTH = 64
STATE = 128
Q = 128
LANES = 128
LOG2E = 1.4426950408889634
VMEM_LIMIT = 60 * 1024 * 1024
F32 = jnp.float32
BF16 = jnp.bfloat16

NN = (((1,), (0,)), ((), ()))
NT = (((1,), (1,)), ((), ()))
TN = (((0,), (0,)), ((), ()))


def mm(a, b, dims=NN):
    return lax.dot_general(a, b, dims, preferred_element_type=F32)


def mm_exact(a, b, dims=NN):
    return lax.dot_general(a, b, dims, preferred_element_type=F32, precision=HIGHEST)


def iota(shape, dim):
    return lax.broadcasted_iota(jnp.int32, shape, dim)


def segment_of(rows, ends_ref, count):
    total = (rows >= ends_ref[0]).astype(jnp.int32)
    for j in range(1, count):
        total = total + (rows >= ends_ref[j]).astype(jnp.int32)
    return total


def scalar_segment(row, ends_ref, count):
    total = jnp.where(row >= ends_ref[0], 1, 0)
    for j in range(1, count):
        total = total + jnp.where(row >= ends_ref[j], 1, 0)
    return total


def sigmoid(v):
    return 0.5 * jnp.tanh(0.5 * v) + 0.5


def softplus(v):
    return jnp.maximum(v, 0.0) + jnp.log1p(jnp.exp(-jnp.abs(v)))


def chunk_masks(chunk, ends_ref, count):
    base = chunk * Q
    rows = iota((Q, Q), 0) + base
    cols = iota((Q, Q), 1) + base
    row_ids = segment_of(rows, ends_ref, count)
    col_ids = segment_of(cols, ends_ref, count)
    same = row_ids == col_ids
    before_id = jnp.where(chunk == 0, -1, scalar_segment(base - 1, ends_ref, count))
    final_id = scalar_segment(base + Q - 1, ends_ref, count)
    carry = (row_ids == before_id).astype(F32)
    last = (row_ids == final_id).astype(F32)
    passing = jnp.where(before_id == final_id, 1.0, 0.0).astype(F32)
    return rows, cols, row_ids, same, carry, last, passing


def decays(dt_raw, par_ref):
    shifted = dt_raw + par_ref[0:1, :]
    step = softplus(shifted)
    decay_rate = jnp.exp(par_ref[1:2, :])
    return shifted, step, decay_rate


def pair_columns(values, pair, first):
    left = jnp.broadcast_to(values[:, 2 * pair : 2 * pair + 1], (Q, LANES))
    right = jnp.broadcast_to(values[:, 2 * pair + 1 : 2 * pair + 2], (Q, LANES))
    return left, right, jnp.where(first, left, right)


def scan_forward(
    heads, ends_ref, xr_ref, small_ref, taps_ref, par_ref, skip_ref,
    xc_ref, pre_ref, bc_ref, y_ref, st_ref, buf, state,
):
    count = ends_ref.shape[0]
    inner = heads * WIDTH
    chunk = pl.program_id(0)

    @pl.when(chunk == 0)
    def _():
        buf[:, 0:8, :] = jnp.zeros((buf.shape[0], 8, LANES), F32)
        state[...] = jnp.zeros(state.shape, F32)

    rows, cols, row_ids, same, carry, last, passing = chunk_masks(chunk, ends_ref, count)
    causal = rows >= cols
    visible = same & causal
    lag_mask = [None]
    for lag in range(1, K):
        earlier = rows - lag
        keep = (segment_of(earlier, ends_ref, count) == row_ids) & (earlier >= 0)
        lag_mask.append(keep.astype(F32))

    small = small_ref[...]

    def convolve(lo, raw):
        span = slice(lo, lo + LANES)
        place = lo // LANES
        buf[place, 8 : 8 + Q, :] = raw
        pre = taps_ref[K : K + 1, span] + taps_ref[K - 1 : K, span] * raw
        for lag in range(1, K):
            pre = pre + taps_ref[K - 1 - lag : K - lag, span] * (
                buf[place, 8 - lag : 8 - lag + Q, :] * lag_mask[lag]
            )
        buf[place, 0:8, :] = raw[Q - 8 : Q, :]
        pre_ref[:, span] = pre.astype(BF16)
        return pre * sigmoid(pre)

    b_f = convolve(inner, small[:, :STATE]).astype(BF16).astype(F32)
    c_b = convolve(inner + STATE, small[:, STATE : 2 * STATE]).astype(BF16)
    b_b = b_f.astype(BF16)
    bc_ref[:, :STATE] = b_b
    bc_ref[:, STATE:] = c_b
    b_t = b_f.T.astype(BF16)

    _, step, decay_rate = decays(small[:, 2 * STATE :], par_ref)
    csum = mm_exact(causal.astype(F32), step * (-LOG2E * decay_rate))
    csum_t = csum.T
    scores = jnp.where(visible, mm(c_b, b_b, NT), 0.0)
    first = iota((Q, LANES), 1) < WIDTH
    first_row = iota((1, LANES), 1) < WIDTH

    wide = 2 * LANES
    for quad in range(0, inner, wide):
        block = slice(quad, quad + wide)
        held = state[:, block]
        held_b = held.astype(BF16)
        st_ref[0, :, block] = held_b
        carried = mm(c_b, held_b)
        weighted, kept = [], []
        for part in range(0, wide, LANES):
            lo = quad + part
            pair = lo // LANES
            span = slice(lo, lo + LANES)
            xc = convolve(lo, xr_ref[:, span].astype(F32)).astype(BF16)
            xc_ref[:, span] = xc
            xc = xc.astype(F32)
            left, right, both = pair_columns(csum, pair, first)
            _, _, step_pair = pair_columns(step, pair, first)
            mix = jnp.concatenate(
                [
                    (scores * jnp.exp2(jnp.minimum(left - csum_t[2 * pair : 2 * pair + 1, :], 0.0))).astype(BF16),
                    (scores * jnp.exp2(jnp.minimum(right - csum_t[2 * pair + 1 : 2 * pair + 2, :], 0.0))).astype(BF16),
                ],
                axis=1,
            )
            fed_b = (xc * step_pair).astype(BF16)
            zero = jnp.zeros((Q, LANES), BF16)
            stacked = jnp.concatenate([jnp.where(first, fed_b, zero), jnp.where(first, zero, fed_b)], axis=0)
            y = mm(mix, stacked) + carried[:, part : part + LANES] * (jnp.exp2(both) * carry)
            y_ref[:, span] = (y + skip_ref[:, span] * xc).astype(BF16)
            closing = both[Q - 1 : Q, :]
            weighted.append((fed_b.astype(F32) * (jnp.exp2(closing - both) * last)).astype(BF16))
            kept.append(jnp.exp2(closing) * passing)
        fresh = mm(b_t, jnp.concatenate(weighted, axis=1))
        state[:, block] = held * jnp.concatenate(kept, axis=1) + fresh


def scan_backward(
    heads, chunks, top, ends_ref, dy_ref, xc_ref, pre_ref, xr_ref, small_ref, bc_ref, st_ref, taps_ref, par_ref,
    skip_ref, sel_ref, *refs,
):
    if top + 1 < chunks:
        state_in, halo_in, _ = refs[:3]
        refs = refs[3:]
    dx_ref, acc_ref, hacc_ref, state_out, halo_out = refs[:5]
    dstate, dpre, ab_hi, ab_lo, v_b, u_b, dyd, fedw, dst_b, through = refs[5:]
    count = ends_ref.shape[0]
    inner = heads * WIDTH
    total_rows = chunks * Q
    chunk = top - pl.program_id(0)

    @pl.when(pl.program_id(0) == 0)
    def _():
        if top + 1 < chunks:
            dpre[:, Q : Q + 8, :] = halo_in[...]
            dstate[...] = state_in[...]
        else:
            dpre[:, Q : Q + 8, :] = jnp.zeros((dpre.shape[0], 8, LANES), F32)
            dstate[...] = jnp.zeros(dstate.shape, F32)
        acc_ref[...] = jnp.zeros(acc_ref.shape, F32)
        hacc_ref[...] = jnp.zeros(hacc_ref.shape, F32)

    rows, cols, row_ids, same, carry, last, passing = chunk_masks(chunk, ends_ref, count)
    causal = rows >= cols
    visible = same & causal
    lag_mask = [None]
    for lag in range(1, K):
        later = rows + lag
        keep = (segment_of(later, ends_ref, count) == row_ids) & (later < total_rows)
        lag_mask.append(keep.astype(F32))

    small = small_ref[...]
    shifted, step, decay_rate = decays(small[:, 2 * STATE :], par_ref)
    csum = mm_exact(causal.astype(F32), step * (-LOG2E * decay_rate))
    csum_t = csum.T
    b_b = bc_ref[:, :STATE]
    c_b = bc_ref[:, STATE:]
    c_t = c_b.astype(F32).T.astype(BF16)
    scores = jnp.where(visible, mm(c_b, b_b, NT), 0.0)
    first = iota((Q, LANES), 1) < WIDTH

    def fold(values):
        return values.reshape(Q // 8, 8, values.shape[1]).sum(axis=0)

    def conv_back(lo, d_conv, raw):
        span = slice(lo, lo + LANES)
        pre = pre_ref[:, span].astype(F32)
        gate = sigmoid(pre)
        d_pre = d_conv * (gate * (1.0 + pre * (1.0 - gate)))
        place = lo // LANES
        dpre[place, 0:Q, :] = d_pre
        d_raw = taps_ref[K - 1 : K, span] * d_pre
        acc_ref[8 * (K - 1) : 8 * K, span] += fold(d_pre * raw)
        acc_ref[8 * K : 8 * K + 8, span] += fold(d_pre)
        for lag in range(1, K):
            moved = dpre[place, lag : lag + Q, :] * lag_mask[lag]
            d_raw = d_raw + taps_ref[K - 1 - lag : K - lag, span] * moved
            acc_ref[8 * (K - 1 - lag) : 8 * (K - lag), span] += fold(moved * raw)
        dpre[place, Q : Q + 8, :] = d_pre[0:8, :]
        dx_ref[:, span] = d_raw.astype(BF16)

    d_scores = jnp.zeros((Q, Q), F32)
    wide = 2 * LANES
    for quad in range(0, inner, wide):
        block = slice(quad, quad + wide)
        held_b = st_ref[0, :, block]
        d_held = dstate[:, block]
        d_held_b = d_held.astype(BF16)
        dst_b[:, block] = d_held_b
        carried = mm(c_b, held_b)
        returned = mm(b_b, d_held_b)
        crossing = (d_held * held_b.astype(F32)).reshape(STATE // 8, 8, wide).sum(axis=0)
        grown_parts, kept_parts = [], []
        for part in range(0, wide, LANES):
            lo = quad + part
            pair = lo // LANES
            span = slice(lo, lo + LANES)
            xc = xc_ref[:, span].astype(F32)
            dy_b = dy_ref[:, span]
            dy = dy_b.astype(F32)
            left, right, both = pair_columns(csum, pair, first)
            _, _, step_pair = pair_columns(step, pair, first)
            fall_left = jnp.exp2(jnp.minimum(left - csum_t[2 * pair : 2 * pair + 1, :], 0.0))
            fall_right = jnp.exp2(jnp.minimum(right - csum_t[2 * pair + 1 : 2 * pair + 2, :], 0.0))
            mix = jnp.concatenate([(scores * fall_left).astype(BF16), (scores * fall_right).astype(BF16)], axis=1)
            fed_b = (xc * step_pair).astype(BF16)
            fed = fed_b.astype(F32)
            zero = jnp.zeros((Q, LANES), BF16)
            stacked = jnp.concatenate([jnp.where(first, fed_b, zero), jnp.where(first, zero, fed_b)], axis=0)
            grown = jnp.exp2(both) * carry
            y = mm(mix, stacked) + carried[:, part : part + LANES] * grown
            d_mix = mm(dy_b, stacked, NT)
            d_scores = d_scores + d_mix[:, :Q] * fall_left + d_mix[:, Q:] * fall_right
            d_fed2 = mm(mix, dy_b, TN)
            d_fed_in = jnp.where(first, d_fed2[:Q], d_fed2[Q:])
            closing = both[Q - 1 : Q, :]
            shrink = jnp.exp2(closing - both) * last
            d_fed_out = returned[:, part : part + LANES] * shrink
            d_fed = d_fed_in + d_fed_out
            straddle = dy * y - fed * d_fed_in
            hi = straddle.astype(BF16)
            ab_hi[:, span] = hi
            ab_lo[:, span] = (straddle - hi.astype(F32)).astype(BF16)
            v_b[:, span] = (fed * d_fed_out).astype(BF16)
            u_b[:, span] = (xc * d_fed).astype(BF16)
            fedw[:, span] = (fed * shrink).astype(BF16)
            grown_parts.append((dy * grown).astype(BF16))
            kept_parts.append(jnp.exp2(closing) * passing)
            acc_ref[8 * K + 8 : 8 * K + 16, span] += fold(dy * xc)
            d_conv = d_fed * step_pair + skip_ref[:, span] * dy
            conv_back(lo, d_conv, xr_ref[:, span].astype(F32))
        dy_grown = jnp.concatenate(grown_parts, axis=1)
        kept = jnp.concatenate(kept_parts, axis=1)
        dyd[:, block] = dy_grown
        through[:, block] = crossing * kept
        dstate[:, block] = d_held * kept + mm(c_t, dy_grown)

    d_scores_b = jnp.where(visible, d_scores, 0.0).astype(BF16)
    d_c = mm(dyd[...], st_ref[0], NT) + mm(d_scores_b, b_b)
    d_b = mm(fedw[...], dst_b[...], NT) + mm(d_scores_b, c_b, TN)
    conv_back(inner, d_b, small[:, :STATE])
    conv_back(inner + STATE, d_c, small[:, STATE : 2 * STATE])

    sel = sel_ref[...]
    red_ab = mm(ab_hi[...], sel) + mm(ab_lo[...], sel)
    red_v = mm(v_b[...], sel)
    red_u = mm(u_b[...], sel)
    thr = through[...]
    thr_hi = thr.astype(BF16)
    red_t = mm(thr_hi, sel) + mm((thr - thr_hi.astype(F32)).astype(BF16), sel)
    red_t = jnp.sum(red_t, axis=0, keepdims=True)
    d_rate = (
        mm_exact((same & (cols >= rows)).astype(F32), red_ab)
        + mm_exact((same & (cols < rows)).astype(F32), red_v)
        + red_t
    )
    d_step = red_u - d_rate * decay_rate
    d_dt = d_step * sigmoid(shifted)
    dx_ref[:, inner + 2 * STATE :] = d_dt.astype(BF16)
    hacc_ref[0:8, :] += fold(d_dt)
    hacc_ref[8:16, :] += fold(d_rate * (-decay_rate * step))
    halo_out[...] = dpre[:, Q : Q + 8, :]
    state_out[...] = dstate[...]


def load_blocks(offsets_ref, parts, whole, sems):
    @pl.when(pl.program_id(0) == 0)
    def _():
        copies = []
        count = sems.shape[0]
        size = whole.shape[0] // count
        for part in parts:
            for j in range(part.shape[0] // size):
                k = len(copies)
                start = pl.multiple_of(offsets_ref[k], 32) if count > 1 else 0
                source = part.at[pl.ds(j * size, size), :]
                copies.append(pltpu.make_async_copy(source, whole.at[pl.ds(start, size), :], sems.at[k]))
        for copy in copies:
            copy.start()
        for copy in copies:
            copy.wait()


def turn_rows(offsets_ref, me_ref, own_ref, other_ref, out_ref, turned):
    depth = own_ref.shape[1]
    rows = own_ref.shape[0]
    for index, source in enumerate((own_ref, other_ref)):
        at = pl.multiple_of(jnp.where(index == 0, me_ref[0], 1 - me_ref[0]) * rows, LANES)
        for lo in range(0, rows, Q):
            tile = source[lo : lo + Q, :].astype(F32)
            scale = lax.rsqrt(jnp.mean(tile * tile, axis=1, keepdims=True) + EPSILON)
            tile = tile * scale
            for left in range(0, depth, LANES):
                turned[left : left + LANES, pl.ds(at + lo, Q)] = tile[:, left : left + LANES].T.astype(BF16)
    count = offsets_ref.shape[0]
    size = depth // count
    for k in range(count):
        start = pl.multiple_of(offsets_ref[k], 32)
        out_ref[k * size : (k + 1) * size, :] = turned[pl.ds(start, size), :]


def project(count, heads, offsets_ref, me_ref, own_ref, other_ref, place_ref, *refs):
    blocks, (x_ref, small_ref, normed_ref, taps_ref, gain_ref, w_out_ref, w_ref, sems, out_sem) = refs[:count], refs[count:]
    load_blocks(offsets_ref, blocks, w_ref, sems)
    keep = pltpu.make_async_copy(w_ref, w_out_ref, out_sem)
    depth, inner = w_ref.shape[0], x_ref.shape[1]
    tile = 256

    @pl.when(pl.program_id(0) == 0)
    def _():
        keep.start()
        spare = w_ref[:, inner + 2 * STATE :]
        pick = jnp.where(iota((8, LANES), 1) == heads + K + 2, 1.0, 0.0).astype(BF16)
        gain_ref[...] = mm(pick, spare, NT)
        lanes = iota((depth, LANES), 1)
        for lo in range(0, inner + 2 * STATE, LANES):
            if lo < inner:
                wanted, row = place_ref[:, :LANES] == lanes + lo, heads
            else:
                wanted, row = place_ref[:, LANES:] == lanes + (lo - inner), heads + 8
            moved = mm(spare, jnp.where(wanted, 1.0, 0.0).astype(BF16), TN)
            taps_ref[:, lo : lo + LANES] = moved[row : row + 8, :]

    rows = jnp.where(pl.program_id(0) == me_ref[0], own_ref[...], other_ref[...]).astype(F32)
    scale = lax.rsqrt(jnp.mean(rows * rows, axis=1, keepdims=True) + EPSILON)
    rows = (rows * scale * gain_ref[0:1, :]).astype(BF16)
    normed_ref[...] = rows
    for lo in range(0, inner, tile):
        x_ref[:, lo : lo + tile] = mm(rows, w_ref[:, lo : lo + tile]).astype(BF16)
    small_ref[...] = mm(rows, w_ref[:, inner:])

    @pl.when(pl.program_id(0) == pl.num_programs(0) - 1)
    def _():
        keep.wait()


def row_sums(lanes):
    return mm_exact(jnp.ones((8, LANES), F32), lanes, NT)


def spread_rows(values):
    pick = jnp.where(iota((8, LANES), 0) == 0, 1.0, 0.0).astype(F32)
    return mm_exact(values, pick, TN)


def gate_forward(normed_ref, w_ref, y_ref, gain_ref, z_ref, gg_ref, sq_ref, square):
    rows, width = z_ref.shape
    size = 256

    @pl.when(pl.program_id(0) == 0)
    def _():
        square[...] = jnp.zeros(square.shape, F32)

    for lo in range(0, rows, size):
        at = slice(lo, lo + size)
        z = mm(normed_ref[at, :], w_ref[...]).astype(BF16)
        z_ref[at, :] = z
        z = z.astype(F32)
        gated = y_ref[at, :].astype(F32) * (z * sigmoid(z))
        gg_ref[at, :] = (gated * gain_ref[K + 1 : K + 2, :]).astype(BF16)
        twice = gated * gated
        for part in range(0, width, LANES):
            square[at, :] += twice[:, part : part + LANES]

    @pl.when(pl.program_id(0) == pl.num_programs(0) - 1)
    def _():
        sq_ref[...] = row_sums(square[...])


def branch(me_ref, ends_ref, gg_ref, own_ref, other_ref, w_ref, mine_ref, away_ref, prod_ref, product):
    rows, width = mine_ref.shape
    size = 256

    @pl.when(pl.program_id(0) == 0)
    def _():
        product[...] = jnp.zeros(product.shape, F32)

    for index, (out_ref, cot_ref) in enumerate(((mine_ref, own_ref), (away_ref, other_ref))):
        first = jnp.where(index == 0, me_ref[0], 1 - me_ref[0]) * rows
        for lo in range(0, rows, size):
            at = pl.ds(pl.multiple_of(first + lo, size), size)
            u = mm(gg_ref[at, :], w_ref[...], NT)
            out_ref[lo : lo + size, :] = u.astype(BF16)
            term = u * cot_ref[lo : lo + size, :].astype(F32)
            for part in range(0, width, LANES):
                product[at, :] += term[:, part : part + LANES]

    @pl.when(pl.program_id(0) == pl.num_programs(0) - 1)
    def _():
        live = iota(product.shape, 0) < ends_ref[ends_ref.shape[0] - 1]
        prod_ref[...] = row_sums(jnp.where(live, product[...], 0.0))


def gate_backward(
    me_ref, ends_ref, own_ref, other_ref, w_ref, y_ref, z_ref, rg_ref, coef_ref, gain_ref,
    dy_ref, dz_ref, acc_ref, rg, coef,
):
    total, width = dy_ref.shape
    rows = own_ref.shape[0]
    size = 256

    @pl.when(pl.program_id(0) == 0)
    def _():
        live = iota(rg.shape, 0) < ends_ref[ends_ref.shape[0] - 1]
        rg[...] = spread_rows(rg_ref[...])
        coef[...] = spread_rows(coef_ref[...])
        rg[...] = jnp.where(live, rg[...], 0.0)

    gain = gain_ref[K + 1 : K + 2, :]
    sums = jnp.zeros((8, width), F32)
    for index, cot_ref in enumerate((own_ref, other_ref)):
        first = jnp.where(index == 0, me_ref[0], 1 - me_ref[0]) * rows
        for lo in range(0, rows, size):
            at = pl.ds(pl.multiple_of(first + lo, size), size)
            ds = mm(cot_ref[lo : lo + size, :], w_ref[...])
            z = z_ref[at, :].astype(F32)
            y = y_ref[at, :].astype(F32)
            scale = jnp.concatenate([rg[at, :]] * (width // LANES), axis=1)
            back = jnp.concatenate([coef[at, :]] * (width // LANES), axis=1)
            gate = sigmoid(z)
            silu = z * gate
            gated = y * silu
            d_normal = ds * scale
            sums = sums + (d_normal * gated).reshape(size // 8, 8, width).sum(axis=0)
            d_gated = d_normal * gain - gated * back
            dy_ref[at, :] = (d_gated * silu).astype(BF16)
            dz_ref[at, :] = (d_gated * y * (gate + silu * (1.0 - gate))).astype(BF16)
    acc_ref[...] = sums


def weight_grad(turned_ref, d_ref, away_ref, keep_ref):
    half = away_ref.shape[0]
    size = 256
    d = d_ref[...]
    for lo in range(0, half, size):
        away_ref[lo : lo + size, :] = mm(turned_ref[lo : lo + size, :], d).astype(BF16)
    for lo in range(0, half, size):
        keep_ref[lo : lo + size, :] = mm(turned_ref[half + lo : half + lo + size, :], d).astype(BF16)


def normed_back(rows_ref, dz_ref, dx_ref, wz_ref, wx_ref, out_ref):
    size = 256
    for lo in range(0, out_ref.shape[0], size):
        at = slice(lo, lo + size)
        total = mm(dz_ref[at, :], wz_ref[...], NT) + mm(dx_ref[at, :], wx_ref[...], NT)
        out_ref[at, :] = total.astype(BF16)


def params():
    return pltpu.CompilerParams(dimension_semantics=("arbitrary",), vmem_limit_bytes=VMEM_LIMIT)


SMALL_COST = pl.CostEstimate(flops=1000, bytes_accessed=1000, transcendentals=0)


def rows_spec(block, width, column=0):
    return pl.BlockSpec((block, width), lambda i: (i, column))


def whole_spec(shape, column=0):
    return pl.BlockSpec(shape, lambda i: (0, column))


def local(
    tokens,
    cotangent,
    lengths,
    norm_gain,
    w_zx,
    w_bc,
    w_dt,
    conv_x,
    conv_x_bias,
    conv_bc,
    conv_bc_bias,
    dt_bias,
    a_log,
    d_skip,
    gate_gain,
    w_out,
):
    n_t = lax.axis_size("tensor")
    n_dp = lax.axis_size("dp")
    me_t = lax.axis_index("tensor")
    me_dp = lax.axis_index("dp")
    own_rows, depth = tokens.shape
    group = own_rows * n_t
    chunks = group // Q
    heads = dt_bias.shape[0]
    inner = heads * WIDTH
    inner_total = inner * n_t
    shard = w_zx.shape[1]
    pairs = [(i, n_t - 1 - i) for i in range(n_t)]

    def swap(v):
        return lax.ppermute(v, "tensor", pairs)

    def in_order(mine, other, axis=0):
        low = jnp.where(me_t == 0, mine, other)
        high = jnp.where(me_t == 0, other, mine)
        return jnp.concatenate([low, high], axis=axis)

    def sum_dp(v):
        step = 1
        while step < n_dp:
            v = v + lax.ppermute(v, "dp", [(i, i ^ step) for i in range(n_dp)])
            step *= 2
        return v

    def after(value, *others):
        return lax.optimization_barrier((value, *others))[0]

    ring = 4
    plane = n_dp // (2 * ring)

    around = [(i, (i + 2 * plane) % n_dp) for i in range(n_dp)]
    across = [(i, i ^ 2) for i in range(n_dp)]
    beside = [(i, i ^ 1) for i in range(n_dp)]

    def send(v, way):
        return lax.ppermute(v, "dp", way)

    by_hand = plane == 2 and shard % 32 == 0

    def whole(v):
        return [lax.all_gather(v, "dp", axis=0, tiled=True)]

    def block_offsets(count, size):
        if count == 1:
            return jnp.zeros((1,), jnp.int32)
        places = []
        for core in range(2):
            for side in range(2):
                for turn in range(ring):
                    level = (me_dp // (2 * plane) - turn + ring) % ring
                    places.append(level * (2 * plane) + ((me_dp % (2 * plane)) ^ (2 * side + core)))
        return jnp.stack(places).astype(jnp.int32) * size

    def relative_order():
        level, side, core = me_dp // 4, (me_dp // 2) % 2, me_dp % 2
        order = []
        for dc in (1, 0):
            for dy in (1, 0):
                for dz in range(1, ring + 1):
                    order.append(((level - dz + ring) % ring) * 4 + (side ^ dy) * 2 + (core ^ dc))
        return order

    def fold_beside(keep, got):
        half = keep.shape[0] // 2
        away = (keep[:half].astype(F32) + got[:half].astype(F32)).astype(BF16)
        return away, keep[half:].astype(F32) + got[half:].astype(F32)

    def fold_turn(total, got, turn):
        part = total[(turn - 1) * shard : turn * shard] + got.astype(F32)
        return part if turn == ring else part.astype(BF16)

    ends = jnp.cumsum(lengths[0]).astype(jnp.int32)
    live = (lax.iota(jnp.int32, group) < ends[-1]).astype(F32)
    live_own = lax.dynamic_slice_in_dim(live, me_t * own_rows, own_rows, 0)
    me = me_t.astype(jnp.int32).reshape(1)

    span_p = conv_x_bias.shape[1]
    span_n = conv_bc_bias.shape[1]
    half_bc = w_bc.shape[1]
    bits = jnp.concatenate([norm_gain, conv_bc.reshape(-1), conv_bc_bias.reshape(-1)])
    bits = jnp.pad(bits, (0, LANES - bits.shape[0]))
    tiny = jnp.concatenate([w_bc.reshape(2 * half_bc, STATE), bits[None]], axis=0)
    other_tiny = swap(tiny)
    other_bc = other_tiny[: 2 * half_bc].reshape(w_bc.shape)
    both_bits = [bits, other_tiny[2 * half_bc]]
    at = norm_gain.shape[0]
    gain_pair = in_order(*[v[:at] for v in both_bits])[:, None]
    taps_bc = in_order(*[v[at : at + conv_bc.size].reshape(2, span_n, K) for v in both_bits], axis=1)
    at += conv_bc.size
    bias_bc = in_order(*[v[at : at + 2 * span_n].reshape(2, span_n, 1) for v in both_bits], axis=1)
    spare_bc = jnp.concatenate([taps_bc, bias_bc], axis=2).reshape(4 * span_n, K + 1)
    spare_x = [conv_x.reshape(shard, K), conv_x_bias.reshape(shard, 1), gate_gain.reshape(shard, 1), gain_pair]
    bc_pair = in_order(w_bc, other_bc, axis=1)
    packed = jnp.concatenate(
        [w_zx[1], bc_pair[0], bc_pair[1], w_dt, *spare_x, jnp.zeros((shard, 8 - K - 3), BF16)]
        + [jnp.pad(spare_bc, ((0, shard - 4 * span_n), (0, LANES - heads - 8 - K - 1)))],
        axis=1,
    )
    gain_pair = gain_pair.astype(F32)
    where = lax.iota(jnp.int32, depth)
    home, inside = where // shard, where % shard
    place_x = (inside // span_p) * WIDTH + home * span_p + inside % span_p
    half_n = 2 * span_n
    place_bc = (inside // half_n) * STATE + home * half_n + inside % half_n
    place = jnp.concatenate([jnp.broadcast_to(v[:, None], (depth, LANES)) for v in (place_x, place_bc)], axis=1)
    par = jnp.concatenate([dt_bias[None], a_log[None], jnp.zeros((6, heads), F32)], axis=0)
    par = jnp.concatenate([par, jnp.zeros((8, LANES - heads), F32)], axis=1)
    skip = jnp.repeat(d_skip, WIDTH)[None]
    members = lax.iota(jnp.int32, inner)[:, None] // WIDTH
    sel = (members == lax.iota(jnp.int32, LANES)[None, :]).astype(BF16)
    smem = pl.BlockSpec(memory_space=pltpu.SMEM)
    vmem = pl.BlockSpec(memory_space=pltpu.VMEM)
    hbm = pl.BlockSpec(memory_space=pl.ANY)
    n_small = 2 * STATE + LANES
    n_conv = inner + 2 * STATE
    w_rest = jnp.concatenate([w_zx[0], w_out.T], axis=1)

    def turn(other_tokens):
        return pl.pallas_call(
            turn_rows,
            in_specs=[smem, smem, vmem, vmem],
            out_specs=vmem,
            out_shape=jax.ShapeDtypeStruct((depth, group), BF16),
            scratch_shapes=[pltpu.VMEM((depth, group), BF16)],
            compiler_params=pltpu.CompilerParams(vmem_limit_bytes=VMEM_LIMIT),
            cost_estimate=SMALL_COST,
            name="turn_rows",
        )((jnp.stack(relative_order()) * shard).astype(jnp.int32), me, tokens, other_tokens)

    if by_hand:
        line, other, line_c, other_c = [packed], [], [], []
        pieces = [tokens[:176], tokens[176:352], tokens[352:]]
        line[0], *pieces = lax.optimization_barrier((packed, *pieces))
        arrived, held_turn, constants = [], [], []
        for step in range(ring + 1):
            made = []
            if step < ring - 1:
                made.append((line, send(line[step], around)))
                made.append((arrived, swap(after(pieces[step], line[step]))))
            if step < ring:
                made.append((other, send(line[step], across)))
                made.append((line_c, send(line[step], beside)))
            if step:
                made.append((other_c, send(other[step - 1], beside)))
            if step == 2:
                zo_all = lax.all_gather(after(w_rest, line[2]), "dp", axis=0, tiled=True)
            if step == 0:
                made += [(constants, v) for v in (place, par, skip, sel)]
            if step == 3:
                other_tokens = jnp.concatenate(arrived, axis=0)
                made.append((held_turn, turn(after(other_tokens, line[3]))))
                other_cot = swap(after(cotangent, other_tokens))
            fresh = lax.optimization_barrier(tuple(value for _, value in made))
            for (place_in, _), value in zip(made, fresh):
                place_in.append(value)
        wx_blocks = line + other + line_c + other_c
        turned = held_turn[0]
        place, par, skip, sel = constants
    else:
        wx_blocks = whole(packed)
        zo_all = whole(w_rest)[0]
        other_tokens, other_cot = swap(tokens), swap(cotangent)
    count = len(wx_blocks)
    offsets = block_offsets(count, shard)
    sems = pltpu.SemaphoreType.DMA((count,))
    tok_own = tokens.astype(F32)
    inv_tok = lax.rsqrt(jnp.mean(tok_own * tok_own, axis=1, keepdims=True) + EPSILON)

    block = own_rows
    steps = group // block
    x_raw, small, normed, taps, gain_in, wx_all = pl.pallas_call(
        partial(project, count, heads),
        grid=(steps,),
        in_specs=[
            smem,
            smem,
            whole_spec((block, depth)),
            whole_spec((block, depth)),
            whole_spec((depth, 2 * LANES)),
        ]
        + [hbm] * count,
        out_specs=[
            rows_spec(block, inner),
            rows_spec(block, n_small),
            rows_spec(block, depth),
            whole_spec((8, n_conv)),
            whole_spec((8, depth)),
            hbm,
        ],
        out_shape=[
            jax.ShapeDtypeStruct((group, inner), BF16),
            jax.ShapeDtypeStruct((group, n_small), F32),
            jax.ShapeDtypeStruct((group, depth), BF16),
            jax.ShapeDtypeStruct((8, n_conv), F32),
            jax.ShapeDtypeStruct((8, depth), F32),
            jax.ShapeDtypeStruct((depth, inner + n_small), BF16),
        ],
        scratch_shapes=[pltpu.VMEM((depth, inner + n_small), BF16), sems, pltpu.SemaphoreType.DMA],
        compiler_params=params(),
        cost_estimate=SMALL_COST,
        name="project",
    )(offsets, me, tokens, other_tokens, place, *wx_blocks)
    xc, pre, bc, y_all, states = pl.pallas_call(
        partial(scan_forward, heads),
        grid=(chunks,),
        in_specs=[
            smem,
            rows_spec(Q, inner),
            rows_spec(Q, n_small),
            whole_spec((8, n_conv)),
            whole_spec((8, LANES)),
            whole_spec((1, inner)),
        ],
        out_specs=[
            rows_spec(Q, inner),
            rows_spec(Q, n_conv),
            rows_spec(Q, 2 * STATE),
            rows_spec(Q, inner),
            pl.BlockSpec((1, STATE, inner), lambda i: (i, 0, 0)),
        ],
        out_shape=[
            jax.ShapeDtypeStruct((group, inner), BF16),
            jax.ShapeDtypeStruct((group, n_conv), BF16),
            jax.ShapeDtypeStruct((group, 2 * STATE), BF16),
            jax.ShapeDtypeStruct((group, inner), BF16),
            jax.ShapeDtypeStruct((chunks, STATE, inner), BF16),
        ],
        scratch_shapes=[pltpu.VMEM((n_conv // LANES, Q + 8, LANES), F32), pltpu.VMEM((STATE, inner), F32)],
        compiler_params=params(),
        cost_estimate=SMALL_COST,
        name="scan_forward",
    )(ends, x_raw, small, taps, par, skip)

    tile = 256
    columns = lambda rows, shift=0: pl.BlockSpec((rows, tile), lambda j: (0, j + shift))
    fixed = lambda shape: pl.BlockSpec(shape, lambda j: (0, 0))
    tiles = inner // tile
    z_all, gg, sq = pl.pallas_call(
        gate_forward,
        grid=(tiles,),
        in_specs=[fixed((group, depth)), columns(depth), columns(group), columns(8)],
        out_specs=[columns(group), columns(group), fixed((8, group))],
        out_shape=[
            jax.ShapeDtypeStruct((group, inner), BF16),
            jax.ShapeDtypeStruct((group, inner), BF16),
            jax.ShapeDtypeStruct((8, group), F32),
        ],
        scratch_shapes=[pltpu.VMEM((group, LANES), F32)],
        compiler_params=params(),
        cost_estimate=SMALL_COST,
        name="gate_forward",
    )(normed, zo_all, y_all, taps)
    sq_got = swap(sq)

    u_own, u_send, prod = pl.pallas_call(
        branch,
        grid=(depth // tile,),
        in_specs=[
            smem,
            smem,
            fixed((group, inner)),
            columns(own_rows),
            columns(own_rows),
            pl.BlockSpec((tile, inner), lambda j: (j, 1)),
        ],
        out_specs=[columns(own_rows), columns(own_rows), fixed((8, group))],
        out_shape=[
            jax.ShapeDtypeStruct((own_rows, depth), BF16),
            jax.ShapeDtypeStruct((own_rows, depth), BF16),
            jax.ShapeDtypeStruct((8, group), F32),
        ],
        scratch_shapes=[pltpu.VMEM((group, LANES), F32)],
        compiler_params=params(),
        cost_estimate=SMALL_COST,
        name="branch",
    )(me, ends, gg, cotangent, other_cot, zo_all)
    prod_got = swap(prod)
    sq_all = sq + after(sq_got, prod)
    inv_gate8 = lax.rsqrt(sq_all / inner_total + EPSILON)
    inv_gate = inv_gate8[0]
    cot_all = in_order(cotangent, other_cot)
    d_branch = (cot_all.astype(F32) * (live * inv_gate)[:, None]).astype(BF16)
    g_out = lax.dot_general(d_branch, gg, TN, preferred_element_type=F32).astype(BF16)
    grad_out = lax.psum_scatter(g_out, "dp", scatter_dimension=0, tiled=True)
    prod_got = after(prod_got, g_out)
    u_recv = swap(after(u_send, g_out))
    inv_own = lax.dynamic_slice_in_dim(inv_gate, me_t * own_rows, own_rows, 0)
    out_branch = (u_own.astype(F32) + u_recv.astype(F32)) * (inv_own * live_own)[:, None]
    layer_out = (tokens.astype(F32) + out_branch).astype(BF16)

    prod_all = prod + prod_got
    coef8 = inv_gate8 * inv_gate8 * inv_gate8 * (prod_all / inner_total)
    dy, dz, gain_acc = pl.pallas_call(
        gate_backward,
        grid=(tiles,),
        in_specs=[
            smem,
            smem,
            fixed((own_rows, depth)),
            fixed((own_rows, depth)),
            columns(depth, tiles),
            columns(group),
            columns(group),
            fixed((8, group)),
            fixed((8, group)),
            columns(8),
        ],
        out_specs=[columns(group), columns(group), columns(8)],
        out_shape=[
            jax.ShapeDtypeStruct((group, inner), BF16),
            jax.ShapeDtypeStruct((group, inner), BF16),
            jax.ShapeDtypeStruct((8, inner), F32),
        ],
        scratch_shapes=[pltpu.VMEM((group, LANES), F32), pltpu.VMEM((group, LANES), F32)],
        compiler_params=params(),
        cost_estimate=SMALL_COST,
        name="gate_backward",
    )(me, ends, cotangent, other_cot, zo_all, y_all, z_all, inv_gate8, coef8, taps)
    dot = partial(lax.dot_general, preferred_element_type=F32)
    front = depth // 2

    def gradient(d, width, first, number):
        outs = pl.BlockSpec((front, width), lambda j: (0, j))
        return pl.pallas_call(
            weight_grad,
            grid=(number,),
            in_specs=[fixed((depth, group)), pl.BlockSpec((group, width), lambda j: (0, j + first))],
            out_specs=[outs, outs],
            out_shape=[jax.ShapeDtypeStruct((front, width * number), BF16)] * 2,
            compiler_params=params(),
            cost_estimate=SMALL_COST,
            name="weight_grad",
        )(turned, d)

    if by_hand:
        g_send, z_keep = gradient(dz, tile, 0, tiles)
        z_got = send(g_send, beside)
        dy = after(dy, z_keep, g_send)
    else:
        grad_z = lax.psum_scatter(dot(normed, dz, TN).astype(BF16), "dp", scatter_dimension=0, tiled=True)

    halo_spec = pl.BlockSpec((n_conv // LANES, 8, LANES), lambda i: (0, 0, 0))

    def backward(top, number, carry):
        back = lambda width: pl.BlockSpec((Q, width), lambda i: (top - i, 0))
        operands = [ends, dy, xc, pre, x_raw, small, bc, states, taps, par, skip, sel, *carry]
        return pl.pallas_call(
            partial(scan_backward, heads, chunks, top),
            grid=(number,),
            in_specs=[
                smem,
                back(inner),
                back(inner),
                back(n_conv),
                back(inner),
                back(n_small),
                back(2 * STATE),
                pl.BlockSpec((1, STATE, inner), lambda i: (top - i, 0, 0)),
                whole_spec((8, n_conv)),
                whole_spec((8, LANES)),
                whole_spec((1, inner)),
                whole_spec((inner, LANES)),
            ]
            + ([whole_spec((STATE, inner)), halo_spec, hbm] if carry else []),
            out_specs=[
                back(inner + n_small),
                whole_spec((8 * (K + 2), n_conv)),
                whole_spec((16, LANES)),
                whole_spec((STATE, inner)),
                halo_spec,
            ],
            out_shape=[
                jax.ShapeDtypeStruct((group, inner + n_small), BF16),
                jax.ShapeDtypeStruct((8 * (K + 2), n_conv), F32),
                jax.ShapeDtypeStruct((16, LANES), F32),
                jax.ShapeDtypeStruct((STATE, inner), F32),
                jax.ShapeDtypeStruct((n_conv // LANES, 8, LANES), F32),
            ],
            scratch_shapes=[
                pltpu.VMEM((STATE, inner), F32),
                pltpu.VMEM((n_conv // LANES, Q + 8, LANES), F32),
                pltpu.VMEM((Q, inner), BF16),
                pltpu.VMEM((Q, inner), BF16),
                pltpu.VMEM((Q, inner), BF16),
                pltpu.VMEM((Q, inner), BF16),
                pltpu.VMEM((Q, inner), BF16),
                pltpu.VMEM((Q, inner), BF16),
                pltpu.VMEM((STATE, inner), BF16),
                pltpu.VMEM((8, inner), F32),
            ],
            input_output_aliases={len(operands) - 1: 0} if carry else {},
            compiler_params=params(),
        cost_estimate=SMALL_COST,
            name="scan_backward",
        )(*operands)

    half_chunks = chunks // 2
    dx, acc_a, hacc_a, d_state, halo = backward(chunks - 1, chunks - half_chunks, ())
    if by_hand:
        z_got, dx = lax.optimization_barrier((z_got, dx))
        z_away, z_keep = fold_beside(z_keep, z_got)
        z_got = send(z_away, across)
        d_state = after(d_state, z_away, z_keep)
    dx, acc, hacc, _, _ = backward(half_chunks - 1, half_chunks, (d_state, halo, dx))
    dx = after(dx, u_recv)
    if by_hand:
        xa_send, xa_keep = gradient(dx, 384, 0, 3)
        xa_got = send(xa_send, beside)
        xb_send, xb_keep = gradient(after(dx, xa_send), 384, 3, 2)
        xb_got = send(xb_send, beside)
        z_got, acc, acc_a = lax.optimization_barrier((z_got, acc, acc_a, xb_send))[:3]
        z_total = z_keep + z_got.astype(F32)
        z_got = send(z_total[:shard].astype(BF16), around)
        xa_got = after(xa_got, xb_send)
        xa_away, xa_keep = fold_beside(xa_keep, xa_got)
        xa_away, grad_out = lax.optimization_barrier((xa_away, grad_out))
        xa_got = send(xa_away, across)
        xb_got = after(xb_got, xa_away, xa_keep)
        xb_away, xb_keep = fold_beside(xb_keep, xb_got)
        xb_got = send(xb_away, across)
        dz, acc, acc_a = lax.optimization_barrier((dz, acc, acc_a, xb_away, xb_keep, z_total))[:3]
    else:
        grad_x = lax.psum_scatter(dot(normed, dx, TN).astype(BF16), "dp", scatter_dimension=0, tiled=True)

    acc = acc + acc_a
    hacc = hacc + hacc_a
    acc = acc.reshape(K + 2, 8, n_conv).sum(axis=1)
    hsum = hacc.reshape(2, 8, LANES).sum(axis=1)
    d_gate = gain_acc.sum(axis=0)
    d_sk = acc[K + 1, :inner].reshape(heads, WIDTH).sum(axis=1)
    shared = acc[: K + 1, inner:]
    headed = [acc[: K + 1, :inner].reshape(-1), d_gate, hsum[:, :heads].reshape(-1), d_sk]
    shared_got = swap(shared)
    vector = jnp.concatenate([(shared + shared_got).reshape(-1)] + headed)
    vector = jnp.concatenate([vector, jnp.zeros((-vector.shape[0] % 1024,), F32)]).reshape(-1, LANES)

    def back_rows(which, dz):
        pick = lambda width: pl.BlockSpec((own_rows, width), lambda j, rows: (rows[0], 0))
        return pl.pallas_call(
            normed_back,
            grid_spec=pltpu.PrefetchScalarGridSpec(
                num_scalar_prefetch=1,
                grid=(depth // tile,),
                in_specs=[
                    pick(inner),
                    pick(inner + n_small),
                    pl.BlockSpec((tile, inner), lambda j, rows: (j, 0)),
                    pl.BlockSpec((tile, inner + n_small), lambda j, rows: (j, 0)),
                ],
                out_specs=pl.BlockSpec((own_rows, tile), lambda j, rows: (0, j)),
            ),
            out_shape=jax.ShapeDtypeStruct((own_rows, depth), BF16),
            compiler_params=params(),
            cost_estimate=SMALL_COST,
            name="normed_back",
        )(which, dz, dx, zo_all, wx_all)

    dn_send = back_rows(n_t - 1 - me, dz)
    if by_hand:
        sizes, dn_parts, at = (160, 128, 112, 112), [], 0
        for size in sizes:
            dn_parts.append(dn_send[at : at + size])
            at += size
        bits_of = lambda turn: [(i, i ^ (1 << turn)) for i in range(n_dp)]
        xa_got, z_got, vector, *dn_parts = lax.optimization_barrier((xa_got, z_got, vector, *dn_parts))
        xa_total = xa_keep + xa_got.astype(F32)
        xa_got = xa_total[:shard].astype(BF16)
        z_got = fold_turn(z_total, z_got, 2)
        moved = [send(xa_got, around), send(z_got, around), swap(dn_parts[0]), send(vector, bits_of(0))]
        dn_own = back_rows(me, after(dz, xa_got, z_got, *dn_parts))
        moved = lax.optimization_barrier((*moved, dn_own, xb_got))
        dn_own = moved[4]
        xb_total = xb_keep + moved[5].astype(F32)
        xb_got = xb_total[:shard].astype(BF16)
        xa_got = fold_turn(xa_total, moved[0], 2)
        z_got = fold_turn(z_total, moved[1], 3)
        dn_got, vector = [moved[2]], vector + moved[3]
        moved = [send(xb_got, around), send(xa_got, around), send(z_got, around)]
        moved = lax.optimization_barrier((*moved, swap(dn_parts[1]), send(vector, bits_of(1))))
        xb_got = fold_turn(xb_total, moved[0], 2)
        xa_got = fold_turn(xa_total, moved[1], 3)
        grad_z = fold_turn(z_total, moved[2], ring) * gain_pair
        dn_got.append(moved[3])
        vector = vector + moved[4]
        moved = [send(xb_got, around), send(xa_got, around), swap(after(dn_parts[2], xb_got)), send(vector, bits_of(2))]
        moved = lax.optimization_barrier((*moved, grad_z, grad_out))
        xb_got = fold_turn(xb_total, moved[0], 3)
        xa_got = fold_turn(xa_total, moved[1], ring)
        dn_got.append(moved[2])
        vector = vector + moved[3]
        grad_z, grad_out = moved[4:]
        moved = [send(xb_got, around), swap(after(dn_parts[3], xb_got)), send(vector, bits_of(3))]
        moved = lax.optimization_barrier(tuple(moved))
        xb_got = fold_turn(xb_total, moved[0], ring)
        dn_got = jnp.concatenate(dn_got + [moved[1]], axis=0)
        vector = vector + moved[2]
        grad_x = jnp.concatenate([xa_got, xb_got], axis=1) * gain_pair
    else:
        vector = sum_dp(vector)
        dn_own = back_rows(me, dz)
        dn_got = swap(dn_send)
    dn = (dn_own.astype(F32) + dn_got.astype(F32)) * gain_in[0:1, :]
    grad_tokens = (
        cotangent.astype(F32)
        + inv_tok * dn
        - tok_own * inv_tok * inv_tok * inv_tok * jnp.mean(dn * tok_own, axis=1, keepdims=True)
    )

    vector = vector.reshape(-1)
    n_bc = (K + 1) * 2 * STATE
    bc_sum = vector[:n_bc].reshape(K + 1, 2, STATE)
    me_all = me_dp * n_t + me_t
    bc_sum = lax.dynamic_slice_in_dim(bc_sum, me_all * span_n, span_n, 2)
    grad_bc_taps = bc_sum[:K].transpose(1, 2, 0).reshape(conv_bc.shape)
    grad_bc_bias = bc_sum[K]
    at = n_bc
    x_sum = vector[at : at + (K + 1) * inner].reshape(K + 1, heads, WIDTH)
    at += (K + 1) * inner
    x_sum = lax.dynamic_slice_in_dim(x_sum, me_dp * span_p, span_p, 2)
    grad_x_taps = x_sum[:K].transpose(1, 2, 0).reshape(conv_x.shape)
    grad_x_bias = x_sum[K]
    grad_gate = lax.dynamic_slice_in_dim(vector[at : at + inner].reshape(heads, WIDTH), me_dp * span_p, span_p, 1)
    at += inner
    grad_dt_bias = vector[at : at + heads]
    grad_a_log = vector[at + heads : at + 2 * heads]
    grad_skip = vector[at + 2 * heads : at + 3 * heads]

    grad_z = grad_z.astype(F32)
    grad_x = grad_x.astype(F32)
    in_part = jnp.sum(w_zx[0].astype(F32) * grad_z, axis=1) + jnp.sum(packed.astype(F32) * grad_x, axis=1)
    in_part = in_part[:, None]
    grad_zx = jnp.stack([grad_z, grad_x[:, :inner]])
    grad_dt = grad_x[:, inner + 2 * STATE : inner + 2 * STATE + heads]
    bc_part = jnp.concatenate([grad_x[:, inner : inner + 2 * STATE], jnp.broadcast_to(in_part, (shard, LANES))], axis=1)
    half = half_bc
    bc_own = lax.dynamic_slice_in_dim(bc_part, me_t * half, half, 0)
    bc_send = lax.dynamic_slice_in_dim(bc_part, (n_t - 1 - me_t) * half, half, 0)
    bc_total = bc_own + swap(bc_send)
    own_gain = norm_gain.astype(F32)
    grad_bc = bc_total[:, : 2 * STATE].reshape(half, 2, STATE).transpose(1, 0, 2)
    grad_in = bc_total[:, 2 * STATE] / own_gain
    return (
        layer_out,
        grad_tokens,
        grad_in,
        grad_zx,
        grad_bc,
        grad_dt,
        grad_x_taps,
        grad_x_bias,
        grad_bc_taps,
        grad_bc_bias,
        grad_dt_bias,
        grad_a_log,
        grad_skip,
        grad_gate,
        grad_out.astype(F32).T,
    )


def solution(mesh):
    both = ("dp", "tensor")
    in_specs = (
        P(both, None),
        P(both, None),
        P("dp", None),
        P(both),
        P(None, "dp", "tensor"),
        P(None, both, None),
        P("dp", "tensor"),
        P("tensor", "dp"),
        P("tensor", "dp"),
        P(None, both),
        P(None, both),
        P("tensor"),
        P("tensor"),
        P("tensor"),
        P("tensor", "dp"),
        P("tensor", "dp"),
    )
    out_specs = (
        P(both, None),
        P(both, None),
        P(both),
        P(None, "dp", "tensor"),
        P(None, both, None),
        P("dp", "tensor"),
        P("tensor", "dp"),
        P("tensor", "dp"),
        P(None, both),
        P(None, both),
        P("tensor"),
        P("tensor"),
        P("tensor"),
        P("tensor", "dp"),
        P("tensor", "dp"),
    )
    return jax.shard_map(local, mesh=mesh, in_specs=in_specs, out_specs=out_specs, check_vma=False)
```

```python
from functools import partial

import jax
import jax.numpy as jnp
from jax import lax
from jax.experimental import pallas as pl
from jax.experimental.pallas import tpu as pltpu
from jax.sharding import PartitionSpec as P

EPSILON = 1e-05
HIGHEST = lax.Precision.HIGHEST
K = 4
WIDTH = 64
STATE = 128
Q = 128
LANES = 128
LOG2E = 1.4426950408889634
VMEM_LIMIT = 60 * 1024 * 1024
F32 = jnp.float32
BF16 = jnp.bfloat16

NN = (((1,), (0,)), ((), ()))
NT = (((1,), (1,)), ((), ()))
TN = (((0,), (0,)), ((), ()))


def mm(a, b, dims=NN):
    return lax.dot_general(a, b, dims, preferred_element_type=F32)


def mm_exact(a, b, dims=NN):
    return lax.dot_general(a, b, dims, preferred_element_type=F32, precision=HIGHEST)


def iota(shape, dim):
    return lax.broadcasted_iota(jnp.int32, shape, dim)


def segment_of(rows, ends_ref, count):
    total = (rows >= ends_ref[0]).astype(jnp.int32)
    for j in range(1, count):
        total = total + (rows >= ends_ref[j]).astype(jnp.int32)
    return total


def scalar_segment(row, ends_ref, count):
    total = jnp.where(row >= ends_ref[0], 1, 0)
    for j in range(1, count):
        total = total + jnp.where(row >= ends_ref[j], 1, 0)
    return total


def sigmoid(v):
    return 0.5 * jnp.tanh(0.5 * v) + 0.5


def softplus(v):
    return jnp.maximum(v, 0.0) + jnp.log1p(jnp.exp(-jnp.abs(v)))


def chunk_masks(chunk, ends_ref, count):
    base = chunk * Q
    rows = iota((Q, Q), 0) + base
    cols = iota((Q, Q), 1) + base
    row_ids = segment_of(rows, ends_ref, count)
    col_ids = segment_of(cols, ends_ref, count)
    same = row_ids == col_ids
    before_id = jnp.where(chunk == 0, -1, scalar_segment(base - 1, ends_ref, count))
    final_id = scalar_segment(base + Q - 1, ends_ref, count)
    carry = (row_ids == before_id).astype(F32)
    last = (row_ids == final_id).astype(F32)
    passing = jnp.where(before_id == final_id, 1.0, 0.0).astype(F32)
    return rows, cols, row_ids, same, carry, last, passing


def decays(dt_raw, par_ref):
    shifted = dt_raw + par_ref[0:1, :]
    step = softplus(shifted)
    decay_rate = jnp.exp(par_ref[1:2, :])
    return shifted, step, decay_rate


def pair_columns(values, pair, first):
    left = jnp.broadcast_to(values[:, 2 * pair : 2 * pair + 1], (Q, LANES))
    right = jnp.broadcast_to(values[:, 2 * pair + 1 : 2 * pair + 2], (Q, LANES))
    return left, right, jnp.where(first, left, right)


def scan_forward(
    heads, ends_ref, xr_ref, small_ref, taps_ref, par_ref, skip_ref,
    xc_ref, pre_ref, bc_ref, y_ref, st_ref, buf, state,
):
    count = ends_ref.shape[0]
    inner = heads * WIDTH
    chunk = pl.program_id(0)

    @pl.when(chunk == 0)
    def _():
        buf[:, 0:8, :] = jnp.zeros((buf.shape[0], 8, LANES), F32)
        state[...] = jnp.zeros(state.shape, F32)

    rows, cols, row_ids, same, carry, last, passing = chunk_masks(chunk, ends_ref, count)
    causal = rows >= cols
    visible = same & causal
    lag_mask = [None]
    for lag in range(1, K):
        earlier = rows - lag
        keep = (segment_of(earlier, ends_ref, count) == row_ids) & (earlier >= 0)
        lag_mask.append(keep.astype(F32))

    small = small_ref[...]

    def convolve(lo, raw):
        span = slice(lo, lo + LANES)
        place = lo // LANES
        buf[place, 8 : 8 + Q, :] = raw
        pre = taps_ref[K : K + 1, span] + taps_ref[K - 1 : K, span] * raw
        for lag in range(1, K):
            pre = pre + taps_ref[K - 1 - lag : K - lag, span] * (
                buf[place, 8 - lag : 8 - lag + Q, :] * lag_mask[lag]
            )
        buf[place, 0:8, :] = raw[Q - 8 : Q, :]
        pre_ref[:, span] = pre.astype(BF16)
        return pre * sigmoid(pre)

    b_f = convolve(inner, small[:, :STATE]).astype(BF16).astype(F32)
    c_b = convolve(inner + STATE, small[:, STATE : 2 * STATE]).astype(BF16)
    b_b = b_f.astype(BF16)
    bc_ref[:, :STATE] = b_b
    bc_ref[:, STATE:] = c_b
    b_t = b_f.T.astype(BF16)

    _, step, decay_rate = decays(small[:, 2 * STATE :], par_ref)
    csum = mm_exact(causal.astype(F32), step * (-LOG2E * decay_rate))
    csum_t = csum.T
    scores = jnp.where(visible, mm(c_b, b_b, NT), 0.0)
    first = iota((Q, LANES), 1) < WIDTH
    first_row = iota((1, LANES), 1) < WIDTH

    wide = 2 * LANES
    for quad in range(0, inner, wide):
        block = slice(quad, quad + wide)
        held = state[:, block]
        held_b = held.astype(BF16)
        st_ref[0, :, block] = held_b
        carried = mm(c_b, held_b)
        weighted, kept = [], []
        for part in range(0, wide, LANES):
            lo = quad + part
            pair = lo // LANES
            span = slice(lo, lo + LANES)
            xc = convolve(lo, xr_ref[:, span].astype(F32)).astype(BF16)
            xc_ref[:, span] = xc
            xc = xc.astype(F32)
            left, right, both = pair_columns(csum, pair, first)
            _, _, step_pair = pair_columns(step, pair, first)
            mix = jnp.concatenate(
                [
                    (scores * jnp.exp2(jnp.minimum(left - csum_t[2 * pair : 2 * pair + 1, :], 0.0))).astype(BF16),
                    (scores * jnp.exp2(jnp.minimum(right - csum_t[2 * pair + 1 : 2 * pair + 2, :], 0.0))).astype(BF16),
                ],
                axis=1,
            )
            fed_b = (xc * step_pair).astype(BF16)
            zero = jnp.zeros((Q, LANES), BF16)
            stacked = jnp.concatenate([jnp.where(first, fed_b, zero), jnp.where(first, zero, fed_b)], axis=0)
            y = mm(mix, stacked) + carried[:, part : part + LANES] * (jnp.exp2(both) * carry)
            y_ref[:, span] = (y + skip_ref[:, span] * xc).astype(BF16)
            closing = both[Q - 1 : Q, :]
            weighted.append((fed_b.astype(F32) * (jnp.exp2(closing - both) * last)).astype(BF16))
            kept.append(jnp.exp2(closing) * passing)
        fresh = mm(b_t, jnp.concatenate(weighted, axis=1))
        state[:, block] = held * jnp.concatenate(kept, axis=1) + fresh


def scan_backward(
    heads, chunks, top, ends_ref, dy_ref, xc_ref, pre_ref, xr_ref, small_ref, bc_ref, st_ref, taps_ref, par_ref,
    skip_ref, sel_ref, *refs,
):
    later_call = top + 1 < chunks
    if later_call:
        state_in, halo_in, acc_in, hacc_in, gain_acc_ref, _ = refs[:6]
        dx_ref, rows_ref, acc_ref, hacc_ref = refs[6:10]
        refs = refs[10:]
    else:
        dx_ref, acc_ref, hacc_ref, state_out, halo_out = refs[:5]
        refs = refs[5:]
    dstate, dpre, ab_hi, ab_lo, v_b, u_b, dyd, fedw, dst_b, through = refs
    count = ends_ref.shape[0]
    inner = heads * WIDTH
    total_rows = chunks * Q
    chunk = top - pl.program_id(0)

    @pl.when(pl.program_id(0) == 0)
    def _():
        if top + 1 < chunks:
            dpre[:, Q : Q + 8, :] = halo_in[...]
            dstate[...] = state_in[...]
            acc_ref[...] = acc_in[...]
            hacc_ref[...] = hacc_in[...]
        else:
            dpre[:, Q : Q + 8, :] = jnp.zeros((dpre.shape[0], 8, LANES), F32)
            dstate[...] = jnp.zeros(dstate.shape, F32)
            acc_ref[...] = jnp.zeros(acc_ref.shape, F32)
            hacc_ref[...] = jnp.zeros(hacc_ref.shape, F32)

    rows, cols, row_ids, same, carry, last, passing = chunk_masks(chunk, ends_ref, count)
    causal = rows >= cols
    visible = same & causal
    lag_mask = [None]
    for lag in range(1, K):
        later = rows + lag
        keep = (segment_of(later, ends_ref, count) == row_ids) & (later < total_rows)
        lag_mask.append(keep.astype(F32))

    small = small_ref[...]
    shifted, step, decay_rate = decays(small[:, 2 * STATE :], par_ref)
    csum = mm_exact(causal.astype(F32), step * (-LOG2E * decay_rate))
    csum_t = csum.T
    b_b = bc_ref[:, :STATE]
    c_b = bc_ref[:, STATE:]
    c_t = c_b.astype(F32).T.astype(BF16)
    scores = jnp.where(visible, mm(c_b, b_b, NT), 0.0)
    first = iota((Q, LANES), 1) < WIDTH

    def fold(values):
        return values.reshape(Q // 8, 8, values.shape[1]).sum(axis=0)

    def conv_back(lo, d_conv, raw):
        span = slice(lo, lo + LANES)
        pre = pre_ref[:, span].astype(F32)
        gate = sigmoid(pre)
        d_pre = d_conv * (gate * (1.0 + pre * (1.0 - gate)))
        place = lo // LANES
        dpre[place, 0:Q, :] = d_pre
        d_raw = taps_ref[K - 1 : K, span] * d_pre
        acc_ref[8 * (K - 1) : 8 * K, span] += fold(d_pre * raw)
        acc_ref[8 * K : 8 * K + 8, span] += fold(d_pre)
        for lag in range(1, K):
            moved = dpre[place, lag : lag + Q, :] * lag_mask[lag]
            d_raw = d_raw + taps_ref[K - 1 - lag : K - lag, span] * moved
            acc_ref[8 * (K - 1 - lag) : 8 * (K - lag), span] += fold(moved * raw)
        dpre[place, Q : Q + 8, :] = d_pre[0:8, :]
        dx_ref[:, span] = d_raw.astype(BF16)

    d_scores = jnp.zeros((Q, Q), F32)
    wide = 2 * LANES
    for quad in range(0, inner, wide):
        block = slice(quad, quad + wide)
        held_b = st_ref[0, :, block]
        d_held = dstate[:, block]
        d_held_b = d_held.astype(BF16)
        dst_b[:, block] = d_held_b
        carried = mm(c_b, held_b)
        returned = mm(b_b, d_held_b)
        crossing = (d_held * held_b.astype(F32)).reshape(STATE // 8, 8, wide).sum(axis=0)
        grown_parts, kept_parts = [], []
        for part in range(0, wide, LANES):
            lo = quad + part
            pair = lo // LANES
            span = slice(lo, lo + LANES)
            xc = xc_ref[:, span].astype(F32)
            dy_b = dy_ref[:, span]
            dy = dy_b.astype(F32)
            left, right, both = pair_columns(csum, pair, first)
            _, _, step_pair = pair_columns(step, pair, first)
            fall_left = jnp.exp2(jnp.minimum(left - csum_t[2 * pair : 2 * pair + 1, :], 0.0))
            fall_right = jnp.exp2(jnp.minimum(right - csum_t[2 * pair + 1 : 2 * pair + 2, :], 0.0))
            mix = jnp.concatenate([(scores * fall_left).astype(BF16), (scores * fall_right).astype(BF16)], axis=1)
            fed_b = (xc * step_pair).astype(BF16)
            fed = fed_b.astype(F32)
            zero = jnp.zeros((Q, LANES), BF16)
            stacked = jnp.concatenate([jnp.where(first, fed_b, zero), jnp.where(first, zero, fed_b)], axis=0)
            grown = jnp.exp2(both) * carry
            y = mm(mix, stacked) + carried[:, part : part + LANES] * grown
            d_mix = mm(dy_b, stacked, NT)
            d_scores = d_scores + d_mix[:, :Q] * fall_left + d_mix[:, Q:] * fall_right
            d_fed2 = mm(mix, dy_b, TN)
            d_fed_in = jnp.where(first, d_fed2[:Q], d_fed2[Q:])
            closing = both[Q - 1 : Q, :]
            shrink = jnp.exp2(closing - both) * last
            d_fed_out = returned[:, part : part + LANES] * shrink
            d_fed = d_fed_in + d_fed_out
            straddle = dy * y - fed * d_fed_in
            hi = straddle.astype(BF16)
            ab_hi[:, span] = hi
            ab_lo[:, span] = (straddle - hi.astype(F32)).astype(BF16)
            v_b[:, span] = (fed * d_fed_out).astype(BF16)
            u_b[:, span] = (xc * d_fed).astype(BF16)
            fedw[:, span] = (fed * shrink).astype(BF16)
            grown_parts.append((dy * grown).astype(BF16))
            kept_parts.append(jnp.exp2(closing) * passing)
            acc_ref[8 * K + 8 : 8 * K + 16, span] += fold(dy * xc)
            d_conv = d_fed * step_pair + skip_ref[:, span] * dy
            conv_back(lo, d_conv, xr_ref[:, span].astype(F32))
        dy_grown = jnp.concatenate(grown_parts, axis=1)
        kept = jnp.concatenate(kept_parts, axis=1)
        dyd[:, block] = dy_grown
        through[:, block] = crossing * kept
        dstate[:, block] = d_held * kept + mm(c_t, dy_grown)

    d_scores_b = jnp.where(visible, d_scores, 0.0).astype(BF16)
    d_c = mm(dyd[...], st_ref[0], NT) + mm(d_scores_b, b_b)
    d_b = mm(fedw[...], dst_b[...], NT) + mm(d_scores_b, c_b, TN)
    conv_back(inner, d_b, small[:, :STATE])
    conv_back(inner + STATE, d_c, small[:, STATE : 2 * STATE])

    sel = sel_ref[...]
    few = sel.shape[0]
    red_ab = mm(sel, ab_hi[...], NT) + mm(sel, ab_lo[...], NT)
    red_v = mm(sel, v_b[...], NT)
    red_u = mm(sel, u_b[...], NT)
    thr = through[...]
    thr_hi = thr.astype(BF16)
    red_t = mm(sel, thr_hi, NT) + mm(sel, (thr - thr_hi.astype(F32)).astype(BF16), NT)
    d_rate = (
        mm_exact(red_ab, (same & (cols >= rows)).astype(F32), NT)
        + mm_exact(red_v, (same & (cols < rows)).astype(F32), NT)
        + jnp.sum(red_t, axis=1, keepdims=True)
    )
    rest = jnp.zeros((Q - few, Q), F32)
    d_rate = jnp.concatenate([d_rate, rest], axis=0).T
    red_u = jnp.concatenate([red_u, rest], axis=0).T
    d_step = red_u - d_rate * decay_rate
    d_dt = d_step * sigmoid(shifted)
    dx_ref[:, inner + 2 * STATE :] = d_dt.astype(BF16)
    hacc_ref[0:8, :] += fold(d_dt)
    hacc_ref[8:16, :] += fold(d_rate * (-decay_rate * step))
    if later_call:

        @pl.when(pl.program_id(0) == pl.num_programs(0) - 1)
        def _():
            rows_ref[...] = jnp.zeros(rows_ref.shape, F32)
            for k in range(K + 2):
                rows_ref[k : k + 1, :] = jnp.sum(acc_ref[8 * k : 8 * k + 8, :], axis=0, keepdims=True)
            rows_ref[K + 2 : K + 3, :inner] = jnp.sum(gain_acc_ref[...], axis=0, keepdims=True)
            for k in range(2):
                total = jnp.sum(hacc_ref[8 * k : 8 * k + 8, :], axis=0, keepdims=True)
                rows_ref[K + 3 : K + 4, k * LANES : (k + 1) * LANES] = total

    else:
        halo_out[...] = dpre[:, Q : Q + 8, :]
        state_out[...] = dstate[...]


def load_blocks(offsets_ref, parts, whole, sems):
    @pl.when(pl.program_id(0) == 0)
    def _():
        copies = []
        count = sems.shape[0]
        size = whole.shape[0] // count
        for part in parts:
            for j in range(part.shape[0] // size):
                k = len(copies)
                start = pl.multiple_of(offsets_ref[k], 32) if count > 1 else 0
                source = part.at[pl.ds(j * size, size), :]
                copies.append(pltpu.make_async_copy(source, whole.at[pl.ds(start, size), :], sems.at[k]))
        for copy in copies:
            copy.start()
        for copy in copies:
            copy.wait()


def turn_rows(offsets_ref, me_ref, own_ref, other_ref, out_ref, turned):
    depth = own_ref.shape[1]
    rows = own_ref.shape[0]
    for index, source in enumerate((own_ref, other_ref)):
        at = pl.multiple_of(jnp.where(index == 0, me_ref[0], 1 - me_ref[0]) * rows, LANES)
        for lo in range(0, rows, Q):
            tile = source[lo : lo + Q, :].astype(F32)
            scale = lax.rsqrt(jnp.mean(tile * tile, axis=1, keepdims=True) + EPSILON)
            tile = tile * scale
            for left in range(0, depth, LANES):
                turned[left : left + LANES, pl.ds(at + lo, Q)] = tile[:, left : left + LANES].T.astype(BF16)
    count = offsets_ref.shape[0]
    size = depth // count
    for k in range(count):
        start = pl.multiple_of(offsets_ref[k], 32)
        out_ref[k * size : (k + 1) * size, :] = turned[pl.ds(start, size), :]


def project(count, heads, offsets_ref, me_ref, own_ref, other_ref, place_ref, *refs):
    blocks, (x_ref, small_ref, normed_ref, taps_ref, gain_ref, w_out_ref, w_ref, sems, out_sem) = refs[:count], refs[count:]
    load_blocks(offsets_ref, blocks, w_ref, sems)
    keep = pltpu.make_async_copy(w_ref, w_out_ref, out_sem)
    depth, inner = w_ref.shape[0], x_ref.shape[1]
    tile = 256

    @pl.when(pl.program_id(0) == 0)
    def _():
        keep.start()
        spare = w_ref[:, inner + 2 * STATE :]
        pick = jnp.where(iota((8, LANES), 1) == heads + K + 2, 1.0, 0.0).astype(BF16)
        gain_ref[...] = mm(pick, spare, NT)
        lanes = iota((depth, LANES), 1)
        for lo in range(0, inner + 2 * STATE, LANES):
            if lo < inner:
                wanted, row = place_ref[:, :LANES] == lanes + lo, heads
            else:
                wanted, row = place_ref[:, LANES:] == lanes + (lo - inner), heads + 8
            moved = mm(spare, jnp.where(wanted, 1.0, 0.0).astype(BF16), TN)
            taps_ref[:, lo : lo + LANES] = moved[row : row + 8, :]

    rows = jnp.where(pl.program_id(0) == me_ref[0], own_ref[...], other_ref[...]).astype(F32)
    scale = lax.rsqrt(jnp.mean(rows * rows, axis=1, keepdims=True) + EPSILON)
    rows = (rows * scale * gain_ref[0:1, :]).astype(BF16)
    normed_ref[...] = rows
    for lo in range(0, inner, tile):
        x_ref[:, lo : lo + tile] = mm(rows, w_ref[:, lo : lo + tile]).astype(BF16)
    small_ref[...] = mm(rows, w_ref[:, inner:])

    @pl.when(pl.program_id(0) == pl.num_programs(0) - 1)
    def _():
        keep.wait()


def row_sums(lanes):
    return mm_exact(jnp.ones((8, LANES), F32), lanes, NT)


def spread_rows(values):
    pick = jnp.where(iota((8, LANES), 0) == 0, 1.0, 0.0).astype(F32)
    return mm_exact(values, pick, TN)


def gate_forward(normed_ref, w_ref, y_ref, gain_ref, z_ref, gg_ref, sq_ref, square):
    rows, width = z_ref.shape
    size = 512

    @pl.when(pl.program_id(0) == 0)
    def _():
        square[...] = jnp.zeros(square.shape, F32)

    for lo in range(0, rows, size):
        at = slice(lo, lo + size)
        z = mm(normed_ref[at, :], w_ref[...]).astype(BF16)
        z_ref[at, :] = z
        z = z.astype(F32)
        gated = y_ref[at, :].astype(F32) * (z * sigmoid(z))
        gg_ref[at, :] = (gated * gain_ref[K + 1 : K + 2, :]).astype(BF16)
        twice = gated * gated
        for part in range(0, width, LANES):
            square[at, :] += twice[:, part : part + LANES]

    @pl.when(pl.program_id(0) == pl.num_programs(0) - 1)
    def _():
        sq_ref[...] = row_sums(square[...])


def branch(me_ref, ends_ref, gg_ref, own_ref, other_ref, w_ref, mine_ref, away_ref, prod_ref, product):
    rows, width = mine_ref.shape
    size = 512

    @pl.when(pl.program_id(0) == 0)
    def _():
        product[...] = jnp.zeros(product.shape, F32)

    for index, (out_ref, cot_ref) in enumerate(((mine_ref, own_ref), (away_ref, other_ref))):
        first = jnp.where(index == 0, me_ref[0], 1 - me_ref[0]) * rows
        for lo in range(0, rows, size):
            at = pl.ds(pl.multiple_of(first + lo, size), size)
            u = mm(gg_ref[at, :], w_ref[...], NT)
            out_ref[lo : lo + size, :] = u.astype(BF16)
            term = u * cot_ref[lo : lo + size, :].astype(F32)
            for part in range(0, width, LANES):
                product[at, :] += term[:, part : part + LANES]

    @pl.when(pl.program_id(0) == pl.num_programs(0) - 1)
    def _():
        live = iota(product.shape, 0) < ends_ref[ends_ref.shape[0] - 1]
        prod_ref[...] = row_sums(jnp.where(live, product[...], 0.0))


def gate_backward(
    me_ref, ends_ref, own_ref, other_ref, w_ref, y_ref, z_ref, rg_ref, coef_ref, gain_ref,
    dy_ref, dz_ref, acc_ref, rg, coef,
):
    total, width = dy_ref.shape
    rows = own_ref.shape[0]
    size = 512

    @pl.when(pl.program_id(0) == 0)
    def _():
        live = iota(rg.shape, 0) < ends_ref[ends_ref.shape[0] - 1]
        rg[...] = spread_rows(rg_ref[...])
        coef[...] = spread_rows(coef_ref[...])
        rg[...] = jnp.where(live, rg[...], 0.0)

    gain = gain_ref[K + 1 : K + 2, :]
    sums = jnp.zeros((8, width), F32)
    for index, cot_ref in enumerate((own_ref, other_ref)):
        first = jnp.where(index == 0, me_ref[0], 1 - me_ref[0]) * rows
        for lo in range(0, rows, size):
            at = pl.ds(pl.multiple_of(first + lo, size), size)
            ds = mm(cot_ref[lo : lo + size, :], w_ref[...])
            z = z_ref[at, :].astype(F32)
            y = y_ref[at, :].astype(F32)
            scale = jnp.concatenate([rg[at, :]] * (width // LANES), axis=1)
            back = jnp.concatenate([coef[at, :]] * (width // LANES), axis=1)
            gate = sigmoid(z)
            silu = z * gate
            gated = y * silu
            d_normal = ds * scale
            sums = sums + (d_normal * gated).reshape(size // 8, 8, width).sum(axis=0)
            d_gated = d_normal * gain - gated * back
            dy_ref[at, :] = (d_gated * silu).astype(BF16)
            dz_ref[at, :] = (d_gated * y * (gate + silu * (1.0 - gate))).astype(BF16)
    acc_ref[...] = sums


def weight_grad(turned_ref, d_ref, away_ref, keep_ref):
    half = away_ref.shape[0]
    size = half
    d = d_ref[...]
    for lo in range(0, half, size):
        away_ref[lo : lo + size, :] = mm(turned_ref[lo : lo + size, :], d).astype(BF16)
    for lo in range(0, half, size):
        keep_ref[lo : lo + size, :] = mm(turned_ref[half + lo : half + lo + size, :], d).astype(BF16)


def normed_back(rows_ref, dz_ref, dx_ref, wz_ref, wx_ref, out_ref):
    size = 512
    for lo in range(0, out_ref.shape[0], size):
        at = slice(lo, lo + size)
        total = mm(dz_ref[at, :], wz_ref[...], NT) + mm(dx_ref[at, :], wx_ref[...], NT)
        out_ref[at, :] = total.astype(BF16)


def params():
    return pltpu.CompilerParams(dimension_semantics=("arbitrary",), vmem_limit_bytes=VMEM_LIMIT)


SMALL_COST = pl.CostEstimate(flops=1000, bytes_accessed=1000, transcendentals=0)


def rows_spec(block, width, column=0):
    return pl.BlockSpec((block, width), lambda i: (i, column))


def whole_spec(shape, column=0):
    return pl.BlockSpec(shape, lambda i: (0, column))


def local(
    tokens,
    cotangent,
    lengths,
    norm_gain,
    w_zx,
    w_bc,
    w_dt,
    conv_x,
    conv_x_bias,
    conv_bc,
    conv_bc_bias,
    dt_bias,
    a_log,
    d_skip,
    gate_gain,
    w_out,
):
    n_t = lax.axis_size("tensor")
    n_dp = lax.axis_size("dp")
    me_t = lax.axis_index("tensor")
    me_dp = lax.axis_index("dp")
    own_rows, depth = tokens.shape
    group = own_rows * n_t
    chunks = group // Q
    heads = dt_bias.shape[0]
    inner = heads * WIDTH
    inner_total = inner * n_t
    shard = w_zx.shape[1]
    pairs = [(i, n_t - 1 - i) for i in range(n_t)]

    def swap(v):
        return lax.ppermute(v, "tensor", pairs)

    def in_order(mine, other, axis=0):
        low = jnp.where(me_t == 0, mine, other)
        high = jnp.where(me_t == 0, other, mine)
        return jnp.concatenate([low, high], axis=axis)

    def sum_dp(v):
        step = 1
        while step < n_dp:
            v = v + lax.ppermute(v, "dp", [(i, i ^ step) for i in range(n_dp)])
            step *= 2
        return v

    def after(value, *others):
        return lax.optimization_barrier((value, *others))[0]

    ring = 4
    plane = n_dp // (2 * ring)

    around = [(i, (i + 2 * plane) % n_dp) for i in range(n_dp)]
    across = [(i, i ^ 2) for i in range(n_dp)]
    beside = [(i, i ^ 1) for i in range(n_dp)]

    def send(v, way):
        return lax.ppermute(v, "dp", way)

    by_hand = plane == 2 and shard % 32 == 0

    def whole(v):
        return [lax.all_gather(v, "dp", axis=0, tiled=True)]

    def block_offsets(count, size):
        if count == 1:
            return jnp.zeros((1,), jnp.int32)
        places = []
        for core in range(2):
            for side in range(2):
                for turn in range(ring):
                    level = (me_dp // (2 * plane) - turn + ring) % ring
                    places.append(level * (2 * plane) + ((me_dp % (2 * plane)) ^ (2 * side + core)))
        return jnp.stack(places).astype(jnp.int32) * size

    def relative_order():
        level, side, core = me_dp // 4, (me_dp // 2) % 2, me_dp % 2
        order = []
        for dc in (1, 0):
            for dy in (1, 0):
                for dz in range(1, ring + 1):
                    order.append(((level - dz + ring) % ring) * 4 + (side ^ dy) * 2 + (core ^ dc))
        return order

    def fold_beside(keep, got):
        half = keep.shape[0] // 2
        away = (keep[:half].astype(F32) + got[:half].astype(F32)).astype(BF16)
        return away, keep[half:].astype(F32) + got[half:].astype(F32)

    def fold_turn(total, got, turn):
        part = total[(turn - 1) * shard : turn * shard] + got.astype(F32)
        return part if turn == ring else part.astype(BF16)

    ends = jnp.cumsum(lengths[0]).astype(jnp.int32)
    live = (lax.iota(jnp.int32, group) < ends[-1]).astype(F32)
    live_own = lax.dynamic_slice_in_dim(live, me_t * own_rows, own_rows, 0)
    me = me_t.astype(jnp.int32).reshape(1)

    span_p = conv_x_bias.shape[1]
    span_n = conv_bc_bias.shape[1]
    half_bc = w_bc.shape[1]
    bits = jnp.concatenate([norm_gain, conv_bc.reshape(-1), conv_bc_bias.reshape(-1)])
    bits = jnp.pad(bits, (0, LANES - bits.shape[0]))
    tiny = jnp.concatenate([w_bc.reshape(2 * half_bc, STATE), bits[None]], axis=0)
    other_tiny = swap(tiny)
    other_bc = other_tiny[: 2 * half_bc].reshape(w_bc.shape)
    both_bits = [bits, other_tiny[2 * half_bc]]
    at = norm_gain.shape[0]
    gain_pair = in_order(*[v[:at] for v in both_bits])[:, None]
    taps_bc = in_order(*[v[at : at + conv_bc.size].reshape(2, span_n, K) for v in both_bits], axis=1)
    at += conv_bc.size
    bias_bc = in_order(*[v[at : at + 2 * span_n].reshape(2, span_n, 1) for v in both_bits], axis=1)
    spare_bc = jnp.concatenate([taps_bc, bias_bc], axis=2).reshape(4 * span_n, K + 1)
    spare_x = [conv_x.reshape(shard, K), conv_x_bias.reshape(shard, 1), gate_gain.reshape(shard, 1), gain_pair]
    bc_pair = in_order(w_bc, other_bc, axis=1)
    packed = jnp.concatenate(
        [w_zx[1], bc_pair[0], bc_pair[1], w_dt, *spare_x, jnp.zeros((shard, 8 - K - 3), BF16)]
        + [jnp.pad(spare_bc, ((0, shard - 4 * span_n), (0, LANES - heads - 8 - K - 1)))],
        axis=1,
    )
    gain_pair = gain_pair.astype(F32)
    where = lax.iota(jnp.int32, depth)
    home, inside = where // shard, where % shard
    place_x = (inside // span_p) * WIDTH + home * span_p + inside % span_p
    half_n = 2 * span_n
    place_bc = (inside // half_n) * STATE + home * half_n + inside % half_n
    place = jnp.concatenate([jnp.broadcast_to(v[:, None], (depth, LANES)) for v in (place_x, place_bc)], axis=1)
    par = jnp.concatenate([dt_bias[None], a_log[None], jnp.zeros((6, heads), F32)], axis=0)
    par = jnp.concatenate([par, jnp.zeros((8, LANES - heads), F32)], axis=1)
    skip = jnp.repeat(d_skip, WIDTH)[None]
    members = lax.iota(jnp.int32, inner)[:, None] // WIDTH
    sel = (members.T == lax.iota(jnp.int32, 32)[:, None]).astype(BF16)
    smem = pl.BlockSpec(memory_space=pltpu.SMEM)
    vmem = pl.BlockSpec(memory_space=pltpu.VMEM)
    hbm = pl.BlockSpec(memory_space=pl.ANY)
    n_small = 2 * STATE + LANES
    n_conv = inner + 2 * STATE
    w_rest = jnp.concatenate([w_zx[0], w_out.T], axis=1)

    def turn(other_tokens):
        return pl.pallas_call(
            turn_rows,
            in_specs=[smem, smem, vmem, vmem],
            out_specs=vmem,
            out_shape=jax.ShapeDtypeStruct((depth, group), BF16),
            scratch_shapes=[pltpu.VMEM((depth, group), BF16)],
            compiler_params=pltpu.CompilerParams(vmem_limit_bytes=VMEM_LIMIT),
            cost_estimate=SMALL_COST,
            name="turn_rows",
        )((jnp.stack(relative_order()) * shard).astype(jnp.int32), me, tokens, other_tokens)

    if by_hand:
        line, other, line_c, other_c = [packed], [], [], []
        pieces = [tokens[:176], tokens[176:352], tokens[352:]]
        arrived, constants = [], []
        for step in range(ring + 1):
            made = []
            if step < ring - 1:
                made.append((line, send(line[step], around)))
            if step < ring:
                made.append((other, send(line[step], across)))
                made.append((line_c, send(line[step], beside)))
            if step:
                made.append((other_c, send(other[step - 1], beside)))
            if 0 < step < ring:
                made.append((arrived, swap(pieces[step - 1])))
            if step == 0:
                made += [(constants, v) for v in (place, par, skip, sel)]
                made += [([], v) for v in pieces]
            if step == 2:
                zo_all = lax.all_gather(after(w_rest, line[2]), "dp", axis=0, tiled=True)
            fresh = lax.optimization_barrier(tuple(value for _, value in made))
            for (place_in, _), value in zip(made, fresh):
                place_in.append(value)
            if step == 0:
                pieces = fresh[-3:]
        other_tokens = jnp.concatenate(arrived, axis=0)
        other_cot = swap(after(cotangent, other_tokens))
        wx_blocks = line + other + line_c + other_c
        place, par, skip, sel = constants
    else:
        wx_blocks = whole(packed)
        zo_all = whole(w_rest)[0]
        other_tokens, other_cot = swap(tokens), swap(cotangent)
    count = len(wx_blocks)
    offsets = block_offsets(count, shard)
    sems = pltpu.SemaphoreType.DMA((count,))
    tok_own = tokens.astype(F32)
    inv_tok = lax.rsqrt(jnp.mean(tok_own * tok_own, axis=1, keepdims=True) + EPSILON)

    block = own_rows
    steps = group // block
    x_raw, small, normed, taps, gain_in, wx_all = pl.pallas_call(
        partial(project, count, heads),
        grid=(steps,),
        in_specs=[
            smem,
            smem,
            whole_spec((block, depth)),
            whole_spec((block, depth)),
            whole_spec((depth, 2 * LANES)),
        ]
        + [hbm] * count,
        out_specs=[
            rows_spec(block, inner),
            rows_spec(block, n_small),
            rows_spec(block, depth),
            whole_spec((8, n_conv)),
            whole_spec((8, depth)),
            hbm,
        ],
        out_shape=[
            jax.ShapeDtypeStruct((group, inner), BF16),
            jax.ShapeDtypeStruct((group, n_small), F32),
            jax.ShapeDtypeStruct((group, depth), BF16),
            jax.ShapeDtypeStruct((8, n_conv), F32),
            jax.ShapeDtypeStruct((8, depth), F32),
            jax.ShapeDtypeStruct((depth, inner + n_small), BF16),
        ],
        scratch_shapes=[pltpu.VMEM((depth, inner + n_small), BF16), sems, pltpu.SemaphoreType.DMA],
        compiler_params=params(),
        cost_estimate=SMALL_COST,
        name="project",
    )(offsets, me, tokens, other_tokens, place, *wx_blocks)
    xc, pre, bc, y_all, states = pl.pallas_call(
        partial(scan_forward, heads),
        grid=(chunks,),
        in_specs=[
            smem,
            rows_spec(Q, inner),
            rows_spec(Q, n_small),
            whole_spec((8, n_conv)),
            whole_spec((8, LANES)),
            whole_spec((1, inner)),
        ],
        out_specs=[
            rows_spec(Q, inner),
            rows_spec(Q, n_conv),
            rows_spec(Q, 2 * STATE),
            rows_spec(Q, inner),
            pl.BlockSpec((1, STATE, inner), lambda i: (i, 0, 0)),
        ],
        out_shape=[
            jax.ShapeDtypeStruct((group, inner), BF16),
            jax.ShapeDtypeStruct((group, n_conv), BF16),
            jax.ShapeDtypeStruct((group, 2 * STATE), BF16),
            jax.ShapeDtypeStruct((group, inner), BF16),
            jax.ShapeDtypeStruct((chunks, STATE, inner), BF16),
        ],
        scratch_shapes=[pltpu.VMEM((n_conv // LANES, Q + 8, LANES), F32), pltpu.VMEM((STATE, inner), F32)],
        compiler_params=params(),
        cost_estimate=SMALL_COST,
        name="scan_forward",
    )(ends, x_raw, small, taps, par, skip)

    cot_all = in_order(cotangent, other_cot)
    if by_hand:
        turned = turn(after(other_tokens, y_all))
        normed, turned, cot_all = lax.optimization_barrier((normed, turned, after(cot_all, y_all)))
    tile = 512
    columns = lambda rows, shift=0: pl.BlockSpec((rows, tile), lambda j: (0, j + shift))
    fixed = lambda shape: pl.BlockSpec(shape, lambda j: (0, 0))
    tiles = inner // tile
    z_all, gg, sq = pl.pallas_call(
        gate_forward,
        grid=(tiles,),
        in_specs=[fixed((group, depth)), columns(depth), columns(group), columns(8)],
        out_specs=[columns(group), columns(group), fixed((8, group))],
        out_shape=[
            jax.ShapeDtypeStruct((group, inner), BF16),
            jax.ShapeDtypeStruct((group, inner), BF16),
            jax.ShapeDtypeStruct((8, group), F32),
        ],
        scratch_shapes=[pltpu.VMEM((group, LANES), F32)],
        compiler_params=params(),
        cost_estimate=SMALL_COST,
        name="gate_forward",
    )(normed, zo_all, y_all, taps)
    sq_got = swap(sq)

    u_own, u_send, prod = pl.pallas_call(
        branch,
        grid=(depth // tile,),
        in_specs=[
            smem,
            smem,
            fixed((group, inner)),
            columns(own_rows),
            columns(own_rows),
            pl.BlockSpec((tile, inner), lambda j: (j, 1)),
        ],
        out_specs=[columns(own_rows), columns(own_rows), fixed((8, group))],
        out_shape=[
            jax.ShapeDtypeStruct((own_rows, depth), BF16),
            jax.ShapeDtypeStruct((own_rows, depth), BF16),
            jax.ShapeDtypeStruct((8, group), F32),
        ],
        scratch_shapes=[pltpu.VMEM((group, LANES), F32)],
        compiler_params=params(),
        cost_estimate=SMALL_COST,
        name="branch",
    )(me, ends, gg, cotangent, other_cot, zo_all)
    prod_got = swap(prod)
    sq_all = sq + after(sq_got, prod)
    inv_gate8 = lax.rsqrt(sq_all / inner_total + EPSILON)
    inv_gate = inv_gate8[0]
    d_branch = (cot_all.astype(F32) * (live * inv_gate)[:, None]).astype(BF16)
    g_out = lax.dot_general(d_branch, gg, TN, preferred_element_type=F32).astype(BF16)
    grad_out = lax.psum_scatter(g_out, "dp", scatter_dimension=0, tiled=True)
    prod_got = after(prod_got, g_out)
    u_recv = swap(after(u_send, g_out))
    inv_own = lax.dynamic_slice_in_dim(inv_gate, me_t * own_rows, own_rows, 0)
    out_branch = (u_own.astype(F32) + u_recv.astype(F32)) * (inv_own * live_own)[:, None]
    layer_out = (tokens.astype(F32) + out_branch).astype(BF16)

    prod_all = prod + prod_got
    coef8 = inv_gate8 * inv_gate8 * inv_gate8 * (prod_all / inner_total)
    dy, dz, gain_acc = pl.pallas_call(
        gate_backward,
        grid=(tiles,),
        in_specs=[
            smem,
            smem,
            fixed((own_rows, depth)),
            fixed((own_rows, depth)),
            columns(depth, tiles),
            columns(group),
            columns(group),
            fixed((8, group)),
            fixed((8, group)),
            columns(8),
        ],
        out_specs=[columns(group), columns(group), columns(8)],
        out_shape=[
            jax.ShapeDtypeStruct((group, inner), BF16),
            jax.ShapeDtypeStruct((group, inner), BF16),
            jax.ShapeDtypeStruct((8, inner), F32),
        ],
        scratch_shapes=[pltpu.VMEM((group, LANES), F32), pltpu.VMEM((group, LANES), F32)],
        compiler_params=params(),
        cost_estimate=SMALL_COST,
        name="gate_backward",
    )(me, ends, cotangent, other_cot, zo_all, y_all, z_all, inv_gate8, coef8, taps)
    dot = partial(lax.dot_general, preferred_element_type=F32)
    front = depth // 2

    def gradient(d, width, first, number):
        outs = pl.BlockSpec((front, width), lambda j: (0, j))
        return pl.pallas_call(
            weight_grad,
            grid=(number,),
            in_specs=[fixed((depth, group)), pl.BlockSpec((group, width), lambda j: (0, j + first))],
            out_specs=[outs, outs],
            out_shape=[jax.ShapeDtypeStruct((front, width * number), BF16)] * 2,
            compiler_params=params(),
            cost_estimate=SMALL_COST,
            name="weight_grad",
        )(turned, d)

    if by_hand:
        g_send, z_keep = gradient(dz, tile, 0, tiles)
        z_got = send(g_send, beside)
        dy = after(dy, z_keep, g_send)
    else:
        grad_z = lax.psum_scatter(dot(normed, dz, TN).astype(BF16), "dp", scatter_dimension=0, tiled=True)

    halo_spec = pl.BlockSpec((n_conv // LANES, 8, LANES), lambda i: (0, 0, 0))

    def backward(top, number, carry):
        back = lambda width: pl.BlockSpec((Q, width), lambda i: (top - i, 0))
        operands = [ends, dy, xc, pre, x_raw, small, bc, states, taps, par, skip, sel, *carry]
        acc_spec = whole_spec((8 * (K + 2), n_conv))
        carry_shapes = [
            jax.ShapeDtypeStruct((STATE, inner), F32),
            jax.ShapeDtypeStruct((n_conv // LANES, 8, LANES), F32),
        ]
        carry_specs = []
        if carry:
            carry_specs = [whole_spec((STATE, inner)), halo_spec, acc_spec, whole_spec((16, LANES))]
            carry_specs += [whole_spec((8, inner)), hbm]
        return pl.pallas_call(
            partial(scan_backward, heads, chunks, top),
            grid=(number,),
            in_specs=[
                smem,
                back(inner),
                back(inner),
                back(n_conv),
                back(inner),
                back(n_small),
                back(2 * STATE),
                pl.BlockSpec((1, STATE, inner), lambda i: (top - i, 0, 0)),
                whole_spec((8, n_conv)),
                whole_spec((8, LANES)),
                whole_spec((1, inner)),
                whole_spec((32, inner)),
            ]
            + carry_specs,
            out_specs=[
                back(inner + n_small),
                *([whole_spec((8, n_conv))] if carry else []),
                acc_spec,
                whole_spec((16, LANES)),
                *([] if carry else [whole_spec((STATE, inner)), halo_spec]),
            ],
            out_shape=[
                jax.ShapeDtypeStruct((group, inner + n_small), BF16),
                *([jax.ShapeDtypeStruct((8, n_conv), F32)] if carry else []),
                jax.ShapeDtypeStruct((8 * (K + 2), n_conv), F32),
                jax.ShapeDtypeStruct((16, LANES), F32),
                *([] if carry else carry_shapes),
            ],
            scratch_shapes=[
                pltpu.VMEM((STATE, inner), F32),
                pltpu.VMEM((n_conv // LANES, Q + 8, LANES), F32),
                pltpu.VMEM((Q, inner), BF16),
                pltpu.VMEM((Q, inner), BF16),
                pltpu.VMEM((Q, inner), BF16),
                pltpu.VMEM((Q, inner), BF16),
                pltpu.VMEM((Q, inner), BF16),
                pltpu.VMEM((Q, inner), BF16),
                pltpu.VMEM((STATE, inner), BF16),
                pltpu.VMEM((8, inner), F32),
            ],
            input_output_aliases={len(operands) - 1: 0} if carry else {},
            compiler_params=params(),
        cost_estimate=SMALL_COST,
            name="scan_backward",
        )(*operands)

    half_chunks = chunks // 2
    dx, acc, hacc, d_state, halo = backward(chunks - 1, chunks - half_chunks, ())
    if by_hand:
        z_got, dx = lax.optimization_barrier((z_got, dx))
        z_away, z_keep = fold_beside(z_keep, z_got)
        z_got = send(z_away, across)
        d_state = after(d_state, z_away, z_keep)
    dx, vector = backward(half_chunks - 1, half_chunks, (d_state, halo, acc, hacc, gain_acc, dx))[:2]
    dx = after(dx, u_recv)
    lanes_shared = lax.iota(jnp.int32, n_conv)[None, :] >= inner
    bits_of = lambda turn: [(i, i ^ (1 << turn)) for i in range(n_dp)]
    if by_hand:
        xa_send, xa_keep = gradient(dx, 384, 0, 3)
        moved = [swap(vector), xa_send]
        moved = lax.optimization_barrier(tuple(moved))
        xa_got = send(moved[1], beside)
        vector = vector + jnp.where(lanes_shared, moved[0], 0.0)
        xb_send, xb_keep = gradient(after(dx, xa_send, vector), 384, 3, 2)
        z_got, xb_send, vector_got = lax.optimization_barrier((z_got, xb_send, send(vector, bits_of(0))))
        xb_got = send(xb_send, beside)
        z_total = z_keep + z_got.astype(F32)
        z_got = send(z_total[:shard].astype(BF16), around)
        vector = vector + vector_got
        xa_got = after(xa_got, z_total, vector)
        xa_away, xa_keep = fold_beside(xa_keep, xa_got)
        xa_away, vector_got = lax.optimization_barrier((xa_away, send(vector, bits_of(1))))
        xa_got = send(xa_away, across)
        vector = vector + vector_got
        xb_got = after(xb_got, xa_away, xa_keep)
        xb_away, xb_keep = fold_beside(xb_keep, xb_got)
        xb_got = send(xb_away, across)
        vector_got = send(vector, bits_of(2))
        dz = after(dz, xb_away, xb_keep, z_total, vector)
    else:
        grad_x = lax.psum_scatter(dot(normed, dx, TN).astype(BF16), "dp", scatter_dimension=0, tiled=True)

    def back_rows(which, dz):
        pick = lambda width: pl.BlockSpec((own_rows, width), lambda j, rows: (rows[0], 0))
        return pl.pallas_call(
            normed_back,
            grid_spec=pltpu.PrefetchScalarGridSpec(
                num_scalar_prefetch=1,
                grid=(depth // tile,),
                in_specs=[
                    pick(inner),
                    pick(inner + n_small),
                    pl.BlockSpec((tile, inner), lambda j, rows: (j, 0)),
                    pl.BlockSpec((tile, inner + n_small), lambda j, rows: (j, 0)),
                ],
                out_specs=pl.BlockSpec((own_rows, tile), lambda j, rows: (0, j)),
            ),
            out_shape=jax.ShapeDtypeStruct((own_rows, depth), BF16),
            compiler_params=params(),
            cost_estimate=SMALL_COST,
            name="normed_back",
        )(which, dz, dx, zo_all, wx_all)

    dn_send = back_rows(n_t - 1 - me, dz)
    if by_hand:
        xa_got, z_got, vector_got, dn_send = lax.optimization_barrier((xa_got, z_got, vector_got, dn_send))
        dn_got = swap(dn_send)
        xa_total = xa_keep + xa_got.astype(F32)
        xa_got = xa_total[:shard].astype(BF16)
        z_got = fold_turn(z_total, z_got, 2)
        vector = vector + vector_got
        moved = [send(xa_got, around), send(z_got, around), send(vector, bits_of(3))]
        dn_own = back_rows(me, after(dz, xa_got, z_got, vector))
        moved = lax.optimization_barrier((*moved, dn_own, xb_got))
        dn_own = moved[3]
        xb_total = xb_keep + moved[4].astype(F32)
        xb_got = xb_total[:shard].astype(BF16)
        xa_got = fold_turn(xa_total, moved[0], 2)
        z_got = fold_turn(z_total, moved[1], 3)
        vector = vector + moved[2]
        moved = [send(xb_got, around), send(xa_got, around), send(z_got, around)]
        moved = lax.optimization_barrier((*moved, grad_out))
        xb_got = fold_turn(xb_total, moved[0], 2)
        xa_got = fold_turn(xa_total, moved[1], 3)
        grad_z = fold_turn(z_total, moved[2], ring) * gain_pair
        grad_out = moved[3].astype(F32).T
        moved = [send(xb_got, around), send(xa_got, around)]
        moved = lax.optimization_barrier((*moved, grad_z, grad_out, dn_got))
        xb_got = fold_turn(xb_total, moved[0], 3)
        xa_got = fold_turn(xa_total, moved[1], ring)
        grad_z, grad_out, dn_got = moved[2:]
        xb_got = send(xb_got, around)
    else:
        vector = sum_dp(vector + jnp.where(lanes_shared, swap(vector), 0.0))
        dn_own = back_rows(me, dz)
        dn_got = swap(dn_send)
        grad_out = grad_out.astype(F32).T
    dn = (dn_own.astype(F32) + dn_got.astype(F32)) * gain_in[0:1, :]
    grad_tokens = (
        cotangent.astype(F32)
        + inv_tok * dn
        - tok_own * inv_tok * inv_tok * inv_tok * jnp.mean(dn * tok_own, axis=1, keepdims=True)
    )

    me_all = me_dp * n_t + me_t
    bc_sum = vector[: K + 1, inner:].reshape(K + 1, 2, STATE)
    bc_sum = lax.dynamic_slice_in_dim(bc_sum, me_all * span_n, span_n, 2)
    grad_bc_taps = bc_sum[:K].transpose(1, 2, 0).reshape(conv_bc.shape)
    grad_bc_bias = bc_sum[K]
    x_sum = vector[: K + 3, :inner].reshape(K + 3, heads, WIDTH)
    grad_skip = x_sum[K + 1].sum(axis=1)
    x_sum = lax.dynamic_slice_in_dim(x_sum, me_dp * span_p, span_p, 2)
    grad_x_taps = x_sum[:K].transpose(1, 2, 0).reshape(conv_x.shape)
    grad_x_bias = x_sum[K]
    grad_gate = x_sum[K + 2]
    grad_dt_bias = vector[K + 3, :heads]
    grad_a_log = vector[K + 3, LANES : LANES + heads]
    tail = (grad_tokens, layer_out, grad_bc_taps, grad_bc_bias, grad_skip, grad_x_taps, grad_x_bias)
    tail = (*tail, grad_gate, grad_dt_bias, grad_a_log)
    if by_hand:
        *tail, xb_got = lax.optimization_barrier((*tail, xb_got))
        grad_x = jnp.concatenate([xa_got, fold_turn(xb_total, xb_got, ring)], axis=1) * gain_pair
    grad_tokens, layer_out, grad_bc_taps, grad_bc_bias, grad_skip, grad_x_taps, grad_x_bias = tail[:7]
    grad_gate, grad_dt_bias, grad_a_log = tail[7:]

    grad_z = grad_z.astype(F32)
    grad_x = grad_x.astype(F32)
    in_part = jnp.sum(w_zx[0].astype(F32) * grad_z, axis=1) + jnp.sum(packed.astype(F32) * grad_x, axis=1)
    in_part = in_part[:, None]
    grad_zx = jnp.stack([grad_z, grad_x[:, :inner]])
    grad_dt = grad_x[:, inner + 2 * STATE : inner + 2 * STATE + heads]
    bc_part = jnp.concatenate([grad_x[:, inner : inner + 2 * STATE], jnp.broadcast_to(in_part, (shard, LANES))], axis=1)
    half = half_bc
    bc_own = lax.dynamic_slice_in_dim(bc_part, me_t * half, half, 0)
    bc_send = lax.dynamic_slice_in_dim(bc_part, (n_t - 1 - me_t) * half, half, 0)
    bc_total = bc_own + swap(bc_send)
    own_gain = norm_gain.astype(F32)
    grad_bc = bc_total[:, : 2 * STATE].reshape(half, 2, STATE).transpose(1, 0, 2)
    grad_in = bc_total[:, 2 * STATE] / own_gain
    return (
        layer_out,
        grad_tokens,
        grad_in,
        grad_zx,
        grad_bc,
        grad_dt,
        grad_x_taps,
        grad_x_bias,
        grad_bc_taps,
        grad_bc_bias,
        grad_dt_bias,
        grad_a_log,
        grad_skip,
        grad_gate,
        grad_out,
    )


def solution(mesh):
    both = ("dp", "tensor")
    in_specs = (
        P(both, None),
        P(both, None),
        P("dp", None),
        P(both),
        P(None, "dp", "tensor"),
        P(None, both, None),
        P("dp", "tensor"),
        P("tensor", "dp"),
        P("tensor", "dp"),
        P(None, both),
        P(None, both),
        P("tensor"),
        P("tensor"),
        P("tensor"),
        P("tensor", "dp"),
        P("tensor", "dp"),
    )
    out_specs = (
        P(both, None),
        P(both, None),
        P(both),
        P(None, "dp", "tensor"),
        P(None, both, None),
        P("dp", "tensor"),
        P("tensor", "dp"),
        P("tensor", "dp"),
        P(None, both),
        P(None, both),
        P("tensor"),
        P("tensor"),
        P("tensor"),
        P("tensor", "dp"),
        P("tensor", "dp"),
    )
    return jax.shard_map(local, mesh=mesh, in_specs=in_specs, out_specs=out_specs, check_vma=False)
```

```python
from functools import partial

import jax
import jax.numpy as jnp
from jax import lax
from jax.experimental import pallas as pl
from jax.experimental.pallas import tpu as pltpu
from jax.sharding import PartitionSpec as P

EPSILON = 1e-05
HIGHEST = lax.Precision.HIGHEST
K = 4
WIDTH = 64
STATE = 128
Q = 128
LANES = 128
LOG2E = 1.4426950408889634
VMEM_LIMIT = 60 * 1024 * 1024
F32 = jnp.float32
BF16 = jnp.bfloat16

NN = (((1,), (0,)), ((), ()))
NT = (((1,), (1,)), ((), ()))
TN = (((0,), (0,)), ((), ()))


def mm(a, b, dims=NN):
    return lax.dot_general(a, b, dims, preferred_element_type=F32)


def mm_exact(a, b, dims=NN):
    return lax.dot_general(a, b, dims, preferred_element_type=F32, precision=HIGHEST)


def iota(shape, dim):
    return lax.broadcasted_iota(jnp.int32, shape, dim)


def segment_of(rows, ends_ref, count):
    total = (rows >= ends_ref[0]).astype(jnp.int32)
    for j in range(1, count):
        total = total + (rows >= ends_ref[j]).astype(jnp.int32)
    return total


def scalar_segment(row, ends_ref, count):
    total = jnp.where(row >= ends_ref[0], 1, 0)
    for j in range(1, count):
        total = total + jnp.where(row >= ends_ref[j], 1, 0)
    return total


def sigmoid(v):
    return 0.5 * jnp.tanh(0.5 * v) + 0.5


def softplus(v):
    return jnp.maximum(v, 0.0) + jnp.log1p(jnp.exp(-jnp.abs(v)))


def chunk_masks(chunk, ends_ref, count):
    base = chunk * Q
    rows = iota((Q, Q), 0) + base
    cols = iota((Q, Q), 1) + base
    row_ids = segment_of(rows, ends_ref, count)
    col_ids = segment_of(cols, ends_ref, count)
    same = row_ids == col_ids
    before_id = jnp.where(chunk == 0, -1, scalar_segment(base - 1, ends_ref, count))
    final_id = scalar_segment(base + Q - 1, ends_ref, count)
    carry = (row_ids == before_id).astype(F32)
    last = (row_ids == final_id).astype(F32)
    passing = jnp.where(before_id == final_id, 1.0, 0.0).astype(F32)
    return rows, cols, row_ids, same, carry, last, passing


def decays(dt_raw, par_ref):
    shifted = dt_raw + par_ref[0:1, :]
    step = softplus(shifted)
    decay_rate = jnp.exp(par_ref[1:2, :])
    return shifted, step, decay_rate


def pair_columns(values, pair, first):
    left = jnp.broadcast_to(values[:, 2 * pair : 2 * pair + 1], (Q, LANES))
    right = jnp.broadcast_to(values[:, 2 * pair + 1 : 2 * pair + 2], (Q, LANES))
    return left, right, jnp.where(first, left, right)


def scan_forward(
    heads, ends_ref, xr_ref, small_ref, taps_ref, par_ref, skip_ref,
    xc_ref, pre_ref, bc_ref, y_ref, st_ref, buf, state,
):
    count = ends_ref.shape[0]
    inner = heads * WIDTH
    chunk = pl.program_id(0)

    @pl.when(chunk == 0)
    def _():
        buf[:, 0:8, :] = jnp.zeros((buf.shape[0], 8, LANES), F32)
        state[...] = jnp.zeros(state.shape, F32)

    rows, cols, row_ids, same, carry, last, passing = chunk_masks(chunk, ends_ref, count)
    causal = rows >= cols
    visible = same & causal
    lag_mask = [None]
    for lag in range(1, K):
        earlier = rows - lag
        keep = (segment_of(earlier, ends_ref, count) == row_ids) & (earlier >= 0)
        lag_mask.append(keep.astype(F32))

    small = small_ref[...]

    def convolve(lo, raw):
        span = slice(lo, lo + LANES)
        place = lo // LANES
        buf[place, 8 : 8 + Q, :] = raw
        pre = taps_ref[K : K + 1, span] + taps_ref[K - 1 : K, span] * raw
        for lag in range(1, K):
            pre = pre + taps_ref[K - 1 - lag : K - lag, span] * (
                buf[place, 8 - lag : 8 - lag + Q, :] * lag_mask[lag]
            )
        buf[place, 0:8, :] = raw[Q - 8 : Q, :]
        pre_ref[:, span] = pre.astype(BF16)
        return pre * sigmoid(pre)

    b_f = convolve(inner, small[:, :STATE]).astype(BF16).astype(F32)
    c_b = convolve(inner + STATE, small[:, STATE : 2 * STATE]).astype(BF16)
    b_b = b_f.astype(BF16)
    bc_ref[:, :STATE] = b_b
    bc_ref[:, STATE:] = c_b
    b_t = b_f.T.astype(BF16)

    _, step, decay_rate = decays(small[:, 2 * STATE :], par_ref)
    csum = mm_exact(causal.astype(F32), step * (-LOG2E * decay_rate))
    csum_t = csum.T
    scores = jnp.where(visible, mm(c_b, b_b, NT), 0.0)
    first = iota((Q, LANES), 1) < WIDTH
    first_row = iota((1, LANES), 1) < WIDTH

    wide = 2 * LANES
    for quad in range(0, inner, wide):
        block = slice(quad, quad + wide)
        held = state[:, block]
        held_b = held.astype(BF16)
        st_ref[0, :, block] = held_b
        carried = mm(c_b, held_b)
        weighted, kept = [], []
        for part in range(0, wide, LANES):
            lo = quad + part
            pair = lo // LANES
            span = slice(lo, lo + LANES)
            xc = convolve(lo, xr_ref[:, span].astype(F32)).astype(BF16)
            xc_ref[:, span] = xc
            xc = xc.astype(F32)
            left, right, both = pair_columns(csum, pair, first)
            _, _, step_pair = pair_columns(step, pair, first)
            mix = jnp.concatenate(
                [
                    (scores * jnp.exp2(jnp.minimum(left - csum_t[2 * pair : 2 * pair + 1, :], 0.0))).astype(BF16),
                    (scores * jnp.exp2(jnp.minimum(right - csum_t[2 * pair + 1 : 2 * pair + 2, :], 0.0))).astype(BF16),
                ],
                axis=1,
            )
            fed_b = (xc * step_pair).astype(BF16)
            zero = jnp.zeros((Q, LANES), BF16)
            stacked = jnp.concatenate([jnp.where(first, fed_b, zero), jnp.where(first, zero, fed_b)], axis=0)
            y = mm(mix, stacked) + carried[:, part : part + LANES] * (jnp.exp2(both) * carry)
            y_ref[:, span] = (y + skip_ref[:, span] * xc).astype(BF16)
            closing = both[Q - 1 : Q, :]
            weighted.append((fed_b.astype(F32) * (jnp.exp2(closing - both) * last)).astype(BF16))
            kept.append(jnp.exp2(closing) * passing)
        fresh = mm(b_t, jnp.concatenate(weighted, axis=1))
        state[:, block] = held * jnp.concatenate(kept, axis=1) + fresh


def scan_backward(
    heads, chunks, top, ends_ref, dy_ref, xc_ref, pre_ref, xr_ref, small_ref, bc_ref, st_ref, taps_ref, par_ref,
    skip_ref, sel_ref, *refs,
):
    later_call = top + 1 < chunks
    if later_call:
        state_in, halo_in, acc_in, hacc_in, gain_acc_ref = refs[:5]
        dxa_ref, dxb_ref, rows_ref, acc_ref, hacc_ref = refs[7:12]
        refs = refs[12:]
    else:
        dxa_ref, dxb_ref, acc_ref, hacc_ref, state_out, halo_out = refs[:6]
        refs = refs[6:]
    dstate, dpre, ab_hi, ab_lo, v_b, u_b, dyd, fedw, dst_b, through = refs
    count = ends_ref.shape[0]
    inner = heads * WIDTH
    total_rows = chunks * Q
    chunk = top - pl.program_id(0)

    @pl.when(pl.program_id(0) == 0)
    def _():
        if top + 1 < chunks:
            dpre[:, Q : Q + 8, :] = halo_in[...]
            dstate[...] = state_in[...]
            acc_ref[...] = acc_in[...]
            hacc_ref[...] = hacc_in[...]
        else:
            dpre[:, Q : Q + 8, :] = jnp.zeros((dpre.shape[0], 8, LANES), F32)
            dstate[...] = jnp.zeros(dstate.shape, F32)
            acc_ref[...] = jnp.zeros(acc_ref.shape, F32)
            hacc_ref[...] = jnp.zeros(hacc_ref.shape, F32)

    rows, cols, row_ids, same, carry, last, passing = chunk_masks(chunk, ends_ref, count)
    causal = rows >= cols
    visible = same & causal
    lag_mask = [None]
    for lag in range(1, K):
        later = rows + lag
        keep = (segment_of(later, ends_ref, count) == row_ids) & (later < total_rows)
        lag_mask.append(keep.astype(F32))

    small = small_ref[...]
    shifted, step, decay_rate = decays(small[:, 2 * STATE :], par_ref)
    csum = mm_exact(causal.astype(F32), step * (-LOG2E * decay_rate))
    csum_t = csum.T
    b_b = bc_ref[:, :STATE]
    c_b = bc_ref[:, STATE:]
    c_t = c_b.astype(F32).T.astype(BF16)
    scores = jnp.where(visible, mm(c_b, b_b, NT), 0.0)
    first = iota((Q, LANES), 1) < WIDTH

    n_a = dxa_ref.shape[1]

    def put(lo, values):
        if lo < n_a:
            dxa_ref[:, lo : lo + LANES] = values.astype(BF16)
        else:
            dxb_ref[:, lo - n_a : lo - n_a + LANES] = values.astype(BF16)

    def fold(values):
        return values.reshape(Q // 8, 8, values.shape[1]).sum(axis=0)

    def conv_back(lo, d_conv, raw):
        span = slice(lo, lo + LANES)
        pre = pre_ref[:, span].astype(F32)
        gate = sigmoid(pre)
        d_pre = d_conv * (gate * (1.0 + pre * (1.0 - gate)))
        place = lo // LANES
        dpre[place, 0:Q, :] = d_pre
        d_raw = taps_ref[K - 1 : K, span] * d_pre
        acc_ref[8 * (K - 1) : 8 * K, span] += fold(d_pre * raw)
        acc_ref[8 * K : 8 * K + 8, span] += fold(d_pre)
        for lag in range(1, K):
            moved = dpre[place, lag : lag + Q, :] * lag_mask[lag]
            d_raw = d_raw + taps_ref[K - 1 - lag : K - lag, span] * moved
            acc_ref[8 * (K - 1 - lag) : 8 * (K - lag), span] += fold(moved * raw)
        dpre[place, Q : Q + 8, :] = d_pre[0:8, :]
        put(lo, d_raw)

    d_scores = jnp.zeros((Q, Q), F32)
    wide = 2 * LANES
    for quad in range(0, inner, wide):
        block = slice(quad, quad + wide)
        held_b = st_ref[0, :, block]
        d_held = dstate[:, block]
        d_held_b = d_held.astype(BF16)
        dst_b[:, block] = d_held_b
        carried = mm(c_b, held_b)
        returned = mm(b_b, d_held_b)
        crossing = (d_held * held_b.astype(F32)).reshape(STATE // 8, 8, wide).sum(axis=0)
        grown_parts, kept_parts = [], []
        for part in range(0, wide, LANES):
            lo = quad + part
            pair = lo // LANES
            span = slice(lo, lo + LANES)
            xc = xc_ref[:, span].astype(F32)
            dy_b = dy_ref[:, span]
            dy = dy_b.astype(F32)
            left, right, both = pair_columns(csum, pair, first)
            _, _, step_pair = pair_columns(step, pair, first)
            fall_left = jnp.exp2(jnp.minimum(left - csum_t[2 * pair : 2 * pair + 1, :], 0.0))
            fall_right = jnp.exp2(jnp.minimum(right - csum_t[2 * pair + 1 : 2 * pair + 2, :], 0.0))
            mix = jnp.concatenate([(scores * fall_left).astype(BF16), (scores * fall_right).astype(BF16)], axis=1)
            fed_b = (xc * step_pair).astype(BF16)
            fed = fed_b.astype(F32)
            zero = jnp.zeros((Q, LANES), BF16)
            stacked = jnp.concatenate([jnp.where(first, fed_b, zero), jnp.where(first, zero, fed_b)], axis=0)
            grown = jnp.exp2(both) * carry
            y = mm(mix, stacked) + carried[:, part : part + LANES] * grown
            d_mix = mm(dy_b, stacked, NT)
            d_scores = d_scores + d_mix[:, :Q] * fall_left + d_mix[:, Q:] * fall_right
            d_fed2 = mm(mix, dy_b, TN)
            d_fed_in = jnp.where(first, d_fed2[:Q], d_fed2[Q:])
            closing = both[Q - 1 : Q, :]
            shrink = jnp.exp2(closing - both) * last
            d_fed_out = returned[:, part : part + LANES] * shrink
            d_fed = d_fed_in + d_fed_out
            straddle = dy * y - fed * d_fed_in
            hi = straddle.astype(BF16)
            ab_hi[:, span] = hi
            ab_lo[:, span] = (straddle - hi.astype(F32)).astype(BF16)
            v_b[:, span] = (fed * d_fed_out).astype(BF16)
            u_b[:, span] = (xc * d_fed).astype(BF16)
            fedw[:, span] = (fed * shrink).astype(BF16)
            grown_parts.append((dy * grown).astype(BF16))
            kept_parts.append(jnp.exp2(closing) * passing)
            acc_ref[8 * K + 8 : 8 * K + 16, span] += fold(dy * xc)
            d_conv = d_fed * step_pair + skip_ref[:, span] * dy
            conv_back(lo, d_conv, xr_ref[:, span].astype(F32))
        dy_grown = jnp.concatenate(grown_parts, axis=1)
        kept = jnp.concatenate(kept_parts, axis=1)
        dyd[:, block] = dy_grown
        through[:, block] = crossing * kept
        dstate[:, block] = d_held * kept + mm(c_t, dy_grown)

    d_scores_b = jnp.where(visible, d_scores, 0.0).astype(BF16)
    d_c = mm(dyd[...], st_ref[0], NT) + mm(d_scores_b, b_b)
    d_b = mm(fedw[...], dst_b[...], NT) + mm(d_scores_b, c_b, TN)
    conv_back(inner, d_b, small[:, :STATE])
    conv_back(inner + STATE, d_c, small[:, STATE : 2 * STATE])

    sel = sel_ref[...]
    red_ab = mm(ab_hi[...], sel) + mm(ab_lo[...], sel)
    red_v = mm(v_b[...], sel)
    red_u = mm(u_b[...], sel)
    thr = through[...]
    thr_hi = thr.astype(BF16)
    red_t = mm(thr_hi, sel) + mm((thr - thr_hi.astype(F32)).astype(BF16), sel)
    d_rate = (
        mm_exact((same & (cols >= rows)).astype(F32), red_ab)
        + mm_exact((same & (cols < rows)).astype(F32), red_v)
        + jnp.sum(red_t, axis=0, keepdims=True)
    )
    d_step = red_u - d_rate * decay_rate
    d_dt = d_step * sigmoid(shifted)
    put(inner + 2 * STATE, d_dt)
    hacc_ref[0:8, :] += fold(d_dt)
    hacc_ref[8:16, :] += fold(d_rate * (-decay_rate * step))
    if later_call:

        @pl.when(pl.program_id(0) == pl.num_programs(0) - 1)
        def _():
            rows_ref[...] = jnp.zeros(rows_ref.shape, F32)
            for k in range(K + 2):
                rows_ref[k : k + 1, :] = jnp.sum(acc_ref[8 * k : 8 * k + 8, :], axis=0, keepdims=True)
            rows_ref[K + 2 : K + 3, :inner] = jnp.sum(gain_acc_ref[...], axis=0, keepdims=True)
            for k in range(2):
                total = jnp.sum(hacc_ref[8 * k : 8 * k + 8, :], axis=0, keepdims=True)
                rows_ref[K + 3 : K + 4, k * LANES : (k + 1) * LANES] = total

    else:
        halo_out[...] = dpre[:, Q : Q + 8, :]
        state_out[...] = dstate[...]


def load_blocks(offsets_ref, parts, whole, sems):
    @pl.when(pl.program_id(0) == 0)
    def _():
        copies = []
        count = sems.shape[0]
        size = whole.shape[0] // count
        for part in parts:
            for j in range(part.shape[0] // size):
                k = len(copies)
                start = pl.multiple_of(offsets_ref[k], 32) if count > 1 else 0
                source = part.at[pl.ds(j * size, size), :]
                copies.append(pltpu.make_async_copy(source, whole.at[pl.ds(start, size), :], sems.at[k]))
        for copy in copies:
            copy.start()
        for copy in copies:
            copy.wait()


def turn_rows(offsets_ref, me_ref, own_ref, other_ref, out_ref, turned):
    depth = own_ref.shape[1]
    rows = own_ref.shape[0]
    for index, source in enumerate((own_ref, other_ref)):
        at = pl.multiple_of(jnp.where(index == 0, me_ref[0], 1 - me_ref[0]) * rows, LANES)
        for lo in range(0, rows, Q):
            tile = source[lo : lo + Q, :].astype(F32)
            scale = lax.rsqrt(jnp.mean(tile * tile, axis=1, keepdims=True) + EPSILON)
            tile = tile * scale
            for left in range(0, depth, LANES):
                turned[left : left + LANES, pl.ds(at + lo, Q)] = tile[:, left : left + LANES].T.astype(BF16)
    count = offsets_ref.shape[0]
    size = depth // count
    for k in range(count):
        start = pl.multiple_of(offsets_ref[k], 32)
        out_ref[k * size : (k + 1) * size, :] = turned[pl.ds(start, size), :]


def project(count, heads, offsets_ref, me_ref, own_ref, other_ref, place_ref, *refs):
    blocks, (x_ref, small_ref, normed_ref, taps_ref, gain_ref, w_out_ref, w_ref, sems, out_sem) = refs[:count], refs[count:]
    load_blocks(offsets_ref, blocks, w_ref, sems)
    keep = pltpu.make_async_copy(w_ref, w_out_ref, out_sem)
    depth, inner = w_ref.shape[0], x_ref.shape[1]
    tile = 512

    @pl.when(pl.program_id(0) == 0)
    def _():
        keep.start()
        spare = w_ref[:, inner + 2 * STATE :]
        turned = spare.astype(F32).T
        gain_ref[...] = jnp.broadcast_to(turned[heads + K + 2 : heads + K + 3, :], gain_ref.shape)
        few = turned[heads : heads + 16, :].astype(BF16)
        lanes = iota((depth, LANES), 1)
        for lo in range(0, inner + 2 * STATE, LANES):
            if lo < inner:
                wanted, row = place_ref[:, :LANES] == lanes + lo, 0
            else:
                wanted, row = place_ref[:, LANES:] == lanes + (lo - inner), 8
            moved = mm(few, jnp.where(wanted, 1.0, 0.0).astype(BF16))
            taps_ref[:, lo : lo + LANES] = moved[row : row + 8, :]

    rows = jnp.where(pl.program_id(0) == me_ref[0], own_ref[...], other_ref[...]).astype(F32)
    scale = lax.rsqrt(jnp.mean(rows * rows, axis=1, keepdims=True) + EPSILON)
    rows = (rows * scale * gain_ref[0:1, :]).astype(BF16)
    normed_ref[...] = rows
    for lo in range(0, inner, tile):
        x_ref[:, lo : lo + tile] = mm(rows, w_ref[:, lo : lo + tile]).astype(BF16)
    small_ref[...] = mm(rows, w_ref[:, inner:])

    @pl.when(pl.program_id(0) == pl.num_programs(0) - 1)
    def _():
        keep.wait()


def row_sums(lanes):
    return mm_exact(jnp.ones((8, LANES), F32), lanes, NT)


def spread_rows(values):
    pick = jnp.where(iota((8, LANES), 0) == 0, 1.0, 0.0).astype(F32)
    return mm_exact(values, pick, TN)


def gate_forward(normed_ref, w_ref, y_ref, gain_ref, z_ref, gg_ref, sq_ref, square):
    rows, width = z_ref.shape
    size = 512

    @pl.when(pl.program_id(0) == 0)
    def _():
        square[...] = jnp.zeros(square.shape, F32)

    for lo in range(0, rows, size):
        at = slice(lo, lo + size)
        z = mm(normed_ref[at, :], w_ref[...]).astype(BF16)
        z_ref[at, :] = z
        z = z.astype(F32)
        gated = y_ref[at, :].astype(F32) * (z * sigmoid(z))
        gg_ref[at, :] = (gated * gain_ref[K + 1 : K + 2, :]).astype(BF16)
        twice = gated * gated
        for part in range(0, width, LANES):
            square[at, :] += twice[:, part : part + LANES]

    @pl.when(pl.program_id(0) == pl.num_programs(0) - 1)
    def _():
        sq_ref[...] = row_sums(square[...])


def branch(me_ref, ends_ref, gg_ref, own_ref, other_ref, w_ref, mine_ref, away_ref, prod_ref, product):
    rows, width = mine_ref.shape
    size = 512

    @pl.when(pl.program_id(0) == 0)
    def _():
        product[...] = jnp.zeros(product.shape, F32)

    for index, (out_ref, cot_ref) in enumerate(((mine_ref, own_ref), (away_ref, other_ref))):
        first = jnp.where(index == 0, me_ref[0], 1 - me_ref[0]) * rows
        for lo in range(0, rows, size):
            at = pl.ds(pl.multiple_of(first + lo, size), size)
            u = mm(gg_ref[at, :], w_ref[...], NT)
            out_ref[lo : lo + size, :] = u.astype(BF16)
            term = u * cot_ref[lo : lo + size, :].astype(F32)
            for part in range(0, width, LANES):
                product[at, :] += term[:, part : part + LANES]

    @pl.when(pl.program_id(0) == pl.num_programs(0) - 1)
    def _():
        live = iota(product.shape, 0) < ends_ref[ends_ref.shape[0] - 1]
        prod_ref[...] = row_sums(jnp.where(live, product[...], 0.0))


def gate_backward(
    me_ref, ends_ref, own_ref, other_ref, w_ref, y_ref, z_ref, rg_ref, coef_ref, gain_ref,
    dy_ref, dz_ref, acc_ref, rg, coef,
):
    total, width = dy_ref.shape
    rows = own_ref.shape[0]
    size = 512

    @pl.when(pl.program_id(0) == 0)
    def _():
        live = iota(rg.shape, 0) < ends_ref[ends_ref.shape[0] - 1]
        rg[...] = spread_rows(rg_ref[...])
        coef[...] = spread_rows(coef_ref[...])
        rg[...] = jnp.where(live, rg[...], 0.0)

    gain = gain_ref[K + 1 : K + 2, :]
    sums = jnp.zeros((8, width), F32)
    for index, cot_ref in enumerate((own_ref, other_ref)):
        first = jnp.where(index == 0, me_ref[0], 1 - me_ref[0]) * rows
        for lo in range(0, rows, size):
            at = pl.ds(pl.multiple_of(first + lo, size), size)
            ds = mm(cot_ref[lo : lo + size, :], w_ref[...])
            z = z_ref[at, :].astype(F32)
            y = y_ref[at, :].astype(F32)
            scale = jnp.concatenate([rg[at, :]] * (width // LANES), axis=1)
            back = jnp.concatenate([coef[at, :]] * (width // LANES), axis=1)
            gate = sigmoid(z)
            silu = z * gate
            gated = y * silu
            d_normal = ds * scale
            sums = sums + (d_normal * gated).reshape(size // 8, 8, width).sum(axis=0)
            d_gated = d_normal * gain - gated * back
            dy_ref[at, :] = (d_gated * silu).astype(BF16)
            dz_ref[at, :] = (d_gated * y * (gate + silu * (1.0 - gate))).astype(BF16)
    acc_ref[...] = sums


def grad_away(turned_ref, d_ref, away_ref):
    away_ref[...] = mm(turned_ref[...], d_ref[...]).astype(BF16)


def grad_keep(turned_ref, d_ref, got_ref, away_ref, keep_ref):
    half = away_ref.shape[0]
    d = d_ref[...]
    away_ref[...] = (mm(turned_ref[:half, :], d) + got_ref[:half, :].astype(F32)).astype(BF16)
    keep_ref[...] = mm(turned_ref[half:, :], d) + got_ref[half:, :].astype(F32)


def normed_back(rows_ref, dz_ref, dxa_ref, dxb_ref, wz_ref, wx_ref, out_ref):
    n_a = dxa_ref.shape[1]
    total = mm(dz_ref[...], wz_ref[...], NT)
    total = total + mm(dxa_ref[...], wx_ref[:, :n_a], NT) + mm(dxb_ref[...], wx_ref[:, n_a:], NT)
    out_ref[...] = total.astype(BF16)


def params():
    return pltpu.CompilerParams(dimension_semantics=("arbitrary",), vmem_limit_bytes=VMEM_LIMIT)


SMALL_COST = pl.CostEstimate(flops=1000, bytes_accessed=1000, transcendentals=0)


def rows_spec(block, width, column=0):
    return pl.BlockSpec((block, width), lambda i: (i, column))


def whole_spec(shape, column=0):
    return pl.BlockSpec(shape, lambda i: (0, column))


def local(
    tokens,
    cotangent,
    lengths,
    norm_gain,
    w_zx,
    w_bc,
    w_dt,
    conv_x,
    conv_x_bias,
    conv_bc,
    conv_bc_bias,
    dt_bias,
    a_log,
    d_skip,
    gate_gain,
    w_out,
):
    n_t = lax.axis_size("tensor")
    n_dp = lax.axis_size("dp")
    me_t = lax.axis_index("tensor")
    me_dp = lax.axis_index("dp")
    own_rows, depth = tokens.shape
    group = own_rows * n_t
    chunks = group // Q
    heads = dt_bias.shape[0]
    inner = heads * WIDTH
    inner_total = inner * n_t
    shard = w_zx.shape[1]
    pairs = [(i, n_t - 1 - i) for i in range(n_t)]

    def swap(v):
        return lax.ppermute(v, "tensor", pairs)

    def in_order(mine, other, axis=0):
        low = jnp.where(me_t == 0, mine, other)
        high = jnp.where(me_t == 0, other, mine)
        return jnp.concatenate([low, high], axis=axis)

    def sum_dp(v):
        step = 1
        while step < n_dp:
            v = v + lax.ppermute(v, "dp", [(i, i ^ step) for i in range(n_dp)])
            step *= 2
        return v

    def after(value, *others):
        return lax.optimization_barrier((value, *others))[0]

    ring = 4
    plane = n_dp // (2 * ring)

    around = [(i, (i + 2 * plane) % n_dp) for i in range(n_dp)]
    across = [(i, i ^ 2) for i in range(n_dp)]
    beside = [(i, i ^ 1) for i in range(n_dp)]

    def send(v, way):
        return lax.ppermute(v, "dp", way)

    by_hand = plane == 2 and shard % 32 == 0

    def whole(v):
        return [lax.all_gather(v, "dp", axis=0, tiled=True)]

    def block_offsets(count, size):
        if count == 1:
            return jnp.zeros((1,), jnp.int32)
        places = []
        for core in range(2):
            for side in range(2):
                for turn in range(ring):
                    level = (me_dp // (2 * plane) - turn + ring) % ring
                    places.append(level * (2 * plane) + ((me_dp % (2 * plane)) ^ (2 * side + core)))
        return jnp.stack(places).astype(jnp.int32) * size

    def relative_order():
        level, side, core = me_dp // 4, (me_dp // 2) % 2, me_dp % 2
        order = []
        for dc in (1, 0):
            for dy in (1, 0):
                for dz in range(1, ring + 1):
                    order.append(((level - dz + ring) % ring) * 4 + (side ^ dy) * 2 + (core ^ dc))
        return order

    back_by = lambda k: [(i, (i - 4 * k) % n_dp) for i in range(n_dp)]

    def send_owners(keep, got):
        sums = [keep[k * shard : (k + 1) * shard] + got[k * shard : (k + 1) * shard].astype(F32) for k in range(ring - 1)]
        sums = lax.optimization_barrier(tuple(value.astype(BF16) for value in sums))
        return sums, [send(value, back_by(k + 1)) for k, value in enumerate(sums)]

    def close(keep, got, came):
        last = slice((ring - 1) * shard, ring * shard)
        total = keep[last] + got[last].astype(F32)
        for value in came:
            total = total + value.astype(F32)
        return total

    ends = jnp.cumsum(lengths[0]).astype(jnp.int32)
    live = (lax.iota(jnp.int32, group) < ends[-1]).astype(F32)
    live_own = lax.dynamic_slice_in_dim(live, me_t * own_rows, own_rows, 0)
    me = me_t.astype(jnp.int32).reshape(1)

    span_p = conv_x_bias.shape[1]
    span_n = conv_bc_bias.shape[1]
    half_bc = w_bc.shape[1]
    bits = jnp.concatenate([norm_gain, conv_bc.reshape(-1), conv_bc_bias.reshape(-1)])
    bits = jnp.pad(bits, (0, LANES - bits.shape[0]))
    tiny = jnp.concatenate([w_bc.reshape(2 * half_bc, STATE), bits[None]], axis=0)
    other_tiny = swap(tiny)
    other_bc = other_tiny[: 2 * half_bc].reshape(w_bc.shape)
    both_bits = [bits, other_tiny[2 * half_bc]]
    at = norm_gain.shape[0]
    gain_pair = in_order(*[v[:at] for v in both_bits])[:, None]
    taps_bc = in_order(*[v[at : at + conv_bc.size].reshape(2, span_n, K) for v in both_bits], axis=1)
    at += conv_bc.size
    bias_bc = in_order(*[v[at : at + 2 * span_n].reshape(2, span_n, 1) for v in both_bits], axis=1)
    spare_bc = jnp.concatenate([taps_bc, bias_bc], axis=2).reshape(4 * span_n, K + 1)
    spare_x = [conv_x.reshape(shard, K), conv_x_bias.reshape(shard, 1), gate_gain.reshape(shard, 1), gain_pair]
    bc_pair = in_order(w_bc, other_bc, axis=1)
    packed = jnp.concatenate(
        [w_zx[1], bc_pair[0], bc_pair[1], w_dt, *spare_x, jnp.zeros((shard, 8 - K - 3), BF16)]
        + [jnp.pad(spare_bc, ((0, shard - 4 * span_n), (0, LANES - heads - 8 - K - 1)))],
        axis=1,
    )
    gain_pair = gain_pair.astype(F32)
    where = after(lax.iota(jnp.int32, depth), packed)
    home, inside = where // shard, where % shard
    place_x = (inside // span_p) * WIDTH + home * span_p + inside % span_p
    half_n = 2 * span_n
    place_bc = (inside // half_n) * STATE + home * half_n + inside % half_n
    place = jnp.concatenate([jnp.broadcast_to(v[:, None], (depth, LANES)) for v in (place_x, place_bc)], axis=1)
    par = jnp.concatenate([dt_bias[None], a_log[None], jnp.zeros((6, heads), F32)], axis=0)
    par = jnp.concatenate([par, jnp.zeros((8, LANES - heads), F32)], axis=1)
    skip = jnp.repeat(d_skip, WIDTH)[None]
    members = lax.iota(jnp.int32, inner)[:, None] // WIDTH
    sel = (members == lax.iota(jnp.int32, LANES)[None, :]).astype(BF16)
    smem = pl.BlockSpec(memory_space=pltpu.SMEM)
    vmem = pl.BlockSpec(memory_space=pltpu.VMEM)
    hbm = pl.BlockSpec(memory_space=pl.ANY)
    n_small = 2 * STATE + LANES
    n_conv = inner + 2 * STATE
    w_rest = jnp.concatenate([w_zx[0], w_out.T], axis=1)

    def turn(other_tokens):
        return pl.pallas_call(
            turn_rows,
            in_specs=[smem, smem, vmem, vmem],
            out_specs=vmem,
            out_shape=jax.ShapeDtypeStruct((depth, group), BF16),
            scratch_shapes=[pltpu.VMEM((depth, group), BF16)],
            compiler_params=pltpu.CompilerParams(vmem_limit_bytes=VMEM_LIMIT),
            cost_estimate=SMALL_COST,
            name="turn_rows",
        )((jnp.stack(relative_order()) * shard).astype(jnp.int32), me, tokens, other_tokens)

    if by_hand:
        line, other, line_c, other_c = [packed], [], [], []
        late = after(tokens, packed)
        pieces = [late[:176], late[176:352], late[352:]]
        arrived, constants = [], []
        for step in range(ring + 1):
            made = []
            if step < ring - 1:
                made.append((line, send(line[step], around)))
            if step < ring:
                made.append((other, send(line[step], across)))
                made.append((line_c, send(line[step], beside)))
            if step:
                made.append((other_c, send(other[step - 1], beside)))
            if 0 < step < ring:
                made.append((arrived, swap(pieces[step - 1])))
            if step == 0:
                made += [(constants, v) for v in (place, par, skip, sel)]
                made += [([], v) for v in pieces]
            if step == 2:
                zo_all = lax.all_gather(after(w_rest, line[2]), "dp", axis=0, tiled=True)
            fresh = lax.optimization_barrier(tuple(value for _, value in made))
            for (place_in, _), value in zip(made, fresh):
                place_in.append(value)
            if step == 0:
                pieces = fresh[-3:]
        other_tokens = jnp.concatenate(arrived, axis=0)
        other_cot = swap(after(cotangent, other_tokens))
        wx_blocks = line + other + line_c + other_c
        place, par, skip, sel = constants
    else:
        wx_blocks = whole(packed)
        zo_all = whole(w_rest)[0]
        other_tokens, other_cot = swap(tokens), swap(cotangent)
    count = len(wx_blocks)
    offsets = block_offsets(count, shard)
    sems = pltpu.SemaphoreType.DMA((count,))
    tok_own = tokens.astype(F32)
    inv_tok = lax.rsqrt(jnp.mean(tok_own * tok_own, axis=1, keepdims=True) + EPSILON)

    block = own_rows
    steps = group // block
    x_raw, small, normed, taps, gain_in, wx_all = pl.pallas_call(
        partial(project, count, heads),
        grid=(steps,),
        in_specs=[
            smem,
            smem,
            whole_spec((block, depth)),
            whole_spec((block, depth)),
            whole_spec((depth, 2 * LANES)),
        ]
        + [hbm] * count,
        out_specs=[
            rows_spec(block, inner),
            rows_spec(block, n_small),
            rows_spec(block, depth),
            whole_spec((8, n_conv)),
            whole_spec((8, depth)),
            hbm,
        ],
        out_shape=[
            jax.ShapeDtypeStruct((group, inner), BF16),
            jax.ShapeDtypeStruct((group, n_small), F32),
            jax.ShapeDtypeStruct((group, depth), BF16),
            jax.ShapeDtypeStruct((8, n_conv), F32),
            jax.ShapeDtypeStruct((8, depth), F32),
            jax.ShapeDtypeStruct((depth, inner + n_small), BF16),
        ],
        scratch_shapes=[pltpu.VMEM((depth, inner + n_small), BF16), sems, pltpu.SemaphoreType.DMA],
        compiler_params=params(),
        cost_estimate=SMALL_COST,
        name="project",
    )(offsets, me, tokens, other_tokens, place, *wx_blocks)
    xc, pre, bc, y_all, states = pl.pallas_call(
        partial(scan_forward, heads),
        grid=(chunks,),
        in_specs=[
            smem,
            rows_spec(Q, inner),
            rows_spec(Q, n_small),
            whole_spec((8, n_conv)),
            whole_spec((8, LANES)),
            whole_spec((1, inner)),
        ],
        out_specs=[
            rows_spec(Q, inner),
            rows_spec(Q, n_conv),
            rows_spec(Q, 2 * STATE),
            rows_spec(Q, inner),
            pl.BlockSpec((1, STATE, inner), lambda i: (i, 0, 0)),
        ],
        out_shape=[
            jax.ShapeDtypeStruct((group, inner), BF16),
            jax.ShapeDtypeStruct((group, n_conv), BF16),
            jax.ShapeDtypeStruct((group, 2 * STATE), BF16),
            jax.ShapeDtypeStruct((group, inner), BF16),
            jax.ShapeDtypeStruct((chunks, STATE, inner), BF16),
        ],
        scratch_shapes=[pltpu.VMEM((n_conv // LANES, Q + 8, LANES), F32), pltpu.VMEM((STATE, inner), F32)],
        compiler_params=params(),
        cost_estimate=SMALL_COST,
        name="scan_forward",
    )(ends, x_raw, small, taps, par, skip)

    cot_all = in_order(cotangent, other_cot)
    if by_hand:
        turned = turn(after(other_tokens, y_all))
        normed, turned, cot_all = lax.optimization_barrier((normed, turned, after(cot_all, y_all)))
    tile = 512
    columns = lambda rows, shift=0: pl.BlockSpec((rows, tile), lambda j: (0, j + shift))
    fixed = lambda shape: pl.BlockSpec(shape, lambda j: (0, 0))
    tiles = inner // tile
    z_all, gg, sq = pl.pallas_call(
        gate_forward,
        grid=(tiles,),
        in_specs=[fixed((group, depth)), columns(depth), columns(group), columns(8)],
        out_specs=[columns(group), columns(group), fixed((8, group))],
        out_shape=[
            jax.ShapeDtypeStruct((group, inner), BF16),
            jax.ShapeDtypeStruct((group, inner), BF16),
            jax.ShapeDtypeStruct((8, group), F32),
        ],
        scratch_shapes=[pltpu.VMEM((group, LANES), F32)],
        compiler_params=params(),
        cost_estimate=SMALL_COST,
        name="gate_forward",
    )(normed, zo_all, y_all, taps)
    sq_got = swap(sq)

    u_own, u_send, prod = pl.pallas_call(
        branch,
        grid=(depth // tile,),
        in_specs=[
            smem,
            smem,
            fixed((group, inner)),
            columns(own_rows),
            columns(own_rows),
            pl.BlockSpec((tile, inner), lambda j: (j, 1)),
        ],
        out_specs=[columns(own_rows), columns(own_rows), fixed((8, group))],
        out_shape=[
            jax.ShapeDtypeStruct((own_rows, depth), BF16),
            jax.ShapeDtypeStruct((own_rows, depth), BF16),
            jax.ShapeDtypeStruct((8, group), F32),
        ],
        scratch_shapes=[pltpu.VMEM((group, LANES), F32)],
        compiler_params=params(),
        cost_estimate=SMALL_COST,
        name="branch",
    )(me, ends, gg, cotangent, other_cot, zo_all)
    prod_got = swap(prod)
    sq_all = sq + after(sq_got, prod)
    inv_gate8 = lax.rsqrt(sq_all / inner_total + EPSILON)
    inv_gate = inv_gate8[0]
    d_branch = (cot_all.astype(F32) * (live * inv_gate)[:, None]).astype(BF16)
    g_out = lax.dot_general(d_branch, gg, TN, preferred_element_type=F32).astype(BF16)
    grad_out = lax.psum_scatter(g_out, "dp", scatter_dimension=0, tiled=True)
    prod_got = after(prod_got, g_out)
    u_recv = swap(after(u_send, g_out))
    inv_own = lax.dynamic_slice_in_dim(inv_gate, me_t * own_rows, own_rows, 0)
    out_branch = (u_own.astype(F32) + u_recv.astype(F32)) * (inv_own * live_own)[:, None]
    layer_out = (tokens.astype(F32) + out_branch).astype(BF16)

    prod_all = prod + prod_got
    coef8 = inv_gate8 * inv_gate8 * inv_gate8 * (prod_all / inner_total)
    dy, dz, gain_acc = pl.pallas_call(
        gate_backward,
        grid=(tiles,),
        in_specs=[
            smem,
            smem,
            fixed((own_rows, depth)),
            fixed((own_rows, depth)),
            columns(depth, tiles),
            columns(group),
            columns(group),
            fixed((8, group)),
            fixed((8, group)),
            columns(8),
        ],
        out_specs=[columns(group), columns(group), columns(8)],
        out_shape=[
            jax.ShapeDtypeStruct((group, inner), BF16),
            jax.ShapeDtypeStruct((group, inner), BF16),
            jax.ShapeDtypeStruct((8, inner), F32),
        ],
        scratch_shapes=[pltpu.VMEM((group, LANES), F32), pltpu.VMEM((group, LANES), F32)],
        compiler_params=params(),
        cost_estimate=SMALL_COST,
        name="gate_backward",
    )(me, ends, cotangent, other_cot, zo_all, y_all, z_all, inv_gate8, coef8, taps)
    dot = partial(lax.dot_general, preferred_element_type=F32)
    front = depth // 2

    def half_rows(which):
        return pl.BlockSpec((front, group), lambda j: (which, 0))

    def column_tiles(rows, width):
        return pl.BlockSpec((rows, width), lambda j: (0, j))

    def away_of(d, width):
        return pl.pallas_call(
            grad_away,
            grid=(d.shape[1] // width,),
            in_specs=[half_rows(0), column_tiles(group, width)],
            out_specs=column_tiles(front, width),
            out_shape=jax.ShapeDtypeStruct((front, d.shape[1]), BF16),
            compiler_params=params(),
            cost_estimate=SMALL_COST,
            name="grad_away",
        )(turned, d)

    def keep_of(d, width, got):
        outs = column_tiles(front // 2, width)
        return pl.pallas_call(
            grad_keep,
            grid=(d.shape[1] // width,),
            in_specs=[half_rows(1), column_tiles(group, width), column_tiles(front, width)],
            out_specs=[outs, outs],
            out_shape=[
                jax.ShapeDtypeStruct((front // 2, d.shape[1]), BF16),
                jax.ShapeDtypeStruct((front // 2, d.shape[1]), F32),
            ],
            compiler_params=params(),
            cost_estimate=SMALL_COST,
            name="grad_keep",
        )(turned, d, got)

    if by_hand:
        g_send = away_of(dz, tile)
        z_got = send(g_send, beside)
        dy = after(dy, g_send)
    else:
        grad_z = lax.psum_scatter(dot(normed, dz, TN).astype(BF16), "dp", scatter_dimension=0, tiled=True)

    halo_spec = pl.BlockSpec((n_conv // LANES, 8, LANES), lambda i: (0, 0, 0))

    def backward(top, number, carry):
        back = lambda width: pl.BlockSpec((Q, width), lambda i: (top - i, 0))
        operands = [ends, dy, xc, pre, x_raw, small, bc, states, taps, par, skip, sel, *carry]
        acc_spec = whole_spec((8 * (K + 2), n_conv))
        carry_shapes = [
            jax.ShapeDtypeStruct((STATE, inner), F32),
            jax.ShapeDtypeStruct((n_conv // LANES, 8, LANES), F32),
        ]
        carry_specs = []
        if carry:
            carry_specs = [whole_spec((STATE, inner)), halo_spec, acc_spec, whole_spec((16, LANES))]
            carry_specs += [whole_spec((8, inner)), hbm, hbm]
        return pl.pallas_call(
            partial(scan_backward, heads, chunks, top),
            grid=(number,),
            in_specs=[
                smem,
                back(inner),
                back(inner),
                back(n_conv),
                back(inner),
                back(n_small),
                back(2 * STATE),
                pl.BlockSpec((1, STATE, inner), lambda i: (top - i, 0, 0)),
                whole_spec((8, n_conv)),
                whole_spec((8, LANES)),
                whole_spec((1, inner)),
                whole_spec((inner, LANES)),
            ]
            + carry_specs,
            out_specs=[
                back(n_a),
                back(n_b),
                *([whole_spec((8, n_conv))] if carry else []),
                acc_spec,
                whole_spec((16, LANES)),
                *([] if carry else [whole_spec((STATE, inner)), halo_spec]),
            ],
            out_shape=[
                jax.ShapeDtypeStruct((group, n_a), BF16),
                jax.ShapeDtypeStruct((group, n_b), BF16),
                *([jax.ShapeDtypeStruct((8, n_conv), F32)] if carry else []),
                jax.ShapeDtypeStruct((8 * (K + 2), n_conv), F32),
                jax.ShapeDtypeStruct((16, LANES), F32),
                *([] if carry else carry_shapes),
            ],
            scratch_shapes=[
                pltpu.VMEM((STATE, inner), F32),
                pltpu.VMEM((n_conv // LANES, Q + 8, LANES), F32),
                pltpu.VMEM((Q, inner), BF16),
                pltpu.VMEM((Q, inner), BF16),
                pltpu.VMEM((Q, inner), BF16),
                pltpu.VMEM((Q, inner), BF16),
                pltpu.VMEM((Q, inner), BF16),
                pltpu.VMEM((Q, inner), BF16),
                pltpu.VMEM((STATE, inner), BF16),
                pltpu.VMEM((8, inner), F32),
            ],
            input_output_aliases={len(operands) - 2: 0, len(operands) - 1: 1} if carry else {},
            compiler_params=params(),
        cost_estimate=SMALL_COST,
            name="scan_backward",
        )(*operands)

    half_chunks = chunks // 2
    n_a = inner * 2 // 3
    n_b = inner + n_small - n_a
    dxa, dxb, acc, hacc, d_state, halo = backward(chunks - 1, chunks - half_chunks, ())
    if by_hand:
        z_away, z_keep = keep_of(dz, tile, after(z_got, dxa))
        z_got = send(z_away, across)
        d_state = after(d_state, z_away)
    dxa, dxb, vector = backward(half_chunks - 1, half_chunks, (d_state, halo, acc, hacc, gain_acc, dxa, dxb))[:3]
    dxa = after(dxa, u_recv)
    lanes_shared = lax.iota(jnp.int32, n_conv)[None, :] >= inner
    bits_of = lambda turn: [(i, i ^ (1 << turn)) for i in range(n_dp)]
    if by_hand:
        a_send = away_of(dxa, 512)
        a_got = send(a_send, beside)
        b_send = away_of(after(dxb, a_send), n_b)
        b_got = send(b_send, beside)
        z_got, b_send = lax.optimization_barrier((z_got, b_send))
        z_sums, z_came = send_owners(z_keep, z_got)
        a_got, dxa = lax.optimization_barrier((a_got, dxa, *z_sums))[:2]
        a_away, a_keep = keep_of(dxa, 512, a_got)
        b_got, vector, a_away, grad_out = lax.optimization_barrier((b_got, vector, a_away, grad_out))
        a_got = send(a_away, across)
        shared_got = swap(vector)
        b_away, b_keep = keep_of(after(dxb, a_away), n_b, b_got)
        b_got = send(b_away, across)
        shared_got, b_away = lax.optimization_barrier((shared_got, b_away))
        vector = vector + jnp.where(lanes_shared, shared_got, 0.0)
        vector_got = send(vector, bits_of(0))
        dz = after(dz, b_away, vector)
    else:
        dx = jnp.concatenate([dxa, dxb], axis=1)
        grad_x = lax.psum_scatter(dot(normed, dx, TN).astype(BF16), "dp", scatter_dimension=0, tiled=True)

    def back_rows(which, dz):
        pick = lambda width: pl.BlockSpec((own_rows, width), lambda j, rows: (rows[0], 0))
        return pl.pallas_call(
            normed_back,
            grid_spec=pltpu.PrefetchScalarGridSpec(
                num_scalar_prefetch=1,
                grid=(depth // tile,),
                in_specs=[
                    pick(inner),
                    pick(n_a),
                    pick(n_b),
                    pl.BlockSpec((tile, inner), lambda j, rows: (j, 0)),
                    pl.BlockSpec((tile, inner + n_small), lambda j, rows: (j, 0)),
                ],
                out_specs=pl.BlockSpec((own_rows, tile), lambda j, rows: (0, j)),
            ),
            out_shape=jax.ShapeDtypeStruct((own_rows, depth), BF16),
            compiler_params=params(),
            cost_estimate=SMALL_COST,
            name="normed_back",
        )(which, dz, dxa, dxb, zo_all, wx_all)

    dn_send = back_rows(n_t - 1 - me, dz)
    tail = ()
    if by_hand:
        w_sum = lambda w, g: jnp.sum(w.astype(F32) * g, axis=1)
        a_got, vector_got, dn_send, z_came = lax.optimization_barrier((a_got, vector_got, dn_send, z_came))
        dn_got = swap(dn_send)
        a_sums, a_came = send_owners(a_keep, a_got)
        grad_z = close(z_keep, z_got, z_came) * gain_pair
        vector = vector + vector_got
        vector_got = send(vector, bits_of(1))
        dn_own = back_rows(me, after(dz, vector, *a_sums))
        vector_got, dn_own, b_got = lax.optimization_barrier((vector_got, dn_own, b_got))
        vector = vector + vector_got
        b_sums, b_came = send_owners(b_keep, b_got)
        vector_got = send(vector, bits_of(2))
        in_part = w_sum(w_zx[0], grad_z)
        vector_got, grad_z, in_part, grad_out, *b_sums = lax.optimization_barrier(
            (vector_got, grad_z, in_part, grad_out, *b_sums)
        )
        grad_out = grad_out.astype(F32).T
        vector = vector + vector_got
        vector_got = send(vector, bits_of(3))
        vector_got, grad_out, layer_out, a_came = lax.optimization_barrier((vector_got, grad_out, layer_out, a_came))
        vector = vector + vector_got
        grad_a = close(a_keep, a_got, a_came) * gain_pair
        in_part = in_part + w_sum(packed[:, :n_a], grad_a)
    else:
        vector = sum_dp(vector + jnp.where(lanes_shared, swap(vector), 0.0))
        dn_own = back_rows(me, dz)
        dn_got = swap(dn_send)
        grad_out = grad_out.astype(F32).T
        grad_z, grad_x = grad_z.astype(F32), grad_x.astype(F32)
        in_part = jnp.sum(w_zx[0].astype(F32) * grad_z, axis=1) + jnp.sum(packed.astype(F32) * grad_x, axis=1)

    me_all = me_dp * n_t + me_t
    bc_sum = vector[: K + 1, inner:].reshape(K + 1, 2, STATE)
    bc_sum = lax.dynamic_slice_in_dim(bc_sum, me_all * span_n, span_n, 2)
    grad_bc_taps = bc_sum[:K].transpose(1, 2, 0).reshape(conv_bc.shape)
    grad_bc_bias = bc_sum[K]
    x_sum = vector[: K + 3, :inner].reshape(K + 3, heads, WIDTH)
    grad_skip = x_sum[K + 1].sum(axis=1)
    x_sum = lax.dynamic_slice_in_dim(x_sum, me_dp * span_p, span_p, 2)
    grad_x_taps = x_sum[:K].transpose(1, 2, 0).reshape(conv_x.shape)
    grad_x_bias = x_sum[K]
    grad_gate = x_sum[K + 2]
    grad_dt_bias = vector[K + 3, :heads]
    grad_a_log = vector[K + 3, LANES : LANES + heads]
    tail = (grad_bc_taps, grad_bc_bias, grad_skip, grad_x_taps, grad_x_bias, grad_gate, grad_dt_bias, grad_a_log)
    if by_hand:
        *tail, dn_got, in_part, grad_a = lax.optimization_barrier((*tail, dn_got, in_part, grad_a))
    grad_bc_taps, grad_bc_bias, grad_skip, grad_x_taps, grad_x_bias, grad_gate, grad_dt_bias, grad_a_log = tail

    dn = (dn_own.astype(F32) + dn_got.astype(F32)) * gain_in[0:1, :]
    grad_tokens = (
        cotangent.astype(F32)
        + inv_tok * dn
        - tok_own * inv_tok * inv_tok * inv_tok * jnp.mean(dn * tok_own, axis=1, keepdims=True)
    )

    if by_hand:
        grad_tokens, b_came = lax.optimization_barrier((grad_tokens, b_came))
        grad_b = close(b_keep, b_got, b_came) * gain_pair
        in_part = in_part + w_sum(packed[:, n_a:], grad_b)
    else:
        grad_a, grad_b = grad_x[:, :n_a], grad_x[:, n_a:]
    at = inner - n_a
    bc_part = jnp.concatenate([grad_b[:, at : at + 2 * STATE], jnp.broadcast_to(in_part[:, None], (shard, LANES))], axis=1)
    grad_zx = jnp.stack([grad_z, jnp.concatenate([grad_a, grad_b[:, :at]], axis=1)])
    grad_dt = grad_b[:, at + 2 * STATE : at + 2 * STATE + heads]
    half = half_bc
    bc_own = lax.dynamic_slice_in_dim(bc_part, me_t * half, half, 0)
    bc_send = lax.dynamic_slice_in_dim(bc_part, (n_t - 1 - me_t) * half, half, 0)
    bc_total = bc_own + swap(bc_send)
    own_gain = norm_gain.astype(F32)
    grad_bc = bc_total[:, : 2 * STATE].reshape(half, 2, STATE).transpose(1, 0, 2)
    grad_in = bc_total[:, 2 * STATE] / own_gain
    return (
        layer_out,
        grad_tokens,
        grad_in,
        grad_zx,
        grad_bc,
        grad_dt,
        grad_x_taps,
        grad_x_bias,
        grad_bc_taps,
        grad_bc_bias,
        grad_dt_bias,
        grad_a_log,
        grad_skip,
        grad_gate,
        grad_out,
    )


def solution(mesh):
    both = ("dp", "tensor")
    in_specs = (
        P(both, None),
        P(both, None),
        P("dp", None),
        P(both),
        P(None, "dp", "tensor"),
        P(None, both, None),
        P("dp", "tensor"),
        P("tensor", "dp"),
        P("tensor", "dp"),
        P(None, both),
        P(None, both),
        P("tensor"),
        P("tensor"),
        P("tensor"),
        P("tensor", "dp"),
        P("tensor", "dp"),
    )
    out_specs = (
        P(both, None),
        P(both, None),
        P(both),
        P(None, "dp", "tensor"),
        P(None, both, None),
        P("dp", "tensor"),
        P("tensor", "dp"),
        P("tensor", "dp"),
        P(None, both),
        P(None, both),
        P("tensor"),
        P("tensor"),
        P("tensor"),
        P("tensor", "dp"),
        P("tensor", "dp"),
    )
    return jax.shard_map(local, mesh=mesh, in_specs=in_specs, out_specs=out_specs, check_vma=False)
```

```python
from functools import partial

import jax
import jax.numpy as jnp
from jax import lax
from jax.experimental import pallas as pl
from jax.experimental.pallas import tpu as pltpu
from jax.sharding import PartitionSpec as P

EPSILON = 1e-05
HIGHEST = lax.Precision.HIGHEST
K = 4
WIDTH = 64
STATE = 128
Q = 128
LANES = 128
LOG2E = 1.4426950408889634
VMEM_LIMIT = 60 * 1024 * 1024
F32 = jnp.float32
BF16 = jnp.bfloat16

NN = (((1,), (0,)), ((), ()))
NT = (((1,), (1,)), ((), ()))
TN = (((0,), (0,)), ((), ()))


def mm(a, b, dims=NN):
    return lax.dot_general(a, b, dims, preferred_element_type=F32)


def mm_exact(a, b, dims=NN):
    return lax.dot_general(a, b, dims, preferred_element_type=F32, precision=HIGHEST)


def iota(shape, dim):
    return lax.broadcasted_iota(jnp.int32, shape, dim)


def segment_of(rows, ends_ref, count):
    total = (rows >= ends_ref[0]).astype(jnp.int32)
    for j in range(1, count):
        total = total + (rows >= ends_ref[j]).astype(jnp.int32)
    return total


def scalar_segment(row, ends_ref, count):
    total = jnp.where(row >= ends_ref[0], 1, 0)
    for j in range(1, count):
        total = total + jnp.where(row >= ends_ref[j], 1, 0)
    return total


def sigmoid(v):
    return 0.5 * jnp.tanh(0.5 * v) + 0.5


def softplus(v):
    return jnp.maximum(v, 0.0) + jnp.log1p(jnp.exp(-jnp.abs(v)))


def chunk_masks(chunk, ends_ref, count):
    base = chunk * Q
    rows = iota((Q, Q), 0) + base
    cols = iota((Q, Q), 1) + base
    row_ids = segment_of(rows, ends_ref, count)
    col_ids = segment_of(cols, ends_ref, count)
    same = row_ids == col_ids
    before_id = jnp.where(chunk == 0, -1, scalar_segment(base - 1, ends_ref, count))
    final_id = scalar_segment(base + Q - 1, ends_ref, count)
    carry = (row_ids == before_id).astype(F32)
    last = (row_ids == final_id).astype(F32)
    passing = jnp.where(before_id == final_id, 1.0, 0.0).astype(F32)
    return rows, cols, row_ids, same, carry, last, passing


def decays(dt_raw, par_ref):
    shifted = dt_raw + par_ref[0:1, :]
    step = softplus(shifted)
    decay_rate = jnp.exp(par_ref[1:2, :])
    return shifted, step, decay_rate


def pair_columns(values, pair, first):
    left = jnp.broadcast_to(values[:, 2 * pair : 2 * pair + 1], (Q, LANES))
    right = jnp.broadcast_to(values[:, 2 * pair + 1 : 2 * pair + 2], (Q, LANES))
    return left, right, jnp.where(first, left, right)


def scan_forward(
    heads, ends_ref, xr_ref, small_ref, taps_ref, par_ref, skip_ref,
    xc_ref, pre_ref, bc_ref, y_ref, st_ref, buf, state,
):
    count = ends_ref.shape[0]
    inner = heads * WIDTH
    chunk = pl.program_id(0)

    @pl.when(chunk == 0)
    def _():
        buf[:, 0:8, :] = jnp.zeros((buf.shape[0], 8, LANES), F32)
        state[...] = jnp.zeros(state.shape, F32)

    rows, cols, row_ids, same, carry, last, passing = chunk_masks(chunk, ends_ref, count)
    causal = rows >= cols
    visible = same & causal
    lag_mask = [None]
    for lag in range(1, K):
        earlier = rows - lag
        keep = (segment_of(earlier, ends_ref, count) == row_ids) & (earlier >= 0)
        lag_mask.append(keep.astype(F32))

    small = small_ref[...]

    def convolve(lo, raw):
        span = slice(lo, lo + LANES)
        place = lo // LANES
        buf[place, 8 : 8 + Q, :] = raw
        pre = taps_ref[K : K + 1, span] + taps_ref[K - 1 : K, span] * raw
        for lag in range(1, K):
            pre = pre + taps_ref[K - 1 - lag : K - lag, span] * (
                buf[place, 8 - lag : 8 - lag + Q, :] * lag_mask[lag]
            )
        buf[place, 0:8, :] = raw[Q - 8 : Q, :]
        pre_ref[:, span] = pre.astype(BF16)
        return pre * sigmoid(pre)

    b_f = convolve(inner, small[:, :STATE]).astype(BF16).astype(F32)
    c_b = convolve(inner + STATE, small[:, STATE : 2 * STATE]).astype(BF16)
    b_b = b_f.astype(BF16)
    bc_ref[:, :STATE] = b_b
    bc_ref[:, STATE:] = c_b
    b_t = b_f.T.astype(BF16)

    _, step, decay_rate = decays(small[:, 2 * STATE :], par_ref)
    csum = mm_exact(causal.astype(F32), step * (-LOG2E * decay_rate))
    csum_t = csum.T
    scores = jnp.where(visible, mm(c_b, b_b, NT), 0.0)
    first = iota((Q, LANES), 1) < WIDTH
    first_row = iota((1, LANES), 1) < WIDTH

    wide = 2 * LANES
    for quad in range(0, inner, wide):
        block = slice(quad, quad + wide)
        held = state[:, block]
        held_b = held.astype(BF16)
        st_ref[0, :, block] = held_b
        carried = mm(c_b, held_b)
        weighted, kept = [], []
        for part in range(0, wide, LANES):
            lo = quad + part
            pair = lo // LANES
            span = slice(lo, lo + LANES)
            xc = convolve(lo, xr_ref[:, span].astype(F32)).astype(BF16)
            xc_ref[:, span] = xc
            xc = xc.astype(F32)
            left, right, both = pair_columns(csum, pair, first)
            _, _, step_pair = pair_columns(step, pair, first)
            mix = jnp.concatenate(
                [
                    (scores * jnp.exp2(jnp.minimum(left - csum_t[2 * pair : 2 * pair + 1, :], 0.0))).astype(BF16),
                    (scores * jnp.exp2(jnp.minimum(right - csum_t[2 * pair + 1 : 2 * pair + 2, :], 0.0))).astype(BF16),
                ],
                axis=1,
            )
            fed_b = (xc * step_pair).astype(BF16)
            zero = jnp.zeros((Q, LANES), BF16)
            stacked = jnp.concatenate([jnp.where(first, fed_b, zero), jnp.where(first, zero, fed_b)], axis=0)
            y = mm(mix, stacked) + carried[:, part : part + LANES] * (jnp.exp2(both) * carry)
            y_ref[:, span] = (y + skip_ref[:, span] * xc).astype(BF16)
            closing = both[Q - 1 : Q, :]
            weighted.append((fed_b.astype(F32) * (jnp.exp2(closing - both) * last)).astype(BF16))
            kept.append(jnp.exp2(closing) * passing)
        fresh = mm(b_t, jnp.concatenate(weighted, axis=1))
        state[:, block] = held * jnp.concatenate(kept, axis=1) + fresh


def scan_backward(
    heads, chunks, top, ends_ref, dy_ref, xc_ref, pre_ref, xr_ref, small_ref, bc_ref, st_ref, taps_ref, par_ref,
    skip_ref, sel_ref, *refs,
):
    later_call = top + 1 < chunks
    if later_call:
        state_in, halo_in, acc_in, hacc_in, gain_acc_ref = refs[:5]
        dxa_ref, dxb_ref, rows_ref, acc_ref, hacc_ref = refs[7:12]
        refs = refs[12:]
    else:
        dxa_ref, dxb_ref, acc_ref, hacc_ref, state_out, halo_out = refs[:6]
        refs = refs[6:]
    dstate, dpre, ab_hi, ab_lo, v_b, u_b, dyd, fedw, dst_b, through = refs
    count = ends_ref.shape[0]
    inner = heads * WIDTH
    total_rows = chunks * Q
    chunk = top - pl.program_id(0)

    @pl.when(pl.program_id(0) == 0)
    def _():
        if top + 1 < chunks:
            dpre[:, Q : Q + 8, :] = halo_in[...]
            dstate[...] = state_in[...]
            acc_ref[...] = acc_in[...]
            hacc_ref[...] = hacc_in[...]
        else:
            dpre[:, Q : Q + 8, :] = jnp.zeros((dpre.shape[0], 8, LANES), F32)
            dstate[...] = jnp.zeros(dstate.shape, F32)
            acc_ref[...] = jnp.zeros(acc_ref.shape, F32)
            hacc_ref[...] = jnp.zeros(hacc_ref.shape, F32)

    rows, cols, row_ids, same, carry, last, passing = chunk_masks(chunk, ends_ref, count)
    causal = rows >= cols
    visible = same & causal
    lag_mask = [None]
    for lag in range(1, K):
        later = rows + lag
        keep = (segment_of(later, ends_ref, count) == row_ids) & (later < total_rows)
        lag_mask.append(keep.astype(F32))

    small = small_ref[...]
    shifted, step, decay_rate = decays(small[:, 2 * STATE :], par_ref)
    csum = mm_exact(causal.astype(F32), step * (-LOG2E * decay_rate))
    csum_t = csum.T
    b_b = bc_ref[:, :STATE]
    c_b = bc_ref[:, STATE:]
    c_t = c_b.astype(F32).T.astype(BF16)
    scores = jnp.where(visible, mm(c_b, b_b, NT), 0.0)
    first = iota((Q, LANES), 1) < WIDTH

    n_a = dxa_ref.shape[1]

    def put(lo, values):
        if lo < n_a:
            dxa_ref[:, lo : lo + LANES] = values.astype(BF16)
        else:
            dxb_ref[:, lo - n_a : lo - n_a + LANES] = values.astype(BF16)

    def fold(values):
        return values.reshape(Q // 8, 8, values.shape[1]).sum(axis=0)

    def conv_back(lo, d_conv, raw):
        span = slice(lo, lo + LANES)
        pre = pre_ref[:, span].astype(F32)
        gate = sigmoid(pre)
        d_pre = d_conv * (gate * (1.0 + pre * (1.0 - gate)))
        place = lo // LANES
        dpre[place, 0:Q, :] = d_pre
        d_raw = taps_ref[K - 1 : K, span] * d_pre
        acc_ref[8 * (K - 1) : 8 * K, span] += fold(d_pre * raw)
        acc_ref[8 * K : 8 * K + 8, span] += fold(d_pre)
        for lag in range(1, K):
            moved = dpre[place, lag : lag + Q, :] * lag_mask[lag]
            d_raw = d_raw + taps_ref[K - 1 - lag : K - lag, span] * moved
            acc_ref[8 * (K - 1 - lag) : 8 * (K - lag), span] += fold(moved * raw)
        dpre[place, Q : Q + 8, :] = d_pre[0:8, :]
        put(lo, d_raw)

    d_scores = jnp.zeros((Q, Q), F32)
    wide = 2 * LANES
    for quad in range(0, inner, wide):
        block = slice(quad, quad + wide)
        held_b = st_ref[0, :, block]
        d_held = dstate[:, block]
        d_held_b = d_held.astype(BF16)
        dst_b[:, block] = d_held_b
        carried = mm(c_b, held_b)
        returned = mm(b_b, d_held_b)
        crossing = (d_held * held_b.astype(F32)).reshape(STATE // 8, 8, wide).sum(axis=0)
        grown_parts, kept_parts = [], []
        for part in range(0, wide, LANES):
            lo = quad + part
            pair = lo // LANES
            span = slice(lo, lo + LANES)
            xc = xc_ref[:, span].astype(F32)
            dy_b = dy_ref[:, span]
            dy = dy_b.astype(F32)
            left, right, both = pair_columns(csum, pair, first)
            _, _, step_pair = pair_columns(step, pair, first)
            fall_left = jnp.exp2(jnp.minimum(left - csum_t[2 * pair : 2 * pair + 1, :], 0.0))
            fall_right = jnp.exp2(jnp.minimum(right - csum_t[2 * pair + 1 : 2 * pair + 2, :], 0.0))
            mix = jnp.concatenate([(scores * fall_left).astype(BF16), (scores * fall_right).astype(BF16)], axis=1)
            fed_b = (xc * step_pair).astype(BF16)
            fed = fed_b.astype(F32)
            zero = jnp.zeros((Q, LANES), BF16)
            stacked = jnp.concatenate([jnp.where(first, fed_b, zero), jnp.where(first, zero, fed_b)], axis=0)
            grown = jnp.exp2(both) * carry
            y = mm(mix, stacked) + carried[:, part : part + LANES] * grown
            d_mix = mm(dy_b, stacked, NT)
            d_scores = d_scores + d_mix[:, :Q] * fall_left + d_mix[:, Q:] * fall_right
            d_fed2 = mm(mix, dy_b, TN)
            d_fed_in = jnp.where(first, d_fed2[:Q], d_fed2[Q:])
            closing = both[Q - 1 : Q, :]
            shrink = jnp.exp2(closing - both) * last
            d_fed_out = returned[:, part : part + LANES] * shrink
            d_fed = d_fed_in + d_fed_out
            straddle = dy * y - fed * d_fed_in
            hi = straddle.astype(BF16)
            ab_hi[:, span] = hi
            ab_lo[:, span] = (straddle - hi.astype(F32)).astype(BF16)
            v_b[:, span] = (fed * d_fed_out).astype(BF16)
            u_b[:, span] = (xc * d_fed).astype(BF16)
            fedw[:, span] = (fed * shrink).astype(BF16)
            grown_parts.append((dy * grown).astype(BF16))
            kept_parts.append(jnp.exp2(closing) * passing)
            acc_ref[8 * K + 8 : 8 * K + 16, span] += fold(dy * xc)
            d_conv = d_fed * step_pair + skip_ref[:, span] * dy
            conv_back(lo, d_conv, xr_ref[:, span].astype(F32))
        dy_grown = jnp.concatenate(grown_parts, axis=1)
        kept = jnp.concatenate(kept_parts, axis=1)
        dyd[:, block] = dy_grown
        through[:, block] = crossing * kept
        dstate[:, block] = d_held * kept + mm(c_t, dy_grown)

    d_scores_b = jnp.where(visible, d_scores, 0.0).astype(BF16)
    d_c = mm(dyd[...], st_ref[0], NT) + mm(d_scores_b, b_b)
    d_b = mm(fedw[...], dst_b[...], NT) + mm(d_scores_b, c_b, TN)
    conv_back(inner, d_b, small[:, :STATE])
    conv_back(inner + STATE, d_c, small[:, STATE : 2 * STATE])

    sel = sel_ref[...]
    red_ab = mm(ab_hi[...], sel) + mm(ab_lo[...], sel)
    red_v = mm(v_b[...], sel)
    red_u = mm(u_b[...], sel)
    thr = through[...]
    thr_hi = thr.astype(BF16)
    red_t = mm(thr_hi, sel) + mm((thr - thr_hi.astype(F32)).astype(BF16), sel)
    d_rate = (
        mm_exact((same & (cols >= rows)).astype(F32), red_ab)
        + mm_exact((same & (cols < rows)).astype(F32), red_v)
        + jnp.sum(red_t, axis=0, keepdims=True)
    )
    d_step = red_u - d_rate * decay_rate
    d_dt = d_step * sigmoid(shifted)
    put(inner + 2 * STATE, d_dt)
    hacc_ref[0:8, :] += fold(d_dt)
    hacc_ref[8:16, :] += fold(d_rate * (-decay_rate * step))
    if later_call:

        @pl.when(pl.program_id(0) == pl.num_programs(0) - 1)
        def _():
            rows_ref[...] = jnp.zeros(rows_ref.shape, F32)
            for k in range(K + 2):
                rows_ref[k : k + 1, :] = jnp.sum(acc_ref[8 * k : 8 * k + 8, :], axis=0, keepdims=True)
            rows_ref[K + 2 : K + 3, :inner] = jnp.sum(gain_acc_ref[...], axis=0, keepdims=True)
            for k in range(2):
                total = jnp.sum(hacc_ref[8 * k : 8 * k + 8, :], axis=0, keepdims=True)
                rows_ref[K + 3 : K + 4, k * LANES : (k + 1) * LANES] = total

    else:
        halo_out[...] = dpre[:, Q : Q + 8, :]
        state_out[...] = dstate[...]


def load_blocks(offsets_ref, parts, whole, sems):
    @pl.when(pl.program_id(0) == 0)
    def _():
        copies = []
        count = sems.shape[0]
        size = whole.shape[0] // count
        for part in parts:
            for j in range(part.shape[0] // size):
                k = len(copies)
                start = pl.multiple_of(offsets_ref[k], 32) if count > 1 else 0
                source = part.at[pl.ds(j * size, size), :]
                copies.append(pltpu.make_async_copy(source, whole.at[pl.ds(start, size), :], sems.at[k]))
        for copy in copies:
            copy.start()
        for copy in copies:
            copy.wait()


def turn_rows(offsets_ref, me_ref, own_ref, other_ref, out_ref, turned):
    depth = own_ref.shape[1]
    rows = own_ref.shape[0]
    for index, source in enumerate((own_ref, other_ref)):
        at = pl.multiple_of(jnp.where(index == 0, me_ref[0], 1 - me_ref[0]) * rows, LANES)
        for lo in range(0, rows, Q):
            tile = source[lo : lo + Q, :].astype(F32)
            scale = lax.rsqrt(jnp.mean(tile * tile, axis=1, keepdims=True) + EPSILON)
            tile = tile * scale
            for left in range(0, depth, LANES):
                turned[left : left + LANES, pl.ds(at + lo, Q)] = tile[:, left : left + LANES].T.astype(BF16)
    count = offsets_ref.shape[0]
    size = depth // count
    for k in range(count):
        start = pl.multiple_of(offsets_ref[k], 32)
        out_ref[k * size : (k + 1) * size, :] = turned[pl.ds(start, size), :]


def project(count, heads, offsets_ref, me_ref, own_ref, other_ref, place_ref, *refs):
    blocks, (x_ref, small_ref, normed_ref, taps_ref, gain_ref, w_out_ref, w_ref, sems, out_sem) = refs[:count], refs[count:]
    load_blocks(offsets_ref, blocks, w_ref, sems)
    keep = pltpu.make_async_copy(w_ref, w_out_ref, out_sem)
    depth, inner = w_ref.shape[0], x_ref.shape[1]
    tile = 512

    @pl.when(pl.program_id(0) == 0)
    def _():
        keep.start()
        spare = w_ref[:, inner + 2 * STATE :]
        turned = spare.astype(F32).T
        gain_ref[...] = jnp.broadcast_to(turned[heads + K + 2 : heads + K + 3, :], gain_ref.shape)
        few = turned[heads : heads + 16, :].astype(BF16)
        lanes = iota((depth, LANES), 1)
        for lo in range(0, inner + 2 * STATE, LANES):
            if lo < inner:
                wanted, row = place_ref[:, :LANES] == lanes + lo, 0
            else:
                wanted, row = place_ref[:, LANES:] == lanes + (lo - inner), 8
            moved = mm(few, jnp.where(wanted, 1.0, 0.0).astype(BF16))
            taps_ref[:, lo : lo + LANES] = moved[row : row + 8, :]

    rows = jnp.where(pl.program_id(0) == me_ref[0], own_ref[...], other_ref[...]).astype(F32)
    scale = lax.rsqrt(jnp.mean(rows * rows, axis=1, keepdims=True) + EPSILON)
    rows = (rows * scale * gain_ref[0:1, :]).astype(BF16)
    normed_ref[...] = rows
    for lo in range(0, inner, tile):
        x_ref[:, lo : lo + tile] = mm(rows, w_ref[:, lo : lo + tile]).astype(BF16)
    small_ref[...] = mm(rows, w_ref[:, inner:])

    @pl.when(pl.program_id(0) == pl.num_programs(0) - 1)
    def _():
        keep.wait()


def row_sums(lanes):
    return mm_exact(jnp.ones((8, LANES), F32), lanes, NT)


def spread_rows(values):
    pick = jnp.where(iota((8, LANES), 0) == 0, 1.0, 0.0).astype(F32)
    return mm_exact(values, pick, TN)


def keep_whole(whole, out_ref, sem):
    keep = pltpu.make_async_copy(whole, out_ref, sem)

    @pl.when(pl.program_id(0) == 0)
    def _():
        keep.start()

    def finish():
        @pl.when(pl.program_id(0) == pl.num_programs(0) - 1)
        def _():
            keep.wait()

    return finish


def gate_forward(count, offsets_ref, normed_ref, y_ref, gain_ref, *refs):
    parts, (z_ref, gg_ref, sq_ref, w_out_ref, square, whole, sems, out_sem) = refs[:count], refs[count:]
    load_blocks(offsets_ref, parts, whole, sems)
    finish = keep_whole(whole, w_out_ref, out_sem)
    rows, width = z_ref.shape
    w = whole[:, pl.ds(pl.multiple_of(pl.program_id(0) * width, width), width)]
    size = 512

    @pl.when(pl.program_id(0) == 0)
    def _():
        square[...] = jnp.zeros(square.shape, F32)

    for lo in range(0, rows, size):
        at = slice(lo, lo + size)
        z = mm(normed_ref[at, :], w).astype(BF16)
        z_ref[at, :] = z
        z = z.astype(F32)
        gated = y_ref[at, :].astype(F32) * (z * sigmoid(z))
        gg_ref[at, :] = (gated * gain_ref[K + 1 : K + 2, :]).astype(BF16)
        twice = gated * gated
        for part in range(0, width, LANES):
            square[at, :] += twice[:, part : part + LANES]

    @pl.when(pl.program_id(0) == pl.num_programs(0) - 1)
    def _():
        sq_ref[...] = row_sums(square[...])

    finish()


def branch(count, offsets_ref, me_ref, ends_ref, gg_ref, own_ref, other_ref, *refs):
    parts, (mine_ref, away_ref, prod_ref, w_out_ref, product, whole, sems, out_sem) = refs[:count], refs[count:]
    load_blocks(offsets_ref, parts, whole, sems)
    finish = keep_whole(whole, w_out_ref, out_sem)
    rows, width = mine_ref.shape
    w = whole[pl.ds(pl.multiple_of(pl.program_id(0) * width, width), width), :]
    size = 512

    @pl.when(pl.program_id(0) == 0)
    def _():
        product[...] = jnp.zeros(product.shape, F32)

    for index, (out_ref, cot_ref) in enumerate(((mine_ref, own_ref), (away_ref, other_ref))):
        first = jnp.where(index == 0, me_ref[0], 1 - me_ref[0]) * rows
        for lo in range(0, rows, size):
            at = pl.ds(pl.multiple_of(first + lo, size), size)
            u = mm(gg_ref[at, :], w, NT)
            out_ref[lo : lo + size, :] = u.astype(BF16)
            term = u * cot_ref[lo : lo + size, :].astype(F32)
            for part in range(0, width, LANES):
                product[at, :] += term[:, part : part + LANES]

    @pl.when(pl.program_id(0) == pl.num_programs(0) - 1)
    def _():
        live = iota(product.shape, 0) < ends_ref[ends_ref.shape[0] - 1]
        prod_ref[...] = row_sums(jnp.where(live, product[...], 0.0))

    finish()


def gate_backward(
    me_ref, ends_ref, own_ref, other_ref, w_ref, y_ref, z_ref, rg_ref, coef_ref, gain_ref,
    dy_ref, dz_ref, acc_ref, rg, coef,
):
    total, width = dy_ref.shape
    rows = own_ref.shape[0]
    size = 512

    @pl.when(pl.program_id(0) == 0)
    def _():
        live = iota(rg.shape, 0) < ends_ref[ends_ref.shape[0] - 1]
        rg[...] = spread_rows(rg_ref[...])
        coef[...] = spread_rows(coef_ref[...])
        rg[...] = jnp.where(live, rg[...], 0.0)

    gain = gain_ref[K + 1 : K + 2, :]
    sums = jnp.zeros((8, width), F32)
    for index, cot_ref in enumerate((own_ref, other_ref)):
        first = jnp.where(index == 0, me_ref[0], 1 - me_ref[0]) * rows
        for lo in range(0, rows, size):
            at = pl.ds(pl.multiple_of(first + lo, size), size)
            ds = mm(cot_ref[lo : lo + size, :], w_ref[...])
            z = z_ref[at, :].astype(F32)
            y = y_ref[at, :].astype(F32)
            scale = jnp.concatenate([rg[at, :]] * (width // LANES), axis=1)
            back = jnp.concatenate([coef[at, :]] * (width // LANES), axis=1)
            gate = sigmoid(z)
            silu = z * gate
            gated = y * silu
            d_normal = ds * scale
            sums = sums + (d_normal * gated).reshape(size // 8, 8, width).sum(axis=0)
            d_gated = d_normal * gain - gated * back
            dy_ref[at, :] = (d_gated * silu).astype(BF16)
            dz_ref[at, :] = (d_gated * y * (gate + silu * (1.0 - gate))).astype(BF16)
    acc_ref[...] = sums


def grad_away(turned_ref, d_ref, away_ref):
    away_ref[...] = mm(turned_ref[...], d_ref[...]).astype(BF16)


def grad_keep(turned_ref, d_ref, got_ref, *refs):
    keep_ref = refs[-1]
    keep_ref[...] = (mm(turned_ref[...], d_ref[...]) + got_ref[...].astype(F32)).astype(BF16)


def grad_split(side_ref, turned_ref, d_ref, got_ref, away_ref, keep_ref, total):
    total[...] = mm(turned_ref[...], d_ref[...]) + got_ref[...].astype(F32)
    size = total.shape[0] // 8
    for k in range(4):
        at = slice(k * size, (k + 1) * size)
        mine = pl.ds(pl.multiple_of((2 * k + side_ref[0]) * size, 32), size)
        others = pl.ds(pl.multiple_of((2 * k + 1 - side_ref[0]) * size, 32), size)
        keep_ref[at, :] = total[mine, :]
        away_ref[at, :] = total[others, :].astype(BF16)


def normed_back(rows_ref, dz_ref, dxa_ref, dxb_ref, wz_ref, wx_ref, out_ref):
    n_a = dxa_ref.shape[1]
    total = mm(dz_ref[...], wz_ref[...], NT)
    total = total + mm(dxa_ref[...], wx_ref[:, :n_a], NT) + mm(dxb_ref[...], wx_ref[:, n_a:], NT)
    out_ref[...] = total.astype(BF16)


def params():
    return pltpu.CompilerParams(dimension_semantics=("arbitrary",), vmem_limit_bytes=VMEM_LIMIT)


SMALL_COST = pl.CostEstimate(flops=1000, bytes_accessed=1000, transcendentals=0)


def rows_spec(block, width, column=0):
    return pl.BlockSpec((block, width), lambda i: (i, column))


def whole_spec(shape, column=0):
    return pl.BlockSpec(shape, lambda i: (0, column))


def local(
    tokens,
    cotangent,
    lengths,
    norm_gain,
    w_zx,
    w_bc,
    w_dt,
    conv_x,
    conv_x_bias,
    conv_bc,
    conv_bc_bias,
    dt_bias,
    a_log,
    d_skip,
    gate_gain,
    w_out,
):
    n_t = lax.axis_size("tensor")
    n_dp = lax.axis_size("dp")
    me_t = lax.axis_index("tensor")
    me_dp = lax.axis_index("dp")
    own_rows, depth = tokens.shape
    group = own_rows * n_t
    chunks = group // Q
    heads = dt_bias.shape[0]
    inner = heads * WIDTH
    inner_total = inner * n_t
    shard = w_zx.shape[1]
    pairs = [(i, n_t - 1 - i) for i in range(n_t)]

    def swap(v):
        return lax.ppermute(v, "tensor", pairs)

    def in_order(mine, other, axis=0):
        low = jnp.where(me_t == 0, mine, other)
        high = jnp.where(me_t == 0, other, mine)
        return jnp.concatenate([low, high], axis=axis)

    def sum_dp(v):
        step = 1
        while step < n_dp:
            v = v + lax.ppermute(v, "dp", [(i, i ^ step) for i in range(n_dp)])
            step *= 2
        return v

    def after(value, *others):
        return lax.optimization_barrier((value, *others))[0]

    ring = 4
    plane = max(n_dp // (2 * ring), 1)
    around = [(i, (i + 2 * plane) % n_dp) for i in range(n_dp)]
    across = [(i, i ^ 2) for i in range(n_dp)]
    beside = [(i, i ^ 1) for i in range(n_dp)]

    def send(v, way):
        return lax.ppermute(v, "dp", way)

    two_level = n_dp == 16 and shard % 32 == 0
    same_core = [[i for i in range(n_dp) if i % 2 == core] for core in range(2)]
    side = me_dp % 2

    def gather(v, axis):
        if not two_level:
            return [lax.all_gather(v, "dp", axis=axis, tiled=True)]
        own = lax.all_gather(v, "dp", axis=axis, tiled=True, axis_index_groups=same_core)
        return [own]

    half = n_dp // 2
    own_order = [2 * k + side for k in range(half)]
    away_order = [2 * k + 1 - side for k in range(half)]
    places = (own_order + away_order) if two_level else [0 * side]
    offsets = (jnp.stack(places) * shard).astype(jnp.int32)
    turn_offsets = (jnp.stack(away_order + own_order) * shard).astype(jnp.int32)

    ends = jnp.cumsum(lengths[0]).astype(jnp.int32)
    live = (lax.iota(jnp.int32, group) < ends[-1]).astype(F32)
    live_own = lax.dynamic_slice_in_dim(live, me_t * own_rows, own_rows, 0)
    me = me_t.astype(jnp.int32).reshape(1)

    span_p = conv_x_bias.shape[1]
    span_n = conv_bc_bias.shape[1]
    half_bc = w_bc.shape[1]
    bits = jnp.concatenate([norm_gain, conv_bc.reshape(-1), conv_bc_bias.reshape(-1)])
    bits = jnp.pad(bits, (0, LANES - bits.shape[0]))
    tiny = jnp.concatenate([w_bc.reshape(2 * half_bc, STATE), bits[None]], axis=0)
    other_tiny = swap(tiny)
    other_bc = other_tiny[: 2 * half_bc].reshape(w_bc.shape)
    both_bits = [bits, other_tiny[2 * half_bc]]
    at = norm_gain.shape[0]
    gain_pair = in_order(*[v[:at] for v in both_bits])[:, None]
    taps_bc = in_order(*[v[at : at + conv_bc.size].reshape(2, span_n, K) for v in both_bits], axis=1)
    at += conv_bc.size
    bias_bc = in_order(*[v[at : at + 2 * span_n].reshape(2, span_n, 1) for v in both_bits], axis=1)
    spare_bc = jnp.concatenate([taps_bc, bias_bc], axis=2).reshape(4 * span_n, K + 1)
    spare_x = [conv_x.reshape(shard, K), conv_x_bias.reshape(shard, 1), gate_gain.reshape(shard, 1), gain_pair]
    bc_pair = in_order(w_bc, other_bc, axis=1)
    packed = jnp.concatenate(
        [w_zx[1], bc_pair[0], bc_pair[1], w_dt, *spare_x, jnp.zeros((shard, 8 - K - 3), BF16)]
        + [jnp.pad(spare_bc, ((0, shard - 4 * span_n), (0, LANES - heads - 8 - K - 1)))],
        axis=1,
    )
    gain_pair = gain_pair.astype(F32)
    where = after(lax.iota(jnp.int32, depth), packed)
    home, inside = where // shard, where % shard
    place_x = (inside // span_p) * WIDTH + home * span_p + inside % span_p
    half_n = 2 * span_n
    place_bc = (inside // half_n) * STATE + home * half_n + inside % half_n
    place = jnp.concatenate([jnp.broadcast_to(v[:, None], (depth, LANES)) for v in (place_x, place_bc)], axis=1)
    par = jnp.concatenate([dt_bias[None], a_log[None], jnp.zeros((6, heads), F32)], axis=0)
    par = jnp.concatenate([par, jnp.zeros((8, LANES - heads), F32)], axis=1)
    skip = jnp.repeat(d_skip, WIDTH)[None]
    members = lax.iota(jnp.int32, inner)[:, None] // WIDTH
    sel = (members == lax.iota(jnp.int32, LANES)[None, :]).astype(BF16)
    smem = pl.BlockSpec(memory_space=pltpu.SMEM)
    vmem = pl.BlockSpec(memory_space=pltpu.VMEM)
    hbm = pl.BlockSpec(memory_space=pl.ANY)
    n_small = 2 * STATE + LANES
    n_conv = inner + 2 * STATE
    w_rest = jnp.stack([w_zx[0], w_out.T])

    def turn(other_tokens):
        return pl.pallas_call(
            turn_rows,
            in_specs=[smem, smem, vmem, vmem],
            out_specs=vmem,
            out_shape=jax.ShapeDtypeStruct((depth, group), BF16),
            scratch_shapes=[pltpu.VMEM((depth, group), BF16)],
            compiler_params=pltpu.CompilerParams(vmem_limit_bytes=VMEM_LIMIT),
            cost_estimate=SMALL_COST,
            name="turn_rows",
        )(turn_offsets, me, tokens, other_tokens)

    other_tokens = swap(after(tokens, other_tiny))
    wx_parts = gather(packed, 0)
    rest_parts = gather(after(w_rest, wx_parts[0]), 1)
    wz_parts, wo_parts = [rest_parts[0][0]], [rest_parts[0][1]]
    if two_level:
        wx_parts.append(send(wx_parts[0], beside))
        wz_parts.append(send(wz_parts[0], beside))
        wo_parts.append(send(after(wo_parts[0], wz_parts[0]), beside))
    other_cot = swap(after(cotangent, other_tokens))
    count = len(wx_parts)
    sems = pltpu.SemaphoreType.DMA((len(places),))
    tok_own = tokens.astype(F32)
    inv_tok = lax.rsqrt(jnp.mean(tok_own * tok_own, axis=1, keepdims=True) + EPSILON)

    block = own_rows
    steps = group // block
    x_raw, small, normed, taps, gain_in, wx_all = pl.pallas_call(
        partial(project, count, heads),
        grid=(steps,),
        in_specs=[
            smem,
            smem,
            whole_spec((block, depth)),
            whole_spec((block, depth)),
            whole_spec((depth, 2 * LANES)),
        ]
        + [hbm] * count,
        out_specs=[
            rows_spec(block, inner),
            rows_spec(block, n_small),
            rows_spec(block, depth),
            whole_spec((8, n_conv)),
            whole_spec((8, depth)),
            hbm,
        ],
        out_shape=[
            jax.ShapeDtypeStruct((group, inner), BF16),
            jax.ShapeDtypeStruct((group, n_small), F32),
            jax.ShapeDtypeStruct((group, depth), BF16),
            jax.ShapeDtypeStruct((8, n_conv), F32),
            jax.ShapeDtypeStruct((8, depth), F32),
            jax.ShapeDtypeStruct((depth, inner + n_small), BF16),
        ],
        scratch_shapes=[pltpu.VMEM((depth, inner + n_small), BF16), sems, pltpu.SemaphoreType.DMA],
        compiler_params=params(),
        cost_estimate=SMALL_COST,
        name="project",
    )(offsets, me, tokens, other_tokens, place, *wx_parts)
    xc, pre, bc, y_all, states = pl.pallas_call(
        partial(scan_forward, heads),
        grid=(chunks,),
        in_specs=[
            smem,
            rows_spec(Q, inner),
            rows_spec(Q, n_small),
            whole_spec((8, n_conv)),
            whole_spec((8, LANES)),
            whole_spec((1, inner)),
        ],
        out_specs=[
            rows_spec(Q, inner),
            rows_spec(Q, n_conv),
            rows_spec(Q, 2 * STATE),
            rows_spec(Q, inner),
            pl.BlockSpec((1, STATE, inner), lambda i: (i, 0, 0)),
        ],
        out_shape=[
            jax.ShapeDtypeStruct((group, inner), BF16),
            jax.ShapeDtypeStruct((group, n_conv), BF16),
            jax.ShapeDtypeStruct((group, 2 * STATE), BF16),
            jax.ShapeDtypeStruct((group, inner), BF16),
            jax.ShapeDtypeStruct((chunks, STATE, inner), BF16),
        ],
        scratch_shapes=[pltpu.VMEM((n_conv // LANES, Q + 8, LANES), F32), pltpu.VMEM((STATE, inner), F32)],
        compiler_params=params(),
        cost_estimate=SMALL_COST,
        name="scan_forward",
    )(ends, x_raw, small, taps, par, skip)

    cot_all = in_order(cotangent, other_cot)
    if two_level:
        turned = turn(after(other_tokens, y_all))
        normed, turned, cot_all = lax.optimization_barrier((normed, turned, after(cot_all, y_all)))
    tile = 512
    whole_w = pltpu.VMEM((depth, inner), BF16)
    whole_shape = jax.ShapeDtypeStruct((depth, inner), BF16)
    columns = lambda rows, shift=0: pl.BlockSpec((rows, tile), lambda j: (0, j + shift))
    fixed = lambda shape: pl.BlockSpec(shape, lambda j: (0, 0))
    tiles = inner // tile
    z_all, gg, sq, wz_all = pl.pallas_call(
        partial(gate_forward, count),
        grid=(tiles,),
        in_specs=[smem, fixed((group, depth)), columns(group), columns(8)] + [hbm] * count,
        out_specs=[columns(group), columns(group), fixed((8, group)), hbm],
        out_shape=[
            jax.ShapeDtypeStruct((group, inner), BF16),
            jax.ShapeDtypeStruct((group, inner), BF16),
            jax.ShapeDtypeStruct((8, group), F32),
            whole_shape,
        ],
        scratch_shapes=[pltpu.VMEM((group, LANES), F32), whole_w, sems, pltpu.SemaphoreType.DMA],
        compiler_params=params(),
        cost_estimate=SMALL_COST,
        name="gate_forward",
    )(offsets, normed, y_all, taps, *wz_parts)
    sq_got = swap(sq)

    u_own, u_send, prod, wo_all = pl.pallas_call(
        partial(branch, count),
        grid=(depth // tile,),
        in_specs=[
            smem,
            smem,
            smem,
            fixed((group, inner)),
            columns(own_rows),
            columns(own_rows),
        ]
        + [hbm] * count,
        out_specs=[columns(own_rows), columns(own_rows), fixed((8, group)), hbm],
        out_shape=[
            jax.ShapeDtypeStruct((own_rows, depth), BF16),
            jax.ShapeDtypeStruct((own_rows, depth), BF16),
            jax.ShapeDtypeStruct((8, group), F32),
            whole_shape,
        ],
        scratch_shapes=[pltpu.VMEM((group, LANES), F32), whole_w, sems, pltpu.SemaphoreType.DMA],
        compiler_params=params(),
        cost_estimate=SMALL_COST,
        name="branch",
    )(offsets, me, ends, gg, cotangent, other_cot, *wo_parts)
    prod_got = swap(prod)
    sq_all = sq + after(sq_got, prod)
    inv_gate8 = lax.rsqrt(sq_all / inner_total + EPSILON)
    inv_gate = inv_gate8[0]
    d_branch = (cot_all.astype(F32) * (live * inv_gate)[:, None]).astype(BF16)
    g_out = lax.dot_general(d_branch, gg, TN, preferred_element_type=F32).astype(BF16)
    grad_out = lax.psum_scatter(g_out, "dp", scatter_dimension=0, tiled=True)
    prod_got = after(prod_got, g_out)
    u_recv = swap(after(u_send, g_out))
    inv_own = lax.dynamic_slice_in_dim(inv_gate, me_t * own_rows, own_rows, 0)
    out_branch = (u_own.astype(F32) + u_recv.astype(F32)) * (inv_own * live_own)[:, None]
    layer_out = (tokens.astype(F32) + out_branch).astype(BF16)

    prod_all = prod + prod_got
    coef8 = inv_gate8 * inv_gate8 * inv_gate8 * (prod_all / inner_total)
    dy, dz, gain_acc = pl.pallas_call(
        gate_backward,
        grid=(tiles,),
        in_specs=[
            smem,
            smem,
            fixed((own_rows, depth)),
            fixed((own_rows, depth)),
            columns(depth),
            columns(group),
            columns(group),
            fixed((8, group)),
            fixed((8, group)),
            columns(8),
        ],
        out_specs=[columns(group), columns(group), columns(8)],
        out_shape=[
            jax.ShapeDtypeStruct((group, inner), BF16),
            jax.ShapeDtypeStruct((group, inner), BF16),
            jax.ShapeDtypeStruct((8, inner), F32),
        ],
        scratch_shapes=[pltpu.VMEM((group, LANES), F32), pltpu.VMEM((group, LANES), F32)],
        compiler_params=params(),
        cost_estimate=SMALL_COST,
        name="gate_backward",
    )(me, ends, cotangent, other_cot, wo_all, y_all, z_all, inv_gate8, coef8, taps)
    dot = partial(lax.dot_general, preferred_element_type=F32)
    front = depth // 2

    def half_rows(which):
        return pl.BlockSpec((front, group), lambda j: (which, 0))

    def column_tiles(rows, width, shift=0):
        return pl.BlockSpec((rows, width), lambda j: (0, j + shift))

    def away_of(d, width):
        return pl.pallas_call(
            grad_away,
            grid=(d.shape[1] // width,),
            in_specs=[half_rows(0), column_tiles(group, width)],
            out_specs=column_tiles(front, width),
            out_shape=jax.ShapeDtypeStruct((front, d.shape[1]), BF16),
            compiler_params=params(),
            cost_estimate=SMALL_COST,
            name="grad_away",
        )(turned, d)

    def keep_of(d, width, got, shift, held):
        return pl.pallas_call(
            grad_keep,
            grid=(d.shape[1] // width,),
            in_specs=[half_rows(1), column_tiles(group, width), column_tiles(front, width)] + [hbm] * len(held),
            out_specs=column_tiles(front, width, shift),
            out_shape=jax.ShapeDtypeStruct((front, inner + n_small), BF16),
            input_output_aliases={3: 0} if held else {},
            compiler_params=params(),
            cost_estimate=SMALL_COST,
            name="grad_keep",
        )(turned, d, got, *held)

    def split_of(d, width, got):
        outs = column_tiles(front // 2, width)
        return pl.pallas_call(
            grad_split,
            grid=(d.shape[1] // width,),
            in_specs=[smem, half_rows(1), column_tiles(group, width), column_tiles(front, width)],
            out_specs=[outs, outs],
            out_shape=[
                jax.ShapeDtypeStruct((front // 2, d.shape[1]), BF16),
                jax.ShapeDtypeStruct((front // 2, d.shape[1]), F32),
            ],
            scratch_shapes=[pltpu.VMEM((front, width), F32)],
            compiler_params=params(),
            cost_estimate=SMALL_COST,
            name="grad_split",
        )(((me_dp // 2) % 2).astype(jnp.int32).reshape(1), turned, d, got)

    if two_level:
        g_send = away_of(dz, tile)
        z_got = send(g_send, beside)
        dy = after(dy, g_send)
    else:
        grad_z = lax.psum_scatter(dot(normed, dz, TN).astype(BF16), "dp", scatter_dimension=0, tiled=True)

    halo_spec = pl.BlockSpec((n_conv // LANES, 8, LANES), lambda i: (0, 0, 0))

    def backward(top, number, carry):
        back = lambda width: pl.BlockSpec((Q, width), lambda i: (top - i, 0))
        operands = [ends, dy, xc, pre, x_raw, small, bc, states, taps, par, skip, sel, *carry]
        acc_spec = whole_spec((8 * (K + 2), n_conv))
        carry_shapes = [
            jax.ShapeDtypeStruct((STATE, inner), F32),
            jax.ShapeDtypeStruct((n_conv // LANES, 8, LANES), F32),
        ]
        carry_specs = []
        if carry:
            carry_specs = [whole_spec((STATE, inner)), halo_spec, acc_spec, whole_spec((16, LANES))]
            carry_specs += [whole_spec((8, inner)), hbm, hbm]
        return pl.pallas_call(
            partial(scan_backward, heads, chunks, top),
            grid=(number,),
            in_specs=[
                smem,
                back(inner),
                back(inner),
                back(n_conv),
                back(inner),
                back(n_small),
                back(2 * STATE),
                pl.BlockSpec((1, STATE, inner), lambda i: (top - i, 0, 0)),
                whole_spec((8, n_conv)),
                whole_spec((8, LANES)),
                whole_spec((1, inner)),
                whole_spec((inner, LANES)),
            ]
            + carry_specs,
            out_specs=[
                back(n_a),
                back(n_b),
                *([whole_spec((8, n_conv))] if carry else []),
                acc_spec,
                whole_spec((16, LANES)),
                *([] if carry else [whole_spec((STATE, inner)), halo_spec]),
            ],
            out_shape=[
                jax.ShapeDtypeStruct((group, n_a), BF16),
                jax.ShapeDtypeStruct((group, n_b), BF16),
                *([jax.ShapeDtypeStruct((8, n_conv), F32)] if carry else []),
                jax.ShapeDtypeStruct((8 * (K + 2), n_conv), F32),
                jax.ShapeDtypeStruct((16, LANES), F32),
                *([] if carry else carry_shapes),
            ],
            scratch_shapes=[
                pltpu.VMEM((STATE, inner), F32),
                pltpu.VMEM((n_conv // LANES, Q + 8, LANES), F32),
                pltpu.VMEM((Q, inner), BF16),
                pltpu.VMEM((Q, inner), BF16),
                pltpu.VMEM((Q, inner), BF16),
                pltpu.VMEM((Q, inner), BF16),
                pltpu.VMEM((Q, inner), BF16),
                pltpu.VMEM((Q, inner), BF16),
                pltpu.VMEM((STATE, inner), BF16),
                pltpu.VMEM((8, inner), F32),
            ],
            input_output_aliases={len(operands) - 2: 0, len(operands) - 1: 1} if carry else {},
            compiler_params=params(),
        cost_estimate=SMALL_COST,
            name="scan_backward",
        )(*operands)

    half_chunks = chunks // 2
    n_b = (inner + n_small) // 3
    n_a = inner + n_small - n_b
    dxa, dxb, acc, hacc, d_state, halo = backward(chunks - 1, chunks - half_chunks, ())
    if two_level:
        z_away, z_keep = split_of(dz, tile, after(z_got, dxa))
        z_got = send(z_away, across)
        d_state = after(d_state, z_away)
    dxa, dxb, vector = backward(half_chunks - 1, half_chunks, (d_state, halo, acc, hacc, gain_acc, dxa, dxb))[:3]
    dxa = after(dxa, u_recv)
    lanes_shared = lax.iota(jnp.int32, n_conv)[None, :] >= inner
    bits_of = lambda turn: [(i, i ^ (1 << turn)) for i in range(n_dp)]
    level = me_dp // (2 * plane)

    def z_part(turn):
        at = ((level - turn + ring) % ring) * shard
        return lax.dynamic_slice_in_dim(z_keep, at, shard, 0) + lax.dynamic_slice_in_dim(z_got, at, shard, 0).astype(F32)

    if two_level:
        a_send = away_of(dxa, n_b)
        a_got = send(a_send, beside)
        b_send = away_of(after(dxb, a_send), n_b)
        b_got = send(b_send, beside)
        shared_got = swap(after(vector, a_send))
        z_got, b_send, shared_got, grad_out = lax.optimization_barrier((z_got, b_send, shared_got, grad_out))
        z_out = z_part(1).astype(BF16)
        z_came = send(z_out, around)
        vector = vector + jnp.where(lanes_shared, shared_got, 0.0)
        a_got, dxa, _, vector = lax.optimization_barrier((a_got, dxa, z_out, vector))
        x_keep = keep_of(dxa, n_b, a_got, 0, [])
        x_keep = keep_of(dxb, n_b, after(b_got, x_keep), 2, [x_keep])
        grad_x = lax.psum_scatter(
            x_keep, "dp", scatter_dimension=0, tiled=True, axis_index_groups=same_core
        )
        dz = after(dz, x_keep)
        vector_got = send(vector, bits_of(0))
    else:
        dx = jnp.concatenate([dxa, dxb], axis=1)
        grad_x = lax.psum_scatter(dot(normed, dx, TN).astype(BF16), "dp", scatter_dimension=0, tiled=True)

    def back_rows(which, dz):
        pick = lambda width: pl.BlockSpec((own_rows, width), lambda j, rows: (rows[0], 0))
        return pl.pallas_call(
            normed_back,
            grid_spec=pltpu.PrefetchScalarGridSpec(
                num_scalar_prefetch=1,
                grid=(depth // tile,),
                in_specs=[
                    pick(inner),
                    pick(n_a),
                    pick(n_b),
                    pl.BlockSpec((tile, inner), lambda j, rows: (j, 0)),
                    pl.BlockSpec((tile, inner + n_small), lambda j, rows: (j, 0)),
                ],
                out_specs=pl.BlockSpec((own_rows, tile), lambda j, rows: (0, j)),
            ),
            out_shape=jax.ShapeDtypeStruct((own_rows, depth), BF16),
            compiler_params=params(),
            cost_estimate=SMALL_COST,
            name="normed_back",
        )(which, dz, dxa, dxb, wz_all, wx_all)

    dn_send = back_rows(n_t - 1 - me, dz)
    if two_level:
        w_sum = lambda w, g: jnp.sum(w.astype(F32) * g, axis=1)
        z_came, vector_got, dn_send = lax.optimization_barrier((z_came, vector_got, dn_send))
        dn_got = swap(dn_send)
        vector = vector + vector_got
        z_out = (z_part(2) + z_came.astype(F32)).astype(BF16)
        z_came, vector_got = send(z_out, around), send(vector, bits_of(1))
        dn_own = back_rows(me, after(dz, vector, z_out))
        z_came, vector_got, dn_own = lax.optimization_barrier((z_came, vector_got, dn_own))
        vector = vector + vector_got
        z_out = (z_part(3) + z_came.astype(F32)).astype(BF16)
        z_came, vector_got = send(z_out, around), send(vector, bits_of(2))
        grad_out, layer_out, z_came, vector_got = lax.optimization_barrier(
            (grad_out.astype(F32).T, layer_out, z_came, vector_got)
        )
        vector = vector + vector_got
        vector_got = send(vector, bits_of(3))
        grad_z = (z_part(ring) + z_came.astype(F32)) * gain_pair
        in_part = w_sum(w_zx[0], grad_z)
        vector_got, grad_z, in_part = lax.optimization_barrier((vector_got, grad_z, in_part))
        vector = vector + vector_got
    else:
        vector = sum_dp(vector + jnp.where(lanes_shared, swap(vector), 0.0))
        dn_own = back_rows(me, dz)
        dn_got = swap(dn_send)
        grad_out = grad_out.astype(F32).T
        grad_z, grad_x = grad_z.astype(F32), grad_x.astype(F32)
        in_part = jnp.sum(w_zx[0].astype(F32) * grad_z, axis=1)

    me_all = me_dp * n_t + me_t
    bc_sum = vector[: K + 1, inner:].reshape(K + 1, 2, STATE)
    bc_sum = lax.dynamic_slice_in_dim(bc_sum, me_all * span_n, span_n, 2)
    grad_bc_taps = bc_sum[:K].transpose(1, 2, 0).reshape(conv_bc.shape)
    grad_bc_bias = bc_sum[K]
    x_sum = vector[: K + 3, :inner].reshape(K + 3, heads, WIDTH)
    grad_skip = x_sum[K + 1].sum(axis=1)
    x_sum = lax.dynamic_slice_in_dim(x_sum, me_dp * span_p, span_p, 2)
    grad_x_taps = x_sum[:K].transpose(1, 2, 0).reshape(conv_x.shape)
    grad_x_bias = x_sum[K]
    grad_gate = x_sum[K + 2]
    grad_dt_bias = vector[K + 3, :heads]
    grad_a_log = vector[K + 3, LANES : LANES + heads]

    dn = (dn_own.astype(F32) + dn_got.astype(F32)) * gain_in[0:1, :]
    grad_tokens = (
        cotangent.astype(F32)
        + inv_tok * dn
        - tok_own * inv_tok * inv_tok * inv_tok * jnp.mean(dn * tok_own, axis=1, keepdims=True)
    )

    if two_level:
        small_outs = (grad_bc_taps, grad_bc_bias, grad_skip, grad_x_taps, grad_x_bias, grad_gate, grad_dt_bias, grad_a_log)
        grad_tokens, *small_outs, grad_x = lax.optimization_barrier((grad_tokens, *small_outs, grad_x))
        grad_bc_taps, grad_bc_bias, grad_skip, grad_x_taps, grad_x_bias, grad_gate, grad_dt_bias, grad_a_log = small_outs
        grad_x = grad_x.astype(F32) * gain_pair
    in_part = in_part + jnp.sum(packed.astype(F32) * grad_x, axis=1)
    at = inner
    bc_part = jnp.concatenate([grad_x[:, at : at + 2 * STATE], jnp.broadcast_to(in_part[:, None], (shard, LANES))], axis=1)
    grad_zx = jnp.stack([grad_z, grad_x[:, :inner]])
    grad_dt = grad_x[:, at + 2 * STATE : at + 2 * STATE + heads]
    half = half_bc
    bc_own = lax.dynamic_slice_in_dim(bc_part, me_t * half, half, 0)
    bc_send = lax.dynamic_slice_in_dim(bc_part, (n_t - 1 - me_t) * half, half, 0)
    bc_total = bc_own + swap(bc_send)
    own_gain = norm_gain.astype(F32)
    grad_bc = bc_total[:, : 2 * STATE].reshape(half, 2, STATE).transpose(1, 0, 2)
    grad_in = bc_total[:, 2 * STATE] / own_gain
    return (
        layer_out,
        grad_tokens,
        grad_in,
        grad_zx,
        grad_bc,
        grad_dt,
        grad_x_taps,
        grad_x_bias,
        grad_bc_taps,
        grad_bc_bias,
        grad_dt_bias,
        grad_a_log,
        grad_skip,
        grad_gate,
        grad_out,
    )


def solution(mesh):
    both = ("dp", "tensor")
    in_specs = (
        P(both, None),
        P(both, None),
        P("dp", None),
        P(both),
        P(None, "dp", "tensor"),
        P(None, both, None),
        P("dp", "tensor"),
        P("tensor", "dp"),
        P("tensor", "dp"),
        P(None, both),
        P(None, both),
        P("tensor"),
        P("tensor"),
        P("tensor"),
        P("tensor", "dp"),
        P("tensor", "dp"),
    )
    out_specs = (
        P(both, None),
        P(both, None),
        P(both),
        P(None, "dp", "tensor"),
        P(None, both, None),
        P("dp", "tensor"),
        P("tensor", "dp"),
        P("tensor", "dp"),
        P(None, both),
        P(None, both),
        P("tensor"),
        P("tensor"),
        P("tensor"),
        P("tensor", "dp"),
        P("tensor", "dp"),
    )
    return jax.shard_map(local, mesh=mesh, in_specs=in_specs, out_specs=out_specs, check_vma=False)
```

```python
from functools import partial

import jax
import jax.numpy as jnp
from jax import lax
from jax.experimental import pallas as pl
from jax.experimental.pallas import tpu as pltpu
from jax.sharding import PartitionSpec as P

EPSILON = 1e-05
HIGHEST = lax.Precision.HIGHEST
K = 4
WIDTH = 64
STATE = 128
Q = 128
LANES = 128
LOG2E = 1.4426950408889634
VMEM_LIMIT = 60 * 1024 * 1024
F32 = jnp.float32
BF16 = jnp.bfloat16

NN = (((1,), (0,)), ((), ()))
NT = (((1,), (1,)), ((), ()))
TN = (((0,), (0,)), ((), ()))


def mm(a, b, dims=NN):
    return lax.dot_general(a, b, dims, preferred_element_type=F32)


def mm_exact(a, b, dims=NN):
    return lax.dot_general(a, b, dims, preferred_element_type=F32, precision=HIGHEST)


def iota(shape, dim):
    return lax.broadcasted_iota(jnp.int32, shape, dim)


def segment_of(rows, ends_ref, count):
    total = (rows >= ends_ref[0]).astype(jnp.int32)
    for j in range(1, count):
        total = total + (rows >= ends_ref[j]).astype(jnp.int32)
    return total


def scalar_segment(row, ends_ref, count):
    total = jnp.where(row >= ends_ref[0], 1, 0)
    for j in range(1, count):
        total = total + jnp.where(row >= ends_ref[j], 1, 0)
    return total


def sigmoid(v):
    return 0.5 * jnp.tanh(0.5 * v) + 0.5


def softplus(v):
    return jnp.maximum(v, 0.0) + jnp.log1p(jnp.exp(-jnp.abs(v)))


def chunk_masks(chunk, ends_ref, count):
    base = chunk * Q
    rows = iota((Q, Q), 0) + base
    cols = iota((Q, Q), 1) + base
    row_ids = segment_of(rows, ends_ref, count)
    col_ids = segment_of(cols, ends_ref, count)
    same = row_ids == col_ids
    before_id = jnp.where(chunk == 0, -1, scalar_segment(base - 1, ends_ref, count))
    final_id = scalar_segment(base + Q - 1, ends_ref, count)
    carry = (row_ids == before_id).astype(F32)
    last = (row_ids == final_id).astype(F32)
    passing = jnp.where(before_id == final_id, 1.0, 0.0).astype(F32)
    return rows, cols, row_ids, same, carry, last, passing


def decays(dt_raw, par_ref):
    shifted = dt_raw + par_ref[0:1, :]
    step = softplus(shifted)
    decay_rate = jnp.exp(par_ref[1:2, :])
    return shifted, step, decay_rate


def pair_columns(values, pair, first):
    left = jnp.broadcast_to(values[:, 2 * pair : 2 * pair + 1], (Q, LANES))
    right = jnp.broadcast_to(values[:, 2 * pair + 1 : 2 * pair + 2], (Q, LANES))
    return left, right, jnp.where(first, left, right)


def scan_forward(
    heads, ends_ref, xr_ref, small_ref, taps_ref, par_ref, skip_ref,
    xc_ref, pre_ref, bc_ref, y_ref, st_ref, buf, state,
):
    count = ends_ref.shape[0]
    inner = heads * WIDTH
    chunk = pl.program_id(0)

    @pl.when(chunk == 0)
    def _():
        buf[:, 0:8, :] = jnp.zeros((buf.shape[0], 8, LANES), F32)
        state[...] = jnp.zeros(state.shape, F32)

    rows, cols, row_ids, same, carry, last, passing = chunk_masks(chunk, ends_ref, count)
    causal = rows >= cols
    visible = same & causal
    lag_mask = [None]
    for lag in range(1, K):
        earlier = rows - lag
        keep = (segment_of(earlier, ends_ref, count) == row_ids) & (earlier >= 0)
        lag_mask.append(keep.astype(F32))

    small = small_ref[...]

    def convolve(lo, raw):
        span = slice(lo, lo + LANES)
        place = lo // LANES
        buf[place, 8 : 8 + Q, :] = raw
        pre = taps_ref[K : K + 1, span] + taps_ref[K - 1 : K, span] * raw
        for lag in range(1, K):
            pre = pre + taps_ref[K - 1 - lag : K - lag, span] * (
                buf[place, 8 - lag : 8 - lag + Q, :] * lag_mask[lag]
            )
        buf[place, 0:8, :] = raw[Q - 8 : Q, :]
        pre_ref[:, span] = pre.astype(BF16)
        return pre * sigmoid(pre)

    b_f = convolve(inner, small[:, :STATE]).astype(BF16).astype(F32)
    c_b = convolve(inner + STATE, small[:, STATE : 2 * STATE]).astype(BF16)
    b_b = b_f.astype(BF16)
    bc_ref[:, :STATE] = b_b
    bc_ref[:, STATE:] = c_b
    b_t = b_f.T.astype(BF16)

    _, step, decay_rate = decays(small[:, 2 * STATE :], par_ref)
    csum = mm_exact(causal.astype(F32), step * (-LOG2E * decay_rate))
    csum_t = csum.T
    scores = jnp.where(visible, mm(c_b, b_b, NT), 0.0)
    first = iota((Q, LANES), 1) < WIDTH
    first_row = iota((1, LANES), 1) < WIDTH

    wide = 2 * LANES
    for quad in range(0, inner, wide):
        block = slice(quad, quad + wide)
        held = state[:, block]
        held_b = held.astype(BF16)
        st_ref[0, :, block] = held_b
        carried = mm(c_b, held_b)
        weighted, kept = [], []
        for part in range(0, wide, LANES):
            lo = quad + part
            pair = lo // LANES
            span = slice(lo, lo + LANES)
            xc = convolve(lo, xr_ref[:, span].astype(F32)).astype(BF16)
            xc_ref[:, span] = xc
            xc = xc.astype(F32)
            left, right, both = pair_columns(csum, pair, first)
            _, _, step_pair = pair_columns(step, pair, first)
            mix = jnp.concatenate(
                [
                    (scores * jnp.exp2(jnp.minimum(left - csum_t[2 * pair : 2 * pair + 1, :], 0.0))).astype(BF16),
                    (scores * jnp.exp2(jnp.minimum(right - csum_t[2 * pair + 1 : 2 * pair + 2, :], 0.0))).astype(BF16),
                ],
                axis=1,
            )
            fed_b = (xc * step_pair).astype(BF16)
            zero = jnp.zeros((Q, LANES), BF16)
            stacked = jnp.concatenate([jnp.where(first, fed_b, zero), jnp.where(first, zero, fed_b)], axis=0)
            y = mm(mix, stacked) + carried[:, part : part + LANES] * (jnp.exp2(both) * carry)
            y_ref[:, span] = (y + skip_ref[:, span] * xc).astype(BF16)
            closing = both[Q - 1 : Q, :]
            weighted.append((fed_b.astype(F32) * (jnp.exp2(closing - both) * last)).astype(BF16))
            kept.append(jnp.exp2(closing) * passing)
        fresh = mm(b_t, jnp.concatenate(weighted, axis=1))
        state[:, block] = held * jnp.concatenate(kept, axis=1) + fresh


def scan_backward(
    heads, chunks, top, ends_ref, dy_ref, xc_ref, pre_ref, xr_ref, small_ref, bc_ref, st_ref, taps_ref, par_ref,
    skip_ref, sel_ref, *refs,
):
    later_call = top + 1 < chunks
    if later_call:
        state_in, halo_in, acc_in, hacc_in, gain_acc_ref = refs[:5]
        dxa_ref, dxb_ref, rows_ref, acc_ref, hacc_ref = refs[7:12]
        refs = refs[12:]
    else:
        dxa_ref, dxb_ref, acc_ref, hacc_ref, state_out, halo_out = refs[:6]
        refs = refs[6:]
    dstate, dpre, ab_hi, ab_lo, v_b, u_b, dyd, fedw, dst_b, through = refs
    count = ends_ref.shape[0]
    inner = heads * WIDTH
    total_rows = chunks * Q
    chunk = top - pl.program_id(0)

    @pl.when(pl.program_id(0) == 0)
    def _():
        if top + 1 < chunks:
            dpre[:, Q : Q + 8, :] = halo_in[...]
            dstate[...] = state_in[...]
            acc_ref[...] = acc_in[...]
            hacc_ref[...] = hacc_in[...]
        else:
            dpre[:, Q : Q + 8, :] = jnp.zeros((dpre.shape[0], 8, LANES), F32)
            dstate[...] = jnp.zeros(dstate.shape, F32)
            acc_ref[...] = jnp.zeros(acc_ref.shape, F32)
            hacc_ref[...] = jnp.zeros(hacc_ref.shape, F32)

    rows, cols, row_ids, same, carry, last, passing = chunk_masks(chunk, ends_ref, count)
    causal = rows >= cols
    visible = same & causal
    lag_mask = [None]
    for lag in range(1, K):
        later = rows + lag
        keep = (segment_of(later, ends_ref, count) == row_ids) & (later < total_rows)
        lag_mask.append(keep.astype(F32))

    small = small_ref[...]
    shifted, step, decay_rate = decays(small[:, 2 * STATE :], par_ref)
    csum = mm_exact(causal.astype(F32), step * (-LOG2E * decay_rate))
    csum_t = csum.T
    b_b = bc_ref[:, :STATE]
    c_b = bc_ref[:, STATE:]
    c_t = c_b.astype(F32).T.astype(BF16)
    scores = jnp.where(visible, mm(c_b, b_b, NT), 0.0)
    first = iota((Q, LANES), 1) < WIDTH

    n_a = dxa_ref.shape[1]

    def put(lo, values):
        if lo < n_a:
            dxa_ref[:, lo : lo + LANES] = values.astype(BF16)
        else:
            dxb_ref[:, lo - n_a : lo - n_a + LANES] = values.astype(BF16)

    def fold(values):
        return values.reshape(Q // 8, 8, values.shape[1]).sum(axis=0)

    def conv_back(lo, d_conv, raw):
        span = slice(lo, lo + LANES)
        pre = pre_ref[:, span].astype(F32)
        gate = sigmoid(pre)
        d_pre = d_conv * (gate * (1.0 + pre * (1.0 - gate)))
        place = lo // LANES
        dpre[place, 0:Q, :] = d_pre
        d_raw = taps_ref[K - 1 : K, span] * d_pre
        acc_ref[8 * (K - 1) : 8 * K, span] += fold(d_pre * raw)
        acc_ref[8 * K : 8 * K + 8, span] += fold(d_pre)
        for lag in range(1, K):
            moved = dpre[place, lag : lag + Q, :] * lag_mask[lag]
            d_raw = d_raw + taps_ref[K - 1 - lag : K - lag, span] * moved
            acc_ref[8 * (K - 1 - lag) : 8 * (K - lag), span] += fold(moved * raw)
        dpre[place, Q : Q + 8, :] = d_pre[0:8, :]
        put(lo, d_raw)

    d_scores = jnp.zeros((Q, Q), F32)
    wide = 2 * LANES
    for quad in range(0, inner, wide):
        block = slice(quad, quad + wide)
        held_b = st_ref[0, :, block]
        d_held = dstate[:, block]
        d_held_b = d_held.astype(BF16)
        dst_b[:, block] = d_held_b
        carried = mm(c_b, held_b)
        returned = mm(b_b, d_held_b)
        crossing = (d_held * held_b.astype(F32)).reshape(STATE // 8, 8, wide).sum(axis=0)
        grown_parts, kept_parts = [], []
        for part in range(0, wide, LANES):
            lo = quad + part
            pair = lo // LANES
            span = slice(lo, lo + LANES)
            xc = xc_ref[:, span].astype(F32)
            dy_b = dy_ref[:, span]
            dy = dy_b.astype(F32)
            left, right, both = pair_columns(csum, pair, first)
            _, _, step_pair = pair_columns(step, pair, first)
            fall_left = jnp.exp2(jnp.minimum(left - csum_t[2 * pair : 2 * pair + 1, :], 0.0))
            fall_right = jnp.exp2(jnp.minimum(right - csum_t[2 * pair + 1 : 2 * pair + 2, :], 0.0))
            mix = jnp.concatenate([(scores * fall_left).astype(BF16), (scores * fall_right).astype(BF16)], axis=1)
            fed_b = (xc * step_pair).astype(BF16)
            fed = fed_b.astype(F32)
            zero = jnp.zeros((Q, LANES), BF16)
            stacked = jnp.concatenate([jnp.where(first, fed_b, zero), jnp.where(first, zero, fed_b)], axis=0)
            grown = jnp.exp2(both) * carry
            y = mm(mix, stacked) + carried[:, part : part + LANES] * grown
            d_mix = mm(dy_b, stacked, NT)
            d_scores = d_scores + d_mix[:, :Q] * fall_left + d_mix[:, Q:] * fall_right
            d_fed2 = mm(mix, dy_b, TN)
            d_fed_in = jnp.where(first, d_fed2[:Q], d_fed2[Q:])
            closing = both[Q - 1 : Q, :]
            shrink = jnp.exp2(closing - both) * last
            d_fed_out = returned[:, part : part + LANES] * shrink
            d_fed = d_fed_in + d_fed_out
            straddle = dy * y - fed * d_fed_in
            hi = straddle.astype(BF16)
            ab_hi[:, span] = hi
            ab_lo[:, span] = (straddle - hi.astype(F32)).astype(BF16)
            v_b[:, span] = (fed * d_fed_out).astype(BF16)
            u_b[:, span] = (xc * d_fed).astype(BF16)
            fedw[:, span] = (fed * shrink).astype(BF16)
            grown_parts.append((dy * grown).astype(BF16))
            kept_parts.append(jnp.exp2(closing) * passing)
            acc_ref[8 * K + 8 : 8 * K + 16, span] += fold(dy * xc)
            d_conv = d_fed * step_pair + skip_ref[:, span] * dy
            conv_back(lo, d_conv, xr_ref[:, span].astype(F32))
        dy_grown = jnp.concatenate(grown_parts, axis=1)
        kept = jnp.concatenate(kept_parts, axis=1)
        dyd[:, block] = dy_grown
        through[:, block] = crossing * kept
        dstate[:, block] = d_held * kept + mm(c_t, dy_grown)

    d_scores_b = jnp.where(visible, d_scores, 0.0).astype(BF16)
    d_c = mm(dyd[...], st_ref[0], NT) + mm(d_scores_b, b_b)
    d_b = mm(fedw[...], dst_b[...], NT) + mm(d_scores_b, c_b, TN)
    conv_back(inner, d_b, small[:, :STATE])
    conv_back(inner + STATE, d_c, small[:, STATE : 2 * STATE])

    sel = sel_ref[...]
    red_ab = mm(ab_hi[...], sel) + mm(ab_lo[...], sel)
    red_v = mm(v_b[...], sel)
    red_u = mm(u_b[...], sel)
    thr = through[...]
    thr_hi = thr.astype(BF16)
    red_t = mm(thr_hi, sel) + mm((thr - thr_hi.astype(F32)).astype(BF16), sel)
    d_rate = (
        mm_exact((same & (cols >= rows)).astype(F32), red_ab)
        + mm_exact((same & (cols < rows)).astype(F32), red_v)
        + jnp.sum(red_t, axis=0, keepdims=True)
    )
    d_step = red_u - d_rate * decay_rate
    d_dt = d_step * sigmoid(shifted)
    put(inner + 2 * STATE, d_dt)
    hacc_ref[0:8, :] += fold(d_dt)
    hacc_ref[8:16, :] += fold(d_rate * (-decay_rate * step))
    if later_call:

        @pl.when(pl.program_id(0) == pl.num_programs(0) - 1)
        def _():
            rows_ref[...] = jnp.zeros(rows_ref.shape, F32)
            for k in range(K + 2):
                rows_ref[k : k + 1, :] = jnp.sum(acc_ref[8 * k : 8 * k + 8, :], axis=0, keepdims=True)
            rows_ref[K + 2 : K + 3, :inner] = jnp.sum(gain_acc_ref[...], axis=0, keepdims=True)
            for k in range(2):
                total = jnp.sum(hacc_ref[8 * k : 8 * k + 8, :], axis=0, keepdims=True)
                rows_ref[K + 3 : K + 4, k * LANES : (k + 1) * LANES] = total

    else:
        halo_out[...] = dpre[:, Q : Q + 8, :]
        state_out[...] = dstate[...]


def load_blocks(offsets_ref, parts, whole, sems):
    @pl.when(pl.program_id(0) == 0)
    def _():
        copies = []
        count = sems.shape[0]
        size = whole.shape[0] // count
        for part in parts:
            for j in range(part.shape[0] // size):
                k = len(copies)
                start = pl.multiple_of(offsets_ref[k], 32) if count > 1 else 0
                source = part.at[pl.ds(j * size, size), :]
                copies.append(pltpu.make_async_copy(source, whole.at[pl.ds(start, size), :], sems.at[k]))
        for copy in copies:
            copy.start()
        for copy in copies:
            copy.wait()


def turn_rows(offsets_ref, me_ref, own_ref, other_ref, out_ref, turned):
    depth = own_ref.shape[1]
    rows = own_ref.shape[0]
    for index, source in enumerate((own_ref, other_ref)):
        at = pl.multiple_of(jnp.where(index == 0, me_ref[0], 1 - me_ref[0]) * rows, LANES)
        for lo in range(0, rows, Q):
            tile = source[lo : lo + Q, :].astype(F32)
            scale = lax.rsqrt(jnp.mean(tile * tile, axis=1, keepdims=True) + EPSILON)
            tile = tile * scale
            for left in range(0, depth, LANES):
                turned[left : left + LANES, pl.ds(at + lo, Q)] = tile[:, left : left + LANES].T.astype(BF16)
    count = offsets_ref.shape[0]
    size = depth // count
    for k in range(count):
        start = pl.multiple_of(offsets_ref[k], 32)
        out_ref[k * size : (k + 1) * size, :] = turned[pl.ds(start, size), :]


def project(count, heads, offsets_ref, me_ref, own_ref, other_ref, place_ref, *refs):
    blocks, (x_ref, small_ref, normed_ref, taps_ref, gain_ref, w_out_ref, w_ref, sems, out_sem) = refs[:count], refs[count:]
    load_blocks(offsets_ref, blocks, w_ref, sems)
    keep = pltpu.make_async_copy(w_ref, w_out_ref, out_sem)
    depth, inner = w_ref.shape[0], x_ref.shape[1]
    tile = 512

    @pl.when(pl.program_id(0) == 0)
    def _():
        keep.start()
        spare = w_ref[:, inner + 2 * STATE :]
        turned = spare.astype(F32).T
        gain_ref[...] = jnp.broadcast_to(turned[heads + K + 2 : heads + K + 3, :], gain_ref.shape)
        few = turned[heads : heads + 16, :].astype(BF16)
        lanes = iota((depth, LANES), 1)
        for lo in range(0, inner + 2 * STATE, LANES):
            if lo < inner:
                wanted, row = place_ref[:, :LANES] == lanes + lo, 0
            else:
                wanted, row = place_ref[:, LANES:] == lanes + (lo - inner), 8
            moved = mm(few, jnp.where(wanted, 1.0, 0.0).astype(BF16))
            taps_ref[:, lo : lo + LANES] = moved[row : row + 8, :]

    rows = jnp.where(pl.program_id(0) == me_ref[0], own_ref[...], other_ref[...]).astype(F32)
    scale = lax.rsqrt(jnp.mean(rows * rows, axis=1, keepdims=True) + EPSILON)
    rows = (rows * scale * gain_ref[0:1, :]).astype(BF16)
    normed_ref[...] = rows
    for lo in range(0, inner, tile):
        x_ref[:, lo : lo + tile] = mm(rows, w_ref[:, lo : lo + tile]).astype(BF16)
    small_ref[...] = mm(rows, w_ref[:, inner:])

    @pl.when(pl.program_id(0) == pl.num_programs(0) - 1)
    def _():
        keep.wait()


def row_sums(lanes):
    return mm_exact(jnp.ones((8, LANES), F32), lanes, NT)


def spread_rows(values):
    pick = jnp.where(iota((8, LANES), 0) == 0, 1.0, 0.0).astype(F32)
    return mm_exact(values, pick, TN)


def gate_forward(normed_ref, w_ref, y_ref, gain_ref, z_ref, gg_ref, sq_ref, square):
    rows, width = z_ref.shape
    size = 512

    @pl.when(pl.program_id(0) == 0)
    def _():
        square[...] = jnp.zeros(square.shape, F32)

    for lo in range(0, rows, size):
        at = slice(lo, lo + size)
        z = mm(normed_ref[at, :], w_ref[...]).astype(BF16)
        z_ref[at, :] = z
        z = z.astype(F32)
        gated = y_ref[at, :].astype(F32) * (z * sigmoid(z))
        gg_ref[at, :] = (gated * gain_ref[K + 1 : K + 2, :]).astype(BF16)
        twice = gated * gated
        for part in range(0, width, LANES):
            square[at, :] += twice[:, part : part + LANES]

    @pl.when(pl.program_id(0) == pl.num_programs(0) - 1)
    def _():
        sq_ref[...] = row_sums(square[...])


def branch(me_ref, ends_ref, gg_ref, own_ref, other_ref, w_ref, mine_ref, away_ref, prod_ref, product):
    rows, width = mine_ref.shape
    size = 512

    @pl.when(pl.program_id(0) == 0)
    def _():
        product[...] = jnp.zeros(product.shape, F32)

    for index, (out_ref, cot_ref) in enumerate(((mine_ref, own_ref), (away_ref, other_ref))):
        first = jnp.where(index == 0, me_ref[0], 1 - me_ref[0]) * rows
        for lo in range(0, rows, size):
            at = pl.ds(pl.multiple_of(first + lo, size), size)
            u = mm(gg_ref[at, :], w_ref[...], NT)
            out_ref[lo : lo + size, :] = u.astype(BF16)
            term = u * cot_ref[lo : lo + size, :].astype(F32)
            for part in range(0, width, LANES):
                product[at, :] += term[:, part : part + LANES]

    @pl.when(pl.program_id(0) == pl.num_programs(0) - 1)
    def _():
        live = iota(product.shape, 0) < ends_ref[ends_ref.shape[0] - 1]
        prod_ref[...] = row_sums(jnp.where(live, product[...], 0.0))


def gate_backward(
    me_ref, ends_ref, own_ref, other_ref, w_ref, y_ref, z_ref, rg_ref, coef_ref, gain_ref,
    dy_ref, dz_ref, acc_ref, rg, coef,
):
    total, width = dy_ref.shape
    rows = own_ref.shape[0]
    size = 512

    @pl.when(pl.program_id(0) == 0)
    def _():
        live = iota(rg.shape, 0) < ends_ref[ends_ref.shape[0] - 1]
        rg[...] = spread_rows(rg_ref[...])
        coef[...] = spread_rows(coef_ref[...])
        rg[...] = jnp.where(live, rg[...], 0.0)

    gain = gain_ref[K + 1 : K + 2, :]
    sums = jnp.zeros((8, width), F32)
    for index, cot_ref in enumerate((own_ref, other_ref)):
        first = jnp.where(index == 0, me_ref[0], 1 - me_ref[0]) * rows
        for lo in range(0, rows, size):
            at = pl.ds(pl.multiple_of(first + lo, size), size)
            ds = mm(cot_ref[lo : lo + size, :], w_ref[...])
            z = z_ref[at, :].astype(F32)
            y = y_ref[at, :].astype(F32)
            scale = jnp.concatenate([rg[at, :]] * (width // LANES), axis=1)
            back = jnp.concatenate([coef[at, :]] * (width // LANES), axis=1)
            gate = sigmoid(z)
            silu = z * gate
            gated = y * silu
            d_normal = ds * scale
            sums = sums + (d_normal * gated).reshape(size // 8, 8, width).sum(axis=0)
            d_gated = d_normal * gain - gated * back
            dy_ref[at, :] = (d_gated * silu).astype(BF16)
            dz_ref[at, :] = (d_gated * y * (gate + silu * (1.0 - gate))).astype(BF16)
    acc_ref[...] = sums


def weight_grad(turned_ref, d_ref, away_ref, keep_ref):
    half = away_ref.shape[0]
    d = d_ref[...]
    away_ref[...] = mm(turned_ref[:half, :], d).astype(BF16)
    keep_ref[...] = mm(turned_ref[half:, :], d).astype(BF16)


def normed_back(rows_ref, dz_ref, dxa_ref, dxb_ref, wz_ref, wx_ref, out_ref):
    n_a = dxa_ref.shape[1]
    total = mm(dz_ref[...], wz_ref[...], NT)
    total = total + mm(dxa_ref[...], wx_ref[:, :n_a], NT) + mm(dxb_ref[...], wx_ref[:, n_a:], NT)
    out_ref[...] = total.astype(BF16)


def params():
    return pltpu.CompilerParams(dimension_semantics=("arbitrary",), vmem_limit_bytes=VMEM_LIMIT)


SMALL_COST = pl.CostEstimate(flops=1000, bytes_accessed=1000, transcendentals=0)


def rows_spec(block, width, column=0):
    return pl.BlockSpec((block, width), lambda i: (i, column))


def whole_spec(shape, column=0):
    return pl.BlockSpec(shape, lambda i: (0, column))


def local(
    tokens,
    cotangent,
    lengths,
    norm_gain,
    w_zx,
    w_bc,
    w_dt,
    conv_x,
    conv_x_bias,
    conv_bc,
    conv_bc_bias,
    dt_bias,
    a_log,
    d_skip,
    gate_gain,
    w_out,
):
    n_t = lax.axis_size("tensor")
    n_dp = lax.axis_size("dp")
    me_t = lax.axis_index("tensor")
    me_dp = lax.axis_index("dp")
    own_rows, depth = tokens.shape
    group = own_rows * n_t
    chunks = group // Q
    heads = dt_bias.shape[0]
    inner = heads * WIDTH
    inner_total = inner * n_t
    shard = w_zx.shape[1]
    pairs = [(i, n_t - 1 - i) for i in range(n_t)]

    def swap(v):
        return lax.ppermute(v, "tensor", pairs)

    def in_order(mine, other, axis=0):
        low = jnp.where(me_t == 0, mine, other)
        high = jnp.where(me_t == 0, other, mine)
        return jnp.concatenate([low, high], axis=axis)

    def sum_dp(v):
        step = 1
        while step < n_dp:
            v = v + lax.ppermute(v, "dp", [(i, i ^ step) for i in range(n_dp)])
            step *= 2
        return v

    def after(value, *others):
        return lax.optimization_barrier((value, *others))[0]

    ring = 4
    plane = n_dp // (2 * ring)

    around = [(i, (i + 2 * plane) % n_dp) for i in range(n_dp)]
    across = [(i, i ^ 2) for i in range(n_dp)]
    beside = [(i, i ^ 1) for i in range(n_dp)]

    def send(v, way):
        return lax.ppermute(v, "dp", way)

    by_hand = plane == 2 and shard % 32 == 0

    def whole(v):
        return [lax.all_gather(v, "dp", axis=0, tiled=True)]

    def block_offsets(count, size):
        if count == 1:
            return jnp.zeros((1,), jnp.int32)
        places = []
        for core in range(2):
            for side in range(2):
                for turn in range(ring):
                    level = (me_dp // (2 * plane) - turn + ring) % ring
                    places.append(level * (2 * plane) + ((me_dp % (2 * plane)) ^ (2 * side + core)))
        return jnp.stack(places).astype(jnp.int32) * size

    def relative_order():
        level, side, core = me_dp // 4, (me_dp // 2) % 2, me_dp % 2
        order = []
        for dc in (1, 0):
            for dy in (1, 0):
                for dz in range(1, ring + 1):
                    order.append(((level - dz + ring) % ring) * 4 + (side ^ dy) * 2 + (core ^ dc))
        return order

    def fold_beside(keep, got):
        half = keep.shape[0] // 2
        away = (keep[:half].astype(F32) + got[:half].astype(F32)).astype(BF16)
        return away, keep[half:].astype(F32) + got[half:].astype(F32)

    def ring_part(keep, got, came, turn):
        at = slice((turn - 1) * shard, turn * shard)
        part = keep[at] + got[at].astype(F32)
        if came is not None:
            part = part + came.astype(F32)
        return part if turn == ring else part.astype(BF16)

    ends = jnp.cumsum(lengths[0]).astype(jnp.int32)
    live = (lax.iota(jnp.int32, group) < ends[-1]).astype(F32)
    live_own = lax.dynamic_slice_in_dim(live, me_t * own_rows, own_rows, 0)
    me = me_t.astype(jnp.int32).reshape(1)

    span_p = conv_x_bias.shape[1]
    span_n = conv_bc_bias.shape[1]
    half_bc = w_bc.shape[1]
    bits = jnp.concatenate([norm_gain, conv_bc.reshape(-1), conv_bc_bias.reshape(-1)])
    bits = jnp.pad(bits, (0, LANES - bits.shape[0]))
    tiny = jnp.concatenate([w_bc.reshape(2 * half_bc, STATE), bits[None]], axis=0)
    other_tiny = swap(tiny)
    other_bc = other_tiny[: 2 * half_bc].reshape(w_bc.shape)
    both_bits = [bits, other_tiny[2 * half_bc]]
    at = norm_gain.shape[0]
    gain_pair = in_order(*[v[:at] for v in both_bits])[:, None]
    taps_bc = in_order(*[v[at : at + conv_bc.size].reshape(2, span_n, K) for v in both_bits], axis=1)
    at += conv_bc.size
    bias_bc = in_order(*[v[at : at + 2 * span_n].reshape(2, span_n, 1) for v in both_bits], axis=1)
    spare_bc = jnp.concatenate([taps_bc, bias_bc], axis=2).reshape(4 * span_n, K + 1)
    spare_x = [conv_x.reshape(shard, K), conv_x_bias.reshape(shard, 1), gate_gain.reshape(shard, 1), gain_pair]
    bc_pair = in_order(w_bc, other_bc, axis=1)
    packed = jnp.concatenate(
        [w_zx[1], bc_pair[0], bc_pair[1], w_dt, *spare_x, jnp.zeros((shard, 8 - K - 3), BF16)]
        + [jnp.pad(spare_bc, ((0, shard - 4 * span_n), (0, LANES - heads - 8 - K - 1)))],
        axis=1,
    )
    gain_pair = gain_pair.astype(F32)
    where = after(lax.iota(jnp.int32, depth), packed)
    home, inside = where // shard, where % shard
    place_x = (inside // span_p) * WIDTH + home * span_p + inside % span_p
    half_n = 2 * span_n
    place_bc = (inside // half_n) * STATE + home * half_n + inside % half_n
    place = jnp.concatenate([jnp.broadcast_to(v[:, None], (depth, LANES)) for v in (place_x, place_bc)], axis=1)
    par = jnp.concatenate([dt_bias[None], a_log[None], jnp.zeros((6, heads), F32)], axis=0)
    par = jnp.concatenate([par, jnp.zeros((8, LANES - heads), F32)], axis=1)
    skip = jnp.repeat(d_skip, WIDTH)[None]
    members = lax.iota(jnp.int32, inner)[:, None] // WIDTH
    sel = (members == lax.iota(jnp.int32, LANES)[None, :]).astype(BF16)
    smem = pl.BlockSpec(memory_space=pltpu.SMEM)
    vmem = pl.BlockSpec(memory_space=pltpu.VMEM)
    hbm = pl.BlockSpec(memory_space=pl.ANY)
    n_small = 2 * STATE + LANES
    n_conv = inner + 2 * STATE
    w_rest = jnp.concatenate([w_zx[0], w_out.T], axis=1)

    def turn(other_tokens):
        return pl.pallas_call(
            turn_rows,
            in_specs=[smem, smem, vmem, vmem],
            out_specs=vmem,
            out_shape=jax.ShapeDtypeStruct((depth, group), BF16),
            scratch_shapes=[pltpu.VMEM((depth, group), BF16)],
            compiler_params=pltpu.CompilerParams(vmem_limit_bytes=VMEM_LIMIT),
            cost_estimate=SMALL_COST,
            name="turn_rows",
        )((jnp.stack(relative_order()) * shard).astype(jnp.int32), me, tokens, other_tokens)

    if by_hand:
        line, other, line_c, other_c = [packed], [], [], []
        late = after(tokens, packed)
        pieces = [late[:176], late[176:352], late[352:]]
        arrived, constants = [], []
        for step in range(ring + 1):
            made = []
            if step < ring - 1:
                made.append((line, send(line[step], around)))
            if step < ring:
                made.append((other, send(line[step], across)))
                made.append((line_c, send(line[step], beside)))
            if step:
                made.append((other_c, send(other[step - 1], beside)))
            if 0 < step < ring:
                made.append((arrived, swap(pieces[step - 1])))
            if step == 0:
                made += [(constants, v) for v in (place, par, skip, sel)]
                made += [([], v) for v in pieces]
            if step == 2:
                zo_all = lax.all_gather(after(w_rest, line[2]), "dp", axis=0, tiled=True)
            fresh = lax.optimization_barrier(tuple(value for _, value in made))
            for (place_in, _), value in zip(made, fresh):
                place_in.append(value)
            if step == 0:
                pieces = fresh[-3:]
        other_tokens = jnp.concatenate(arrived, axis=0)
        other_cot = swap(after(cotangent, other_tokens))
        wx_blocks = line + other + line_c + other_c
        place, par, skip, sel = constants
    else:
        wx_blocks = whole(packed)
        zo_all = whole(w_rest)[0]
        other_tokens, other_cot = swap(tokens), swap(cotangent)
    count = len(wx_blocks)
    offsets = block_offsets(count, shard)
    sems = pltpu.SemaphoreType.DMA((count,))
    tok_own = tokens.astype(F32)
    inv_tok = lax.rsqrt(jnp.mean(tok_own * tok_own, axis=1, keepdims=True) + EPSILON)

    block = own_rows
    steps = group // block
    x_raw, small, normed, taps, gain_in, wx_all = pl.pallas_call(
        partial(project, count, heads),
        grid=(steps,),
        in_specs=[
            smem,
            smem,
            whole_spec((block, depth)),
            whole_spec((block, depth)),
            whole_spec((depth, 2 * LANES)),
        ]
        + [hbm] * count,
        out_specs=[
            rows_spec(block, inner),
            rows_spec(block, n_small),
            rows_spec(block, depth),
            whole_spec((8, n_conv)),
            whole_spec((8, depth)),
            hbm,
        ],
        out_shape=[
            jax.ShapeDtypeStruct((group, inner), BF16),
            jax.ShapeDtypeStruct((group, n_small), F32),
            jax.ShapeDtypeStruct((group, depth), BF16),
            jax.ShapeDtypeStruct((8, n_conv), F32),
            jax.ShapeDtypeStruct((8, depth), F32),
            jax.ShapeDtypeStruct((depth, inner + n_small), BF16),
        ],
        scratch_shapes=[pltpu.VMEM((depth, inner + n_small), BF16), sems, pltpu.SemaphoreType.DMA],
        compiler_params=params(),
        cost_estimate=SMALL_COST,
        name="project",
    )(offsets, me, tokens, other_tokens, place, *wx_blocks)
    xc, pre, bc, y_all, states = pl.pallas_call(
        partial(scan_forward, heads),
        grid=(chunks,),
        in_specs=[
            smem,
            rows_spec(Q, inner),
            rows_spec(Q, n_small),
            whole_spec((8, n_conv)),
            whole_spec((8, LANES)),
            whole_spec((1, inner)),
        ],
        out_specs=[
            rows_spec(Q, inner),
            rows_spec(Q, n_conv),
            rows_spec(Q, 2 * STATE),
            rows_spec(Q, inner),
            pl.BlockSpec((1, STATE, inner), lambda i: (i, 0, 0)),
        ],
        out_shape=[
            jax.ShapeDtypeStruct((group, inner), BF16),
            jax.ShapeDtypeStruct((group, n_conv), BF16),
            jax.ShapeDtypeStruct((group, 2 * STATE), BF16),
            jax.ShapeDtypeStruct((group, inner), BF16),
            jax.ShapeDtypeStruct((chunks, STATE, inner), BF16),
        ],
        scratch_shapes=[pltpu.VMEM((n_conv // LANES, Q + 8, LANES), F32), pltpu.VMEM((STATE, inner), F32)],
        compiler_params=params(),
        cost_estimate=SMALL_COST,
        name="scan_forward",
    )(ends, x_raw, small, taps, par, skip)

    cot_all = in_order(cotangent, other_cot)
    if by_hand:
        turned = turn(after(other_tokens, y_all))
        normed, turned, cot_all = lax.optimization_barrier((normed, turned, after(cot_all, y_all)))
    tile = 512
    columns = lambda rows, shift=0: pl.BlockSpec((rows, tile), lambda j: (0, j + shift))
    fixed = lambda shape: pl.BlockSpec(shape, lambda j: (0, 0))
    tiles = inner // tile
    z_all, gg, sq = pl.pallas_call(
        gate_forward,
        grid=(tiles,),
        in_specs=[fixed((group, depth)), columns(depth), columns(group), columns(8)],
        out_specs=[columns(group), columns(group), fixed((8, group))],
        out_shape=[
            jax.ShapeDtypeStruct((group, inner), BF16),
            jax.ShapeDtypeStruct((group, inner), BF16),
            jax.ShapeDtypeStruct((8, group), F32),
        ],
        scratch_shapes=[pltpu.VMEM((group, LANES), F32)],
        compiler_params=params(),
        cost_estimate=SMALL_COST,
        name="gate_forward",
    )(normed, zo_all, y_all, taps)
    sq_got = swap(sq)

    u_own, u_send, prod = pl.pallas_call(
        branch,
        grid=(depth // tile,),
        in_specs=[
            smem,
            smem,
            fixed((group, inner)),
            columns(own_rows),
            columns(own_rows),
            pl.BlockSpec((tile, inner), lambda j: (j, 1)),
        ],
        out_specs=[columns(own_rows), columns(own_rows), fixed((8, group))],
        out_shape=[
            jax.ShapeDtypeStruct((own_rows, depth), BF16),
            jax.ShapeDtypeStruct((own_rows, depth), BF16),
            jax.ShapeDtypeStruct((8, group), F32),
        ],
        scratch_shapes=[pltpu.VMEM((group, LANES), F32)],
        compiler_params=params(),
        cost_estimate=SMALL_COST,
        name="branch",
    )(me, ends, gg, cotangent, other_cot, zo_all)
    prod_got = swap(prod)
    sq_all = sq + after(sq_got, prod)
    inv_gate8 = lax.rsqrt(sq_all / inner_total + EPSILON)
    inv_gate = inv_gate8[0]
    d_branch = (cot_all.astype(F32) * (live * inv_gate)[:, None]).astype(BF16)
    g_out = lax.dot_general(d_branch, gg, TN, preferred_element_type=F32).astype(BF16)
    grad_out = lax.psum_scatter(g_out, "dp", scatter_dimension=0, tiled=True)
    prod_got = after(prod_got, g_out)
    u_recv = swap(after(u_send, g_out))
    inv_own = lax.dynamic_slice_in_dim(inv_gate, me_t * own_rows, own_rows, 0)
    out_branch = (u_own.astype(F32) + u_recv.astype(F32)) * (inv_own * live_own)[:, None]
    layer_out = (tokens.astype(F32) + out_branch).astype(BF16)

    prod_all = prod + prod_got
    coef8 = inv_gate8 * inv_gate8 * inv_gate8 * (prod_all / inner_total)
    dy, dz, gain_acc = pl.pallas_call(
        gate_backward,
        grid=(tiles,),
        in_specs=[
            smem,
            smem,
            fixed((own_rows, depth)),
            fixed((own_rows, depth)),
            columns(depth, tiles),
            columns(group),
            columns(group),
            fixed((8, group)),
            fixed((8, group)),
            columns(8),
        ],
        out_specs=[columns(group), columns(group), columns(8)],
        out_shape=[
            jax.ShapeDtypeStruct((group, inner), BF16),
            jax.ShapeDtypeStruct((group, inner), BF16),
            jax.ShapeDtypeStruct((8, inner), F32),
        ],
        scratch_shapes=[pltpu.VMEM((group, LANES), F32), pltpu.VMEM((group, LANES), F32)],
        compiler_params=params(),
        cost_estimate=SMALL_COST,
        name="gate_backward",
    )(me, ends, cotangent, other_cot, zo_all, y_all, z_all, inv_gate8, coef8, taps)
    dot = partial(lax.dot_general, preferred_element_type=F32)
    front = depth // 2

    def gradient(d, width):
        outs = pl.BlockSpec((front, width), lambda j: (0, j))
        return pl.pallas_call(
            weight_grad,
            grid=(d.shape[1] // width,),
            in_specs=[fixed((depth, group)), pl.BlockSpec((group, width), lambda j: (0, j))],
            out_specs=[outs, outs],
            out_shape=[jax.ShapeDtypeStruct((front, d.shape[1]), BF16)] * 2,
            compiler_params=params(),
            cost_estimate=SMALL_COST,
            name="weight_grad",
        )(turned, d)

    if by_hand:
        g_send, z_keep = gradient(dz, tile)
        z_got = send(g_send, beside)
        dy = after(dy, z_keep, g_send)
    else:
        grad_z = lax.psum_scatter(dot(normed, dz, TN).astype(BF16), "dp", scatter_dimension=0, tiled=True)

    halo_spec = pl.BlockSpec((n_conv // LANES, 8, LANES), lambda i: (0, 0, 0))

    def backward(top, number, carry):
        back = lambda width: pl.BlockSpec((Q, width), lambda i: (top - i, 0))
        operands = [ends, dy, xc, pre, x_raw, small, bc, states, taps, par, skip, sel, *carry]
        acc_spec = whole_spec((8 * (K + 2), n_conv))
        carry_shapes = [
            jax.ShapeDtypeStruct((STATE, inner), F32),
            jax.ShapeDtypeStruct((n_conv // LANES, 8, LANES), F32),
        ]
        carry_specs = []
        if carry:
            carry_specs = [whole_spec((STATE, inner)), halo_spec, acc_spec, whole_spec((16, LANES))]
            carry_specs += [whole_spec((8, inner)), hbm, hbm]
        return pl.pallas_call(
            partial(scan_backward, heads, chunks, top),
            grid=(number,),
            in_specs=[
                smem,
                back(inner),
                back(inner),
                back(n_conv),
                back(inner),
                back(n_small),
                back(2 * STATE),
                pl.BlockSpec((1, STATE, inner), lambda i: (top - i, 0, 0)),
                whole_spec((8, n_conv)),
                whole_spec((8, LANES)),
                whole_spec((1, inner)),
                whole_spec((inner, LANES)),
            ]
            + carry_specs,
            out_specs=[
                back(n_a),
                back(n_b),
                *([whole_spec((8, n_conv))] if carry else []),
                acc_spec,
                whole_spec((16, LANES)),
                *([] if carry else [whole_spec((STATE, inner)), halo_spec]),
            ],
            out_shape=[
                jax.ShapeDtypeStruct((group, n_a), BF16),
                jax.ShapeDtypeStruct((group, n_b), BF16),
                *([jax.ShapeDtypeStruct((8, n_conv), F32)] if carry else []),
                jax.ShapeDtypeStruct((8 * (K + 2), n_conv), F32),
                jax.ShapeDtypeStruct((16, LANES), F32),
                *([] if carry else carry_shapes),
            ],
            scratch_shapes=[
                pltpu.VMEM((STATE, inner), F32),
                pltpu.VMEM((n_conv // LANES, Q + 8, LANES), F32),
                pltpu.VMEM((Q, inner), BF16),
                pltpu.VMEM((Q, inner), BF16),
                pltpu.VMEM((Q, inner), BF16),
                pltpu.VMEM((Q, inner), BF16),
                pltpu.VMEM((Q, inner), BF16),
                pltpu.VMEM((Q, inner), BF16),
                pltpu.VMEM((STATE, inner), BF16),
                pltpu.VMEM((8, inner), F32),
            ],
            input_output_aliases={len(operands) - 2: 0, len(operands) - 1: 1} if carry else {},
            compiler_params=params(),
        cost_estimate=SMALL_COST,
            name="scan_backward",
        )(*operands)

    half_chunks = chunks // 2
    n_b = (inner + n_small) // 3
    n_a = inner + n_small - n_b
    dxa, dxb, acc, hacc, d_state, halo = backward(chunks - 1, chunks - half_chunks, ())
    if by_hand:
        z_got, dxa = lax.optimization_barrier((z_got, dxa))
        z_away, z_keep = fold_beside(z_keep, z_got)
        z_got = send(z_away, across)
        d_state = after(d_state, z_away, z_keep)
    dxa, dxb, vector = backward(half_chunks - 1, half_chunks, (d_state, halo, acc, hacc, gain_acc, dxa, dxb))[:3]
    dxa = after(dxa, u_recv)
    lanes_shared = lax.iota(jnp.int32, n_conv)[None, :] >= inner
    bits_of = lambda turn: [(i, i ^ (1 << turn)) for i in range(n_dp)]
    if by_hand:
        g_x = dot(normed, dxa, TN).astype(BF16)
        g_x, grad_out = lax.optimization_barrier((g_x, grad_out))
        grad_a = lax.psum_scatter(g_x, "dp", scatter_dimension=0, tiled=True)
        z_got, dxb, vector = lax.optimization_barrier((z_got, dxb, vector, g_x))[:3]
        z_out = ring_part(z_keep, z_got, None, 1)
        z_came = send(z_out, around)
        shared_got = swap(vector)
        b_send, b_keep = gradient(after(dxb, z_out), n_b)
        b_got = send(b_send, beside)
        shared_got, z_came, b_keep = lax.optimization_barrier((shared_got, z_came, b_keep))
        vector = vector + jnp.where(lanes_shared, shared_got, 0.0)
        z_out = ring_part(z_keep, z_got, z_came, 2)
        z_came, vector_got = send(z_out, around), send(vector, bits_of(0))
        dz = after(dz, b_send, b_keep, z_out, vector)
    else:
        dx = jnp.concatenate([dxa, dxb], axis=1)
        grad_x = lax.psum_scatter(dot(normed, dx, TN).astype(BF16), "dp", scatter_dimension=0, tiled=True)

    def back_rows(which, dz):
        pick = lambda width: pl.BlockSpec((own_rows, width), lambda j, rows: (rows[0], 0))
        return pl.pallas_call(
            normed_back,
            grid_spec=pltpu.PrefetchScalarGridSpec(
                num_scalar_prefetch=1,
                grid=(depth // tile,),
                in_specs=[
                    pick(inner),
                    pick(n_a),
                    pick(n_b),
                    pl.BlockSpec((tile, inner), lambda j, rows: (j, 0)),
                    pl.BlockSpec((tile, inner + n_small), lambda j, rows: (j, 0)),
                ],
                out_specs=pl.BlockSpec((own_rows, tile), lambda j, rows: (0, j)),
            ),
            out_shape=jax.ShapeDtypeStruct((own_rows, depth), BF16),
            compiler_params=params(),
            cost_estimate=SMALL_COST,
            name="normed_back",
        )(which, dz, dxa, dxb, zo_all, wx_all)

    dn_send = back_rows(n_t - 1 - me, dz)
    if by_hand:
        w_sum = lambda w, g: jnp.sum(w.astype(F32) * g, axis=1)
        b_got, vector_got, dn_send, z_came = lax.optimization_barrier((b_got, vector_got, dn_send, z_came))
        dn_got = swap(dn_send)
        b_away, b_keep = fold_beside(b_keep, b_got)
        b_got = send(b_away, across)
        vector = vector + vector_got
        z_out = ring_part(z_keep, z_got, z_came, 3)
        z_came, vector_got = send(z_out, around), send(vector, bits_of(1))
        dn_own = back_rows(me, after(dz, vector, z_out, b_away, b_keep))
        vector_got, dn_own, b_got, z_came = lax.optimization_barrier((vector_got, dn_own, b_got, z_came))
        vector = vector + vector_got
        b_out = ring_part(b_keep, b_got, None, 1)
        b_came, vector_got = send(b_out, around), send(vector, bits_of(2))
        grad_z = ring_part(z_keep, z_got, z_came, ring) * gain_pair
        in_part = w_sum(w_zx[0], grad_z)
        vector_got, grad_z, in_part, b_came = lax.optimization_barrier((vector_got, grad_z, in_part, b_came))
        vector = vector + vector_got
        b_out = ring_part(b_keep, b_got, b_came, 2)
        b_came, vector_got = send(b_out, around), send(vector, bits_of(3))
        grad_out = grad_out.astype(F32).T
        vector_got, grad_out, layer_out, b_came = lax.optimization_barrier((vector_got, grad_out, layer_out, b_came))
        vector = vector + vector_got
        b_came = send(ring_part(b_keep, b_got, b_came, 3), around)
    else:
        vector = sum_dp(vector + jnp.where(lanes_shared, swap(vector), 0.0))
        dn_own = back_rows(me, dz)
        dn_got = swap(dn_send)
        grad_out = grad_out.astype(F32).T
        grad_z, grad_x = grad_z.astype(F32), grad_x.astype(F32)
        in_part = jnp.sum(w_zx[0].astype(F32) * grad_z, axis=1) + jnp.sum(packed.astype(F32) * grad_x, axis=1)

    me_all = me_dp * n_t + me_t
    bc_sum = vector[: K + 1, inner:].reshape(K + 1, 2, STATE)
    bc_sum = lax.dynamic_slice_in_dim(bc_sum, me_all * span_n, span_n, 2)
    grad_bc_taps = bc_sum[:K].transpose(1, 2, 0).reshape(conv_bc.shape)
    grad_bc_bias = bc_sum[K]
    x_sum = vector[: K + 3, :inner].reshape(K + 3, heads, WIDTH)
    grad_skip = x_sum[K + 1].sum(axis=1)
    x_sum = lax.dynamic_slice_in_dim(x_sum, me_dp * span_p, span_p, 2)
    grad_x_taps = x_sum[:K].transpose(1, 2, 0).reshape(conv_x.shape)
    grad_x_bias = x_sum[K]
    grad_gate = x_sum[K + 2]
    grad_dt_bias = vector[K + 3, :heads]
    grad_a_log = vector[K + 3, LANES : LANES + heads]
    dn = (dn_own.astype(F32) + dn_got.astype(F32)) * gain_in[0:1, :]
    grad_tokens = (
        cotangent.astype(F32)
        + inv_tok * dn
        - tok_own * inv_tok * inv_tok * inv_tok * jnp.mean(dn * tok_own, axis=1, keepdims=True)
    )

    if by_hand:
        grad_b = ring_part(b_keep, b_got, b_came, ring) * gain_pair
        in_part = in_part + w_sum(packed[:, n_a:], grad_b)
        outs = (grad_bc_taps, grad_bc_bias, grad_skip, grad_x_taps, grad_x_bias, grad_gate, grad_dt_bias, grad_a_log)
        outs = lax.optimization_barrier((*outs, grad_tokens, grad_b, in_part, grad_a))
        grad_bc_taps, grad_bc_bias, grad_skip, grad_x_taps, grad_x_bias, grad_gate, grad_dt_bias, grad_a_log = outs[:8]
        grad_tokens, grad_b, in_part, grad_a = outs[8:]
        grad_a = grad_a.astype(F32)
        in_part = in_part + w_sum(packed[:, :n_a], grad_a)
    else:
        grad_a, grad_b = grad_x[:, :n_a], grad_x[:, n_a:]
    at = inner - n_a
    bc_part = jnp.concatenate([grad_b[:, at : at + 2 * STATE], jnp.broadcast_to(in_part[:, None], (shard, LANES))], axis=1)
    grad_zx = jnp.stack([grad_z, jnp.concatenate([grad_a, grad_b[:, :at]], axis=1)])
    grad_dt = grad_b[:, at + 2 * STATE : at + 2 * STATE + heads]
    half = half_bc
    bc_own = lax.dynamic_slice_in_dim(bc_part, me_t * half, half, 0)
    bc_send = lax.dynamic_slice_in_dim(bc_part, (n_t - 1 - me_t) * half, half, 0)
    bc_total = bc_own + swap(bc_send)
    own_gain = norm_gain.astype(F32)
    grad_bc = bc_total[:, : 2 * STATE].reshape(half, 2, STATE).transpose(1, 0, 2)
    grad_in = bc_total[:, 2 * STATE] / own_gain
    return (
        layer_out,
        grad_tokens,
        grad_in,
        grad_zx,
        grad_bc,
        grad_dt,
        grad_x_taps,
        grad_x_bias,
        grad_bc_taps,
        grad_bc_bias,
        grad_dt_bias,
        grad_a_log,
        grad_skip,
        grad_gate,
        grad_out,
    )


def solution(mesh):
    both = ("dp", "tensor")
    in_specs = (
        P(both, None),
        P(both, None),
        P("dp", None),
        P(both),
        P(None, "dp", "tensor"),
        P(None, both, None),
        P("dp", "tensor"),
        P("tensor", "dp"),
        P("tensor", "dp"),
        P(None, both),
        P(None, both),
        P("tensor"),
        P("tensor"),
        P("tensor"),
        P("tensor", "dp"),
        P("tensor", "dp"),
    )
    out_specs = (
        P(both, None),
        P(both, None),
        P(both),
        P(None, "dp", "tensor"),
        P(None, both, None),
        P("dp", "tensor"),
        P("tensor", "dp"),
        P("tensor", "dp"),
        P(None, both),
        P(None, both),
        P("tensor"),
        P("tensor"),
        P("tensor"),
        P("tensor", "dp"),
        P("tensor", "dp"),
    )
    return jax.shard_map(local, mesh=mesh, in_specs=in_specs, out_specs=out_specs, check_vma=False)
```

```python
from functools import partial

import jax
import jax.numpy as jnp
from jax import lax
from jax.experimental import pallas as pl
from jax.experimental.pallas import tpu as pltpu
from jax.sharding import PartitionSpec as P

EPSILON = 1e-05
HIGHEST = lax.Precision.HIGHEST
K = 4
WIDTH = 64
STATE = 128
Q = 128
LANES = 128
LOG2E = 1.4426950408889634
VMEM_LIMIT = 60 * 1024 * 1024
F32 = jnp.float32
BF16 = jnp.bfloat16

NN = (((1,), (0,)), ((), ()))
NT = (((1,), (1,)), ((), ()))
TN = (((0,), (0,)), ((), ()))


def mm(a, b, dims=NN):
    return lax.dot_general(a, b, dims, preferred_element_type=F32)


def mm_exact(a, b, dims=NN):
    return lax.dot_general(a, b, dims, preferred_element_type=F32, precision=HIGHEST)


def iota(shape, dim):
    return lax.broadcasted_iota(jnp.int32, shape, dim)


def segment_of(rows, ends_ref, count):
    total = (rows >= ends_ref[0]).astype(jnp.int32)
    for j in range(1, count):
        total = total + (rows >= ends_ref[j]).astype(jnp.int32)
    return total


def scalar_segment(row, ends_ref, count):
    total = jnp.where(row >= ends_ref[0], 1, 0)
    for j in range(1, count):
        total = total + jnp.where(row >= ends_ref[j], 1, 0)
    return total


def sigmoid(v):
    return 0.5 * jnp.tanh(0.5 * v) + 0.5


def softplus(v):
    return jnp.maximum(v, 0.0) + jnp.log1p(jnp.exp(-jnp.abs(v)))


def chunk_masks(chunk, ends_ref, count):
    base = chunk * Q
    rows = iota((Q, Q), 0) + base
    cols = iota((Q, Q), 1) + base
    row_ids = segment_of(rows, ends_ref, count)
    col_ids = segment_of(cols, ends_ref, count)
    same = row_ids == col_ids
    before_id = jnp.where(chunk == 0, -1, scalar_segment(base - 1, ends_ref, count))
    final_id = scalar_segment(base + Q - 1, ends_ref, count)
    carry = (row_ids == before_id).astype(F32)
    last = (row_ids == final_id).astype(F32)
    passing = jnp.where(before_id == final_id, 1.0, 0.0).astype(F32)
    return rows, cols, row_ids, same, carry, last, passing


def decays(dt_raw, par_ref):
    shifted = dt_raw + par_ref[0:1, :]
    step = softplus(shifted)
    decay_rate = jnp.exp(par_ref[1:2, :])
    return shifted, step, decay_rate


def pair_columns(values, pair, first):
    left = jnp.broadcast_to(values[:, 2 * pair : 2 * pair + 1], (Q, LANES))
    right = jnp.broadcast_to(values[:, 2 * pair + 1 : 2 * pair + 2], (Q, LANES))
    return left, right, jnp.where(first, left, right)


def scan_forward(
    heads, ends_ref, xr_ref, small_ref, taps_ref, par_ref, skip_ref,
    xc_ref, pre_ref, bc_ref, y_ref, st_ref, buf, state,
):
    count = ends_ref.shape[0]
    inner = heads * WIDTH
    chunk = pl.program_id(0)

    @pl.when(chunk == 0)
    def _():
        buf[:, 0:8, :] = jnp.zeros((buf.shape[0], 8, LANES), F32)
        state[...] = jnp.zeros(state.shape, F32)

    rows, cols, row_ids, same, carry, last, passing = chunk_masks(chunk, ends_ref, count)
    causal = rows >= cols
    visible = same & causal
    lag_mask = [None]
    for lag in range(1, K):
        earlier = rows - lag
        keep = (segment_of(earlier, ends_ref, count) == row_ids) & (earlier >= 0)
        lag_mask.append(keep.astype(F32))

    small = small_ref[...]

    def convolve(lo, raw):
        span = slice(lo, lo + LANES)
        place = lo // LANES
        buf[place, 8 : 8 + Q, :] = raw
        pre = taps_ref[K : K + 1, span] + taps_ref[K - 1 : K, span] * raw
        for lag in range(1, K):
            pre = pre + taps_ref[K - 1 - lag : K - lag, span] * (
                buf[place, 8 - lag : 8 - lag + Q, :] * lag_mask[lag]
            )
        buf[place, 0:8, :] = raw[Q - 8 : Q, :]
        pre_ref[:, span] = pre.astype(BF16)
        return pre * sigmoid(pre)

    b_f = convolve(inner, small[:, :STATE]).astype(BF16).astype(F32)
    c_b = convolve(inner + STATE, small[:, STATE : 2 * STATE]).astype(BF16)
    b_b = b_f.astype(BF16)
    bc_ref[:, :STATE] = b_b
    bc_ref[:, STATE:] = c_b
    b_t = b_f.T.astype(BF16)

    _, step, decay_rate = decays(small[:, 2 * STATE :], par_ref)
    csum = mm_exact(causal.astype(F32), step * (-LOG2E * decay_rate))
    csum_t = csum.T
    scores = jnp.where(visible, mm(c_b, b_b, NT), 0.0)
    first = iota((Q, LANES), 1) < WIDTH
    first_row = iota((1, LANES), 1) < WIDTH

    wide = 2 * LANES
    for quad in range(0, inner, wide):
        block = slice(quad, quad + wide)
        held = state[:, block]
        held_b = held.astype(BF16)
        st_ref[0, :, block] = held_b
        carried = mm(c_b, held_b)
        weighted, kept = [], []
        for part in range(0, wide, LANES):
            lo = quad + part
            pair = lo // LANES
            span = slice(lo, lo + LANES)
            xc = convolve(lo, xr_ref[:, span].astype(F32)).astype(BF16)
            xc_ref[:, span] = xc
            xc = xc.astype(F32)
            left, right, both = pair_columns(csum, pair, first)
            _, _, step_pair = pair_columns(step, pair, first)
            mix = jnp.concatenate(
                [
                    (scores * jnp.exp2(jnp.minimum(left - csum_t[2 * pair : 2 * pair + 1, :], 0.0))).astype(BF16),
                    (scores * jnp.exp2(jnp.minimum(right - csum_t[2 * pair + 1 : 2 * pair + 2, :], 0.0))).astype(BF16),
                ],
                axis=1,
            )
            fed_b = (xc * step_pair).astype(BF16)
            zero = jnp.zeros((Q, LANES), BF16)
            stacked = jnp.concatenate([jnp.where(first, fed_b, zero), jnp.where(first, zero, fed_b)], axis=0)
            y = mm(mix, stacked) + carried[:, part : part + LANES] * (jnp.exp2(both) * carry)
            y_ref[:, span] = (y + skip_ref[:, span] * xc).astype(BF16)
            closing = both[Q - 1 : Q, :]
            weighted.append((fed_b.astype(F32) * (jnp.exp2(closing - both) * last)).astype(BF16))
            kept.append(jnp.exp2(closing) * passing)
        fresh = mm(b_t, jnp.concatenate(weighted, axis=1))
        state[:, block] = held * jnp.concatenate(kept, axis=1) + fresh


def scan_backward(
    base, last_call, chunks, ends_ref, dy_ref, xc_ref, pre_ref, xr_ref, small_ref, bc_ref, st_ref, taps_ref,
    par_ref, skip_ref, sel_ref, *refs,
):
    if last_call:
        pre_bc_ref, taps_bc_ref, part_in, acc_in, hacc_in, gain_acc_ref = refs[:6]
        dx_ref, rows_ref, acc_ref, hacc_ref = refs[6:10]
        refs = refs[10:]
    else:
        dx_ref, part_ref, acc_ref, hacc_ref = refs[:4]
        refs = refs[4:]
    dstate, dpre, ab_hi, ab_lo, v_b, u_b, dyd, fedw, dst_b, through = refs
    count = ends_ref.shape[0]
    inner = dy_ref.shape[1]
    total_rows = chunks * Q
    chunk = chunks - 1 - pl.program_id(0)

    @pl.when(pl.program_id(0) == 0)
    def _():
        dpre[:, Q : Q + 8, :] = jnp.zeros((dpre.shape[0], 8, LANES), F32)
        dstate[...] = jnp.zeros(dstate.shape, F32)
        acc_ref[...] = jnp.zeros(acc_ref.shape, F32)
        hacc_ref[...] = hacc_in[...] if last_call else jnp.zeros(hacc_ref.shape, F32)

    rows, cols, row_ids, same, carry, last, passing = chunk_masks(chunk, ends_ref, count)
    causal = rows >= cols
    visible = same & causal
    lag_mask = [None]
    for lag in range(1, K):
        later = rows + lag
        keep = (segment_of(later, ends_ref, count) == row_ids) & (later < total_rows)
        lag_mask.append(keep.astype(F32))

    small = small_ref[...]
    shifted, step, decay_rate = decays(small[:, 2 * STATE :], par_ref)
    csum = mm_exact(causal.astype(F32), step * (-LOG2E * decay_rate))
    csum_t = csum.T
    b_b = bc_ref[:, :STATE]
    c_b = bc_ref[:, STATE:]
    c_t = c_b.astype(F32).T.astype(BF16)
    scores = jnp.where(visible, mm(c_b, b_b, NT), 0.0)
    first = iota((Q, LANES), 1) < WIDTH

    def fold(values):
        return values.reshape(Q // 8, 8, values.shape[1]).sum(axis=0)

    def conv_back(lo, d_conv, raw, pre, taps, at):
        span = slice(lo, lo + LANES)
        place = lo // LANES
        gate = sigmoid(pre)
        d_pre = d_conv * (gate * (1.0 + pre * (1.0 - gate)))
        dpre[place, 0:Q, :] = d_pre
        d_raw = taps[K - 1 : K, at] * d_pre
        acc_ref[8 * (K - 1) : 8 * K, span] += fold(d_pre * raw)
        acc_ref[8 * K : 8 * K + 8, span] += fold(d_pre)
        for lag in range(1, K):
            moved = dpre[place, lag : lag + Q, :] * lag_mask[lag]
            d_raw = d_raw + taps[K - 1 - lag : K - lag, at] * moved
            acc_ref[8 * (K - 1 - lag) : 8 * (K - lag), span] += fold(moved * raw)
        dpre[place, Q : Q + 8, :] = d_pre[0:8, :]
        dx_ref[:, span] = d_raw.astype(BF16)

    d_scores = jnp.zeros((Q, Q), F32)
    wide = 2 * LANES
    for quad in range(0, inner, wide):
        block = slice(quad, quad + wide)
        held_b = st_ref[0, :, block]
        d_held = dstate[:, block]
        d_held_b = d_held.astype(BF16)
        dst_b[:, block] = d_held_b
        carried = mm(c_b, held_b)
        returned = mm(b_b, d_held_b)
        crossing = (d_held * held_b.astype(F32)).reshape(STATE // 8, 8, wide).sum(axis=0)
        grown_parts, kept_parts = [], []
        for part in range(0, wide, LANES):
            lo = quad + part
            pair = (base + lo) // LANES
            span = slice(lo, lo + LANES)
            xc = xc_ref[:, span].astype(F32)
            dy_b = dy_ref[:, span]
            dy = dy_b.astype(F32)
            left, right, both = pair_columns(csum, pair, first)
            _, _, step_pair = pair_columns(step, pair, first)
            fall_left = jnp.exp2(jnp.minimum(left - csum_t[2 * pair : 2 * pair + 1, :], 0.0))
            fall_right = jnp.exp2(jnp.minimum(right - csum_t[2 * pair + 1 : 2 * pair + 2, :], 0.0))
            mix = jnp.concatenate([(scores * fall_left).astype(BF16), (scores * fall_right).astype(BF16)], axis=1)
            fed_b = (xc * step_pair).astype(BF16)
            fed = fed_b.astype(F32)
            zero = jnp.zeros((Q, LANES), BF16)
            stacked = jnp.concatenate([jnp.where(first, fed_b, zero), jnp.where(first, zero, fed_b)], axis=0)
            grown = jnp.exp2(both) * carry
            y = mm(mix, stacked) + carried[:, part : part + LANES] * grown
            d_mix = mm(dy_b, stacked, NT)
            d_scores = d_scores + d_mix[:, :Q] * fall_left + d_mix[:, Q:] * fall_right
            d_fed2 = mm(mix, dy_b, TN)
            d_fed_in = jnp.where(first, d_fed2[:Q], d_fed2[Q:])
            closing = both[Q - 1 : Q, :]
            shrink = jnp.exp2(closing - both) * last
            d_fed_out = returned[:, part : part + LANES] * shrink
            d_fed = d_fed_in + d_fed_out
            straddle = dy * y - fed * d_fed_in
            hi = straddle.astype(BF16)
            ab_hi[:, span] = hi
            ab_lo[:, span] = (straddle - hi.astype(F32)).astype(BF16)
            v_b[:, span] = (fed * d_fed_out).astype(BF16)
            u_b[:, span] = (xc * d_fed).astype(BF16)
            fedw[:, span] = (fed * shrink).astype(BF16)
            grown_parts.append((dy * grown).astype(BF16))
            kept_parts.append(jnp.exp2(closing) * passing)
            acc_ref[8 * K + 8 : 8 * K + 16, span] += fold(dy * xc)
            d_conv = d_fed * step_pair + skip_ref[:, span] * dy
            conv_back(lo, d_conv, xr_ref[:, span].astype(F32), pre_ref[:, span].astype(F32), taps_ref, span)
        dy_grown = jnp.concatenate(grown_parts, axis=1)
        kept = jnp.concatenate(kept_parts, axis=1)
        dyd[:, block] = dy_grown
        through[:, block] = crossing * kept
        dstate[:, block] = d_held * kept + mm(c_t, dy_grown)

    d_scores_b = jnp.where(visible, d_scores, 0.0).astype(BF16)
    d_c = mm(dyd[...], st_ref[0], NT) + mm(d_scores_b, b_b)
    d_b = mm(fedw[...], dst_b[...], NT) + mm(d_scores_b, c_b, TN)
    sel = sel_ref[...]
    red_ab = mm(ab_hi[...], sel) + mm(ab_lo[...], sel)
    red_v = mm(v_b[...], sel)
    red_u = mm(u_b[...], sel)
    thr = through[...]
    thr_hi = thr.astype(BF16)
    red_t = mm(thr_hi, sel) + mm((thr - thr_hi.astype(F32)).astype(BF16), sel)
    d_rate = (
        mm_exact((same & (cols >= rows)).astype(F32), red_ab)
        + mm_exact((same & (cols < rows)).astype(F32), red_v)
        + jnp.sum(red_t, axis=0, keepdims=True)
    )
    d_step = red_u - d_rate * decay_rate
    d_dt = d_step * sigmoid(shifted)
    hacc_ref[0:8, :] += fold(d_dt)
    hacc_ref[8:16, :] += fold(d_rate * (-decay_rate * step))
    if not last_call:
        part_ref[:, :STATE] = d_b
        part_ref[:, STATE : 2 * STATE] = d_c
        part_ref[:, 2 * STATE :] = d_dt
        return

    for k, d_conv in enumerate((d_b, d_c)):
        at = slice(k * STATE, (k + 1) * STATE)
        pre = pre_bc_ref[:, at].astype(F32)
        conv_back(inner + k * STATE, d_conv + part_in[:, at], small[:, at], pre, taps_bc_ref, at)
    dx_ref[:, inner + 2 * STATE :] = (d_dt + part_in[:, 2 * STATE :]).astype(BF16)

    @pl.when(pl.program_id(0) == pl.num_programs(0) - 1)
    def _():
        before = acc_in.shape[1]
        whole = before + inner
        rows_ref[...] = jnp.zeros(rows_ref.shape, F32)
        for k in range(K + 2):
            block = slice(8 * k, 8 * k + 8)
            rows_ref[k : k + 1, :before] = jnp.sum(acc_in[block, :], axis=0, keepdims=True)
            rows_ref[k : k + 1, before:] = jnp.sum(acc_ref[block, :], axis=0, keepdims=True)
        rows_ref[K + 2 : K + 3, :whole] = jnp.sum(gain_acc_ref[...], axis=0, keepdims=True)
        for k in range(2):
            total = jnp.sum(hacc_ref[8 * k : 8 * k + 8, :], axis=0, keepdims=True)
            rows_ref[K + 3 : K + 4, k * LANES : (k + 1) * LANES] = total


def load_blocks(offsets_ref, parts, whole, sems, size, columns, first=0):
    @pl.when(pl.program_id(0) == 0)
    def _():
        copies = []
        for part in parts:
            for j in range(part.shape[0] // size):
                k = first + len(copies)
                start = 0 if size == whole.shape[0] else pl.multiple_of(offsets_ref[k], 32)
                source = part.at[pl.ds(j * size, size), :]
                copies.append(pltpu.make_async_copy(source, whole.at[pl.ds(start, size), slice(*columns)], sems.at[k]))
        for copy in copies:
            copy.start()
        for copy in copies:
            copy.wait()


def turn_rows(offsets_ref, me_ref, own_ref, other_ref, out_ref, turned):
    depth = own_ref.shape[1]
    rows = own_ref.shape[0]
    for index, source in enumerate((own_ref, other_ref)):
        at = pl.multiple_of(jnp.where(index == 0, me_ref[0], 1 - me_ref[0]) * rows, LANES)
        for lo in range(0, rows, Q):
            tile = source[lo : lo + Q, :].astype(F32)
            scale = lax.rsqrt(jnp.mean(tile * tile, axis=1, keepdims=True) + EPSILON)
            tile = tile * scale
            for left in range(0, depth, LANES):
                turned[left : left + LANES, pl.ds(at + lo, Q)] = tile[:, left : left + LANES].T.astype(BF16)
    count = offsets_ref.shape[0]
    size = depth // count
    for k in range(count):
        start = pl.multiple_of(offsets_ref[k], 32)
        out_ref[k * size : (k + 1) * size, :] = turned[pl.ds(start, size), :]


def project(counts, heads, size, offsets_ref, me_ref, own_ref, other_ref, place_ref, *refs):
    count = sum(counts)
    blocks, (x_ref, small_ref, normed_ref, taps_ref, gain_ref, w_out_ref, w_ref, sems, out_sem) = refs[:count], refs[count:]
    split = x_ref.shape[1]
    shards = w_ref.shape[0] // size
    load_blocks(offsets_ref, blocks[: counts[0]], w_ref, sems, size, (0, split))
    load_blocks(offsets_ref, blocks[counts[0] :], w_ref, sems, size, (split, w_ref.shape[1]), shards)
    keep = pltpu.make_async_copy(w_ref, w_out_ref, out_sem)
    depth, inner = w_ref.shape[0], x_ref.shape[1]
    tile = 512

    @pl.when(pl.program_id(0) == 0)
    def _():
        keep.start()
        spare = w_ref[:, inner + 2 * STATE :]
        turned = spare.astype(F32).T
        gain_ref[...] = jnp.broadcast_to(turned[heads + K + 2 : heads + K + 3, :], gain_ref.shape)
        few = turned[heads : heads + 16, :].astype(BF16)
        lanes = iota((depth, LANES), 1)
        for lo in range(0, inner + 2 * STATE, LANES):
            if lo < inner:
                wanted, row = place_ref[:, :LANES] == lanes + lo, 0
            else:
                wanted, row = place_ref[:, LANES:] == lanes + (lo - inner), 8
            moved = mm(few, jnp.where(wanted, 1.0, 0.0).astype(BF16))
            taps_ref[:, lo : lo + LANES] = moved[row : row + 8, :]

    rows = jnp.where(pl.program_id(0) == me_ref[0], own_ref[...], other_ref[...]).astype(F32)
    scale = lax.rsqrt(jnp.mean(rows * rows, axis=1, keepdims=True) + EPSILON)
    rows = (rows * scale * gain_ref[0:1, :]).astype(BF16)
    normed_ref[...] = rows
    for lo in range(0, inner, tile):
        x_ref[:, lo : lo + tile] = mm(rows, w_ref[:, lo : lo + tile]).astype(BF16)
    small_ref[...] = mm(rows, w_ref[:, inner:])

    @pl.when(pl.program_id(0) == pl.num_programs(0) - 1)
    def _():
        keep.wait()


def row_sums(lanes):
    return mm_exact(jnp.ones((8, LANES), F32), lanes, NT)


def spread_rows(values):
    pick = jnp.where(iota((8, LANES), 0) == 0, 1.0, 0.0).astype(F32)
    return mm_exact(values, pick, TN)


def gate_forward(normed_ref, w_ref, y_ref, gain_ref, z_ref, gg_ref, sq_ref, square):
    rows, width = z_ref.shape
    size = 512

    @pl.when(pl.program_id(0) == 0)
    def _():
        square[...] = jnp.zeros(square.shape, F32)

    for lo in range(0, rows, size):
        at = slice(lo, lo + size)
        z = mm(normed_ref[at, :], w_ref[...]).astype(BF16)
        z_ref[at, :] = z
        z = z.astype(F32)
        gated = y_ref[at, :].astype(F32) * (z * sigmoid(z))
        gg_ref[at, :] = (gated * gain_ref[K + 1 : K + 2, :]).astype(BF16)
        twice = gated * gated
        for part in range(0, width, LANES):
            square[at, :] += twice[:, part : part + LANES]

    @pl.when(pl.program_id(0) == pl.num_programs(0) - 1)
    def _():
        sq_ref[...] = row_sums(square[...])


def branch(me_ref, ends_ref, gg_ref, own_ref, other_ref, w_ref, mine_ref, away_ref, prod_ref, product):
    rows, width = mine_ref.shape
    size = 512

    @pl.when(pl.program_id(0) == 0)
    def _():
        product[...] = jnp.zeros(product.shape, F32)

    for index, (out_ref, cot_ref) in enumerate(((mine_ref, own_ref), (away_ref, other_ref))):
        first = jnp.where(index == 0, me_ref[0], 1 - me_ref[0]) * rows
        for lo in range(0, rows, size):
            at = pl.ds(pl.multiple_of(first + lo, size), size)
            u = mm(gg_ref[at, :], w_ref[...], NT)
            out_ref[lo : lo + size, :] = u.astype(BF16)
            term = u * cot_ref[lo : lo + size, :].astype(F32)
            for part in range(0, width, LANES):
                product[at, :] += term[:, part : part + LANES]

    @pl.when(pl.program_id(0) == pl.num_programs(0) - 1)
    def _():
        live = iota(product.shape, 0) < ends_ref[ends_ref.shape[0] - 1]
        prod_ref[...] = row_sums(jnp.where(live, product[...], 0.0))


def gate_backward(
    me_ref, ends_ref, own_ref, other_ref, w_ref, y_ref, z_ref, rg_ref, coef_ref, gain_ref,
    dy_ref, dz_ref, acc_ref, rg, coef,
):
    total, width = dy_ref.shape
    rows = own_ref.shape[0]
    size = 512

    @pl.when(pl.program_id(0) == 0)
    def _():
        live = iota(rg.shape, 0) < ends_ref[ends_ref.shape[0] - 1]
        rg[...] = spread_rows(rg_ref[...])
        coef[...] = spread_rows(coef_ref[...])
        rg[...] = jnp.where(live, rg[...], 0.0)

    gain = gain_ref[K + 1 : K + 2, :]
    sums = jnp.zeros((8, width), F32)
    for index, cot_ref in enumerate((own_ref, other_ref)):
        first = jnp.where(index == 0, me_ref[0], 1 - me_ref[0]) * rows
        for lo in range(0, rows, size):
            at = pl.ds(pl.multiple_of(first + lo, size), size)
            ds = mm(cot_ref[lo : lo + size, :], w_ref[...])
            z = z_ref[at, :].astype(F32)
            y = y_ref[at, :].astype(F32)
            scale = jnp.concatenate([rg[at, :]] * (width // LANES), axis=1)
            back = jnp.concatenate([coef[at, :]] * (width // LANES), axis=1)
            gate = sigmoid(z)
            silu = z * gate
            gated = y * silu
            d_normal = ds * scale
            sums = sums + (d_normal * gated).reshape(size // 8, 8, width).sum(axis=0)
            d_gated = d_normal * gain - gated * back
            dy_ref[at, :] = (d_gated * silu).astype(BF16)
            dz_ref[at, :] = (d_gated * y * (gate + silu * (1.0 - gate))).astype(BF16)
    acc_ref[...] = sums


def weight_grad(turned_ref, d_ref, away_ref, keep_ref):
    half = away_ref.shape[0]
    d = d_ref[...]
    away_ref[...] = mm(turned_ref[:half, :], d).astype(BF16)
    keep_ref[...] = mm(turned_ref[half:, :], d).astype(BF16)


def normed_back(rows_ref, dz_ref, dxa_ref, dxb_ref, wz_ref, wx_ref, out_ref):
    n_a = dxa_ref.shape[1]
    total = mm(dz_ref[...], wz_ref[...], NT)
    total = total + mm(dxa_ref[...], wx_ref[:, :n_a], NT) + mm(dxb_ref[...], wx_ref[:, n_a:], NT)
    out_ref[...] = total.astype(BF16)


def params():
    return pltpu.CompilerParams(dimension_semantics=("arbitrary",), vmem_limit_bytes=VMEM_LIMIT)


SMALL_COST = pl.CostEstimate(flops=1000, bytes_accessed=1000, transcendentals=0)


def rows_spec(block, width, column=0):
    return pl.BlockSpec((block, width), lambda i: (i, column))


def whole_spec(shape, column=0):
    return pl.BlockSpec(shape, lambda i: (0, column))


def local(
    tokens,
    cotangent,
    lengths,
    norm_gain,
    w_zx,
    w_bc,
    w_dt,
    conv_x,
    conv_x_bias,
    conv_bc,
    conv_bc_bias,
    dt_bias,
    a_log,
    d_skip,
    gate_gain,
    w_out,
):
    n_t = lax.axis_size("tensor")
    n_dp = lax.axis_size("dp")
    me_t = lax.axis_index("tensor")
    me_dp = lax.axis_index("dp")
    own_rows, depth = tokens.shape
    group = own_rows * n_t
    chunks = group // Q
    heads = dt_bias.shape[0]
    inner = heads * WIDTH
    inner_total = inner * n_t
    shard = w_zx.shape[1]
    pairs = [(i, n_t - 1 - i) for i in range(n_t)]

    def swap(v):
        return lax.ppermute(v, "tensor", pairs)

    def in_order(mine, other, axis=0):
        low = jnp.where(me_t == 0, mine, other)
        high = jnp.where(me_t == 0, other, mine)
        return jnp.concatenate([low, high], axis=axis)

    def sum_dp(v):
        step = 1
        while step < n_dp:
            v = v + lax.ppermute(v, "dp", [(i, i ^ step) for i in range(n_dp)])
            step *= 2
        return v

    def after(value, *others):
        return lax.optimization_barrier((value, *others))[0]

    ring = 4
    plane = n_dp // (2 * ring)

    around = [(i, (i + 2 * plane) % n_dp) for i in range(n_dp)]
    across = [(i, i ^ 2) for i in range(n_dp)]
    beside = [(i, i ^ 1) for i in range(n_dp)]

    def send(v, way):
        return lax.ppermute(v, "dp", way)

    by_hand = plane == 2 and shard % 32 == 0

    def whole(v):
        return [lax.all_gather(v, "dp", axis=0, tiled=True)]

    def relative_order():
        level, side, core = me_dp // 4, (me_dp // 2) % 2, me_dp % 2
        order = []
        for dc in (1, 0):
            for dy in (1, 0):
                for dz in range(1, ring + 1):
                    order.append(((level - dz + ring) % ring) * 4 + (side ^ dy) * 2 + (core ^ dc))
        return order

    def fold_away(keep, got):
        half = keep.shape[0] // 2
        return (keep[:half].astype(F32) + got[:half].astype(F32)).astype(BF16), got

    def ring_part(keep, core, got, came, turn):
        low, high = (turn - 1) * shard, turn * shard
        half = keep.shape[0] // 2
        part = keep[half + low : half + high].astype(F32) + core[half + low : half + high].astype(F32)
        part = part + got[low:high].astype(F32)
        if came is not None:
            part = part + came.astype(F32)
        return part if turn == ring else part.astype(BF16)

    ends = jnp.cumsum(lengths[0]).astype(jnp.int32)
    live = (lax.iota(jnp.int32, group) < ends[-1]).astype(F32)
    live_own = lax.dynamic_slice_in_dim(live, me_t * own_rows, own_rows, 0)
    me = me_t.astype(jnp.int32).reshape(1)

    span_p = conv_x_bias.shape[1]
    span_n = conv_bc_bias.shape[1]
    half_bc = w_bc.shape[1]
    bits = jnp.concatenate([norm_gain, conv_bc.reshape(-1), conv_bc_bias.reshape(-1)])
    bits = jnp.pad(bits, (0, LANES - bits.shape[0]))
    tiny = jnp.concatenate([w_bc.reshape(2 * half_bc, STATE), bits[None]], axis=0)
    other_tiny = swap(tiny)
    other_bc = other_tiny[: 2 * half_bc].reshape(w_bc.shape)
    both_bits = [bits, other_tiny[2 * half_bc]]
    at = norm_gain.shape[0]
    gain_pair = in_order(*[v[:at] for v in both_bits])[:, None]
    taps_bc = in_order(*[v[at : at + conv_bc.size].reshape(2, span_n, K) for v in both_bits], axis=1)
    at += conv_bc.size
    bias_bc = in_order(*[v[at : at + 2 * span_n].reshape(2, span_n, 1) for v in both_bits], axis=1)
    spare_bc = jnp.concatenate([taps_bc, bias_bc], axis=2).reshape(4 * span_n, K + 1)
    spare_x = [conv_x.reshape(shard, K), conv_x_bias.reshape(shard, 1), gate_gain.reshape(shard, 1), gain_pair]
    bc_pair = in_order(w_bc, other_bc, axis=1)
    w_x = w_zx[1]
    w_small = jnp.concatenate(
        [bc_pair[0], bc_pair[1], w_dt, *spare_x, jnp.zeros((shard, 8 - K - 3), BF16)]
        + [jnp.pad(spare_bc, ((0, shard - 4 * span_n), (0, LANES - heads - 8 - K - 1)))],
        axis=1,
    )
    gain_pair = gain_pair.astype(F32)
    where = after(lax.iota(jnp.int32, depth), w_small)
    home, inside = where // shard, where % shard
    place_x = (inside // span_p) * WIDTH + home * span_p + inside % span_p
    half_n = 2 * span_n
    place_bc = (inside // half_n) * STATE + home * half_n + inside % half_n
    place = jnp.concatenate([jnp.broadcast_to(v[:, None], (depth, LANES)) for v in (place_x, place_bc)], axis=1)
    par = jnp.concatenate([dt_bias[None], a_log[None], jnp.zeros((6, heads), F32)], axis=0)
    par = jnp.concatenate([par, jnp.zeros((8, LANES - heads), F32)], axis=1)
    skip = jnp.repeat(d_skip, WIDTH)[None]
    members = lax.iota(jnp.int32, inner)[:, None] // WIDTH
    sel = (members == lax.iota(jnp.int32, LANES)[None, :]).astype(BF16)
    smem = pl.BlockSpec(memory_space=pltpu.SMEM)
    vmem = pl.BlockSpec(memory_space=pltpu.VMEM)
    hbm = pl.BlockSpec(memory_space=pl.ANY)
    n_small = 2 * STATE + LANES
    n_conv = inner + 2 * STATE
    w_rest = jnp.concatenate([w_zx[0], w_out.T], axis=1)

    def turn(other_tokens):
        return pl.pallas_call(
            turn_rows,
            in_specs=[smem, smem, vmem, vmem],
            out_specs=vmem,
            out_shape=jax.ShapeDtypeStruct((depth, group), BF16),
            scratch_shapes=[pltpu.VMEM((depth, group), BF16)],
            compiler_params=pltpu.CompilerParams(vmem_limit_bytes=VMEM_LIMIT),
            cost_estimate=SMALL_COST,
            name="turn_rows",
        )((jnp.stack(relative_order()) * shard).astype(jnp.int32), me, tokens, other_tokens)

    def place_of(turn, side, core):
        level = (me_dp // (2 * plane) - turn + ring) % ring
        return (level * (2 * plane) + ((me_dp % (2 * plane)) ^ (2 * side + core))) * shard

    together = lambda *values: list(lax.optimization_barrier(tuple(values)))
    joined = lambda *values: jnp.concatenate(values, axis=0)
    if by_hand:
        shift = lambda k: [(i, (i + 2 * plane * k) % n_dp) for i in range(n_dp)]
        l1, o0, c0 = together(send(w_x, around), send(w_x, across), send(w_x, beside))
        late, w_small = together(tokens, w_small, l1, o0, c0)[:2]
        pieces = [late[:176], late[176:352], late[352:]]
        l2, o1, s1, s2, s3 = together(
            send(l1, around), send(l1, across), send(w_small, shift(1)), send(w_small, shift(2)), send(w_small, shift(3))
        )
        w_rest = after(jnp.concatenate([w_zx[0], w_out.T], axis=1), l2)
        zo_all = lax.all_gather(w_rest, "dp", axis=0, tiled=True)
        small_line = joined(w_small, s1, s2, s3)
        l3, o2, c1, small_across, t0 = together(
            send(l2, around), send(l2, across), send(joined(l1, o0), beside), send(small_line, across), swap(pieces[0])
        )
        o3, c2, small_beside, t1, place, par, skip, sel = together(
            send(l3, across), send(joined(l2, o1), beside), send(joined(small_line, small_across), beside),
            swap(after(pieces[1], t0)), place, par, skip, sel,
        )
        c3, t2 = together(send(joined(l3, o2, o3), beside), swap(after(pieces[2], t1)))
        other_tokens = joined(t0, t1, t2)
        other_cot = swap(after(cotangent, other_tokens))
        wx_parts = [w_x, l1, l2, l3, o0, o1, o2, o3, c0, c1, c2, c3]
        order = [(t, 0, 0) for t in range(4)] + [(t, 1, 0) for t in range(4)]
        order += [(0, 0, 1), (1, 0, 1), (0, 1, 1), (2, 0, 1), (1, 1, 1), (3, 0, 1), (2, 1, 1), (3, 1, 1)]
        small_parts = [small_line, small_across, small_beside]
        order += [(t, side, core) for core in range(2) for side in range(2) for t in range(4)]
        offsets = jnp.stack([place_of(*key) for key in order]).astype(jnp.int32)
    else:
        wx_parts, small_parts = whole(w_x), whole(w_small)
        zo_all = whole(jnp.concatenate([w_zx[0], w_out.T], axis=1))[0]
        other_tokens, other_cot = swap(tokens), swap(cotangent)
        offsets = jnp.zeros((2,), jnp.int32)
    counts = (len(wx_parts), len(small_parts))
    sems = pltpu.SemaphoreType.DMA((offsets.shape[0],))
    tok_own = tokens.astype(F32)
    inv_tok = lax.rsqrt(jnp.mean(tok_own * tok_own, axis=1, keepdims=True) + EPSILON)

    block = own_rows
    steps = group // block
    x_raw, small, normed, taps, gain_in, wx_all = pl.pallas_call(
        partial(project, counts, heads, shard if by_hand else depth),
        grid=(steps,),
        in_specs=[
            smem,
            smem,
            whole_spec((block, depth)),
            whole_spec((block, depth)),
            whole_spec((depth, 2 * LANES)),
        ]
        + [hbm] * sum(counts),
        out_specs=[
            rows_spec(block, inner),
            rows_spec(block, n_small),
            rows_spec(block, depth),
            whole_spec((8, n_conv)),
            whole_spec((8, depth)),
            hbm,
        ],
        out_shape=[
            jax.ShapeDtypeStruct((group, inner), BF16),
            jax.ShapeDtypeStruct((group, n_small), F32),
            jax.ShapeDtypeStruct((group, depth), BF16),
            jax.ShapeDtypeStruct((8, n_conv), F32),
            jax.ShapeDtypeStruct((8, depth), F32),
            jax.ShapeDtypeStruct((depth, inner + n_small), BF16),
        ],
        scratch_shapes=[pltpu.VMEM((depth, inner + n_small), BF16), sems, pltpu.SemaphoreType.DMA],
        compiler_params=params(),
        cost_estimate=SMALL_COST,
        name="project",
    )(offsets, me, tokens, other_tokens, place, *wx_parts, *small_parts)
    xc, pre, bc, y_all, states = pl.pallas_call(
        partial(scan_forward, heads),
        grid=(chunks,),
        in_specs=[
            smem,
            rows_spec(Q, inner),
            rows_spec(Q, n_small),
            whole_spec((8, n_conv)),
            whole_spec((8, LANES)),
            whole_spec((1, inner)),
        ],
        out_specs=[
            rows_spec(Q, inner),
            rows_spec(Q, n_conv),
            rows_spec(Q, 2 * STATE),
            rows_spec(Q, inner),
            pl.BlockSpec((1, STATE, inner), lambda i: (i, 0, 0)),
        ],
        out_shape=[
            jax.ShapeDtypeStruct((group, inner), BF16),
            jax.ShapeDtypeStruct((group, n_conv), BF16),
            jax.ShapeDtypeStruct((group, 2 * STATE), BF16),
            jax.ShapeDtypeStruct((group, inner), BF16),
            jax.ShapeDtypeStruct((chunks, STATE, inner), BF16),
        ],
        scratch_shapes=[pltpu.VMEM((n_conv // LANES, Q + 8, LANES), F32), pltpu.VMEM((STATE, inner), F32)],
        compiler_params=params(),
        cost_estimate=SMALL_COST,
        name="scan_forward",
    )(ends, x_raw, small, taps, par, skip)

    cot_all = in_order(cotangent, other_cot)
    if by_hand:
        turned = turn(after(other_tokens, y_all))
        normed, turned, cot_all = lax.optimization_barrier((normed, turned, after(cot_all, y_all)))
    tile = 512
    columns = lambda rows, shift=0: pl.BlockSpec((rows, tile), lambda j: (0, j + shift))
    fixed = lambda shape: pl.BlockSpec(shape, lambda j: (0, 0))
    tiles = inner // tile
    z_all, gg, sq = pl.pallas_call(
        gate_forward,
        grid=(tiles,),
        in_specs=[fixed((group, depth)), columns(depth), columns(group), columns(8)],
        out_specs=[columns(group), columns(group), fixed((8, group))],
        out_shape=[
            jax.ShapeDtypeStruct((group, inner), BF16),
            jax.ShapeDtypeStruct((group, inner), BF16),
            jax.ShapeDtypeStruct((8, group), F32),
        ],
        scratch_shapes=[pltpu.VMEM((group, LANES), F32)],
        compiler_params=params(),
        cost_estimate=SMALL_COST,
        name="gate_forward",
    )(normed, zo_all, y_all, taps)
    sq_got = swap(sq)

    u_own, u_send, prod = pl.pallas_call(
        branch,
        grid=(depth // tile,),
        in_specs=[
            smem,
            smem,
            fixed((group, inner)),
            columns(own_rows),
            columns(own_rows),
            pl.BlockSpec((tile, inner), lambda j: (j, 1)),
        ],
        out_specs=[columns(own_rows), columns(own_rows), fixed((8, group))],
        out_shape=[
            jax.ShapeDtypeStruct((own_rows, depth), BF16),
            jax.ShapeDtypeStruct((own_rows, depth), BF16),
            jax.ShapeDtypeStruct((8, group), F32),
        ],
        scratch_shapes=[pltpu.VMEM((group, LANES), F32)],
        compiler_params=params(),
        cost_estimate=SMALL_COST,
        name="branch",
    )(me, ends, gg, cotangent, other_cot, zo_all)
    prod_got = swap(prod)
    sq_all = sq + after(sq_got, prod)
    inv_gate8 = lax.rsqrt(sq_all / inner_total + EPSILON)
    inv_gate = inv_gate8[0]
    d_branch = (cot_all.astype(F32) * (live * inv_gate)[:, None]).astype(BF16)
    g_out = lax.dot_general(d_branch, gg, TN, preferred_element_type=F32).astype(BF16)
    grad_out = lax.psum_scatter(g_out, "dp", scatter_dimension=0, tiled=True)
    prod_got = after(prod_got, g_out)
    u_recv = swap(after(u_send, g_out))
    inv_own = lax.dynamic_slice_in_dim(inv_gate, me_t * own_rows, own_rows, 0)
    out_branch = (u_own.astype(F32) + u_recv.astype(F32)) * (inv_own * live_own)[:, None]
    layer_out = (tokens.astype(F32) + out_branch).astype(BF16)

    prod_all = prod + prod_got
    coef8 = inv_gate8 * inv_gate8 * inv_gate8 * (prod_all / inner_total)
    dy, dz, gain_acc = pl.pallas_call(
        gate_backward,
        grid=(tiles,),
        in_specs=[
            smem,
            smem,
            fixed((own_rows, depth)),
            fixed((own_rows, depth)),
            columns(depth, tiles),
            columns(group),
            columns(group),
            fixed((8, group)),
            fixed((8, group)),
            columns(8),
        ],
        out_specs=[columns(group), columns(group), columns(8)],
        out_shape=[
            jax.ShapeDtypeStruct((group, inner), BF16),
            jax.ShapeDtypeStruct((group, inner), BF16),
            jax.ShapeDtypeStruct((8, inner), F32),
        ],
        scratch_shapes=[pltpu.VMEM((group, LANES), F32), pltpu.VMEM((group, LANES), F32)],
        compiler_params=params(),
        cost_estimate=SMALL_COST,
        name="gate_backward",
    )(me, ends, cotangent, other_cot, zo_all, y_all, z_all, inv_gate8, coef8, taps)
    dot = partial(lax.dot_general, preferred_element_type=F32)
    front = depth // 2

    def gradient(d, width):
        outs = pl.BlockSpec((front, width), lambda j: (0, j))
        return pl.pallas_call(
            weight_grad,
            grid=(d.shape[1] // width,),
            in_specs=[fixed((depth, group)), pl.BlockSpec((group, width), lambda j: (0, j))],
            out_specs=[outs, outs],
            out_shape=[jax.ShapeDtypeStruct((front, d.shape[1]), BF16)] * 2,
            compiler_params=params(),
            cost_estimate=SMALL_COST,
            name="weight_grad",
        )(turned, d)

    if by_hand:
        g_send, z_keep = gradient(dz, tile)
        z_got = send(g_send, beside)
        dy = after(dy, z_keep, g_send)
    else:
        grad_z = lax.psum_scatter(dot(normed, dz, TN).astype(BF16), "dp", scatter_dimension=0, tiled=True)

    n_a = inner * 2 // 3
    n_b = inner + n_small - n_a

    def backward(base, width, carry):
        at = base // width
        back = lambda size, column: pl.BlockSpec((Q, size), lambda i: (chunks - 1 - i, column))
        operands = [ends, dy, xc, pre, x_raw, small, bc, states, taps, par, skip, sel]
        in_specs = [
            smem,
            back(width, at),
            back(width, at),
            back(width, at),
            back(width, at),
            back(n_small, 0),
            back(2 * STATE, 0),
            pl.BlockSpec((1, STATE, width), lambda i: (chunks - 1 - i, 0, at)),
            whole_spec((8, width), at),
            whole_spec((8, LANES)),
            whole_spec((1, width), at),
            pl.BlockSpec((width, LANES), lambda i: (at, 0)),
        ]
        tiles_held = width + (2 * STATE if carry else 0)
        acc_shape, hacc_shape = (8 * (K + 2), tiles_held), (16, LANES)
        if carry:
            last = inner // (2 * STATE)
            operands += [pre, taps, *carry]
            in_specs += [back(2 * STATE, last), whole_spec((8, 2 * STATE), last), back(n_small, 0)]
            in_specs += [whole_spec((8 * (K + 2), base)), whole_spec(hacc_shape), whole_spec((8, inner))]
            out_specs = [back(n_b, 0), whole_spec((8, n_conv))]
            out_shape = [jax.ShapeDtypeStruct((group, n_b), BF16), jax.ShapeDtypeStruct((8, n_conv), F32)]
        else:
            out_specs = [back(width, 0), back(n_small, 0)]
            out_shape = [jax.ShapeDtypeStruct((group, width), BF16), jax.ShapeDtypeStruct((group, n_small), F32)]
        return pl.pallas_call(
            partial(scan_backward, base, bool(carry), chunks),
            grid=(chunks,),
            in_specs=in_specs,
            out_specs=out_specs + [whole_spec(acc_shape), whole_spec(hacc_shape)],
            out_shape=out_shape + [jax.ShapeDtypeStruct(acc_shape, F32), jax.ShapeDtypeStruct(hacc_shape, F32)],
            scratch_shapes=[
                pltpu.VMEM((STATE, width), F32),
                pltpu.VMEM((tiles_held // LANES, Q + 8, LANES), F32),
                *[pltpu.VMEM((Q, width), BF16)] * 6,
                pltpu.VMEM((STATE, width), BF16),
                pltpu.VMEM((8, width), F32),
            ],
            compiler_params=params(),
            cost_estimate=SMALL_COST,
            name="scan_backward",
        )(*operands)

    dxa, part, acc, hacc = backward(0, n_a, ())
    if by_hand:
        z_got, dxa = lax.optimization_barrier((z_got, dxa))
        z_away, z_core = fold_away(z_keep, z_got)
        z_got = send(z_away, across)
        dxa, part = lax.optimization_barrier((dxa, part, z_away))[:2]
        g_x, grad_out = lax.optimization_barrier((dot(normed, dxa, TN).astype(BF16), grad_out))
        grad_a = lax.psum_scatter(g_x, "dp", scatter_dimension=0, tiled=True)
        part = after(part, g_x)
    dxb, vector = backward(n_a, inner - n_a, (part, acc, hacc, gain_acc))[:2]
    dxb = after(dxb, u_recv)
    lanes_shared = lax.iota(jnp.int32, n_conv)[None, :] >= inner
    bits_of = lambda turn: [(i, i ^ (1 << turn)) for i in range(n_dp)]
    if by_hand:
        z_got, dxb, vector = lax.optimization_barrier((z_got, dxb, vector))
        z_out = ring_part(z_keep, z_core, z_got, None, 1)
        z_came = send(z_out, around)
        shared_got = swap(vector)
        b_send, b_keep = gradient(after(dxb, z_out), n_b)
        b_got = send(b_send, beside)
        shared_got, z_came, b_keep = lax.optimization_barrier((shared_got, z_came, b_keep))
        vector = vector + jnp.where(lanes_shared, shared_got, 0.0)
        z_out = ring_part(z_keep, z_core, z_got, z_came, 2)
        z_came, vector_got = send(z_out, around), send(vector, bits_of(0))
        dz = after(dz, b_send, b_keep, z_out, vector)
    else:
        dx = jnp.concatenate([dxa, dxb], axis=1)
        grad_x = lax.psum_scatter(dot(normed, dx, TN).astype(BF16), "dp", scatter_dimension=0, tiled=True)

    def back_rows(which, dz):
        pick = lambda width: pl.BlockSpec((own_rows, width), lambda j, rows: (rows[0], 0))
        return pl.pallas_call(
            normed_back,
            grid_spec=pltpu.PrefetchScalarGridSpec(
                num_scalar_prefetch=1,
                grid=(depth // tile,),
                in_specs=[
                    pick(inner),
                    pick(n_a),
                    pick(n_b),
                    pl.BlockSpec((tile, inner), lambda j, rows: (j, 0)),
                    pl.BlockSpec((tile, inner + n_small), lambda j, rows: (j, 0)),
                ],
                out_specs=pl.BlockSpec((own_rows, tile), lambda j, rows: (0, j)),
            ),
            out_shape=jax.ShapeDtypeStruct((own_rows, depth), BF16),
            compiler_params=params(),
            cost_estimate=SMALL_COST,
            name="normed_back",
        )(which, dz, dxa, dxb, zo_all, wx_all)

    dn_send = back_rows(n_t - 1 - me, dz)
    if by_hand:
        w_sum = lambda w, g: jnp.sum(w.astype(F32) * g, axis=1)
        b_got, vector_got, dn_send, z_came = lax.optimization_barrier((b_got, vector_got, dn_send, z_came))
        dn_got = swap(dn_send)
        b_away, b_core = fold_away(b_keep, b_got)
        b_got = send(b_away, across)
        vector = vector + vector_got
        z_out = ring_part(z_keep, z_core, z_got, z_came, 3)
        z_came, vector_got = send(z_out, around), send(vector, bits_of(1))
        dn_own = back_rows(me, after(dz, vector, z_out, b_away))
        vector_got, dn_own, b_got, z_came = lax.optimization_barrier((vector_got, dn_own, b_got, z_came))
        vector = vector + vector_got
        b_out = ring_part(b_keep, b_core, b_got, None, 1)
        b_came, vector_got = send(b_out, around), send(vector, bits_of(2))
        grad_z = ring_part(z_keep, z_core, z_got, z_came, ring) * gain_pair
        in_part = w_sum(w_zx[0], grad_z)
        vector_got, grad_z, in_part, b_came = lax.optimization_barrier((vector_got, grad_z, in_part, b_came))
        vector = vector + vector_got
        b_out = ring_part(b_keep, b_core, b_got, b_came, 2)
        b_came, vector_got = send(b_out, around), send(vector, bits_of(3))
        grad_out = grad_out.astype(F32).T
        vector_got, grad_out, layer_out, b_came = lax.optimization_barrier((vector_got, grad_out, layer_out, b_came))
        vector = vector + vector_got
        b_came = send(ring_part(b_keep, b_core, b_got, b_came, 3), around)
    else:
        vector = sum_dp(vector + jnp.where(lanes_shared, swap(vector), 0.0))
        dn_own = back_rows(me, dz)
        dn_got = swap(dn_send)
        grad_out = grad_out.astype(F32).T
        grad_z, grad_x = grad_z.astype(F32), grad_x.astype(F32)
        in_part = jnp.sum(w_zx[0].astype(F32) * grad_z, axis=1) + jnp.sum(jnp.concatenate([w_x, w_small], axis=1).astype(F32) * grad_x, axis=1)

    me_all = me_dp * n_t + me_t
    bc_sum = vector[: K + 1, inner:].reshape(K + 1, 2, STATE)
    bc_sum = lax.dynamic_slice_in_dim(bc_sum, me_all * span_n, span_n, 2)
    grad_bc_taps = bc_sum[:K].transpose(1, 2, 0).reshape(conv_bc.shape)
    grad_bc_bias = bc_sum[K]
    x_sum = vector[: K + 3, :inner].reshape(K + 3, heads, WIDTH)
    grad_skip = x_sum[K + 1].sum(axis=1)
    x_sum = lax.dynamic_slice_in_dim(x_sum, me_dp * span_p, span_p, 2)
    grad_x_taps = x_sum[:K].transpose(1, 2, 0).reshape(conv_x.shape)
    grad_x_bias = x_sum[K]
    grad_gate = x_sum[K + 2]
    grad_dt_bias = vector[K + 3, :heads]
    grad_a_log = vector[K + 3, LANES : LANES + heads]
    dn = (dn_own.astype(F32) + dn_got.astype(F32)) * gain_in[0:1, :]
    grad_tokens = (
        cotangent.astype(F32)
        + inv_tok * dn
        - tok_own * inv_tok * inv_tok * inv_tok * jnp.mean(dn * tok_own, axis=1, keepdims=True)
    )

    if by_hand:
        grad_b = ring_part(b_keep, b_core, b_got, b_came, ring) * gain_pair
        in_part = in_part + w_sum(w_x[:, n_a:], grad_b[:, : inner - n_a]) + w_sum(w_small, grad_b[:, inner - n_a :])
        outs = (grad_bc_taps, grad_bc_bias, grad_skip, grad_x_taps, grad_x_bias, grad_gate, grad_dt_bias, grad_a_log)
        outs = lax.optimization_barrier((*outs, grad_tokens, grad_b, in_part, grad_a))
        grad_bc_taps, grad_bc_bias, grad_skip, grad_x_taps, grad_x_bias, grad_gate, grad_dt_bias, grad_a_log = outs[:8]
        grad_tokens, grad_b, in_part, grad_a = outs[8:]
        grad_a = grad_a.astype(F32)
        in_part = in_part + w_sum(w_x[:, :n_a], grad_a)
    else:
        grad_a, grad_b = grad_x[:, :n_a], grad_x[:, n_a:]
    at = inner - n_a
    bc_part = jnp.concatenate([grad_b[:, at : at + 2 * STATE], jnp.broadcast_to(in_part[:, None], (shard, LANES))], axis=1)
    grad_zx = jnp.stack([grad_z, jnp.concatenate([grad_a, grad_b[:, :at]], axis=1)])
    grad_dt = grad_b[:, at + 2 * STATE : at + 2 * STATE + heads]
    half = half_bc
    bc_own = lax.dynamic_slice_in_dim(bc_part, me_t * half, half, 0)
    bc_send = lax.dynamic_slice_in_dim(bc_part, (n_t - 1 - me_t) * half, half, 0)
    bc_total = bc_own + swap(bc_send)
    own_gain = norm_gain.astype(F32)
    grad_bc = bc_total[:, : 2 * STATE].reshape(half, 2, STATE).transpose(1, 0, 2)
    grad_in = bc_total[:, 2 * STATE] / own_gain
    return (
        layer_out,
        grad_tokens,
        grad_in,
        grad_zx,
        grad_bc,
        grad_dt,
        grad_x_taps,
        grad_x_bias,
        grad_bc_taps,
        grad_bc_bias,
        grad_dt_bias,
        grad_a_log,
        grad_skip,
        grad_gate,
        grad_out,
    )


def solution(mesh):
    both = ("dp", "tensor")
    in_specs = (
        P(both, None),
        P(both, None),
        P("dp", None),
        P(both),
        P(None, "dp", "tensor"),
        P(None, both, None),
        P("dp", "tensor"),
        P("tensor", "dp"),
        P("tensor", "dp"),
        P(None, both),
        P(None, both),
        P("tensor"),
        P("tensor"),
        P("tensor"),
        P("tensor", "dp"),
        P("tensor", "dp"),
    )
    out_specs = (
        P(both, None),
        P(both, None),
        P(both),
        P(None, "dp", "tensor"),
        P(None, both, None),
        P("dp", "tensor"),
        P("tensor", "dp"),
        P("tensor", "dp"),
        P(None, both),
        P(None, both),
        P("tensor"),
        P("tensor"),
        P("tensor"),
        P("tensor", "dp"),
        P("tensor", "dp"),
    )
    return jax.shard_map(local, mesh=mesh, in_specs=in_specs, out_specs=out_specs, check_vma=False)
```

```python
from functools import partial

import jax
import jax.numpy as jnp
from jax import lax
from jax.experimental import pallas as pl
from jax.experimental.pallas import tpu as pltpu
from jax.sharding import PartitionSpec as P

EPSILON = 1e-05
HIGHEST = lax.Precision.HIGHEST
K = 4
WIDTH = 64
STATE = 128
Q = 128
LANES = 128
LOG2E = 1.4426950408889634
VMEM_LIMIT = 60 * 1024 * 1024
F32 = jnp.float32
BF16 = jnp.bfloat16

NN = (((1,), (0,)), ((), ()))
NT = (((1,), (1,)), ((), ()))
TN = (((0,), (0,)), ((), ()))


def mm(a, b, dims=NN):
    return lax.dot_general(a, b, dims, preferred_element_type=F32)


def mm_exact(a, b, dims=NN):
    return lax.dot_general(a, b, dims, preferred_element_type=F32, precision=HIGHEST)


def iota(shape, dim):
    return lax.broadcasted_iota(jnp.int32, shape, dim)


def segment_of(rows, ends_ref, count):
    total = (rows >= ends_ref[0]).astype(jnp.int32)
    for j in range(1, count):
        total = total + (rows >= ends_ref[j]).astype(jnp.int32)
    return total


def scalar_segment(row, ends_ref, count):
    total = jnp.where(row >= ends_ref[0], 1, 0)
    for j in range(1, count):
        total = total + jnp.where(row >= ends_ref[j], 1, 0)
    return total


def sigmoid(v):
    return 0.5 * jnp.tanh(0.5 * v) + 0.5


def softplus(v):
    return jnp.maximum(v, 0.0) + jnp.log1p(jnp.exp(-jnp.abs(v)))


def chunk_masks(chunk, ends_ref, count):
    base = chunk * Q
    rows = iota((Q, Q), 0) + base
    cols = iota((Q, Q), 1) + base
    row_ids = segment_of(rows, ends_ref, count)
    col_ids = segment_of(cols, ends_ref, count)
    same = row_ids == col_ids
    before_id = jnp.where(chunk == 0, -1, scalar_segment(base - 1, ends_ref, count))
    final_id = scalar_segment(base + Q - 1, ends_ref, count)
    carry = (row_ids == before_id).astype(F32)
    last = (row_ids == final_id).astype(F32)
    passing = jnp.where(before_id == final_id, 1.0, 0.0).astype(F32)
    return rows, cols, row_ids, same, carry, last, passing


def decays(dt_raw, par_ref):
    shifted = dt_raw + par_ref[0:1, :]
    step = softplus(shifted)
    decay_rate = jnp.exp(par_ref[1:2, :])
    return shifted, step, decay_rate


def pair_columns(values, pair, first):
    left = jnp.broadcast_to(values[:, 2 * pair : 2 * pair + 1], (Q, LANES))
    right = jnp.broadcast_to(values[:, 2 * pair + 1 : 2 * pair + 2], (Q, LANES))
    return left, right, jnp.where(first, left, right)


def scan_forward(
    heads, ends_ref, xr_ref, small_ref, taps_ref, par_ref, skip_ref,
    xc_ref, pre_ref, bc_ref, y_ref, st_ref, buf, state,
):
    count = ends_ref.shape[0]
    inner = heads * WIDTH
    chunk = pl.program_id(0)

    @pl.when(chunk == 0)
    def _():
        buf[:, 0:8, :] = jnp.zeros((buf.shape[0], 8, LANES), F32)
        state[...] = jnp.zeros(state.shape, F32)

    rows, cols, row_ids, same, carry, last, passing = chunk_masks(chunk, ends_ref, count)
    causal = rows >= cols
    visible = same & causal
    lag_mask = [None]
    for lag in range(1, K):
        earlier = rows - lag
        keep = (segment_of(earlier, ends_ref, count) == row_ids) & (earlier >= 0)
        lag_mask.append(keep.astype(F32))

    small = small_ref[...]

    def convolve(lo, raw):
        span = slice(lo, lo + LANES)
        place = lo // LANES
        buf[place, 8 : 8 + Q, :] = raw
        pre = taps_ref[K : K + 1, span] + taps_ref[K - 1 : K, span] * raw
        for lag in range(1, K):
            pre = pre + taps_ref[K - 1 - lag : K - lag, span] * (
                buf[place, 8 - lag : 8 - lag + Q, :] * lag_mask[lag]
            )
        buf[place, 0:8, :] = raw[Q - 8 : Q, :]
        pre_ref[:, span] = pre.astype(BF16)
        return pre * sigmoid(pre)

    b_f = convolve(inner, small[:, :STATE]).astype(BF16).astype(F32)
    c_b = convolve(inner + STATE, small[:, STATE : 2 * STATE]).astype(BF16)
    b_b = b_f.astype(BF16)
    bc_ref[:, :STATE] = b_b
    bc_ref[:, STATE:] = c_b
    b_t = b_f.T.astype(BF16)

    _, step, decay_rate = decays(small[:, 2 * STATE :], par_ref)
    csum = mm_exact(causal.astype(F32), step * (-LOG2E * decay_rate))
    csum_t = csum.T
    scores = jnp.where(visible, mm(c_b, b_b, NT), 0.0)
    first = iota((Q, LANES), 1) < WIDTH
    first_row = iota((1, LANES), 1) < WIDTH

    wide = 2 * LANES
    for quad in range(0, inner, wide):
        block = slice(quad, quad + wide)
        held = state[:, block]
        held_b = held.astype(BF16)
        st_ref[0, :, block] = held_b
        carried = mm(c_b, held_b)
        weighted, kept = [], []
        for part in range(0, wide, LANES):
            lo = quad + part
            pair = lo // LANES
            span = slice(lo, lo + LANES)
            xc = convolve(lo, xr_ref[:, span].astype(F32)).astype(BF16)
            xc_ref[:, span] = xc
            xc = xc.astype(F32)
            left, right, both = pair_columns(csum, pair, first)
            _, _, step_pair = pair_columns(step, pair, first)
            mix = jnp.concatenate(
                [
                    (scores * jnp.exp2(jnp.minimum(left - csum_t[2 * pair : 2 * pair + 1, :], 0.0))).astype(BF16),
                    (scores * jnp.exp2(jnp.minimum(right - csum_t[2 * pair + 1 : 2 * pair + 2, :], 0.0))).astype(BF16),
                ],
                axis=1,
            )
            fed_b = (xc * step_pair).astype(BF16)
            zero = jnp.zeros((Q, LANES), BF16)
            stacked = jnp.concatenate([jnp.where(first, fed_b, zero), jnp.where(first, zero, fed_b)], axis=0)
            y = mm(mix, stacked) + carried[:, part : part + LANES] * (jnp.exp2(both) * carry)
            y_ref[:, span] = (y + skip_ref[:, span] * xc).astype(BF16)
            closing = both[Q - 1 : Q, :]
            weighted.append((fed_b.astype(F32) * (jnp.exp2(closing - both) * last)).astype(BF16))
            kept.append(jnp.exp2(closing) * passing)
        fresh = mm(b_t, jnp.concatenate(weighted, axis=1))
        state[:, block] = held * jnp.concatenate(kept, axis=1) + fresh


def scan_backward(
    base, last_call, chunks, ends_ref, dy_ref, xc_ref, pre_ref, xr_ref, small_ref, bc_ref, st_ref, taps_ref,
    par_ref, skip_ref, sel_ref, *refs,
):
    if last_call:
        pre_bc_ref, taps_bc_ref, part_in, acc_in, hacc_in, gain_acc_ref = refs[:6]
        dx_ref, rows_ref, acc_ref, hacc_ref = refs[6:10]
        refs = refs[10:]
    else:
        dx_ref, part_ref, acc_ref, hacc_ref = refs[:4]
        refs = refs[4:]
    dstate, dpre, ab_hi, ab_lo, v_b, u_b, dyd, fedw, dst_b, through = refs
    count = ends_ref.shape[0]
    inner = dy_ref.shape[1]
    total_rows = chunks * Q
    chunk = chunks - 1 - pl.program_id(0)

    @pl.when(pl.program_id(0) == 0)
    def _():
        dpre[:, Q : Q + 8, :] = jnp.zeros((dpre.shape[0], 8, LANES), F32)
        dstate[...] = jnp.zeros(dstate.shape, F32)
        acc_ref[...] = jnp.zeros(acc_ref.shape, F32)
        hacc_ref[...] = hacc_in[...] if last_call else jnp.zeros(hacc_ref.shape, F32)

    rows, cols, row_ids, same, carry, last, passing = chunk_masks(chunk, ends_ref, count)
    causal = rows >= cols
    visible = same & causal
    lag_mask = [None]
    for lag in range(1, K):
        later = rows + lag
        keep = (segment_of(later, ends_ref, count) == row_ids) & (later < total_rows)
        lag_mask.append(keep.astype(F32))

    small = small_ref[...]
    shifted, step, decay_rate = decays(small[:, 2 * STATE :], par_ref)
    csum = mm_exact(causal.astype(F32), step * (-LOG2E * decay_rate))
    csum_t = csum.T
    b_b = bc_ref[:, :STATE]
    c_b = bc_ref[:, STATE:]
    c_t = c_b.astype(F32).T.astype(BF16)
    scores = jnp.where(visible, mm(c_b, b_b, NT), 0.0)
    first = iota((Q, LANES), 1) < WIDTH

    def fold(values):
        return values.reshape(Q // 8, 8, values.shape[1]).sum(axis=0)

    def conv_back(lo, d_conv, raw, pre, taps, at):
        span = slice(lo, lo + LANES)
        place = lo // LANES
        gate = sigmoid(pre)
        d_pre = d_conv * (gate * (1.0 + pre * (1.0 - gate)))
        dpre[place, 0:Q, :] = d_pre
        d_raw = taps[K - 1 : K, at] * d_pre
        acc_ref[8 * (K - 1) : 8 * K, span] += fold(d_pre * raw)
        acc_ref[8 * K : 8 * K + 8, span] += fold(d_pre)
        for lag in range(1, K):
            moved = dpre[place, lag : lag + Q, :] * lag_mask[lag]
            d_raw = d_raw + taps[K - 1 - lag : K - lag, at] * moved
            acc_ref[8 * (K - 1 - lag) : 8 * (K - lag), span] += fold(moved * raw)
        dpre[place, Q : Q + 8, :] = d_pre[0:8, :]
        dx_ref[:, span] = d_raw.astype(BF16)

    d_scores = jnp.zeros((Q, Q), F32)
    wide = 2 * LANES
    for quad in range(0, inner, wide):
        block = slice(quad, quad + wide)
        held_b = st_ref[0, :, block]
        d_held = dstate[:, block]
        d_held_b = d_held.astype(BF16)
        dst_b[:, block] = d_held_b
        carried = mm(c_b, held_b)
        returned = mm(b_b, d_held_b)
        crossing = (d_held * held_b.astype(F32)).reshape(STATE // 8, 8, wide).sum(axis=0)
        grown_parts, kept_parts = [], []
        for part in range(0, wide, LANES):
            lo = quad + part
            pair = (base + lo) // LANES
            span = slice(lo, lo + LANES)
            xc = xc_ref[:, span].astype(F32)
            dy_b = dy_ref[:, span]
            dy = dy_b.astype(F32)
            left, right, both = pair_columns(csum, pair, first)
            _, _, step_pair = pair_columns(step, pair, first)
            fall_left = jnp.exp2(jnp.minimum(left - csum_t[2 * pair : 2 * pair + 1, :], 0.0))
            fall_right = jnp.exp2(jnp.minimum(right - csum_t[2 * pair + 1 : 2 * pair + 2, :], 0.0))
            mix = jnp.concatenate([(scores * fall_left).astype(BF16), (scores * fall_right).astype(BF16)], axis=1)
            fed_b = (xc * step_pair).astype(BF16)
            fed = fed_b.astype(F32)
            zero = jnp.zeros((Q, LANES), BF16)
            stacked = jnp.concatenate([jnp.where(first, fed_b, zero), jnp.where(first, zero, fed_b)], axis=0)
            grown = jnp.exp2(both) * carry
            y = mm(mix, stacked) + carried[:, part : part + LANES] * grown
            d_mix = mm(dy_b, stacked, NT)
            d_scores = d_scores + d_mix[:, :Q] * fall_left + d_mix[:, Q:] * fall_right
            d_fed2 = mm(mix, dy_b, TN)
            d_fed_in = jnp.where(first, d_fed2[:Q], d_fed2[Q:])
            closing = both[Q - 1 : Q, :]
            shrink = jnp.exp2(closing - both) * last
            d_fed_out = returned[:, part : part + LANES] * shrink
            d_fed = d_fed_in + d_fed_out
            straddle = dy * y - fed * d_fed_in
            hi = straddle.astype(BF16)
            ab_hi[:, span] = hi
            ab_lo[:, span] = (straddle - hi.astype(F32)).astype(BF16)
            v_b[:, span] = (fed * d_fed_out).astype(BF16)
            u_b[:, span] = (xc * d_fed).astype(BF16)
            fedw[:, span] = (fed * shrink).astype(BF16)
            grown_parts.append((dy * grown).astype(BF16))
            kept_parts.append(jnp.exp2(closing) * passing)
            acc_ref[8 * K + 8 : 8 * K + 16, span] += fold(dy * xc)
            d_conv = d_fed * step_pair + skip_ref[:, span] * dy
            conv_back(lo, d_conv, xr_ref[:, span].astype(F32), pre_ref[:, span].astype(F32), taps_ref, span)
        dy_grown = jnp.concatenate(grown_parts, axis=1)
        kept = jnp.concatenate(kept_parts, axis=1)
        dyd[:, block] = dy_grown
        through[:, block] = crossing * kept
        dstate[:, block] = d_held * kept + mm(c_t, dy_grown)

    d_scores_b = jnp.where(visible, d_scores, 0.0).astype(BF16)
    d_c = mm(dyd[...], st_ref[0], NT) + mm(d_scores_b, b_b)
    d_b = mm(fedw[...], dst_b[...], NT) + mm(d_scores_b, c_b, TN)
    sel = sel_ref[...]
    red_ab = mm(ab_hi[...], sel) + mm(ab_lo[...], sel)
    red_v = mm(v_b[...], sel)
    red_u = mm(u_b[...], sel)
    thr = through[...]
    thr_hi = thr.astype(BF16)
    red_t = mm(thr_hi, sel) + mm((thr - thr_hi.astype(F32)).astype(BF16), sel)
    d_rate = (
        mm_exact((same & (cols >= rows)).astype(F32), red_ab)
        + mm_exact((same & (cols < rows)).astype(F32), red_v)
        + jnp.sum(red_t, axis=0, keepdims=True)
    )
    d_step = red_u - d_rate * decay_rate
    d_dt = d_step * sigmoid(shifted)
    hacc_ref[0:8, :] += fold(d_dt)
    hacc_ref[8:16, :] += fold(d_rate * (-decay_rate * step))
    if not last_call:
        part_ref[:, :STATE] = d_b
        part_ref[:, STATE : 2 * STATE] = d_c
        part_ref[:, 2 * STATE :] = d_dt
        return

    for k, d_conv in enumerate((d_b, d_c)):
        at = slice(k * STATE, (k + 1) * STATE)
        pre = pre_bc_ref[:, at].astype(F32)
        conv_back(inner + k * STATE, d_conv + part_in[:, at], small[:, at], pre, taps_bc_ref, at)
    dx_ref[:, inner + 2 * STATE :] = (d_dt + part_in[:, 2 * STATE :]).astype(BF16)

    @pl.when(pl.program_id(0) == pl.num_programs(0) - 1)
    def _():
        before = acc_in.shape[1]
        whole = before + inner
        rows_ref[...] = jnp.zeros(rows_ref.shape, F32)
        for k in range(K + 2):
            block = slice(8 * k, 8 * k + 8)
            rows_ref[k : k + 1, :before] = jnp.sum(acc_in[block, :], axis=0, keepdims=True)
            rows_ref[k : k + 1, before:] = jnp.sum(acc_ref[block, :], axis=0, keepdims=True)
        rows_ref[K + 2 : K + 3, :whole] = jnp.sum(gain_acc_ref[...], axis=0, keepdims=True)
        for k in range(2):
            total = jnp.sum(hacc_ref[8 * k : 8 * k + 8, :], axis=0, keepdims=True)
            rows_ref[K + 3 : K + 4, k * LANES : (k + 1) * LANES] = total


def load_blocks(offsets_ref, parts, whole, sems, size, columns, first=0):
    @pl.when(pl.program_id(0) == 0)
    def _():
        copies = []
        for part in parts:
            for j in range(part.shape[0] // size):
                k = first + len(copies)
                start = 0 if size == whole.shape[0] else pl.multiple_of(offsets_ref[k], 32)
                source = part.at[pl.ds(j * size, size), :]
                copies.append(pltpu.make_async_copy(source, whole.at[pl.ds(start, size), slice(*columns)], sems.at[k]))
        for copy in copies:
            copy.start()
        for copy in copies:
            copy.wait()


def turn_rows(offsets_ref, source_ref, out_ref, turned):
    rows, depth = source_ref.shape
    for lo in range(0, rows, Q):
        tile = source_ref[lo : lo + Q, :].astype(F32)
        tile = tile * lax.rsqrt(jnp.mean(tile * tile, axis=1, keepdims=True) + EPSILON)
        for left in range(0, depth, LANES):
            turned[left : left + LANES, lo : lo + Q] = tile[:, left : left + LANES].T.astype(BF16)
    count = offsets_ref.shape[0]
    size = depth // count
    for k in range(count):
        start = pl.multiple_of(offsets_ref[k], 32)
        out_ref[k * size : (k + 1) * size, :] = turned[pl.ds(start, size), :]


def project(counts, heads, size, offsets_ref, me_ref, own_ref, other_ref, place_ref, *refs):
    count = sum(counts)
    blocks, (x_ref, small_ref, normed_ref, taps_ref, gain_ref, w_out_ref, w_ref, sems, out_sem) = refs[:count], refs[count:]
    split = x_ref.shape[1]
    shards = w_ref.shape[0] // size
    load_blocks(offsets_ref, blocks[: counts[0]], w_ref, sems, size, (0, split))
    load_blocks(offsets_ref, blocks[counts[0] :], w_ref, sems, size, (split, w_ref.shape[1]), shards)
    keep = pltpu.make_async_copy(w_ref, w_out_ref, out_sem)
    depth, inner = w_ref.shape[0], x_ref.shape[1]
    tile = 512

    @pl.when(pl.program_id(0) == 0)
    def _():
        keep.start()
        spare = w_ref[:, inner + 2 * STATE :]
        turned = spare.astype(F32).T
        gain_ref[...] = jnp.broadcast_to(turned[heads + K + 2 : heads + K + 3, :], gain_ref.shape)
        few = turned[heads : heads + 16, :].astype(BF16)
        lanes = iota((depth, LANES), 1)
        for lo in range(0, inner + 2 * STATE, LANES):
            if lo < inner:
                wanted, row = place_ref[:, :LANES] == lanes + lo, 0
            else:
                wanted, row = place_ref[:, LANES:] == lanes + (lo - inner), 8
            moved = mm(few, jnp.where(wanted, 1.0, 0.0).astype(BF16))
            taps_ref[:, lo : lo + LANES] = moved[row : row + 8, :]

    rows = jnp.where(pl.program_id(0) == me_ref[0], own_ref[...], other_ref[...]).astype(F32)
    scale = lax.rsqrt(jnp.mean(rows * rows, axis=1, keepdims=True) + EPSILON)
    rows = (rows * scale * gain_ref[0:1, :]).astype(BF16)
    normed_ref[...] = rows
    for lo in range(0, inner, tile):
        x_ref[:, lo : lo + tile] = mm(rows, w_ref[:, lo : lo + tile]).astype(BF16)
    small_ref[...] = mm(rows, w_ref[:, inner:])

    @pl.when(pl.program_id(0) == pl.num_programs(0) - 1)
    def _():
        keep.wait()


def row_sums(lanes):
    return mm_exact(jnp.ones((8, LANES), F32), lanes, NT)


def spread_rows(values):
    pick = jnp.where(iota((8, LANES), 0) == 0, 1.0, 0.0).astype(F32)
    return mm_exact(values, pick, TN)


def gate_forward(normed_ref, w_ref, y_ref, gain_ref, z_ref, gg_ref, sq_ref, square):
    rows, width = z_ref.shape
    size = 512

    @pl.when(pl.program_id(0) == 0)
    def _():
        square[...] = jnp.zeros(square.shape, F32)

    for lo in range(0, rows, size):
        at = slice(lo, lo + size)
        z = mm(normed_ref[at, :], w_ref[...]).astype(BF16)
        z_ref[at, :] = z
        z = z.astype(F32)
        gated = y_ref[at, :].astype(F32) * (z * sigmoid(z))
        gg_ref[at, :] = (gated * gain_ref[K + 1 : K + 2, :]).astype(BF16)
        twice = gated * gated
        for part in range(0, width, LANES):
            square[at, :] += twice[:, part : part + LANES]

    @pl.when(pl.program_id(0) == pl.num_programs(0) - 1)
    def _():
        sq_ref[...] = row_sums(square[...])


def branch(me_ref, ends_ref, gg_ref, own_ref, other_ref, w_ref, mine_ref, away_ref, prod_ref, product):
    rows, width = mine_ref.shape
    size = 512

    @pl.when(pl.program_id(0) == 0)
    def _():
        product[...] = jnp.zeros(product.shape, F32)

    for index, (out_ref, cot_ref) in enumerate(((mine_ref, own_ref), (away_ref, other_ref))):
        first = jnp.where(index == 0, me_ref[0], 1 - me_ref[0]) * rows
        for lo in range(0, rows, size):
            at = pl.ds(pl.multiple_of(first + lo, size), size)
            u = mm(gg_ref[at, :], w_ref[...], NT)
            out_ref[lo : lo + size, :] = u.astype(BF16)
            term = u * cot_ref[lo : lo + size, :].astype(F32)
            for part in range(0, width, LANES):
                product[at, :] += term[:, part : part + LANES]

    @pl.when(pl.program_id(0) == pl.num_programs(0) - 1)
    def _():
        live = iota(product.shape, 0) < ends_ref[ends_ref.shape[0] - 1]
        prod_ref[...] = row_sums(jnp.where(live, product[...], 0.0))


def gate_backward(
    me_ref, ends_ref, own_ref, other_ref, w_ref, y_ref, z_ref, rg_ref, coef_ref, gain_ref,
    dy_ref, dz_ref, acc_ref, rg, coef,
):
    total, width = dy_ref.shape
    rows = own_ref.shape[0]
    size = 512

    @pl.when(pl.program_id(0) == 0)
    def _():
        live = iota(rg.shape, 0) < ends_ref[ends_ref.shape[0] - 1]
        rg[...] = spread_rows(rg_ref[...])
        coef[...] = spread_rows(coef_ref[...])
        rg[...] = jnp.where(live, rg[...], 0.0)

    gain = gain_ref[K + 1 : K + 2, :]
    sums = jnp.zeros((8, width), F32)
    for index, cot_ref in enumerate((own_ref, other_ref)):
        first = jnp.where(index == 0, me_ref[0], 1 - me_ref[0]) * rows
        for lo in range(0, rows, size):
            at = pl.ds(pl.multiple_of(first + lo, size), size)
            ds = mm(cot_ref[lo : lo + size, :], w_ref[...])
            z = z_ref[at, :].astype(F32)
            y = y_ref[at, :].astype(F32)
            scale = jnp.concatenate([rg[at, :]] * (width // LANES), axis=1)
            back = jnp.concatenate([coef[at, :]] * (width // LANES), axis=1)
            gate = sigmoid(z)
            silu = z * gate
            gated = y * silu
            d_normal = ds * scale
            sums = sums + (d_normal * gated).reshape(size // 8, 8, width).sum(axis=0)
            d_gated = d_normal * gain - gated * back
            dy_ref[at, :] = (d_gated * silu).astype(BF16)
            dz_ref[at, :] = (d_gated * y * (gate + silu * (1.0 - gate))).astype(BF16)
    acc_ref[...] = sums


def weight_grad(me_ref, own_ref, other_ref, d_ref, away_ref, keep_ref):
    half, rows = away_ref.shape[0], own_ref.shape[1]
    mine = d_ref[pl.ds(pl.multiple_of(me_ref[0] * rows, rows), rows), :]
    theirs = d_ref[pl.ds(pl.multiple_of((1 - me_ref[0]) * rows, rows), rows), :]
    for at, ref in ((0, away_ref), (half, keep_ref)):
        total = mm(own_ref[at : at + half, :], mine) + mm(other_ref[at : at + half, :], theirs)
        ref[...] = total.astype(BF16)


def normed_back(rows_ref, dz_ref, dxa_ref, dxb_ref, wz_ref, wx_ref, out_ref):
    n_a = dxa_ref.shape[1]
    total = mm(dz_ref[...], wz_ref[...], NT)
    total = total + mm(dxa_ref[...], wx_ref[:, :n_a], NT) + mm(dxb_ref[...], wx_ref[:, n_a:], NT)
    out_ref[...] = total.astype(BF16)


def params():
    return pltpu.CompilerParams(dimension_semantics=("arbitrary",), vmem_limit_bytes=VMEM_LIMIT)


SMALL_COST = pl.CostEstimate(flops=1000, bytes_accessed=1000, transcendentals=0)


def rows_spec(block, width, column=0):
    return pl.BlockSpec((block, width), lambda i: (i, column))


def whole_spec(shape, column=0):
    return pl.BlockSpec(shape, lambda i: (0, column))


def local(
    tokens,
    cotangent,
    lengths,
    norm_gain,
    w_zx,
    w_bc,
    w_dt,
    conv_x,
    conv_x_bias,
    conv_bc,
    conv_bc_bias,
    dt_bias,
    a_log,
    d_skip,
    gate_gain,
    w_out,
):
    n_t = lax.axis_size("tensor")
    n_dp = lax.axis_size("dp")
    me_t = lax.axis_index("tensor")
    me_dp = lax.axis_index("dp")
    own_rows, depth = tokens.shape
    group = own_rows * n_t
    chunks = group // Q
    heads = dt_bias.shape[0]
    inner = heads * WIDTH
    inner_total = inner * n_t
    shard = w_zx.shape[1]
    pairs = [(i, n_t - 1 - i) for i in range(n_t)]

    def swap(v):
        return lax.ppermute(v, "tensor", pairs)

    def in_order(mine, other, axis=0):
        low = jnp.where(me_t == 0, mine, other)
        high = jnp.where(me_t == 0, other, mine)
        return jnp.concatenate([low, high], axis=axis)

    def sum_dp(v):
        step = 1
        while step < n_dp:
            v = v + lax.ppermute(v, "dp", [(i, i ^ step) for i in range(n_dp)])
            step *= 2
        return v

    def after(value, *others):
        return lax.optimization_barrier((value, *others))[0]

    ring = 4
    plane = n_dp // (2 * ring)

    around = [(i, (i + 2 * plane) % n_dp) for i in range(n_dp)]
    across = [(i, i ^ 2) for i in range(n_dp)]
    beside = [(i, i ^ 1) for i in range(n_dp)]

    def send(v, way):
        return lax.ppermute(v, "dp", way)

    by_hand = plane == 2 and shard % 32 == 0

    def whole(v):
        return [lax.all_gather(v, "dp", axis=0, tiled=True)]

    def relative_order():
        level, side, core = me_dp // 4, (me_dp // 2) % 2, me_dp % 2
        order = []
        for dc in (1, 0):
            for dy in (1, 0):
                for dz in range(1, ring + 1):
                    order.append(((level - dz + ring) % ring) * 4 + (side ^ dy) * 2 + (core ^ dc))
        return order

    def fold_away(keep, got):
        half = keep.shape[0] // 2
        return (keep[:half].astype(F32) + got[:half].astype(F32)).astype(BF16), got

    def ring_part(keep, core, got, came, turn):
        low, high = (turn - 1) * shard, turn * shard
        half = keep.shape[0] // 2
        part = keep[half + low : half + high].astype(F32) + core[half + low : half + high].astype(F32)
        part = part + got[low:high].astype(F32)
        if came is not None:
            part = part + came.astype(F32)
        return part if turn == ring else part.astype(BF16)

    ends = jnp.cumsum(lengths[0]).astype(jnp.int32)
    live = (lax.iota(jnp.int32, group) < ends[-1]).astype(F32)
    live_own = lax.dynamic_slice_in_dim(live, me_t * own_rows, own_rows, 0)
    me = me_t.astype(jnp.int32).reshape(1)

    span_p = conv_x_bias.shape[1]
    span_n = conv_bc_bias.shape[1]
    half_bc = w_bc.shape[1]
    bits = jnp.concatenate([norm_gain, conv_bc.reshape(-1), conv_bc_bias.reshape(-1)])
    bits = jnp.pad(bits, (0, LANES - bits.shape[0]))
    tiny = jnp.concatenate([w_bc.reshape(2 * half_bc, STATE), bits[None]], axis=0)
    other_tiny = swap(tiny)
    other_bc = other_tiny[: 2 * half_bc].reshape(w_bc.shape)
    both_bits = [bits, other_tiny[2 * half_bc]]
    at = norm_gain.shape[0]
    gain_pair = in_order(*[v[:at] for v in both_bits])[:, None]
    taps_bc = in_order(*[v[at : at + conv_bc.size].reshape(2, span_n, K) for v in both_bits], axis=1)
    at += conv_bc.size
    bias_bc = in_order(*[v[at : at + 2 * span_n].reshape(2, span_n, 1) for v in both_bits], axis=1)
    spare_bc = jnp.concatenate([taps_bc, bias_bc], axis=2).reshape(4 * span_n, K + 1)
    spare_x = [conv_x.reshape(shard, K), conv_x_bias.reshape(shard, 1), gate_gain.reshape(shard, 1), gain_pair]
    bc_pair = in_order(w_bc, other_bc, axis=1)
    w_x = w_zx[1]
    w_small = jnp.concatenate(
        [bc_pair[0], bc_pair[1], w_dt, *spare_x, jnp.zeros((shard, 8 - K - 3), BF16)]
        + [jnp.pad(spare_bc, ((0, shard - 4 * span_n), (0, LANES - heads - 8 - K - 1)))],
        axis=1,
    )
    gain_pair = gain_pair.astype(F32)
    where = after(lax.iota(jnp.int32, depth), w_small)
    home, inside = where // shard, where % shard
    place_x = (inside // span_p) * WIDTH + home * span_p + inside % span_p
    half_n = 2 * span_n
    place_bc = (inside // half_n) * STATE + home * half_n + inside % half_n
    place = jnp.concatenate([jnp.broadcast_to(v[:, None], (depth, LANES)) for v in (place_x, place_bc)], axis=1)
    par = jnp.concatenate([dt_bias[None], a_log[None], jnp.zeros((6, heads), F32)], axis=0)
    par = jnp.concatenate([par, jnp.zeros((8, LANES - heads), F32)], axis=1)
    skip = jnp.repeat(d_skip, WIDTH)[None]
    members = lax.iota(jnp.int32, inner)[:, None] // WIDTH
    sel = (members == lax.iota(jnp.int32, LANES)[None, :]).astype(BF16)
    smem = pl.BlockSpec(memory_space=pltpu.SMEM)
    vmem = pl.BlockSpec(memory_space=pltpu.VMEM)
    hbm = pl.BlockSpec(memory_space=pl.ANY)
    n_small = 2 * STATE + LANES
    n_conv = inner + 2 * STATE
    w_rest = jnp.concatenate([w_zx[0], w_out.T], axis=1)

    def turn(rows):
        return pl.pallas_call(
            turn_rows,
            in_specs=[smem, vmem],
            out_specs=vmem,
            out_shape=jax.ShapeDtypeStruct((depth, own_rows), BF16),
            scratch_shapes=[pltpu.VMEM((depth, own_rows), BF16)],
            compiler_params=pltpu.CompilerParams(vmem_limit_bytes=VMEM_LIMIT),
            cost_estimate=SMALL_COST,
            name="turn_rows",
        )((jnp.stack(relative_order()) * shard).astype(jnp.int32), rows)

    def place_of(turn, side, core):
        level = (me_dp // (2 * plane) - turn + ring) % ring
        return (level * (2 * plane) + ((me_dp % (2 * plane)) ^ (2 * side + core))) * shard

    together = lambda *values: list(lax.optimization_barrier(tuple(values)))
    joined = lambda *values: jnp.concatenate(values, axis=0)
    if by_hand:
        shift = lambda k: [(i, (i + 2 * plane * k) % n_dp) for i in range(n_dp)]
        l1, o0, c0, t0 = together(send(w_x, around), send(w_x, across), send(w_x, beside), swap(tokens[:160]))
        late, w_small = together(tokens, w_small, l1, o0, c0)[:2]
        l2, o1, s1, s2, s3, turned_own = together(
            send(l1, around), send(l1, across), send(w_small, shift(1)), send(w_small, shift(2)), send(w_small, shift(3)),
            turn(late),
        )
        w_rest = after(jnp.concatenate([w_zx[0], w_out.T], axis=1), l2)
        zo_all = lax.all_gather(w_rest, "dp", axis=0, tiled=True)
        small_line = joined(w_small, s1, s2, s3)
        l3, o2, c1, small_across, t1 = together(
            send(l2, around), send(l2, across), send(joined(l1, o0), beside), send(small_line, across), swap(late[160:336])
        )
        o3, c2, small_beside, t2, place, par, skip, sel = together(
            send(l3, across), send(joined(l2, o1), beside), send(joined(small_line, small_across), beside),
            swap(after(late[336:], t1)), place, par, skip, sel,
        )
        other_tokens = joined(t0, t1, t2)
        c3, turned_other, other_tokens = together(send(joined(l3, o2, o3), beside), turn(other_tokens), other_tokens)
        other_cot = swap(after(cotangent, other_tokens))
        wx_parts = [w_x, l1, l2, l3, o0, o1, o2, o3, c0, c1, c2, c3]
        order = [(t, 0, 0) for t in range(4)] + [(t, 1, 0) for t in range(4)]
        order += [(0, 0, 1), (1, 0, 1), (0, 1, 1), (2, 0, 1), (1, 1, 1), (3, 0, 1), (2, 1, 1), (3, 1, 1)]
        small_parts = [small_line, small_across, small_beside]
        order += [(t, side, core) for core in range(2) for side in range(2) for t in range(4)]
        offsets = jnp.stack([place_of(*key) for key in order]).astype(jnp.int32)
    else:
        wx_parts, small_parts = whole(w_x), whole(w_small)
        zo_all = whole(jnp.concatenate([w_zx[0], w_out.T], axis=1))[0]
        other_tokens, other_cot = swap(tokens), swap(cotangent)
        offsets = jnp.zeros((2,), jnp.int32)
    counts = (len(wx_parts), len(small_parts))
    sems = pltpu.SemaphoreType.DMA((offsets.shape[0],))
    tok_own = tokens.astype(F32)
    inv_tok = lax.rsqrt(jnp.mean(tok_own * tok_own, axis=1, keepdims=True) + EPSILON)

    block = own_rows
    steps = group // block
    x_raw, small, normed, taps, gain_in, wx_all = pl.pallas_call(
        partial(project, counts, heads, shard if by_hand else depth),
        grid=(steps,),
        in_specs=[
            smem,
            smem,
            whole_spec((block, depth)),
            whole_spec((block, depth)),
            whole_spec((depth, 2 * LANES)),
        ]
        + [hbm] * sum(counts),
        out_specs=[
            rows_spec(block, inner),
            rows_spec(block, n_small),
            rows_spec(block, depth),
            whole_spec((8, n_conv)),
            whole_spec((8, depth)),
            hbm,
        ],
        out_shape=[
            jax.ShapeDtypeStruct((group, inner), BF16),
            jax.ShapeDtypeStruct((group, n_small), F32),
            jax.ShapeDtypeStruct((group, depth), BF16),
            jax.ShapeDtypeStruct((8, n_conv), F32),
            jax.ShapeDtypeStruct((8, depth), F32),
            jax.ShapeDtypeStruct((depth, inner + n_small), BF16),
        ],
        scratch_shapes=[pltpu.VMEM((depth, inner + n_small), BF16), sems, pltpu.SemaphoreType.DMA],
        compiler_params=params(),
        cost_estimate=SMALL_COST,
        name="project",
    )(offsets, me, tokens, other_tokens, place, *wx_parts, *small_parts)
    xc, pre, bc, y_all, states = pl.pallas_call(
        partial(scan_forward, heads),
        grid=(chunks,),
        in_specs=[
            smem,
            rows_spec(Q, inner),
            rows_spec(Q, n_small),
            whole_spec((8, n_conv)),
            whole_spec((8, LANES)),
            whole_spec((1, inner)),
        ],
        out_specs=[
            rows_spec(Q, inner),
            rows_spec(Q, n_conv),
            rows_spec(Q, 2 * STATE),
            rows_spec(Q, inner),
            pl.BlockSpec((1, STATE, inner), lambda i: (i, 0, 0)),
        ],
        out_shape=[
            jax.ShapeDtypeStruct((group, inner), BF16),
            jax.ShapeDtypeStruct((group, n_conv), BF16),
            jax.ShapeDtypeStruct((group, 2 * STATE), BF16),
            jax.ShapeDtypeStruct((group, inner), BF16),
            jax.ShapeDtypeStruct((chunks, STATE, inner), BF16),
        ],
        scratch_shapes=[pltpu.VMEM((n_conv // LANES, Q + 8, LANES), F32), pltpu.VMEM((STATE, inner), F32)],
        compiler_params=params(),
        cost_estimate=SMALL_COST,
        name="scan_forward",
    )(ends, x_raw, small, taps, par, skip)

    cot_all = in_order(cotangent, other_cot)
    if by_hand:
        normed, cot_all = lax.optimization_barrier((normed, after(cot_all, y_all)))
    tile = 512
    columns = lambda rows, shift=0: pl.BlockSpec((rows, tile), lambda j: (0, j + shift))
    fixed = lambda shape: pl.BlockSpec(shape, lambda j: (0, 0))
    tiles = inner // tile
    z_all, gg, sq = pl.pallas_call(
        gate_forward,
        grid=(tiles,),
        in_specs=[fixed((group, depth)), columns(depth), columns(group), columns(8)],
        out_specs=[columns(group), columns(group), fixed((8, group))],
        out_shape=[
            jax.ShapeDtypeStruct((group, inner), BF16),
            jax.ShapeDtypeStruct((group, inner), BF16),
            jax.ShapeDtypeStruct((8, group), F32),
        ],
        scratch_shapes=[pltpu.VMEM((group, LANES), F32)],
        compiler_params=params(),
        cost_estimate=SMALL_COST,
        name="gate_forward",
    )(normed, zo_all, y_all, taps)
    sq_got = swap(sq)

    u_own, u_send, prod = pl.pallas_call(
        branch,
        grid=(depth // tile,),
        in_specs=[
            smem,
            smem,
            fixed((group, inner)),
            columns(own_rows),
            columns(own_rows),
            pl.BlockSpec((tile, inner), lambda j: (j, 1)),
        ],
        out_specs=[columns(own_rows), columns(own_rows), fixed((8, group))],
        out_shape=[
            jax.ShapeDtypeStruct((own_rows, depth), BF16),
            jax.ShapeDtypeStruct((own_rows, depth), BF16),
            jax.ShapeDtypeStruct((8, group), F32),
        ],
        scratch_shapes=[pltpu.VMEM((group, LANES), F32)],
        compiler_params=params(),
        cost_estimate=SMALL_COST,
        name="branch",
    )(me, ends, gg, cotangent, other_cot, zo_all)
    prod_got = swap(prod)
    sq_all = sq + after(sq_got, prod)
    inv_gate8 = lax.rsqrt(sq_all / inner_total + EPSILON)
    inv_gate = inv_gate8[0]
    d_branch = (cot_all.astype(F32) * (live * inv_gate)[:, None]).astype(BF16)
    g_out = lax.dot_general(d_branch, gg, TN, preferred_element_type=F32).astype(BF16)
    grad_out = lax.psum_scatter(g_out, "dp", scatter_dimension=0, tiled=True)
    prod_got = after(prod_got, g_out)
    u_recv = swap(after(u_send, g_out))
    inv_own = lax.dynamic_slice_in_dim(inv_gate, me_t * own_rows, own_rows, 0)
    out_branch = (u_own.astype(F32) + u_recv.astype(F32)) * (inv_own * live_own)[:, None]
    layer_out = (tokens.astype(F32) + out_branch).astype(BF16)

    prod_all = prod + prod_got
    coef8 = inv_gate8 * inv_gate8 * inv_gate8 * (prod_all / inner_total)
    dy, dz, gain_acc = pl.pallas_call(
        gate_backward,
        grid=(tiles,),
        in_specs=[
            smem,
            smem,
            fixed((own_rows, depth)),
            fixed((own_rows, depth)),
            columns(depth, tiles),
            columns(group),
            columns(group),
            fixed((8, group)),
            fixed((8, group)),
            columns(8),
        ],
        out_specs=[columns(group), columns(group), columns(8)],
        out_shape=[
            jax.ShapeDtypeStruct((group, inner), BF16),
            jax.ShapeDtypeStruct((group, inner), BF16),
            jax.ShapeDtypeStruct((8, inner), F32),
        ],
        scratch_shapes=[pltpu.VMEM((group, LANES), F32), pltpu.VMEM((group, LANES), F32)],
        compiler_params=params(),
        cost_estimate=SMALL_COST,
        name="gate_backward",
    )(me, ends, cotangent, other_cot, zo_all, y_all, z_all, inv_gate8, coef8, taps)
    dot = partial(lax.dot_general, preferred_element_type=F32)
    front = depth // 2

    def gradient(d, width):
        outs = pl.BlockSpec((front, width), lambda j: (0, j))
        return pl.pallas_call(
            weight_grad,
            grid=(d.shape[1] // width,),
            in_specs=[smem, fixed((depth, own_rows)), fixed((depth, own_rows)), pl.BlockSpec((group, width), lambda j: (0, j))],
            out_specs=[outs, outs],
            out_shape=[jax.ShapeDtypeStruct((front, d.shape[1]), BF16)] * 2,
            compiler_params=params(),
            cost_estimate=SMALL_COST,
            name="weight_grad",
        )(me, turned_own, turned_other, d)

    if by_hand:
        g_send, z_keep = gradient(dz, tile)
        z_got = send(g_send, beside)
        dy = after(dy, z_keep, g_send)
    else:
        grad_z = lax.psum_scatter(dot(normed, dz, TN).astype(BF16), "dp", scatter_dimension=0, tiled=True)

    n_a = inner * 2 // 3
    n_b = inner + n_small - n_a

    def backward(base, width, carry):
        at = base // width
        back = lambda size, column: pl.BlockSpec((Q, size), lambda i: (chunks - 1 - i, column))
        operands = [ends, dy, xc, pre, x_raw, small, bc, states, taps, par, skip, sel]
        in_specs = [
            smem,
            back(width, at),
            back(width, at),
            back(width, at),
            back(width, at),
            back(n_small, 0),
            back(2 * STATE, 0),
            pl.BlockSpec((1, STATE, width), lambda i: (chunks - 1 - i, 0, at)),
            whole_spec((8, width), at),
            whole_spec((8, LANES)),
            whole_spec((1, width), at),
            pl.BlockSpec((width, LANES), lambda i: (at, 0)),
        ]
        tiles_held = width + (2 * STATE if carry else 0)
        acc_shape, hacc_shape = (8 * (K + 2), tiles_held), (16, LANES)
        if carry:
            last = inner // (2 * STATE)
            operands += [pre, taps, *carry]
            in_specs += [back(2 * STATE, last), whole_spec((8, 2 * STATE), last), back(n_small, 0)]
            in_specs += [whole_spec((8 * (K + 2), base)), whole_spec(hacc_shape), whole_spec((8, inner))]
            out_specs = [back(n_b, 0), whole_spec((8, n_conv))]
            out_shape = [jax.ShapeDtypeStruct((group, n_b), BF16), jax.ShapeDtypeStruct((8, n_conv), F32)]
        else:
            out_specs = [back(width, 0), back(n_small, 0)]
            out_shape = [jax.ShapeDtypeStruct((group, width), BF16), jax.ShapeDtypeStruct((group, n_small), F32)]
        return pl.pallas_call(
            partial(scan_backward, base, bool(carry), chunks),
            grid=(chunks,),
            in_specs=in_specs,
            out_specs=out_specs + [whole_spec(acc_shape), whole_spec(hacc_shape)],
            out_shape=out_shape + [jax.ShapeDtypeStruct(acc_shape, F32), jax.ShapeDtypeStruct(hacc_shape, F32)],
            scratch_shapes=[
                pltpu.VMEM((STATE, width), F32),
                pltpu.VMEM((tiles_held // LANES, Q + 8, LANES), F32),
                *[pltpu.VMEM((Q, width), BF16)] * 6,
                pltpu.VMEM((STATE, width), BF16),
                pltpu.VMEM((8, width), F32),
            ],
            compiler_params=params(),
            cost_estimate=SMALL_COST,
            name="scan_backward",
        )(*operands)

    dxa, part, acc, hacc = backward(0, n_a, ())
    if by_hand:
        z_got, dxa = lax.optimization_barrier((z_got, dxa))
        z_away, z_core = fold_away(z_keep, z_got)
        z_got = send(z_away, across)
        dxa, part = lax.optimization_barrier((dxa, part, z_away))[:2]
        g_x, grad_out = lax.optimization_barrier((dot(normed, dxa, TN).astype(BF16), grad_out))
        grad_a = lax.psum_scatter(g_x, "dp", scatter_dimension=0, tiled=True)
        part = after(part, g_x)
    dxb, vector = backward(n_a, inner - n_a, (part, acc, hacc, gain_acc))[:2]
    dxb = after(dxb, u_recv)
    lanes_shared = lax.iota(jnp.int32, n_conv)[None, :] >= inner
    bits_of = lambda turn: [(i, i ^ (1 << turn)) for i in range(n_dp)]
    if by_hand:
        z_got, dxb, vector = lax.optimization_barrier((z_got, dxb, vector))
        z_out = ring_part(z_keep, z_core, z_got, None, 1)
        z_came = send(z_out, around)
        shared_got = swap(vector)
        b_send, b_keep = gradient(after(dxb, z_out), n_b)
        b_got = send(b_send, beside)
        shared_got, z_came, b_keep = lax.optimization_barrier((shared_got, z_came, b_keep))
        vector = vector + jnp.where(lanes_shared, shared_got, 0.0)
        z_out = ring_part(z_keep, z_core, z_got, z_came, 2)
        z_came, vector_got = send(z_out, around), send(vector, bits_of(0))
        dz = after(dz, b_send, b_keep, z_out, vector)
    else:
        dx = jnp.concatenate([dxa, dxb], axis=1)
        grad_x = lax.psum_scatter(dot(normed, dx, TN).astype(BF16), "dp", scatter_dimension=0, tiled=True)

    def back_rows(which, dz):
        pick = lambda width: pl.BlockSpec((own_rows, width), lambda j, rows: (rows[0], 0))
        return pl.pallas_call(
            normed_back,
            grid_spec=pltpu.PrefetchScalarGridSpec(
                num_scalar_prefetch=1,
                grid=(depth // tile,),
                in_specs=[
                    pick(inner),
                    pick(n_a),
                    pick(n_b),
                    pl.BlockSpec((tile, inner), lambda j, rows: (j, 0)),
                    pl.BlockSpec((tile, inner + n_small), lambda j, rows: (j, 0)),
                ],
                out_specs=pl.BlockSpec((own_rows, tile), lambda j, rows: (0, j)),
            ),
            out_shape=jax.ShapeDtypeStruct((own_rows, depth), BF16),
            compiler_params=params(),
            cost_estimate=SMALL_COST,
            name="normed_back",
        )(which, dz, dxa, dxb, zo_all, wx_all)

    dn_send = back_rows(n_t - 1 - me, dz)
    if by_hand:
        w_sum = lambda w, g: jnp.sum(w.astype(F32) * g, axis=1)
        b_got, vector_got, dn_send, z_came = lax.optimization_barrier((b_got, vector_got, dn_send, z_came))
        b_away, b_core = fold_away(b_keep, b_got)
        b_got = send(b_away, across)
        dn_got = swap(after(dn_send, b_away))
        vector = vector + after(vector_got, b_away)
        z_out = ring_part(z_keep, z_core, z_got, after(z_came, b_away), 3)
        z_came, vector_got = send(z_out, around), send(vector, bits_of(1))
        dn_own = back_rows(me, after(dz, vector, z_out, b_away))
        vector_got, dn_own, b_got, z_came = lax.optimization_barrier((vector_got, dn_own, b_got, z_came))
        vector = vector + vector_got
        b_out = ring_part(b_keep, b_core, b_got, None, 1)
        b_came, vector_got = send(b_out, around), send(vector, bits_of(2))
        grad_z = ring_part(z_keep, z_core, z_got, z_came, ring) * gain_pair
        in_part = w_sum(w_zx[0], grad_z)
        vector_got, grad_z, in_part, b_came = lax.optimization_barrier((vector_got, grad_z, in_part, b_came))
        vector = vector + vector_got
        b_out = ring_part(b_keep, b_core, b_got, b_came, 2)
        b_came, vector_got = send(b_out, around), send(vector, bits_of(3))
        grad_out = grad_out.astype(F32).T
        vector_got, grad_out, layer_out, b_came, grad_a = lax.optimization_barrier(
            (vector_got, grad_out, layer_out, b_came, grad_a)
        )
        vector = vector + vector_got
        b_came = send(ring_part(b_keep, b_core, b_got, b_came, 3), around)
    else:
        vector = sum_dp(vector + jnp.where(lanes_shared, swap(vector), 0.0))
        dn_own = back_rows(me, dz)
        dn_got = swap(dn_send)
        grad_out = grad_out.astype(F32).T
        grad_z, grad_x = grad_z.astype(F32), grad_x.astype(F32)
        in_part = jnp.sum(w_zx[0].astype(F32) * grad_z, axis=1) + jnp.sum(jnp.concatenate([w_x, w_small], axis=1).astype(F32) * grad_x, axis=1)

    me_all = me_dp * n_t + me_t
    bc_sum = vector[: K + 1, inner:].reshape(K + 1, 2, STATE)
    bc_sum = lax.dynamic_slice_in_dim(bc_sum, me_all * span_n, span_n, 2)
    grad_bc_taps = bc_sum[:K].transpose(1, 2, 0).reshape(conv_bc.shape)
    grad_bc_bias = bc_sum[K]
    x_sum = vector[: K + 3, :inner].reshape(K + 3, heads, WIDTH)
    grad_skip = x_sum[K + 1].sum(axis=1)
    x_sum = lax.dynamic_slice_in_dim(x_sum, me_dp * span_p, span_p, 2)
    grad_x_taps = x_sum[:K].transpose(1, 2, 0).reshape(conv_x.shape)
    grad_x_bias = x_sum[K]
    grad_gate = x_sum[K + 2]
    grad_dt_bias = vector[K + 3, :heads]
    grad_a_log = vector[K + 3, LANES : LANES + heads]
    dn = (dn_own.astype(F32) + dn_got.astype(F32)) * gain_in[0:1, :]
    grad_tokens = (
        cotangent.astype(F32)
        + inv_tok * dn
        - tok_own * inv_tok * inv_tok * inv_tok * jnp.mean(dn * tok_own, axis=1, keepdims=True)
    )

    if by_hand:
        grad_b = ring_part(b_keep, b_core, b_got, b_came, ring) * gain_pair
        in_part = in_part + w_sum(w_x[:, n_a:], grad_b[:, : inner - n_a]) + w_sum(w_small, grad_b[:, inner - n_a :])
        outs = (grad_bc_taps, grad_bc_bias, grad_skip, grad_x_taps, grad_x_bias, grad_gate, grad_dt_bias, grad_a_log)
        outs = lax.optimization_barrier((*outs, grad_tokens, grad_b, in_part, grad_a))
        grad_bc_taps, grad_bc_bias, grad_skip, grad_x_taps, grad_x_bias, grad_gate, grad_dt_bias, grad_a_log = outs[:8]
        grad_tokens, grad_b, in_part, grad_a = outs[8:]
        grad_a = grad_a.astype(F32)
        in_part = in_part + w_sum(w_x[:, :n_a], grad_a)
    else:
        grad_a, grad_b = grad_x[:, :n_a], grad_x[:, n_a:]
    at = inner - n_a
    bc_part = jnp.concatenate([grad_b[:, at : at + 2 * STATE], jnp.broadcast_to(in_part[:, None], (shard, LANES))], axis=1)
    grad_zx = jnp.stack([grad_z, jnp.concatenate([grad_a, grad_b[:, :at]], axis=1)])
    grad_dt = grad_b[:, at + 2 * STATE : at + 2 * STATE + heads]
    half = half_bc
    bc_own = lax.dynamic_slice_in_dim(bc_part, me_t * half, half, 0)
    bc_send = lax.dynamic_slice_in_dim(bc_part, (n_t - 1 - me_t) * half, half, 0)
    bc_total = bc_own + swap(bc_send)
    own_gain = norm_gain.astype(F32)
    grad_bc = bc_total[:, : 2 * STATE].reshape(half, 2, STATE).transpose(1, 0, 2)
    grad_in = bc_total[:, 2 * STATE] / own_gain
    return (
        layer_out,
        grad_tokens,
        grad_in,
        grad_zx,
        grad_bc,
        grad_dt,
        grad_x_taps,
        grad_x_bias,
        grad_bc_taps,
        grad_bc_bias,
        grad_dt_bias,
        grad_a_log,
        grad_skip,
        grad_gate,
        grad_out,
    )


def solution(mesh):
    both = ("dp", "tensor")
    in_specs = (
        P(both, None),
        P(both, None),
        P("dp", None),
        P(both),
        P(None, "dp", "tensor"),
        P(None, both, None),
        P("dp", "tensor"),
        P("tensor", "dp"),
        P("tensor", "dp"),
        P(None, both),
        P(None, both),
        P("tensor"),
        P("tensor"),
        P("tensor"),
        P("tensor", "dp"),
        P("tensor", "dp"),
    )
    out_specs = (
        P(both, None),
        P(both, None),
        P(both),
        P(None, "dp", "tensor"),
        P(None, both, None),
        P("dp", "tensor"),
        P("tensor", "dp"),
        P("tensor", "dp"),
        P(None, both),
        P(None, both),
        P("tensor"),
        P("tensor"),
        P("tensor"),
        P("tensor", "dp"),
        P("tensor", "dp"),
    )
    return jax.shard_map(local, mesh=mesh, in_specs=in_specs, out_specs=out_specs, check_vma=False)
```

```python
from functools import partial

import jax
import jax.numpy as jnp
from jax import lax
from jax.experimental import pallas as pl
from jax.experimental.pallas import tpu as pltpu
from jax.sharding import PartitionSpec as P

EPSILON = 1e-05
HIGHEST = lax.Precision.HIGHEST
K = 4
WIDTH = 64
STATE = 128
Q = 128
LANES = 128
LOG2E = 1.4426950408889634
VMEM_LIMIT = 60 * 1024 * 1024
F32 = jnp.float32
BF16 = jnp.bfloat16

NN = (((1,), (0,)), ((), ()))
NT = (((1,), (1,)), ((), ()))
TN = (((0,), (0,)), ((), ()))


def mm(a, b, dims=NN):
    return lax.dot_general(a, b, dims, preferred_element_type=F32)


def mm_exact(a, b, dims=NN):
    return lax.dot_general(a, b, dims, preferred_element_type=F32, precision=HIGHEST)


def iota(shape, dim):
    return lax.broadcasted_iota(jnp.int32, shape, dim)


def segment_of(rows, ends_ref, count):
    total = (rows >= ends_ref[0]).astype(jnp.int32)
    for j in range(1, count):
        total = total + (rows >= ends_ref[j]).astype(jnp.int32)
    return total


def scalar_segment(row, ends_ref, count):
    total = jnp.where(row >= ends_ref[0], 1, 0)
    for j in range(1, count):
        total = total + jnp.where(row >= ends_ref[j], 1, 0)
    return total


def sigmoid(v):
    return 0.5 * jnp.tanh(0.5 * v) + 0.5


def softplus(v):
    return jnp.maximum(v, 0.0) + jnp.log1p(jnp.exp(-jnp.abs(v)))


def chunk_masks(chunk, ends_ref, count):
    base = chunk * Q
    rows = iota((Q, Q), 0) + base
    cols = iota((Q, Q), 1) + base
    row_ids = segment_of(rows, ends_ref, count)
    col_ids = segment_of(cols, ends_ref, count)
    same = row_ids == col_ids
    before_id = jnp.where(chunk == 0, -1, scalar_segment(base - 1, ends_ref, count))
    final_id = scalar_segment(base + Q - 1, ends_ref, count)
    carry = (row_ids == before_id).astype(F32)
    last = (row_ids == final_id).astype(F32)
    passing = jnp.where(before_id == final_id, 1.0, 0.0).astype(F32)
    return rows, cols, row_ids, same, carry, last, passing


def decays(dt_raw, par_ref):
    shifted = dt_raw + par_ref[0:1, :]
    step = softplus(shifted)
    decay_rate = jnp.exp(par_ref[1:2, :])
    return shifted, step, decay_rate


def pair_columns(values, pair, first):
    left = jnp.broadcast_to(values[:, 2 * pair : 2 * pair + 1], (Q, LANES))
    right = jnp.broadcast_to(values[:, 2 * pair + 1 : 2 * pair + 2], (Q, LANES))
    return left, right, jnp.where(first, left, right)


def scan_forward(
    heads, ends_ref, xr_ref, small_ref, taps_ref, par_ref, skip_ref,
    xc_ref, pre_ref, bc_ref, y_ref, st_ref, buf, state,
):
    count = ends_ref.shape[0]
    inner = heads * WIDTH
    chunk = pl.program_id(0)

    @pl.when(chunk == 0)
    def _():
        buf[:, 0:8, :] = jnp.zeros((buf.shape[0], 8, LANES), F32)
        state[...] = jnp.zeros(state.shape, F32)

    rows, cols, row_ids, same, carry, last, passing = chunk_masks(chunk, ends_ref, count)
    causal = rows >= cols
    visible = same & causal
    lag_mask = [None]
    for lag in range(1, K):
        earlier = rows - lag
        keep = (segment_of(earlier, ends_ref, count) == row_ids) & (earlier >= 0)
        lag_mask.append(keep.astype(F32))

    small = small_ref[...]

    def convolve(lo, raw):
        span = slice(lo, lo + LANES)
        place = lo // LANES
        buf[place, 8 : 8 + Q, :] = raw
        pre = taps_ref[K : K + 1, span] + taps_ref[K - 1 : K, span] * raw
        for lag in range(1, K):
            pre = pre + taps_ref[K - 1 - lag : K - lag, span] * (
                buf[place, 8 - lag : 8 - lag + Q, :] * lag_mask[lag]
            )
        buf[place, 0:8, :] = raw[Q - 8 : Q, :]
        pre_ref[:, span] = pre.astype(BF16)
        return pre * sigmoid(pre)

    b_f = convolve(inner, small[:, :STATE]).astype(BF16).astype(F32)
    c_b = convolve(inner + STATE, small[:, STATE : 2 * STATE]).astype(BF16)
    b_b = b_f.astype(BF16)
    bc_ref[:, :STATE] = b_b
    bc_ref[:, STATE:] = c_b
    b_t = b_f.T.astype(BF16)

    _, step, decay_rate = decays(small[:, 2 * STATE :], par_ref)
    csum = mm_exact(causal.astype(F32), step * (-LOG2E * decay_rate))
    csum_t = csum.T
    scores = jnp.where(visible, mm(c_b, b_b, NT), 0.0)
    first = iota((Q, LANES), 1) < WIDTH
    first_row = iota((1, LANES), 1) < WIDTH

    wide = 2 * LANES
    for quad in range(0, inner, wide):
        block = slice(quad, quad + wide)
        held = state[:, block]
        held_b = held.astype(BF16)
        st_ref[0, :, block] = held_b
        carried = mm(c_b, held_b)
        weighted, kept = [], []
        for part in range(0, wide, LANES):
            lo = quad + part
            pair = lo // LANES
            span = slice(lo, lo + LANES)
            xc = convolve(lo, xr_ref[:, span].astype(F32)).astype(BF16)
            xc_ref[:, span] = xc
            xc = xc.astype(F32)
            left, right, both = pair_columns(csum, pair, first)
            _, _, step_pair = pair_columns(step, pair, first)
            mix = jnp.concatenate(
                [
                    (scores * jnp.exp2(jnp.minimum(left - csum_t[2 * pair : 2 * pair + 1, :], 0.0))).astype(BF16),
                    (scores * jnp.exp2(jnp.minimum(right - csum_t[2 * pair + 1 : 2 * pair + 2, :], 0.0))).astype(BF16),
                ],
                axis=1,
            )
            fed_b = (xc * step_pair).astype(BF16)
            zero = jnp.zeros((Q, LANES), BF16)
            stacked = jnp.concatenate([jnp.where(first, fed_b, zero), jnp.where(first, zero, fed_b)], axis=0)
            y = mm(mix, stacked) + carried[:, part : part + LANES] * (jnp.exp2(both) * carry)
            y_ref[:, span] = (y + skip_ref[:, span] * xc).astype(BF16)
            closing = both[Q - 1 : Q, :]
            weighted.append((fed_b.astype(F32) * (jnp.exp2(closing - both) * last)).astype(BF16))
            kept.append(jnp.exp2(closing) * passing)
        fresh = mm(b_t, jnp.concatenate(weighted, axis=1))
        state[:, block] = held * jnp.concatenate(kept, axis=1) + fresh


def scan_backward(
    base, last_call, chunks, ends_ref, dy_ref, xc_ref, pre_ref, xr_ref, small_ref, bc_ref, st_ref, taps_ref,
    par_ref, skip_ref, sel_ref, *refs,
):
    if last_call:
        pre_bc_ref, taps_bc_ref, part_in, acc_in, hacc_in, gain_acc_ref = refs[:6]
        dx_ref, rows_ref, acc_ref, hacc_ref = refs[6:10]
        refs = refs[10:]
    else:
        dx_ref, part_ref, acc_ref, hacc_ref = refs[:4]
        refs = refs[4:]
    dstate, dpre, ab_hi, ab_lo, v_b, u_b, dyd, fedw, dst_b, through = refs
    count = ends_ref.shape[0]
    inner = dy_ref.shape[1]
    total_rows = chunks * Q
    chunk = chunks - 1 - pl.program_id(0)

    @pl.when(pl.program_id(0) == 0)
    def _():
        dpre[:, Q : Q + 8, :] = jnp.zeros((dpre.shape[0], 8, LANES), F32)
        dstate[...] = jnp.zeros(dstate.shape, F32)
        acc_ref[...] = jnp.zeros(acc_ref.shape, F32)
        hacc_ref[...] = hacc_in[...] if last_call else jnp.zeros(hacc_ref.shape, F32)

    rows, cols, row_ids, same, carry, last, passing = chunk_masks(chunk, ends_ref, count)
    causal = rows >= cols
    visible = same & causal
    lag_mask = [None]
    for lag in range(1, K):
        later = rows + lag
        keep = (segment_of(later, ends_ref, count) == row_ids) & (later < total_rows)
        lag_mask.append(keep.astype(F32))

    small = small_ref[...]
    shifted, step, decay_rate = decays(small[:, 2 * STATE :], par_ref)
    csum = mm_exact(causal.astype(F32), step * (-LOG2E * decay_rate))
    csum_t = csum.T
    b_b = bc_ref[:, :STATE]
    c_b = bc_ref[:, STATE:]
    c_t = c_b.astype(F32).T.astype(BF16)
    scores = jnp.where(visible, mm(c_b, b_b, NT), 0.0)
    first = iota((Q, LANES), 1) < WIDTH

    def fold(values):
        return values.reshape(Q // 8, 8, values.shape[1]).sum(axis=0)

    def conv_back(lo, d_conv, raw, pre, taps, at):
        span = slice(lo, lo + LANES)
        place = lo // LANES
        gate = sigmoid(pre)
        d_pre = d_conv * (gate * (1.0 + pre * (1.0 - gate)))
        dpre[place, 0:Q, :] = d_pre
        d_raw = taps[K - 1 : K, at] * d_pre
        acc_ref[8 * (K - 1) : 8 * K, span] += fold(d_pre * raw)
        acc_ref[8 * K : 8 * K + 8, span] += fold(d_pre)
        for lag in range(1, K):
            moved = dpre[place, lag : lag + Q, :] * lag_mask[lag]
            d_raw = d_raw + taps[K - 1 - lag : K - lag, at] * moved
            acc_ref[8 * (K - 1 - lag) : 8 * (K - lag), span] += fold(moved * raw)
        dpre[place, Q : Q + 8, :] = d_pre[0:8, :]
        dx_ref[:, span] = d_raw.astype(BF16)

    d_scores = jnp.zeros((Q, Q), F32)
    wide = 2 * LANES
    for quad in range(0, inner, wide):
        block = slice(quad, quad + wide)
        held_b = st_ref[0, :, block]
        d_held = dstate[:, block]
        d_held_b = d_held.astype(BF16)
        dst_b[:, block] = d_held_b
        carried = mm(c_b, held_b)
        returned = mm(b_b, d_held_b)
        crossing = (d_held * held_b.astype(F32)).reshape(STATE // 8, 8, wide).sum(axis=0)
        grown_parts, kept_parts = [], []
        for part in range(0, wide, LANES):
            lo = quad + part
            pair = (base + lo) // LANES
            span = slice(lo, lo + LANES)
            xc = xc_ref[:, span].astype(F32)
            dy_b = dy_ref[:, span]
            dy = dy_b.astype(F32)
            left, right, both = pair_columns(csum, pair, first)
            _, _, step_pair = pair_columns(step, pair, first)
            fall_left = jnp.exp2(jnp.minimum(left - csum_t[2 * pair : 2 * pair + 1, :], 0.0))
            fall_right = jnp.exp2(jnp.minimum(right - csum_t[2 * pair + 1 : 2 * pair + 2, :], 0.0))
            mix = jnp.concatenate([(scores * fall_left).astype(BF16), (scores * fall_right).astype(BF16)], axis=1)
            fed_b = (xc * step_pair).astype(BF16)
            fed = fed_b.astype(F32)
            zero = jnp.zeros((Q, LANES), BF16)
            stacked = jnp.concatenate([jnp.where(first, fed_b, zero), jnp.where(first, zero, fed_b)], axis=0)
            grown = jnp.exp2(both) * carry
            y = mm(mix, stacked) + carried[:, part : part + LANES] * grown
            d_mix = mm(dy_b, stacked, NT)
            d_scores = d_scores + d_mix[:, :Q] * fall_left + d_mix[:, Q:] * fall_right
            d_fed2 = mm(mix, dy_b, TN)
            d_fed_in = jnp.where(first, d_fed2[:Q], d_fed2[Q:])
            closing = both[Q - 1 : Q, :]
            shrink = jnp.exp2(closing - both) * last
            d_fed_out = returned[:, part : part + LANES] * shrink
            d_fed = d_fed_in + d_fed_out
            straddle = dy * y - fed * d_fed_in
            hi = straddle.astype(BF16)
            ab_hi[:, span] = hi
            ab_lo[:, span] = (straddle - hi.astype(F32)).astype(BF16)
            v_b[:, span] = (fed * d_fed_out).astype(BF16)
            u_b[:, span] = (xc * d_fed).astype(BF16)
            fedw[:, span] = (fed * shrink).astype(BF16)
            grown_parts.append((dy * grown).astype(BF16))
            kept_parts.append(jnp.exp2(closing) * passing)
            acc_ref[8 * K + 8 : 8 * K + 16, span] += fold(dy * xc)
            d_conv = d_fed * step_pair + skip_ref[:, span] * dy
            conv_back(lo, d_conv, xr_ref[:, span].astype(F32), pre_ref[:, span].astype(F32), taps_ref, span)
        dy_grown = jnp.concatenate(grown_parts, axis=1)
        kept = jnp.concatenate(kept_parts, axis=1)
        dyd[:, block] = dy_grown
        through[:, block] = crossing * kept
        dstate[:, block] = d_held * kept + mm(c_t, dy_grown)

    d_scores_b = jnp.where(visible, d_scores, 0.0).astype(BF16)
    d_c = mm(dyd[...], st_ref[0], NT) + mm(d_scores_b, b_b)
    d_b = mm(fedw[...], dst_b[...], NT) + mm(d_scores_b, c_b, TN)
    sel = sel_ref[...]
    red_ab = mm(ab_hi[...], sel) + mm(ab_lo[...], sel)
    red_v = mm(v_b[...], sel)
    red_u = mm(u_b[...], sel)
    thr = through[...]
    thr_hi = thr.astype(BF16)
    red_t = mm(thr_hi, sel) + mm((thr - thr_hi.astype(F32)).astype(BF16), sel)
    d_rate = (
        mm_exact((same & (cols >= rows)).astype(F32), red_ab)
        + mm_exact((same & (cols < rows)).astype(F32), red_v)
        + jnp.sum(red_t, axis=0, keepdims=True)
    )
    d_step = red_u - d_rate * decay_rate
    d_dt = d_step * sigmoid(shifted)
    hacc_ref[0:8, :] += fold(d_dt)
    hacc_ref[8:16, :] += fold(d_rate * (-decay_rate * step))
    if not last_call:
        part_ref[:, :STATE] = d_b
        part_ref[:, STATE : 2 * STATE] = d_c
        part_ref[:, 2 * STATE :] = d_dt
        return

    for k, d_conv in enumerate((d_b, d_c)):
        at = slice(k * STATE, (k + 1) * STATE)
        pre = pre_bc_ref[:, at].astype(F32)
        conv_back(inner + k * STATE, d_conv + part_in[:, at], small[:, at], pre, taps_bc_ref, at)
    dx_ref[:, inner + 2 * STATE :] = (d_dt + part_in[:, 2 * STATE :]).astype(BF16)

    @pl.when(pl.program_id(0) == pl.num_programs(0) - 1)
    def _():
        before = acc_in.shape[1]
        whole = before + inner
        rows_ref[...] = jnp.zeros(rows_ref.shape, F32)
        for k in range(K + 2):
            block = slice(8 * k, 8 * k + 8)
            rows_ref[k : k + 1, :before] = jnp.sum(acc_in[block, :], axis=0, keepdims=True)
            rows_ref[k : k + 1, before:] = jnp.sum(acc_ref[block, :], axis=0, keepdims=True)
        rows_ref[K + 2 : K + 3, :whole] = jnp.sum(gain_acc_ref[...], axis=0, keepdims=True)
        for k in range(2):
            total = jnp.sum(hacc_ref[8 * k : 8 * k + 8, :], axis=0, keepdims=True)
            rows_ref[K + 3 : K + 4, k * LANES : (k + 1) * LANES] = total


def load_blocks(offsets_ref, parts, whole, sems, size, columns, first=0):
    @pl.when(pl.program_id(0) == 0)
    def _():
        copies = []
        for part in parts:
            for j in range(part.shape[0] // size):
                k = first + len(copies)
                start = 0 if size == whole.shape[0] else pl.multiple_of(offsets_ref[k], 32)
                source = part.at[pl.ds(j * size, size), :]
                copies.append(pltpu.make_async_copy(source, whole.at[pl.ds(start, size), slice(*columns)], sems.at[k]))
        for copy in copies:
            copy.start()
        for copy in copies:
            copy.wait()


def turn_rows(offsets_ref, source_ref, out_ref, turned):
    rows, depth = source_ref.shape
    for lo in range(0, rows, Q):
        tile = source_ref[lo : lo + Q, :].astype(F32)
        tile = tile * lax.rsqrt(jnp.mean(tile * tile, axis=1, keepdims=True) + EPSILON)
        for left in range(0, depth, LANES):
            turned[left : left + LANES, lo : lo + Q] = tile[:, left : left + LANES].T.astype(BF16)
    count = offsets_ref.shape[0]
    size = depth // count
    for k in range(count):
        start = pl.multiple_of(offsets_ref[k], 32)
        out_ref[k * size : (k + 1) * size, :] = turned[pl.ds(start, size), :]


def project(counts, heads, size, offsets_ref, me_ref, own_ref, other_ref, place_ref, *refs):
    count = sum(counts)
    blocks, (x_ref, small_ref, normed_ref, taps_ref, gain_ref, w_out_ref, w_ref, sems, out_sem) = refs[:count], refs[count:]
    split = x_ref.shape[1]
    shards = w_ref.shape[0] // size
    load_blocks(offsets_ref, blocks[: counts[0]], w_ref, sems, size, (0, split))
    load_blocks(offsets_ref, blocks[counts[0] :], w_ref, sems, size, (split, w_ref.shape[1]), shards)
    keep = pltpu.make_async_copy(w_ref, w_out_ref, out_sem)
    depth, inner = w_ref.shape[0], x_ref.shape[1]
    tile = 512

    @pl.when(pl.program_id(0) == 0)
    def _():
        keep.start()
        spare = w_ref[:, inner + 2 * STATE :]
        turned = spare.astype(F32).T
        gain_ref[...] = jnp.broadcast_to(turned[heads + K + 2 : heads + K + 3, :], gain_ref.shape)
        few = turned[heads : heads + 16, :].astype(BF16)
        lanes = iota((depth, LANES), 1)
        for lo in range(0, inner + 2 * STATE, LANES):
            if lo < inner:
                wanted, row = place_ref[:, :LANES] == lanes + lo, 0
            else:
                wanted, row = place_ref[:, LANES:] == lanes + (lo - inner), 8
            moved = mm(few, jnp.where(wanted, 1.0, 0.0).astype(BF16))
            taps_ref[:, lo : lo + LANES] = moved[row : row + 8, :]

    rows = jnp.where(pl.program_id(0) == me_ref[0], own_ref[...], other_ref[...]).astype(F32)
    scale = lax.rsqrt(jnp.mean(rows * rows, axis=1, keepdims=True) + EPSILON)
    rows = (rows * scale * gain_ref[0:1, :]).astype(BF16)
    normed_ref[...] = rows
    for lo in range(0, inner, tile):
        x_ref[:, lo : lo + tile] = mm(rows, w_ref[:, lo : lo + tile]).astype(BF16)
    small_ref[...] = mm(rows, w_ref[:, inner:])

    @pl.when(pl.program_id(0) == pl.num_programs(0) - 1)
    def _():
        keep.wait()


def row_sums(lanes):
    return mm_exact(jnp.ones((8, LANES), F32), lanes, NT)


def spread_rows(values):
    pick = jnp.where(iota((8, LANES), 0) == 0, 1.0, 0.0).astype(F32)
    return mm_exact(values, pick, TN)


def gate_forward(normed_ref, w_ref, y_ref, gain_ref, z_ref, gg_ref, sq_ref, square):
    rows, width = z_ref.shape
    size = 512

    @pl.when(pl.program_id(0) == 0)
    def _():
        square[...] = jnp.zeros(square.shape, F32)

    for lo in range(0, rows, size):
        at = slice(lo, lo + size)
        z = mm(normed_ref[at, :], w_ref[...]).astype(BF16)
        z_ref[at, :] = z
        z = z.astype(F32)
        gated = y_ref[at, :].astype(F32) * (z * sigmoid(z))
        gg_ref[at, :] = (gated * gain_ref[K + 1 : K + 2, :]).astype(BF16)
        twice = gated * gated
        for part in range(0, width, LANES):
            square[at, :] += twice[:, part : part + LANES]

    @pl.when(pl.program_id(0) == pl.num_programs(0) - 1)
    def _():
        sq_ref[...] = row_sums(square[...])


def branch(me_ref, ends_ref, gg_ref, own_ref, other_ref, w_ref, mine_ref, away_ref, prod_ref, product):
    rows, width = mine_ref.shape
    size = 512

    @pl.when(pl.program_id(0) == 0)
    def _():
        product[...] = jnp.zeros(product.shape, F32)

    for index, (out_ref, cot_ref) in enumerate(((mine_ref, own_ref), (away_ref, other_ref))):
        first = jnp.where(index == 0, me_ref[0], 1 - me_ref[0]) * rows
        for lo in range(0, rows, size):
            at = pl.ds(pl.multiple_of(first + lo, size), size)
            u = mm(gg_ref[at, :], w_ref[...], NT)
            out_ref[lo : lo + size, :] = u.astype(BF16)
            term = u * cot_ref[lo : lo + size, :].astype(F32)
            for part in range(0, width, LANES):
                product[at, :] += term[:, part : part + LANES]

    @pl.when(pl.program_id(0) == pl.num_programs(0) - 1)
    def _():
        live = iota(product.shape, 0) < ends_ref[ends_ref.shape[0] - 1]
        prod_ref[...] = row_sums(jnp.where(live, product[...], 0.0))


def gate_backward(
    me_ref, ends_ref, own_ref, other_ref, w_ref, y_ref, z_ref, rg_ref, coef_ref, gain_ref,
    dy_ref, dz_ref, acc_ref, rg, coef,
):
    total, width = dy_ref.shape
    rows = own_ref.shape[0]
    size = 512

    @pl.when(pl.program_id(0) == 0)
    def _():
        live = iota(rg.shape, 0) < ends_ref[ends_ref.shape[0] - 1]
        rg[...] = spread_rows(rg_ref[...])
        coef[...] = spread_rows(coef_ref[...])
        rg[...] = jnp.where(live, rg[...], 0.0)

    gain = gain_ref[K + 1 : K + 2, :]
    sums = jnp.zeros((8, width), F32)
    for index, cot_ref in enumerate((own_ref, other_ref)):
        first = jnp.where(index == 0, me_ref[0], 1 - me_ref[0]) * rows
        for lo in range(0, rows, size):
            at = pl.ds(pl.multiple_of(first + lo, size), size)
            ds = mm(cot_ref[lo : lo + size, :], w_ref[...])
            z = z_ref[at, :].astype(F32)
            y = y_ref[at, :].astype(F32)
            scale = jnp.concatenate([rg[at, :]] * (width // LANES), axis=1)
            back = jnp.concatenate([coef[at, :]] * (width // LANES), axis=1)
            gate = sigmoid(z)
            silu = z * gate
            gated = y * silu
            d_normal = ds * scale
            sums = sums + (d_normal * gated).reshape(size // 8, 8, width).sum(axis=0)
            d_gated = d_normal * gain - gated * back
            dy_ref[at, :] = (d_gated * silu).astype(BF16)
            dz_ref[at, :] = (d_gated * y * (gate + silu * (1.0 - gate))).astype(BF16)
    acc_ref[...] = sums


def weight_grad(me_ref, own_ref, other_ref, d_ref, away_ref, keep_ref):
    half, rows = away_ref.shape[0], own_ref.shape[1]
    mine = d_ref[pl.ds(pl.multiple_of(me_ref[0] * rows, rows), rows), :]
    theirs = d_ref[pl.ds(pl.multiple_of((1 - me_ref[0]) * rows, rows), rows), :]
    for at, ref in ((0, away_ref), (half, keep_ref)):
        total = mm(own_ref[at : at + half, :], mine) + mm(other_ref[at : at + half, :], theirs)
        ref[...] = total.astype(BF16)


def normed_back(rows_ref, dz_ref, dxa_ref, dxb_ref, wz_ref, wx_ref, out_ref):
    n_a = dxa_ref.shape[1]
    total = mm(dz_ref[...], wz_ref[...], NT)
    total = total + mm(dxa_ref[...], wx_ref[:, :n_a], NT) + mm(dxb_ref[...], wx_ref[:, n_a:], NT)
    out_ref[...] = total.astype(BF16)


def params():
    return pltpu.CompilerParams(dimension_semantics=("arbitrary",), vmem_limit_bytes=VMEM_LIMIT)


SMALL_COST = pl.CostEstimate(flops=1000, bytes_accessed=1000, transcendentals=0)


def rows_spec(block, width, column=0):
    return pl.BlockSpec((block, width), lambda i: (i, column))


def whole_spec(shape, column=0):
    return pl.BlockSpec(shape, lambda i: (0, column))


def local(
    tokens,
    cotangent,
    lengths,
    norm_gain,
    w_zx,
    w_bc,
    w_dt,
    conv_x,
    conv_x_bias,
    conv_bc,
    conv_bc_bias,
    dt_bias,
    a_log,
    d_skip,
    gate_gain,
    w_out,
):
    n_t = lax.axis_size("tensor")
    n_dp = lax.axis_size("dp")
    me_t = lax.axis_index("tensor")
    me_dp = lax.axis_index("dp")
    own_rows, depth = tokens.shape
    group = own_rows * n_t
    chunks = group // Q
    heads = dt_bias.shape[0]
    inner = heads * WIDTH
    inner_total = inner * n_t
    shard = w_zx.shape[1]
    pairs = [(i, n_t - 1 - i) for i in range(n_t)]

    def swap(v):
        return lax.ppermute(v, "tensor", pairs)

    def in_order(mine, other, axis=0):
        low = jnp.where(me_t == 0, mine, other)
        high = jnp.where(me_t == 0, other, mine)
        return jnp.concatenate([low, high], axis=axis)

    def sum_dp(v):
        step = 1
        while step < n_dp:
            v = v + lax.ppermute(v, "dp", [(i, i ^ step) for i in range(n_dp)])
            step *= 2
        return v

    def after(value, *others):
        return lax.optimization_barrier((value, *others))[0]

    ring = 4
    plane = n_dp // (2 * ring)

    around = [(i, (i + 2 * plane) % n_dp) for i in range(n_dp)]
    across = [(i, i ^ 2) for i in range(n_dp)]
    beside = [(i, i ^ 1) for i in range(n_dp)]

    def send(v, way):
        return lax.ppermute(v, "dp", way)

    by_hand = plane == 2 and shard % 32 == 0

    def whole(v):
        return [lax.all_gather(v, "dp", axis=0, tiled=True)]

    def relative_order():
        level, side, core = me_dp // 4, (me_dp // 2) % 2, me_dp % 2
        order = []
        for dc in (1, 0):
            for dy in (1, 0):
                for dz in range(1, ring + 1):
                    order.append(((level - dz + ring) % ring) * 4 + (side ^ dy) * 2 + (core ^ dc))
        return order

    def fold_away(keep, got):
        half = keep.shape[0] // 2
        return (keep[:half].astype(F32) + got[:half].astype(F32)).astype(BF16), got

    def ring_part(keep, core, got, came, turn):
        low, high = (turn - 1) * shard, turn * shard
        half = keep.shape[0] // 2
        part = keep[half + low : half + high].astype(F32) + core[half + low : half + high].astype(F32)
        part = part + got[low:high].astype(F32)
        if came is not None:
            part = part + came.astype(F32)
        return part if turn == ring else part.astype(BF16)

    ends = jnp.cumsum(lengths[0]).astype(jnp.int32)
    live = (lax.iota(jnp.int32, group) < ends[-1]).astype(F32)
    live_own = lax.dynamic_slice_in_dim(live, me_t * own_rows, own_rows, 0)
    me = me_t.astype(jnp.int32).reshape(1)

    span_p = conv_x_bias.shape[1]
    span_n = conv_bc_bias.shape[1]
    half_bc = w_bc.shape[1]
    bits = jnp.concatenate([norm_gain, conv_bc.reshape(-1), conv_bc_bias.reshape(-1)])
    bits = jnp.pad(bits, (0, LANES - bits.shape[0]))
    tiny = jnp.concatenate([w_bc.reshape(2 * half_bc, STATE), bits[None]], axis=0)
    other_tiny = swap(tiny)
    other_bc = other_tiny[: 2 * half_bc].reshape(w_bc.shape)
    both_bits = [bits, other_tiny[2 * half_bc]]
    at = norm_gain.shape[0]
    gain_pair = in_order(*[v[:at] for v in both_bits])[:, None]
    taps_bc = in_order(*[v[at : at + conv_bc.size].reshape(2, span_n, K) for v in both_bits], axis=1)
    at += conv_bc.size
    bias_bc = in_order(*[v[at : at + 2 * span_n].reshape(2, span_n, 1) for v in both_bits], axis=1)
    spare_bc = jnp.concatenate([taps_bc, bias_bc], axis=2).reshape(4 * span_n, K + 1)
    spare_x = [conv_x.reshape(shard, K), conv_x_bias.reshape(shard, 1), gate_gain.reshape(shard, 1), gain_pair]
    bc_pair = in_order(w_bc, other_bc, axis=1)
    w_x = w_zx[1]
    w_small = jnp.concatenate(
        [bc_pair[0], bc_pair[1], w_dt, *spare_x, jnp.zeros((shard, 8 - K - 3), BF16)]
        + [jnp.pad(spare_bc, ((0, shard - 4 * span_n), (0, LANES - heads - 8 - K - 1)))],
        axis=1,
    )
    gain_pair = gain_pair.astype(F32)
    where = after(lax.iota(jnp.int32, depth), w_small)
    home, inside = where // shard, where % shard
    place_x = (inside // span_p) * WIDTH + home * span_p + inside % span_p
    half_n = 2 * span_n
    place_bc = (inside // half_n) * STATE + home * half_n + inside % half_n
    place = jnp.concatenate([jnp.broadcast_to(v[:, None], (depth, LANES)) for v in (place_x, place_bc)], axis=1)
    par = jnp.concatenate([dt_bias[None], a_log[None], jnp.zeros((6, heads), F32)], axis=0)
    par = jnp.concatenate([par, jnp.zeros((8, LANES - heads), F32)], axis=1)
    skip = jnp.repeat(d_skip, WIDTH)[None]
    members = lax.iota(jnp.int32, inner)[:, None] // WIDTH
    sel = (members == lax.iota(jnp.int32, LANES)[None, :]).astype(BF16)
    smem = pl.BlockSpec(memory_space=pltpu.SMEM)
    vmem = pl.BlockSpec(memory_space=pltpu.VMEM)
    hbm = pl.BlockSpec(memory_space=pl.ANY)
    n_small = 2 * STATE + LANES
    n_conv = inner + 2 * STATE
    w_rest = jnp.concatenate([w_zx[0], w_out.T], axis=1)

    def turn(rows):
        return pl.pallas_call(
            turn_rows,
            in_specs=[smem, vmem],
            out_specs=vmem,
            out_shape=jax.ShapeDtypeStruct((depth, own_rows), BF16),
            scratch_shapes=[pltpu.VMEM((depth, own_rows), BF16)],
            compiler_params=pltpu.CompilerParams(vmem_limit_bytes=VMEM_LIMIT),
            cost_estimate=SMALL_COST,
            name="turn_rows",
        )((jnp.stack(relative_order()) * shard).astype(jnp.int32), rows)

    def place_of(turn, side, core):
        level = (me_dp // (2 * plane) - turn + ring) % ring
        return (level * (2 * plane) + ((me_dp % (2 * plane)) ^ (2 * side + core))) * shard

    together = lambda *values: list(lax.optimization_barrier(tuple(values)))
    joined = lambda *values: jnp.concatenate(values, axis=0)
    if by_hand:
        shift = lambda k: [(i, (i + 2 * plane * k) % n_dp) for i in range(n_dp)]
        l1, o0, c0 = together(send(w_x, around), send(w_x, across), send(w_x, beside))
        late, w_small = together(tokens, w_small, l1, o0, c0)[:2]
        l2, o1, s1, s2, s3, turned_own = together(
            send(l1, around), send(l1, across), send(w_small, shift(1)), send(w_small, shift(2)), send(w_small, shift(3)),
            turn(late),
        )
        w_rest = after(jnp.concatenate([w_zx[0], w_out.T], axis=1), l2)
        zo_all = lax.all_gather(w_rest, "dp", axis=0, tiled=True)
        small_line = joined(w_small, s1, s2, s3)
        split = own_rows // 2
        l3, o2, c1, small_across, t0 = together(
            send(l2, around), send(l2, across), send(joined(l1, o0), beside), send(small_line, across), swap(late[:split])
        )
        o3, c2, small_beside, t1, place, par, skip, sel = together(
            send(l3, across), send(joined(l2, o1), beside), send(joined(small_line, small_across), beside),
            swap(after(late[split:], t0)), place, par, skip, sel,
        )
        other_tokens = joined(t0, t1)
        c3, turned_other, other_tokens = together(send(joined(l3, o2, o3), beside), turn(other_tokens), other_tokens)
        other_cot = swap(after(cotangent, other_tokens))
        wx_parts = [w_x, l1, l2, l3, o0, o1, o2, o3, c0, c1, c2, c3]
        order = [(t, 0, 0) for t in range(4)] + [(t, 1, 0) for t in range(4)]
        order += [(0, 0, 1), (1, 0, 1), (0, 1, 1), (2, 0, 1), (1, 1, 1), (3, 0, 1), (2, 1, 1), (3, 1, 1)]
        small_parts = [small_line, small_across, small_beside]
        order += [(t, side, core) for core in range(2) for side in range(2) for t in range(4)]
        offsets = jnp.stack([place_of(*key) for key in order]).astype(jnp.int32)
    else:
        wx_parts, small_parts = whole(w_x), whole(w_small)
        zo_all = whole(jnp.concatenate([w_zx[0], w_out.T], axis=1))[0]
        other_tokens, other_cot = swap(tokens), swap(cotangent)
        offsets = jnp.zeros((2,), jnp.int32)
    counts = (len(wx_parts), len(small_parts))
    sems = pltpu.SemaphoreType.DMA((offsets.shape[0],))
    tok_own = tokens.astype(F32)
    inv_tok = lax.rsqrt(jnp.mean(tok_own * tok_own, axis=1, keepdims=True) + EPSILON)

    block = own_rows
    steps = group // block
    x_raw, small, normed, taps, gain_in, wx_all = pl.pallas_call(
        partial(project, counts, heads, shard if by_hand else depth),
        grid=(steps,),
        in_specs=[
            smem,
            smem,
            whole_spec((block, depth)),
            whole_spec((block, depth)),
            whole_spec((depth, 2 * LANES)),
        ]
        + [hbm] * sum(counts),
        out_specs=[
            rows_spec(block, inner),
            rows_spec(block, n_small),
            rows_spec(block, depth),
            whole_spec((8, n_conv)),
            whole_spec((8, depth)),
            hbm,
        ],
        out_shape=[
            jax.ShapeDtypeStruct((group, inner), BF16),
            jax.ShapeDtypeStruct((group, n_small), F32),
            jax.ShapeDtypeStruct((group, depth), BF16),
            jax.ShapeDtypeStruct((8, n_conv), F32),
            jax.ShapeDtypeStruct((8, depth), F32),
            jax.ShapeDtypeStruct((depth, inner + n_small), BF16),
        ],
        scratch_shapes=[pltpu.VMEM((depth, inner + n_small), BF16), sems, pltpu.SemaphoreType.DMA],
        compiler_params=params(),
        cost_estimate=SMALL_COST,
        name="project",
    )(offsets, me, tokens, other_tokens, place, *wx_parts, *small_parts)
    xc, pre, bc, y_all, states = pl.pallas_call(
        partial(scan_forward, heads),
        grid=(chunks,),
        in_specs=[
            smem,
            rows_spec(Q, inner),
            rows_spec(Q, n_small),
            whole_spec((8, n_conv)),
            whole_spec((8, LANES)),
            whole_spec((1, inner)),
        ],
        out_specs=[
            rows_spec(Q, inner),
            rows_spec(Q, n_conv),
            rows_spec(Q, 2 * STATE),
            rows_spec(Q, inner),
            pl.BlockSpec((1, STATE, inner), lambda i: (i, 0, 0)),
        ],
        out_shape=[
            jax.ShapeDtypeStruct((group, inner), BF16),
            jax.ShapeDtypeStruct((group, n_conv), BF16),
            jax.ShapeDtypeStruct((group, 2 * STATE), BF16),
            jax.ShapeDtypeStruct((group, inner), BF16),
            jax.ShapeDtypeStruct((chunks, STATE, inner), BF16),
        ],
        scratch_shapes=[pltpu.VMEM((n_conv // LANES, Q + 8, LANES), F32), pltpu.VMEM((STATE, inner), F32)],
        compiler_params=params(),
        cost_estimate=SMALL_COST,
        name="scan_forward",
    )(ends, x_raw, small, taps, par, skip)

    cot_all = in_order(cotangent, other_cot)
    if by_hand:
        normed, cot_all = lax.optimization_barrier((normed, after(cot_all, y_all)))
    tile = 512
    columns = lambda rows, shift=0: pl.BlockSpec((rows, tile), lambda j: (0, j + shift))
    fixed = lambda shape: pl.BlockSpec(shape, lambda j: (0, 0))
    tiles = inner // tile
    z_all, gg, sq = pl.pallas_call(
        gate_forward,
        grid=(tiles,),
        in_specs=[fixed((group, depth)), columns(depth), columns(group), columns(8)],
        out_specs=[columns(group), columns(group), fixed((8, group))],
        out_shape=[
            jax.ShapeDtypeStruct((group, inner), BF16),
            jax.ShapeDtypeStruct((group, inner), BF16),
            jax.ShapeDtypeStruct((8, group), F32),
        ],
        scratch_shapes=[pltpu.VMEM((group, LANES), F32)],
        compiler_params=params(),
        cost_estimate=SMALL_COST,
        name="gate_forward",
    )(normed, zo_all, y_all, taps)
    sq_got = swap(sq)

    u_own, u_send, prod = pl.pallas_call(
        branch,
        grid=(depth // tile,),
        in_specs=[
            smem,
            smem,
            fixed((group, inner)),
            columns(own_rows),
            columns(own_rows),
            pl.BlockSpec((tile, inner), lambda j: (j, 1)),
        ],
        out_specs=[columns(own_rows), columns(own_rows), fixed((8, group))],
        out_shape=[
            jax.ShapeDtypeStruct((own_rows, depth), BF16),
            jax.ShapeDtypeStruct((own_rows, depth), BF16),
            jax.ShapeDtypeStruct((8, group), F32),
        ],
        scratch_shapes=[pltpu.VMEM((group, LANES), F32)],
        compiler_params=params(),
        cost_estimate=SMALL_COST,
        name="branch",
    )(me, ends, gg, cotangent, other_cot, zo_all)
    prod_got = swap(prod)
    sq_all = sq + after(sq_got, prod)
    inv_gate8 = lax.rsqrt(sq_all / inner_total + EPSILON)
    inv_gate = inv_gate8[0]
    d_branch = (cot_all.astype(F32) * (live * inv_gate)[:, None]).astype(BF16)
    g_out = lax.dot_general(d_branch, gg, TN, preferred_element_type=F32).astype(BF16)
    grad_out = lax.psum_scatter(g_out, "dp", scatter_dimension=0, tiled=True)
    prod_got = after(prod_got, g_out)
    u_recv = swap(after(u_send, g_out))
    inv_own = lax.dynamic_slice_in_dim(inv_gate, me_t * own_rows, own_rows, 0)
    out_branch = (u_own.astype(F32) + u_recv.astype(F32)) * (inv_own * live_own)[:, None]
    layer_out = (tokens.astype(F32) + out_branch).astype(BF16)

    prod_all = prod + prod_got
    coef8 = inv_gate8 * inv_gate8 * inv_gate8 * (prod_all / inner_total)
    dy, dz, gain_acc = pl.pallas_call(
        gate_backward,
        grid=(tiles,),
        in_specs=[
            smem,
            smem,
            fixed((own_rows, depth)),
            fixed((own_rows, depth)),
            columns(depth, tiles),
            columns(group),
            columns(group),
            fixed((8, group)),
            fixed((8, group)),
            columns(8),
        ],
        out_specs=[columns(group), columns(group), columns(8)],
        out_shape=[
            jax.ShapeDtypeStruct((group, inner), BF16),
            jax.ShapeDtypeStruct((group, inner), BF16),
            jax.ShapeDtypeStruct((8, inner), F32),
        ],
        scratch_shapes=[pltpu.VMEM((group, LANES), F32), pltpu.VMEM((group, LANES), F32)],
        compiler_params=params(),
        cost_estimate=SMALL_COST,
        name="gate_backward",
    )(me, ends, cotangent, other_cot, zo_all, y_all, z_all, inv_gate8, coef8, taps)
    dot = partial(lax.dot_general, preferred_element_type=F32)
    front = depth // 2

    def gradient(d, width):
        outs = pl.BlockSpec((front, width), lambda j: (0, j))
        return pl.pallas_call(
            weight_grad,
            grid=(d.shape[1] // width,),
            in_specs=[smem, fixed((depth, own_rows)), fixed((depth, own_rows)), pl.BlockSpec((group, width), lambda j: (0, j))],
            out_specs=[outs, outs],
            out_shape=[jax.ShapeDtypeStruct((front, d.shape[1]), BF16)] * 2,
            compiler_params=params(),
            cost_estimate=SMALL_COST,
            name="weight_grad",
        )(me, turned_own, turned_other, d)

    if by_hand:
        g_send, z_keep = gradient(dz, tile)
        z_got = send(g_send, beside)
        dy = after(dy, z_keep, g_send)
    else:
        grad_z = lax.psum_scatter(dot(normed, dz, TN).astype(BF16), "dp", scatter_dimension=0, tiled=True)

    n_a = inner * 2 // 3
    n_b = inner + n_small - n_a

    def backward(base, width, carry):
        at = base // width
        back = lambda size, column: pl.BlockSpec((Q, size), lambda i: (chunks - 1 - i, column))
        operands = [ends, dy, xc, pre, x_raw, small, bc, states, taps, par, skip, sel]
        in_specs = [
            smem,
            back(width, at),
            back(width, at),
            back(width, at),
            back(width, at),
            back(n_small, 0),
            back(2 * STATE, 0),
            pl.BlockSpec((1, STATE, width), lambda i: (chunks - 1 - i, 0, at)),
            whole_spec((8, width), at),
            whole_spec((8, LANES)),
            whole_spec((1, width), at),
            pl.BlockSpec((width, LANES), lambda i: (at, 0)),
        ]
        tiles_held = width + (2 * STATE if carry else 0)
        acc_shape, hacc_shape = (8 * (K + 2), tiles_held), (16, LANES)
        if carry:
            last = inner // (2 * STATE)
            operands += [pre, taps, *carry]
            in_specs += [back(2 * STATE, last), whole_spec((8, 2 * STATE), last), back(n_small, 0)]
            in_specs += [whole_spec((8 * (K + 2), base)), whole_spec(hacc_shape), whole_spec((8, inner))]
            out_specs = [back(n_b, 0), whole_spec((8, n_conv))]
            out_shape = [jax.ShapeDtypeStruct((group, n_b), BF16), jax.ShapeDtypeStruct((8, n_conv), F32)]
        else:
            out_specs = [back(width, 0), back(n_small, 0)]
            out_shape = [jax.ShapeDtypeStruct((group, width), BF16), jax.ShapeDtypeStruct((group, n_small), F32)]
        return pl.pallas_call(
            partial(scan_backward, base, bool(carry), chunks),
            grid=(chunks,),
            in_specs=in_specs,
            out_specs=out_specs + [whole_spec(acc_shape), whole_spec(hacc_shape)],
            out_shape=out_shape + [jax.ShapeDtypeStruct(acc_shape, F32), jax.ShapeDtypeStruct(hacc_shape, F32)],
            scratch_shapes=[
                pltpu.VMEM((STATE, width), F32),
                pltpu.VMEM((tiles_held // LANES, Q + 8, LANES), F32),
                *[pltpu.VMEM((Q, width), BF16)] * 6,
                pltpu.VMEM((STATE, width), BF16),
                pltpu.VMEM((8, width), F32),
            ],
            compiler_params=params(),
            cost_estimate=SMALL_COST,
            name="scan_backward",
        )(*operands)

    dxa, part, acc, hacc = backward(0, n_a, ())
    if by_hand:
        z_got, dxa = lax.optimization_barrier((z_got, dxa))
        z_away, z_core = fold_away(z_keep, z_got)
        z_got = send(z_away, across)
        dxa, part = lax.optimization_barrier((dxa, part, z_away))[:2]
        g_x, grad_out = lax.optimization_barrier((dot(normed, dxa, TN).astype(BF16), grad_out))
        grad_a = lax.psum_scatter(g_x, "dp", scatter_dimension=0, tiled=True)
        part = after(part, g_x)
    dxb, vector = backward(n_a, inner - n_a, (part, acc, hacc, gain_acc))[:2]
    dxb = after(dxb, u_recv)
    lanes_shared = lax.iota(jnp.int32, n_conv)[None, :] >= inner
    bits_of = lambda turn: [(i, i ^ (1 << turn)) for i in range(n_dp)]
    if by_hand:
        z_got, dxb, vector = lax.optimization_barrier((z_got, dxb, vector))
        z_out = ring_part(z_keep, z_core, z_got, None, 1)
        z_came = send(z_out, around)
        shared_got = swap(vector)
        b_send, b_keep = gradient(after(dxb, z_out), n_b)
        b_got = send(b_send, beside)
        shared_got, z_came, b_keep = lax.optimization_barrier((shared_got, z_came, b_keep))
        vector = vector + jnp.where(lanes_shared, shared_got, 0.0)
        z_out = ring_part(z_keep, z_core, z_got, z_came, 2)
        z_came, vector_got = send(z_out, around), send(vector, bits_of(0))
        dz = after(dz, b_send, b_keep, z_out, vector)
    else:
        dx = jnp.concatenate([dxa, dxb], axis=1)
        grad_x = lax.psum_scatter(dot(normed, dx, TN).astype(BF16), "dp", scatter_dimension=0, tiled=True)

    def back_rows(which, dz):
        pick = lambda width: pl.BlockSpec((own_rows, width), lambda j, rows: (rows[0], 0))
        return pl.pallas_call(
            normed_back,
            grid_spec=pltpu.PrefetchScalarGridSpec(
                num_scalar_prefetch=1,
                grid=(depth // tile,),
                in_specs=[
                    pick(inner),
                    pick(n_a),
                    pick(n_b),
                    pl.BlockSpec((tile, inner), lambda j, rows: (j, 0)),
                    pl.BlockSpec((tile, inner + n_small), lambda j, rows: (j, 0)),
                ],
                out_specs=pl.BlockSpec((own_rows, tile), lambda j, rows: (0, j)),
            ),
            out_shape=jax.ShapeDtypeStruct((own_rows, depth), BF16),
            compiler_params=params(),
            cost_estimate=SMALL_COST,
            name="normed_back",
        )(which, dz, dxa, dxb, zo_all, wx_all)

    dn_send = back_rows(n_t - 1 - me, dz)
    if by_hand:
        w_sum = lambda w, g: jnp.sum(w.astype(F32) * g, axis=1)
        b_got, vector_got, dn_send, z_came = lax.optimization_barrier((b_got, vector_got, dn_send, z_came))
        b_away, b_core = fold_away(b_keep, b_got)
        b_got = send(b_away, across)
        dn_got = swap(after(dn_send, b_away))
        vector = vector + after(vector_got, b_away)
        vector_got = send(vector, bits_of(1))
        dn_own = back_rows(me, after(dz, vector, b_away))
        vector_got, dn_own, b_got, z_came, grad_a = lax.optimization_barrier((vector_got, dn_own, b_got, z_came, grad_a))
        vector = vector + vector_got
        b_out = ring_part(b_keep, b_core, b_got, None, 1)
        b_came = send(b_out, around)
        z_out = ring_part(z_keep, z_core, z_got, z_came, 3)
        z_came, vector_got = send(z_out, around), send(vector, bits_of(2))
        grad_a = grad_a.astype(F32)
        in_part = w_sum(w_x[:, :n_a], grad_a)
        vector_got, z_came, in_part, b_came = lax.optimization_barrier((vector_got, z_came, in_part, b_came))
        vector = vector + vector_got
        b_out = ring_part(b_keep, b_core, b_got, b_came, 2)
        b_came, vector_got = send(b_out, around), send(vector, bits_of(3))
        grad_z = ring_part(z_keep, z_core, z_got, z_came, ring) * gain_pair
        in_part = in_part + w_sum(w_zx[0], grad_z)
        grad_out = grad_out.astype(F32).T
        vector_got, grad_out, layer_out, b_came, grad_z, in_part = lax.optimization_barrier(
            (vector_got, grad_out, layer_out, b_came, grad_z, in_part)
        )
        vector = vector + vector_got
        b_came = send(ring_part(b_keep, b_core, b_got, b_came, 3), around)
    else:
        vector = sum_dp(vector + jnp.where(lanes_shared, swap(vector), 0.0))
        dn_own = back_rows(me, dz)
        dn_got = swap(dn_send)
        grad_out = grad_out.astype(F32).T
        grad_z, grad_x = grad_z.astype(F32), grad_x.astype(F32)
        in_part = jnp.sum(w_zx[0].astype(F32) * grad_z, axis=1) + jnp.sum(jnp.concatenate([w_x, w_small], axis=1).astype(F32) * grad_x, axis=1)

    me_all = me_dp * n_t + me_t
    bc_sum = vector[: K + 1, inner:].reshape(K + 1, 2, STATE)
    bc_sum = lax.dynamic_slice_in_dim(bc_sum, me_all * span_n, span_n, 2)
    grad_bc_taps = bc_sum[:K].transpose(1, 2, 0).reshape(conv_bc.shape)
    grad_bc_bias = bc_sum[K]
    x_sum = vector[: K + 3, :inner].reshape(K + 3, heads, WIDTH)
    grad_skip = x_sum[K + 1].sum(axis=1)
    x_sum = lax.dynamic_slice_in_dim(x_sum, me_dp * span_p, span_p, 2)
    grad_x_taps = x_sum[:K].transpose(1, 2, 0).reshape(conv_x.shape)
    grad_x_bias = x_sum[K]
    grad_gate = x_sum[K + 2]
    grad_dt_bias = vector[K + 3, :heads]
    grad_a_log = vector[K + 3, LANES : LANES + heads]
    dn = (dn_own.astype(F32) + dn_got.astype(F32)) * gain_in[0:1, :]
    grad_tokens = (
        cotangent.astype(F32)
        + inv_tok * dn
        - tok_own * inv_tok * inv_tok * inv_tok * jnp.mean(dn * tok_own, axis=1, keepdims=True)
    )

    if by_hand:
        outs = (grad_bc_taps, grad_bc_bias, grad_skip, grad_x_taps, grad_x_bias, grad_gate, grad_dt_bias, grad_a_log)
        outs = lax.optimization_barrier((*outs, grad_tokens, b_came))
        grad_bc_taps, grad_bc_bias, grad_skip, grad_x_taps, grad_x_bias, grad_gate, grad_dt_bias, grad_a_log = outs[:8]
        grad_tokens, b_came = outs[8:]
        grad_b = ring_part(b_keep, b_core, b_got, b_came, ring) * gain_pair
        in_part = in_part + w_sum(w_x[:, n_a:], grad_b[:, : inner - n_a]) + w_sum(w_small, grad_b[:, inner - n_a :])
    else:
        grad_a, grad_b = grad_x[:, :n_a], grad_x[:, n_a:]
    at = inner - n_a
    bc_part = jnp.concatenate([grad_b[:, at : at + 2 * STATE], jnp.broadcast_to(in_part[:, None], (shard, LANES))], axis=1)
    grad_zx = jnp.stack([grad_z, jnp.concatenate([grad_a, grad_b[:, :at]], axis=1)])
    grad_dt = grad_b[:, at + 2 * STATE : at + 2 * STATE + heads]
    half = half_bc
    bc_own = lax.dynamic_slice_in_dim(bc_part, me_t * half, half, 0)
    bc_send = lax.dynamic_slice_in_dim(bc_part, (n_t - 1 - me_t) * half, half, 0)
    bc_total = bc_own + swap(bc_send)
    own_gain = norm_gain.astype(F32)
    grad_bc = bc_total[:, : 2 * STATE].reshape(half, 2, STATE).transpose(1, 0, 2)
    grad_in = bc_total[:, 2 * STATE] / own_gain
    return (
        layer_out,
        grad_tokens,
        grad_in,
        grad_zx,
        grad_bc,
        grad_dt,
        grad_x_taps,
        grad_x_bias,
        grad_bc_taps,
        grad_bc_bias,
        grad_dt_bias,
        grad_a_log,
        grad_skip,
        grad_gate,
        grad_out,
    )


def solution(mesh):
    both = ("dp", "tensor")
    in_specs = (
        P(both, None),
        P(both, None),
        P("dp", None),
        P(both),
        P(None, "dp", "tensor"),
        P(None, both, None),
        P("dp", "tensor"),
        P("tensor", "dp"),
        P("tensor", "dp"),
        P(None, both),
        P(None, both),
        P("tensor"),
        P("tensor"),
        P("tensor"),
        P("tensor", "dp"),
        P("tensor", "dp"),
    )
    out_specs = (
        P(both, None),
        P(both, None),
        P(both),
        P(None, "dp", "tensor"),
        P(None, both, None),
        P("dp", "tensor"),
        P("tensor", "dp"),
        P("tensor", "dp"),
        P(None, both),
        P(None, both),
        P("tensor"),
        P("tensor"),
        P("tensor"),
        P("tensor", "dp"),
        P("tensor", "dp"),
    )
    return jax.shard_map(local, mesh=mesh, in_specs=in_specs, out_specs=out_specs, check_vma=False)
```

```python
from functools import partial

import jax
import jax.numpy as jnp
from jax import lax
from jax.experimental import pallas as pl
from jax.experimental.pallas import tpu as pltpu
from jax.sharding import PartitionSpec as P

EPSILON = 1e-05
HIGHEST = lax.Precision.HIGHEST
K = 4
WIDTH = 64
STATE = 128
Q = 128
LANES = 128
LOG2E = 1.4426950408889634
VMEM_LIMIT = 60 * 1024 * 1024
F32 = jnp.float32
BF16 = jnp.bfloat16

NN = (((1,), (0,)), ((), ()))
NT = (((1,), (1,)), ((), ()))
TN = (((0,), (0,)), ((), ()))


def mm(a, b, dims=NN):
    return lax.dot_general(a, b, dims, preferred_element_type=F32)


def mm_exact(a, b, dims=NN):
    return lax.dot_general(a, b, dims, preferred_element_type=F32, precision=HIGHEST)


def iota(shape, dim):
    return lax.broadcasted_iota(jnp.int32, shape, dim)


def segment_of(rows, ends_ref, count):
    total = (rows >= ends_ref[0]).astype(jnp.int32)
    for j in range(1, count):
        total = total + (rows >= ends_ref[j]).astype(jnp.int32)
    return total


def scalar_segment(row, ends_ref, count):
    total = jnp.where(row >= ends_ref[0], 1, 0)
    for j in range(1, count):
        total = total + jnp.where(row >= ends_ref[j], 1, 0)
    return total


def sigmoid(v):
    return 0.5 * jnp.tanh(0.5 * v) + 0.5


def softplus(v):
    return jnp.maximum(v, 0.0) + jnp.log1p(jnp.exp(-jnp.abs(v)))


def chunk_masks(chunk, ends_ref, count):
    base = chunk * Q
    rows = iota((Q, Q), 0) + base
    cols = iota((Q, Q), 1) + base
    row_ids = segment_of(rows, ends_ref, count)
    col_ids = segment_of(cols, ends_ref, count)
    same = row_ids == col_ids
    before_id = jnp.where(chunk == 0, -1, scalar_segment(base - 1, ends_ref, count))
    final_id = scalar_segment(base + Q - 1, ends_ref, count)
    carry = (row_ids == before_id).astype(F32)
    last = (row_ids == final_id).astype(F32)
    passing = jnp.where(before_id == final_id, 1.0, 0.0).astype(F32)
    return rows, cols, row_ids, same, carry, last, passing


def decays(dt_raw, par_ref):
    shifted = dt_raw + par_ref[0:1, :]
    step = softplus(shifted)
    decay_rate = jnp.exp(par_ref[1:2, :])
    return shifted, step, decay_rate


def pair_columns(values, pair, first):
    left = jnp.broadcast_to(values[:, 2 * pair : 2 * pair + 1], (Q, LANES))
    right = jnp.broadcast_to(values[:, 2 * pair + 1 : 2 * pair + 2], (Q, LANES))
    return left, right, jnp.where(first, left, right)


def scan_forward(
    heads, ends_ref, xr_ref, small_ref, taps_ref, par_ref, skip_ref,
    xc_ref, pre_ref, bc_ref, y_ref, st_ref, buf, state,
):
    count = ends_ref.shape[0]
    inner = heads * WIDTH
    chunk = pl.program_id(0)

    @pl.when(chunk == 0)
    def _():
        buf[:, 0:8, :] = jnp.zeros((buf.shape[0], 8, LANES), F32)
        state[...] = jnp.zeros(state.shape, F32)

    rows, cols, row_ids, same, carry, last, passing = chunk_masks(chunk, ends_ref, count)
    causal = rows >= cols
    visible = same & causal
    lag_mask = [None]
    for lag in range(1, K):
        earlier = rows - lag
        keep = (segment_of(earlier, ends_ref, count) == row_ids) & (earlier >= 0)
        lag_mask.append(keep.astype(F32))

    small = small_ref[...]

    def convolve(lo, raw):
        span = slice(lo, lo + LANES)
        place = lo // LANES
        buf[place, 8 : 8 + Q, :] = raw
        pre = taps_ref[K : K + 1, span] + taps_ref[K - 1 : K, span] * raw
        for lag in range(1, K):
            pre = pre + taps_ref[K - 1 - lag : K - lag, span] * (
                buf[place, 8 - lag : 8 - lag + Q, :] * lag_mask[lag]
            )
        buf[place, 0:8, :] = raw[Q - 8 : Q, :]
        pre_ref[:, span] = pre.astype(BF16)
        return pre * sigmoid(pre)

    b_f = convolve(inner, small[:, :STATE]).astype(BF16).astype(F32)
    c_b = convolve(inner + STATE, small[:, STATE : 2 * STATE]).astype(BF16)
    b_b = b_f.astype(BF16)
    bc_ref[:, :STATE] = b_b
    bc_ref[:, STATE:] = c_b
    b_t = b_f.T.astype(BF16)

    _, step, decay_rate = decays(small[:, 2 * STATE :], par_ref)
    csum = mm_exact(causal.astype(F32), step * (-LOG2E * decay_rate))
    csum_t = csum.T
    scores = jnp.where(visible, mm(c_b, b_b, NT), 0.0)
    first = iota((Q, LANES), 1) < WIDTH
    first_row = iota((1, LANES), 1) < WIDTH

    wide = 2 * LANES
    for quad in range(0, inner, wide):
        block = slice(quad, quad + wide)
        held = state[:, block]
        held_b = held.astype(BF16)
        st_ref[0, :, block] = held_b
        carried = mm(c_b, held_b)
        weighted, kept = [], []
        for part in range(0, wide, LANES):
            lo = quad + part
            pair = lo // LANES
            span = slice(lo, lo + LANES)
            xc = convolve(lo, xr_ref[:, span].astype(F32)).astype(BF16)
            xc_ref[:, span] = xc
            xc = xc.astype(F32)
            left, right, both = pair_columns(csum, pair, first)
            _, _, step_pair = pair_columns(step, pair, first)
            mix = jnp.concatenate(
                [
                    (scores * jnp.exp2(jnp.minimum(left - csum_t[2 * pair : 2 * pair + 1, :], 0.0))).astype(BF16),
                    (scores * jnp.exp2(jnp.minimum(right - csum_t[2 * pair + 1 : 2 * pair + 2, :], 0.0))).astype(BF16),
                ],
                axis=1,
            )
            fed_b = (xc * step_pair).astype(BF16)
            zero = jnp.zeros((Q, LANES), BF16)
            stacked = jnp.concatenate([jnp.where(first, fed_b, zero), jnp.where(first, zero, fed_b)], axis=0)
            y = mm(mix, stacked) + carried[:, part : part + LANES] * (jnp.exp2(both) * carry)
            y_ref[:, span] = (y + skip_ref[:, span] * xc).astype(BF16)
            closing = both[Q - 1 : Q, :]
            weighted.append((fed_b.astype(F32) * (jnp.exp2(closing - both) * last)).astype(BF16))
            kept.append(jnp.exp2(closing) * passing)
        fresh = mm(b_t, jnp.concatenate(weighted, axis=1))
        state[:, block] = held * jnp.concatenate(kept, axis=1) + fresh


def scan_backward(
    base, last_call, chunks, ends_ref, dy_ref, xc_ref, pre_ref, xr_ref, small_ref, bc_ref, st_ref, taps_ref,
    par_ref, skip_ref, sel_ref, *refs,
):
    if last_call:
        pre_bc_ref, taps_bc_ref, part_in, acc_in, hacc_in, gain_acc_ref = refs[:6]
        dx_ref, rows_ref, acc_ref, hacc_ref = refs[6:10]
        refs = refs[10:]
    else:
        dx_ref, part_ref, acc_ref, hacc_ref = refs[:4]
        refs = refs[4:]
    dstate, dpre, ab_hi, ab_lo, v_b, u_b, dyd, fedw, dst_b, through = refs
    count = ends_ref.shape[0]
    inner = dy_ref.shape[1]
    total_rows = chunks * Q
    chunk = chunks - 1 - pl.program_id(0)

    @pl.when(pl.program_id(0) == 0)
    def _():
        dpre[:, Q : Q + 8, :] = jnp.zeros((dpre.shape[0], 8, LANES), F32)
        dstate[...] = jnp.zeros(dstate.shape, F32)
        acc_ref[...] = jnp.zeros(acc_ref.shape, F32)
        hacc_ref[...] = hacc_in[...] if last_call else jnp.zeros(hacc_ref.shape, F32)

    rows, cols, row_ids, same, carry, last, passing = chunk_masks(chunk, ends_ref, count)
    causal = rows >= cols
    visible = same & causal
    lag_mask = [None]
    for lag in range(1, K):
        later = rows + lag
        keep = (segment_of(later, ends_ref, count) == row_ids) & (later < total_rows)
        lag_mask.append(keep.astype(F32))

    small = small_ref[...]
    shifted, step, decay_rate = decays(small[:, 2 * STATE :], par_ref)
    csum = mm_exact(causal.astype(F32), step * (-LOG2E * decay_rate))
    csum_t = csum.T
    b_b = bc_ref[:, :STATE]
    c_b = bc_ref[:, STATE:]
    c_t = c_b.astype(F32).T.astype(BF16)
    scores = jnp.where(visible, mm(c_b, b_b, NT), 0.0)
    first = iota((Q, LANES), 1) < WIDTH

    def fold(values):
        return values.reshape(Q // 8, 8, values.shape[1]).sum(axis=0)

    def conv_back(lo, d_conv, raw, pre, taps, at):
        span = slice(lo, lo + LANES)
        place = lo // LANES
        gate = sigmoid(pre)
        d_pre = d_conv * (gate * (1.0 + pre * (1.0 - gate)))
        dpre[place, 0:Q, :] = d_pre
        d_raw = taps[K - 1 : K, at] * d_pre
        acc_ref[8 * (K - 1) : 8 * K, span] += fold(d_pre * raw)
        acc_ref[8 * K : 8 * K + 8, span] += fold(d_pre)
        for lag in range(1, K):
            moved = dpre[place, lag : lag + Q, :] * lag_mask[lag]
            d_raw = d_raw + taps[K - 1 - lag : K - lag, at] * moved
            acc_ref[8 * (K - 1 - lag) : 8 * (K - lag), span] += fold(moved * raw)
        dpre[place, Q : Q + 8, :] = d_pre[0:8, :]
        dx_ref[:, span] = d_raw.astype(BF16)

    d_scores = jnp.zeros((Q, Q), F32)
    wide = 2 * LANES
    for quad in range(0, inner, wide):
        block = slice(quad, quad + wide)
        held_b = st_ref[0, :, block]
        d_held = dstate[:, block]
        d_held_b = d_held.astype(BF16)
        dst_b[:, block] = d_held_b
        carried = mm(c_b, held_b)
        returned = mm(b_b, d_held_b)
        crossing = (d_held * held_b.astype(F32)).reshape(STATE // 8, 8, wide).sum(axis=0)
        grown_parts, kept_parts = [], []
        for part in range(0, wide, LANES):
            lo = quad + part
            pair = (base + lo) // LANES
            span = slice(lo, lo + LANES)
            xc = xc_ref[:, span].astype(F32)
            dy_b = dy_ref[:, span]
            dy = dy_b.astype(F32)
            left, right, both = pair_columns(csum, pair, first)
            _, _, step_pair = pair_columns(step, pair, first)
            fall_left = jnp.exp2(jnp.minimum(left - csum_t[2 * pair : 2 * pair + 1, :], 0.0))
            fall_right = jnp.exp2(jnp.minimum(right - csum_t[2 * pair + 1 : 2 * pair + 2, :], 0.0))
            mix = jnp.concatenate([(scores * fall_left).astype(BF16), (scores * fall_right).astype(BF16)], axis=1)
            fed_b = (xc * step_pair).astype(BF16)
            fed = fed_b.astype(F32)
            zero = jnp.zeros((Q, LANES), BF16)
            stacked = jnp.concatenate([jnp.where(first, fed_b, zero), jnp.where(first, zero, fed_b)], axis=0)
            grown = jnp.exp2(both) * carry
            y = mm(mix, stacked) + carried[:, part : part + LANES] * grown
            d_mix = mm(dy_b, stacked, NT)
            d_scores = d_scores + d_mix[:, :Q] * fall_left + d_mix[:, Q:] * fall_right
            d_fed2 = mm(mix, dy_b, TN)
            d_fed_in = jnp.where(first, d_fed2[:Q], d_fed2[Q:])
            closing = both[Q - 1 : Q, :]
            shrink = jnp.exp2(closing - both) * last
            d_fed_out = returned[:, part : part + LANES] * shrink
            d_fed = d_fed_in + d_fed_out
            straddle = dy * y - fed * d_fed_in
            hi = straddle.astype(BF16)
            ab_hi[:, span] = hi
            ab_lo[:, span] = (straddle - hi.astype(F32)).astype(BF16)
            v_b[:, span] = (fed * d_fed_out).astype(BF16)
            u_b[:, span] = (xc * d_fed).astype(BF16)
            fedw[:, span] = (fed * shrink).astype(BF16)
            grown_parts.append((dy * grown).astype(BF16))
            kept_parts.append(jnp.exp2(closing) * passing)
            acc_ref[8 * K + 8 : 8 * K + 16, span] += fold(dy * xc)
            d_conv = d_fed * step_pair + skip_ref[:, span] * dy
            conv_back(lo, d_conv, xr_ref[:, span].astype(F32), pre_ref[:, span].astype(F32), taps_ref, span)
        dy_grown = jnp.concatenate(grown_parts, axis=1)
        kept = jnp.concatenate(kept_parts, axis=1)
        dyd[:, block] = dy_grown
        through[:, block] = crossing * kept
        dstate[:, block] = d_held * kept + mm(c_t, dy_grown)

    d_scores_b = jnp.where(visible, d_scores, 0.0).astype(BF16)
    d_c = mm(dyd[...], st_ref[0], NT) + mm(d_scores_b, b_b)
    d_b = mm(fedw[...], dst_b[...], NT) + mm(d_scores_b, c_b, TN)
    sel = sel_ref[...]
    red_ab = mm(ab_hi[...], sel) + mm(ab_lo[...], sel)
    red_v = mm(v_b[...], sel)
    red_u = mm(u_b[...], sel)
    thr = through[...]
    thr_hi = thr.astype(BF16)
    red_t = mm(thr_hi, sel) + mm((thr - thr_hi.astype(F32)).astype(BF16), sel)
    d_rate = (
        mm_exact((same & (cols >= rows)).astype(F32), red_ab)
        + mm_exact((same & (cols < rows)).astype(F32), red_v)
        + jnp.sum(red_t, axis=0, keepdims=True)
    )
    d_step = red_u - d_rate * decay_rate
    d_dt = d_step * sigmoid(shifted)
    hacc_ref[0:8, :] += fold(d_dt)
    hacc_ref[8:16, :] += fold(d_rate * (-decay_rate * step))
    if not last_call:
        part_ref[:, :STATE] = d_b
        part_ref[:, STATE : 2 * STATE] = d_c
        part_ref[:, 2 * STATE :] = d_dt
        return

    for k, d_conv in enumerate((d_b, d_c)):
        at = slice(k * STATE, (k + 1) * STATE)
        pre = pre_bc_ref[:, at].astype(F32)
        conv_back(inner + k * STATE, d_conv + part_in[:, at], small[:, at], pre, taps_bc_ref, at)
    dx_ref[:, inner + 2 * STATE :] = (d_dt + part_in[:, 2 * STATE :]).astype(BF16)

    @pl.when(pl.program_id(0) == pl.num_programs(0) - 1)
    def _():
        before = acc_in.shape[1]
        whole = before + inner
        rows_ref[...] = jnp.zeros(rows_ref.shape, F32)
        for k in range(K + 2):
            block = slice(8 * k, 8 * k + 8)
            rows_ref[k : k + 1, :before] = jnp.sum(acc_in[block, :], axis=0, keepdims=True)
            rows_ref[k : k + 1, before:] = jnp.sum(acc_ref[block, :], axis=0, keepdims=True)
        rows_ref[K + 2 : K + 3, :whole] = jnp.sum(gain_acc_ref[...], axis=0, keepdims=True)
        for k in range(2):
            total = jnp.sum(hacc_ref[8 * k : 8 * k + 8, :], axis=0, keepdims=True)
            rows_ref[K + 3 : K + 4, k * LANES : (k + 1) * LANES] = total


def load_blocks(offsets_ref, parts, whole, sems, size, columns, first=0):
    @pl.when(pl.program_id(0) == 0)
    def _():
        copies = []
        for part in parts:
            for j in range(part.shape[0] // size):
                k = first + len(copies)
                start = 0 if size == whole.shape[0] else pl.multiple_of(offsets_ref[k], 32)
                source = part.at[pl.ds(j * size, size), :]
                copies.append(pltpu.make_async_copy(source, whole.at[pl.ds(start, size), slice(*columns)], sems.at[k]))
        for copy in copies:
            copy.start()
        for copy in copies:
            copy.wait()


def turn_rows(offsets_ref, source_ref, out_ref, turned):
    rows, depth = source_ref.shape
    for lo in range(0, rows, Q):
        tile = source_ref[lo : lo + Q, :].astype(F32)
        tile = tile * lax.rsqrt(jnp.mean(tile * tile, axis=1, keepdims=True) + EPSILON)
        for left in range(0, depth, LANES):
            turned[left : left + LANES, lo : lo + Q] = tile[:, left : left + LANES].T.astype(BF16)
    count = offsets_ref.shape[0]
    size = depth // count
    for k in range(count):
        start = pl.multiple_of(offsets_ref[k], 32)
        out_ref[k * size : (k + 1) * size, :] = turned[pl.ds(start, size), :]


def project(counts, heads, size, offsets_ref, me_ref, own_ref, other_ref, place_ref, *refs):
    count = sum(counts)
    blocks, (x_ref, small_ref, normed_ref, taps_ref, gain_ref, w_out_ref, w_ref, sems, out_sem) = refs[:count], refs[count:]
    split = x_ref.shape[1]
    shards = w_ref.shape[0] // size
    load_blocks(offsets_ref, blocks[: counts[0]], w_ref, sems, size, (0, split))
    load_blocks(offsets_ref, blocks[counts[0] :], w_ref, sems, size, (split, w_ref.shape[1]), shards)
    keep = pltpu.make_async_copy(w_ref, w_out_ref, out_sem)
    depth, inner = w_ref.shape[0], x_ref.shape[1]
    tile = 512

    @pl.when(pl.program_id(0) == 0)
    def _():
        keep.start()
        spare = w_ref[:, inner + 2 * STATE :]
        turned = spare.astype(F32).T
        gain_ref[...] = jnp.broadcast_to(turned[heads + K + 2 : heads + K + 3, :], gain_ref.shape)
        few = turned[heads : heads + 16, :].astype(BF16)
        lanes = iota((depth, LANES), 1)
        for lo in range(0, inner + 2 * STATE, LANES):
            if lo < inner:
                wanted, row = place_ref[:, :LANES] == lanes + lo, 0
            else:
                wanted, row = place_ref[:, LANES:] == lanes + (lo - inner), 8
            moved = mm(few, jnp.where(wanted, 1.0, 0.0).astype(BF16))
            taps_ref[:, lo : lo + LANES] = moved[row : row + 8, :]

    rows = jnp.where(pl.program_id(0) == me_ref[0], own_ref[...], other_ref[...]).astype(F32)
    scale = lax.rsqrt(jnp.mean(rows * rows, axis=1, keepdims=True) + EPSILON)
    rows = (rows * scale * gain_ref[0:1, :]).astype(BF16)
    normed_ref[...] = rows
    for lo in range(0, inner, tile):
        x_ref[:, lo : lo + tile] = mm(rows, w_ref[:, lo : lo + tile]).astype(BF16)
    small_ref[...] = mm(rows, w_ref[:, inner:])

    @pl.when(pl.program_id(0) == pl.num_programs(0) - 1)
    def _():
        keep.wait()


def row_sums(lanes):
    return mm_exact(jnp.ones((8, LANES), F32), lanes, NT)


def spread_rows(values):
    pick = jnp.where(iota((8, LANES), 0) == 0, 1.0, 0.0).astype(F32)
    return mm_exact(values, pick, TN)


def gate_forward(normed_ref, w_ref, y_ref, gain_ref, z_ref, gg_ref, sq_ref, square):
    rows, width = z_ref.shape
    size = 512

    @pl.when(pl.program_id(0) == 0)
    def _():
        square[...] = jnp.zeros(square.shape, F32)

    for lo in range(0, rows, size):
        at = slice(lo, lo + size)
        z = mm(normed_ref[at, :], w_ref[...]).astype(BF16)
        z_ref[at, :] = z
        z = z.astype(F32)
        gated = y_ref[at, :].astype(F32) * (z * sigmoid(z))
        gg_ref[at, :] = (gated * gain_ref[K + 1 : K + 2, :]).astype(BF16)
        twice = gated * gated
        for part in range(0, width, LANES):
            square[at, :] += twice[:, part : part + LANES]

    @pl.when(pl.program_id(0) == pl.num_programs(0) - 1)
    def _():
        sq_ref[...] = row_sums(square[...])


def branch(me_ref, ends_ref, gg_ref, own_ref, other_ref, w_ref, mine_ref, away_ref, prod_ref, product):
    rows, width = mine_ref.shape
    size = 512

    @pl.when(pl.program_id(0) == 0)
    def _():
        product[...] = jnp.zeros(product.shape, F32)

    for index, (out_ref, cot_ref) in enumerate(((mine_ref, own_ref), (away_ref, other_ref))):
        first = jnp.where(index == 0, me_ref[0], 1 - me_ref[0]) * rows
        for lo in range(0, rows, size):
            at = pl.ds(pl.multiple_of(first + lo, size), size)
            u = mm(gg_ref[at, :], w_ref[...], NT)
            out_ref[lo : lo + size, :] = u.astype(BF16)
            term = u * cot_ref[lo : lo + size, :].astype(F32)
            for part in range(0, width, LANES):
                product[at, :] += term[:, part : part + LANES]

    @pl.when(pl.program_id(0) == pl.num_programs(0) - 1)
    def _():
        live = iota(product.shape, 0) < ends_ref[ends_ref.shape[0] - 1]
        prod_ref[...] = row_sums(jnp.where(live, product[...], 0.0))


def gate_backward(
    me_ref, ends_ref, own_ref, other_ref, w_ref, y_ref, z_ref, rg_ref, coef_ref, gain_ref,
    dy_ref, dz_ref, acc_ref, rg, coef,
):
    total, width = dy_ref.shape
    rows = own_ref.shape[0]
    size = 512

    @pl.when(pl.program_id(0) == 0)
    def _():
        live = iota(rg.shape, 0) < ends_ref[ends_ref.shape[0] - 1]
        rg[...] = spread_rows(rg_ref[...])
        coef[...] = spread_rows(coef_ref[...])
        rg[...] = jnp.where(live, rg[...], 0.0)

    gain = gain_ref[K + 1 : K + 2, :]
    sums = jnp.zeros((8, width), F32)
    for index, cot_ref in enumerate((own_ref, other_ref)):
        first = jnp.where(index == 0, me_ref[0], 1 - me_ref[0]) * rows
        for lo in range(0, rows, size):
            at = pl.ds(pl.multiple_of(first + lo, size), size)
            ds = mm(cot_ref[lo : lo + size, :], w_ref[...])
            z = z_ref[at, :].astype(F32)
            y = y_ref[at, :].astype(F32)
            scale = jnp.concatenate([rg[at, :]] * (width // LANES), axis=1)
            back = jnp.concatenate([coef[at, :]] * (width // LANES), axis=1)
            gate = sigmoid(z)
            silu = z * gate
            gated = y * silu
            d_normal = ds * scale
            sums = sums + (d_normal * gated).reshape(size // 8, 8, width).sum(axis=0)
            d_gated = d_normal * gain - gated * back
            dy_ref[at, :] = (d_gated * silu).astype(BF16)
            dz_ref[at, :] = (d_gated * y * (gate + silu * (1.0 - gate))).astype(BF16)
    acc_ref[...] = sums


def weight_grad(me_ref, own_ref, other_ref, d_ref, away_ref, keep_ref):
    half, rows = away_ref.shape[0], own_ref.shape[1]
    mine = d_ref[pl.ds(pl.multiple_of(me_ref[0] * rows, rows), rows), :]
    theirs = d_ref[pl.ds(pl.multiple_of((1 - me_ref[0]) * rows, rows), rows), :]
    for at, ref in ((0, away_ref), (half, keep_ref)):
        total = mm(own_ref[at : at + half, :], mine) + mm(other_ref[at : at + half, :], theirs)
        ref[...] = total.astype(BF16)


def normed_back(rows_ref, dz_ref, dxa_ref, dxb_ref, wz_ref, wx_ref, out_ref):
    n_a = dxa_ref.shape[1]
    total = mm(dz_ref[...], wz_ref[...], NT)
    total = total + mm(dxa_ref[...], wx_ref[:, :n_a], NT) + mm(dxb_ref[...], wx_ref[:, n_a:], NT)
    out_ref[...] = total.astype(BF16)


def params():
    return pltpu.CompilerParams(dimension_semantics=("arbitrary",), vmem_limit_bytes=VMEM_LIMIT)


SMALL_COST = pl.CostEstimate(flops=1000, bytes_accessed=1000, transcendentals=0)


def rows_spec(block, width, column=0):
    return pl.BlockSpec((block, width), lambda i: (i, column))


def whole_spec(shape, column=0):
    return pl.BlockSpec(shape, lambda i: (0, column))


def local(
    tokens,
    cotangent,
    lengths,
    norm_gain,
    w_zx,
    w_bc,
    w_dt,
    conv_x,
    conv_x_bias,
    conv_bc,
    conv_bc_bias,
    dt_bias,
    a_log,
    d_skip,
    gate_gain,
    w_out,
):
    n_t = lax.axis_size("tensor")
    n_dp = lax.axis_size("dp")
    me_t = lax.axis_index("tensor")
    me_dp = lax.axis_index("dp")
    own_rows, depth = tokens.shape
    group = own_rows * n_t
    chunks = group // Q
    heads = dt_bias.shape[0]
    inner = heads * WIDTH
    inner_total = inner * n_t
    shard = w_zx.shape[1]
    pairs = [(i, n_t - 1 - i) for i in range(n_t)]

    def swap(v):
        return lax.ppermute(v, "tensor", pairs)

    def in_order(mine, other, axis=0):
        low = jnp.where(me_t == 0, mine, other)
        high = jnp.where(me_t == 0, other, mine)
        return jnp.concatenate([low, high], axis=axis)

    def sum_dp(v):
        step = 1
        while step < n_dp:
            v = v + lax.ppermute(v, "dp", [(i, i ^ step) for i in range(n_dp)])
            step *= 2
        return v

    def after(value, *others):
        return lax.optimization_barrier((value, *others))[0]

    ring = 4
    plane = n_dp // (2 * ring)

    around = [(i, (i + 2 * plane) % n_dp) for i in range(n_dp)]
    across = [(i, i ^ 2) for i in range(n_dp)]
    beside = [(i, i ^ 1) for i in range(n_dp)]

    def send(v, way):
        return lax.ppermute(v, "dp", way)

    by_hand = plane == 2 and shard % 32 == 0

    def whole(v):
        return [lax.all_gather(v, "dp", axis=0, tiled=True)]

    def relative_order():
        level, side, core = me_dp // 4, (me_dp // 2) % 2, me_dp % 2
        order = []
        for dc in (1, 0):
            for dy in (1, 0):
                for dz in range(1, ring + 1):
                    order.append(((level - dz + ring) % ring) * 4 + (side ^ dy) * 2 + (core ^ dc))
        return order

    def fold_away(keep, got):
        half = keep.shape[0] // 2
        return (keep[:half].astype(F32) + got[:half].astype(F32)).astype(BF16), got

    def ring_part(keep, core, got, came, turn):
        low, high = (turn - 1) * shard, turn * shard
        half = keep.shape[0] // 2
        part = keep[half + low : half + high].astype(F32) + core[half + low : half + high].astype(F32)
        part = part + got[low:high].astype(F32)
        if came is not None:
            part = part + came.astype(F32)
        return part if turn == ring else part.astype(BF16)

    ends = jnp.cumsum(lengths[0]).astype(jnp.int32)
    live = (lax.iota(jnp.int32, group) < ends[-1]).astype(F32)
    live_own = lax.dynamic_slice_in_dim(live, me_t * own_rows, own_rows, 0)
    me = me_t.astype(jnp.int32).reshape(1)

    span_p = conv_x_bias.shape[1]
    span_n = conv_bc_bias.shape[1]
    half_bc = w_bc.shape[1]
    bits = jnp.concatenate([norm_gain, conv_bc.reshape(-1), conv_bc_bias.reshape(-1)])
    bits = jnp.pad(bits, (0, LANES - bits.shape[0]))
    tiny = jnp.concatenate([w_bc.reshape(2 * half_bc, STATE), bits[None]], axis=0)
    other_tiny = swap(tiny)
    other_bc = other_tiny[: 2 * half_bc].reshape(w_bc.shape)
    both_bits = [bits, other_tiny[2 * half_bc]]
    at = norm_gain.shape[0]
    gain_pair = in_order(*[v[:at] for v in both_bits])[:, None]
    taps_bc = in_order(*[v[at : at + conv_bc.size].reshape(2, span_n, K) for v in both_bits], axis=1)
    at += conv_bc.size
    bias_bc = in_order(*[v[at : at + 2 * span_n].reshape(2, span_n, 1) for v in both_bits], axis=1)
    spare_bc = jnp.concatenate([taps_bc, bias_bc], axis=2).reshape(4 * span_n, K + 1)
    spare_x = [conv_x.reshape(shard, K), conv_x_bias.reshape(shard, 1), gate_gain.reshape(shard, 1), gain_pair]
    bc_pair = in_order(w_bc, other_bc, axis=1)
    w_x = w_zx[1]
    w_small = jnp.concatenate(
        [bc_pair[0], bc_pair[1], w_dt, *spare_x, jnp.zeros((shard, 8 - K - 3), BF16)]
        + [jnp.pad(spare_bc, ((0, shard - 4 * span_n), (0, LANES - heads - 8 - K - 1)))],
        axis=1,
    )
    gain_pair = gain_pair.astype(F32)
    where = after(lax.iota(jnp.int32, depth), w_small)
    home, inside = where // shard, where % shard
    place_x = (inside // span_p) * WIDTH + home * span_p + inside % span_p
    half_n = 2 * span_n
    place_bc = (inside // half_n) * STATE + home * half_n + inside % half_n
    place = jnp.concatenate([jnp.broadcast_to(v[:, None], (depth, LANES)) for v in (place_x, place_bc)], axis=1)
    par = jnp.concatenate([dt_bias[None], a_log[None], jnp.zeros((6, heads), F32)], axis=0)
    par = jnp.concatenate([par, jnp.zeros((8, LANES - heads), F32)], axis=1)
    skip = jnp.repeat(d_skip, WIDTH)[None]
    members = lax.iota(jnp.int32, inner)[:, None] // WIDTH
    sel = (members == lax.iota(jnp.int32, LANES)[None, :]).astype(BF16)
    smem = pl.BlockSpec(memory_space=pltpu.SMEM)
    vmem = pl.BlockSpec(memory_space=pltpu.VMEM)
    hbm = pl.BlockSpec(memory_space=pl.ANY)
    n_small = 2 * STATE + LANES
    n_conv = inner + 2 * STATE
    w_rest = jnp.concatenate([w_zx[0], w_out.T], axis=1)

    def turn(rows):
        return pl.pallas_call(
            turn_rows,
            in_specs=[smem, vmem],
            out_specs=vmem,
            out_shape=jax.ShapeDtypeStruct((depth, own_rows), BF16),
            scratch_shapes=[pltpu.VMEM((depth, own_rows), BF16)],
            compiler_params=pltpu.CompilerParams(vmem_limit_bytes=VMEM_LIMIT),
            cost_estimate=SMALL_COST,
            name="turn_rows",
        )((jnp.stack(relative_order()) * shard).astype(jnp.int32), rows)

    def place_of(turn, side, core):
        level = (me_dp // (2 * plane) - turn + ring) % ring
        return (level * (2 * plane) + ((me_dp % (2 * plane)) ^ (2 * side + core))) * shard

    together = lambda *values: list(lax.optimization_barrier(tuple(values)))
    joined = lambda *values: jnp.concatenate(values, axis=0)
    if by_hand:
        shift = lambda k: [(i, (i + 2 * plane * k) % n_dp) for i in range(n_dp)]
        l1, o0, c0 = together(send(w_x, around), send(w_x, across), send(w_x, beside))
        late, w_small = together(tokens, w_small, l1, o0, c0)[:2]
        l2, o1, s1, s2, s3, turned_own = together(
            send(l1, around), send(l1, across), send(w_small, shift(1)), send(w_small, shift(2)), send(w_small, shift(3)),
            turn(late),
        )
        w_rest = after(jnp.concatenate([w_zx[0], w_out.T], axis=1), l2)
        zo_all = lax.all_gather(w_rest, "dp", axis=0, tiled=True)
        small_line = joined(w_small, s1, s2, s3)
        split = own_rows // 2
        l3, o2, c1, small_across, t0 = together(
            send(l2, around), send(l2, across), send(joined(l1, o0), beside), send(small_line, across), swap(late[:split])
        )
        o3, c2, small_beside, t1, place, par, skip, sel = together(
            send(l3, across), send(joined(l2, o1), beside), send(joined(small_line, small_across), beside),
            swap(after(late[split:], t0)), place, par, skip, sel,
        )
        other_tokens = joined(t0, t1)
        c3, turned_other, other_tokens = together(send(joined(l3, o2, o3), beside), turn(other_tokens), other_tokens)
        other_cot = swap(after(cotangent, other_tokens))
        wx_parts = [w_x, l1, l2, l3, o0, o1, o2, o3, c0, c1, c2, c3]
        order = [(t, 0, 0) for t in range(4)] + [(t, 1, 0) for t in range(4)]
        order += [(0, 0, 1), (1, 0, 1), (0, 1, 1), (2, 0, 1), (1, 1, 1), (3, 0, 1), (2, 1, 1), (3, 1, 1)]
        small_parts = [small_line, small_across, small_beside]
        order += [(t, side, core) for core in range(2) for side in range(2) for t in range(4)]
        offsets = jnp.stack([place_of(*key) for key in order]).astype(jnp.int32)
    else:
        wx_parts, small_parts = whole(w_x), whole(w_small)
        zo_all = whole(jnp.concatenate([w_zx[0], w_out.T], axis=1))[0]
        other_tokens, other_cot = swap(tokens), swap(cotangent)
        offsets = jnp.zeros((2,), jnp.int32)
    counts = (len(wx_parts), len(small_parts))
    sems = pltpu.SemaphoreType.DMA((offsets.shape[0],))
    tok_own = tokens.astype(F32)
    inv_tok = lax.rsqrt(jnp.mean(tok_own * tok_own, axis=1, keepdims=True) + EPSILON)

    block = own_rows
    steps = group // block
    x_raw, small, normed, taps, gain_in, wx_all = pl.pallas_call(
        partial(project, counts, heads, shard if by_hand else depth),
        grid=(steps,),
        in_specs=[
            smem,
            smem,
            whole_spec((block, depth)),
            whole_spec((block, depth)),
            whole_spec((depth, 2 * LANES)),
        ]
        + [hbm] * sum(counts),
        out_specs=[
            rows_spec(block, inner),
            rows_spec(block, n_small),
            rows_spec(block, depth),
            whole_spec((8, n_conv)),
            whole_spec((8, depth)),
            hbm,
        ],
        out_shape=[
            jax.ShapeDtypeStruct((group, inner), BF16),
            jax.ShapeDtypeStruct((group, n_small), F32),
            jax.ShapeDtypeStruct((group, depth), BF16),
            jax.ShapeDtypeStruct((8, n_conv), F32),
            jax.ShapeDtypeStruct((8, depth), F32),
            jax.ShapeDtypeStruct((depth, inner + n_small), BF16),
        ],
        scratch_shapes=[pltpu.VMEM((depth, inner + n_small), BF16), sems, pltpu.SemaphoreType.DMA],
        compiler_params=params(),
        cost_estimate=SMALL_COST,
        name="project",
    )(offsets, me, tokens, other_tokens, place, *wx_parts, *small_parts)
    xc, pre, bc, y_all, states = pl.pallas_call(
        partial(scan_forward, heads),
        grid=(chunks,),
        in_specs=[
            smem,
            rows_spec(Q, inner),
            rows_spec(Q, n_small),
            whole_spec((8, n_conv)),
            whole_spec((8, LANES)),
            whole_spec((1, inner)),
        ],
        out_specs=[
            rows_spec(Q, inner),
            rows_spec(Q, n_conv),
            rows_spec(Q, 2 * STATE),
            rows_spec(Q, inner),
            pl.BlockSpec((1, STATE, inner), lambda i: (i, 0, 0)),
        ],
        out_shape=[
            jax.ShapeDtypeStruct((group, inner), BF16),
            jax.ShapeDtypeStruct((group, n_conv), BF16),
            jax.ShapeDtypeStruct((group, 2 * STATE), BF16),
            jax.ShapeDtypeStruct((group, inner), BF16),
            jax.ShapeDtypeStruct((chunks, STATE, inner), BF16),
        ],
        scratch_shapes=[pltpu.VMEM((n_conv // LANES, Q + 8, LANES), F32), pltpu.VMEM((STATE, inner), F32)],
        compiler_params=params(),
        cost_estimate=SMALL_COST,
        name="scan_forward",
    )(ends, x_raw, small, taps, par, skip)

    cot_all = in_order(cotangent, other_cot)
    if by_hand:
        normed, cot_all = lax.optimization_barrier((normed, after(cot_all, y_all)))
    tile = 512
    columns = lambda rows, shift=0: pl.BlockSpec((rows, tile), lambda j: (0, j + shift))
    fixed = lambda shape: pl.BlockSpec(shape, lambda j: (0, 0))
    tiles = inner // tile
    z_all, gg, sq = pl.pallas_call(
        gate_forward,
        grid=(tiles,),
        in_specs=[fixed((group, depth)), columns(depth), columns(group), columns(8)],
        out_specs=[columns(group), columns(group), fixed((8, group))],
        out_shape=[
            jax.ShapeDtypeStruct((group, inner), BF16),
            jax.ShapeDtypeStruct((group, inner), BF16),
            jax.ShapeDtypeStruct((8, group), F32),
        ],
        scratch_shapes=[pltpu.VMEM((group, LANES), F32)],
        compiler_params=params(),
        cost_estimate=SMALL_COST,
        name="gate_forward",
    )(normed, zo_all, y_all, taps)
    sq_got = swap(sq)

    sq_all = sq + sq_got
    inv_gate8 = lax.rsqrt(sq_all / inner_total + EPSILON)
    inv_gate = inv_gate8[0]
    d_branch = (cot_all.astype(F32) * (live * inv_gate)[:, None]).astype(BF16)
    g_out = lax.dot_general(d_branch, gg, TN, preferred_element_type=F32).astype(BF16)
    grad_out = lax.psum_scatter(g_out, "dp", scatter_dimension=0, tiled=True)
    gg = after(gg, g_out)
    u_own, u_send, prod = pl.pallas_call(
        branch,
        grid=(depth // tile,),
        in_specs=[
            smem,
            smem,
            fixed((group, inner)),
            columns(own_rows),
            columns(own_rows),
            pl.BlockSpec((tile, inner), lambda j: (j, 1)),
        ],
        out_specs=[columns(own_rows), columns(own_rows), fixed((8, group))],
        out_shape=[
            jax.ShapeDtypeStruct((own_rows, depth), BF16),
            jax.ShapeDtypeStruct((own_rows, depth), BF16),
            jax.ShapeDtypeStruct((8, group), F32),
        ],
        scratch_shapes=[pltpu.VMEM((group, LANES), F32)],
        compiler_params=params(),
        cost_estimate=SMALL_COST,
        name="branch",
    )(me, ends, gg, cotangent, other_cot, zo_all)
    prod_got = swap(prod)
    u_recv = swap(u_send)
    inv_own = lax.dynamic_slice_in_dim(inv_gate, me_t * own_rows, own_rows, 0)
    out_branch = (u_own.astype(F32) + u_recv.astype(F32)) * (inv_own * live_own)[:, None]
    layer_out = (tokens.astype(F32) + out_branch).astype(BF16)

    prod_all = prod + prod_got
    coef8 = inv_gate8 * inv_gate8 * inv_gate8 * (prod_all / inner_total)
    dy, dz, gain_acc = pl.pallas_call(
        gate_backward,
        grid=(tiles,),
        in_specs=[
            smem,
            smem,
            fixed((own_rows, depth)),
            fixed((own_rows, depth)),
            columns(depth, tiles),
            columns(group),
            columns(group),
            fixed((8, group)),
            fixed((8, group)),
            columns(8),
        ],
        out_specs=[columns(group), columns(group), columns(8)],
        out_shape=[
            jax.ShapeDtypeStruct((group, inner), BF16),
            jax.ShapeDtypeStruct((group, inner), BF16),
            jax.ShapeDtypeStruct((8, inner), F32),
        ],
        scratch_shapes=[pltpu.VMEM((group, LANES), F32), pltpu.VMEM((group, LANES), F32)],
        compiler_params=params(),
        cost_estimate=SMALL_COST,
        name="gate_backward",
    )(me, ends, cotangent, other_cot, zo_all, y_all, z_all, inv_gate8, coef8, taps)
    dot = partial(lax.dot_general, preferred_element_type=F32)
    front = depth // 2

    def gradient(d, width):
        outs = pl.BlockSpec((front, width), lambda j: (0, j))
        return pl.pallas_call(
            weight_grad,
            grid=(d.shape[1] // width,),
            in_specs=[smem, fixed((depth, own_rows)), fixed((depth, own_rows)), pl.BlockSpec((group, width), lambda j: (0, j))],
            out_specs=[outs, outs],
            out_shape=[jax.ShapeDtypeStruct((front, d.shape[1]), BF16)] * 2,
            compiler_params=params(),
            cost_estimate=SMALL_COST,
            name="weight_grad",
        )(me, turned_own, turned_other, d)

    if by_hand:
        g_send, z_keep = gradient(dz, tile)
        z_got = send(g_send, beside)
        dy = after(dy, z_keep, g_send)
    else:
        grad_z = lax.psum_scatter(dot(normed, dz, TN).astype(BF16), "dp", scatter_dimension=0, tiled=True)

    n_a = inner * 2 // 3
    n_b = inner + n_small - n_a

    def backward(base, width, carry):
        at = base // width
        back = lambda size, column: pl.BlockSpec((Q, size), lambda i: (chunks - 1 - i, column))
        operands = [ends, dy, xc, pre, x_raw, small, bc, states, taps, par, skip, sel]
        in_specs = [
            smem,
            back(width, at),
            back(width, at),
            back(width, at),
            back(width, at),
            back(n_small, 0),
            back(2 * STATE, 0),
            pl.BlockSpec((1, STATE, width), lambda i: (chunks - 1 - i, 0, at)),
            whole_spec((8, width), at),
            whole_spec((8, LANES)),
            whole_spec((1, width), at),
            pl.BlockSpec((width, LANES), lambda i: (at, 0)),
        ]
        tiles_held = width + (2 * STATE if carry else 0)
        acc_shape, hacc_shape = (8 * (K + 2), tiles_held), (16, LANES)
        if carry:
            last = inner // (2 * STATE)
            operands += [pre, taps, *carry]
            in_specs += [back(2 * STATE, last), whole_spec((8, 2 * STATE), last), back(n_small, 0)]
            in_specs += [whole_spec((8 * (K + 2), base)), whole_spec(hacc_shape), whole_spec((8, inner))]
            out_specs = [back(n_b, 0), whole_spec((8, n_conv))]
            out_shape = [jax.ShapeDtypeStruct((group, n_b), BF16), jax.ShapeDtypeStruct((8, n_conv), F32)]
        else:
            out_specs = [back(width, 0), back(n_small, 0)]
            out_shape = [jax.ShapeDtypeStruct((group, width), BF16), jax.ShapeDtypeStruct((group, n_small), F32)]
        return pl.pallas_call(
            partial(scan_backward, base, bool(carry), chunks),
            grid=(chunks,),
            in_specs=in_specs,
            out_specs=out_specs + [whole_spec(acc_shape), whole_spec(hacc_shape)],
            out_shape=out_shape + [jax.ShapeDtypeStruct(acc_shape, F32), jax.ShapeDtypeStruct(hacc_shape, F32)],
            scratch_shapes=[
                pltpu.VMEM((STATE, width), F32),
                pltpu.VMEM((tiles_held // LANES, Q + 8, LANES), F32),
                *[pltpu.VMEM((Q, width), BF16)] * 6,
                pltpu.VMEM((STATE, width), BF16),
                pltpu.VMEM((8, width), F32),
            ],
            compiler_params=params(),
            cost_estimate=SMALL_COST,
            name="scan_backward",
        )(*operands)

    dxa, part, acc, hacc = backward(0, n_a, ())
    if by_hand:
        z_got, dxa = lax.optimization_barrier((z_got, dxa))
        z_away, z_core = fold_away(z_keep, z_got)
        z_got = send(z_away, across)
        dxa, part = lax.optimization_barrier((dxa, part, z_away))[:2]
        g_x, grad_out = lax.optimization_barrier((dot(normed, after(dxa, u_recv), TN).astype(BF16), grad_out))
        grad_a = lax.psum_scatter(g_x, "dp", scatter_dimension=0, tiled=True)
        part = after(part, g_x)
    dxb, vector = backward(n_a, inner - n_a, (part, acc, hacc, gain_acc))[:2]
    lanes_shared = lax.iota(jnp.int32, n_conv)[None, :] >= inner
    bits_of = lambda turn: [(i, i ^ (1 << turn)) for i in range(n_dp)]
    if by_hand:
        z_got, dxb, vector = lax.optimization_barrier((z_got, dxb, vector))
        z_out = ring_part(z_keep, z_core, z_got, None, 1)
        z_came = send(z_out, around)
        shared_got = swap(vector)
        b_send, b_keep = gradient(after(dxb, z_out), n_b)
        b_got = send(b_send, beside)
        shared_got, z_came, b_keep = lax.optimization_barrier((shared_got, z_came, b_keep))
        vector = vector + jnp.where(lanes_shared, shared_got, 0.0)
        z_out = ring_part(z_keep, z_core, z_got, z_came, 2)
        z_came, vector_got = send(z_out, around), send(vector, bits_of(0))
        dz = after(dz, b_send, b_keep, z_out, vector)
    else:
        dx = jnp.concatenate([dxa, dxb], axis=1)
        grad_x = lax.psum_scatter(dot(normed, dx, TN).astype(BF16), "dp", scatter_dimension=0, tiled=True)

    def back_rows(which, dz):
        pick = lambda width: pl.BlockSpec((own_rows, width), lambda j, rows: (rows[0], 0))
        return pl.pallas_call(
            normed_back,
            grid_spec=pltpu.PrefetchScalarGridSpec(
                num_scalar_prefetch=1,
                grid=(depth // tile,),
                in_specs=[
                    pick(inner),
                    pick(n_a),
                    pick(n_b),
                    pl.BlockSpec((tile, inner), lambda j, rows: (j, 0)),
                    pl.BlockSpec((tile, inner + n_small), lambda j, rows: (j, 0)),
                ],
                out_specs=pl.BlockSpec((own_rows, tile), lambda j, rows: (0, j)),
            ),
            out_shape=jax.ShapeDtypeStruct((own_rows, depth), BF16),
            compiler_params=params(),
            cost_estimate=SMALL_COST,
            name="normed_back",
        )(which, dz, dxa, dxb, zo_all, wx_all)

    dn_send = back_rows(n_t - 1 - me, dz)
    if by_hand:
        w_sum = lambda w, g: jnp.sum(w.astype(F32) * g, axis=1)
        b_got, vector_got, dn_send, z_came = lax.optimization_barrier((b_got, vector_got, dn_send, z_came))
        b_away, b_core = fold_away(b_keep, b_got)
        b_got = send(b_away, across)
        dn_got = swap(after(dn_send, b_away))
        vector = vector + after(vector_got, b_away)
        vector_got = send(vector, bits_of(1))
        dn_own = back_rows(me, after(dz, vector, b_away))
        vector_got, dn_own, b_got, z_came, grad_a = lax.optimization_barrier((vector_got, dn_own, b_got, z_came, grad_a))
        vector = vector + vector_got
        b_out = ring_part(b_keep, b_core, b_got, None, 1)
        b_came = send(b_out, around)
        z_out = ring_part(z_keep, z_core, z_got, z_came, 3)
        z_came, vector_got = send(z_out, around), send(vector, bits_of(2))
        grad_a = grad_a.astype(F32)
        in_part = w_sum(w_x[:, :n_a], grad_a)
        vector_got, z_came, in_part, b_came = lax.optimization_barrier((vector_got, z_came, in_part, b_came))
        vector = vector + vector_got
        b_out = ring_part(b_keep, b_core, b_got, b_came, 2)
        b_came, vector_got = send(b_out, around), send(vector, bits_of(3))
        grad_z = ring_part(z_keep, z_core, z_got, z_came, ring) * gain_pair
        in_part = in_part + w_sum(w_zx[0], grad_z)
        grad_out = grad_out.astype(F32).T
        vector_got, grad_out, layer_out, b_came, grad_z, in_part = lax.optimization_barrier(
            (vector_got, grad_out, layer_out, b_came, grad_z, in_part)
        )
        vector = vector + vector_got
        b_came = send(ring_part(b_keep, b_core, b_got, b_came, 3), around)
    else:
        vector = sum_dp(vector + jnp.where(lanes_shared, swap(vector), 0.0))
        dn_own = back_rows(me, dz)
        dn_got = swap(dn_send)
        grad_out = grad_out.astype(F32).T
        grad_z, grad_x = grad_z.astype(F32), grad_x.astype(F32)
        in_part = jnp.sum(w_zx[0].astype(F32) * grad_z, axis=1) + jnp.sum(jnp.concatenate([w_x, w_small], axis=1).astype(F32) * grad_x, axis=1)

    me_all = me_dp * n_t + me_t
    bc_sum = vector[: K + 1, inner:].reshape(K + 1, 2, STATE)
    bc_sum = lax.dynamic_slice_in_dim(bc_sum, me_all * span_n, span_n, 2)
    grad_bc_taps = bc_sum[:K].transpose(1, 2, 0).reshape(conv_bc.shape)
    grad_bc_bias = bc_sum[K]
    x_sum = vector[: K + 3, :inner].reshape(K + 3, heads, WIDTH)
    grad_skip = x_sum[K + 1].sum(axis=1)
    x_sum = lax.dynamic_slice_in_dim(x_sum, me_dp * span_p, span_p, 2)
    grad_x_taps = x_sum[:K].transpose(1, 2, 0).reshape(conv_x.shape)
    grad_x_bias = x_sum[K]
    grad_gate = x_sum[K + 2]
    grad_dt_bias = vector[K + 3, :heads]
    grad_a_log = vector[K + 3, LANES : LANES + heads]
    dn = (dn_own.astype(F32) + dn_got.astype(F32)) * gain_in[0:1, :]
    grad_tokens = (
        cotangent.astype(F32)
        + inv_tok * dn
        - tok_own * inv_tok * inv_tok * inv_tok * jnp.mean(dn * tok_own, axis=1, keepdims=True)
    )

    if by_hand:
        outs = (grad_bc_taps, grad_bc_bias, grad_skip, grad_x_taps, grad_x_bias, grad_gate, grad_dt_bias, grad_a_log)
        outs = lax.optimization_barrier((*outs, grad_tokens, b_came))
        grad_bc_taps, grad_bc_bias, grad_skip, grad_x_taps, grad_x_bias, grad_gate, grad_dt_bias, grad_a_log = outs[:8]
        grad_tokens, b_came = outs[8:]
        grad_b = ring_part(b_keep, b_core, b_got, b_came, ring) * gain_pair
        in_part = in_part + w_sum(w_x[:, n_a:], grad_b[:, : inner - n_a]) + w_sum(w_small, grad_b[:, inner - n_a :])
    else:
        grad_a, grad_b = grad_x[:, :n_a], grad_x[:, n_a:]
    at = inner - n_a
    bc_part = jnp.concatenate([grad_b[:, at : at + 2 * STATE], jnp.broadcast_to(in_part[:, None], (shard, LANES))], axis=1)
    grad_zx = jnp.stack([grad_z, jnp.concatenate([grad_a, grad_b[:, :at]], axis=1)])
    grad_dt = grad_b[:, at + 2 * STATE : at + 2 * STATE + heads]
    half = half_bc
    bc_own = lax.dynamic_slice_in_dim(bc_part, me_t * half, half, 0)
    bc_send = lax.dynamic_slice_in_dim(bc_part, (n_t - 1 - me_t) * half, half, 0)
    bc_total = bc_own + swap(bc_send)
    own_gain = norm_gain.astype(F32)
    grad_bc = bc_total[:, : 2 * STATE].reshape(half, 2, STATE).transpose(1, 0, 2)
    grad_in = bc_total[:, 2 * STATE] / own_gain
    return (
        layer_out,
        grad_tokens,
        grad_in,
        grad_zx,
        grad_bc,
        grad_dt,
        grad_x_taps,
        grad_x_bias,
        grad_bc_taps,
        grad_bc_bias,
        grad_dt_bias,
        grad_a_log,
        grad_skip,
        grad_gate,
        grad_out,
    )


def solution(mesh):
    both = ("dp", "tensor")
    in_specs = (
        P(both, None),
        P(both, None),
        P("dp", None),
        P(both),
        P(None, "dp", "tensor"),
        P(None, both, None),
        P("dp", "tensor"),
        P("tensor", "dp"),
        P("tensor", "dp"),
        P(None, both),
        P(None, both),
        P("tensor"),
        P("tensor"),
        P("tensor"),
        P("tensor", "dp"),
        P("tensor", "dp"),
    )
    out_specs = (
        P(both, None),
        P(both, None),
        P(both),
        P(None, "dp", "tensor"),
        P(None, both, None),
        P("dp", "tensor"),
        P("tensor", "dp"),
        P("tensor", "dp"),
        P(None, both),
        P(None, both),
        P("tensor"),
        P("tensor"),
        P("tensor"),
        P("tensor", "dp"),
        P("tensor", "dp"),
    )
    return jax.shard_map(local, mesh=mesh, in_specs=in_specs, out_specs=out_specs, check_vma=False)
```

```python
from functools import partial

import jax
import jax.numpy as jnp
from jax import lax
from jax.experimental import pallas as pl
from jax.experimental.pallas import tpu as pltpu
from jax.sharding import PartitionSpec as P

EPSILON = 1e-05
HIGHEST = lax.Precision.HIGHEST
K = 4
WIDTH = 64
STATE = 128
Q = 128
LANES = 128
LOG2E = 1.4426950408889634
VMEM_LIMIT = 60 * 1024 * 1024
F32 = jnp.float32
BF16 = jnp.bfloat16

NN = (((1,), (0,)), ((), ()))
NT = (((1,), (1,)), ((), ()))
TN = (((0,), (0,)), ((), ()))


def mm(a, b, dims=NN):
    return lax.dot_general(a, b, dims, preferred_element_type=F32)


def mm_exact(a, b, dims=NN):
    return lax.dot_general(a, b, dims, preferred_element_type=F32, precision=HIGHEST)


def iota(shape, dim):
    return lax.broadcasted_iota(jnp.int32, shape, dim)


def segment_of(rows, ends_ref, count):
    total = (rows >= ends_ref[0]).astype(jnp.int32)
    for j in range(1, count):
        total = total + (rows >= ends_ref[j]).astype(jnp.int32)
    return total


def scalar_segment(row, ends_ref, count):
    total = jnp.where(row >= ends_ref[0], 1, 0)
    for j in range(1, count):
        total = total + jnp.where(row >= ends_ref[j], 1, 0)
    return total


def sigmoid(v):
    return 0.5 * jnp.tanh(0.5 * v) + 0.5


def softplus(v):
    return jnp.maximum(v, 0.0) + jnp.log1p(jnp.exp(-jnp.abs(v)))


def chunk_masks(chunk, ends_ref, count):
    base = chunk * Q
    rows = iota((Q, Q), 0) + base
    cols = iota((Q, Q), 1) + base
    row_ids = segment_of(rows, ends_ref, count)
    col_ids = segment_of(cols, ends_ref, count)
    same = row_ids == col_ids
    before_id = jnp.where(chunk == 0, -1, scalar_segment(base - 1, ends_ref, count))
    final_id = scalar_segment(base + Q - 1, ends_ref, count)
    carry = (row_ids == before_id).astype(F32)
    last = (row_ids == final_id).astype(F32)
    passing = jnp.where(before_id == final_id, 1.0, 0.0).astype(F32)
    return rows, cols, row_ids, same, carry, last, passing


def decays(dt_raw, par_ref):
    shifted = dt_raw + par_ref[0:1, :]
    step = softplus(shifted)
    decay_rate = jnp.exp(par_ref[1:2, :])
    return shifted, step, decay_rate


def pair_columns(values, pair, first):
    left = jnp.broadcast_to(values[:, 2 * pair : 2 * pair + 1], (Q, LANES))
    right = jnp.broadcast_to(values[:, 2 * pair + 1 : 2 * pair + 2], (Q, LANES))
    return left, right, jnp.where(first, left, right)


def scan_forward(
    heads, ends_ref, xr_ref, small_ref, taps_ref, par_ref, skip_ref,
    xc_ref, pre_ref, bc_ref, y_ref, st_ref, buf, state,
):
    count = ends_ref.shape[0]
    inner = heads * WIDTH
    chunk = pl.program_id(0)

    @pl.when(chunk == 0)
    def _():
        buf[:, 0:8, :] = jnp.zeros((buf.shape[0], 8, LANES), F32)
        state[...] = jnp.zeros(state.shape, F32)

    rows, cols, row_ids, same, carry, last, passing = chunk_masks(chunk, ends_ref, count)
    causal = rows >= cols
    visible = same & causal
    lag_mask = [None]
    for lag in range(1, K):
        earlier = rows - lag
        keep = (segment_of(earlier, ends_ref, count) == row_ids) & (earlier >= 0)
        lag_mask.append(keep.astype(F32))

    small = small_ref[...]

    def convolve(lo, raw):
        span = slice(lo, lo + LANES)
        place = lo // LANES
        buf[place, 8 : 8 + Q, :] = raw
        pre = taps_ref[K : K + 1, span] + taps_ref[K - 1 : K, span] * raw
        for lag in range(1, K):
            pre = pre + taps_ref[K - 1 - lag : K - lag, span] * (
                buf[place, 8 - lag : 8 - lag + Q, :] * lag_mask[lag]
            )
        buf[place, 0:8, :] = raw[Q - 8 : Q, :]
        pre_ref[:, span] = pre.astype(BF16)
        return pre * sigmoid(pre)

    b_f = convolve(inner, small[:, :STATE]).astype(BF16).astype(F32)
    c_b = convolve(inner + STATE, small[:, STATE : 2 * STATE]).astype(BF16)
    b_b = b_f.astype(BF16)
    bc_ref[:, :STATE] = b_b
    bc_ref[:, STATE:] = c_b
    b_t = b_f.T.astype(BF16)

    _, step, decay_rate = decays(small[:, 2 * STATE :], par_ref)
    csum = mm_exact(causal.astype(F32), step * (-LOG2E * decay_rate))
    csum_t = csum.T
    scores = jnp.where(visible, mm(c_b, b_b, NT), 0.0)
    first = iota((Q, LANES), 1) < WIDTH
    first_row = iota((1, LANES), 1) < WIDTH

    wide = 2 * LANES
    for quad in range(0, inner, wide):
        block = slice(quad, quad + wide)
        held = state[:, block]
        held_b = held.astype(BF16)
        st_ref[0, :, block] = held_b
        carried = mm(c_b, held_b)
        weighted, kept = [], []
        for part in range(0, wide, LANES):
            lo = quad + part
            pair = lo // LANES
            span = slice(lo, lo + LANES)
            xc = convolve(lo, xr_ref[:, span].astype(F32)).astype(BF16)
            xc_ref[:, span] = xc
            xc = xc.astype(F32)
            left, right, both = pair_columns(csum, pair, first)
            _, _, step_pair = pair_columns(step, pair, first)
            mix = jnp.concatenate(
                [
                    (scores * jnp.exp2(jnp.minimum(left - csum_t[2 * pair : 2 * pair + 1, :], 0.0))).astype(BF16),
                    (scores * jnp.exp2(jnp.minimum(right - csum_t[2 * pair + 1 : 2 * pair + 2, :], 0.0))).astype(BF16),
                ],
                axis=1,
            )
            fed_b = (xc * step_pair).astype(BF16)
            zero = jnp.zeros((Q, LANES), BF16)
            stacked = jnp.concatenate([jnp.where(first, fed_b, zero), jnp.where(first, zero, fed_b)], axis=0)
            y = mm(mix, stacked) + carried[:, part : part + LANES] * (jnp.exp2(both) * carry)
            y_ref[:, span] = (y + skip_ref[:, span] * xc).astype(BF16)
            closing = both[Q - 1 : Q, :]
            weighted.append((fed_b.astype(F32) * (jnp.exp2(closing - both) * last)).astype(BF16))
            kept.append(jnp.exp2(closing) * passing)
        fresh = mm(b_t, jnp.concatenate(weighted, axis=1))
        state[:, block] = held * jnp.concatenate(kept, axis=1) + fresh


def scan_backward(
    heads, chunks, top, ends_ref, dy_ref, xc_ref, pre_ref, xr_ref, small_ref, bc_ref, st_ref, taps_ref, par_ref,
    skip_ref, sel_ref, *refs,
):
    later_call = top + 1 < chunks
    if later_call:
        state_in, halo_in, acc_in, hacc_in, gain_acc_ref = refs[:5]
        dxa_ref, dxb_ref, rows_ref, acc_ref, hacc_ref = refs[7:12]
        refs = refs[12:]
    else:
        dxa_ref, dxb_ref, acc_ref, hacc_ref, state_out, halo_out = refs[:6]
        refs = refs[6:]
    dstate, dpre, ab_hi, ab_lo, v_b, u_b, dyd, fedw, dst_b, through = refs
    count = ends_ref.shape[0]
    inner = heads * WIDTH
    total_rows = chunks * Q
    chunk = top - pl.program_id(0)

    @pl.when(pl.program_id(0) == 0)
    def _():
        if top + 1 < chunks:
            dpre[:, Q : Q + 8, :] = halo_in[...]
            dstate[...] = state_in[...]
            acc_ref[...] = acc_in[...]
            hacc_ref[...] = hacc_in[...]
        else:
            dpre[:, Q : Q + 8, :] = jnp.zeros((dpre.shape[0], 8, LANES), F32)
            dstate[...] = jnp.zeros(dstate.shape, F32)
            acc_ref[...] = jnp.zeros(acc_ref.shape, F32)
            hacc_ref[...] = jnp.zeros(hacc_ref.shape, F32)

    rows, cols, row_ids, same, carry, last, passing = chunk_masks(chunk, ends_ref, count)
    causal = rows >= cols
    visible = same & causal
    lag_mask = [None]
    for lag in range(1, K):
        later = rows + lag
        keep = (segment_of(later, ends_ref, count) == row_ids) & (later < total_rows)
        lag_mask.append(keep.astype(F32))

    small = small_ref[...]
    shifted, step, decay_rate = decays(small[:, 2 * STATE :], par_ref)
    csum = mm_exact(causal.astype(F32), step * (-LOG2E * decay_rate))
    csum_t = csum.T
    b_b = bc_ref[:, :STATE]
    c_b = bc_ref[:, STATE:]
    c_t = c_b.astype(F32).T.astype(BF16)
    scores = jnp.where(visible, mm(c_b, b_b, NT), 0.0)
    first = iota((Q, LANES), 1) < WIDTH

    n_a = dxa_ref.shape[1]

    def put(lo, values):
        if lo < n_a:
            dxa_ref[:, lo : lo + LANES] = values.astype(BF16)
        else:
            dxb_ref[:, lo - n_a : lo - n_a + LANES] = values.astype(BF16)

    def fold(values):
        return values.reshape(Q // 8, 8, values.shape[1]).sum(axis=0)

    def conv_back(lo, d_conv, raw):
        span = slice(lo, lo + LANES)
        pre = pre_ref[:, span].astype(F32)
        gate = sigmoid(pre)
        d_pre = d_conv * (gate * (1.0 + pre * (1.0 - gate)))
        place = lo // LANES
        dpre[place, 0:Q, :] = d_pre
        d_raw = taps_ref[K - 1 : K, span] * d_pre
        acc_ref[8 * (K - 1) : 8 * K, span] += fold(d_pre * raw)
        acc_ref[8 * K : 8 * K + 8, span] += fold(d_pre)
        for lag in range(1, K):
            moved = dpre[place, lag : lag + Q, :] * lag_mask[lag]
            d_raw = d_raw + taps_ref[K - 1 - lag : K - lag, span] * moved
            acc_ref[8 * (K - 1 - lag) : 8 * (K - lag), span] += fold(moved * raw)
        dpre[place, Q : Q + 8, :] = d_pre[0:8, :]
        put(lo, d_raw)

    d_scores = jnp.zeros((Q, Q), F32)
    wide = 2 * LANES
    for quad in range(0, inner, wide):
        block = slice(quad, quad + wide)
        held_b = st_ref[0, :, block]
        d_held = dstate[:, block]
        d_held_b = d_held.astype(BF16)
        dst_b[:, block] = d_held_b
        carried = mm(c_b, held_b)
        returned = mm(b_b, d_held_b)
        crossing = (d_held * held_b.astype(F32)).reshape(STATE // 8, 8, wide).sum(axis=0)
        grown_parts, kept_parts = [], []
        for part in range(0, wide, LANES):
            lo = quad + part
            pair = lo // LANES
            span = slice(lo, lo + LANES)
            xc = xc_ref[:, span].astype(F32)
            dy_b = dy_ref[:, span]
            dy = dy_b.astype(F32)
            left, right, both = pair_columns(csum, pair, first)
            _, _, step_pair = pair_columns(step, pair, first)
            fall_left = jnp.exp2(jnp.minimum(left - csum_t[2 * pair : 2 * pair + 1, :], 0.0))
            fall_right = jnp.exp2(jnp.minimum(right - csum_t[2 * pair + 1 : 2 * pair + 2, :], 0.0))
            mix = jnp.concatenate([(scores * fall_left).astype(BF16), (scores * fall_right).astype(BF16)], axis=1)
            fed_b = (xc * step_pair).astype(BF16)
            fed = fed_b.astype(F32)
            zero = jnp.zeros((Q, LANES), BF16)
            stacked = jnp.concatenate([jnp.where(first, fed_b, zero), jnp.where(first, zero, fed_b)], axis=0)
            grown = jnp.exp2(both) * carry
            y = mm(mix, stacked) + carried[:, part : part + LANES] * grown
            d_mix = mm(dy_b, stacked, NT)
            d_scores = d_scores + d_mix[:, :Q] * fall_left + d_mix[:, Q:] * fall_right
            d_fed2 = mm(mix, dy_b, TN)
            d_fed_in = jnp.where(first, d_fed2[:Q], d_fed2[Q:])
            closing = both[Q - 1 : Q, :]
            shrink = jnp.exp2(closing - both) * last
            d_fed_out = returned[:, part : part + LANES] * shrink
            d_fed = d_fed_in + d_fed_out
            straddle = dy * y - fed * d_fed_in
            hi = straddle.astype(BF16)
            ab_hi[:, span] = hi
            ab_lo[:, span] = (straddle - hi.astype(F32)).astype(BF16)
            v_b[:, span] = (fed * d_fed_out).astype(BF16)
            u_b[:, span] = (xc * d_fed).astype(BF16)
            fedw[:, span] = (fed * shrink).astype(BF16)
            grown_parts.append((dy * grown).astype(BF16))
            kept_parts.append(jnp.exp2(closing) * passing)
            acc_ref[8 * K + 8 : 8 * K + 16, span] += fold(dy * xc)
            d_conv = d_fed * step_pair + skip_ref[:, span] * dy
            conv_back(lo, d_conv, xr_ref[:, span].astype(F32))
        dy_grown = jnp.concatenate(grown_parts, axis=1)
        kept = jnp.concatenate(kept_parts, axis=1)
        dyd[:, block] = dy_grown
        through[:, block] = crossing * kept
        dstate[:, block] = d_held * kept + mm(c_t, dy_grown)

    d_scores_b = jnp.where(visible, d_scores, 0.0).astype(BF16)
    d_c = mm(dyd[...], st_ref[0], NT) + mm(d_scores_b, b_b)
    d_b = mm(fedw[...], dst_b[...], NT) + mm(d_scores_b, c_b, TN)
    conv_back(inner, d_b, small[:, :STATE])
    conv_back(inner + STATE, d_c, small[:, STATE : 2 * STATE])

    sel = sel_ref[...]
    red_ab = mm(ab_hi[...], sel) + mm(ab_lo[...], sel)
    red_v = mm(v_b[...], sel)
    red_u = mm(u_b[...], sel)
    thr = through[...]
    thr_hi = thr.astype(BF16)
    red_t = mm(thr_hi, sel) + mm((thr - thr_hi.astype(F32)).astype(BF16), sel)
    d_rate = (
        mm_exact((same & (cols >= rows)).astype(F32), red_ab)
        + mm_exact((same & (cols < rows)).astype(F32), red_v)
        + jnp.sum(red_t, axis=0, keepdims=True)
    )
    d_step = red_u - d_rate * decay_rate
    d_dt = d_step * sigmoid(shifted)
    put(inner + 2 * STATE, d_dt)
    hacc_ref[0:8, :] += fold(d_dt)
    hacc_ref[8:16, :] += fold(d_rate * (-decay_rate * step))
    if later_call:

        @pl.when(pl.program_id(0) == pl.num_programs(0) - 1)
        def _():
            rows_ref[...] = jnp.zeros(rows_ref.shape, F32)
            for k in range(K + 2):
                rows_ref[k : k + 1, :] = jnp.sum(acc_ref[8 * k : 8 * k + 8, :], axis=0, keepdims=True)
            rows_ref[K + 2 : K + 3, :inner] = jnp.sum(gain_acc_ref[...], axis=0, keepdims=True)
            for k in range(2):
                total = jnp.sum(hacc_ref[8 * k : 8 * k + 8, :], axis=0, keepdims=True)
                rows_ref[K + 3 : K + 4, k * LANES : (k + 1) * LANES] = total

    else:
        halo_out[...] = dpre[:, Q : Q + 8, :]
        state_out[...] = dstate[...]


def load_blocks(offsets_ref, parts, whole, sems, size, columns, first=0):
    @pl.when(pl.program_id(0) == 0)
    def _():
        copies = []
        for part in parts:
            for j in range(part.shape[0] // size):
                k = first + len(copies)
                start = 0 if size == whole.shape[0] else pl.multiple_of(offsets_ref[k], 32)
                source = part.at[pl.ds(j * size, size), :]
                copies.append(pltpu.make_async_copy(source, whole.at[pl.ds(start, size), slice(*columns)], sems.at[k]))
        for copy in copies:
            copy.start()
        for copy in copies:
            copy.wait()


def turn_rows(offsets_ref, source_ref, out_ref, turned):
    rows, depth = source_ref.shape
    for lo in range(0, rows, Q):
        tile = source_ref[lo : lo + Q, :].astype(F32)
        tile = tile * lax.rsqrt(jnp.mean(tile * tile, axis=1, keepdims=True) + EPSILON)
        for left in range(0, depth, LANES):
            turned[left : left + LANES, lo : lo + Q] = tile[:, left : left + LANES].T.astype(BF16)
    count = offsets_ref.shape[0]
    size = depth // count
    for k in range(count):
        start = pl.multiple_of(offsets_ref[k], 32)
        out_ref[k * size : (k + 1) * size, :] = turned[pl.ds(start, size), :]


def project(counts, heads, size, offsets_ref, me_ref, own_ref, other_ref, place_ref, *refs):
    count = sum(counts)
    blocks, (x_ref, small_ref, normed_ref, taps_ref, gain_ref, w_out_ref, w_ref, sems, out_sem) = refs[:count], refs[count:]
    split = x_ref.shape[1]
    shards = w_ref.shape[0] // size
    load_blocks(offsets_ref, blocks[: counts[0]], w_ref, sems, size, (0, split))
    load_blocks(offsets_ref, blocks[counts[0] :], w_ref, sems, size, (split, w_ref.shape[1]), shards)
    keep = pltpu.make_async_copy(w_ref, w_out_ref, out_sem)
    depth, inner = w_ref.shape[0], x_ref.shape[1]
    tile = 512

    @pl.when(pl.program_id(0) == 0)
    def _():
        keep.start()
        spare = w_ref[:, inner + 2 * STATE :]
        turned = spare.astype(F32).T
        gain_ref[...] = jnp.broadcast_to(turned[heads + K + 2 : heads + K + 3, :], gain_ref.shape)
        few = turned[heads : heads + 16, :].astype(BF16)
        lanes = iota((depth, LANES), 1)
        for lo in range(0, inner + 2 * STATE, LANES):
            if lo < inner:
                wanted, row = place_ref[:, :LANES] == lanes + lo, 0
            else:
                wanted, row = place_ref[:, LANES:] == lanes + (lo - inner), 8
            moved = mm(few, jnp.where(wanted, 1.0, 0.0).astype(BF16))
            taps_ref[:, lo : lo + LANES] = moved[row : row + 8, :]

    rows = jnp.where(pl.program_id(0) == me_ref[0], own_ref[...], other_ref[...]).astype(F32)
    scale = lax.rsqrt(jnp.mean(rows * rows, axis=1, keepdims=True) + EPSILON)
    rows = (rows * scale * gain_ref[0:1, :]).astype(BF16)
    normed_ref[...] = rows
    for lo in range(0, inner, tile):
        x_ref[:, lo : lo + tile] = mm(rows, w_ref[:, lo : lo + tile]).astype(BF16)
    small_ref[...] = mm(rows, w_ref[:, inner:])

    @pl.when(pl.program_id(0) == pl.num_programs(0) - 1)
    def _():
        keep.wait()


def row_sums(lanes):
    return mm_exact(jnp.ones((8, LANES), F32), lanes, NT)


def spread_rows(values):
    pick = jnp.where(iota((8, LANES), 0) == 0, 1.0, 0.0).astype(F32)
    return mm_exact(values, pick, TN)


def gate_forward(normed_ref, w_ref, y_ref, gain_ref, z_ref, gg_ref, sq_ref, square):
    rows, width = z_ref.shape
    size = 512

    @pl.when(pl.program_id(0) == 0)
    def _():
        square[...] = jnp.zeros(square.shape, F32)

    for lo in range(0, rows, size):
        at = slice(lo, lo + size)
        z = mm(normed_ref[at, :], w_ref[...]).astype(BF16)
        z_ref[at, :] = z
        z = z.astype(F32)
        gated = y_ref[at, :].astype(F32) * (z * sigmoid(z))
        gg_ref[at, :] = (gated * gain_ref[K + 1 : K + 2, :]).astype(BF16)
        twice = gated * gated
        for part in range(0, width, LANES):
            square[at, :] += twice[:, part : part + LANES]

    @pl.when(pl.program_id(0) == pl.num_programs(0) - 1)
    def _():
        sq_ref[...] = row_sums(square[...])


def branch(me_ref, ends_ref, gg_ref, own_ref, other_ref, w_ref, mine_ref, away_ref, prod_ref, product):
    rows, width = mine_ref.shape
    size = 512

    @pl.when(pl.program_id(0) == 0)
    def _():
        product[...] = jnp.zeros(product.shape, F32)

    for index, (out_ref, cot_ref) in enumerate(((mine_ref, own_ref), (away_ref, other_ref))):
        first = jnp.where(index == 0, me_ref[0], 1 - me_ref[0]) * rows
        for lo in range(0, rows, size):
            at = pl.ds(pl.multiple_of(first + lo, size), size)
            u = mm(gg_ref[at, :], w_ref[...], NT)
            out_ref[lo : lo + size, :] = u.astype(BF16)
            term = u * cot_ref[lo : lo + size, :].astype(F32)
            for part in range(0, width, LANES):
                product[at, :] += term[:, part : part + LANES]

    @pl.when(pl.program_id(0) == pl.num_programs(0) - 1)
    def _():
        live = iota(product.shape, 0) < ends_ref[ends_ref.shape[0] - 1]
        prod_ref[...] = row_sums(jnp.where(live, product[...], 0.0))


def gate_backward(
    me_ref, ends_ref, own_ref, other_ref, w_ref, y_ref, z_ref, rg_ref, coef_ref, gain_ref,
    dy_ref, dz_ref, acc_ref, rg, coef,
):
    total, width = dy_ref.shape
    rows = own_ref.shape[0]
    size = 512

    @pl.when(pl.program_id(0) == 0)
    def _():
        live = iota(rg.shape, 0) < ends_ref[ends_ref.shape[0] - 1]
        rg[...] = spread_rows(rg_ref[...])
        coef[...] = spread_rows(coef_ref[...])
        rg[...] = jnp.where(live, rg[...], 0.0)

    gain = gain_ref[K + 1 : K + 2, :]
    sums = jnp.zeros((8, width), F32)
    for index, cot_ref in enumerate((own_ref, other_ref)):
        first = jnp.where(index == 0, me_ref[0], 1 - me_ref[0]) * rows
        for lo in range(0, rows, size):
            at = pl.ds(pl.multiple_of(first + lo, size), size)
            ds = mm(cot_ref[lo : lo + size, :], w_ref[...])
            z = z_ref[at, :].astype(F32)
            y = y_ref[at, :].astype(F32)
            scale = jnp.concatenate([rg[at, :]] * (width // LANES), axis=1)
            back = jnp.concatenate([coef[at, :]] * (width // LANES), axis=1)
            gate = sigmoid(z)
            silu = z * gate
            gated = y * silu
            d_normal = ds * scale
            sums = sums + (d_normal * gated).reshape(size // 8, 8, width).sum(axis=0)
            d_gated = d_normal * gain - gated * back
            dy_ref[at, :] = (d_gated * silu).astype(BF16)
            dz_ref[at, :] = (d_gated * y * (gate + silu * (1.0 - gate))).astype(BF16)
    acc_ref[...] = sums


def weight_grad(me_ref, own_ref, other_ref, d_ref, away_ref, keep_ref):
    half, rows = away_ref.shape[0], own_ref.shape[1]
    mine = d_ref[pl.ds(pl.multiple_of(me_ref[0] * rows, rows), rows), :]
    theirs = d_ref[pl.ds(pl.multiple_of((1 - me_ref[0]) * rows, rows), rows), :]
    for at, ref in ((0, away_ref), (half, keep_ref)):
        total = mm(own_ref[at : at + half, :], mine) + mm(other_ref[at : at + half, :], theirs)
        ref[...] = total.astype(BF16)


def normed_back(rows_ref, dz_ref, dxa_ref, dxb_ref, wz_ref, wx_ref, out_ref):
    n_a = dxa_ref.shape[1]
    total = mm(dz_ref[...], wz_ref[...], NT)
    total = total + mm(dxa_ref[...], wx_ref[:, :n_a], NT) + mm(dxb_ref[...], wx_ref[:, n_a:], NT)
    out_ref[...] = total.astype(BF16)


def params():
    return pltpu.CompilerParams(dimension_semantics=("arbitrary",), vmem_limit_bytes=VMEM_LIMIT)


SMALL_COST = pl.CostEstimate(flops=1000, bytes_accessed=1000, transcendentals=0)


def rows_spec(block, width, column=0):
    return pl.BlockSpec((block, width), lambda i: (i, column))


def whole_spec(shape, column=0):
    return pl.BlockSpec(shape, lambda i: (0, column))


def local(
    tokens,
    cotangent,
    lengths,
    norm_gain,
    w_zx,
    w_bc,
    w_dt,
    conv_x,
    conv_x_bias,
    conv_bc,
    conv_bc_bias,
    dt_bias,
    a_log,
    d_skip,
    gate_gain,
    w_out,
):
    n_t = lax.axis_size("tensor")
    n_dp = lax.axis_size("dp")
    me_t = lax.axis_index("tensor")
    me_dp = lax.axis_index("dp")
    own_rows, depth = tokens.shape
    group = own_rows * n_t
    chunks = group // Q
    heads = dt_bias.shape[0]
    inner = heads * WIDTH
    inner_total = inner * n_t
    shard = w_zx.shape[1]
    pairs = [(i, n_t - 1 - i) for i in range(n_t)]

    def swap(v):
        return lax.ppermute(v, "tensor", pairs)

    def in_order(mine, other, axis=0):
        low = jnp.where(me_t == 0, mine, other)
        high = jnp.where(me_t == 0, other, mine)
        return jnp.concatenate([low, high], axis=axis)

    def sum_dp(v):
        step = 1
        while step < n_dp:
            v = v + lax.ppermute(v, "dp", [(i, i ^ step) for i in range(n_dp)])
            step *= 2
        return v

    def after(value, *others):
        return lax.optimization_barrier((value, *others))[0]

    ring = 4
    plane = n_dp // (2 * ring)

    around = [(i, (i + 2 * plane) % n_dp) for i in range(n_dp)]
    across = [(i, i ^ 2) for i in range(n_dp)]
    beside = [(i, i ^ 1) for i in range(n_dp)]

    def send(v, way):
        return lax.ppermute(v, "dp", way)

    by_hand = plane == 2 and shard % 32 == 0

    def whole(v):
        return [lax.all_gather(v, "dp", axis=0, tiled=True)]

    def relative_order():
        level, side, core = me_dp // 4, (me_dp // 2) % 2, me_dp % 2
        order = []
        for dc in (1, 0):
            for dy in (1, 0):
                for dz in range(1, ring + 1):
                    order.append(((level - dz + ring) % ring) * 4 + (side ^ dy) * 2 + (core ^ dc))
        return order

    def fold_beside(keep, got):
        half = keep.shape[0] // 2
        away = (keep[:half].astype(F32) + got[:half].astype(F32)).astype(BF16)
        return away, keep[half:].astype(F32) + got[half:].astype(F32)

    def ring_part(keep, got, came, turn):
        at = slice((turn - 1) * shard, turn * shard)
        part = keep[at] + got[at].astype(F32)
        if came is not None:
            part = part + came.astype(F32)
        return part if turn == ring else part.astype(BF16)

    ends = jnp.cumsum(lengths[0]).astype(jnp.int32)
    live = (lax.iota(jnp.int32, group) < ends[-1]).astype(F32)
    live_own = lax.dynamic_slice_in_dim(live, me_t * own_rows, own_rows, 0)
    me = me_t.astype(jnp.int32).reshape(1)

    span_p = conv_x_bias.shape[1]
    span_n = conv_bc_bias.shape[1]
    half_bc = w_bc.shape[1]
    bits = jnp.concatenate([norm_gain, conv_bc.reshape(-1), conv_bc_bias.reshape(-1)])
    bits = jnp.pad(bits, (0, LANES - bits.shape[0]))
    tiny = jnp.concatenate([w_bc.reshape(2 * half_bc, STATE), bits[None]], axis=0)
    other_tiny = swap(tiny)
    other_bc = other_tiny[: 2 * half_bc].reshape(w_bc.shape)
    both_bits = [bits, other_tiny[2 * half_bc]]
    at = norm_gain.shape[0]
    gain_pair = in_order(*[v[:at] for v in both_bits])[:, None]
    taps_bc = in_order(*[v[at : at + conv_bc.size].reshape(2, span_n, K) for v in both_bits], axis=1)
    at += conv_bc.size
    bias_bc = in_order(*[v[at : at + 2 * span_n].reshape(2, span_n, 1) for v in both_bits], axis=1)
    spare_bc = jnp.concatenate([taps_bc, bias_bc], axis=2).reshape(4 * span_n, K + 1)
    spare_x = [conv_x.reshape(shard, K), conv_x_bias.reshape(shard, 1), gate_gain.reshape(shard, 1), gain_pair]
    bc_pair = in_order(w_bc, other_bc, axis=1)
    w_x = w_zx[1]
    w_small = jnp.concatenate(
        [bc_pair[0], bc_pair[1], w_dt, *spare_x, jnp.zeros((shard, 8 - K - 3), BF16)]
        + [jnp.pad(spare_bc, ((0, shard - 4 * span_n), (0, LANES - heads - 8 - K - 1)))],
        axis=1,
    )
    gain_pair = gain_pair.astype(F32)
    where = after(lax.iota(jnp.int32, depth), w_small)
    home, inside = where // shard, where % shard
    place_x = (inside // span_p) * WIDTH + home * span_p + inside % span_p
    half_n = 2 * span_n
    place_bc = (inside // half_n) * STATE + home * half_n + inside % half_n
    place = jnp.concatenate([jnp.broadcast_to(v[:, None], (depth, LANES)) for v in (place_x, place_bc)], axis=1)
    par = jnp.concatenate([dt_bias[None], a_log[None], jnp.zeros((6, heads), F32)], axis=0)
    par = jnp.concatenate([par, jnp.zeros((8, LANES - heads), F32)], axis=1)
    skip = jnp.repeat(d_skip, WIDTH)[None]
    members = lax.iota(jnp.int32, inner)[:, None] // WIDTH
    sel = (members == lax.iota(jnp.int32, LANES)[None, :]).astype(BF16)
    smem = pl.BlockSpec(memory_space=pltpu.SMEM)
    vmem = pl.BlockSpec(memory_space=pltpu.VMEM)
    hbm = pl.BlockSpec(memory_space=pl.ANY)
    n_small = 2 * STATE + LANES
    n_conv = inner + 2 * STATE
    w_rest = jnp.concatenate([w_zx[0], w_out.T], axis=1)

    def turn(rows):
        return pl.pallas_call(
            turn_rows,
            in_specs=[smem, vmem],
            out_specs=vmem,
            out_shape=jax.ShapeDtypeStruct((depth, own_rows), BF16),
            scratch_shapes=[pltpu.VMEM((depth, own_rows), BF16)],
            compiler_params=pltpu.CompilerParams(vmem_limit_bytes=VMEM_LIMIT),
            cost_estimate=SMALL_COST,
            name="turn_rows",
        )((jnp.stack(relative_order()) * shard).astype(jnp.int32), rows)

    def place_of(turn, side, core):
        level = (me_dp // (2 * plane) - turn + ring) % ring
        return (level * (2 * plane) + ((me_dp % (2 * plane)) ^ (2 * side + core))) * shard

    together = lambda *values: list(lax.optimization_barrier(tuple(values)))
    joined = lambda *values: jnp.concatenate(values, axis=0)
    if by_hand:
        shift = lambda k: [(i, (i + 2 * plane * k) % n_dp) for i in range(n_dp)]
        l1, o0, c0 = together(send(w_x, around), send(w_x, across), send(w_x, beside))
        late, w_small = together(tokens, w_small, l1, o0, c0)[:2]
        l2, o1, s1, s2, s3, turned_own = together(
            send(l1, around), send(l1, across), send(w_small, shift(1)), send(w_small, shift(2)), send(w_small, shift(3)),
            turn(late),
        )
        w_rest = after(jnp.concatenate([w_zx[0], w_out.T], axis=1), l2)
        zo_all = lax.all_gather(w_rest, "dp", axis=0, tiled=True)
        small_line = joined(w_small, s1, s2, s3)
        split = own_rows // 2
        l3, o2, c1, small_across, t0 = together(
            send(l2, around), send(l2, across), send(joined(l1, o0), beside), send(small_line, across), swap(late[:split])
        )
        o3, c2, small_beside, t1, place, par, skip, sel = together(
            send(l3, across), send(joined(l2, o1), beside), send(joined(small_line, small_across), beside),
            swap(after(late[split:], t0)), place, par, skip, sel,
        )
        other_tokens = joined(t0, t1)
        c3, turned_other, other_tokens = together(send(joined(l3, o2, o3), beside), turn(other_tokens), other_tokens)
        other_cot = swap(after(cotangent, other_tokens))
        wx_parts = [w_x, l1, l2, l3, o0, o1, o2, o3, c0, c1, c2, c3]
        order = [(t, 0, 0) for t in range(4)] + [(t, 1, 0) for t in range(4)]
        order += [(0, 0, 1), (1, 0, 1), (0, 1, 1), (2, 0, 1), (1, 1, 1), (3, 0, 1), (2, 1, 1), (3, 1, 1)]
        small_parts = [small_line, small_across, small_beside]
        order += [(t, side, core) for core in range(2) for side in range(2) for t in range(4)]
        offsets = jnp.stack([place_of(*key) for key in order]).astype(jnp.int32)
    else:
        wx_parts, small_parts = whole(w_x), whole(w_small)
        zo_all = whole(jnp.concatenate([w_zx[0], w_out.T], axis=1))[0]
        other_tokens, other_cot = swap(tokens), swap(cotangent)
        offsets = jnp.zeros((2,), jnp.int32)
    counts = (len(wx_parts), len(small_parts))
    sems = pltpu.SemaphoreType.DMA((offsets.shape[0],))
    tok_own = tokens.astype(F32)
    inv_tok = lax.rsqrt(jnp.mean(tok_own * tok_own, axis=1, keepdims=True) + EPSILON)

    block = own_rows
    steps = group // block
    x_raw, small, normed, taps, gain_in, wx_all = pl.pallas_call(
        partial(project, counts, heads, shard if by_hand else depth),
        grid=(steps,),
        in_specs=[
            smem,
            smem,
            whole_spec((block, depth)),
            whole_spec((block, depth)),
            whole_spec((depth, 2 * LANES)),
        ]
        + [hbm] * sum(counts),
        out_specs=[
            rows_spec(block, inner),
            rows_spec(block, n_small),
            rows_spec(block, depth),
            whole_spec((8, n_conv)),
            whole_spec((8, depth)),
            hbm,
        ],
        out_shape=[
            jax.ShapeDtypeStruct((group, inner), BF16),
            jax.ShapeDtypeStruct((group, n_small), F32),
            jax.ShapeDtypeStruct((group, depth), BF16),
            jax.ShapeDtypeStruct((8, n_conv), F32),
            jax.ShapeDtypeStruct((8, depth), F32),
            jax.ShapeDtypeStruct((depth, inner + n_small), BF16),
        ],
        scratch_shapes=[pltpu.VMEM((depth, inner + n_small), BF16), sems, pltpu.SemaphoreType.DMA],
        compiler_params=params(),
        cost_estimate=SMALL_COST,
        name="project",
    )(offsets, me, tokens, other_tokens, place, *wx_parts, *small_parts)
    xc, pre, bc, y_all, states = pl.pallas_call(
        partial(scan_forward, heads),
        grid=(chunks,),
        in_specs=[
            smem,
            rows_spec(Q, inner),
            rows_spec(Q, n_small),
            whole_spec((8, n_conv)),
            whole_spec((8, LANES)),
            whole_spec((1, inner)),
        ],
        out_specs=[
            rows_spec(Q, inner),
            rows_spec(Q, n_conv),
            rows_spec(Q, 2 * STATE),
            rows_spec(Q, inner),
            pl.BlockSpec((1, STATE, inner), lambda i: (i, 0, 0)),
        ],
        out_shape=[
            jax.ShapeDtypeStruct((group, inner), BF16),
            jax.ShapeDtypeStruct((group, n_conv), BF16),
            jax.ShapeDtypeStruct((group, 2 * STATE), BF16),
            jax.ShapeDtypeStruct((group, inner), BF16),
            jax.ShapeDtypeStruct((chunks, STATE, inner), BF16),
        ],
        scratch_shapes=[pltpu.VMEM((n_conv // LANES, Q + 8, LANES), F32), pltpu.VMEM((STATE, inner), F32)],
        compiler_params=params(),
        cost_estimate=SMALL_COST,
        name="scan_forward",
    )(ends, x_raw, small, taps, par, skip)

    cot_all = in_order(cotangent, other_cot)
    if by_hand:
        normed, cot_all = lax.optimization_barrier((normed, after(cot_all, y_all)))
    tile = 512
    columns = lambda rows, shift=0: pl.BlockSpec((rows, tile), lambda j: (0, j + shift))
    fixed = lambda shape: pl.BlockSpec(shape, lambda j: (0, 0))
    tiles = inner // tile
    z_all, gg, sq = pl.pallas_call(
        gate_forward,
        grid=(tiles,),
        in_specs=[fixed((group, depth)), columns(depth), columns(group), columns(8)],
        out_specs=[columns(group), columns(group), fixed((8, group))],
        out_shape=[
            jax.ShapeDtypeStruct((group, inner), BF16),
            jax.ShapeDtypeStruct((group, inner), BF16),
            jax.ShapeDtypeStruct((8, group), F32),
        ],
        scratch_shapes=[pltpu.VMEM((group, LANES), F32)],
        compiler_params=params(),
        cost_estimate=SMALL_COST,
        name="gate_forward",
    )(normed, zo_all, y_all, taps)
    sq_got = swap(sq)

    u_own, u_send, prod = pl.pallas_call(
        branch,
        grid=(depth // tile,),
        in_specs=[
            smem,
            smem,
            fixed((group, inner)),
            columns(own_rows),
            columns(own_rows),
            pl.BlockSpec((tile, inner), lambda j: (j, 1)),
        ],
        out_specs=[columns(own_rows), columns(own_rows), fixed((8, group))],
        out_shape=[
            jax.ShapeDtypeStruct((own_rows, depth), BF16),
            jax.ShapeDtypeStruct((own_rows, depth), BF16),
            jax.ShapeDtypeStruct((8, group), F32),
        ],
        scratch_shapes=[pltpu.VMEM((group, LANES), F32)],
        compiler_params=params(),
        cost_estimate=SMALL_COST,
        name="branch",
    )(me, ends, gg, cotangent, other_cot, zo_all)
    prod_got = swap(prod)
    sq_all = sq + after(sq_got, prod)
    inv_gate8 = lax.rsqrt(sq_all / inner_total + EPSILON)
    inv_gate = inv_gate8[0]
    d_branch = (cot_all.astype(F32) * (live * inv_gate)[:, None]).astype(BF16)
    g_out = lax.dot_general(d_branch, gg, TN, preferred_element_type=F32).astype(BF16)
    grad_out = lax.psum_scatter(g_out, "dp", scatter_dimension=0, tiled=True)
    prod_got = after(prod_got, g_out)
    u_recv = swap(after(u_send, g_out))
    inv_own = lax.dynamic_slice_in_dim(inv_gate, me_t * own_rows, own_rows, 0)
    out_branch = (u_own.astype(F32) + u_recv.astype(F32)) * (inv_own * live_own)[:, None]
    layer_out = (tokens.astype(F32) + out_branch).astype(BF16)

    prod_all = prod + prod_got
    coef8 = inv_gate8 * inv_gate8 * inv_gate8 * (prod_all / inner_total)
    dy, dz, gain_acc = pl.pallas_call(
        gate_backward,
        grid=(tiles,),
        in_specs=[
            smem,
            smem,
            fixed((own_rows, depth)),
            fixed((own_rows, depth)),
            columns(depth, tiles),
            columns(group),
            columns(group),
            fixed((8, group)),
            fixed((8, group)),
            columns(8),
        ],
        out_specs=[columns(group), columns(group), columns(8)],
        out_shape=[
            jax.ShapeDtypeStruct((group, inner), BF16),
            jax.ShapeDtypeStruct((group, inner), BF16),
            jax.ShapeDtypeStruct((8, inner), F32),
        ],
        scratch_shapes=[pltpu.VMEM((group, LANES), F32), pltpu.VMEM((group, LANES), F32)],
        compiler_params=params(),
        cost_estimate=SMALL_COST,
        name="gate_backward",
    )(me, ends, cotangent, other_cot, zo_all, y_all, z_all, inv_gate8, coef8, taps)
    dot = partial(lax.dot_general, preferred_element_type=F32)
    front = depth // 2

    def gradient(d, width):
        outs = pl.BlockSpec((front, width), lambda j: (0, j))
        return pl.pallas_call(
            weight_grad,
            grid=(d.shape[1] // width,),
            in_specs=[smem, fixed((depth, own_rows)), fixed((depth, own_rows)), pl.BlockSpec((group, width), lambda j: (0, j))],
            out_specs=[outs, outs],
            out_shape=[jax.ShapeDtypeStruct((front, d.shape[1]), BF16)] * 2,
            compiler_params=params(),
            cost_estimate=SMALL_COST,
            name="weight_grad",
        )(me, turned_own, turned_other, d)

    if by_hand:
        g_send, z_keep = gradient(dz, tile)
        z_got = send(g_send, beside)
        dy = after(dy, z_keep, g_send)
    else:
        grad_z = lax.psum_scatter(dot(normed, dz, TN).astype(BF16), "dp", scatter_dimension=0, tiled=True)

    halo_spec = pl.BlockSpec((n_conv // LANES, 8, LANES), lambda i: (0, 0, 0))

    def backward(top, number, carry):
        back = lambda width: pl.BlockSpec((Q, width), lambda i: (top - i, 0))
        operands = [ends, dy, xc, pre, x_raw, small, bc, states, taps, par, skip, sel, *carry]
        acc_spec = whole_spec((8 * (K + 2), n_conv))
        carry_shapes = [
            jax.ShapeDtypeStruct((STATE, inner), F32),
            jax.ShapeDtypeStruct((n_conv // LANES, 8, LANES), F32),
        ]
        carry_specs = []
        if carry:
            carry_specs = [whole_spec((STATE, inner)), halo_spec, acc_spec, whole_spec((16, LANES))]
            carry_specs += [whole_spec((8, inner)), hbm, hbm]
        return pl.pallas_call(
            partial(scan_backward, heads, chunks, top),
            grid=(number,),
            in_specs=[
                smem,
                back(inner),
                back(inner),
                back(n_conv),
                back(inner),
                back(n_small),
                back(2 * STATE),
                pl.BlockSpec((1, STATE, inner), lambda i: (top - i, 0, 0)),
                whole_spec((8, n_conv)),
                whole_spec((8, LANES)),
                whole_spec((1, inner)),
                whole_spec((inner, LANES)),
            ]
            + carry_specs,
            out_specs=[
                back(n_a),
                back(n_b),
                *([whole_spec((8, n_conv))] if carry else []),
                acc_spec,
                whole_spec((16, LANES)),
                *([] if carry else [whole_spec((STATE, inner)), halo_spec]),
            ],
            out_shape=[
                jax.ShapeDtypeStruct((group, n_a), BF16),
                jax.ShapeDtypeStruct((group, n_b), BF16),
                *([jax.ShapeDtypeStruct((8, n_conv), F32)] if carry else []),
                jax.ShapeDtypeStruct((8 * (K + 2), n_conv), F32),
                jax.ShapeDtypeStruct((16, LANES), F32),
                *([] if carry else carry_shapes),
            ],
            scratch_shapes=[
                pltpu.VMEM((STATE, inner), F32),
                pltpu.VMEM((n_conv // LANES, Q + 8, LANES), F32),
                pltpu.VMEM((Q, inner), BF16),
                pltpu.VMEM((Q, inner), BF16),
                pltpu.VMEM((Q, inner), BF16),
                pltpu.VMEM((Q, inner), BF16),
                pltpu.VMEM((Q, inner), BF16),
                pltpu.VMEM((Q, inner), BF16),
                pltpu.VMEM((STATE, inner), BF16),
                pltpu.VMEM((8, inner), F32),
            ],
            input_output_aliases={len(operands) - 2: 0, len(operands) - 1: 1} if carry else {},
            compiler_params=params(),
        cost_estimate=SMALL_COST,
            name="scan_backward",
        )(*operands)

    half_chunks = chunks // 2
    n_b = (inner + n_small) // 3
    n_a = inner + n_small - n_b
    dxa, dxb, acc, hacc, d_state, halo = backward(chunks - 1, chunks - half_chunks, ())
    if by_hand:
        z_got, dxa = lax.optimization_barrier((z_got, dxa))
        z_away, z_keep = fold_beside(z_keep, z_got)
        z_got = send(z_away, across)
        d_state = after(d_state, z_away, z_keep)
    dxa, dxb, vector = backward(half_chunks - 1, half_chunks, (d_state, halo, acc, hacc, gain_acc, dxa, dxb))[:3]
    dxa = after(dxa, u_recv)
    lanes_shared = lax.iota(jnp.int32, n_conv)[None, :] >= inner
    bits_of = lambda turn: [(i, i ^ (1 << turn)) for i in range(n_dp)]
    if by_hand:
        g_x = dot(normed, dxa, TN).astype(BF16)
        g_x, grad_out = lax.optimization_barrier((g_x, grad_out))
        grad_a = lax.psum_scatter(g_x, "dp", scatter_dimension=0, tiled=True)
        z_got, dxb, vector = lax.optimization_barrier((z_got, dxb, vector, g_x))[:3]
        z_out = ring_part(z_keep, z_got, None, 1)
        z_came = send(z_out, around)
        shared_got = swap(vector)
        b_send, b_keep = gradient(after(dxb, z_out), n_b)
        b_got = send(b_send, beside)
        shared_got, z_came, b_keep = lax.optimization_barrier((shared_got, z_came, b_keep))
        vector = vector + jnp.where(lanes_shared, shared_got, 0.0)
        z_out = ring_part(z_keep, z_got, z_came, 2)
        z_came, vector_got = send(z_out, around), send(vector, bits_of(0))
        dz = after(dz, b_send, b_keep, z_out, vector)
    else:
        dx = jnp.concatenate([dxa, dxb], axis=1)
        grad_x = lax.psum_scatter(dot(normed, dx, TN).astype(BF16), "dp", scatter_dimension=0, tiled=True)

    def back_rows(which, dz):
        pick = lambda width: pl.BlockSpec((own_rows, width), lambda j, rows: (rows[0], 0))
        return pl.pallas_call(
            normed_back,
            grid_spec=pltpu.PrefetchScalarGridSpec(
                num_scalar_prefetch=1,
                grid=(depth // tile,),
                in_specs=[
                    pick(inner),
                    pick(n_a),
                    pick(n_b),
                    pl.BlockSpec((tile, inner), lambda j, rows: (j, 0)),
                    pl.BlockSpec((tile, inner + n_small), lambda j, rows: (j, 0)),
                ],
                out_specs=pl.BlockSpec((own_rows, tile), lambda j, rows: (0, j)),
            ),
            out_shape=jax.ShapeDtypeStruct((own_rows, depth), BF16),
            compiler_params=params(),
            cost_estimate=SMALL_COST,
            name="normed_back",
        )(which, dz, dxa, dxb, zo_all, wx_all)

    dn_send = back_rows(n_t - 1 - me, dz)
    if by_hand:
        w_sum = lambda w, g: jnp.sum(w.astype(F32) * g, axis=1)
        b_got, vector_got, dn_send, z_came = lax.optimization_barrier((b_got, vector_got, dn_send, z_came))
        dn_got = swap(dn_send)
        b_away, b_keep = fold_beside(b_keep, b_got)
        b_got = send(b_away, across)
        vector = vector + vector_got
        z_out = ring_part(z_keep, z_got, z_came, 3)
        z_came, vector_got = send(z_out, around), send(vector, bits_of(1))
        dn_own = back_rows(me, after(dz, vector, z_out, b_away, b_keep))
        vector_got, dn_own, b_got, z_came = lax.optimization_barrier((vector_got, dn_own, b_got, z_came))
        vector = vector + vector_got
        b_out = ring_part(b_keep, b_got, None, 1)
        b_came, vector_got = send(b_out, around), send(vector, bits_of(2))
        grad_z = ring_part(z_keep, z_got, z_came, ring) * gain_pair
        in_part = w_sum(w_zx[0], grad_z)
        vector_got, grad_z, in_part, b_came = lax.optimization_barrier((vector_got, grad_z, in_part, b_came))
        vector = vector + vector_got
        b_out = ring_part(b_keep, b_got, b_came, 2)
        b_came, vector_got = send(b_out, around), send(vector, bits_of(3))
        grad_out = grad_out.astype(F32).T
        vector_got, grad_out, layer_out, b_came = lax.optimization_barrier((vector_got, grad_out, layer_out, b_came))
        vector = vector + vector_got
        b_came = send(ring_part(b_keep, b_got, b_came, 3), around)
    else:
        vector = sum_dp(vector + jnp.where(lanes_shared, swap(vector), 0.0))
        dn_own = back_rows(me, dz)
        dn_got = swap(dn_send)
        grad_out = grad_out.astype(F32).T
        grad_z, grad_x = grad_z.astype(F32), grad_x.astype(F32)
        in_part = jnp.sum(w_zx[0].astype(F32) * grad_z, axis=1) + jnp.sum(jnp.concatenate([w_x, w_small], axis=1).astype(F32) * grad_x, axis=1)

    me_all = me_dp * n_t + me_t
    bc_sum = vector[: K + 1, inner:].reshape(K + 1, 2, STATE)
    bc_sum = lax.dynamic_slice_in_dim(bc_sum, me_all * span_n, span_n, 2)
    grad_bc_taps = bc_sum[:K].transpose(1, 2, 0).reshape(conv_bc.shape)
    grad_bc_bias = bc_sum[K]
    x_sum = vector[: K + 3, :inner].reshape(K + 3, heads, WIDTH)
    grad_skip = x_sum[K + 1].sum(axis=1)
    x_sum = lax.dynamic_slice_in_dim(x_sum, me_dp * span_p, span_p, 2)
    grad_x_taps = x_sum[:K].transpose(1, 2, 0).reshape(conv_x.shape)
    grad_x_bias = x_sum[K]
    grad_gate = x_sum[K + 2]
    grad_dt_bias = vector[K + 3, :heads]
    grad_a_log = vector[K + 3, LANES : LANES + heads]
    dn = (dn_own.astype(F32) + dn_got.astype(F32)) * gain_in[0:1, :]
    grad_tokens = (
        cotangent.astype(F32)
        + inv_tok * dn
        - tok_own * inv_tok * inv_tok * inv_tok * jnp.mean(dn * tok_own, axis=1, keepdims=True)
    )

    if by_hand:
        grad_b = ring_part(b_keep, b_got, b_came, ring) * gain_pair
        in_part = in_part + w_sum(w_x[:, n_a:], grad_b[:, : inner - n_a]) + w_sum(w_small, grad_b[:, inner - n_a :])
        outs = (grad_bc_taps, grad_bc_bias, grad_skip, grad_x_taps, grad_x_bias, grad_gate, grad_dt_bias, grad_a_log)
        outs = lax.optimization_barrier((*outs, grad_tokens, grad_b, in_part, grad_a))
        grad_bc_taps, grad_bc_bias, grad_skip, grad_x_taps, grad_x_bias, grad_gate, grad_dt_bias, grad_a_log = outs[:8]
        grad_tokens, grad_b, in_part, grad_a = outs[8:]
        grad_a = grad_a.astype(F32)
        in_part = in_part + w_sum(w_x[:, :n_a], grad_a)
    else:
        grad_a, grad_b = grad_x[:, :n_a], grad_x[:, n_a:]
    at = inner - n_a
    bc_part = jnp.concatenate([grad_b[:, at : at + 2 * STATE], jnp.broadcast_to(in_part[:, None], (shard, LANES))], axis=1)
    grad_zx = jnp.stack([grad_z, jnp.concatenate([grad_a, grad_b[:, :at]], axis=1)])
    grad_dt = grad_b[:, at + 2 * STATE : at + 2 * STATE + heads]
    half = half_bc
    bc_own = lax.dynamic_slice_in_dim(bc_part, me_t * half, half, 0)
    bc_send = lax.dynamic_slice_in_dim(bc_part, (n_t - 1 - me_t) * half, half, 0)
    bc_total = bc_own + swap(bc_send)
    own_gain = norm_gain.astype(F32)
    grad_bc = bc_total[:, : 2 * STATE].reshape(half, 2, STATE).transpose(1, 0, 2)
    grad_in = bc_total[:, 2 * STATE] / own_gain
    return (
        layer_out,
        grad_tokens,
        grad_in,
        grad_zx,
        grad_bc,
        grad_dt,
        grad_x_taps,
        grad_x_bias,
        grad_bc_taps,
        grad_bc_bias,
        grad_dt_bias,
        grad_a_log,
        grad_skip,
        grad_gate,
        grad_out,
    )


def solution(mesh):
    both = ("dp", "tensor")
    in_specs = (
        P(both, None),
        P(both, None),
        P("dp", None),
        P(both),
        P(None, "dp", "tensor"),
        P(None, both, None),
        P("dp", "tensor"),
        P("tensor", "dp"),
        P("tensor", "dp"),
        P(None, both),
        P(None, both),
        P("tensor"),
        P("tensor"),
        P("tensor"),
        P("tensor", "dp"),
        P("tensor", "dp"),
    )
    out_specs = (
        P(both, None),
        P(both, None),
        P(both),
        P(None, "dp", "tensor"),
        P(None, both, None),
        P("dp", "tensor"),
        P("tensor", "dp"),
        P("tensor", "dp"),
        P(None, both),
        P(None, both),
        P("tensor"),
        P("tensor"),
        P("tensor"),
        P("tensor", "dp"),
        P("tensor", "dp"),
    )
    return jax.shard_map(local, mesh=mesh, in_specs=in_specs, out_specs=out_specs, check_vma=False)
```

```python
from functools import partial

import jax
import jax.numpy as jnp
from jax import lax
from jax.experimental import pallas as pl
from jax.experimental.pallas import tpu as pltpu
from jax.sharding import PartitionSpec as P

EPSILON = 1e-05
HIGHEST = lax.Precision.HIGHEST
K = 4
WIDTH = 64
STATE = 128
Q = 128
LANES = 128
LOG2E = 1.4426950408889634
VMEM_LIMIT = 60 * 1024 * 1024
F32 = jnp.float32
BF16 = jnp.bfloat16

NN = (((1,), (0,)), ((), ()))
NT = (((1,), (1,)), ((), ()))
TN = (((0,), (0,)), ((), ()))


def mm(a, b, dims=NN):
    return lax.dot_general(a, b, dims, preferred_element_type=F32)


def mm_exact(a, b, dims=NN):
    return lax.dot_general(a, b, dims, preferred_element_type=F32, precision=HIGHEST)


def iota(shape, dim):
    return lax.broadcasted_iota(jnp.int32, shape, dim)


def segment_of(rows, ends_ref, count):
    total = (rows >= ends_ref[0]).astype(jnp.int32)
    for j in range(1, count):
        total = total + (rows >= ends_ref[j]).astype(jnp.int32)
    return total


def scalar_segment(row, ends_ref, count):
    total = jnp.where(row >= ends_ref[0], 1, 0)
    for j in range(1, count):
        total = total + jnp.where(row >= ends_ref[j], 1, 0)
    return total


def sigmoid(v):
    return 0.5 * jnp.tanh(0.5 * v) + 0.5


def softplus(v):
    return jnp.maximum(v, 0.0) + jnp.log1p(jnp.exp(-jnp.abs(v)))


def chunk_masks(chunk, ends_ref, count):
    base = chunk * Q
    rows = iota((Q, Q), 0) + base
    cols = iota((Q, Q), 1) + base
    row_ids = segment_of(rows, ends_ref, count)
    col_ids = segment_of(cols, ends_ref, count)
    same = row_ids == col_ids
    before_id = jnp.where(chunk == 0, -1, scalar_segment(base - 1, ends_ref, count))
    final_id = scalar_segment(base + Q - 1, ends_ref, count)
    carry = (row_ids == before_id).astype(F32)
    last = (row_ids == final_id).astype(F32)
    passing = jnp.where(before_id == final_id, 1.0, 0.0).astype(F32)
    return rows, cols, row_ids, same, carry, last, passing


def decays(dt_raw, par_ref):
    shifted = dt_raw + par_ref[0:1, :]
    step = softplus(shifted)
    decay_rate = jnp.exp(par_ref[1:2, :])
    return shifted, step, decay_rate


def pair_columns(values, pair, first):
    left = jnp.broadcast_to(values[:, 2 * pair : 2 * pair + 1], (Q, LANES))
    right = jnp.broadcast_to(values[:, 2 * pair + 1 : 2 * pair + 2], (Q, LANES))
    return left, right, jnp.where(first, left, right)


def scan_forward(
    heads, ends_ref, xr_ref, small_ref, taps_ref, par_ref, skip_ref,
    xc_ref, pre_ref, bc_ref, y_ref, st_ref, buf, state,
):
    count = ends_ref.shape[0]
    inner = heads * WIDTH
    chunk = pl.program_id(0)

    @pl.when(chunk == 0)
    def _():
        buf[:, 0:8, :] = jnp.zeros((buf.shape[0], 8, LANES), F32)
        state[...] = jnp.zeros(state.shape, F32)

    rows, cols, row_ids, same, carry, last, passing = chunk_masks(chunk, ends_ref, count)
    causal = rows >= cols
    visible = same & causal
    lag_mask = [None]
    for lag in range(1, K):
        earlier = rows - lag
        keep = (segment_of(earlier, ends_ref, count) == row_ids) & (earlier >= 0)
        lag_mask.append(keep.astype(F32))

    small = small_ref[...]

    def convolve(lo, raw):
        span = slice(lo, lo + LANES)
        place = lo // LANES
        buf[place, 8 : 8 + Q, :] = raw
        pre = taps_ref[K : K + 1, span] + taps_ref[K - 1 : K, span] * raw
        for lag in range(1, K):
            pre = pre + taps_ref[K - 1 - lag : K - lag, span] * (
                buf[place, 8 - lag : 8 - lag + Q, :] * lag_mask[lag]
            )
        buf[place, 0:8, :] = raw[Q - 8 : Q, :]
        pre_ref[:, span] = pre.astype(BF16)
        return pre * sigmoid(pre)

    b_f = convolve(inner, small[:, :STATE]).astype(BF16).astype(F32)
    c_b = convolve(inner + STATE, small[:, STATE : 2 * STATE]).astype(BF16)
    b_b = b_f.astype(BF16)
    bc_ref[:, :STATE] = b_b
    bc_ref[:, STATE:] = c_b
    b_t = b_f.T.astype(BF16)

    _, step, decay_rate = decays(small[:, 2 * STATE :], par_ref)
    csum = mm_exact(causal.astype(F32), step * (-LOG2E * decay_rate))
    csum_t = csum.T
    scores = jnp.where(visible, mm(c_b, b_b, NT), 0.0)
    first = iota((Q, LANES), 1) < WIDTH
    first_row = iota((1, LANES), 1) < WIDTH

    wide = 2 * LANES
    for quad in range(0, inner, wide):
        block = slice(quad, quad + wide)
        held = state[:, block]
        held_b = held.astype(BF16)
        st_ref[0, :, block] = held_b
        carried = mm(c_b, held_b)
        weighted, kept = [], []
        for part in range(0, wide, LANES):
            lo = quad + part
            pair = lo // LANES
            span = slice(lo, lo + LANES)
            xc = convolve(lo, xr_ref[:, span].astype(F32)).astype(BF16)
            xc_ref[:, span] = xc
            xc = xc.astype(F32)
            left, right, both = pair_columns(csum, pair, first)
            _, _, step_pair = pair_columns(step, pair, first)
            mix = jnp.concatenate(
                [
                    (scores * jnp.exp2(jnp.minimum(left - csum_t[2 * pair : 2 * pair + 1, :], 0.0))).astype(BF16),
                    (scores * jnp.exp2(jnp.minimum(right - csum_t[2 * pair + 1 : 2 * pair + 2, :], 0.0))).astype(BF16),
                ],
                axis=1,
            )
            fed_b = (xc * step_pair).astype(BF16)
            zero = jnp.zeros((Q, LANES), BF16)
            stacked = jnp.concatenate([jnp.where(first, fed_b, zero), jnp.where(first, zero, fed_b)], axis=0)
            y = mm(mix, stacked) + carried[:, part : part + LANES] * (jnp.exp2(both) * carry)
            y_ref[:, span] = (y + skip_ref[:, span] * xc).astype(BF16)
            closing = both[Q - 1 : Q, :]
            weighted.append((fed_b.astype(F32) * (jnp.exp2(closing - both) * last)).astype(BF16))
            kept.append(jnp.exp2(closing) * passing)
        fresh = mm(b_t, jnp.concatenate(weighted, axis=1))
        state[:, block] = held * jnp.concatenate(kept, axis=1) + fresh


def scan_backward(
    heads, chunks, top, ends_ref, dy_ref, xc_ref, pre_ref, xr_ref, small_ref, bc_ref, st_ref, taps_ref, par_ref,
    skip_ref, sel_ref, *refs,
):
    later_call = top + 1 < chunks
    if later_call:
        state_in, halo_in, acc_in, hacc_in, gain_acc_ref = refs[:5]
        dxa_ref, dxb_ref, rows_ref, acc_ref, hacc_ref = refs[7:12]
        refs = refs[12:]
    else:
        dxa_ref, dxb_ref, acc_ref, hacc_ref, state_out, halo_out = refs[:6]
        refs = refs[6:]
    dstate, dpre, ab_hi, ab_lo, v_b, u_b, dyd, fedw, dst_b, through = refs
    count = ends_ref.shape[0]
    inner = heads * WIDTH
    total_rows = chunks * Q
    chunk = top - pl.program_id(0)

    @pl.when(pl.program_id(0) == 0)
    def _():
        if top + 1 < chunks:
            dpre[:, Q : Q + 8, :] = halo_in[...]
            dstate[...] = state_in[...]
            acc_ref[...] = acc_in[...]
            hacc_ref[...] = hacc_in[...]
        else:
            dpre[:, Q : Q + 8, :] = jnp.zeros((dpre.shape[0], 8, LANES), F32)
            dstate[...] = jnp.zeros(dstate.shape, F32)
            acc_ref[...] = jnp.zeros(acc_ref.shape, F32)
            hacc_ref[...] = jnp.zeros(hacc_ref.shape, F32)

    rows, cols, row_ids, same, carry, last, passing = chunk_masks(chunk, ends_ref, count)
    causal = rows >= cols
    visible = same & causal
    lag_mask = [None]
    for lag in range(1, K):
        later = rows + lag
        keep = (segment_of(later, ends_ref, count) == row_ids) & (later < total_rows)
        lag_mask.append(keep.astype(F32))

    small = small_ref[...]
    shifted, step, decay_rate = decays(small[:, 2 * STATE :], par_ref)
    csum = mm_exact(causal.astype(F32), step * (-LOG2E * decay_rate))
    csum_t = csum.T
    b_b = bc_ref[:, :STATE]
    c_b = bc_ref[:, STATE:]
    c_t = c_b.astype(F32).T.astype(BF16)
    scores = jnp.where(visible, mm(c_b, b_b, NT), 0.0)
    first = iota((Q, LANES), 1) < WIDTH

    n_a = dxa_ref.shape[1]

    def put(lo, values):
        if lo < n_a:
            dxa_ref[:, lo : lo + LANES] = values.astype(BF16)
        else:
            dxb_ref[:, lo - n_a : lo - n_a + LANES] = values.astype(BF16)

    def fold(values):
        return values.reshape(Q // 8, 8, values.shape[1]).sum(axis=0)

    def conv_back(lo, d_conv, raw):
        span = slice(lo, lo + LANES)
        pre = pre_ref[:, span].astype(F32)
        gate = sigmoid(pre)
        d_pre = d_conv * (gate * (1.0 + pre * (1.0 - gate)))
        place = lo // LANES
        dpre[place, 0:Q, :] = d_pre
        d_raw = taps_ref[K - 1 : K, span] * d_pre
        acc_ref[8 * (K - 1) : 8 * K, span] += fold(d_pre * raw)
        acc_ref[8 * K : 8 * K + 8, span] += fold(d_pre)
        for lag in range(1, K):
            moved = dpre[place, lag : lag + Q, :] * lag_mask[lag]
            d_raw = d_raw + taps_ref[K - 1 - lag : K - lag, span] * moved
            acc_ref[8 * (K - 1 - lag) : 8 * (K - lag), span] += fold(moved * raw)
        dpre[place, Q : Q + 8, :] = d_pre[0:8, :]
        put(lo, d_raw)

    d_scores = jnp.zeros((Q, Q), F32)
    wide = 2 * LANES
    for quad in range(0, inner, wide):
        block = slice(quad, quad + wide)
        held_b = st_ref[0, :, block]
        d_held = dstate[:, block]
        d_held_b = d_held.astype(BF16)
        dst_b[:, block] = d_held_b
        carried = mm(c_b, held_b)
        returned = mm(b_b, d_held_b)
        crossing = (d_held * held_b.astype(F32)).reshape(STATE // 8, 8, wide).sum(axis=0)
        grown_parts, kept_parts = [], []
        for part in range(0, wide, LANES):
            lo = quad + part
            pair = lo // LANES
            span = slice(lo, lo + LANES)
            xc = xc_ref[:, span].astype(F32)
            dy_b = dy_ref[:, span]
            dy = dy_b.astype(F32)
            left, right, both = pair_columns(csum, pair, first)
            _, _, step_pair = pair_columns(step, pair, first)
            fall_left = jnp.exp2(jnp.minimum(left - csum_t[2 * pair : 2 * pair + 1, :], 0.0))
            fall_right = jnp.exp2(jnp.minimum(right - csum_t[2 * pair + 1 : 2 * pair + 2, :], 0.0))
            mix = jnp.concatenate([(scores * fall_left).astype(BF16), (scores * fall_right).astype(BF16)], axis=1)
            fed_b = (xc * step_pair).astype(BF16)
            fed = fed_b.astype(F32)
            zero = jnp.zeros((Q, LANES), BF16)
            stacked = jnp.concatenate([jnp.where(first, fed_b, zero), jnp.where(first, zero, fed_b)], axis=0)
            grown = jnp.exp2(both) * carry
            y = mm(mix, stacked) + carried[:, part : part + LANES] * grown
            d_mix = mm(dy_b, stacked, NT)
            d_scores = d_scores + d_mix[:, :Q] * fall_left + d_mix[:, Q:] * fall_right
            d_fed2 = mm(mix, dy_b, TN)
            d_fed_in = jnp.where(first, d_fed2[:Q], d_fed2[Q:])
            closing = both[Q - 1 : Q, :]
            shrink = jnp.exp2(closing - both) * last
            d_fed_out = returned[:, part : part + LANES] * shrink
            d_fed = d_fed_in + d_fed_out
            straddle = dy * y - fed * d_fed_in
            hi = straddle.astype(BF16)
            ab_hi[:, span] = hi
            ab_lo[:, span] = (straddle - hi.astype(F32)).astype(BF16)
            v_b[:, span] = (fed * d_fed_out).astype(BF16)
            u_b[:, span] = (xc * d_fed).astype(BF16)
            fedw[:, span] = (fed * shrink).astype(BF16)
            grown_parts.append((dy * grown).astype(BF16))
            kept_parts.append(jnp.exp2(closing) * passing)
            acc_ref[8 * K + 8 : 8 * K + 16, span] += fold(dy * xc)
            d_conv = d_fed * step_pair + skip_ref[:, span] * dy
            conv_back(lo, d_conv, xr_ref[:, span].astype(F32))
        dy_grown = jnp.concatenate(grown_parts, axis=1)
        kept = jnp.concatenate(kept_parts, axis=1)
        dyd[:, block] = dy_grown
        through[:, block] = crossing * kept
        dstate[:, block] = d_held * kept + mm(c_t, dy_grown)

    d_scores_b = jnp.where(visible, d_scores, 0.0).astype(BF16)
    d_c = mm(dyd[...], st_ref[0], NT) + mm(d_scores_b, b_b)
    d_b = mm(fedw[...], dst_b[...], NT) + mm(d_scores_b, c_b, TN)
    conv_back(inner, d_b, small[:, :STATE])
    conv_back(inner + STATE, d_c, small[:, STATE : 2 * STATE])

    sel = sel_ref[...]
    red_ab = mm(ab_hi[...], sel) + mm(ab_lo[...], sel)
    red_v = mm(v_b[...], sel)
    red_u = mm(u_b[...], sel)
    thr = through[...]
    thr_hi = thr.astype(BF16)
    red_t = mm(thr_hi, sel) + mm((thr - thr_hi.astype(F32)).astype(BF16), sel)
    d_rate = (
        mm_exact((same & (cols >= rows)).astype(F32), red_ab)
        + mm_exact((same & (cols < rows)).astype(F32), red_v)
        + jnp.sum(red_t, axis=0, keepdims=True)
    )
    d_step = red_u - d_rate * decay_rate
    d_dt = d_step * sigmoid(shifted)
    put(inner + 2 * STATE, d_dt)
    hacc_ref[0:8, :] += fold(d_dt)
    hacc_ref[8:16, :] += fold(d_rate * (-decay_rate * step))
    if later_call:

        @pl.when(pl.program_id(0) == pl.num_programs(0) - 1)
        def _():
            rows_ref[...] = jnp.zeros(rows_ref.shape, F32)
            for k in range(K + 2):
                rows_ref[k : k + 1, :] = jnp.sum(acc_ref[8 * k : 8 * k + 8, :], axis=0, keepdims=True)
            rows_ref[K + 2 : K + 3, :inner] = jnp.sum(gain_acc_ref[...], axis=0, keepdims=True)
            for k in range(2):
                total = jnp.sum(hacc_ref[8 * k : 8 * k + 8, :], axis=0, keepdims=True)
                rows_ref[K + 3 : K + 4, k * LANES : (k + 1) * LANES] = total

    else:
        halo_out[...] = dpre[:, Q : Q + 8, :]
        state_out[...] = dstate[...]


def load_blocks(offsets_ref, parts, whole, sems, size, columns, first=0):
    @pl.when(pl.program_id(0) == 0)
    def _():
        copies = []
        for part in parts:
            for j in range(part.shape[0] // size):
                k = first + len(copies)
                start = 0 if size == whole.shape[0] else pl.multiple_of(offsets_ref[k], 32)
                source = part.at[pl.ds(j * size, size), :]
                copies.append(pltpu.make_async_copy(source, whole.at[pl.ds(start, size), slice(*columns)], sems.at[k]))
        for copy in copies:
            copy.start()
        for copy in copies:
            copy.wait()


def turn_rows(offsets_ref, source_ref, out_ref, turned):
    rows, depth = source_ref.shape
    for lo in range(0, rows, Q):
        tile = source_ref[lo : lo + Q, :].astype(F32)
        tile = tile * lax.rsqrt(jnp.mean(tile * tile, axis=1, keepdims=True) + EPSILON)
        for left in range(0, depth, LANES):
            turned[left : left + LANES, lo : lo + Q] = tile[:, left : left + LANES].T.astype(BF16)
    count = offsets_ref.shape[0]
    size = depth // count
    for k in range(count):
        start = pl.multiple_of(offsets_ref[k], 32)
        out_ref[k * size : (k + 1) * size, :] = turned[pl.ds(start, size), :]


def project(counts, heads, size, offsets_ref, me_ref, own_ref, other_ref, place_ref, *refs):
    count = sum(counts)
    blocks, (x_ref, small_ref, normed_ref, taps_ref, gain_ref, w_out_ref, w_ref, sems, out_sem) = refs[:count], refs[count:]
    split = x_ref.shape[1]
    shards = w_ref.shape[0] // size
    load_blocks(offsets_ref, blocks[: counts[0]], w_ref, sems, size, (0, split))
    load_blocks(offsets_ref, blocks[counts[0] :], w_ref, sems, size, (split, w_ref.shape[1]), shards)
    keep = pltpu.make_async_copy(w_ref, w_out_ref, out_sem)
    depth, inner = w_ref.shape[0], x_ref.shape[1]
    tile = 512

    @pl.when(pl.program_id(0) == 0)
    def _():
        keep.start()
        spare = w_ref[:, inner + 2 * STATE :]
        turned = spare.astype(F32).T
        gain_ref[...] = jnp.broadcast_to(turned[heads + K + 2 : heads + K + 3, :], gain_ref.shape)
        few = turned[heads : heads + 16, :].astype(BF16)
        lanes = iota((depth, LANES), 1)
        for lo in range(0, inner + 2 * STATE, LANES):
            if lo < inner:
                wanted, row = place_ref[:, :LANES] == lanes + lo, 0
            else:
                wanted, row = place_ref[:, LANES:] == lanes + (lo - inner), 8
            moved = mm(few, jnp.where(wanted, 1.0, 0.0).astype(BF16))
            taps_ref[:, lo : lo + LANES] = moved[row : row + 8, :]

    rows = jnp.where(pl.program_id(0) == me_ref[0], own_ref[...], other_ref[...]).astype(F32)
    scale = lax.rsqrt(jnp.mean(rows * rows, axis=1, keepdims=True) + EPSILON)
    rows = (rows * scale * gain_ref[0:1, :]).astype(BF16)
    normed_ref[...] = rows
    for lo in range(0, inner, tile):
        x_ref[:, lo : lo + tile] = mm(rows, w_ref[:, lo : lo + tile]).astype(BF16)
    small_ref[...] = mm(rows, w_ref[:, inner:])

    @pl.when(pl.program_id(0) == pl.num_programs(0) - 1)
    def _():
        keep.wait()


def row_sums(lanes):
    return mm_exact(jnp.ones((8, LANES), F32), lanes, NT)


def spread_rows(values):
    pick = jnp.where(iota((8, LANES), 0) == 0, 1.0, 0.0).astype(F32)
    return mm_exact(values, pick, TN)


def gate_forward(normed_ref, w_ref, y_ref, gain_ref, z_ref, gg_ref, sq_ref, square):
    rows, width = z_ref.shape
    size = 512

    @pl.when(pl.program_id(0) == 0)
    def _():
        square[...] = jnp.zeros(square.shape, F32)

    for lo in range(0, rows, size):
        at = slice(lo, lo + size)
        z = mm(normed_ref[at, :], w_ref[...]).astype(BF16)
        z_ref[at, :] = z
        z = z.astype(F32)
        gated = y_ref[at, :].astype(F32) * (z * sigmoid(z))
        gg_ref[at, :] = (gated * gain_ref[K + 1 : K + 2, :]).astype(BF16)
        twice = gated * gated
        for part in range(0, width, LANES):
            square[at, :] += twice[:, part : part + LANES]

    @pl.when(pl.program_id(0) == pl.num_programs(0) - 1)
    def _():
        sq_ref[...] = row_sums(square[...])


def branch(me_ref, ends_ref, gg_ref, own_ref, other_ref, w_ref, mine_ref, away_ref, prod_ref, product):
    rows, width = mine_ref.shape
    size = 512

    @pl.when(pl.program_id(0) == 0)
    def _():
        product[...] = jnp.zeros(product.shape, F32)

    for index, (out_ref, cot_ref) in enumerate(((mine_ref, own_ref), (away_ref, other_ref))):
        first = jnp.where(index == 0, me_ref[0], 1 - me_ref[0]) * rows
        for lo in range(0, rows, size):
            at = pl.ds(pl.multiple_of(first + lo, size), size)
            u = mm(gg_ref[at, :], w_ref[...], NT)
            out_ref[lo : lo + size, :] = u.astype(BF16)
            term = u * cot_ref[lo : lo + size, :].astype(F32)
            for part in range(0, width, LANES):
                product[at, :] += term[:, part : part + LANES]

    @pl.when(pl.program_id(0) == pl.num_programs(0) - 1)
    def _():
        live = iota(product.shape, 0) < ends_ref[ends_ref.shape[0] - 1]
        prod_ref[...] = row_sums(jnp.where(live, product[...], 0.0))


def gate_backward(
    me_ref, ends_ref, own_ref, other_ref, w_ref, y_ref, z_ref, rg_ref, coef_ref, gain_ref,
    dy_ref, dz_ref, acc_ref, rg, coef,
):
    total, width = dy_ref.shape
    rows = own_ref.shape[0]
    size = 512

    @pl.when(pl.program_id(0) == 0)
    def _():
        live = iota(rg.shape, 0) < ends_ref[ends_ref.shape[0] - 1]
        rg[...] = spread_rows(rg_ref[...])
        coef[...] = spread_rows(coef_ref[...])
        rg[...] = jnp.where(live, rg[...], 0.0)

    gain = gain_ref[K + 1 : K + 2, :]
    sums = jnp.zeros((8, width), F32)
    for index, cot_ref in enumerate((own_ref, other_ref)):
        first = jnp.where(index == 0, me_ref[0], 1 - me_ref[0]) * rows
        for lo in range(0, rows, size):
            at = pl.ds(pl.multiple_of(first + lo, size), size)
            ds = mm(cot_ref[lo : lo + size, :], w_ref[...])
            z = z_ref[at, :].astype(F32)
            y = y_ref[at, :].astype(F32)
            scale = jnp.concatenate([rg[at, :]] * (width // LANES), axis=1)
            back = jnp.concatenate([coef[at, :]] * (width // LANES), axis=1)
            gate = sigmoid(z)
            silu = z * gate
            gated = y * silu
            d_normal = ds * scale
            sums = sums + (d_normal * gated).reshape(size // 8, 8, width).sum(axis=0)
            d_gated = d_normal * gain - gated * back
            dy_ref[at, :] = (d_gated * silu).astype(BF16)
            dz_ref[at, :] = (d_gated * y * (gate + silu * (1.0 - gate))).astype(BF16)
    acc_ref[...] = sums


def weight_grad(me_ref, own_ref, other_ref, d_ref, away_ref, keep_ref):
    half, rows = away_ref.shape[0], own_ref.shape[1]
    mine = d_ref[pl.ds(pl.multiple_of(me_ref[0] * rows, rows), rows), :]
    theirs = d_ref[pl.ds(pl.multiple_of((1 - me_ref[0]) * rows, rows), rows), :]
    for at, ref in ((0, away_ref), (half, keep_ref)):
        total = mm(own_ref[at : at + half, :], mine) + mm(other_ref[at : at + half, :], theirs)
        ref[...] = total.astype(BF16)


def add_away(keep_ref, core_ref, away_ref):
    away_ref[...] = (keep_ref[...].astype(F32) + core_ref[...].astype(F32)).astype(BF16)


def normed_back(rows_ref, dz_ref, dxa_ref, dxb_ref, wz_ref, wx_ref, out_ref):
    n_a = dxa_ref.shape[1]
    total = mm(dz_ref[...], wz_ref[...], NT)
    total = total + mm(dxa_ref[...], wx_ref[:, :n_a], NT) + mm(dxb_ref[...], wx_ref[:, n_a:], NT)
    out_ref[...] = total.astype(BF16)


def params():
    return pltpu.CompilerParams(dimension_semantics=("arbitrary",), vmem_limit_bytes=VMEM_LIMIT)


SMALL_COST = pl.CostEstimate(flops=1000, bytes_accessed=1000, transcendentals=0)


def rows_spec(block, width, column=0):
    return pl.BlockSpec((block, width), lambda i: (i, column))


def whole_spec(shape, column=0):
    return pl.BlockSpec(shape, lambda i: (0, column))


def local(
    tokens,
    cotangent,
    lengths,
    norm_gain,
    w_zx,
    w_bc,
    w_dt,
    conv_x,
    conv_x_bias,
    conv_bc,
    conv_bc_bias,
    dt_bias,
    a_log,
    d_skip,
    gate_gain,
    w_out,
):
    n_t = lax.axis_size("tensor")
    n_dp = lax.axis_size("dp")
    me_t = lax.axis_index("tensor")
    me_dp = lax.axis_index("dp")
    own_rows, depth = tokens.shape
    group = own_rows * n_t
    chunks = group // Q
    heads = dt_bias.shape[0]
    inner = heads * WIDTH
    inner_total = inner * n_t
    shard = w_zx.shape[1]
    pairs = [(i, n_t - 1 - i) for i in range(n_t)]

    def swap(v):
        return lax.ppermute(v, "tensor", pairs)

    def in_order(mine, other, axis=0):
        low = jnp.where(me_t == 0, mine, other)
        high = jnp.where(me_t == 0, other, mine)
        return jnp.concatenate([low, high], axis=axis)

    def sum_dp(v):
        step = 1
        while step < n_dp:
            v = v + lax.ppermute(v, "dp", [(i, i ^ step) for i in range(n_dp)])
            step *= 2
        return v

    def after(value, *others):
        return lax.optimization_barrier((value, *others))[0]

    ring = 4
    plane = n_dp // (2 * ring)

    around = [(i, (i + 2 * plane) % n_dp) for i in range(n_dp)]
    across = [(i, i ^ 2) for i in range(n_dp)]
    beside = [(i, i ^ 1) for i in range(n_dp)]

    def send(v, way):
        return lax.ppermute(v, "dp", way)

    by_hand = plane == 2 and shard % 32 == 0

    def whole(v):
        return [lax.all_gather(v, "dp", axis=0, tiled=True)]

    def relative_order():
        level, side, core = me_dp // 4, (me_dp // 2) % 2, me_dp % 2
        order = []
        for dc in (1, 0):
            for dy in (1, 0):
                for dz in range(1, ring + 1):
                    order.append(((level - dz + ring) % ring) * 4 + (side ^ dy) * 2 + (core ^ dc))
        return order

    def fold_away(keep, got):
        half, width = keep.shape[0] // 2, keep.shape[1]
        spec = pl.BlockSpec((half // 4, width), lambda i: (i, 0))
        return pl.pallas_call(
            add_away,
            grid=(4,),
            in_specs=[spec, spec],
            out_specs=spec,
            out_shape=jax.ShapeDtypeStruct((half, width), BF16),
            compiler_params=params(),
            cost_estimate=SMALL_COST,
            name="add_away",
        )(keep, got)

    def ring_part(keep, core, got, came, turn):
        low, high = (turn - 1) * shard, turn * shard
        half = keep.shape[0] // 2
        part = keep[half + low : half + high].astype(F32) + core[half + low : half + high].astype(F32)
        part = part + got[low:high].astype(F32)
        if came is not None:
            part = part + came.astype(F32)
        return part if turn == ring else part.astype(BF16)

    ends = jnp.cumsum(lengths[0]).astype(jnp.int32)
    live = (lax.iota(jnp.int32, group) < ends[-1]).astype(F32)
    live_own = lax.dynamic_slice_in_dim(live, me_t * own_rows, own_rows, 0)
    me = me_t.astype(jnp.int32).reshape(1)

    span_p = conv_x_bias.shape[1]
    span_n = conv_bc_bias.shape[1]
    half_bc = w_bc.shape[1]
    bits = jnp.concatenate([norm_gain, conv_bc.reshape(-1), conv_bc_bias.reshape(-1)])
    bits = jnp.pad(bits, (0, LANES - bits.shape[0]))
    tiny = jnp.concatenate([w_bc.reshape(2 * half_bc, STATE), bits[None]], axis=0)
    other_tiny = swap(tiny)
    other_bc = other_tiny[: 2 * half_bc].reshape(w_bc.shape)
    both_bits = [bits, other_tiny[2 * half_bc]]
    at = norm_gain.shape[0]
    gain_pair = in_order(*[v[:at] for v in both_bits])[:, None]
    taps_bc = in_order(*[v[at : at + conv_bc.size].reshape(2, span_n, K) for v in both_bits], axis=1)
    at += conv_bc.size
    bias_bc = in_order(*[v[at : at + 2 * span_n].reshape(2, span_n, 1) for v in both_bits], axis=1)
    spare_bc = jnp.concatenate([taps_bc, bias_bc], axis=2).reshape(4 * span_n, K + 1)
    spare_x = [conv_x.reshape(shard, K), conv_x_bias.reshape(shard, 1), gate_gain.reshape(shard, 1), gain_pair]
    bc_pair = in_order(w_bc, other_bc, axis=1)
    w_x = w_zx[1]
    w_small = jnp.concatenate(
        [bc_pair[0], bc_pair[1], w_dt, *spare_x, jnp.zeros((shard, 8 - K - 3), BF16)]
        + [jnp.pad(spare_bc, ((0, shard - 4 * span_n), (0, LANES - heads - 8 - K - 1)))],
        axis=1,
    )
    gain_pair = gain_pair.astype(F32)
    where = after(lax.iota(jnp.int32, depth), w_small)
    home, inside = where // shard, where % shard
    place_x = (inside // span_p) * WIDTH + home * span_p + inside % span_p
    half_n = 2 * span_n
    place_bc = (inside // half_n) * STATE + home * half_n + inside % half_n
    place = jnp.concatenate([jnp.broadcast_to(v[:, None], (depth, LANES)) for v in (place_x, place_bc)], axis=1)
    par = jnp.concatenate([dt_bias[None], a_log[None], jnp.zeros((6, heads), F32)], axis=0)
    par = jnp.concatenate([par, jnp.zeros((8, LANES - heads), F32)], axis=1)
    skip = jnp.repeat(d_skip, WIDTH)[None]
    members = lax.iota(jnp.int32, inner)[:, None] // WIDTH
    sel = (members == lax.iota(jnp.int32, LANES)[None, :]).astype(BF16)
    smem = pl.BlockSpec(memory_space=pltpu.SMEM)
    vmem = pl.BlockSpec(memory_space=pltpu.VMEM)
    hbm = pl.BlockSpec(memory_space=pl.ANY)
    n_small = 2 * STATE + LANES
    n_conv = inner + 2 * STATE
    w_rest = jnp.concatenate([w_zx[0], w_out.T], axis=1)

    def turn(rows):
        return pl.pallas_call(
            turn_rows,
            in_specs=[smem, vmem],
            out_specs=vmem,
            out_shape=jax.ShapeDtypeStruct((depth, own_rows), BF16),
            scratch_shapes=[pltpu.VMEM((depth, own_rows), BF16)],
            compiler_params=pltpu.CompilerParams(vmem_limit_bytes=VMEM_LIMIT),
            cost_estimate=SMALL_COST,
            name="turn_rows",
        )((jnp.stack(relative_order()) * shard).astype(jnp.int32), rows)

    def place_of(turn, side, core):
        level = (me_dp // (2 * plane) - turn + ring) % ring
        return (level * (2 * plane) + ((me_dp % (2 * plane)) ^ (2 * side + core))) * shard

    together = lambda *values: list(lax.optimization_barrier(tuple(values)))
    joined = lambda *values: jnp.concatenate(values, axis=0)
    if by_hand:
        shift = lambda k: [(i, (i + 2 * plane * k) % n_dp) for i in range(n_dp)]
        l1, o0, c0 = together(send(w_x, around), send(w_x, across), send(w_x, beside))
        late, w_small = together(tokens, w_small, l1, o0, c0)[:2]
        l2, o1, s1, s2, s3, turned_own = together(
            send(l1, around), send(l1, across), send(w_small, shift(1)), send(w_small, shift(2)), send(w_small, shift(3)),
            turn(late),
        )
        w_rest = after(jnp.concatenate([w_zx[0], w_out.T], axis=1), l2)
        zo_all = lax.all_gather(w_rest, "dp", axis=0, tiled=True)
        small_line = joined(w_small, s1, s2, s3)
        split = own_rows // 2
        l3, o2, c1, small_across, t0 = together(
            send(l2, around), send(l2, across), send(joined(l1, o0), beside), send(small_line, across), swap(late[:split])
        )
        o3, c2, small_beside, t1, place, par, skip, sel = together(
            send(l3, across), send(joined(l2, o1), beside), send(joined(small_line, small_across), beside),
            swap(after(late[split:], t0)), place, par, skip, sel,
        )
        other_tokens = joined(t0, t1)
        c3, turned_other, other_tokens = together(send(joined(l3, o2, o3), beside), turn(other_tokens), other_tokens)
        other_cot = swap(after(cotangent, other_tokens))
        wx_parts = [w_x, l1, l2, l3, o0, o1, o2, o3, c0, c1, c2, c3]
        order = [(t, 0, 0) for t in range(4)] + [(t, 1, 0) for t in range(4)]
        order += [(0, 0, 1), (1, 0, 1), (0, 1, 1), (2, 0, 1), (1, 1, 1), (3, 0, 1), (2, 1, 1), (3, 1, 1)]
        small_parts = [small_line, small_across, small_beside]
        order += [(t, side, core) for core in range(2) for side in range(2) for t in range(4)]
        offsets = jnp.stack([place_of(*key) for key in order]).astype(jnp.int32)
    else:
        wx_parts, small_parts = whole(w_x), whole(w_small)
        zo_all = whole(jnp.concatenate([w_zx[0], w_out.T], axis=1))[0]
        other_tokens, other_cot = swap(tokens), swap(cotangent)
        offsets = jnp.zeros((2,), jnp.int32)
    counts = (len(wx_parts), len(small_parts))
    sems = pltpu.SemaphoreType.DMA((offsets.shape[0],))
    tok_own = tokens.astype(F32)
    inv_tok = lax.rsqrt(jnp.mean(tok_own * tok_own, axis=1, keepdims=True) + EPSILON)

    block = own_rows
    steps = group // block
    x_raw, small, normed, taps, gain_in, wx_all = pl.pallas_call(
        partial(project, counts, heads, shard if by_hand else depth),
        grid=(steps,),
        in_specs=[
            smem,
            smem,
            whole_spec((block, depth)),
            whole_spec((block, depth)),
            whole_spec((depth, 2 * LANES)),
        ]
        + [hbm] * sum(counts),
        out_specs=[
            rows_spec(block, inner),
            rows_spec(block, n_small),
            rows_spec(block, depth),
            whole_spec((8, n_conv)),
            whole_spec((8, depth)),
            hbm,
        ],
        out_shape=[
            jax.ShapeDtypeStruct((group, inner), BF16),
            jax.ShapeDtypeStruct((group, n_small), F32),
            jax.ShapeDtypeStruct((group, depth), BF16),
            jax.ShapeDtypeStruct((8, n_conv), F32),
            jax.ShapeDtypeStruct((8, depth), F32),
            jax.ShapeDtypeStruct((depth, inner + n_small), BF16),
        ],
        scratch_shapes=[pltpu.VMEM((depth, inner + n_small), BF16), sems, pltpu.SemaphoreType.DMA],
        compiler_params=params(),
        cost_estimate=SMALL_COST,
        name="project",
    )(offsets, me, tokens, other_tokens, place, *wx_parts, *small_parts)
    xc, pre, bc, y_all, states = pl.pallas_call(
        partial(scan_forward, heads),
        grid=(chunks,),
        in_specs=[
            smem,
            rows_spec(Q, inner),
            rows_spec(Q, n_small),
            whole_spec((8, n_conv)),
            whole_spec((8, LANES)),
            whole_spec((1, inner)),
        ],
        out_specs=[
            rows_spec(Q, inner),
            rows_spec(Q, n_conv),
            rows_spec(Q, 2 * STATE),
            rows_spec(Q, inner),
            pl.BlockSpec((1, STATE, inner), lambda i: (i, 0, 0)),
        ],
        out_shape=[
            jax.ShapeDtypeStruct((group, inner), BF16),
            jax.ShapeDtypeStruct((group, n_conv), BF16),
            jax.ShapeDtypeStruct((group, 2 * STATE), BF16),
            jax.ShapeDtypeStruct((group, inner), BF16),
            jax.ShapeDtypeStruct((chunks, STATE, inner), BF16),
        ],
        scratch_shapes=[pltpu.VMEM((n_conv // LANES, Q + 8, LANES), F32), pltpu.VMEM((STATE, inner), F32)],
        compiler_params=params(),
        cost_estimate=SMALL_COST,
        name="scan_forward",
    )(ends, x_raw, small, taps, par, skip)

    cot_all = in_order(cotangent, other_cot)
    if by_hand:
        normed, cot_all = lax.optimization_barrier((normed, after(cot_all, y_all)))
    tile = 512
    columns = lambda rows, shift=0: pl.BlockSpec((rows, tile), lambda j: (0, j + shift))
    fixed = lambda shape: pl.BlockSpec(shape, lambda j: (0, 0))
    tiles = inner // tile
    z_all, gg, sq = pl.pallas_call(
        gate_forward,
        grid=(tiles,),
        in_specs=[fixed((group, depth)), columns(depth), columns(group), columns(8)],
        out_specs=[columns(group), columns(group), fixed((8, group))],
        out_shape=[
            jax.ShapeDtypeStruct((group, inner), BF16),
            jax.ShapeDtypeStruct((group, inner), BF16),
            jax.ShapeDtypeStruct((8, group), F32),
        ],
        scratch_shapes=[pltpu.VMEM((group, LANES), F32)],
        compiler_params=params(),
        cost_estimate=SMALL_COST,
        name="gate_forward",
    )(normed, zo_all, y_all, taps)
    sq_got = swap(sq)

    u_own, u_send, prod = pl.pallas_call(
        branch,
        grid=(depth // tile,),
        in_specs=[
            smem,
            smem,
            fixed((group, inner)),
            columns(own_rows),
            columns(own_rows),
            pl.BlockSpec((tile, inner), lambda j: (j, 1)),
        ],
        out_specs=[columns(own_rows), columns(own_rows), fixed((8, group))],
        out_shape=[
            jax.ShapeDtypeStruct((own_rows, depth), BF16),
            jax.ShapeDtypeStruct((own_rows, depth), BF16),
            jax.ShapeDtypeStruct((8, group), F32),
        ],
        scratch_shapes=[pltpu.VMEM((group, LANES), F32)],
        compiler_params=params(),
        cost_estimate=SMALL_COST,
        name="branch",
    )(me, ends, gg, cotangent, other_cot, zo_all)
    prod_got = swap(prod)
    sq_all = sq + after(sq_got, prod)
    inv_gate8 = lax.rsqrt(sq_all / inner_total + EPSILON)
    inv_gate = inv_gate8[0]
    d_branch = (cot_all.astype(F32) * (live * inv_gate)[:, None]).astype(BF16)
    g_out = lax.dot_general(d_branch, gg, TN, preferred_element_type=F32).astype(BF16)
    grad_out = lax.psum_scatter(g_out, "dp", scatter_dimension=0, tiled=True)
    prod_got = after(prod_got, g_out)
    u_recv = swap(after(u_send, g_out))
    inv_own = lax.dynamic_slice_in_dim(inv_gate, me_t * own_rows, own_rows, 0)
    out_branch = (u_own.astype(F32) + u_recv.astype(F32)) * (inv_own * live_own)[:, None]
    layer_out = (tokens.astype(F32) + out_branch).astype(BF16)

    prod_all = prod + prod_got
    coef8 = inv_gate8 * inv_gate8 * inv_gate8 * (prod_all / inner_total)
    dy, dz, gain_acc = pl.pallas_call(
        gate_backward,
        grid=(tiles,),
        in_specs=[
            smem,
            smem,
            fixed((own_rows, depth)),
            fixed((own_rows, depth)),
            columns(depth, tiles),
            columns(group),
            columns(group),
            fixed((8, group)),
            fixed((8, group)),
            columns(8),
        ],
        out_specs=[columns(group), columns(group), columns(8)],
        out_shape=[
            jax.ShapeDtypeStruct((group, inner), BF16),
            jax.ShapeDtypeStruct((group, inner), BF16),
            jax.ShapeDtypeStruct((8, inner), F32),
        ],
        scratch_shapes=[pltpu.VMEM((group, LANES), F32), pltpu.VMEM((group, LANES), F32)],
        compiler_params=params(),
        cost_estimate=SMALL_COST,
        name="gate_backward",
    )(me, ends, cotangent, other_cot, zo_all, y_all, z_all, inv_gate8, coef8, taps)
    dot = partial(lax.dot_general, preferred_element_type=F32)
    front = depth // 2

    def gradient(d, width):
        outs = pl.BlockSpec((front, width), lambda j: (0, j))
        return pl.pallas_call(
            weight_grad,
            grid=(d.shape[1] // width,),
            in_specs=[smem, fixed((depth, own_rows)), fixed((depth, own_rows)), pl.BlockSpec((group, width), lambda j: (0, j))],
            out_specs=[outs, outs],
            out_shape=[jax.ShapeDtypeStruct((front, d.shape[1]), BF16)] * 2,
            compiler_params=params(),
            cost_estimate=SMALL_COST,
            name="weight_grad",
        )(me, turned_own, turned_other, d)

    if by_hand:
        g_send, z_keep = gradient(dz, tile)
        z_got = send(g_send, beside)
        dy = after(dy, z_keep, g_send)
    else:
        grad_z = lax.psum_scatter(dot(normed, dz, TN).astype(BF16), "dp", scatter_dimension=0, tiled=True)

    halo_spec = pl.BlockSpec((n_conv // LANES, 8, LANES), lambda i: (0, 0, 0))

    def backward(top, number, carry):
        back = lambda width: pl.BlockSpec((Q, width), lambda i: (top - i, 0))
        operands = [ends, dy, xc, pre, x_raw, small, bc, states, taps, par, skip, sel, *carry]
        acc_spec = whole_spec((8 * (K + 2), n_conv))
        carry_shapes = [
            jax.ShapeDtypeStruct((STATE, inner), F32),
            jax.ShapeDtypeStruct((n_conv // LANES, 8, LANES), F32),
        ]
        carry_specs = []
        if carry:
            carry_specs = [whole_spec((STATE, inner)), halo_spec, acc_spec, whole_spec((16, LANES))]
            carry_specs += [whole_spec((8, inner)), hbm, hbm]
        return pl.pallas_call(
            partial(scan_backward, heads, chunks, top),
            grid=(number,),
            in_specs=[
                smem,
                back(inner),
                back(inner),
                back(n_conv),
                back(inner),
                back(n_small),
                back(2 * STATE),
                pl.BlockSpec((1, STATE, inner), lambda i: (top - i, 0, 0)),
                whole_spec((8, n_conv)),
                whole_spec((8, LANES)),
                whole_spec((1, inner)),
                whole_spec((inner, LANES)),
            ]
            + carry_specs,
            out_specs=[
                back(n_a),
                back(n_b),
                *([whole_spec((8, n_conv))] if carry else []),
                acc_spec,
                whole_spec((16, LANES)),
                *([] if carry else [whole_spec((STATE, inner)), halo_spec]),
            ],
            out_shape=[
                jax.ShapeDtypeStruct((group, n_a), BF16),
                jax.ShapeDtypeStruct((group, n_b), BF16),
                *([jax.ShapeDtypeStruct((8, n_conv), F32)] if carry else []),
                jax.ShapeDtypeStruct((8 * (K + 2), n_conv), F32),
                jax.ShapeDtypeStruct((16, LANES), F32),
                *([] if carry else carry_shapes),
            ],
            scratch_shapes=[
                pltpu.VMEM((STATE, inner), F32),
                pltpu.VMEM((n_conv // LANES, Q + 8, LANES), F32),
                pltpu.VMEM((Q, inner), BF16),
                pltpu.VMEM((Q, inner), BF16),
                pltpu.VMEM((Q, inner), BF16),
                pltpu.VMEM((Q, inner), BF16),
                pltpu.VMEM((Q, inner), BF16),
                pltpu.VMEM((Q, inner), BF16),
                pltpu.VMEM((STATE, inner), BF16),
                pltpu.VMEM((8, inner), F32),
            ],
            input_output_aliases={len(operands) - 2: 0, len(operands) - 1: 1} if carry else {},
            compiler_params=params(),
        cost_estimate=SMALL_COST,
            name="scan_backward",
        )(*operands)

    half_chunks = chunks // 2
    n_b = (inner + n_small) // 3
    n_a = inner + n_small - n_b
    dxa, dxb, acc, hacc, d_state, halo = backward(chunks - 1, chunks - half_chunks, ())
    if by_hand:
        z_got, dxa = lax.optimization_barrier((z_got, dxa))
        z_core, z_away = z_got, fold_away(z_keep, z_got)
        z_got = send(z_away, across)
        d_state = after(d_state, z_away)
    dxa, dxb, vector = backward(half_chunks - 1, half_chunks, (d_state, halo, acc, hacc, gain_acc, dxa, dxb))[:3]
    dxa = after(dxa, u_recv)
    lanes_shared = lax.iota(jnp.int32, n_conv)[None, :] >= inner
    bits_of = lambda turn: [(i, i ^ (1 << turn)) for i in range(n_dp)]
    if by_hand:
        g_x = dot(normed, dxa, TN).astype(BF16)
        g_x, grad_out = lax.optimization_barrier((g_x, grad_out))
        grad_a = lax.psum_scatter(g_x, "dp", scatter_dimension=0, tiled=True)
        z_got, dxb, vector = lax.optimization_barrier((z_got, dxb, vector, g_x))[:3]
        z_out = ring_part(z_keep, z_core, z_got, None, 1)
        z_came = send(z_out, around)
        shared_got = swap(vector)
        b_send, b_keep = gradient(after(dxb, z_out), n_b)
        b_got = send(b_send, beside)
        shared_got, z_came, b_keep = lax.optimization_barrier((shared_got, z_came, b_keep))
        vector = vector + jnp.where(lanes_shared, shared_got, 0.0)
        z_out = ring_part(z_keep, z_core, z_got, z_came, 2)
        z_came, vector_got = send(z_out, around), send(vector, bits_of(0))
        dz = after(dz, b_send, b_keep, z_out, vector)
    else:
        dx = jnp.concatenate([dxa, dxb], axis=1)
        grad_x = lax.psum_scatter(dot(normed, dx, TN).astype(BF16), "dp", scatter_dimension=0, tiled=True)

    def back_rows(which, dz):
        pick = lambda width: pl.BlockSpec((own_rows, width), lambda j, rows: (rows[0], 0))
        return pl.pallas_call(
            normed_back,
            grid_spec=pltpu.PrefetchScalarGridSpec(
                num_scalar_prefetch=1,
                grid=(depth // tile,),
                in_specs=[
                    pick(inner),
                    pick(n_a),
                    pick(n_b),
                    pl.BlockSpec((tile, inner), lambda j, rows: (j, 0)),
                    pl.BlockSpec((tile, inner + n_small), lambda j, rows: (j, 0)),
                ],
                out_specs=pl.BlockSpec((own_rows, tile), lambda j, rows: (0, j)),
            ),
            out_shape=jax.ShapeDtypeStruct((own_rows, depth), BF16),
            compiler_params=params(),
            cost_estimate=SMALL_COST,
            name="normed_back",
        )(which, dz, dxa, dxb, zo_all, wx_all)

    dn_send = back_rows(n_t - 1 - me, dz)
    if by_hand:
        w_sum = lambda w, g: jnp.sum(w.astype(F32) * g, axis=1)
        b_got, vector_got, dn_send, z_came = lax.optimization_barrier((b_got, vector_got, dn_send, z_came))
        dn_got = swap(dn_send)
        b_core, b_away = b_got, fold_away(b_keep, b_got)
        b_got = send(b_away, across)
        vector = vector + vector_got
        z_out = ring_part(z_keep, z_core, z_got, z_came, 3)
        z_came, vector_got = send(z_out, around), send(vector, bits_of(1))
        dn_own = back_rows(me, after(dz, vector, z_out, b_away))
        vector_got, dn_own, b_got, z_came = lax.optimization_barrier((vector_got, dn_own, b_got, z_came))
        vector = vector + vector_got
        b_out = ring_part(b_keep, b_core, b_got, None, 1)
        b_came, vector_got = send(b_out, around), send(vector, bits_of(2))
        grad_z = ring_part(z_keep, z_core, z_got, z_came, ring) * gain_pair
        in_part = w_sum(w_zx[0], grad_z)
        vector_got, grad_z, in_part, b_came = lax.optimization_barrier((vector_got, grad_z, in_part, b_came))
        vector = vector + vector_got
        b_out = ring_part(b_keep, b_core, b_got, b_came, 2)
        b_came, vector_got = send(b_out, around), send(vector, bits_of(3))
        grad_out = grad_out.astype(F32).T
        vector_got, grad_out, layer_out, b_came = lax.optimization_barrier((vector_got, grad_out, layer_out, b_came))
        vector = vector + vector_got
        b_came = send(ring_part(b_keep, b_core, b_got, b_came, 3), around)
    else:
        vector = sum_dp(vector + jnp.where(lanes_shared, swap(vector), 0.0))
        dn_own = back_rows(me, dz)
        dn_got = swap(dn_send)
        grad_out = grad_out.astype(F32).T
        grad_z, grad_x = grad_z.astype(F32), grad_x.astype(F32)
        in_part = jnp.sum(w_zx[0].astype(F32) * grad_z, axis=1) + jnp.sum(jnp.concatenate([w_x, w_small], axis=1).astype(F32) * grad_x, axis=1)

    me_all = me_dp * n_t + me_t
    bc_sum = vector[: K + 1, inner:].reshape(K + 1, 2, STATE)
    bc_sum = lax.dynamic_slice_in_dim(bc_sum, me_all * span_n, span_n, 2)
    grad_bc_taps = bc_sum[:K].transpose(1, 2, 0).reshape(conv_bc.shape)
    grad_bc_bias = bc_sum[K]
    x_sum = vector[: K + 3, :inner].reshape(K + 3, heads, WIDTH)
    grad_skip = x_sum[K + 1].sum(axis=1)
    x_sum = lax.dynamic_slice_in_dim(x_sum, me_dp * span_p, span_p, 2)
    grad_x_taps = x_sum[:K].transpose(1, 2, 0).reshape(conv_x.shape)
    grad_x_bias = x_sum[K]
    grad_gate = x_sum[K + 2]
    grad_dt_bias = vector[K + 3, :heads]
    grad_a_log = vector[K + 3, LANES : LANES + heads]
    dn = (dn_own.astype(F32) + dn_got.astype(F32)) * gain_in[0:1, :]
    grad_tokens = (
        cotangent.astype(F32)
        + inv_tok * dn
        - tok_own * inv_tok * inv_tok * inv_tok * jnp.mean(dn * tok_own, axis=1, keepdims=True)
    )

    if by_hand:
        grad_b = ring_part(b_keep, b_core, b_got, b_came, ring) * gain_pair
        in_part = in_part + w_sum(w_x[:, n_a:], grad_b[:, : inner - n_a]) + w_sum(w_small, grad_b[:, inner - n_a :])
        outs = (grad_bc_taps, grad_bc_bias, grad_skip, grad_x_taps, grad_x_bias, grad_gate, grad_dt_bias, grad_a_log)
        outs = lax.optimization_barrier((*outs, grad_tokens, grad_b, in_part, grad_a))
        grad_bc_taps, grad_bc_bias, grad_skip, grad_x_taps, grad_x_bias, grad_gate, grad_dt_bias, grad_a_log = outs[:8]
        grad_tokens, grad_b, in_part, grad_a = outs[8:]
        grad_a = grad_a.astype(F32)
        in_part = in_part + w_sum(w_x[:, :n_a], grad_a)
    else:
        grad_a, grad_b = grad_x[:, :n_a], grad_x[:, n_a:]
    at = inner - n_a
    bc_part = jnp.concatenate([grad_b[:, at : at + 2 * STATE], jnp.broadcast_to(in_part[:, None], (shard, LANES))], axis=1)
    grad_zx = jnp.stack([grad_z, jnp.concatenate([grad_a, grad_b[:, :at]], axis=1)])
    grad_dt = grad_b[:, at + 2 * STATE : at + 2 * STATE + heads]
    half = half_bc
    bc_own = lax.dynamic_slice_in_dim(bc_part, me_t * half, half, 0)
    bc_send = lax.dynamic_slice_in_dim(bc_part, (n_t - 1 - me_t) * half, half, 0)
    bc_total = bc_own + swap(bc_send)
    own_gain = norm_gain.astype(F32)
    grad_bc = bc_total[:, : 2 * STATE].reshape(half, 2, STATE).transpose(1, 0, 2)
    grad_in = bc_total[:, 2 * STATE] / own_gain
    return (
        layer_out,
        grad_tokens,
        grad_in,
        grad_zx,
        grad_bc,
        grad_dt,
        grad_x_taps,
        grad_x_bias,
        grad_bc_taps,
        grad_bc_bias,
        grad_dt_bias,
        grad_a_log,
        grad_skip,
        grad_gate,
        grad_out,
    )


def solution(mesh):
    both = ("dp", "tensor")
    in_specs = (
        P(both, None),
        P(both, None),
        P("dp", None),
        P(both),
        P(None, "dp", "tensor"),
        P(None, both, None),
        P("dp", "tensor"),
        P("tensor", "dp"),
        P("tensor", "dp"),
        P(None, both),
        P(None, both),
        P("tensor"),
        P("tensor"),
        P("tensor"),
        P("tensor", "dp"),
        P("tensor", "dp"),
    )
    out_specs = (
        P(both, None),
        P(both, None),
        P(both),
        P(None, "dp", "tensor"),
        P(None, both, None),
        P("dp", "tensor"),
        P("tensor", "dp"),
        P("tensor", "dp"),
        P(None, both),
        P(None, both),
        P("tensor"),
        P("tensor"),
        P("tensor"),
        P("tensor", "dp"),
        P("tensor", "dp"),
    )
    return jax.shard_map(local, mesh=mesh, in_specs=in_specs, out_specs=out_specs, check_vma=False)
```
